32 devices in a mesh: mol: 16 (over z, x, core), tp: 2 (over y).
Axes of the slice: x: 2, y: 2, z: 4, core: 2. Of those that a mesh axis runs over, the one named last changes fastest.
Arguments:
- hidden_in: bfloat16 [16384, 768], P(('mol', 'tp')), may hold values from -6 to 6
- positions: float32 [3, 16384], P(None, ('mol', 'tp')), may hold values from -8 to 8
- atom_types: int32 [16384], P(('mol', 'tp')), may hold values from 0 to 15
- hop_counts: int32 [16384, 64], P(('mol', 'tp')), may hold values from 0 to 15
- edge_types: int32 [16384, 64], P(('mol', 'tp')), may hold values from 0 to 7
- lengths: int32 [256], P('mol'), may hold values from 20 to 60
- branches: int32 [256, 2], P(('mol', 'tp')), may hold values from 0 to 1, as said below
- attn_gain: float32 [768], replicated, may hold values from 0.5 to 1.5
- attn_shift: float32 [768], replicated, may hold values from -1.75 to 1.75
- qkv_weight: bfloat16 [768, 3, 768], P(None, None, 'tp'), may hold values from -0.21875 to 0.21875
- proj_weight: bfloat16 [768, 768], P('tp'), may hold values from -0.875 to 0.875
- ffn_gain: float32 [768], replicated, may hold values from 0.5 to 1.5
- ffn_shift: float32 [768], replicated, may hold values from -1.75 to 1.75
- up_weight: bfloat16 [768, 768], P(None, 'tp'), may hold values from -0.21875 to 0.21875
- up_bias: float32 [768], replicated, may hold values from -3 to 3
- down_weight: bfloat16 [768, 768], P('tp'), may hold values from -0.21875 to 0.21875
- down_bias: float32 [768], replicated, may hold values from -1.75 to 1.75
- kernel_scale: float32 [16, 16], replicated, may hold values from 0.5 to 1.5
- kernel_shift: float32 [16, 16], replicated, may hold values from -3 to 3
- centers: float32 [128], replicated, may hold values from 0 to 6
- spreads: float32 [128], replicated, may hold values from 0.5 to 2
- first_weight: bfloat16 [128, 128], replicated, may hold values from -1.5 to 1.5
- first_bias: float32 [128], replicated, may hold values from -3 to 3
- second_weight: bfloat16 [128, 32], replicated, may hold values from -0.75 to 0.75
- hop_table: float32 [16, 32], replicated, may hold values from -3 to 3
- edge_table: float32 [8, 32], replicated, may hold values from -3 to 3
- cotangent: bfloat16 [16384, 768], P(('mol', 'tp')), may hold values from -6 to 6
Outputs:
- output: bfloat16 [16384, 768], P(('mol', 'tp'))
- grad_input: bfloat16 [16384, 768], P(('mol', 'tp'))
- grad_attn_gain: float32 [768], replicated
- grad_attn_shift: float32 [768], replicated
- grad_qkv_weight: float32 [768, 3, 768], P(None, None, 'tp')
- grad_proj_weight: float32 [768, 768], P('tp')
- grad_ffn_gain: float32 [768], replicated
- grad_ffn_shift: float32 [768], replicated
- grad_up_weight: float32 [768, 768], P(None, 'tp')
- grad_up_bias: float32 [768], replicated
- grad_down_weight: float32 [768, 768], P('tp')
- grad_down_bias: float32 [768], replicated
- grad_kernel_scale: float32 [16, 16], replicated
- grad_kernel_shift: float32 [16, 16], replicated
- grad_centers: float32 [128], replicated
- grad_spreads: float32 [128], replicated
- grad_first_weight: float32 [128, 128], replicated
- grad_first_bias: float32 [128], replicated
- grad_second_weight: float32 [128, 32], replicated
- grad_hop_table: float32 [16, 32], replicated
- grad_edge_table: float32 [8, 32], replicated
The draws below stay inside these ranges and needn't reach their ends.
Inputs may be any that keep to these rules, and one draw needn't show every extreme that they name: The molecule of slot s occupies its first lengths[s] atom positions; the other positions of the slot are padding and are never attended to. `branches`: column 0 is a molecule's 2D flag and column 1 its 3D flag; every row has at least one set, and 2D-only, 3D-only and joint molecules all occur.
All inputs are finite; a program needn't handle non-finite values.
Results may differ from the reference program's by a relative error of at most 0.025.
Values may be sent and summed in bfloat16 or wider, within the bound.
A program may use at most 192 MiB of HBM per device.

```python
import math
import jax
import jax.numpy as jnp
from jax import lax

D = 768
H = 32
HD = 24
FF = 768
K = 128
SLOT = 64
HOPS = 16
EDGES = 8
ATOMS = 16
LEN_MIN = 20
LEN_MAX = 60
SLOTS_DEV = 16
SLOTS = 256
TOKENS = 16384


def draw_branches(key, part):
    key = jax.random.fold_in(key, 11)
    kinds = jax.random.randint(key, (SLOTS,), 0, 3)
    return jnp.stack([(kinds != 1).astype(jnp.int32), (kinds != 0).astype(jnp.int32)], axis=1)


def set_ends(array, key, low, largest):
    longest = array.shape.index(max(array.shape))
    spots = []
    for shift in (0, 1):
        where = [jax.random.randint(jax.random.fold_in(key, axis), (), 0, length) for axis, length in enumerate(array.shape)]
        where[longest] = (where[longest] + shift) % array.shape[longest]
        spots.append(tuple(where))
    return array.at[spots[0]].set(low).at[spots[1]].set(largest)


def block_scale(key, dims, shards, smallest, largest):
    level = 1.0
    for axis_at, parts in shards:
        heights = jax.random.uniform(jax.random.fold_in(jax.random.fold_in(key, 6), axis_at), (parts,), jnp.float32, smallest / len(shards), largest / len(shards))
        level = level * jnp.repeat(jnp.exp(heights), dims[axis_at] // parts).reshape((-1,) + (1,) * (len(dims) - 1 - axis_at))
    return level


def gaussian(own_key, dims, deviation, limit, split=(), held_as=jnp.bfloat16):
    values = jax.random.normal(own_key, dims, jnp.float32) * deviation
    if len(split) > 0:
        values = block_scale(own_key, dims, split, -0.22, 0.18) * values
    return jnp.clip(values, min=-limit, max=limit).astype(held_as)


def setup_inputs(seed: int = 0) -> dict:
    seeds = jax.random.split(jax.random.key(seed), 28)
    hidden_in = gaussian(seeds[0], (TOKENS, D), 1.0, 6.0, ((0, 32),))
    positions = gaussian(seeds[1], (3, TOKENS), 1.5, 8.0, ((1, 32),), jnp.float32)
    atom_types = set_ends(jax.random.randint(seeds[2], (TOKENS,), 0, ATOMS), jax.random.fold_in(seeds[2], 1), 0, ATOMS - 1).astype(jnp.int32)
    hop_counts = set_ends(jax.random.randint(seeds[3], (TOKENS, SLOT), 0, HOPS), jax.random.fold_in(seeds[3], 1), 0, HOPS - 1).astype(jnp.int32)
    edge_types = set_ends(jax.random.randint(seeds[4], (TOKENS, SLOT), 0, EDGES), jax.random.fold_in(seeds[4], 1), 0, EDGES - 1).astype(jnp.int32)
    lengths = set_ends(jax.random.randint(seeds[5], (SLOTS,), LEN_MIN, LEN_MAX + 1), jax.random.fold_in(seeds[5], 1), LEN_MIN, LEN_MAX).astype(jnp.int32)
    branches = draw_branches(jax.random.fold_in(seeds[27], 71), 0)
    attn_gain = jnp.clip(1.0 + 0.1 * jax.random.normal(seeds[7], (D,), jnp.float32), 0.5, 1.5)
    attn_shift = gaussian(seeds[8], (D,), 0.3, 1.75, (), jnp.float32)
    qkv_weight = gaussian(seeds[9], (D, 3, D), D ** -0.5, 0.21875, ((2, 2),))
    proj_weight = gaussian(seeds[10], (D, D), (D // 16) ** -0.5, 0.875, ((0, 2),))
    ffn_gain = jnp.clip(1.0 + 0.1 * jax.random.normal(seeds[11], (D,), jnp.float32), 0.5, 1.5)
    ffn_shift = gaussian(seeds[12], (D,), 0.3, 1.75, (), jnp.float32)
    up_weight = gaussian(seeds[13], (D, FF), D ** -0.5, 0.21875, ((1, 2),))
    up_bias = gaussian(seeds[14], (FF,), 0.5, 3.0, (), jnp.float32)
    down_weight = gaussian(seeds[15], (FF, D), FF ** -0.5, 0.21875, ((0, 2),))
    down_bias = gaussian(seeds[16], (D,), 0.3, 1.75, (), jnp.float32)
    kernel_scale = jnp.clip(jax.random.uniform(seeds[17], (ATOMS, ATOMS), jnp.float32, 0.5, 1.5), 0.5, 1.5)
    kernel_shift = gaussian(seeds[18], (ATOMS, ATOMS), 0.5, 3.0, (), jnp.float32)
    centers = jnp.clip(jax.random.uniform(seeds[19], (K,), jnp.float32, 0.0, 6.0), 0.0, 6.0)
    spreads = jnp.clip(jnp.exp(jax.random.uniform(seeds[20], (K,), jnp.float32, math.log(0.5), math.log(2.0))), 0.5, 2.0)
    first_weight = gaussian(seeds[21], (K, K), (K // 8) ** -0.5, 1.5)
    first_bias = gaussian(seeds[22], (K,), 0.5, 3.0, (), jnp.float32)
    second_weight = gaussian(seeds[23], (K, H), (K // 2) ** -0.5, 0.75)
    hop_table = gaussian(seeds[24], (HOPS, H), 0.5, 3.0, (), jnp.float32)
    edge_table = gaussian(seeds[25], (EDGES, H), 0.5, 3.0, (), jnp.float32)
    cotangent = gaussian(seeds[26], (TOKENS, D), 1.0, 6.0, ((0, 32),))
    return dict(hidden_in=hidden_in, positions=positions, atom_types=atom_types, hop_counts=hop_counts, edge_types=edge_types, lengths=lengths, branches=branches, attn_gain=attn_gain, attn_shift=attn_shift, qkv_weight=qkv_weight, proj_weight=proj_weight, ffn_gain=ffn_gain, ffn_shift=ffn_shift, up_weight=up_weight, up_bias=up_bias, down_weight=down_weight, down_bias=down_bias, kernel_scale=kernel_scale, kernel_shift=kernel_shift, centers=centers, spreads=spreads, first_weight=first_weight, first_bias=first_bias, second_weight=second_weight, hop_table=hop_table, edge_table=edge_table, cotangent=cotangent)


@jax.custom_vjp
def low(v):
    return lax.optimization_barrier(v.astype(jnp.bfloat16)).astype(jnp.float32)

@jax.custom_vjp
def low_back(v):
    return v

def low_keep(v):
    return (low(v), None)

def low_pass(kept, grad):
    return (grad,)

def back_keep(v):
    return (v, None)

def back_low(kept, grad):
    return (low(grad),)
low.defvjp(low_keep, low_pass)
low_back.defvjp(back_keep, back_low)
highest = lax.Precision.HIGHEST
neg_large = -1e+30
root_tau = 2.5066282746310002

def matmul(left, right):
    return jnp.dot(left, right, precision=highest)

def layer_norm(values, gain, shift):
    row_mean = lax.optimization_barrier(jnp.mean(values, axis=-1, keepdims=True))
    centred = values - row_mean
    variance = lax.optimization_barrier(jnp.mean(centred * centred, axis=-1, keepdims=True))
    return centred * lax.rsqrt(variance + 1e-05) * gain + shift

def gelu_exact(values):
    return jax.nn.gelu(values, approximate=False)

def pair_bias(kernels, coords, atoms, hops, edges, branch):
    kernel_scale, kernel_shift, centers, spreads, first_weight, first_bias, second_weight, hop_table, edge_table = kernels
    slot_count = branch.shape[0]
    points = coords.reshape(3, slot_count, SLOT)
    offsets = points[:, :, :, None] - points[:, :, None, :]
    distance = jnp.sqrt(lax.optimization_barrier(jnp.sum(offsets * offsets, axis=0)))
    atom_kind = atoms.reshape(slot_count, SLOT)
    left_kind = atom_kind[:, :, None]
    right_kind = atom_kind[:, None, :]
    argument = kernel_scale[left_kind, right_kind] * distance + kernel_shift[left_kind, right_kind]
    standard = (argument[..., None] - centers) / spreads
    gauss = low(jnp.exp(-0.5 * standard * standard) / (root_tau * spreads)).reshape(-1, K)
    first = low_back(matmul(gauss, first_weight) + first_bias)
    second = low(gelu_exact(first))
    space_bias = matmul(second, second_weight).reshape(slot_count, SLOT, SLOT, H)
    graph_bias = hop_table[hops.reshape(slot_count, SLOT, SLOT)] + edge_table[edges.reshape(slot_count, SLOT, SLOT)]
    branch_flags = branch.astype(jnp.float32)
    return branch_flags[:, 0, None, None, None] * graph_bias + branch_flags[:, 1, None, None, None] * space_bias

def layer_block(weights, hidden, coords, atoms, hops, edges, lengths, branch):
    attn_gain, attn_shift, qkv_weight, proj_weight, ffn_gain, ffn_shift, up_weight, up_bias, down_weight, down_bias = weights[:10]
    kernels = weights[10:]
    slot_count = lengths.shape[0]
    normed = low(layer_norm(hidden, attn_gain, attn_shift))
    joined = low(low_back(matmul(normed, qkv_weight.reshape(D, 3 * D))))
    head_shape = (slot_count, SLOT, H, HD)
    queries = joined[:, :D].reshape(head_shape)
    key_rows = joined[:, D:2 * D].reshape(head_shape)
    value_rows = joined[:, 2 * D:].reshape(head_shape)
    bias = low(low_back(pair_bias(kernels, coords, atoms, hops, edges, branch)))
    scores = jnp.einsum('sihc,sjhc->shij', queries, key_rows, precision=highest) * HD ** (-0.5)
    scores = scores + jnp.transpose(bias, (0, 3, 1, 2))
    key_valid = jnp.arange(SLOT)[None, :] < lengths[:, None]
    scores = low_back(jnp.where(key_valid[:, None, None, :], scores, neg_large))
    row_max = lax.optimization_barrier(jnp.max(scores, axis=-1, keepdims=True))
    exp_scores = jnp.exp(scores - row_max)
    attn_prob = low(exp_scores / lax.optimization_barrier(jnp.sum(exp_scores, axis=-1, keepdims=True)))
    attended = jnp.einsum('shij,sjhc->sihc', attn_prob, value_rows, precision=highest).reshape(slot_count * SLOT, D)
    attended = low(low_back(attended))
    resid = hidden + low_back(matmul(attended, proj_weight))
    normed_f = low(layer_norm(resid, ffn_gain, ffn_shift))
    pre_act = low_back(matmul(normed_f, up_weight) + up_bias)
    activated = low(gelu_exact(pre_act))
    return resid + matmul(activated, down_weight) + down_bias

def reference(hidden_in, positions, atom_types, hop_counts, edge_types, lengths, branches, attn_gain, attn_shift, qkv_weight, proj_weight, ffn_gain, ffn_shift, up_weight, up_bias, down_weight, down_bias, kernel_scale, kernel_shift, centers, spreads, first_weight, first_bias, second_weight, hop_table, edge_table, cotangent):
    weights = (attn_gain.astype(jnp.float32), attn_shift.astype(jnp.float32), qkv_weight.astype(jnp.float32), proj_weight.astype(jnp.float32), ffn_gain.astype(jnp.float32), ffn_shift.astype(jnp.float32), up_weight.astype(jnp.float32), up_bias.astype(jnp.float32), down_weight.astype(jnp.float32), down_bias.astype(jnp.float32), kernel_scale.astype(jnp.float32), kernel_shift.astype(jnp.float32), centers.astype(jnp.float32), spreads.astype(jnp.float32), first_weight.astype(jnp.float32), first_bias.astype(jnp.float32), second_weight.astype(jnp.float32), hop_table.astype(jnp.float32), edge_table.astype(jnp.float32))
    block_slots = SLOTS_DEV // 2
    block_count = SLOTS // block_slots
    block_rows = block_slots * SLOT
    statics = (positions.astype(jnp.float32).reshape(3, block_count, block_rows).transpose(1, 0, 2), atom_types.reshape(block_count, block_rows), hop_counts.reshape(block_count, block_rows, SLOT), edge_types.reshape(block_count, block_rows, SLOT), lengths.reshape(block_count, block_slots), branches.reshape(block_count, block_slots, 2))

    def forward(weight_set, hidden):

        def run_block(pieces):
            return layer_block(weight_set, pieces[0], pieces[1], pieces[2], pieces[3], pieces[4], pieces[5], pieces[6])
        stacked = (hidden.reshape(block_count, block_rows, D),) + statics
        return lax.map(jax.checkpoint(run_block), stacked).reshape(TOKENS, D)
    result, pullback = jax.vjp(forward, weights, hidden_in.astype(jnp.float32))
    grad_weights, grad_hidden = pullback(cotangent.astype(jnp.float32))
    g_attn_gain, g_attn_shift, g_qkv, g_proj, g_ffn_gain, g_ffn_shift, g_up, g_up_bias, g_down, g_down_bias, g_scale, g_shift, g_centers, g_spreads, g_first, g_first_bias, g_second, g_hop, g_edge = grad_weights
    return (result.astype(jnp.bfloat16), grad_hidden.astype(jnp.bfloat16), g_attn_gain, g_attn_shift, g_qkv, g_proj, g_ffn_gain, g_ffn_shift, g_up, g_up_bias, g_down, g_down_bias, g_scale, g_shift, g_centers, g_spreads, g_first, g_first_bias, g_second, g_hop, g_edge)
```

```python
import jax
import jax.numpy as jnp
from jax import lax
from jax.experimental import pallas as pl
from jax.experimental.pallas import tpu as pltpu
from jax.sharding import PartitionSpec as P

D = 768
H = 32
HD = 24
FF = 768
K = 128
SLOT = 64
HALF = SLOT // 2
PAIRS = SLOT * SLOT
HOPS = 16
EDGES = 8
ATOMS = 16
GROUP = 4
GROUPS = H // GROUP
HOT = 32

highest = lax.Precision.HIGHEST
neg_large = -1e30
root_tau = 2.5066282746310002
root_half = 0.7071067811865476
inv_root_tau = 0.3989422804014327
head_scale = HD ** (-0.5)
VMEM_BYTES = 60 * 1024 * 1024

f32 = jnp.float32
bf16 = jnp.bfloat16


def dot_nn(left, right, precision=None):
    return lax.dot_general(left, right, (((1,), (0,)), ((), ())), precision=precision, preferred_element_type=f32)


def dot_nt(left, right, precision=None):
    return lax.dot_general(left, right, (((1,), (1,)), ((), ())), precision=precision, preferred_element_type=f32)


def dot_tn(left, right, precision=None):
    return lax.dot_general(left, right, (((0,), (0,)), ((), ())), precision=precision, preferred_element_type=f32)


def iota(shape, dim):
    return lax.broadcasted_iota(jnp.int32, shape, dim)


def gelu_parts(values):
    below = 0.5 + 0.5 * lax.erf(values * root_half)
    density = jnp.exp(-0.5 * values * values) * inv_root_tau
    return values * below, below + values * density


def to_column(row):
    size = row.shape[1]
    same = iota((size, size), 0) == iota((size, size), 1)
    return jnp.sum(jnp.where(same, row, 0.0), axis=1, keepdims=True)


def half_swap(values):
    return pltpu.roll(values, 64, 1)


def low_lanes(rows):
    return iota((rows, 128), 1) < 64


def pair_forward_kernel(
    pos_ref, atom_ref, hop_ref, edge_ref, flag_ref, scale_ref, shift_ref, cen_ref, spr_ref,
    w1_ref, b1_ref, w2_ref, hopt_ref, edget_ref,
    bias_out, arg_out, dist_out, gauss_out, second_out, slope_out, hop_out, edge_out, atom_out,
    cols, w1t, base, lhs,
):
    step = pl.program_id(0)

    @pl.when(step == 0)
    def _():
        cen = to_column(cen_ref[...])
        spr = to_column(spr_ref[...])
        cols[0] = jnp.broadcast_to(cen, (K, 128))
        cols[1] = jnp.broadcast_to(root_half / spr, (K, 128))
        cols[2] = jnp.broadcast_to(-jnp.log(root_tau * spr), (K, 128))
        cols[3] = jnp.broadcast_to(to_column(b1_ref[...]), (K, 128))
        w1t[...] = w1_ref[...].astype(f32).T.astype(bf16)
        table = jnp.concatenate([hopt_ref[...], edget_ref[...], jnp.zeros((HOT - HOPS - EDGES, H), f32)], axis=0)
        first = table.astype(bf16).astype(f32)
        second = (table - first).astype(bf16).astype(f32)
        third = table - first - second
        stack = jnp.concatenate([w2_ref[...].astype(f32), first, second, third, jnp.zeros((32, H), f32)], axis=0)
        stack = jnp.concatenate([stack, jnp.zeros((256, 128 - H), f32)], axis=1)
        base[...] = stack.T[:H]

    low = low_lanes(HALF)
    low_row = low_lanes(1)
    atoms = atom_ref[...].astype(f32)
    rows = [pos_ref[c : c + 1, :] for c in range(3)] + [atoms]
    columns = [to_column(row) for row in rows]
    hop_all = hop_ref[...].astype(f32).T
    edge_all = edge_ref[...].astype(f32).T
    for s in range(2):
        double = []
        for row in rows:
            turned = half_swap(row)
            double.append(jnp.where(low_row, row, turned) if s == 0 else jnp.where(low_row, turned, row))
        total = None
        for c in range(3):
            lo = columns[c][64 * s : 64 * s + 32]
            hi = columns[c][64 * s + 32 : 64 * s + 64]
            offset = jnp.where(low, lo, hi) - double[c]
            total = offset * offset if total is None else total + offset * offset
        distance = jnp.sqrt(total)
        key_hot = (columns[3][64 * s : 64 * s + 64] == iota((SLOT, ATOMS), 1).astype(f32)).astype(f32)
        query_hot = (double[3] == iota((ATOMS, 128), 0).astype(f32)).astype(f32)
        picked = []
        for table in (scale_ref, shift_ref):
            both = dot_nn(dot_nt(key_hot, table[...], highest), query_hot, highest)
            picked.append(jnp.where(low, both[:HALF], both[HALF:]))
        arg_out[s] = picked[0] * distance + picked[1]
        dist_out[s] = distance
        for source, target in ((hop_all, hop_out), (edge_all, edge_out)):
            top, bottom = source[:HALF], source[HALF:]
            if s == 0:
                target[s] = jnp.where(low, top, half_swap(bottom))
            else:
                target[s] = jnp.where(low, half_swap(top), bottom)
        atom_out[s] = jnp.broadcast_to(double[3], (8, 128))
        graph_on = flag_ref[2 * step + s, 0].astype(f32)
        space_on = flag_ref[2 * step + s, 1].astype(f32)
        factor = jnp.where(iota((H, 256), 1) < K, space_on, graph_on)
        lhs[s] = (base[...] * factor).astype(bf16)

    def tile(t, _):
        for s in range(2):
            r = 2 * t
            arg = jnp.concatenate([arg_out[s, pl.ds(r, 1), :], arg_out[s, pl.ds(r + 1, 1), :]], axis=1)
            hop = jnp.concatenate([hop_out[s, pl.ds(r, 1), :], hop_out[s, pl.ds(r + 1, 1), :]], axis=1)
            edge = jnp.concatenate([edge_out[s, pl.ds(r, 1), :], edge_out[s, pl.ds(r + 1, 1), :]], axis=1)

            def wide(index):
                return jnp.concatenate([cols[index], cols[index]], axis=1)

            u = (arg - wide(0)) * wide(1)
            gauss = jnp.exp(wide(2) - u * u).astype(bf16)
            where = pl.ds(pl.multiple_of(t * 256, 256), 256)
            gauss_out[s, :, where] = gauss
            first = dot_nn(w1t[...], gauss) + wide(3)
            second, slope = gelu_parts(first)
            second = second.astype(bf16)
            second_out[s, :, where] = second
            slope_out[s, :, where] = slope.astype(bf16)
            hot = jnp.concatenate(
                [
                    (hop == iota((HOPS, 256), 0).astype(f32)).astype(f32),
                    (edge == iota((HOT - HOPS, 256), 0).astype(f32)).astype(f32),
                ],
                axis=0,
            ).astype(bf16)
            bias = dot_nn(lhs[s, :, : K + 3 * HOT], jnp.concatenate([second, hot, hot, hot], axis=0))
            bias = bias.astype(bf16).astype(f32)
            bias_out[s, pl.ds(r, H, stride=HALF), :] = bias[:, :128]
            bias_out[s, pl.ds(r + 1, H, stride=HALF), :] = bias[:, 128:]
        return 0

    lax.fori_loop(0, HALF // 2, tile, 0)


def whole_spec(shape):
    return pl.BlockSpec(shape, lambda *_: (0,) * len(shape))


def pair_forward(positions, atoms, hops, edges, flags, kernels):
    scale, shift, centers, spreads, w1, b1, w2, hop_table, edge_table = kernels
    slots = flags.shape[0]
    per = lambda rows, lanes: pl.BlockSpec((2, rows, lanes), lambda g: (g, 0, 0))
    out = lambda rows, lanes, kind: jax.ShapeDtypeStruct((slots, rows, lanes), kind)
    return pl.pallas_call(
        pair_forward_kernel,
        grid=(slots // 2,),
        in_specs=[
            pl.BlockSpec((3, 128), lambda g: (0, g)),
            pl.BlockSpec((1, 128), lambda g: (0, g)),
            pl.BlockSpec((128, SLOT), lambda g: (g, 0)),
            pl.BlockSpec((128, SLOT), lambda g: (g, 0)),
            pl.BlockSpec(memory_space=pltpu.SMEM),
            whole_spec((ATOMS, ATOMS)),
            whole_spec((ATOMS, ATOMS)),
            whole_spec((1, K)),
            whole_spec((1, K)),
            whole_spec((K, K)),
            whole_spec((1, K)),
            whole_spec((K, H)),
            whole_spec((HOPS, H)),
            whole_spec((EDGES, H)),
        ],
        out_specs=[
            per(H * HALF, 128), per(HALF, 128), per(HALF, 128), per(K, PAIRS), per(K, PAIRS), per(K, PAIRS),
            per(HALF, 128), per(HALF, 128), per(8, 128),
        ],
        out_shape=[
            out(H * HALF, 128, f32), out(HALF, 128, f32), out(HALF, 128, f32), out(K, PAIRS, bf16),
            out(K, PAIRS, bf16), out(K, PAIRS, bf16), out(HALF, 128, f32), out(HALF, 128, f32), out(8, 128, f32),
        ],
        scratch_shapes=[
            pltpu.VMEM((4, K, 128), f32),
            pltpu.VMEM((K, K), bf16),
            pltpu.VMEM((H, 256), f32),
            pltpu.VMEM((2, H, 256), bf16),
        ],
        compiler_params=pltpu.CompilerParams(vmem_limit_bytes=VMEM_BYTES),
        name="pair_forward",
    )(
        positions, atoms.reshape(1, -1), hops, edges, flags, scale, shift, centers.reshape(1, K),
        spreads.reshape(1, K), w1, b1.reshape(1, K), w2, hop_table, edge_table,
    )


def pair_backward_kernel(
    dbias_ref, arg_ref, dist_ref, gauss_ref, second_ref, slope_ref, hop_ref, edge_ref, atom_ref, flag_ref,
    cen_ref, spr_ref, w1_ref, w2_ref,
    mixed_out, kern_out, table_out,
    cols, dfirst, dspace, dargs, hots, sums,
):
    slot = pl.program_id(0)

    @pl.when(slot == 0)
    def _():
        spr = to_column(spr_ref[...])
        cols[0] = jnp.broadcast_to(to_column(cen_ref[...]), (K, 128))
        cols[1] = jnp.broadcast_to(1.0 / spr, (K, 128))
        sums[...] = jnp.zeros_like(sums)
        mixed_out[...] = jnp.zeros_like(mixed_out)
        table_out[...] = jnp.zeros_like(table_out)

    graph_on = flag_ref[slot, 0].astype(f32)
    space_on = flag_ref[slot, 1].astype(f32)
    w2 = (w2_ref[...].astype(f32) * space_on).astype(bf16)

    def tile(t, carry):
        r = 2 * t
        two = lambda ref: jnp.concatenate([ref[0, pl.ds(r, 1), :], ref[0, pl.ds(r + 1, 1), :]], axis=1)
        wide = lambda index: jnp.concatenate([cols[index], cols[index]], axis=1)
        where = pl.ds(pl.multiple_of(t * 256, 256), 256)
        grad = jnp.concatenate(
            [dbias_ref[0, pl.ds(r, H, stride=HALF), :], dbias_ref[0, pl.ds(r + 1, H, stride=HALF), :]], axis=1
        )
        dspace[:, where] = jnp.concatenate([grad * space_on, grad * graph_on], axis=0).astype(bf16)
        d_second = dot_nn(w2, grad.astype(bf16))
        d_first = (d_second * slope_ref[0, :, where].astype(f32)).astype(bf16)
        dfirst[:, where] = d_first
        d_gauss = dot_nn(w1_ref[...], d_first)
        inv = wide(1)
        u = (two(arg_ref) - wide(0)) * inv
        q = d_gauss * gauss_ref[0, :, where].astype(f32)
        w = q * u
        sums[0] += w[:, :128] + w[:, 128:]
        extra = w * u - q
        sums[1] += extra[:, :128] + extra[:, 128:]
        darg = -jnp.sum(w * inv, axis=0, keepdims=True)
        dargs[pl.ds(r, 1), :] = darg[:, :128]
        dargs[pl.ds(r + 1, 1), :] = darg[:, 128:]
        hop, edge = two(hop_ref), two(edge_ref)
        edge_hot = (edge == iota((HOT - HOPS, 256), 0).astype(f32)).astype(f32)
        edge_hot = jnp.where(iota((HOT - HOPS, 256), 0) == EDGES, 1.0, edge_hot)
        hots[:, where] = jnp.concatenate(
            [(hop == iota((HOPS, 256), 0).astype(f32)).astype(f32), edge_hot], axis=0
        ).astype(bf16)
        return carry

    lax.fori_loop(0, HALF // 2, tile, 0)
    left = jnp.concatenate([gauss_ref[0], second_ref[0], hots[...]], axis=0)
    right = jnp.concatenate([dfirst[...], dspace[...]], axis=0)
    mixed_out[...] += dot_nt(left, right)
    low = low_lanes(ATOMS)
    query_hot = (atom_ref[0, 0:1, :] == iota((ATOMS, 128), 0).astype(f32)).astype(f32)
    for index in range(2):
        values = dargs[...] * dist_ref[0] if index == 0 else dargs[...]
        part = jnp.where(
            low,
            dot_nn(query_hot[:, :HALF], values, highest),
            dot_nn(query_hot[:, HALF:SLOT], values, highest),
        )
        table_out[index] += dot_nt(query_hot, part, highest)

    @pl.when(slot == pl.num_programs(0) - 1)
    def _():
        kern_out[...] = jnp.sum(sums[...] * cols[1], axis=2, keepdims=True) + jnp.zeros((2, K, 128), f32)


def pair_backward(dbias, kept, flags, kernels):
    scale, shift, centers, spreads, w1, b1, w2, hop_table, edge_table = kernels
    arg, dist, gauss, second, slope, hop, edge, atom = kept
    slots = flags.shape[0]
    per = lambda rows, lanes: pl.BlockSpec((1, rows, lanes), lambda g: (g, 0, 0))
    mixed, kern, table = pl.pallas_call(
        pair_backward_kernel,
        grid=(slots,),
        in_specs=[
            per(H * HALF, 128), per(HALF, 128), per(HALF, 128), per(K, PAIRS), per(K, PAIRS), per(K, PAIRS),
            per(HALF, 128), per(HALF, 128), per(8, 128), pl.BlockSpec(memory_space=pltpu.SMEM),
            whole_spec((1, K)), whole_spec((1, K)), whole_spec((K, K)), whole_spec((K, H)),
        ],
        out_specs=[whole_spec((2 * K + HOT, K + 2 * H)), whole_spec((2, K, 128)), whole_spec((2, ATOMS, ATOMS))],
        out_shape=[
            jax.ShapeDtypeStruct((2 * K + HOT, K + 2 * H), f32),
            jax.ShapeDtypeStruct((2, K, 128), f32),
            jax.ShapeDtypeStruct((2, ATOMS, ATOMS), f32),
        ],
        scratch_shapes=[
            pltpu.VMEM((2, K, 128), f32),
            pltpu.VMEM((K, PAIRS), bf16),
            pltpu.VMEM((2 * H, PAIRS), bf16),
            pltpu.VMEM((HALF, 128), f32),
            pltpu.VMEM((HOT, PAIRS), bf16),
            pltpu.VMEM((2, K, 128), f32),
        ],
        compiler_params=pltpu.CompilerParams(vmem_limit_bytes=VMEM_BYTES),
        name="pair_backward",
    )(dbias, arg, dist, gauss, second, slope, hop, edge, atom, flags, centers.reshape(1, K), spreads.reshape(1, K), w1, w2)
    grad_first = mixed[:K, :K]
    grad_second = mixed[K : 2 * K, K : K + H]
    grad_hop = mixed[2 * K : 2 * K + HOPS, K + H :]
    grad_edge = mixed[2 * K + HOPS : 2 * K + HOPS + EDGES, K + H :]
    grad_first_bias = mixed[2 * K + HOPS + EDGES, :K]
    return (
        table[0], table[1], kern[0, :, 0], kern[1, :, 0], grad_first, grad_first_bias, grad_second, grad_hop, grad_edge,
    )


def window(group):
    first = GROUP * HD * group
    start = first // 128 * 128
    width = 128 if first - start + GROUP * HD <= 128 else 256
    return start, width, first - start


def head_masks(group, kind):
    _, width, offset = window(group)
    lane = iota((1, width), 1)
    return [
        ((lane >= offset + HD * h) & (lane < offset + HD * (h + 1))).astype(f32).astype(kind) for h in range(GROUP)
    ]


def spread_heads(values, group):
    return jnp.concatenate([values * mask for mask in head_masks(group, bf16)], axis=0)


def gather_heads(values, group):
    masks = head_masks(group, f32)
    total = values[:SLOT] * masks[0]
    for h in range(1, GROUP):
        total = total + values[SLOT * h : SLOT * (h + 1)] * masks[h]
    return total


def standardize(values):
    centred = values - jnp.mean(values, axis=-1, keepdims=True)
    inv_std = lax.rsqrt(jnp.mean(centred * centred, axis=-1, keepdims=True) + 1e-05)
    return centred * inv_std, inv_std


def norm_back(d_normed, scaled, inv_std, gain):
    weighted = d_normed * gain
    inner_a = jnp.mean(weighted, axis=-1, keepdims=True)
    inner_b = jnp.mean(weighted * scaled, axis=-1, keepdims=True)
    return inv_std * (weighted - inner_a - scaled * inner_b)


def column_sum(values):
    return jnp.sum(values, axis=0, keepdims=True)


def forward_kernel(
    len_ref, hidden_ref, cot_ref, bias_ref, wqkv_ref, proj_ref, up_ref, down_ref,
    ag_ref, as_ref, fg_ref, fs_ref, ub_ref, db_ref,
    output_ref, normed_ref, joined_ref, prob_ref, datt_ref, dresid_ref, gdown_ref, gup_ref, gproj_ref, small_ref,
    mixed, attended, normed_f, activated, d_pre, d_branch,
):
    tokens = hidden_ref.shape[0]
    slots = tokens // SLOT
    chunk = min(256, tokens)
    first_slot = lax.axis_index("tp") * slots

    def project(c, _):
        rows = pl.ds(pl.multiple_of(c * chunk, chunk), chunk)
        scaled, _unused = standardize(hidden_ref[rows, :].astype(f32))
        normed = (scaled * ag_ref[...] + as_ref[...]).astype(bf16)
        normed_ref[rows, :] = normed
        for m in range(3):
            joined_ref[rows, m * D : (m + 1) * D] = dot_nn(normed, wqkv_ref[:, m * D : (m + 1) * D]).astype(bf16)
        return 0

    lax.fori_loop(0, tokens // chunk, project, 0)
    low = low_lanes(HALF)

    def attend(s, _):
        rows = pl.ds(pl.multiple_of(s * SLOT, SLOT), SLOT)
        length = len_ref[first_slot + s]
        valid = iota((SLOT, GROUP * SLOT), 0) < length
        mixed[...] = jnp.zeros_like(mixed)
        for g in range(GROUPS):
            start, width, _offset = window(g)
            q = joined_ref[rows, start : start + width]
            k = joined_ref[rows, D + start : D + start + width]
            v = joined_ref[rows, 2 * D + start : 2 * D + start + width]
            scores = dot_nt(k, spread_heads(q, g)) * head_scale
            parts = []
            for pair in range(GROUP // 2):
                head = GROUP * g + 2 * pair
                one = bias_ref[s, head * HALF : (head + 1) * HALF, :]
                two = bias_ref[s, (head + 1) * HALF : (head + 2) * HALF, :]
                top = jnp.where(low, one, half_swap(two))
                bottom = jnp.where(low, half_swap(one), two)
                parts.append(jnp.concatenate([top, bottom], axis=0))
            scores = jnp.where(valid, scores + jnp.concatenate(parts, axis=1), neg_large)
            weights = jnp.exp(scores - jnp.max(scores, axis=0, keepdims=True))
            prob = (weights * (1.0 / jnp.sum(weights, axis=0, keepdims=True))).astype(bf16)
            prob_ref[s, :, g * GROUP * SLOT : (g + 1) * GROUP * SLOT] = prob
            mixed[:, start : start + width] += gather_heads(dot_tn(prob, v), g)
        attended[rows, :] = mixed[...].astype(bf16)
        return 0

    lax.fori_loop(0, slots, attend, 0)
    small_ref[...] = jnp.zeros_like(small_ref)

    def feed(c, _):
        rows = pl.ds(pl.multiple_of(c * chunk, chunk), chunk)
        resid = hidden_ref[rows, :].astype(f32) + dot_nn(attended[rows, :], proj_ref[...])
        scaled, inv_std = standardize(resid)
        normed = (scaled * fg_ref[...] + fs_ref[...]).astype(bf16)
        normed_f[rows, :] = normed
        value, slope = gelu_parts(dot_nn(normed, up_ref[...]) + ub_ref[...])
        active = value.astype(bf16)
        activated[rows, :] = active
        output_ref[rows, :] = (resid + dot_nn(active, down_ref[...]) + db_ref[...]).astype(bf16)
        cot = cot_ref[rows, :]
        cot_wide = cot.astype(f32)
        d_hidden = (dot_nt(cot, down_ref[...]) * slope).astype(bf16)
        d_pre[rows, :] = d_hidden
        d_normed = dot_nt(d_hidden, up_ref[...])
        d_resid = cot_wide + norm_back(d_normed, scaled, inv_std, fg_ref[...])
        dresid_ref[rows, :] = d_resid
        branch = d_resid.astype(bf16)
        d_branch[rows, :] = branch
        datt_ref[rows, :] = dot_nt(branch, proj_ref[...]).astype(bf16)
        small_ref[0:1, :] += column_sum(d_normed * scaled)
        small_ref[1:2, :] += column_sum(d_normed)
        small_ref[2:3, :] += column_sum(d_hidden.astype(f32))
        small_ref[3:4, :] += column_sum(cot_wide)
        return 0

    lax.fori_loop(0, tokens // chunk, feed, 0)
    for part in range(3):
        cols = slice(256 * part, 256 * (part + 1))
        gdown_ref[cols, :] = dot_tn(activated[:, cols], cot_ref[...]).astype(bf16)
        gup_ref[cols, :] = dot_tn(normed_f[:, cols], d_pre[...]).astype(bf16)
        gproj_ref[cols, :] = dot_tn(attended[:, cols], d_branch[...]).astype(bf16)


def vmem(count):
    return [pl.BlockSpec(memory_space=pltpu.VMEM)] * count


def layer_forward(lengths, hidden, cot, bias, wqkv, proj, up, down, vectors):
    tokens = hidden.shape[0]
    slots = tokens // SLOT
    shape = jax.ShapeDtypeStruct
    return pl.pallas_call(
        forward_kernel,
        in_specs=[pl.BlockSpec(memory_space=pltpu.SMEM)] + vmem(13),
        out_specs=vmem(10),
        out_shape=[
            shape((tokens, D), bf16), shape((tokens, D), bf16), shape((tokens, 3 * D), bf16),
            shape((slots, SLOT, H * SLOT), bf16), shape((tokens, D), bf16), shape((tokens, D), f32),
            shape((FF, D), bf16), shape((D, FF), bf16), shape((D, D), bf16), shape((8, D), f32),
        ],
        scratch_shapes=[pltpu.VMEM((SLOT, D), f32)] + [pltpu.VMEM((tokens, D), bf16)] * 5,
        compiler_params=pltpu.CompilerParams(vmem_limit_bytes=VMEM_BYTES),
        name="layer_forward",
    )(lengths, hidden, cot, bias, wqkv, proj, up, down, *[v.reshape(1, -1) for v in vectors])


def backward_kernel(
    hidden_ref, joined_ref, prob_ref, datt_ref, dresid_ref, normed_ref, wqkv_ref, gain_ref,
    ginput_ref, gqkv_ref, dbias_ref, small_ref,
    d_joined, dq, dk, dv,
):
    tokens = hidden_ref.shape[0]
    slots = tokens // SLOT
    chunk = min(256, tokens)
    low = low_lanes(HALF)

    def attend_back(s, _):
        rows = pl.ds(pl.multiple_of(s * SLOT, SLOT), SLOT)
        dq[...] = jnp.zeros_like(dq)
        dk[...] = jnp.zeros_like(dk)
        dv[...] = jnp.zeros_like(dv)
        for g in range(GROUPS):
            start, width, _offset = window(g)
            lanes = slice(start, start + width)
            k = joined_ref[rows, D + start : D + start + width]
            v = joined_ref[rows, 2 * D + start : 2 * D + start + width]
            q_heads = spread_heads(joined_ref[rows, lanes], g)
            d_heads = spread_heads(datt_ref[rows, lanes], g)
            prob = prob_ref[s, :, g * GROUP * SLOT : (g + 1) * GROUP * SLOT]
            wide = prob.astype(f32)
            d_prob = dot_nt(v, d_heads)
            inner = jnp.sum(wide * d_prob, axis=0, keepdims=True)
            d_scores = (wide * (d_prob - inner)).astype(bf16)
            dv[:, lanes] += dot_nn(prob, d_heads)
            dk[:, lanes] += dot_nn(d_scores, q_heads)
            dq[:, lanes] += gather_heads(dot_tn(d_scores, k), g)
            d_wide = d_scores.astype(f32)
            for pair in range(GROUP // 2):
                head = GROUP * g + 2 * pair
                top = d_wide[:HALF, 128 * pair : 128 * (pair + 1)]
                bottom = d_wide[HALF:, 128 * pair : 128 * (pair + 1)]
                dbias_ref[s, head * HALF : (head + 1) * HALF, :] = jnp.where(low, top, half_swap(bottom))
                dbias_ref[s, (head + 1) * HALF : (head + 2) * HALF, :] = jnp.where(low, half_swap(top), bottom)
        d_joined[rows, 0:D] = (dq[...] * head_scale).astype(bf16)
        d_joined[rows, D : 2 * D] = (dk[...] * head_scale).astype(bf16)
        d_joined[rows, 2 * D : 3 * D] = dv[...].astype(bf16)
        return 0

    lax.fori_loop(0, slots, attend_back, 0)
    for part in range(3):
        cols = slice(256 * part, 256 * (part + 1))
        gqkv_ref[cols, :] = dot_tn(normed_ref[:, cols], d_joined[...]).astype(bf16)
    small_ref[...] = jnp.zeros_like(small_ref)

    def finish(c, _):
        rows = pl.ds(pl.multiple_of(c * chunk, chunk), chunk)
        d_normed = dot_nt(d_joined[rows, :], wqkv_ref[...])
        scaled, inv_std = standardize(hidden_ref[rows, :].astype(f32))
        grad = dresid_ref[rows, :] + norm_back(d_normed, scaled, inv_std, gain_ref[...])
        ginput_ref[rows, :] = grad.astype(bf16)
        small_ref[0:1, :] += column_sum(d_normed * scaled)
        small_ref[1:2, :] += column_sum(d_normed)
        return 0

    lax.fori_loop(0, tokens // chunk, finish, 0)


def layer_backward(hidden, joined, prob, datt, dresid, normed, wqkv, gain):
    tokens = hidden.shape[0]
    slots = tokens // SLOT
    shape = jax.ShapeDtypeStruct
    return pl.pallas_call(
        backward_kernel,
        in_specs=vmem(8),
        out_specs=vmem(4),
        out_shape=[
            shape((tokens, D), bf16), shape((D, 3 * D), bf16), shape((slots, H * HALF, 128), f32), shape((8, D), f32),
        ],
        scratch_shapes=[pltpu.VMEM((tokens, 3 * D), bf16)] + [pltpu.VMEM((SLOT, D), f32)] * 3,
        compiler_params=pltpu.CompilerParams(vmem_limit_bytes=VMEM_BYTES),
        name="layer_backward",
    )(hidden, joined, prob, datt, dresid, normed, wqkv, gain.reshape(1, -1))


def body(
    hidden_in, positions, atom_types, hop_counts, edge_types, lengths, branches,
    attn_gain, attn_shift, qkv_weight, proj_weight, ffn_gain, ffn_shift, up_weight, up_bias, down_weight, down_bias,
    kernel_scale, kernel_shift, centers, spreads, first_weight, first_bias, second_weight, hop_table, edge_table,
    cotangent,
):
    kernels = (
        kernel_scale, kernel_shift, centers, spreads, first_weight, first_bias, second_weight, hop_table, edge_table,
    )
    wqkv = lax.all_gather(qkv_weight, "tp", axis=2, tiled=True).reshape(D, 3 * D)
    proj = lax.all_gather(proj_weight, "tp", axis=0, tiled=True)
    up = lax.all_gather(up_weight, "tp", axis=1, tiled=True)
    down = lax.all_gather(down_weight, "tp", axis=0, tiled=True)
    bias, *kept = pair_forward(positions, atom_types, hop_counts, edge_types, branches, kernels)
    output, normed, joined, prob, datt, dresid, g_down, g_up, g_proj, small_f = layer_forward(
        lengths, hidden_in, cotangent, bias, wqkv, proj, up, down,
        (attn_gain, attn_shift, ffn_gain, ffn_shift, up_bias, down_bias),
    )
    grad_input, g_qkv, dbias, small_a = layer_backward(
        hidden_in, joined, prob, datt, dresid, normed, wqkv, attn_gain
    )
    pair_grads = pair_backward(dbias, kept, branches, kernels)

    def reduce(grad, dim):
        part = lax.psum_scatter(grad, "tp", scatter_dimension=dim, tiled=True)
        return lax.psum(part, "mol").astype(f32)

    grad_down = reduce(g_down, 0)
    grad_up = reduce(g_up, 1)
    grad_proj = reduce(g_proj, 0)
    grad_qkv = reduce(g_qkv.reshape(D, 3, D), 2)
    small = (small_a[0], small_a[1], small_f[0], small_f[1], small_f[2], small_f[3]) + pair_grads
    sizes = [v.size for v in small]
    flat = lax.psum(jnp.concatenate([v.reshape(-1) for v in small]), ("mol", "tp"))
    parts = []
    at = 0
    for value, size in zip(small, sizes):
        parts.append(flat[at : at + size].reshape(value.shape))
        at += size
    (
        grad_attn_gain, grad_attn_shift, grad_ffn_gain, grad_ffn_shift, grad_up_bias, grad_down_bias,
        grad_scale, grad_shift, grad_centers, grad_spreads, grad_first, grad_first_bias, grad_second,
        grad_hop, grad_edge,
    ) = parts
    return (
        output, grad_input, grad_attn_gain, grad_attn_shift, grad_qkv, grad_proj, grad_ffn_gain, grad_ffn_shift,
        grad_up, grad_up_bias, grad_down, grad_down_bias, grad_scale, grad_shift, grad_centers, grad_spreads,
        grad_first, grad_first_bias, grad_second, grad_hop, grad_edge,
    )


def solution(mesh):
    rows = P(("mol", "tp"), None)
    all_of = P()
    in_specs = (
        rows, P(None, ("mol", "tp")), P(("mol", "tp")), rows, rows, P("mol"), rows, all_of, all_of,
        P(None, None, "tp"), P("tp", None), all_of, all_of, P(None, "tp"), all_of, P("tp", None),
    ) + (all_of,) * 10 + (rows,)
    out_specs = (
        rows, rows, all_of, all_of, P(None, None, "tp"), P("tp", None), all_of, all_of, P(None, "tp"), all_of,
        P("tp", None),
    ) + (all_of,) * 10
    return jax.shard_map(body, mesh=mesh, in_specs=in_specs, out_specs=out_specs, check_vma=False)
```

```python
import functools

import jax
import jax.numpy as jnp
from jax import lax
from jax.experimental import pallas as pl
from jax.experimental.pallas import tpu as pltpu
from jax.sharding import PartitionSpec as P

D = 768
H = 32
HD = 24
FF = 768
K = 128
SLOT = 64
HALF = SLOT // 2
HALF_D = D // 2
PAIRS = SLOT * SLOT
HOPS = 16
EDGES = 8
ATOMS = 16
GROUP = 4
GROUPS = H // GROUP
HOT = 32

highest = lax.Precision.HIGHEST
neg_large = -1e30
root_tau = 2.5066282746310002
root_half = 0.7071067811865476
inv_root_tau = 0.3989422804014327
head_scale = HD ** (-0.5)
VMEM_BYTES = 60 * 1024 * 1024

MESH = pl.DeviceIdType.MESH
f32 = jnp.float32
bf16 = jnp.bfloat16


def dot_nn(left, right, precision=None):
    return lax.dot_general(left, right, (((1,), (0,)), ((), ())), precision=precision, preferred_element_type=f32)


def dot_nt(left, right, precision=None):
    return lax.dot_general(left, right, (((1,), (1,)), ((), ())), precision=precision, preferred_element_type=f32)


def dot_tn(left, right, precision=None):
    return lax.dot_general(left, right, (((0,), (0,)), ((), ())), precision=precision, preferred_element_type=f32)


def iota(shape, dim):
    return lax.broadcasted_iota(jnp.int32, shape, dim)


def gelu_parts(values):
    below = 0.5 + 0.5 * lax.erf(values * root_half)
    density = jnp.exp(-0.5 * values * values) * inv_root_tau
    return values * below, below + values * density


def to_column(row):
    size = row.shape[1]
    same = iota((size, size), 0) == iota((size, size), 1)
    return jnp.sum(jnp.where(same, row, 0.0), axis=1, keepdims=True)


def half_swap(values):
    return pltpu.roll(values, 64, 1)


def low_lanes(rows):
    return iota((rows, 128), 1) < 64


def place():
    mol = lax.axis_index("mol")
    return mol % 2, (mol // 2) % 2, mol // 4, lax.axis_index("tp")


def greet(peers):
    barrier = pltpu.get_barrier_semaphore()
    for peer in peers:
        pl.semaphore_signal(barrier, inc=1, device_id=peer, device_id_type=MESH)
    pl.semaphore_wait(barrier, len(peers))


class Gather:
    def __init__(self, own, whole, sends, recvs, locals_):
        self.own, self.whole, self.sends, self.recvs, self.locals_ = own, whole, sends, recvs, locals_
        self.core, self.x, z, self.tp = place()
        mol = lax.axis_index("mol")
        self.over_tp = {"tp": 1 - self.tp}
        self.over_x = {"mol": mol + 2 - 4 * self.x}
        self.over_core = {"mol": mol + 1 - 2 * self.core}

    def rows(self, ref, quarter):
        count = ref.shape[-2] // 4
        return pl.ds(pl.multiple_of(quarter * count, count), count)

    def part(self, index, quarter):
        ref = self.whole[index].at[1 - self.tp]
        return ref.at[..., self.rows(ref, quarter), :]

    def copy(self, index, kind):
        quarter = self.x * 2 + self.core
        if kind == 0:
            own = self.own[index]
            src = own.at[..., self.rows(own, quarter), :]
            ref = self.whole[index].at[self.tp]
            dst, peer = ref.at[..., self.rows(ref, quarter), :], self.over_tp
        elif kind == 1:
            src = dst = self.part(index, quarter)
            peer = self.over_x
        else:
            src = dst = self.part(index, quarter if kind == 2 else (1 - self.x) * 2 + self.core)
            peer = self.over_core
        return pltpu.make_async_remote_copy(
            src_ref=src, dst_ref=dst, send_sem=self.sends.at[index, kind], recv_sem=self.recvs.at[index, kind],
            device_id=peer, device_id_type=MESH,
        )

    def local(self, index):
        return pltpu.make_async_copy(self.own[index], self.whole[index].at[self.tp], self.locals_.at[index])

    def start(self):
        greet([self.over_tp, self.over_x, self.over_core])
        for index in range(4):
            self.copy(index, 0).start()
        for index in range(4):
            self.local(index).start()

    def onward_x(self, index):
        self.copy(index, 0).wait_recv()
        self.copy(index, 1).start()
        self.copy(index, 2).start()

    def onward_core(self, index):
        self.copy(index, 1).wait_recv()
        self.copy(index, 3).start()

    def finish(self):
        for index in range(4):
            self.local(index).wait()
            self.copy(index, 2).wait_recv()
            self.copy(index, 3).wait_recv()
            for kind in range(4):
                self.copy(index, kind).wait_send()


def pair_forward_kernel(remote, *refs):
    (
        pos_ref, atom_ref, hop_ref, edge_ref, flag_ref, scale_ref, shift_ref, cen_ref, spr_ref,
        w1_ref, b1_ref, w2_ref, hopt_ref, edget_ref,
    ) = refs[:14]
    refs = refs[14:]
    if remote:
        own, refs = refs[:4], refs[4:]
    bias_out, arg_out, dist_out, gauss_out, second_out, slope_out, hop_out, edge_out, atom_out = refs[:9]
    refs = refs[9:]
    if remote:
        whole, refs = refs[:4], refs[4:]
    cols, w1t, base, lhs = refs[:4]
    step = pl.program_id(0)
    if remote:
        gather = Gather(own, whole, *refs[4:])
        pl.when(step == 0)(gather.start)

        @pl.when(step == 1)
        def _():
            gather.onward_x(0)

        @pl.when(step == 2)
        def _():
            for index in range(1, 4):
                gather.onward_x(index)
            gather.onward_core(0)

        @pl.when(step == 3)
        def _():
            for index in range(1, 4):
                gather.onward_core(index)

    @pl.when(step == 0)
    def _():
        cen = to_column(cen_ref[...].reshape(1, K))
        spr = to_column(spr_ref[...].reshape(1, K))
        cols[0] = jnp.broadcast_to(cen, (K, 128))
        cols[1] = jnp.broadcast_to(root_half / spr, (K, 128))
        cols[2] = jnp.broadcast_to(-jnp.log(root_tau * spr), (K, 128))
        cols[3] = jnp.broadcast_to(to_column(b1_ref[...].reshape(1, K)), (K, 128))
        w1t[...] = w1_ref[...].astype(f32).T.astype(bf16)
        table = jnp.concatenate([hopt_ref[...], edget_ref[...], jnp.zeros((128 - HOPS - EDGES, H), f32)], axis=0)
        table = jnp.concatenate([table, jnp.zeros((128, 128 - H), f32)], axis=1).T[:H, :HOT]
        first = table.astype(bf16).astype(f32)
        second = (table - first).astype(bf16).astype(f32)
        third = table - first - second
        base[...] = jnp.concatenate([w2_ref[...].astype(f32), first, second, third, jnp.zeros((H, 32), f32)], axis=1)

    low = low_lanes(HALF)
    low_row = low_lanes(1)
    atoms = atom_ref[...].astype(f32).reshape(1, 128)
    rows = [pos_ref[c : c + 1, :] for c in range(3)] + [atoms]
    columns = [to_column(row) for row in rows]
    hop_all = hop_ref[...].astype(f32)
    edge_all = edge_ref[...].astype(f32)
    for s in range(2):
        double = []
        for row in rows:
            turned = half_swap(row)
            double.append(jnp.where(low_row, row, turned) if s == 0 else jnp.where(low_row, turned, row))
        total = None
        for c in range(3):
            lo = columns[c][64 * s : 64 * s + 32]
            hi = columns[c][64 * s + 32 : 64 * s + 64]
            offset = jnp.where(low, lo, hi) - double[c]
            total = offset * offset if total is None else total + offset * offset
        distance = jnp.sqrt(total)
        key_hot = (columns[3][64 * s : 64 * s + 64] == iota((SLOT, ATOMS), 1).astype(f32)).astype(f32)
        query_hot = (double[3] == iota((ATOMS, 128), 0).astype(f32)).astype(f32)
        picked = []
        for table in (scale_ref, shift_ref):
            both = dot_nn(dot_nt(key_hot, table[...], highest), query_hot, highest)
            picked.append(jnp.where(low, both[:HALF], both[HALF:]))
        arg_out[s] = picked[0] * distance + picked[1]
        dist_out[s] = distance
        for source, target in ((hop_all, hop_out), (edge_all, edge_out)):
            top, bottom = source[:HALF], source[HALF:]
            if s == 0:
                target[s] = jnp.where(low, top, half_swap(bottom))
            else:
                target[s] = jnp.where(low, half_swap(top), bottom)
        atom_out[s] = jnp.broadcast_to(double[3], (8, 128))
        graph_on = flag_ref[0, 2 * step + s].astype(f32)
        space_on = flag_ref[1, 2 * step + s].astype(f32)
        factor = jnp.where(iota((H, 256), 1) < K, space_on, graph_on)
        lhs[s] = (base[...] * factor).astype(bf16)

    def tile(t, _):
        for s in range(2):
            r = 2 * t
            arg = jnp.concatenate([arg_out[s, pl.ds(r, 1), :], arg_out[s, pl.ds(r + 1, 1), :]], axis=1)
            hop = jnp.concatenate([hop_out[s, pl.ds(r, 1), :], hop_out[s, pl.ds(r + 1, 1), :]], axis=1)
            edge = jnp.concatenate([edge_out[s, pl.ds(r, 1), :], edge_out[s, pl.ds(r + 1, 1), :]], axis=1)

            def wide(index):
                return jnp.concatenate([cols[index], cols[index]], axis=1)

            u = (arg - wide(0)) * wide(1)
            gauss = jnp.exp(wide(2) - u * u).astype(bf16)
            where = pl.ds(pl.multiple_of(t * 256, 256), 256)
            gauss_out[s, :, where] = gauss
            first = dot_nn(w1t[...], gauss) + wide(3)
            second, slope = gelu_parts(first)
            second = second.astype(bf16)
            second_out[s, :, where] = second
            slope_out[s, :, where] = slope.astype(bf16)
            hot = jnp.concatenate(
                [
                    (hop == iota((HOPS, 256), 0).astype(f32)).astype(f32),
                    (edge == iota((HOT - HOPS, 256), 0).astype(f32)).astype(f32),
                ],
                axis=0,
            ).astype(bf16)
            bias = dot_nn(lhs[s, :, : K + 3 * HOT], jnp.concatenate([second, hot, hot, hot], axis=0))
            bias = bias.astype(bf16).astype(f32)
            bias_out[s, pl.ds(r, H, stride=HALF), :] = bias[:, :128]
            bias_out[s, pl.ds(r + 1, H, stride=HALF), :] = bias[:, 128:]
        return 0

    lax.fori_loop(0, HALF // 2, tile, 0)
    if remote:
        pl.when(step == pl.num_programs(0) - 1)(gather.finish)


def whole_spec(shape):
    return pl.BlockSpec(shape, lambda *_: (0,) * len(shape))


def pair_forward(positions, atoms, hops, edges, flags, kernels, weights=None):
    scale, shift, centers, spreads, w1, b1, w2, hop_table, edge_table = kernels
    slots = flags.shape[0]
    per = lambda rows, lanes: pl.BlockSpec((2, rows, lanes), lambda g: (g, 0, 0))
    out = lambda rows, lanes, kind: jax.ShapeDtypeStruct((slots, rows, lanes), kind)
    remote = weights is not None
    anywhere = [pl.BlockSpec(memory_space=pl.ANY)] * (4 if remote else 0)
    weights = weights if remote else ()
    copies = [pltpu.SemaphoreType.DMA((4, 4))] * 2 + [pltpu.SemaphoreType.DMA((4,))] if remote else []
    results = pl.pallas_call(
        functools.partial(pair_forward_kernel, remote),
        grid=(slots // 2,),
        in_specs=[
            pl.BlockSpec((3, 128), lambda g: (0, g)),
            pl.BlockSpec((128,), lambda g: (g,)),
            pl.BlockSpec((SLOT, 128), lambda g: (0, g)),
            pl.BlockSpec((SLOT, 128), lambda g: (0, g)),
            pl.BlockSpec(memory_space=pltpu.SMEM),
            whole_spec((ATOMS, ATOMS)),
            whole_spec((ATOMS, ATOMS)),
            whole_spec((K,)),
            whole_spec((K,)),
            whole_spec((K, K)),
            whole_spec((K,)),
            whole_spec((H, K)),
            whole_spec((HOPS, H)),
            whole_spec((EDGES, H)),
        ] + anywhere,
        out_specs=[
            per(H * HALF, 128), per(HALF, 128), per(HALF, 128), per(K, PAIRS), per(K, PAIRS), per(K, PAIRS),
            per(HALF, 128), per(HALF, 128), per(8, 128),
        ] + anywhere,
        out_shape=[
            out(H * HALF, 128, f32), out(HALF, 128, f32), out(HALF, 128, f32), out(K, PAIRS, bf16),
            out(K, PAIRS, bf16), out(K, PAIRS, bf16), out(HALF, 128, f32), out(HALF, 128, f32), out(8, 128, f32),
        ] + [jax.ShapeDtypeStruct((2,) + w.shape, bf16) for w in weights],
        scratch_shapes=[
            pltpu.VMEM((4, K, 128), f32),
            pltpu.VMEM((K, K), bf16),
            pltpu.VMEM((H, 256), f32),
            pltpu.VMEM((2, H, 256), bf16),
        ] + copies,
        compiler_params=pltpu.CompilerParams(
            vmem_limit_bytes=VMEM_BYTES, **(dict(collective_id=0, has_side_effects=True) if remote else {})
        ),
        name="pair_forward",
    )(
        positions, atoms, hops.T, edges.T, flags.T, scale, shift, centers, spreads, w1, b1, w2.T, hop_table,
        edge_table, *weights,
    )
    return results[0], results[1:9], results[9:]


def window(group):
    first = GROUP * HD * group
    start = first // 128 * 128
    width = 128 if first - start + GROUP * HD <= 128 else 256
    return start, width, first - start


def head_masks(group, kind):
    _, width, offset = window(group)
    lane = iota((1, width), 1)
    return [
        ((lane >= offset + HD * h) & (lane < offset + HD * (h + 1))).astype(f32).astype(kind) for h in range(GROUP)
    ]


def spread_heads(values, group):
    return jnp.concatenate([values * mask for mask in head_masks(group, bf16)], axis=0)


def gather_heads(values, group):
    masks = head_masks(group, f32)
    total = values[:SLOT] * masks[0]
    for h in range(1, GROUP):
        total = total + values[SLOT * h : SLOT * (h + 1)] * masks[h]
    return total


def standardize(values):
    centred = values - jnp.mean(values, axis=-1, keepdims=True)
    inv_std = lax.rsqrt(jnp.mean(centred * centred, axis=-1, keepdims=True) + 1e-05)
    return centred * inv_std, inv_std


def norm_back(d_normed, scaled, inv_std, gain):
    weighted = d_normed * gain
    inner_a = jnp.mean(weighted, axis=-1, keepdims=True)
    inner_b = jnp.mean(weighted * scaled, axis=-1, keepdims=True)
    return inv_std * (weighted - inner_a - scaled * inner_b)


def column_sum(values):
    return jnp.sum(values, axis=0, keepdims=True)


def row_of(ref):
    return ref[...].reshape(1, ref.shape[0])


def forward_kernel(
    len_ref, hidden_ref, cot_ref, bias_ref, wqkv_ref, up_ref, proj_ref, down_ref,
    ag_ref, as_ref, fg_ref, fs_ref, ub_ref, db_ref,
    output_ref, normed_ref, joined_ref, prob_ref, datt_ref, dresid_ref, grads_ref, small_ref,
    mixed, attended, normed_f, activated, d_pre, d_branch,
):
    tokens = hidden_ref.shape[0]
    slots = tokens // SLOT
    chunk = min(256, tokens)
    first_slot = lax.axis_index("tp") * slots

    def project(c, _):
        rows = pl.ds(pl.multiple_of(c * chunk, chunk), chunk)
        scaled, _unused = standardize(hidden_ref[rows, :].astype(f32))
        normed = (scaled * row_of(ag_ref) + row_of(as_ref)).astype(bf16)
        normed_ref[rows, :] = normed
        for m in range(3):
            for t in range(2):
                at = m * D + t * HALF_D
                joined_ref[rows, at : at + HALF_D] = dot_nn(normed, wqkv_ref[t, m]).astype(bf16)
        return 0

    lax.fori_loop(0, tokens // chunk, project, 0)
    low = low_lanes(HALF)

    def attend(s, _):
        rows = pl.ds(pl.multiple_of(s * SLOT, SLOT), SLOT)
        length = len_ref[first_slot + s]
        valid = iota((SLOT, GROUP * SLOT), 0) < length
        mixed[...] = jnp.zeros_like(mixed)
        for g in range(GROUPS):
            start, width, _offset = window(g)
            q = joined_ref[rows, start : start + width]
            k = joined_ref[rows, D + start : D + start + width]
            v = joined_ref[rows, 2 * D + start : 2 * D + start + width]
            scores = dot_nt(k, spread_heads(q, g)) * head_scale
            parts = []
            for pair in range(GROUP // 2):
                head = GROUP * g + 2 * pair
                one = bias_ref[s, head * HALF : (head + 1) * HALF, :]
                two = bias_ref[s, (head + 1) * HALF : (head + 2) * HALF, :]
                top = jnp.where(low, one, half_swap(two))
                bottom = jnp.where(low, half_swap(one), two)
                parts.append(jnp.concatenate([top, bottom], axis=0))
            scores = jnp.where(valid, scores + jnp.concatenate(parts, axis=1), neg_large)
            weights = jnp.exp(scores - jnp.max(scores, axis=0, keepdims=True))
            prob = (weights * (1.0 / jnp.sum(weights, axis=0, keepdims=True))).astype(bf16)
            prob_ref[s, :, g * GROUP * SLOT : (g + 1) * GROUP * SLOT] = prob
            mixed[:, start : start + width] += gather_heads(dot_tn(prob, v), g)
        attended[rows, :] = mixed[...].astype(bf16)
        return 0

    lax.fori_loop(0, slots, attend, 0)
    small_ref[...] = jnp.zeros_like(small_ref)

    def feed(c, _):
        rows = pl.ds(pl.multiple_of(c * chunk, chunk), chunk)
        halves = [slice(0, HALF_D), slice(HALF_D, D)]
        resid = hidden_ref[rows, :].astype(f32)
        for t in range(2):
            resid = resid + dot_nn(attended[rows, halves[t]], proj_ref[t])
        scaled, inv_std = standardize(resid)
        normed = (scaled * row_of(fg_ref) + row_of(fs_ref)).astype(bf16)
        normed_f[rows, :] = normed
        pre = jnp.concatenate([dot_nn(normed, up_ref[t]) for t in range(2)], axis=1)
        value, slope = gelu_parts(pre + row_of(ub_ref))
        active = value.astype(bf16)
        activated[rows, :] = active
        result = resid + row_of(db_ref)
        for t in range(2):
            result = result + dot_nn(active[:, halves[t]], down_ref[t])
        output_ref[rows, :] = result.astype(bf16)
        cot = cot_ref[rows, :]
        cot_wide = cot.astype(f32)
        d_active = jnp.concatenate([dot_nt(cot, down_ref[t]) for t in range(2)], axis=1)
        d_hidden = (d_active * slope).astype(bf16)
        d_pre[rows, :] = d_hidden
        d_normed = dot_nt(d_hidden[:, halves[0]], up_ref[0]) + dot_nt(d_hidden[:, halves[1]], up_ref[1])
        d_resid = cot_wide + norm_back(d_normed, scaled, inv_std, row_of(fg_ref))
        dresid_ref[rows, :] = d_resid
        branch = d_resid.astype(bf16)
        d_branch[rows, :] = branch
        for t in range(2):
            datt_ref[rows, halves[t]] = dot_nt(branch, proj_ref[t]).astype(bf16)
        small_ref[0:1, :] += column_sum(d_normed * scaled)
        small_ref[1:2, :] += column_sum(d_normed)
        small_ref[2:3, :] += column_sum(d_hidden.astype(f32))
        small_ref[3:4, :] += column_sum(cot_wide)
        return 0

    lax.fori_loop(0, tokens // chunk, feed, 0)
    for t in range(2):
        half = slice(t * HALF_D, (t + 1) * HALF_D)
        grads_ref[t, 0] = dot_tn(normed_f[...], d_pre[:, half]).astype(bf16)
        for block, left, right in ((1, attended, d_branch), (2, activated, cot_ref)):
            grad = dot_tn(left[:, half], right[...]).astype(bf16)
            grads_ref[t, block, :HALF_D, :] = grad[:, :HALF_D]
            grads_ref[t, block, HALF_D:, :] = grad[:, HALF_D:]


def vmem(count):
    return [pl.BlockSpec(memory_space=pltpu.VMEM)] * count


def layer_forward(lengths, hidden, cot, bias, weights, vectors):
    tokens = hidden.shape[0]
    slots = tokens // SLOT
    shape = jax.ShapeDtypeStruct
    return pl.pallas_call(
        forward_kernel,
        in_specs=[pl.BlockSpec(memory_space=pltpu.SMEM)] + vmem(13),
        out_specs=vmem(8),
        out_shape=[
            shape((tokens, D), bf16), shape((tokens, D), bf16), shape((tokens, 3 * D), bf16),
            shape((slots, SLOT, H * SLOT), bf16), shape((tokens, D), bf16), shape((tokens, D), f32),
            shape((2, 3, D, HALF_D), bf16), shape((8, D), f32),
        ],
        scratch_shapes=[pltpu.VMEM((SLOT, D), f32)] + [pltpu.VMEM((tokens, D), bf16)] * 5,
        compiler_params=pltpu.CompilerParams(vmem_limit_bytes=VMEM_BYTES),
        name="layer_forward",
    )(lengths, hidden, cot, bias, *weights, *vectors)


class Peers:
    def __init__(self):
        self.core, self.x, self.z, self.tp = place()
        mol = lax.axis_index("mol")
        self.over_core = {"mol": mol + 1 - 2 * self.core}
        self.over_x = {"mol": mol + 2 - 4 * self.x}
        self.over_tp = {"tp": 1 - self.tp}
        self.turn = [lax.rem(self.z + d, 4) for d in range(4)]
        self.over_z = [{"mol": self.turn[d] * 4 + self.x * 2 + self.core} for d in range(4)]

    def everyone(self):
        return [self.over_core, self.over_x, self.over_tp] + self.over_z[1:]


def span(start, size):
    return pl.ds(pl.multiple_of(start, size), size)


def add_rows(target, source, rows):
    step = 96 if rows % 96 == 0 else rows

    def piece(i, _):
        at = pl.ds(pl.multiple_of(i * step, step), step)
        target[at, :] = (target[at, :].astype(f32) + source[at, :].astype(f32)).astype(target.dtype)
        return 0

    lax.fori_loop(0, rows // step, piece, 0)


class Reduction:
    def __init__(self, peers, part, total, from_core, from_tp, from_x, from_z, sends, recvs):
        self.peers, self.part, self.total = peers, part, total
        self.from_core, self.from_tp, self.from_x, self.from_z = from_core, from_tp, from_x, from_z
        self.sends, self.recvs = sends, recvs
        p = peers
        self.at_core = p.core * 384
        self.at_x = self.at_core + p.x * 192

    def copy(self, b, kind):
        p = self.peers
        part, total = self.part, self.total
        if kind == 0:
            src, dst, peer = part.at[:, b, span((1 - p.core) * 384, 384)], self.from_core.at[:, b], p.over_core
        elif kind == 1:
            src, dst, peer = part.at[1 - p.tp, b, span(self.at_core, 384)], self.from_tp.at[b], p.over_tp
        elif kind == 2:
            src, dst, peer = part.at[p.tp, b, span(self.at_core + (1 - p.x) * 192, 192)], self.from_x.at[b], p.over_x
        elif kind < 6:
            d = kind - 2
            src, dst, peer = part.at[p.tp, b, span(self.at_x + p.turn[d] * 48, 48)], self.from_z.at[b, d - 1], p.over_z[d]
        elif kind < 9:
            src = dst = total.at[b, span(self.at_x + p.z * 48, 48)]
            peer = p.over_z[kind - 5]
        elif kind == 9:
            src = dst = total.at[b, span(self.at_x, 192)]
            peer = p.over_x
        else:
            src = dst = total.at[b, span(self.at_core, 384)]
            peer = p.over_core
        return pltpu.make_async_remote_copy(
            src_ref=src, dst_ref=dst, send_sem=self.sends.at[b, kind], recv_sem=self.recvs.at[b, kind],
            device_id=peer, device_id_type=MESH,
        )

    def act(self, b, stage):
        p = self.peers
        if stage == 0:
            self.copy(b, 0).start()
        elif stage == 1:
            self.copy(b, 0).wait_recv()
            add_rows(self.part.at[1 - p.tp, b, span(self.at_core, 384)], self.from_core.at[1 - p.tp, b], 384)
            self.copy(b, 1).start()
            add_rows(self.part.at[p.tp, b, span(self.at_core, 384)], self.from_core.at[p.tp, b], 384)
        elif stage == 2:
            self.copy(b, 1).wait_recv()
            away, mine = (1 - p.x) * 192, p.x * 192
            add_rows(self.part.at[p.tp, b, span(self.at_core + away, 192)], self.from_tp.at[b, span(away, 192)], 192)
            self.copy(b, 2).start()
            add_rows(self.part.at[p.tp, b, span(self.at_core + mine, 192)], self.from_tp.at[b, span(mine, 192)], 192)
        elif stage == 3:
            self.copy(b, 2).wait_recv()
            add_rows(self.part.at[p.tp, b, span(self.at_x, 192)], self.from_x.at[b], 192)
            for kind in (3, 4, 5):
                self.copy(b, kind).start()
        elif stage == 4:
            for kind in (3, 4, 5):
                self.copy(b, kind).wait_recv()
            mine = span(self.at_x + p.z * 48, 48)
            value = self.part[p.tp, b, mine, :].astype(f32)
            for d in range(3):
                value = value + self.from_z[b, d].astype(f32)
            self.total[b, mine, :] = value.astype(bf16)
            for kind in (6, 7, 8):
                self.copy(b, kind).start()
        elif stage == 5:
            for kind in (6, 7, 8):
                self.copy(b, kind).wait_recv()
            self.copy(b, 9).start()
        elif stage == 6:
            self.copy(b, 9).wait_recv()
            self.copy(b, 10).start()
        elif stage == 7:
            self.copy(b, 10).wait_recv()
        else:
            for kind in range(11):
                self.copy(b, kind).wait_send()


class SmallReduction:
    def __init__(self, peers, part, total, from_core, from_tp, from_x, from_z, sends, recvs):
        self.peers, self.part, self.total = peers, part, total
        self.from_core, self.from_tp, self.from_x, self.from_z = from_core, from_tp, from_x, from_z
        self.sends, self.recvs = sends, recvs
        p = peers
        self.at_core = p.core * 128
        self.at_tp = self.at_core + p.tp * 64
        self.at_x = self.at_tp + p.x * 32

    def copy(self, kind):
        p = self.peers
        part, total = self.part, self.total
        if kind == 0:
            src, dst, peer = part.at[span((1 - p.core) * 128, 128)], self.from_core, p.over_core
        elif kind == 1:
            src, dst, peer = part.at[span(self.at_core + (1 - p.tp) * 64, 64)], self.from_tp, p.over_tp
        elif kind == 2:
            src, dst, peer = part.at[span(self.at_tp + (1 - p.x) * 32, 32)], self.from_x, p.over_x
        elif kind < 6:
            d = kind - 2
            src, dst, peer = part.at[span(self.at_x + p.turn[d] * 8, 8)], self.from_z.at[d - 1], p.over_z[d]
        elif kind < 9:
            src = dst = total.at[span(self.at_x + p.z * 8, 8)]
            peer = p.over_z[kind - 5]
        elif kind == 9:
            src = dst = total.at[span(self.at_x, 32)]
            peer = p.over_x
        elif kind == 10:
            src = dst = total.at[span(self.at_tp, 64)]
            peer = p.over_tp
        else:
            src = dst = total.at[span(self.at_core, 128)]
            peer = p.over_core
        return pltpu.make_async_remote_copy(
            src_ref=src, dst_ref=dst, send_sem=self.sends.at[kind], recv_sem=self.recvs.at[kind],
            device_id=peer, device_id_type=MESH,
        )

    def act(self, stage):
        p = self.peers
        if stage == 0:
            self.copy(0).start()
        elif stage == 1:
            self.copy(0).wait_recv()
            add_rows(self.part.at[span(self.at_core, 128)], self.from_core, 128)
            self.copy(1).start()
        elif stage == 2:
            self.copy(1).wait_recv()
            add_rows(self.part.at[span(self.at_tp, 64)], self.from_tp, 64)
            self.copy(2).start()
        elif stage == 3:
            self.copy(2).wait_recv()
            add_rows(self.part.at[span(self.at_x, 32)], self.from_x, 32)
            for kind in (3, 4, 5):
                self.copy(kind).start()
        elif stage == 4:
            for kind in (3, 4, 5):
                self.copy(kind).wait_recv()
            mine = span(self.at_x + p.z * 8, 8)
            self.total[mine, :] = self.part[mine, :] + self.from_z[0] + self.from_z[1] + self.from_z[2]
            for kind in (6, 7, 8):
                self.copy(kind).start()
        elif stage == 5:
            for kind in (6, 7, 8):
                self.copy(kind).wait_recv()
            self.copy(9).start()
        elif stage == 6:
            self.copy(9).wait_recv()
            self.copy(10).start()
        elif stage == 7:
            self.copy(10).wait_recv()
            self.copy(11).start()
        elif stage == 8:
            self.copy(11).wait_recv()
        else:
            for kind in range(12):
                self.copy(kind).wait_send()


def big_scratch():
    return [
        pltpu.VMEM((2, 3, 384, HALF_D), bf16), pltpu.VMEM((3, 384, HALF_D), bf16), pltpu.VMEM((3, 192, HALF_D), bf16),
        pltpu.VMEM((3, 3, 48, HALF_D), bf16), pltpu.SemaphoreType.DMA((3, 11)), pltpu.SemaphoreType.DMA((3, 11)),
    ]


def small_scratch():
    return [
        pltpu.VMEM((128, 128), f32), pltpu.VMEM((64, 128), f32), pltpu.VMEM((32, 128), f32),
        pltpu.VMEM((3, 8, 128), f32), pltpu.SemaphoreType.DMA((12,)), pltpu.SemaphoreType.DMA((12,)),
    ]


def backward_kernel(remote, *refs):
    (
        hidden_ref, joined_ref, prob_ref, datt_ref, dresid_ref, normed_ref, wqkv_ref, gain_ref, small_ref,
        arg_ref, dist_ref, hop_ref, edge_ref, atom_ref, flag_ref, cen_ref, spr_ref, w1_ref, w2_ref,
        gauss_hbm, second_hbm, slope_hbm,
    ) = refs[:22]
    refs = refs[22:]
    if remote:
        fgrads_hbm, ginput_ref, ftotal, qtotal, stotal = refs[:5]
        refs = refs[5:]
        fpart, qpart, spart = refs[:3]
        refs = refs[3:]
    else:
        ginput_ref, qpart, spart = refs[:3]
        refs = refs[3:]
    (
        d_joined, dq, dk, dv, dbias, cols, dfirst, dspace, hots, dargs, sums, acc_first, acc_second, acc_table,
        gauss_buf, second_buf, slope_buf, loads,
    ) = refs[:18]
    refs = refs[18:]
    tokens = hidden_ref.shape[0]
    slots = tokens // SLOT
    chunk = min(256, tokens)
    low = low_lanes(HALF)

    def load(slot):
        bank = lax.rem(slot, 2)
        return [
            pltpu.make_async_copy(src.at[slot], dst.at[bank], loads.at[bank, index])
            for index, (src, dst) in enumerate(
                ((gauss_hbm, gauss_buf), (second_hbm, second_buf), (slope_hbm, slope_buf))
            )
        ]

    for slot in range(2):
        for item in load(slot):
            item.start()
    if remote:
        peers = Peers()
        fload = pltpu.make_async_copy(fgrads_hbm, fpart, refs[18])
        fload.start()
        ffn = Reduction(peers, fpart, ftotal, *refs[0:6])
        qkv = Reduction(peers, qpart, qtotal, *refs[6:12])
        small = SmallReduction(peers, spart, stotal, *refs[12:18])
        greet(peers.everyone())
        fload.wait()
        for b in range(3):
            ffn.act(b, 0)

    def chain(reduction, time):
        for b in range(3):
            if 1 <= time - b <= 8:
                reduction.act(b, time - b)

    def at_time(index, first, steps):
        if remote:
            for k, step in enumerate(steps):
                pl.when(index == first + k)(step)

    def attend_back(s, _):
        rows = pl.ds(pl.multiple_of(s * SLOT, SLOT), SLOT)
        dq[...] = jnp.zeros_like(dq)
        dk[...] = jnp.zeros_like(dk)
        dv[...] = jnp.zeros_like(dv)
        for g in range(GROUPS):
            start, width, _offset = window(g)
            lanes = slice(start, start + width)
            k = joined_ref[rows, D + start : D + start + width]
            v = joined_ref[rows, 2 * D + start : 2 * D + start + width]
            q_heads = spread_heads(joined_ref[rows, lanes], g)
            d_heads = spread_heads(datt_ref[rows, lanes], g)
            prob = prob_ref[s, :, g * GROUP * SLOT : (g + 1) * GROUP * SLOT]
            wide = prob.astype(f32)
            d_prob = dot_nt(v, d_heads)
            inner = jnp.sum(wide * d_prob, axis=0, keepdims=True)
            d_scores = (wide * (d_prob - inner)).astype(bf16)
            dv[:, lanes] += dot_nn(prob, d_heads)
            dk[:, lanes] += dot_nn(d_scores, q_heads)
            dq[:, lanes] += gather_heads(dot_tn(d_scores, k), g)
            d_wide = d_scores.astype(f32)
            for pair in range(GROUP // 2):
                head = GROUP * g + 2 * pair
                top = d_wide[:HALF, 128 * pair : 128 * (pair + 1)]
                bottom = d_wide[HALF:, 128 * pair : 128 * (pair + 1)]
                dbias[s, head * HALF : (head + 1) * HALF, :] = jnp.where(low, top, half_swap(bottom))
                dbias[s, (head + 1) * HALF : (head + 2) * HALF, :] = jnp.where(low, half_swap(top), bottom)
        d_joined[rows, 0:D] = (dq[...] * head_scale).astype(bf16)
        d_joined[rows, D : 2 * D] = (dk[...] * head_scale).astype(bf16)
        d_joined[rows, 2 * D : 3 * D] = dv[...].astype(bf16)
        at_time(s, 0, [functools.partial(chain, ffn, time) for time in range(1, 9)] if remote else [])
        return 0

    lax.fori_loop(0, slots, attend_back, 0)
    for m in range(3):
        for t in range(2):
            at = m * D + t * HALF_D
            qpart[t, m] = dot_tn(normed_ref[...], d_joined[:, at : at + HALF_D]).astype(bf16)
        if remote:
            qkv.act(m, 0)
    if remote:
        chain(ffn, 9)

    spart[...] = jnp.zeros_like(spart)

    def finish(c, totals):
        rows = pl.ds(pl.multiple_of(c * chunk, chunk), chunk)
        d_normed = None
        for m in range(3):
            for t in range(2):
                at = m * D + t * HALF_D
                term = dot_nt(d_joined[rows, at : at + HALF_D], wqkv_ref[t, m])
                d_normed = term if d_normed is None else d_normed + term
        scaled, inv_std = standardize(hidden_ref[rows, :].astype(f32))
        grad = dresid_ref[rows, :] + norm_back(d_normed, scaled, inv_std, row_of(gain_ref))
        ginput_ref[rows, :] = grad.astype(bf16)
        return (totals[0] + column_sum(d_normed * scaled), totals[1] + column_sum(d_normed))

    zero_row = jnp.zeros((1, D), f32)
    gain_sum, shift_sum = lax.fori_loop(0, tokens // chunk, finish, (zero_row, zero_row))
    vectors = [gain_sum, shift_sum] + [small_ref[i : i + 1, :] for i in range(4)]
    for v, vector in enumerate(vectors):
        for i in range(D // 128):
            at = VECTOR_ROWS + v * (D // 128) + i
            spart[at : at + 1, :] = vector[:, 128 * i : 128 * (i + 1)]
    if remote:
        chain(ffn, 10)
        chain(qkv, 1)

    spr = to_column(row_of(spr_ref))
    cols[0] = jnp.broadcast_to(to_column(row_of(cen_ref)), (K, 128))
    cols[1] = jnp.broadcast_to(1.0 / spr, (K, 128))
    for ref in (sums, acc_first, acc_second, acc_table):
        ref[...] = jnp.zeros_like(ref)

    def pair_back(slot, _):
        bank = lax.rem(slot, 2)
        graph_on = flag_ref[0, slot].astype(f32)
        space_on = flag_ref[1, slot].astype(f32)
        w2 = (w2_ref[...] * space_on.astype(bf16))
        for item in load(slot):
            item.wait()

        def tile(t, carry):
            r = 2 * t
            two = lambda ref: jnp.concatenate([ref[slot, pl.ds(r, 1), :], ref[slot, pl.ds(r + 1, 1), :]], axis=1)
            wide = lambda index: jnp.concatenate([cols[index], cols[index]], axis=1)
            where = pl.ds(pl.multiple_of(t * 256, 256), 256)
            grad = jnp.concatenate(
                [dbias[slot, pl.ds(r, H, stride=HALF), :], dbias[slot, pl.ds(r + 1, H, stride=HALF), :]], axis=1
            )
            dspace[:, where] = jnp.concatenate([grad * space_on, grad * graph_on], axis=0).astype(bf16)
            d_second = dot_tn(w2, grad.astype(bf16))
            d_first = (d_second * slope_buf[bank, :, where].astype(f32)).astype(bf16)
            dfirst[:, where] = d_first
            d_gauss = dot_nn(w1_ref[...], d_first)
            inv = wide(1)
            u = (two(arg_ref) - wide(0)) * inv
            q = d_gauss * gauss_buf[bank, :, where].astype(f32)
            w = q * u
            sums[0] += w[:, :128] + w[:, 128:]
            extra = w * u - q
            sums[1] += extra[:, :128] + extra[:, 128:]
            darg = -jnp.sum(w * inv, axis=0, keepdims=True)
            dargs[pl.ds(r, 1), :] = darg[:, :128]
            dargs[pl.ds(r + 1, 1), :] = darg[:, 128:]
            hop, edge = two(hop_ref), two(edge_ref)
            edge_hot = (edge == iota((HOT - HOPS, 256), 0).astype(f32)).astype(f32)
            edge_hot = jnp.where(iota((HOT - HOPS, 256), 0) == EDGES, 1.0, edge_hot)
            hots[:, where] = jnp.concatenate(
                [(hop == iota((HOPS, 256), 0).astype(f32)).astype(f32), edge_hot], axis=0
            ).astype(bf16)
            return carry

        lax.fori_loop(0, HALF // 2, tile, 0)
        acc_first[...] += dot_nt(jnp.concatenate([gauss_buf[bank], hots[...]], axis=0), dfirst[...])
        acc_second[...] += dot_nt(dspace[...], jnp.concatenate([second_buf[bank], hots[...]], axis=0))

        @pl.when(slot + 2 < slots)
        def _():
            for item in load(slot + 2):
                item.start()

        query_hot = (atom_ref[slot, 0:1, :] == iota((ATOMS, 128), 0).astype(f32)).astype(f32)
        low_atoms = low_lanes(ATOMS)
        for index in range(2):
            values = dargs[...] * dist_ref[slot] if index == 0 else dargs[...]
            part = jnp.where(
                low_atoms,
                dot_nn(query_hot[:, :HALF], values, highest),
                dot_nn(query_hot[:, HALF:SLOT], values, highest),
            )
            acc_table[index] += dot_nt(query_hot, part, highest)
        at_time(slot, 0, [functools.partial(chain, qkv, time) for time in range(2, 10)] if remote else [])
        return 0

    lax.fori_loop(0, slots, pair_back, 0)
    spart[0:K, :] = acc_first[0:K, :]
    spart[SECOND_ROWS : SECOND_ROWS + H, :] = acc_second[:H, :K]
    spart[TABLE_ROWS : TABLE_ROWS + H, :HOT] = acc_second[H:, K : K + HOT]
    for index in range(2):
        spart[TABLE_ROWS + ATOMS * index : TABLE_ROWS + ATOMS * (index + 1), HOT : HOT + ATOMS] = acc_table[index]
    spart[KERNEL_ROWS : KERNEL_ROWS + 1, :] = acc_first[K + HOPS + EDGES : K + HOPS + EDGES + 1, :]
    for index in range(2):
        column = jnp.sum(sums[index] * cols[1], axis=1, keepdims=True)
        same = iota((K, K), 0) == iota((K, K), 1)
        spart[KERNEL_ROWS + 1 + index : KERNEL_ROWS + 2 + index, :] = jnp.sum(
            jnp.where(same, column, 0.0), axis=0, keepdims=True
        )
    if remote:
        small.act(0)
        chain(qkv, 10)
        for stage in range(1, 10):
            small.act(stage)


SECOND_ROWS = K
TABLE_ROWS = SECOND_ROWS + H
KERNEL_ROWS = TABLE_ROWS + H
VECTOR_ROWS = KERNEL_ROWS + 8
SMALL_ROWS = 256


def layer_backward(hidden, joined, prob, datt, dresid, normed, wqkv, gain, small, kept, flags, kernels, fgrads, remote):
    scale, shift, centers, spreads, w1, b1, w2, hop_table, edge_table = kernels
    arg, dist, gauss, second, slope, hop, edge, atom = kept
    tokens = hidden.shape[0]
    slots = tokens // SLOT
    shape = jax.ShapeDtypeStruct
    anywhere = pl.BlockSpec(memory_space=pl.ANY)
    smem = pl.BlockSpec(memory_space=pltpu.SMEM)
    total = shape((3, D, HALF_D), bf16)
    part = shape((2, 3, D, HALF_D), bf16)
    rows = shape((SMALL_ROWS, 128), f32)
    work = [
        pltpu.VMEM((tokens, 3 * D), bf16), pltpu.VMEM((SLOT, D), f32), pltpu.VMEM((SLOT, D), f32),
        pltpu.VMEM((SLOT, D), f32), pltpu.VMEM((slots, H * HALF, 128), f32), pltpu.VMEM((2, K, 128), f32),
        pltpu.VMEM((K, PAIRS), bf16), pltpu.VMEM((2 * H, PAIRS), bf16), pltpu.VMEM((HOT, PAIRS), bf16),
        pltpu.VMEM((HALF, 128), f32), pltpu.VMEM((2, K, 128), f32), pltpu.VMEM((K + HOT, K), f32),
        pltpu.VMEM((2 * H, K + HOT), f32), pltpu.VMEM((2, ATOMS, ATOMS), f32),
        pltpu.VMEM((2, K, PAIRS), bf16), pltpu.VMEM((2, K, PAIRS), bf16), pltpu.VMEM((2, K, PAIRS), bf16),
        pltpu.SemaphoreType.DMA((2, 3)),
    ]
    parts = [pltpu.VMEM(part.shape, bf16), pltpu.VMEM(part.shape, bf16), pltpu.VMEM(rows.shape, f32)]
    sums = big_scratch() + big_scratch() + small_scratch() + [pltpu.SemaphoreType.DMA]
    return pl.pallas_call(
        functools.partial(backward_kernel, remote),
        in_specs=vmem(14) + [smem] + vmem(4) + [anywhere] * (4 if remote else 3),
        out_specs=vmem(4 if remote else 3),
        out_shape=[shape((tokens, D), bf16)] + ([total, total, rows] if remote else [part, rows]),
        scratch_shapes=(parts if remote else []) + work + (sums if remote else []),
        compiler_params=pltpu.CompilerParams(
            vmem_limit_bytes=VMEM_BYTES, **(dict(collective_id=1, has_side_effects=True) if remote else {})
        ),
        name="layer_backward",
    )(
        hidden, joined, prob, datt, dresid, normed, wqkv, gain, small, arg, dist, hop, edge, atom, flags.T,
        centers, spreads, w1, w2.T, gauss, second, slope, *((fgrads,) if remote else ()),
    )


def unpack_kernel(
    fsum_ref, qsum_ref, rows_ref,
    again, ashift, qkv, proj, fgain, fshift, up, up_bias, down, down_bias, scale, shift, centers, spreads,
    first, first_bias, second, hop, edge,
):
    qkv[...] = qsum_ref[...].astype(f32)
    up[...] = fsum_ref[0].astype(f32)
    for block, ref in ((1, proj), (2, down)):
        ref[:, :HALF_D] = fsum_ref[block, :HALF_D].astype(f32)
        ref[:, HALF_D:] = fsum_ref[block, HALF_D:].astype(f32)
    for v, ref in enumerate((again, ashift, fgain, fshift, up_bias, down_bias)):
        for i in range(D // 128):
            ref[pl.ds(128 * i, 128)] = rows_ref[VECTOR_ROWS + v * (D // 128) + i, :]
    first[...] = rows_ref[0:K, :]
    second[...] = rows_ref[SECOND_ROWS : SECOND_ROWS + H, :]
    table = rows_ref[TABLE_ROWS : TABLE_ROWS + H, :]
    scale[...] = table[:ATOMS, HOT : HOT + ATOMS]
    shift[...] = table[ATOMS:, HOT : HOT + ATOMS]
    turned = jnp.concatenate([table, jnp.zeros((128 - H, 128), f32)], axis=0).T
    hop[...] = turned[:HOPS, :H]
    edge[...] = turned[HOPS : HOPS + EDGES, :H]
    for i, ref in enumerate((first_bias, centers, spreads)):
        ref[...] = rows_ref[KERNEL_ROWS + i, :]


def unpack(fsum, qsum, rows):
    vec = jax.ShapeDtypeStruct((D,), f32)
    line = jax.ShapeDtypeStruct((K,), f32)
    mat = lambda *dims: jax.ShapeDtypeStruct(dims, f32)
    return pl.pallas_call(
        unpack_kernel,
        in_specs=vmem(3),
        out_specs=vmem(19),
        out_shape=[
            vec, vec, mat(3, D, HALF_D), mat(HALF_D, D), vec, vec, mat(D, HALF_D), vec, mat(HALF_D, D), vec,
            mat(ATOMS, ATOMS), mat(ATOMS, ATOMS), line, line, mat(K, K), line, mat(H, K), mat(HOPS, H), mat(EDGES, H),
        ],
        compiler_params=pltpu.CompilerParams(vmem_limit_bytes=VMEM_BYTES),
        name="unpack",
    )(fsum, qsum, rows)


def whole_weights(qkv_weight, up_weight, proj_weight, down_weight):
    columns = lambda w: jnp.stack(jnp.split(w, 2, axis=-1))
    rows = lambda w: jnp.stack(jnp.split(w, 2, axis=0))
    gather = lambda w, dim: lax.all_gather(w, "tp", axis=dim, tiled=True)
    return (
        columns(gather(qkv_weight.transpose(1, 0, 2), 2)), columns(gather(up_weight, 1)),
        rows(gather(proj_weight, 0)), rows(gather(down_weight, 0)),
    )


def sum_grads(fgrads, qgrads, small):
    total_f, total_q, rows = lax.psum((fgrads, qgrads, small), ("mol", "tp"))
    share = D // lax.axis_size("tp")
    at = lax.axis_index("tp") * share
    columns = lambda w: lax.dynamic_slice_in_dim(jnp.concatenate([w[0], w[1]], axis=-1), at, share, w.ndim - 2)
    rows_of = lambda w: lax.dynamic_slice_in_dim(
        jnp.concatenate([jnp.concatenate([w[t, :HALF_D], w[t, HALF_D:]], axis=1) for t in range(2)]), at, share, 0
    )
    wide = lambda v: v.astype(f32)
    big = (wide(columns(total_q)), wide(columns(total_f[:, 0])), wide(rows_of(total_f[:, 1])), wide(rows_of(total_f[:, 2])))
    return big, rows


def body(
    mesh_shape,
    hidden_in, positions, atom_types, hop_counts, edge_types, lengths, branches,
    attn_gain, attn_shift, qkv_weight, proj_weight, ffn_gain, ffn_shift, up_weight, up_bias, down_weight, down_bias,
    kernel_scale, kernel_shift, centers, spreads, first_weight, first_bias, second_weight, hop_table, edge_table,
    cotangent,
):
    kernels = (
        kernel_scale, kernel_shift, centers, spreads, first_weight, first_bias, second_weight, hop_table, edge_table,
    )
    remote = mesh_shape["tp"] == 2 and mesh_shape["mol"] == 16
    own = (qkv_weight.transpose(1, 0, 2), up_weight, proj_weight, down_weight)
    bias, kept, weights = pair_forward(
        positions, atom_types, hop_counts, edge_types, branches, kernels, own if remote else None
    )
    if not remote:
        weights = whole_weights(qkv_weight, up_weight, proj_weight, down_weight)
    output, normed, joined, prob, datt, dresid, fgrads, small = layer_forward(
        lengths, hidden_in, cotangent, bias, weights, (attn_gain, attn_shift, ffn_gain, ffn_shift, up_bias, down_bias)
    )
    grad_input, *sums = layer_backward(
        hidden_in, joined, prob, datt, dresid, normed, weights[0], attn_gain, small, kept, branches, kernels, fgrads,
        remote,
    )
    if remote:
        fsum, qsum, rows = sums
    else:
        big, rows = sum_grads(fgrads, *sums)
        fsum = jnp.zeros((3, D, HALF_D), bf16)
        qsum = fsum
    grads = list(unpack(fsum, qsum, rows))
    if not remote:
        grads[2], grads[6], grads[3], grads[8] = big
    grads[2] = grads[2].transpose(1, 0, 2)
    grads[16] = grads[16].T
    return (output, grad_input, *grads)


def solution(mesh):
    rows = P(("mol", "tp"), None)
    all_of = P()
    in_specs = (
        rows, P(None, ("mol", "tp")), P(("mol", "tp")), rows, rows, P("mol"), rows, all_of, all_of,
        P(None, None, "tp"), P("tp", None), all_of, all_of, P(None, "tp"), all_of, P("tp", None),
    ) + (all_of,) * 10 + (rows,)
    out_specs = (
        rows, rows, all_of, all_of, P(None, None, "tp"), P("tp", None), all_of, all_of, P(None, "tp"), all_of,
        P("tp", None),
    ) + (all_of,) * 10
    step = functools.partial(body, dict(mesh.shape))
    return jax.shard_map(step, mesh=mesh, in_specs=in_specs, out_specs=out_specs, check_vma=False)
```

```python
import functools
from types import SimpleNamespace

import jax
import jax.numpy as jnp
from jax import lax
from jax.experimental import pallas as pl
from jax.experimental.pallas import tpu as pltpu
from jax.sharding import PartitionSpec as P

D = 768
H = 32
HD = 24
FF = 768
K = 128
SLOT = 64
HALF = SLOT // 2
HALF_D = D // 2
PAIRS = SLOT * SLOT
HOPS = 16
EDGES = 8
ATOMS = 16
GROUP = 4
GROUPS = H // GROUP
HOT = 32

highest = lax.Precision.HIGHEST
neg_large = -1e30
root_tau = 2.5066282746310002
root_half = 0.7071067811865476
inv_root_tau = 0.3989422804014327
head_scale = HD ** (-0.5)
VMEM_BYTES = 62 * 1024 * 1024
TILE = 512

SECOND_ROWS = K
TABLE_ROWS = SECOND_ROWS + H
KERNEL_ROWS = TABLE_ROWS + H
VECTOR_ROWS = KERNEL_ROWS + 8
SMALL_ROWS = 256

MESH = pl.DeviceIdType.MESH
f32 = jnp.float32
bf16 = jnp.bfloat16


def dot_nn(left, right, precision=None):
    return lax.dot_general(left, right, (((1,), (0,)), ((), ())), precision=precision, preferred_element_type=f32)


def dot_nt(left, right, precision=None):
    return lax.dot_general(left, right, (((1,), (1,)), ((), ())), precision=precision, preferred_element_type=f32)


def dot_tn(left, right, precision=None):
    return lax.dot_general(left, right, (((0,), (0,)), ((), ())), precision=precision, preferred_element_type=f32)


def iota(shape, dim):
    return lax.broadcasted_iota(jnp.int32, shape, dim)


def gelu_parts(values):
    below = 0.5 + 0.5 * lax.erf(values * root_half)
    density = jnp.exp(-0.5 * values * values) * inv_root_tau
    return values * below, below + values * density


def to_column(row):
    size = row.shape[1]
    same = iota((size, size), 0) == iota((size, size), 1)
    return jnp.sum(jnp.where(same, row, 0.0), axis=1, keepdims=True)


def half_swap(values):
    return pltpu.roll(values, 64, 1)


def low_lanes(rows):
    return iota((rows, 128), 1) < 64


def vmem(count):
    return [pl.BlockSpec(memory_space=pltpu.VMEM)] * count


def row_of(ref):
    return ref[...].reshape(1, ref.shape[0])


def place():
    mol = lax.axis_index("mol")
    return mol % 2, (mol // 2) % 2, mol // 4, lax.axis_index("tp")


def greet(peers):
    barrier = pltpu.get_barrier_semaphore()
    for peer in peers:
        pl.semaphore_signal(barrier, inc=1, device_id=peer, device_id_type=MESH)
    pl.semaphore_wait(barrier, len(peers))


def window(group):
    first = GROUP * HD * group
    start = first // 128 * 128
    width = 128 if first - start + GROUP * HD <= 128 else 256
    return start, width, first - start


def head_masks(group, kind):
    _, width, offset = window(group)
    lane = iota((1, width), 1)
    return [
        ((lane >= offset + HD * h) & (lane < offset + HD * (h + 1))).astype(f32).astype(kind) for h in range(GROUP)
    ]


def spread_heads(values, group):
    return jnp.concatenate([values * mask for mask in head_masks(group, bf16)], axis=0)


def gather_heads(values, group):
    masks = head_masks(group, f32)
    total = values[:SLOT] * masks[0]
    for h in range(1, GROUP):
        total = total + values[SLOT * h : SLOT * (h + 1)] * masks[h]
    return total


def standardize(values):
    centred = values - jnp.mean(values, axis=-1, keepdims=True)
    inv_std = lax.rsqrt(jnp.mean(centred * centred, axis=-1, keepdims=True) + 1e-05)
    return centred * inv_std, inv_std


def norm_back(d_normed, scaled, inv_std, gain):
    weighted = d_normed * gain
    inner_a = jnp.mean(weighted, axis=-1, keepdims=True)
    inner_b = jnp.mean(weighted * scaled, axis=-1, keepdims=True)
    return inv_std * (weighted - inner_a - scaled * inner_b)


def column_sum(values):
    return jnp.sum(values, axis=0, keepdims=True)


class Peers:
    def __init__(self):
        self.core, self.x, self.z, self.tp = place()
        mol = lax.axis_index("mol")
        self.over_core = {"mol": mol + 1 - 2 * self.core}
        self.over_x = {"mol": mol + 2 - 4 * self.x}
        self.over_tp = {"tp": 1 - self.tp}
        self.turn = [lax.rem(self.z + d, 4) for d in range(4)]
        self.over_z = [{"mol": self.turn[d] * 4 + self.x * 2 + self.core} for d in range(4)]

    def everyone(self):
        return [self.over_core, self.over_x, self.over_tp] + self.over_z[1:]


def span(start, size):
    return pl.ds(pl.multiple_of(start, size), size)


def add_rows(target, source, rows):
    step = 96 if rows % 96 == 0 else rows

    def piece(i, _):
        at = pl.ds(pl.multiple_of(i * step, step), step)
        target[at, :] = (target[at, :].astype(f32) + source[at, :].astype(f32)).astype(target.dtype)
        return 0

    lax.fori_loop(0, rows // step, piece, 0)


class Reduction:
    def __init__(self, peers, part, total, from_core, from_tp, from_x, from_z, sends, recvs):
        self.peers, self.part, self.total = peers, part, total
        self.from_core, self.from_tp, self.from_x, self.from_z = from_core, from_tp, from_x, from_z
        self.sends, self.recvs = sends, recvs
        p = peers
        self.at_core = p.core * 384
        self.at_x = self.at_core + p.x * 192

    def copy(self, b, kind):
        p = self.peers
        part, total = self.part, self.total
        if kind == 0:
            src, dst, peer = part.at[:, b, span((1 - p.core) * 384, 384)], self.from_core.at[:, b], p.over_core
        elif kind == 1:
            src, dst, peer = part.at[1 - p.tp, b, span(self.at_core, 384)], self.from_tp.at[b], p.over_tp
        elif kind == 2:
            src, dst, peer = part.at[p.tp, b, span(self.at_core + (1 - p.x) * 192, 192)], self.from_x.at[b], p.over_x
        elif kind < 6:
            d = kind - 2
            src, dst, peer = part.at[p.tp, b, span(self.at_x + p.turn[d] * 48, 48)], self.from_z.at[b, d - 1], p.over_z[d]
        elif kind < 9:
            src = dst = total.at[b, span(self.at_x + p.z * 48, 48)]
            peer = p.over_z[kind - 5]
        elif kind == 9:
            src = dst = total.at[b, span(self.at_x, 192)]
            peer = p.over_x
        else:
            src = dst = total.at[b, span(self.at_core, 384)]
            peer = p.over_core
        return pltpu.make_async_remote_copy(
            src_ref=src, dst_ref=dst, send_sem=self.sends.at[b, kind], recv_sem=self.recvs.at[b, kind],
            device_id=peer, device_id_type=MESH,
        )

    def act(self, b, stage):
        p = self.peers
        if stage == 0:
            self.copy(b, 0).start()
        elif stage == 1:
            self.copy(b, 0).wait_recv()
            add_rows(self.part.at[1 - p.tp, b, span(self.at_core, 384)], self.from_core.at[1 - p.tp, b], 384)
            self.copy(b, 1).start()
            add_rows(self.part.at[p.tp, b, span(self.at_core, 384)], self.from_core.at[p.tp, b], 384)
        elif stage == 2:
            self.copy(b, 1).wait_recv()
            away, mine = (1 - p.x) * 192, p.x * 192
            add_rows(self.part.at[p.tp, b, span(self.at_core + away, 192)], self.from_tp.at[b, span(away, 192)], 192)
            self.copy(b, 2).start()
            add_rows(self.part.at[p.tp, b, span(self.at_core + mine, 192)], self.from_tp.at[b, span(mine, 192)], 192)
        elif stage == 3:
            self.copy(b, 2).wait_recv()
            add_rows(self.part.at[p.tp, b, span(self.at_x, 192)], self.from_x.at[b], 192)
            for kind in (3, 4, 5):
                self.copy(b, kind).start()
        elif stage == 4:
            for kind in (3, 4, 5):
                self.copy(b, kind).wait_recv()
            mine = span(self.at_x + p.z * 48, 48)
            value = self.part[p.tp, b, mine, :].astype(f32)
            for d in range(3):
                value = value + self.from_z[b, d].astype(f32)
            self.total[b, mine, :] = value.astype(bf16)
            for kind in (6, 7, 8):
                self.copy(b, kind).start()
        elif stage == 5:
            for kind in (6, 7, 8):
                self.copy(b, kind).wait_recv()
            self.copy(b, 9).start()
        elif stage == 6:
            self.copy(b, 9).wait_recv()
            self.copy(b, 10).start()
        elif stage == 7:
            self.copy(b, 10).wait_recv()
        else:
            for kind in range(11):
                self.copy(b, kind).wait_send()


class SmallReduction:
    def __init__(self, peers, part, total, from_core, from_tp, from_x, from_z, sends, recvs):
        self.peers, self.part, self.total = peers, part, total
        self.from_core, self.from_tp, self.from_x, self.from_z = from_core, from_tp, from_x, from_z
        self.sends, self.recvs = sends, recvs
        p = peers
        self.at_core = p.core * 128
        self.at_tp = self.at_core + p.tp * 64
        self.at_x = self.at_tp + p.x * 32

    def copy(self, kind):
        p = self.peers
        part, total = self.part, self.total
        if kind == 0:
            src, dst, peer = part.at[span((1 - p.core) * 128, 128)], self.from_core, p.over_core
        elif kind == 1:
            src, dst, peer = part.at[span(self.at_core + (1 - p.tp) * 64, 64)], self.from_tp, p.over_tp
        elif kind == 2:
            src, dst, peer = part.at[span(self.at_tp + (1 - p.x) * 32, 32)], self.from_x, p.over_x
        elif kind < 6:
            d = kind - 2
            src, dst, peer = part.at[span(self.at_x + p.turn[d] * 8, 8)], self.from_z.at[d - 1], p.over_z[d]
        elif kind < 9:
            src = dst = total.at[span(self.at_x + p.z * 8, 8)]
            peer = p.over_z[kind - 5]
        elif kind == 9:
            src = dst = total.at[span(self.at_x, 32)]
            peer = p.over_x
        elif kind == 10:
            src = dst = total.at[span(self.at_tp, 64)]
            peer = p.over_tp
        else:
            src = dst = total.at[span(self.at_core, 128)]
            peer = p.over_core
        return pltpu.make_async_remote_copy(
            src_ref=src, dst_ref=dst, send_sem=self.sends.at[kind], recv_sem=self.recvs.at[kind],
            device_id=peer, device_id_type=MESH,
        )

    def act(self, stage):
        p = self.peers
        if stage == 0:
            self.copy(0).start()
        elif stage == 1:
            self.copy(0).wait_recv()
            add_rows(self.part.at[span(self.at_core, 128)], self.from_core, 128)
            self.copy(1).start()
        elif stage == 2:
            self.copy(1).wait_recv()
            add_rows(self.part.at[span(self.at_tp, 64)], self.from_tp, 64)
            self.copy(2).start()
        elif stage == 3:
            self.copy(2).wait_recv()
            add_rows(self.part.at[span(self.at_x, 32)], self.from_x, 32)
            for kind in (3, 4, 5):
                self.copy(kind).start()
        elif stage == 4:
            for kind in (3, 4, 5):
                self.copy(kind).wait_recv()
            mine = span(self.at_x + p.z * 8, 8)
            self.total[mine, :] = self.part[mine, :] + self.from_z[0] + self.from_z[1] + self.from_z[2]
            for kind in (6, 7, 8):
                self.copy(kind).start()
        elif stage == 5:
            for kind in (6, 7, 8):
                self.copy(kind).wait_recv()
            self.copy(9).start()
        elif stage == 6:
            self.copy(9).wait_recv()
            self.copy(10).start()
        elif stage == 7:
            self.copy(10).wait_recv()
            self.copy(11).start()
        elif stage == 8:
            self.copy(11).wait_recv()
        else:
            for kind in range(12):
                self.copy(kind).wait_send()


def big_scratch():
    return [
        pltpu.VMEM((2, 3, 384, HALF_D), bf16), pltpu.VMEM((3, 384, HALF_D), bf16), pltpu.VMEM((3, 192, HALF_D), bf16),
        pltpu.VMEM((3, 3, 48, HALF_D), bf16), pltpu.SemaphoreType.DMA((3, 11)), pltpu.SemaphoreType.DMA((3, 11)),
    ]


def small_scratch():
    return [
        pltpu.VMEM((128, 128), f32), pltpu.VMEM((64, 128), f32), pltpu.VMEM((32, 128), f32),
        pltpu.VMEM((3, 8, 128), f32), pltpu.SemaphoreType.DMA((12,)), pltpu.SemaphoreType.DMA((12,)),
    ]


class Gather:
    def __init__(self, peers, own, whole, sends, recvs):
        self.peers, self.own, self.whole, self.sends, self.recvs = peers, own, whole, sends, recvs
        self.quarter = peers.x * 2 + peers.core
        self.next_quarter = (1 - peers.x) * 2 + peers.core

    def rows(self, ref, quarter):
        count = ref.shape[-2] // 4
        return ref.at[..., span(quarter * count, count), :]

    def copy(self, index, kind):
        p = self.peers
        if kind == 0:
            src = self.rows(self.own[index], self.quarter)
            dst, peer = self.rows(self.whole[index].at[p.tp], self.quarter), p.over_tp
        elif kind == 1:
            src = dst = self.rows(self.whole[index].at[1 - p.tp], self.quarter)
            peer = p.over_x
        else:
            src = dst = self.rows(self.whole[index].at[1 - p.tp], self.quarter if kind == 2 else self.next_quarter)
            peer = p.over_core
        return pltpu.make_async_remote_copy(
            src_ref=src, dst_ref=dst, send_sem=self.sends.at[index, kind], recv_sem=self.recvs.at[index, kind],
            device_id=peer, device_id_type=MESH,
        )

    def start(self):
        for index in range(4):
            self.copy(index, 0).start()

    def onward_x(self, index):
        self.copy(index, 0).wait_recv()
        self.copy(index, 1).start()
        self.copy(index, 2).start()

    def onward_core(self, index):
        self.copy(index, 1).wait_recv()
        self.copy(index, 3).start()

    def arrive(self, index):
        self.copy(index, 2).wait_recv()
        self.copy(index, 3).wait_recv()

    def finish(self):
        for index in range(4):
            for kind in range(4):
                self.copy(index, kind).wait_send()


def widen(values):
    return jnp.concatenate([values] * (TILE // 128), axis=1)


def strips():
    return [slice(16 * i, 16 * (i + 1)) for i in range(K // 16)]


def four_rows(ref, slot, first):
    return jnp.concatenate([ref[slot, pl.ds(first + i, 1), :] for i in range(TILE // 128)], axis=1)


def hot_rows(values, count):
    return (values == iota((count, TILE), 0).astype(f32)).astype(f32)


def fold_lanes(values):
    total = values[:, :128]
    for i in range(1, TILE // 128):
        total = total + values[:, 128 * i : 128 * (i + 1)]
    return total


def prepare_pairs(r):
    spr = to_column(row_of(r.spreads))
    r.cols[0] = jnp.broadcast_to(to_column(row_of(r.centers)), (K, 128))
    r.cols[1] = jnp.broadcast_to(root_half / spr, (K, 128))
    r.cols[2] = jnp.broadcast_to(-jnp.log(root_tau * spr), (K, 128))
    r.cols[3] = jnp.broadcast_to(to_column(row_of(r.first_bias)), (K, 128))
    r.cols[4] = jnp.broadcast_to(1.0 / spr, (K, 128))
    r.w1t[...] = r.first_weight[...].astype(f32).T.astype(bf16)
    second = r.second_weight[...].astype(f32)
    r.w2[...] = jnp.concatenate([second, jnp.zeros((128 - H, K), f32)], axis=0).T.astype(bf16)
    table = jnp.concatenate([r.hop_table[...], r.edge_table[...], jnp.zeros((128 - HOPS - EDGES, H), f32)], axis=0)
    table = jnp.concatenate([table, jnp.zeros((128, 128 - H), f32)], axis=1).T[:H, :HOT]
    one = table.astype(bf16).astype(f32)
    two = (table - one).astype(bf16).astype(f32)
    three = table - one - two
    r.base[...] = jnp.concatenate([second, one, two, three, jnp.zeros((H, 32), f32)], axis=1)


def pair_tables(r, slot):
    low = low_lanes(HALF)
    low_row = low_lanes(1)
    lanes = span(lax.div(slot, 2) * 128, 128)
    turn = lax.rem(slot, 2) * 64
    atoms = r.atoms[lanes].astype(f32).reshape(1, 128)
    rows = [pltpu.roll(row, turn, 1) for row in [r.positions[c : c + 1, lanes] for c in range(3)] + [atoms]]
    double = [jnp.where(low_row, row, half_swap(row)) for row in rows]
    columns = [to_column(row[:, :SLOT]) for row in rows]
    total = None
    for c in range(3):
        offset = jnp.where(low, columns[c][:HALF], columns[c][HALF:]) - double[c]
        total = offset * offset if total is None else total + offset * offset
    distance = jnp.sqrt(total)
    key_hot = (columns[3] == iota((SLOT, ATOMS), 1).astype(f32)).astype(f32)
    query_hot = (double[3] == iota((ATOMS, 128), 0).astype(f32)).astype(f32)
    picked = []
    for table in (r.kernel_scale, r.kernel_shift):
        both = dot_nn(dot_nt(key_hot, table[...], highest), query_hot, highest)
        picked.append(jnp.where(low, both[:HALF], both[HALF:]))
    r.argument[slot] = picked[0] * distance + picked[1]
    r.distance[slot] = distance
    for source, target in ((r.hops, r.hop_rows), (r.edges, r.edge_rows)):
        values = pltpu.roll(source[:, lanes].astype(f32), turn, 1)
        target[slot] = jnp.where(low, values[:HALF], half_swap(values[HALF:]))
    r.atom_rows[slot] = jnp.broadcast_to(double[3], (8, 128))


def pair_forward(r, slot):
    bank = lax.rem(slot, 2)
    graph_on = r.flags[0, slot].astype(f32)
    space_on = r.flags[1, slot].astype(f32)
    factor = jnp.where(iota((H, 256), 1) < K, space_on, graph_on)
    r.lhs[...] = (r.base[...] * factor).astype(bf16)

    def tile(t, _):
        for part in range(2):
            first_row = 8 * t + 4 * part
            where = span(t * 2 * TILE + part * TILE, TILE)
            arg = four_rows(r.argument, slot, first_row)
            pieces = []
            for rows in strips():
                u = (arg - widen(r.cols[0, rows])) * widen(r.cols[1, rows])
                pieces.append(jnp.exp(widen(r.cols[2, rows]) - u * u).astype(bf16))
                r.gauss[bank, rows, where] = pieces[-1]
            first = dot_nn(r.w1t[...], jnp.concatenate(pieces, axis=0))
            pieces = []
            for rows in strips():
                value, slope = gelu_parts(first[rows] + widen(r.cols[3, rows]))
                pieces.append(value.astype(bf16))
                r.second[bank, rows, where] = pieces[-1]
                r.slope[bank, rows, where] = slope.astype(bf16)
            hot = jnp.concatenate(
                [
                    hot_rows(four_rows(r.hop_rows, slot, first_row), HOPS),
                    hot_rows(four_rows(r.edge_rows, slot, first_row), HOT - HOPS),
                ],
                axis=0,
            ).astype(bf16)
            bias = dot_nn(r.lhs[:, : K + 3 * HOT], jnp.concatenate(pieces + [hot] * 3, axis=0))
            bias = bias.astype(bf16).astype(f32)
            for i in range(TILE // 128):
                r.bias[slot, pl.ds(first_row + i, H, stride=HALF), :] = bias[:, 128 * i : 128 * (i + 1)]
        return 0

    lax.fori_loop(0, PAIRS // (2 * TILE), tile, 0)


def pair_backward(r, slot, between):
    bank = lax.rem(slot, 2)
    graph_on = r.flags[0, slot].astype(f32)
    space_on = r.flags[1, slot].astype(f32)
    w2 = r.w2[:, :H] * space_on.astype(bf16)

    def tile(t, _):
        for part in range(2):
            first_row = 8 * t + 4 * part
            where = span(t * 2 * TILE + part * TILE, TILE)
            arg = four_rows(r.argument, slot, first_row)
            grad = jnp.concatenate(
                [r.bias[slot, pl.ds(first_row + i, H, stride=HALF), :] for i in range(TILE // 128)], axis=1
            )
            r.dspace[:, where] = jnp.concatenate([grad * space_on, grad * graph_on], axis=0).astype(bf16)
            d_second = dot_nn(w2, grad.astype(bf16))
            pieces = []
            for rows in strips():
                pieces.append((d_second[rows] * r.slope[bank, rows, where].astype(f32)).astype(bf16))
                r.dfirst[rows, where] = pieces[-1]
            d_gauss = dot_nn(r.first_weight[...], jnp.concatenate(pieces, axis=0))
            d_arg = None
            for rows in strips():
                inv = widen(r.cols[4, rows])
                u = (arg - widen(r.cols[0, rows])) * inv
                q = d_gauss[rows] * r.gauss[bank, rows, where].astype(f32)
                w = q * u
                r.sums[0, rows] += fold_lanes(w)
                r.sums[1, rows] += fold_lanes(w * u - q)
                w = w * inv
                w = w[:8] + w[8:]
                d_arg = w if d_arg is None else d_arg + w
            d_arg = -jnp.sum(d_arg, axis=0, keepdims=True)
            for i in range(TILE // 128):
                r.dargs[pl.ds(first_row + i, 1), :] = d_arg[:, 128 * i : 128 * (i + 1)]
            edge_hot = hot_rows(four_rows(r.edge_rows, slot, first_row), HOT - HOPS)
            edge_hot = jnp.where(iota((HOT - HOPS, TILE), 0) == EDGES, 1.0, edge_hot)
            r.hots[:, where] = jnp.concatenate(
                [hot_rows(four_rows(r.hop_rows, slot, first_row), HOPS), edge_hot], axis=0
            ).astype(bf16)
        return 0

    lax.fori_loop(0, PAIRS // (2 * TILE), tile, 0)
    between()
    r.acc_first[...] += dot_nt(jnp.concatenate([r.gauss[bank], r.hots[...]], axis=0), r.dfirst[...])
    r.acc_second[...] += dot_nt(r.dspace[...], jnp.concatenate([r.second[bank], r.hots[...]], axis=0))
    query_hot = (r.atom_rows[slot, 0:1, :] == iota((ATOMS, 128), 0).astype(f32)).astype(f32)
    for index in range(2):
        values = r.dargs[...] * r.distance[slot] if index == 0 else r.dargs[...]
        part = jnp.where(
            low_lanes(ATOMS),
            dot_nn(query_hot[:, :HALF], values, highest),
            dot_nn(query_hot[:, HALF:SLOT], values, highest),
        )
        r.acc_table[index] += dot_nt(query_hot, part, highest)


def attend(r, s, first_slot):
    low = low_lanes(HALF)
    rows = span(s * SLOT, SLOT)
    valid = iota((SLOT, GROUP * SLOT), 0) < r.lengths[first_slot + s]
    r.work[0] = jnp.zeros((SLOT, D), f32)
    for g in range(GROUPS):
        start, width, _ = window(g)
        q = r.joined[rows, start : start + width]
        k = r.joined[rows, D + start : D + start + width]
        v = r.joined[rows, 2 * D + start : 2 * D + start + width]
        scores = dot_nt(k, spread_heads(q, g)) * head_scale
        parts = []
        for pair in range(GROUP // 2):
            head = GROUP * g + 2 * pair
            one = r.bias[s, head * HALF : (head + 1) * HALF, :]
            two = r.bias[s, (head + 1) * HALF : (head + 2) * HALF, :]
            top = jnp.where(low, one, half_swap(two))
            bottom = jnp.where(low, half_swap(one), two)
            parts.append(jnp.concatenate([top, bottom], axis=0))
        scores = jnp.where(valid, scores + jnp.concatenate(parts, axis=1), neg_large)
        weights = jnp.exp(scores - jnp.max(scores, axis=0, keepdims=True))
        prob = (weights * (1.0 / jnp.sum(weights, axis=0, keepdims=True))).astype(bf16)
        r.prob[s, :, g * GROUP * SLOT : (g + 1) * GROUP * SLOT] = prob
        r.work[0, :, start : start + width] += gather_heads(dot_tn(prob, v), g)
    r.attended[rows, :] = r.work[0].astype(bf16)


def attend_back(r, s):
    low = low_lanes(HALF)
    rows = span(s * SLOT, SLOT)
    r.work[...] = jnp.zeros((3, SLOT, D), f32)
    for g in range(GROUPS):
        start, width, _ = window(g)
        lanes = slice(start, start + width)
        k = r.joined[rows, D + start : D + start + width]
        v = r.joined[rows, 2 * D + start : 2 * D + start + width]
        q_heads = spread_heads(r.joined[rows, lanes], g)
        d_heads = spread_heads(r.d_attended[rows, lanes], g)
        prob = r.prob[s, :, g * GROUP * SLOT : (g + 1) * GROUP * SLOT]
        wide = prob.astype(f32)
        d_prob = dot_nt(v, d_heads)
        inner = jnp.sum(wide * d_prob, axis=0, keepdims=True)
        d_scores = (wide * (d_prob - inner)).astype(bf16)
        r.work[0, :, lanes] += gather_heads(dot_tn(d_scores, k), g)
        r.work[1, :, lanes] += dot_nn(d_scores, q_heads)
        r.work[2, :, lanes] += dot_nn(prob, d_heads)
        d_wide = d_scores.astype(f32)
        for pair in range(GROUP // 2):
            head = GROUP * g + 2 * pair
            top = d_wide[:HALF, 128 * pair : 128 * (pair + 1)]
            bottom = d_wide[HALF:, 128 * pair : 128 * (pair + 1)]
            r.bias[s, head * HALF : (head + 1) * HALF, :] = jnp.where(low, top, half_swap(bottom))
            r.bias[s, (head + 1) * HALF : (head + 2) * HALF, :] = jnp.where(low, half_swap(top), bottom)
    r.joined[rows, 0:D] = (r.work[0] * head_scale).astype(bf16)
    r.joined[rows, D : 2 * D] = (r.work[1] * head_scale).astype(bf16)
    r.joined[rows, 2 * D : 3 * D] = r.work[2].astype(bf16)


def project(r, rows):
    scaled, _ = standardize(r.hidden[rows, :].astype(f32))
    normed = (scaled * row_of(r.attn_gain) + row_of(r.attn_shift)).astype(bf16)
    r.normed_a[rows, :] = normed
    for m in range(3):
        for t in range(2):
            at = m * D + t * HALF_D
            r.joined[rows, at : at + HALF_D] = dot_nn(normed, r.wqkv[t, m]).astype(bf16)


def feed(r, rows):
    halves = [slice(0, HALF_D), slice(HALF_D, D)]
    resid = r.hidden[rows, :].astype(f32)
    for t in range(2):
        resid = resid + dot_nn(r.attended[rows, halves[t]], r.wproj[t])
    scaled, inv_std = standardize(resid)
    normed = (scaled * row_of(r.ffn_gain) + row_of(r.ffn_shift)).astype(bf16)
    r.normed_f[rows, :] = normed
    pre = jnp.concatenate([dot_nn(normed, r.wup[t]) for t in range(2)], axis=1)
    value, slope = gelu_parts(pre + row_of(r.up_bias))
    active = value.astype(bf16)
    r.activated[rows, :] = active
    result = resid + row_of(r.down_bias)
    for t in range(2):
        result = result + dot_nn(active[:, halves[t]], r.wdown[t])
    r.out_rows[rows, :] = result.astype(bf16)
    cot = r.cotangent[rows, :]
    cot_wide = cot.astype(f32)
    d_active = jnp.concatenate([dot_nt(cot, r.wdown[t]) for t in range(2)], axis=1)
    d_hidden = (d_active * slope).astype(bf16)
    r.d_pre[rows, :] = d_hidden
    d_normed = dot_nt(d_hidden[:, halves[0]], r.wup[0]) + dot_nt(d_hidden[:, halves[1]], r.wup[1])
    d_resid = cot_wide + norm_back(d_normed, scaled, inv_std, row_of(r.ffn_gain))
    r.d_resid[rows, :] = d_resid
    branch = d_resid.astype(bf16)
    r.d_branch[rows, :] = branch
    for t in range(2):
        r.d_attended[rows, halves[t]] = dot_nt(branch, r.wproj[t]).astype(bf16)
    r.vectors[2:3, :] += column_sum(d_normed * scaled)
    r.vectors[3:4, :] += column_sum(d_normed)
    r.vectors[4:5, :] += column_sum(d_hidden.astype(f32))
    r.vectors[5:6, :] += column_sum(cot_wide)


def feed_grads(r, block):
    for t in range(2):
        half = slice(t * HALF_D, (t + 1) * HALF_D)
        if block == 0:
            r.fpart[t, 0] = dot_tn(r.normed_f[...], r.d_pre[:, half]).astype(bf16)
        else:
            left, right = (r.attended, r.d_branch) if block == 1 else (r.activated, r.cotangent)
            grad = dot_tn(left[:, half], right[...]).astype(bf16)
            r.fpart[t, block, :HALF_D, :] = grad[:, :HALF_D]
            r.fpart[t, block, HALF_D:, :] = grad[:, HALF_D:]


def finish_input(r, rows):
    d_normed = None
    for m in range(3):
        for t in range(2):
            at = m * D + t * HALF_D
            term = dot_nt(r.joined[rows, at : at + HALF_D], r.wqkv[t, m])
            d_normed = term if d_normed is None else d_normed + term
    scaled, inv_std = standardize(r.hidden[rows, :].astype(f32))
    grad = r.d_resid[rows, :] + norm_back(d_normed, scaled, inv_std, row_of(r.attn_gain))
    r.in_rows[rows, :] = grad.astype(bf16)
    r.vectors[0:1, :] += column_sum(d_normed * scaled)
    r.vectors[1:2, :] += column_sum(d_normed)


def pack_small(r):
    for v in range(6):
        for i in range(D // 128):
            at = VECTOR_ROWS + v * (D // 128) + i
            r.spart[at : at + 1, :] = r.vectors[v : v + 1, 128 * i : 128 * (i + 1)]
    r.spart[0:K, :] = r.acc_first[0:K, :]
    r.spart[SECOND_ROWS : SECOND_ROWS + H, :] = r.acc_second[:H, :K]
    r.spart[TABLE_ROWS : TABLE_ROWS + H, :HOT] = r.acc_second[H:, K : K + HOT]
    for index in range(2):
        rows = slice(TABLE_ROWS + ATOMS * index, TABLE_ROWS + ATOMS * (index + 1))
        r.spart[rows, HOT : HOT + ATOMS] = r.acc_table[index]
    ones = K + HOPS + EDGES
    r.spart[KERNEL_ROWS : KERNEL_ROWS + 1, :] = r.acc_first[ones : ones + 1, :]
    for index in range(2):
        column = jnp.sum(r.sums[index] * r.cols[4], axis=1, keepdims=True)
        same = iota((K, K), 0) == iota((K, K), 1)
        at = KERNEL_ROWS + 1 + index
        r.spart[at : at + 1, :] = jnp.sum(jnp.where(same, column, 0.0), axis=0, keepdims=True)


def layer_kernel(remote, names, *refs):
    r = SimpleNamespace(**dict(zip(names, refs)))
    tokens = r.hidden.shape[0]
    slots = tokens // SLOT
    chunk = min(256, tokens)
    peers = Peers()
    whole = [r.wqkv, r.wup, r.wproj, r.wdown]
    given = [r.given_qkv, r.given_up, r.given_proj, r.given_down]
    targets = [w.at[peers.tp] for w in whole] if remote else whole
    loads = [
        pltpu.make_async_copy(src, dst, r.load_sems.at[i])
        for i, (src, dst) in enumerate(
            [(r.given_hidden, r.hidden), (r.given_cotangent, r.cotangent)] + list(zip(given, targets))
        )
    ]
    for load in loads:
        load.start()

    def each_chunk(work):
        def one(c, _):
            work(r, span(c * chunk, chunk))
            return 0

        lax.fori_loop(0, tokens // chunk, one, 0)

    def move(slot, index, back):
        bank = lax.rem(slot, 2)
        far = (r.gauss_far, r.second_far, r.slope_far)[index].at[slot]
        near = (r.gauss, r.second, r.slope)[index].at[bank]
        pair = (far, near) if back else (near, far)
        return pltpu.make_async_copy(*pair, r.pair_sems.at[bank, index])

    def start_moves(slot, back):
        for index in range(3):
            move(slot, index, back).start()

    def wait_moves(slot, back):
        for index in range(3):
            move(slot, index, back).wait()

    if remote:
        gather = Gather(peers, given, whole, r.gather_sends, r.gather_recvs)
        ffn = Reduction(
            peers, r.fpart, r.ftotal, r.f_core, r.f_tp, r.f_x, r.f_z, r.f_sends, r.f_recvs
        )
        qkv = Reduction(
            peers, r.qpart, r.qtotal, r.q_core, r.q_tp, r.q_x, r.q_z, r.q_sends, r.q_recvs
        )
        small = SmallReduction(
            peers, r.spart, r.stotal, r.s_core, r.s_tp, r.s_x, r.s_z, r.s_sends, r.s_recvs
        )
        greet(peers.everyone())
        gather.start()

    def chain(reduction, time):
        def run():
            for b in range(3):
                if 1 <= time - b <= 8:
                    reduction.act(b, time - b)

        return run

    def at_time(index, plan):
        if remote:
            for k, steps in plan.items():

                @pl.when(index == k)
                def _(steps=steps):
                    for step in steps:
                        step()

    prepare_pairs(r)
    gather_plan = {}
    if remote:
        gather_plan = {
            1: [functools.partial(gather.onward_x, 0)],
            2: [functools.partial(gather.onward_x, 1), functools.partial(gather.onward_x, 2)],
            3: [functools.partial(gather.onward_x, 3), functools.partial(gather.onward_core, 0)],
            4: [functools.partial(gather.onward_core, i) for i in (1, 2)],
            5: [functools.partial(gather.onward_core, 3)],
        }

    def pairs(slot, _):
        pair_tables(r, slot)
        pl.when(slot >= 2)(lambda: wait_moves(slot - 2, False))
        pair_forward(r, slot)
        start_moves(slot, False)
        at_time(slot, gather_plan)
        return 0

    lax.fori_loop(0, slots, pairs, 0)
    loads[0].wait()
    loads[2].wait()
    if remote:
        gather.arrive(0)
    each_chunk(project)
    first_slot = peers.tp * slots

    def attend_one(s, _):
        attend(r, s, first_slot)
        return 0

    lax.fori_loop(0, slots, attend_one, 0)
    for load in [loads[1]] + loads[3:]:
        load.wait()
    if remote:
        for index in range(1, 4):
            gather.arrive(index)
    r.vectors[...] = jnp.zeros_like(r.vectors)
    each_chunk(feed)
    store_out = pltpu.make_async_copy(r.out_rows, r.output, r.store_sems.at[0])
    store_out.start()
    for slot in (slots - 2, slots - 1):
        wait_moves(slot, False)
    start_moves(0, True)
    start_moves(1, True)
    for block in range(3):
        feed_grads(r, block)
        if remote:
            ffn.act(block, 0)

    def back_one(s, _):
        attend_back(r, s)
        at_time(s, {k: [chain(ffn, k + 1)] for k in range(8)} if remote else {})
        return 0

    lax.fori_loop(0, slots, back_one, 0)
    for m in range(3):
        for t in range(2):
            at = m * D + t * HALF_D
            r.qpart[t, m] = dot_tn(r.normed_a[...], r.joined[:, at : at + HALF_D]).astype(bf16)
        if remote:
            qkv.act(m, 0)
    if remote:
        chain(ffn, 9)()
    each_chunk(finish_input)
    store_in = pltpu.make_async_copy(r.in_rows, r.grad_input, r.store_sems.at[1])
    store_in.start()
    if remote:
        chain(ffn, 10)()
        chain(qkv, 1)()
    for ref in (r.sums, r.acc_first, r.acc_second, r.acc_table, r.spart):
        ref[...] = jnp.zeros_like(ref)

    def pairs_back(slot, _):
        wait_moves(slot, True)
        pair_backward(r, slot, lambda: None)
        pl.when(slot + 2 < slots)(lambda: start_moves(slot + 2, True))
        at_time(slot, {k: [chain(qkv, k + 2)] for k in range(8)} if remote else {})
        return 0

    lax.fori_loop(0, slots, pairs_back, 0)
    pack_small(r)
    if remote:
        small.act(0)
        chain(qkv, 10)()
        for stage in range(1, 10):
            small.act(stage)
        gather.finish()
    store_out.wait()
    store_in.wait()


def layer(remote, group_slots, tokens, arrays):
    slots = tokens // SLOT
    part, total, rows = (2, 3, D, HALF_D), (3, D, HALF_D), (SMALL_ROWS, 128)
    whole = {"qkv": part, "up": (2, D, HALF_D), "proj": (2, HALF_D, D), "down": (2, HALF_D, D)}
    scalars = ("lengths", "flags")
    far = tuple("given_" + name for name in ("hidden", "cotangent", "qkv", "up", "proj", "down"))
    space = lambda name: pltpu.SMEM if name in scalars else pl.ANY if name in far else pltpu.VMEM
    in_names = list(arrays)
    outs = {
        "output": ((tokens, D), bf16), "grad_input": ((tokens, D), bf16), "gauss_far": ((slots, K, PAIRS), bf16),
        "second_far": ((slots, K, PAIRS), bf16), "slope_far": ((slots, K, PAIRS), bf16),
    }
    near = (
        {"ftotal": (total, bf16), "qtotal": (total, bf16), "stotal": (rows, f32)}
        if remote
        else {"fpart": (part, bf16), "qpart": (part, bf16), "spart": (rows, f32)}
    )
    v = pltpu.VMEM
    sem = pltpu.SemaphoreType.DMA
    tokens_d = lambda kind: v((tokens, D), kind)
    scratch = {
        "hidden": tokens_d(bf16), "cotangent": tokens_d(bf16), "wqkv": v(whole["qkv"], bf16),
        "wup": v(whole["up"], bf16), "wproj": v(whole["proj"], bf16), "wdown": v(whole["down"], bf16),
        "load_sems": sem((6,)), "pair_sems": sem((2, 3)), "store_sems": sem((2,)),
        "cols": v((5, K, 128), f32), "w1t": v((K, K), bf16), "w2": v((K, 128), bf16), "base": v((H, 256), f32),
        "lhs": v((H, 256), bf16), "argument": v((slots, HALF, 128), f32), "distance": v((slots, HALF, 128), f32),
        "hop_rows": v((slots, HALF, 128), f32), "edge_rows": v((slots, HALF, 128), f32),
        "atom_rows": v((slots, 8, 128), f32), "bias": v((slots, H * HALF, 128), f32),
        "gauss": v((2, K, PAIRS), bf16), "second": v((2, K, PAIRS), bf16), "slope": v((2, K, PAIRS), bf16),
        "normed_a": tokens_d(bf16), "joined": v((tokens, 3 * D), bf16), "prob": v((slots, SLOT, H * SLOT), bf16),
        "work": v((3, SLOT, D), f32), "attended": tokens_d(bf16), "normed_f": tokens_d(bf16),
        "activated": tokens_d(bf16), "out_rows": tokens_d(bf16), "d_pre": tokens_d(bf16), "d_resid": tokens_d(f32),
        "d_branch": tokens_d(bf16), "d_attended": tokens_d(bf16), "in_rows": tokens_d(bf16), "vectors": v((8, D), f32),
        "dfirst": v((K, PAIRS), bf16), "dspace": v((2 * H, PAIRS), bf16), "hots": v((HOT, PAIRS), bf16),
        "dargs": v((HALF, 128), f32), "sums": v((2, K, 128), f32), "acc_first": v((K + HOT, K), f32),
        "acc_second": v((2 * H, K + HOT), f32), "acc_table": v((2, ATOMS, ATOMS), f32),
    }
    if remote:
        scratch |= {"fpart": v(part, bf16), "qpart": v(part, bf16), "spart": v(rows, f32)}
        for name in ("f", "q"):
            keys = ("_core", "_tp", "_x", "_z", "_sends", "_recvs")
            scratch |= {name + key: item for key, item in zip(keys, big_scratch())}
        keys = ("s_core", "s_tp", "s_x", "s_z", "s_sends", "s_recvs")
        scratch |= dict(zip(keys, small_scratch()))
        scratch |= {"gather_sends": sem((4, 4)), "gather_recvs": sem((4, 4))}
    names = in_names + list(outs) + list(near) + list(scratch)
    results = pl.pallas_call(
        functools.partial(layer_kernel, remote, names),
        in_specs=[pl.BlockSpec(memory_space=space(name)) for name in in_names],
        out_specs=[pl.BlockSpec(memory_space=pl.ANY)] * len(outs) + vmem(len(near)),
        out_shape=[jax.ShapeDtypeStruct(*item) for item in list(outs.values()) + list(near.values())],
        scratch_shapes=list(scratch.values()),
        compiler_params=pltpu.CompilerParams(
            vmem_limit_bytes=VMEM_BYTES, **(dict(collective_id=0, has_side_effects=True) if remote else {})
        ),
        name="layer",
    )(*arrays.values())
    return results[0], results[1], results[len(outs) :]


def unpack_kernel(
    fsum_ref, qsum_ref, rows_ref,
    again, ashift, qkv, proj, fgain, fshift, up, up_bias, down, down_bias, scale, shift, centers, spreads,
    first, first_bias, second, hop, edge,
):
    qkv[...] = qsum_ref[...].astype(f32)
    up[...] = fsum_ref[0].astype(f32)
    for block, ref in ((1, proj), (2, down)):
        ref[:, :HALF_D] = fsum_ref[block, :HALF_D].astype(f32)
        ref[:, HALF_D:] = fsum_ref[block, HALF_D:].astype(f32)
    for v, ref in enumerate((again, ashift, fgain, fshift, up_bias, down_bias)):
        for i in range(D // 128):
            ref[pl.ds(128 * i, 128)] = rows_ref[VECTOR_ROWS + v * (D // 128) + i, :]
    first[...] = rows_ref[0:K, :]
    second[...] = rows_ref[SECOND_ROWS : SECOND_ROWS + H, :]
    table = rows_ref[TABLE_ROWS : TABLE_ROWS + H, :]
    scale[...] = table[:ATOMS, HOT : HOT + ATOMS]
    shift[...] = table[ATOMS:, HOT : HOT + ATOMS]
    turned = jnp.concatenate([table, jnp.zeros((128 - H, 128), f32)], axis=0).T
    hop[...] = turned[:HOPS, :H]
    edge[...] = turned[HOPS : HOPS + EDGES, :H]
    for i, ref in enumerate((first_bias, centers, spreads)):
        ref[...] = rows_ref[KERNEL_ROWS + i, :]


def unpack(fsum, qsum, rows):
    vec = jax.ShapeDtypeStruct((D,), f32)
    line = jax.ShapeDtypeStruct((K,), f32)
    mat = lambda *dims: jax.ShapeDtypeStruct(dims, f32)
    return pl.pallas_call(
        unpack_kernel,
        in_specs=vmem(3),
        out_specs=vmem(19),
        out_shape=[
            vec, vec, mat(3, D, HALF_D), mat(HALF_D, D), vec, vec, mat(D, HALF_D), vec, mat(HALF_D, D), vec,
            mat(ATOMS, ATOMS), mat(ATOMS, ATOMS), line, line, mat(K, K), line, mat(H, K), mat(HOPS, H), mat(EDGES, H),
        ],
        compiler_params=pltpu.CompilerParams(vmem_limit_bytes=VMEM_BYTES),
        name="unpack",
    )(fsum, qsum, rows)


def whole_weights(qkv_weight, up_weight, proj_weight, down_weight):
    columns = lambda w: jnp.stack(jnp.split(w, 2, axis=-1))
    rows = lambda w: jnp.stack(jnp.split(w, 2, axis=0))
    gather = lambda w, dim: lax.all_gather(w, "tp", axis=dim, tiled=True)
    return (
        columns(gather(qkv_weight.transpose(1, 0, 2), 2)), columns(gather(up_weight, 1)),
        rows(gather(proj_weight, 0)), rows(gather(down_weight, 0)),
    )


def sum_grads(fgrads, qgrads, small):
    total_f, total_q, rows = lax.psum((fgrads, qgrads, small), ("mol", "tp"))
    share = D // lax.axis_size("tp")
    at = lax.axis_index("tp") * share
    columns = lambda w: lax.dynamic_slice_in_dim(jnp.concatenate([w[0], w[1]], axis=-1), at, share, w.ndim - 2)
    rows_of = lambda w: lax.dynamic_slice_in_dim(
        jnp.concatenate([jnp.concatenate([w[t, :HALF_D], w[t, HALF_D:]], axis=1) for t in range(2)]), at, share, 0
    )
    wide = lambda v: v.astype(f32)
    big = (wide(columns(total_q)), wide(columns(total_f[:, 0])), wide(rows_of(total_f[:, 1])), wide(rows_of(total_f[:, 2])))
    return big, rows


def body(
    mesh_shape,
    hidden_in, positions, atom_types, hop_counts, edge_types, lengths, branches,
    attn_gain, attn_shift, qkv_weight, proj_weight, ffn_gain, ffn_shift, up_weight, up_bias, down_weight, down_bias,
    kernel_scale, kernel_shift, centers, spreads, first_weight, first_bias, second_weight, hop_table, edge_table,
    cotangent,
):
    remote = mesh_shape["tp"] == 2 and mesh_shape["mol"] == 16
    if remote:
        weights = (qkv_weight.transpose(1, 0, 2), up_weight, proj_weight, down_weight)
    else:
        weights = whole_weights(qkv_weight, up_weight, proj_weight, down_weight)
    arrays = dict(
        lengths=lengths, flags=branches.T, positions=positions, atoms=atom_types, hops=hop_counts.T,
        edges=edge_types.T, kernel_scale=kernel_scale, kernel_shift=kernel_shift, centers=centers, spreads=spreads,
        first_weight=first_weight, first_bias=first_bias, second_weight=second_weight.T, hop_table=hop_table,
        edge_table=edge_table, attn_gain=attn_gain, attn_shift=attn_shift, ffn_gain=ffn_gain, ffn_shift=ffn_shift,
        up_bias=up_bias, down_bias=down_bias, given_hidden=hidden_in, given_cotangent=cotangent,
        given_qkv=weights[0], given_up=weights[1], given_proj=weights[2], given_down=weights[3],
    )
    output, grad_input, sums = layer(remote, lengths.shape[0], hidden_in.shape[0], arrays)
    if remote:
        fsum, qsum, rows = sums
    else:
        big, rows = sum_grads(*sums)
        fsum = jnp.zeros((3, D, HALF_D), bf16)
        qsum = fsum
    grads = list(unpack(fsum, qsum, rows))
    if not remote:
        grads[2], grads[6], grads[3], grads[8] = big
    grads[2] = grads[2].transpose(1, 0, 2)
    grads[16] = grads[16].T
    return (output, grad_input, *grads)


def solution(mesh):
    rows = P(("mol", "tp"), None)
    all_of = P()
    in_specs = (
        rows, P(None, ("mol", "tp")), P(("mol", "tp")), rows, rows, P("mol"), rows, all_of, all_of,
        P(None, None, "tp"), P("tp", None), all_of, all_of, P(None, "tp"), all_of, P("tp", None),
    ) + (all_of,) * 10 + (rows,)
    out_specs = (
        rows, rows, all_of, all_of, P(None, None, "tp"), P("tp", None), all_of, all_of, P(None, "tp"), all_of,
        P("tp", None),
    ) + (all_of,) * 10
    step = functools.partial(body, dict(mesh.shape))
    return jax.shard_map(step, mesh=mesh, in_specs=in_specs, out_specs=out_specs, check_vma=False)
```

```python
import functools
from types import SimpleNamespace

import jax
import jax.numpy as jnp
from jax import lax
from jax.experimental import pallas as pl
from jax.experimental.pallas import tpu as pltpu
from jax.sharding import PartitionSpec as P

D = 768
H = 32
HD = 24
FF = 768
K = 128
SLOT = 64
HALF = SLOT // 2
HALF_D = D // 2
PAIRS = SLOT * SLOT
HOPS = 16
EDGES = 8
ATOMS = 16
GROUP = 4
GROUPS = H // GROUP
HOT = 32

highest = lax.Precision.HIGHEST
neg_large = -1e30
root_tau = 2.5066282746310002
root_half = 0.7071067811865476
inv_root_tau = 0.3989422804014327
head_scale = HD ** (-0.5)
VMEM_BYTES = 62 * 1024 * 1024
TILE = 512

SECOND_ROWS = K
TABLE_ROWS = SECOND_ROWS + H
KERNEL_ROWS = TABLE_ROWS + H
VECTOR_ROWS = KERNEL_ROWS + 8
SMALL_ROWS = 256

MESH = pl.DeviceIdType.MESH
f32 = jnp.float32
bf16 = jnp.bfloat16


def dot_nn(left, right, precision=None):
    return lax.dot_general(left, right, (((1,), (0,)), ((), ())), precision=precision, preferred_element_type=f32)


def dot_nt(left, right, precision=None):
    return lax.dot_general(left, right, (((1,), (1,)), ((), ())), precision=precision, preferred_element_type=f32)


def dot_tn(left, right, precision=None):
    return lax.dot_general(left, right, (((0,), (0,)), ((), ())), precision=precision, preferred_element_type=f32)


def iota(shape, dim):
    return lax.broadcasted_iota(jnp.int32, shape, dim)


def gelu_parts(values):
    size = jnp.abs(values)
    bell = jnp.exp(values * values * -0.5)
    denominator = 1.0 + (0.3275911 * root_half) * size
    t = pl.reciprocal(denominator, approx=True)
    t = t * (2.0 - denominator * t)
    series = 0.5 * 1.061405429
    for factor in (-1.453152027, 1.421413741, -0.284496736, 0.254829592):
        series = series * t + 0.5 * factor
    tail = series * t * bell
    gelu = jnp.maximum(values, 0.0) - size * tail
    outer = tail - size * (bell * inv_root_tau)
    return gelu, jnp.where(values >= 0.0, 1.0 - outer, outer)


def to_column(row):
    size = row.shape[1]
    same = iota((size, size), 0) == iota((size, size), 1)
    return jnp.sum(jnp.where(same, row, 0.0), axis=1, keepdims=True)


def half_swap(values):
    return pltpu.roll(values, 64, 1)


def low_lanes(rows):
    return iota((rows, 128), 1) < 64


def vmem(count):
    return [pl.BlockSpec(memory_space=pltpu.VMEM)] * count


def row_of(ref):
    return ref[...].reshape(1, ref.shape[0])


def place():
    mol = lax.axis_index("mol")
    return mol % 2, (mol // 2) % 2, mol // 4, lax.axis_index("tp")


def greet(peers):
    barrier = pltpu.get_barrier_semaphore()
    for peer in peers:
        pl.semaphore_signal(barrier, inc=1, device_id=peer, device_id_type=MESH)
    pl.semaphore_wait(barrier, len(peers))


def window(group):
    first = GROUP * HD * group
    start = first // 128 * 128
    width = 128 if first - start + GROUP * HD <= 128 else 256
    return start, width, first - start


def head_masks(group, kind):
    _, width, offset = window(group)
    lane = iota((1, width), 1)
    return [
        ((lane >= offset + HD * h) & (lane < offset + HD * (h + 1))).astype(f32).astype(kind) for h in range(GROUP)
    ]


def spread_heads(values, group):
    return jnp.concatenate([values * mask for mask in head_masks(group, bf16)], axis=0)


def gather_heads(values, group):
    masks = head_masks(group, f32)
    total = values[:SLOT] * masks[0]
    for h in range(1, GROUP):
        total = total + values[SLOT * h : SLOT * (h + 1)] * masks[h]
    return total


def standardize(values):
    centred = values - jnp.mean(values, axis=-1, keepdims=True)
    inv_std = lax.rsqrt(jnp.mean(centred * centred, axis=-1, keepdims=True) + 1e-05)
    return centred * inv_std, inv_std


def norm_back(d_normed, scaled, inv_std, gain):
    weighted = d_normed * gain
    inner_a = jnp.mean(weighted, axis=-1, keepdims=True)
    inner_b = jnp.mean(weighted * scaled, axis=-1, keepdims=True)
    return inv_std * (weighted - inner_a - scaled * inner_b)


def column_sum(values):
    return jnp.sum(values, axis=0, keepdims=True)


class Peers:
    def __init__(self):
        self.core, self.x, self.z, self.tp = place()
        mol = lax.axis_index("mol")
        self.over_core = {"mol": mol + 1 - 2 * self.core}
        self.over_x = {"mol": mol + 2 - 4 * self.x}
        self.over_tp = {"tp": 1 - self.tp}
        self.turn = [lax.rem(self.z + d, 4) for d in range(4)]
        self.over_z = [{"mol": self.turn[d] * 4 + self.x * 2 + self.core} for d in range(4)]

    def neighbour(self, k):
        core = self.core + (1 - 2 * self.core) * (k & 1)
        x = self.x + (1 - 2 * self.x) * (k >> 1 & 1)
        tp = self.tp + (1 - 2 * self.tp) * (k >> 2)
        return core * 4 + tp * 2 + x, {"mol": self.z * 4 + x * 2 + core, "tp": tp}

    def everyone(self):
        return [self.neighbour(k)[1] for k in range(1, 8)] + self.over_z[1:]


def span(start, size):
    return pl.ds(pl.multiple_of(start, size), size)


def add_rows(target, source, rows):
    step = 96 if rows % 96 == 0 else rows

    def piece(i, _):
        at = pl.ds(pl.multiple_of(i * step, step), step)
        target[at, :] = (target[at, :].astype(f32) + source[at, :].astype(f32)).astype(target.dtype)
        return 0

    lax.fori_loop(0, rows // step, piece, 0)


class Reduction:
    def __init__(self, peers, part, total, from_core, from_tp, from_x, from_z, sends, recvs):
        self.peers, self.part, self.total = peers, part, total
        self.from_core, self.from_tp, self.from_x, self.from_z = from_core, from_tp, from_x, from_z
        self.sends, self.recvs = sends, recvs
        p = peers
        self.at_core = p.core * 384
        self.at_x = self.at_core + p.x * 192

    def copy(self, b, kind):
        p = self.peers
        part, total = self.part, self.total
        if kind == 0:
            src, dst, peer = part.at[:, b, span((1 - p.core) * 384, 384)], self.from_core.at[:, b], p.over_core
        elif kind == 1:
            src, dst, peer = part.at[1 - p.tp, b, span(self.at_core, 384)], self.from_tp.at[b], p.over_tp
        elif kind == 2:
            src, dst, peer = part.at[p.tp, b, span(self.at_core + (1 - p.x) * 192, 192)], self.from_x.at[b], p.over_x
        elif kind < 6:
            d = kind - 2
            src, dst, peer = part.at[p.tp, b, span(self.at_x + p.turn[d] * 48, 48)], self.from_z.at[b, d - 1], p.over_z[d]
        elif kind < 9:
            src = dst = total.at[b, span(self.at_x + p.z * 48, 48)]
            peer = p.over_z[kind - 5]
        elif kind == 9:
            src = dst = total.at[b, span(self.at_x, 192)]
            peer = p.over_x
        else:
            src = dst = total.at[b, span(self.at_core, 384)]
            peer = p.over_core
        return pltpu.make_async_remote_copy(
            src_ref=src, dst_ref=dst, send_sem=self.sends.at[b, kind], recv_sem=self.recvs.at[b, kind],
            device_id=peer, device_id_type=MESH,
        )

    def act(self, b, stage):
        p = self.peers
        if stage == 0:
            self.copy(b, 0).start()
        elif stage == 1:
            self.copy(b, 0).wait_recv()
            add_rows(self.part.at[1 - p.tp, b, span(self.at_core, 384)], self.from_core.at[1 - p.tp, b], 384)
            self.copy(b, 1).start()
            add_rows(self.part.at[p.tp, b, span(self.at_core, 384)], self.from_core.at[p.tp, b], 384)
        elif stage == 2:
            self.copy(b, 1).wait_recv()
            away, mine = (1 - p.x) * 192, p.x * 192
            add_rows(self.part.at[p.tp, b, span(self.at_core + away, 192)], self.from_tp.at[b, span(away, 192)], 192)
            self.copy(b, 2).start()
            add_rows(self.part.at[p.tp, b, span(self.at_core + mine, 192)], self.from_tp.at[b, span(mine, 192)], 192)
        elif stage == 3:
            self.copy(b, 2).wait_recv()
            add_rows(self.part.at[p.tp, b, span(self.at_x, 192)], self.from_x.at[b], 192)
            for kind in (3, 4, 5):
                self.copy(b, kind).start()
        elif stage == 4:
            for kind in (3, 4, 5):
                self.copy(b, kind).wait_recv()
            mine = span(self.at_x + p.z * 48, 48)
            value = self.part[p.tp, b, mine, :].astype(f32)
            for d in range(3):
                value = value + self.from_z[b, d].astype(f32)
            self.total[b, mine, :] = value.astype(bf16)
            for kind in (6, 7, 8):
                self.copy(b, kind).start()
        elif stage == 5:
            for kind in (6, 7, 8):
                self.copy(b, kind).wait_recv()
            self.copy(b, 9).start()
        elif stage == 6:
            self.copy(b, 9).wait_recv()
            self.copy(b, 10).start()
        elif stage == 7:
            self.copy(b, 10).wait_recv()
        else:
            for kind in range(11):
                self.copy(b, kind).wait_send()


class SmallReduction:
    def __init__(self, peers, part, total, from_near, from_z, sends, recvs):
        self.peers, self.part, self.total, self.from_near, self.from_z = peers, part, total, from_near, from_z
        self.sends, self.recvs = sends, recvs
        p = peers
        self.near = [p.neighbour(k) for k in range(8)]
        self.at_near = self.near[0][0] * 32

    def copy(self, kind):
        p = self.peers
        part, total = self.part, self.total
        if kind < 7:
            index, peer = self.near[kind + 1]
            src, dst = part.at[span(index * 32, 32)], self.from_near.at[kind]
        elif kind < 10:
            d = kind - 6
            src, dst, peer = part.at[span(self.at_near + p.turn[d] * 8, 8)], self.from_z.at[d - 1], p.over_z[d]
        elif kind < 13:
            src = dst = total.at[span(self.at_near + p.z * 8, 8)]
            peer = p.over_z[kind - 9]
        else:
            src = dst = total.at[span(self.at_near, 32)]
            peer = self.near[kind - 12][1]
        return pltpu.make_async_remote_copy(
            src_ref=src, dst_ref=dst, send_sem=self.sends.at[kind], recv_sem=self.recvs.at[kind],
            device_id=peer, device_id_type=MESH,
        )

    def act(self, stage):
        p = self.peers
        hops = (range(0, 7), range(7, 10), range(10, 13), range(13, 20))
        if stage == 5:
            for kind in range(20):
                self.copy(kind).wait_send()
            return
        if stage > 0:
            for kind in hops[stage - 1]:
                self.copy(kind).wait_recv()
        if stage == 1:
            mine = span(self.at_near, 32)
            value = self.part[mine, :]
            for k in range(7):
                value = value + self.from_near[k]
            self.part[mine, :] = value
        elif stage == 2:
            mine = span(self.at_near + p.z * 8, 8)
            self.total[mine, :] = self.part[mine, :] + self.from_z[0] + self.from_z[1] + self.from_z[2]
        if stage < 4:
            for kind in hops[stage]:
                self.copy(kind).start()


def big_scratch():
    return [
        pltpu.VMEM((2, 3, 384, HALF_D), bf16), pltpu.VMEM((3, 384, HALF_D), bf16), pltpu.VMEM((3, 192, HALF_D), bf16),
        pltpu.VMEM((3, 3, 48, HALF_D), bf16), pltpu.SemaphoreType.DMA((3, 11)), pltpu.SemaphoreType.DMA((3, 11)),
    ]


def small_scratch():
    return [
        pltpu.VMEM((7, 32, 128), f32), pltpu.VMEM((3, 8, 128), f32),
        pltpu.SemaphoreType.DMA((20,)), pltpu.SemaphoreType.DMA((20,)),
    ]


class Gather:
    pieces = 6

    def __init__(self, peers, own, whole, sends, recvs):
        self.peers, self.own, self.whole, self.sends, self.recvs = peers, own, whole, sends, recvs
        self.quarter = peers.x * 2 + peers.core
        self.next_quarter = (1 - peers.x) * 2 + peers.core

    def rows(self, ref, quarter):
        count = ref.shape[0] // 4
        return ref.at[span(quarter * count, count), :]

    def copy(self, index, kind):
        p = self.peers
        if kind == 0:
            src = self.rows(self.own(index), self.quarter)
            dst, peer = self.rows(self.whole(index, p.tp), self.quarter), p.over_tp
        elif kind == 1:
            src = dst = self.rows(self.whole(index, 1 - p.tp), self.quarter)
            peer = p.over_x
        else:
            src = dst = self.rows(self.whole(index, 1 - p.tp), self.quarter if kind == 2 else self.next_quarter)
            peer = p.over_core
        return pltpu.make_async_remote_copy(
            src_ref=src, dst_ref=dst, send_sem=self.sends.at[index, kind], recv_sem=self.recvs.at[index, kind],
            device_id=peer, device_id_type=MESH,
        )

    def start(self):
        for index in range(self.pieces):
            self.copy(index, 0).start()

    def onward_x(self, index):
        self.copy(index, 0).wait_recv()
        self.copy(index, 1).start()
        self.copy(index, 2).start()

    def onward_core(self, index):
        self.copy(index, 1).wait_recv()
        self.copy(index, 3).start()

    def arrive(self, index):
        self.copy(index, 2).wait_recv()
        self.copy(index, 3).wait_recv()

    def finish(self):
        for index in range(self.pieces):
            for kind in range(4):
                self.copy(index, kind).wait_send()


def widen(values):
    return jnp.concatenate([values] * (TILE // 128), axis=1)


def strips():
    return [slice(16 * i, 16 * (i + 1)) for i in range(K // 16)]


def four_rows(ref, slot, first):
    return jnp.concatenate([ref[slot, pl.ds(first + i, 1), :] for i in range(TILE // 128)], axis=1)


def hot_rows(values, count):
    return (values == iota((count, TILE), 0).astype(f32)).astype(f32)


def fold_lanes(values):
    total = values[:, :128]
    for i in range(1, TILE // 128):
        total = total + values[:, 128 * i : 128 * (i + 1)]
    return total


def prepare_pairs(r):
    spr = to_column(row_of(r.spreads))
    r.cols[0] = jnp.broadcast_to(to_column(row_of(r.centers)), (K, 128))
    r.cols[1] = jnp.broadcast_to(root_half / spr, (K, 128))
    r.cols[2] = jnp.broadcast_to(-jnp.log(root_tau * spr), (K, 128))
    r.cols[3] = jnp.broadcast_to(to_column(row_of(r.first_bias)), (K, 128))
    r.cols[4] = jnp.broadcast_to(1.0 / spr, (K, 128))
    r.w1t[...] = r.first_weight[...].astype(f32).T.astype(bf16)
    second = r.second_weight[...].astype(f32)
    r.w2[...] = jnp.concatenate([second, jnp.zeros((128 - H, K), f32)], axis=0).T.astype(bf16)
    table = jnp.concatenate([r.hop_table[...], r.edge_table[...], jnp.zeros((128 - HOPS - EDGES, H), f32)], axis=0)
    table = jnp.concatenate([table, jnp.zeros((128, 128 - H), f32)], axis=1).T[:H, :HOT]
    one = table.astype(bf16).astype(f32)
    two = (table - one).astype(bf16).astype(f32)
    three = table - one - two
    r.base[...] = jnp.concatenate([second, one, two, three, jnp.zeros((H, 32), f32)], axis=1)


def pair_tables(r, slot):
    low = low_lanes(HALF)
    low_row = low_lanes(1)
    lanes = span(lax.div(slot, 2) * 128, 128)
    turn = lax.rem(slot, 2) * 64
    atoms = r.atoms[lanes].astype(f32).reshape(1, 128)
    rows = [pltpu.roll(row, turn, 1) for row in [r.positions[c : c + 1, lanes] for c in range(3)] + [atoms]]
    double = [jnp.where(low_row, row, half_swap(row)) for row in rows]
    columns = [to_column(row[:, :SLOT]) for row in rows]
    total = None
    for c in range(3):
        offset = jnp.where(low, columns[c][:HALF], columns[c][HALF:]) - double[c]
        total = offset * offset if total is None else total + offset * offset
    distance = jnp.sqrt(total)
    key_hot = (columns[3] == iota((SLOT, ATOMS), 1).astype(f32)).astype(f32)
    query_hot = (double[3] == iota((ATOMS, 128), 0).astype(f32)).astype(f32)
    picked = []
    for table in (r.kernel_scale, r.kernel_shift):
        both = dot_nn(dot_nt(key_hot, table[...], highest), query_hot, highest)
        picked.append(jnp.where(low, both[:HALF], both[HALF:]))
    r.argument[slot] = picked[0] * distance + picked[1]
    r.distance[slot] = distance
    for source, target in ((r.hops, r.hop_rows), (r.edges, r.edge_rows)):
        values = pltpu.roll(source[:, lanes].astype(f32), turn, 1)
        target[slot] = jnp.where(low, values[:HALF], half_swap(values[HALF:]))
    r.atom_rows[slot] = jnp.broadcast_to(double[3], (8, 128))


def pair_forward(r, slot):
    bank = lax.rem(slot, 2)
    graph_on = r.flags[0, slot].astype(f32)
    space_on = r.flags[1, slot].astype(f32)
    factor = jnp.where(iota((H, 256), 1) < K, space_on, graph_on)
    r.lhs[...] = (r.base[...] * factor).astype(bf16)

    def tile(t, _):
        for part in range(2):
            first_row = 8 * t + 4 * part
            where = span(t * 2 * TILE + part * TILE, TILE)
            arg = four_rows(r.argument, slot, first_row)
            pieces = []
            for rows in strips():
                u = (arg - widen(r.cols[0, rows])) * widen(r.cols[1, rows])
                pieces.append(jnp.exp(widen(r.cols[2, rows]) - u * u).astype(bf16))
                r.gauss[bank, rows, where] = pieces[-1]
            first = dot_nn(r.w1t[...], jnp.concatenate(pieces, axis=0))
            pieces = []
            for rows in strips():
                value, slope = gelu_parts(first[rows] + widen(r.cols[3, rows]))
                pieces.append(value.astype(bf16))
                r.second[bank, rows, where] = pieces[-1]
                r.slope[bank, rows, where] = slope.astype(bf16)
            hot = jnp.concatenate(
                [
                    hot_rows(four_rows(r.hop_rows, slot, first_row), HOPS),
                    hot_rows(four_rows(r.edge_rows, slot, first_row), HOT - HOPS),
                ],
                axis=0,
            ).astype(bf16)
            bias = dot_nn(r.lhs[:, : K + 3 * HOT], jnp.concatenate(pieces + [hot] * 3, axis=0))
            bias = bias.astype(bf16).astype(f32)
            for i in range(TILE // 128):
                r.bias[slot, pl.ds(first_row + i, H, stride=HALF), :] = bias[:, 128 * i : 128 * (i + 1)]
        return 0

    lax.fori_loop(0, PAIRS // (2 * TILE), tile, 0)


def pair_backward(r, slot, between):
    bank = lax.rem(slot, 2)
    graph_on = r.flags[0, slot].astype(f32)
    space_on = r.flags[1, slot].astype(f32)
    w2 = r.w2[:, :H] * space_on.astype(bf16)

    def tile(t, _):
        for part in range(2):
            first_row = 8 * t + 4 * part
            where = span(t * 2 * TILE + part * TILE, TILE)
            arg = four_rows(r.argument, slot, first_row)
            grad = jnp.concatenate(
                [r.bias[slot, pl.ds(first_row + i, H, stride=HALF), :] for i in range(TILE // 128)], axis=1
            )
            r.dspace[:, where] = jnp.concatenate([grad * space_on, grad * graph_on], axis=0).astype(bf16)
            d_second = dot_nn(w2, grad.astype(bf16))
            pieces = []
            for rows in strips():
                pieces.append((d_second[rows] * r.slope[bank, rows, where].astype(f32)).astype(bf16))
                r.dfirst[rows, where] = pieces[-1]
            d_gauss = dot_nn(r.first_weight[...], jnp.concatenate(pieces, axis=0))
            d_arg = None
            for rows in strips():
                inv = widen(r.cols[4, rows])
                u = (arg - widen(r.cols[0, rows])) * inv
                q = d_gauss[rows] * r.gauss[bank, rows, where].astype(f32)
                w = q * u
                r.sums[0, rows] += fold_lanes(w)
                r.sums[1, rows] += fold_lanes(w * u - q)
                w = w * inv
                w = w[:8] + w[8:]
                d_arg = w if d_arg is None else d_arg + w
            d_arg = -jnp.sum(d_arg, axis=0, keepdims=True)
            for i in range(TILE // 128):
                r.dargs[pl.ds(first_row + i, 1), :] = d_arg[:, 128 * i : 128 * (i + 1)]
            edge_hot = hot_rows(four_rows(r.edge_rows, slot, first_row), HOT - HOPS)
            edge_hot = jnp.where(iota((HOT - HOPS, TILE), 0) == EDGES, 1.0, edge_hot)
            r.hots[:, where] = jnp.concatenate(
                [hot_rows(four_rows(r.hop_rows, slot, first_row), HOPS), edge_hot], axis=0
            ).astype(bf16)
        return 0

    lax.fori_loop(0, PAIRS // (2 * TILE), tile, 0)
    between()
    left = jnp.concatenate([r.gauss[bank], r.second[bank], r.hots[...]], axis=0)
    r.acc_mixed[...] += dot_nt(left, jnp.concatenate([r.dfirst[...], r.dspace[...]], axis=0))
    query_hot = (r.atom_rows[slot, 0:1, :] == iota((ATOMS, 128), 0).astype(f32)).astype(f32)
    for index in range(2):
        values = r.dargs[...] * r.distance[slot] if index == 0 else r.dargs[...]
        part = jnp.where(
            low_lanes(ATOMS),
            dot_nn(query_hot[:, :HALF], values, highest),
            dot_nn(query_hot[:, HALF:SLOT], values, highest),
        )
        r.acc_table[index] += dot_nt(query_hot, part, highest)


def attend(r, s, first_slot):
    low = low_lanes(HALF)
    rows = span(s * SLOT, SLOT)
    valid = iota((SLOT, GROUP * SLOT), 0) < r.lengths[first_slot + s]
    r.work[0] = jnp.zeros((SLOT, D), f32)
    for g in range(GROUPS):
        start, width, _ = window(g)
        q = r.joined[rows, start : start + width]
        k = r.joined[rows, D + start : D + start + width]
        v = r.joined[rows, 2 * D + start : 2 * D + start + width]
        scores = dot_nt(k, spread_heads(q, g)) * head_scale
        parts = []
        for pair in range(GROUP // 2):
            head = GROUP * g + 2 * pair
            one = r.bias[s, head * HALF : (head + 1) * HALF, :]
            two = r.bias[s, (head + 1) * HALF : (head + 2) * HALF, :]
            top = jnp.where(low, one, half_swap(two))
            bottom = jnp.where(low, half_swap(one), two)
            parts.append(jnp.concatenate([top, bottom], axis=0))
        scores = jnp.where(valid, scores + jnp.concatenate(parts, axis=1), neg_large)
        weights = jnp.exp(scores - jnp.max(scores, axis=0, keepdims=True))
        prob = (weights * (1.0 / jnp.sum(weights, axis=0, keepdims=True))).astype(bf16)
        r.prob[s, :, g * GROUP * SLOT : (g + 1) * GROUP * SLOT] = prob
        r.work[0, :, start : start + width] += gather_heads(dot_tn(prob, v), g)
    r.attended[rows, :] = r.work[0].astype(bf16)


def attend_back(r, s):
    low = low_lanes(HALF)
    rows = span(s * SLOT, SLOT)
    r.work[...] = jnp.zeros((3, SLOT, D), f32)
    for g in range(GROUPS):
        start, width, _ = window(g)
        lanes = slice(start, start + width)
        k = r.joined[rows, D + start : D + start + width]
        v = r.joined[rows, 2 * D + start : 2 * D + start + width]
        q_heads = spread_heads(r.joined[rows, lanes], g)
        d_heads = spread_heads(r.d_attended[rows, lanes], g)
        prob = r.prob[s, :, g * GROUP * SLOT : (g + 1) * GROUP * SLOT]
        wide = prob.astype(f32)
        d_prob = dot_nt(v, d_heads)
        inner = jnp.sum(wide * d_prob, axis=0, keepdims=True)
        d_scores = (wide * (d_prob - inner)).astype(bf16)
        r.work[0, :, lanes] += gather_heads(dot_tn(d_scores, k), g)
        r.work[1, :, lanes] += dot_nn(d_scores, q_heads)
        r.work[2, :, lanes] += dot_nn(prob, d_heads)
        d_wide = d_scores.astype(f32)
        for pair in range(GROUP // 2):
            head = GROUP * g + 2 * pair
            top = d_wide[:HALF, 128 * pair : 128 * (pair + 1)]
            bottom = d_wide[HALF:, 128 * pair : 128 * (pair + 1)]
            r.bias[s, head * HALF : (head + 1) * HALF, :] = jnp.where(low, top, half_swap(bottom))
            r.bias[s, (head + 1) * HALF : (head + 2) * HALF, :] = jnp.where(low, half_swap(top), bottom)
    r.joined[rows, 0:D] = (r.work[0] * head_scale).astype(bf16)
    r.joined[rows, D : 2 * D] = (r.work[1] * head_scale).astype(bf16)
    r.joined[rows, 2 * D : 3 * D] = r.work[2].astype(bf16)


def project(r, rows):
    scaled, _ = standardize(r.hidden[rows, :].astype(f32))
    normed = (scaled * row_of(r.attn_gain) + row_of(r.attn_shift)).astype(bf16)
    r.normed_a[rows, :] = normed
    for m in range(3):
        for t in range(2):
            at = m * D + t * HALF_D
            r.joined[rows, at : at + HALF_D] = dot_nn(normed, r.wqkv[t, m]).astype(bf16)


def feed(r, rows):
    halves = [slice(0, HALF_D), slice(HALF_D, D)]
    resid = r.hidden[rows, :].astype(f32)
    for t in range(2):
        resid = resid + dot_nn(r.attended[rows, halves[t]], r.wproj[t])
    scaled, inv_std = standardize(resid)
    normed = (scaled * row_of(r.ffn_gain) + row_of(r.ffn_shift)).astype(bf16)
    r.normed_f[rows, :] = normed
    pre = jnp.concatenate([dot_nn(normed, r.wup[t]) for t in range(2)], axis=1)
    value, slope = gelu_parts(pre + row_of(r.up_bias))
    active = value.astype(bf16)
    r.activated[rows, :] = active
    result = resid + row_of(r.down_bias)
    for t in range(2):
        result = result + dot_nn(active[:, halves[t]], r.wdown[t])
    r.out_rows[rows, :] = result.astype(bf16)
    cot = r.cotangent[rows, :]
    cot_wide = cot.astype(f32)
    d_active = jnp.concatenate([dot_nt(cot, r.wdown[t]) for t in range(2)], axis=1)
    d_hidden = (d_active * slope).astype(bf16)
    r.d_pre[rows, :] = d_hidden
    d_normed = dot_nt(d_hidden[:, halves[0]], r.wup[0]) + dot_nt(d_hidden[:, halves[1]], r.wup[1])
    d_resid = cot_wide + norm_back(d_normed, scaled, inv_std, row_of(r.ffn_gain))
    r.d_resid[rows, :] = d_resid
    branch = d_resid.astype(bf16)
    r.d_branch[rows, :] = branch
    for t in range(2):
        r.d_attended[rows, halves[t]] = dot_nt(branch, r.wproj[t]).astype(bf16)
    r.vectors[2:3, :] += column_sum(d_normed * scaled)
    r.vectors[3:4, :] += column_sum(d_normed)
    r.vectors[4:5, :] += column_sum(d_hidden.astype(f32))
    r.vectors[5:6, :] += column_sum(cot_wide)


def feed_grads(r, block):
    for t in range(2):
        half = slice(t * HALF_D, (t + 1) * HALF_D)
        if block == 0:
            r.fpart[t, 0] = dot_tn(r.normed_f[...], r.d_pre[:, half]).astype(bf16)
        else:
            left, right = (r.attended, r.d_branch) if block == 1 else (r.activated, r.cotangent)
            grad = dot_tn(left[:, half], right[...]).astype(bf16)
            r.fpart[t, block, :HALF_D, :] = grad[:, :HALF_D]
            r.fpart[t, block, HALF_D:, :] = grad[:, HALF_D:]


def finish_input(r, rows):
    d_normed = None
    for m in range(3):
        for t in range(2):
            at = m * D + t * HALF_D
            term = dot_nt(r.joined[rows, at : at + HALF_D], r.wqkv[t, m])
            d_normed = term if d_normed is None else d_normed + term
    scaled, inv_std = standardize(r.hidden[rows, :].astype(f32))
    grad = r.d_resid[rows, :] + norm_back(d_normed, scaled, inv_std, row_of(r.attn_gain))
    r.in_rows[rows, :] = grad.astype(bf16)
    r.vectors[0:1, :] += column_sum(d_normed * scaled)
    r.vectors[1:2, :] += column_sum(d_normed)


def square_turn(values):
    rows, lanes = values.shape
    if lanes < 128:
        values = jnp.concatenate([values, jnp.zeros((rows, 128 - lanes), f32)], axis=1)
    if rows < 128:
        values = jnp.concatenate([values, jnp.zeros((128 - rows, 128), f32)], axis=0)
    return values.T


def pack_small(r):
    for v in range(6):
        for i in range(D // 128):
            at = VECTOR_ROWS + v * (D // 128) + i
            r.spart[at : at + 1, :] = r.vectors[v : v + 1, 128 * i : 128 * (i + 1)]
    r.spart[0:K, :] = r.acc_mixed[0:K, :K]
    r.spart[SECOND_ROWS : SECOND_ROWS + H, :] = square_turn(r.acc_mixed[K : 2 * K, K:])[:H]
    r.spart[TABLE_ROWS : TABLE_ROWS + H, :HOT] = square_turn(r.acc_mixed[2 * K :, K:])[H : 2 * H, :HOT]
    for index in range(2):
        rows = slice(TABLE_ROWS + ATOMS * index, TABLE_ROWS + ATOMS * (index + 1))
        r.spart[rows, HOT : HOT + ATOMS] = r.acc_table[index]
    ones = 2 * K + HOPS + EDGES
    r.spart[KERNEL_ROWS : KERNEL_ROWS + 1, :] = r.acc_mixed[ones : ones + 1, :K]
    for index in range(2):
        column = jnp.sum(r.sums[index] * r.cols[4], axis=1, keepdims=True)
        same = iota((K, K), 0) == iota((K, K), 1)
        at = KERNEL_ROWS + 1 + index
        r.spart[at : at + 1, :] = jnp.sum(jnp.where(same, column, 0.0), axis=0, keepdims=True)


def layer_kernel(remote, names, *refs):
    r = SimpleNamespace(**dict(zip(names, refs)))
    tokens = r.hidden.shape[0]
    slots = tokens // SLOT
    chunk = min(256, tokens)
    peers = Peers()
    whole = [r.wqkv, r.wup, r.wproj, r.wdown]
    given = [r.given_qkv, r.given_up, r.given_proj, r.given_down]
    targets = [w.at[peers.tp] for w in whole] if remote else whole
    loads = [
        pltpu.make_async_copy(src, dst, r.load_sems.at[i])
        for i, (src, dst) in enumerate(
            [(r.given_hidden, r.hidden), (r.given_cotangent, r.cotangent)] + list(zip(given, targets))
        )
    ]
    for load in loads:
        load.start()

    def each_chunk(work):
        def one(c, _):
            work(r, span(c * chunk, chunk))
            return 0

        lax.fori_loop(0, tokens // chunk, one, 0)

    def move(slot, index, back):
        bank = lax.rem(slot, 2)
        far = (r.gauss_far, r.second_far, r.slope_far)[index].at[slot]
        near = (r.gauss, r.second, r.slope)[index].at[bank]
        pair = (far, near) if back else (near, far)
        return pltpu.make_async_copy(*pair, r.pair_sems.at[bank, index])

    def start_moves(slot, back):
        for index in range(3):
            move(slot, index, back).start()

    def wait_moves(slot, back):
        for index in range(3):
            move(slot, index, back).wait()

    if remote:
        def own_piece(index):
            return given[0].at[index] if index < 3 else given[index - 2]

        def whole_piece(index, tp):
            return whole[0].at[tp, index] if index < 3 else whole[index - 2].at[tp]

        gather = Gather(peers, own_piece, whole_piece, r.gather_sends, r.gather_recvs)
        ffn = Reduction(
            peers, r.fpart, r.ftotal, r.f_core, r.f_tp, r.f_x, r.f_z, r.f_sends, r.f_recvs
        )
        qkv = Reduction(
            peers, r.qpart, r.qtotal, r.q_core, r.q_tp, r.q_x, r.q_z, r.q_sends, r.q_recvs
        )
        small = SmallReduction(
            peers, r.spart, r.stotal, r.s_near, r.s_z, r.s_sends, r.s_recvs
        )
        greet(peers.everyone())
        gather.start()

    def at_time(index, plan):
        if remote:
            for k, steps in plan.items():

                @pl.when(index == k)
                def _(steps=steps):
                    run(steps)

    def run(steps):
        if remote:
            for act, *where in steps:
                act(*where)

    prepare_pairs(r)
    gather_plan = {}
    if remote:
        x, core = gather.onward_x, gather.onward_core
        gather_plan = {
            0: [(x, 0)], 1: [(x, 1), (core, 0)], 2: [(x, 2), (core, 1)], 3: [(x, 3), (core, 2)],
            4: [(x, 4), (core, 3), (x, 5)], 5: [(core, 4)], 6: [(core, 5)],
        }

    def pairs(slot, _):
        pair_tables(r, slot)
        pl.when(slot >= 2)(lambda: wait_moves(slot - 2, False))
        pair_forward(r, slot)
        start_moves(slot, False)
        at_time(slot, gather_plan)
        return 0

    lax.fori_loop(0, slots, pairs, 0)
    loads[0].wait()
    loads[2].wait()
    if remote:
        for index in range(3):
            gather.arrive(index)
    each_chunk(project)
    first_slot = peers.tp * slots

    def attend_one(s, _):
        attend(r, s, first_slot)
        return 0

    lax.fori_loop(0, slots, attend_one, 0)
    for load in [loads[1]] + loads[3:]:
        load.wait()
    if remote:
        for index in range(3, 6):
            gather.arrive(index)
    r.vectors[...] = jnp.zeros_like(r.vectors)
    each_chunk(feed)
    store_out = pltpu.make_async_copy(r.out_rows, r.output, r.store_sems.at[0])
    store_out.start()
    for slot in (slots - 2, slots - 1):
        wait_moves(slot, False)
    start_moves(0, True)
    start_moves(1, True)
    f, q = (ffn.act, qkv.act) if remote else (None, None)
    for block in range(3):
        feed_grads(r, block)
        run([(f, block, 0)])
    run([(f, 0, 1)])

    back_plan = {
        0: [(f, 1, 1), (f, 2, 1)], 3: [(f, 0, 2)], 4: [(f, 0, 3)], 5: [(f, 0, 4), (f, 1, 2)],
        6: [(f, 0, 5), (f, 1, 3)], 7: [(f, 0, 6), (f, 1, 4)],
    }

    def back_one(s, _):
        attend_back(r, s)
        at_time(s, back_plan)
        return 0

    lax.fori_loop(0, slots, back_one, 0)
    for m in range(3):
        for t in range(2):
            at = m * D + t * HALF_D
            r.qpart[t, m] = dot_tn(r.normed_a[...], r.joined[:, at : at + HALF_D]).astype(bf16)
        run([(q, m, 0)])
    run([(q, 0, 1), (f, 2, 2), (f, 1, 5)])
    each_chunk(finish_input)
    store_in = pltpu.make_async_copy(r.in_rows, r.grad_input, r.store_sems.at[1])
    store_in.start()
    run([(q, 1, 1), (q, 2, 1), (f, 2, 3), (f, 1, 6)])
    for ref in (r.sums, r.acc_mixed, r.acc_table, r.spart):
        ref[...] = jnp.zeros_like(ref)
    pair_plan = {
        0: [(f, 2, 4), (q, 0, 2)], 1: [(f, 2, 5)], 2: [(q, 0, 3), (f, 2, 6)], 3: [(q, 1, 2)],
        4: [(q, 0, 4), (q, 1, 3)], 5: [(q, 0, 5)], 6: [(q, 2, 2), (q, 1, 4), (q, 0, 6)],
        7: [(q, 2, 3), (q, 1, 5)], 8: [(q, 2, 4), (q, 1, 6)], 9: [(q, 2, 5)], 10: [(q, 2, 6)],
    }

    def pairs_back(slot, _):
        wait_moves(slot, True)
        pair_backward(r, slot, lambda: at_time(2 * slot, pair_plan))
        pl.when(slot + 2 < slots)(lambda: start_moves(slot + 2, True))
        at_time(2 * slot + 1, pair_plan)
        return 0

    lax.fori_loop(0, slots, pairs_back, 0)
    pack_small(r)
    if remote:
        for stage in range(5):
            small.act(stage)
        for reduction in (ffn, qkv):
            for stage in (7, 8):
                for b in range(3):
                    reduction.act(b, stage)
        small.act(5)
        gather.finish()
    store_out.wait()
    store_in.wait()


def layer(remote, group_slots, tokens, arrays):
    slots = tokens // SLOT
    part, total, rows = (2, 3, D, HALF_D), (3, D, HALF_D), (SMALL_ROWS, 128)
    whole = {"qkv": part, "up": (2, D, HALF_D), "proj": (2, HALF_D, D), "down": (2, HALF_D, D)}
    scalars = ("lengths", "flags")
    far = tuple("given_" + name for name in ("hidden", "cotangent", "qkv", "up", "proj", "down"))
    space = lambda name: pltpu.SMEM if name in scalars else pl.ANY if name in far else pltpu.VMEM
    in_names = list(arrays)
    outs = {
        "output": ((tokens, D), bf16), "grad_input": ((tokens, D), bf16), "gauss_far": ((slots, K, PAIRS), bf16),
        "second_far": ((slots, K, PAIRS), bf16), "slope_far": ((slots, K, PAIRS), bf16),
    }
    near = (
        {"ftotal": (total, bf16), "qtotal": (total, bf16), "stotal": (rows, f32)}
        if remote
        else {"fpart": (part, bf16), "qpart": (part, bf16), "spart": (rows, f32)}
    )
    v = pltpu.VMEM
    sem = pltpu.SemaphoreType.DMA
    tokens_d = lambda kind: v((tokens, D), kind)
    scratch = {
        "hidden": tokens_d(bf16), "cotangent": tokens_d(bf16), "wqkv": v(whole["qkv"], bf16),
        "wup": v(whole["up"], bf16), "wproj": v(whole["proj"], bf16), "wdown": v(whole["down"], bf16),
        "load_sems": sem((6,)), "pair_sems": sem((2, 3)), "store_sems": sem((2,)),
        "cols": v((5, K, 128), f32), "w1t": v((K, K), bf16), "w2": v((K, 128), bf16), "base": v((H, 256), f32),
        "lhs": v((H, 256), bf16), "argument": v((slots, HALF, 128), f32), "distance": v((slots, HALF, 128), f32),
        "hop_rows": v((slots, HALF, 128), f32), "edge_rows": v((slots, HALF, 128), f32),
        "atom_rows": v((slots, 8, 128), f32), "bias": v((slots, H * HALF, 128), f32),
        "gauss": v((2, K, PAIRS), bf16), "second": v((2, K, PAIRS), bf16), "slope": v((2, K, PAIRS), bf16),
        "normed_a": tokens_d(bf16), "joined": v((tokens, 3 * D), bf16), "prob": v((slots, SLOT, H * SLOT), bf16),
        "work": v((3, SLOT, D), f32), "attended": tokens_d(bf16), "normed_f": tokens_d(bf16),
        "activated": tokens_d(bf16), "out_rows": tokens_d(bf16), "d_pre": tokens_d(bf16), "d_resid": tokens_d(f32),
        "d_branch": tokens_d(bf16), "d_attended": tokens_d(bf16), "in_rows": tokens_d(bf16), "vectors": v((8, D), f32),
        "dfirst": v((K, PAIRS), bf16), "dspace": v((2 * H, PAIRS), bf16), "hots": v((HOT, PAIRS), bf16),
        "dargs": v((HALF, 128), f32), "sums": v((2, K, 128), f32), "acc_mixed": v((2 * K + HOT, K + 2 * H), f32),
        "acc_table": v((2, ATOMS, ATOMS), f32),
    }
    if remote:
        scratch |= {"fpart": v(part, bf16), "qpart": v(part, bf16), "spart": v(rows, f32)}
        for name in ("f", "q"):
            keys = ("_core", "_tp", "_x", "_z", "_sends", "_recvs")
            scratch |= {name + key: item for key, item in zip(keys, big_scratch())}
        keys = ("s_near", "s_z", "s_sends", "s_recvs")
        scratch |= dict(zip(keys, small_scratch()))
        scratch |= {"gather_sends": sem((6, 4)), "gather_recvs": sem((6, 4))}
    names = in_names + list(outs) + list(near) + list(scratch)
    results = pl.pallas_call(
        functools.partial(layer_kernel, remote, names),
        in_specs=[pl.BlockSpec(memory_space=space(name)) for name in in_names],
        out_specs=[pl.BlockSpec(memory_space=pl.ANY)] * len(outs) + vmem(len(near)),
        out_shape=[jax.ShapeDtypeStruct(*item) for item in list(outs.values()) + list(near.values())],
        scratch_shapes=list(scratch.values()),
        compiler_params=pltpu.CompilerParams(
            vmem_limit_bytes=VMEM_BYTES, **(dict(collective_id=0, has_side_effects=True) if remote else {})
        ),
        name="layer",
    )(*arrays.values())
    return results[0], results[1], results[len(outs) :]


def unpack_kernel(
    qsum, up_sum, proj_low, proj_high, down_low, down_high, out_rows, in_rows, rows_ref,
    output, grad_input, again, ashift, qkv, proj, fgain, fshift, up, up_bias, down, down_bias, scale, shift, centers,
    spreads, first, first_bias, second, hop, edge,
):
    output[...] = out_rows[...]
    grad_input[...] = in_rows[...]
    qkv[...] = qsum[...].astype(f32)
    up[...] = up_sum[0].astype(f32)
    for low, high, ref in ((proj_low, proj_high, proj), (down_low, down_high, down)):
        ref[:, :HALF_D] = low[0].astype(f32)
        ref[:, HALF_D:] = high[0].astype(f32)

    @pl.when(pl.program_id(0) == 0)
    def _():
        for v, ref in enumerate((again, ashift, fgain, fshift, up_bias, down_bias)):
            for i in range(D // 128):
                ref[pl.ds(128 * i, 128)] = rows_ref[VECTOR_ROWS + v * (D // 128) + i, :]
        first[...] = rows_ref[0:K, :]
        second[...] = rows_ref[SECOND_ROWS : SECOND_ROWS + H, :]
        table = rows_ref[TABLE_ROWS : TABLE_ROWS + H, :]
        scale[...] = table[:ATOMS, HOT : HOT + ATOMS]
        shift[...] = table[ATOMS:, HOT : HOT + ATOMS]
        turned = square_turn(table)
        hop[...] = turned[:HOPS, :H]
        edge[...] = turned[HOPS : HOPS + EDGES, :H]
        for i, ref in enumerate((first_bias, centers, spreads)):
            ref[...] = rows_ref[KERNEL_ROWS + i, :]


def unpack(out_rows, in_rows, fsum, qsum, rows):
    steps = 4
    tokens = out_rows.shape[0]
    shape = jax.ShapeDtypeStruct
    vec, line = shape((D,), f32), shape((K,), f32)
    mat = lambda *dims: shape(dims, f32)
    whole = lambda item: pl.BlockSpec(item.shape, lambda i: (0,) * len(item.shape))
    by_rows = lambda count, lanes: pl.BlockSpec((count // steps, lanes), lambda i: (i, 0))
    piece = lambda block, count, skip: pl.BlockSpec((1, count, HALF_D), lambda i: (block, i + skip, 0))
    token_rows = by_rows(tokens, D)
    all_q = pl.BlockSpec((3, D // steps, HALF_D), lambda i: (0, i, 0))
    half = HALF_D // steps
    small = [mat(ATOMS, ATOMS), mat(ATOMS, ATOMS), line, line, mat(K, K), line, mat(H, K), mat(HOPS, H), mat(EDGES, H)]
    return pl.pallas_call(
        unpack_kernel,
        grid=(steps,),
        in_specs=[
            all_q, piece(0, D // steps, 0), piece(1, half, 0), piece(1, half, steps), piece(2, half, 0),
            piece(2, half, steps), token_rows, token_rows, whole(rows),
        ],
        out_specs=[
            token_rows, token_rows, whole(vec), whole(vec), all_q, by_rows(HALF_D, D), whole(vec), whole(vec),
            by_rows(D, HALF_D), whole(vec), by_rows(HALF_D, D), whole(vec),
        ] + [whole(item) for item in small],
        out_shape=[
            shape((tokens, D), bf16), shape((tokens, D), bf16), vec, vec, mat(3, D, HALF_D), mat(HALF_D, D), vec, vec,
            mat(D, HALF_D), vec, mat(HALF_D, D), vec,
        ] + small,
        compiler_params=pltpu.CompilerParams(vmem_limit_bytes=VMEM_BYTES),
        name="unpack",
    )(qsum, fsum, fsum, fsum, fsum, fsum, out_rows, in_rows, rows)


def whole_weights(qkv_weight, up_weight, proj_weight, down_weight):
    columns = lambda w: jnp.stack(jnp.split(w, 2, axis=-1))
    rows = lambda w: jnp.stack(jnp.split(w, 2, axis=0))
    gather = lambda w, dim: lax.all_gather(w, "tp", axis=dim, tiled=True)
    return (
        columns(gather(qkv_weight.transpose(1, 0, 2), 2)), columns(gather(up_weight, 1)),
        rows(gather(proj_weight, 0)), rows(gather(down_weight, 0)),
    )


def sum_grads(fgrads, qgrads, small):
    total_f, total_q, rows = lax.psum((fgrads, qgrads, small), ("mol", "tp"))
    share = D // lax.axis_size("tp")
    at = lax.axis_index("tp") * share
    columns = lambda w: lax.dynamic_slice_in_dim(jnp.concatenate([w[0], w[1]], axis=-1), at, share, w.ndim - 2)
    rows_of = lambda w: lax.dynamic_slice_in_dim(
        jnp.concatenate([jnp.concatenate([w[t, :HALF_D], w[t, HALF_D:]], axis=1) for t in range(2)]), at, share, 0
    )
    wide = lambda v: v.astype(f32)
    big = (wide(columns(total_q)), wide(columns(total_f[:, 0])), wide(rows_of(total_f[:, 1])), wide(rows_of(total_f[:, 2])))
    return big, rows


def body(
    mesh_shape,
    hidden_in, positions, atom_types, hop_counts, edge_types, lengths, branches,
    attn_gain, attn_shift, qkv_weight, proj_weight, ffn_gain, ffn_shift, up_weight, up_bias, down_weight, down_bias,
    kernel_scale, kernel_shift, centers, spreads, first_weight, first_bias, second_weight, hop_table, edge_table,
    cotangent,
):
    remote = mesh_shape["tp"] == 2 and mesh_shape["mol"] == 16 and branches.shape[0] == 8
    if remote:
        weights = (qkv_weight.transpose(1, 0, 2), up_weight, proj_weight, down_weight)
    else:
        weights = whole_weights(qkv_weight, up_weight, proj_weight, down_weight)
    arrays = dict(
        lengths=lengths, flags=branches.T, positions=positions, atoms=atom_types, hops=hop_counts.T,
        edges=edge_types.T, kernel_scale=kernel_scale, kernel_shift=kernel_shift, centers=centers, spreads=spreads,
        first_weight=first_weight, first_bias=first_bias, second_weight=second_weight.T, hop_table=hop_table,
        edge_table=edge_table, attn_gain=attn_gain, attn_shift=attn_shift, ffn_gain=ffn_gain, ffn_shift=ffn_shift,
        up_bias=up_bias, down_bias=down_bias, given_hidden=hidden_in, given_cotangent=cotangent,
        given_qkv=weights[0], given_up=weights[1], given_proj=weights[2], given_down=weights[3],
    )
    output, grad_input, sums = layer(remote, lengths.shape[0], hidden_in.shape[0], arrays)
    if remote:
        fsum, qsum, rows = sums
    else:
        big, rows = sum_grads(*sums)
        fsum = jnp.zeros((3, D, HALF_D), bf16)
        qsum = fsum
    output, grad_input, *grads = unpack(output, grad_input, fsum, qsum, rows)
    if not remote:
        grads[2], grads[6], grads[3], grads[8] = big
    grads[2] = grads[2].transpose(1, 0, 2)
    grads[16] = grads[16].T
    return (output, grad_input, *grads)


def solution(mesh):
    rows = P(("mol", "tp"), None)
    all_of = P()
    in_specs = (
        rows, P(None, ("mol", "tp")), P(("mol", "tp")), rows, rows, P("mol"), rows, all_of, all_of,
        P(None, None, "tp"), P("tp", None), all_of, all_of, P(None, "tp"), all_of, P("tp", None),
    ) + (all_of,) * 10 + (rows,)
    out_specs = (
        rows, rows, all_of, all_of, P(None, None, "tp"), P("tp", None), all_of, all_of, P(None, "tp"), all_of,
        P("tp", None),
    ) + (all_of,) * 10
    step = functools.partial(body, dict(mesh.shape))
    return jax.shard_map(step, mesh=mesh, in_specs=in_specs, out_specs=out_specs, check_vma=False)
```

```python
import functools
from types import SimpleNamespace

import jax
import jax.numpy as jnp
from jax import lax
from jax.experimental import pallas as pl
from jax.experimental.pallas import tpu as pltpu
from jax.sharding import PartitionSpec as P

D = 768
H = 32
HD = 24
FF = 768
K = 128
SLOT = 64
HALF = SLOT // 2
HALF_D = D // 2
PAIRS = SLOT * SLOT
HOPS = 16
EDGES = 8
ATOMS = 16
GROUP = 4
GROUPS = H // GROUP
HOT = 32

highest = lax.Precision.HIGHEST
neg_large = -1e30
root_tau = 2.5066282746310002
root_half = 0.7071067811865476
inv_root_tau = 0.3989422804014327
head_scale = HD ** (-0.5)
VMEM_BYTES = 62 * 1024 * 1024
TILE = 512

SECOND_ROWS = K
TABLE_ROWS = SECOND_ROWS + H
KERNEL_ROWS = TABLE_ROWS + H
VECTOR_ROWS = KERNEL_ROWS + 8
SMALL_ROWS = 256

MESH = pl.DeviceIdType.MESH
f32 = jnp.float32
bf16 = jnp.bfloat16


def dot_nn(left, right, precision=None):
    return lax.dot_general(left, right, (((1,), (0,)), ((), ())), precision=precision, preferred_element_type=f32)


def dot_nt(left, right, precision=None):
    return lax.dot_general(left, right, (((1,), (1,)), ((), ())), precision=precision, preferred_element_type=f32)


def dot_tn(left, right, precision=None):
    return lax.dot_general(left, right, (((0,), (0,)), ((), ())), precision=precision, preferred_element_type=f32)


def iota(shape, dim):
    return lax.broadcasted_iota(jnp.int32, shape, dim)


def gelu_parts(values):
    size = jnp.abs(values)
    bell = jnp.exp(values * values * -0.5)
    denominator = 1.0 + (0.3275911 * root_half) * size
    t = pl.reciprocal(denominator, approx=True)
    t = t * (2.0 - denominator * t)
    series = 0.5 * 1.061405429
    for factor in (-1.453152027, 1.421413741, -0.284496736, 0.254829592):
        series = series * t + 0.5 * factor
    tail = series * t * bell
    gelu = jnp.maximum(values, 0.0) - size * tail
    outer = tail - size * (bell * inv_root_tau)
    return gelu, jnp.where(values >= 0.0, 1.0 - outer, outer)


def to_column(row):
    size = row.shape[1]
    same = iota((size, size), 0) == iota((size, size), 1)
    return jnp.sum(jnp.where(same, row, 0.0), axis=1, keepdims=True)


def half_swap(values):
    return pltpu.roll(values, 64, 1)


def low_lanes(rows):
    return iota((rows, 128), 1) < 64


def vmem(count):
    return [pl.BlockSpec(memory_space=pltpu.VMEM)] * count


def row_of(ref):
    return ref[...].reshape(1, ref.shape[0])


def place():
    mol = lax.axis_index("mol")
    return mol % 2, (mol // 2) % 2, mol // 4, lax.axis_index("tp")


def greet(peers):
    barrier = pltpu.get_barrier_semaphore()
    for peer in peers:
        pl.semaphore_signal(barrier, inc=1, device_id=peer, device_id_type=MESH)
    pl.semaphore_wait(barrier, len(peers))


def window(group):
    first = GROUP * HD * group
    start = first // 128 * 128
    width = 128 if first - start + GROUP * HD <= 128 else 256
    return start, width, first - start


def head_masks(group, kind):
    _, width, offset = window(group)
    lane = iota((1, width), 1)
    return [
        ((lane >= offset + HD * h) & (lane < offset + HD * (h + 1))).astype(f32).astype(kind) for h in range(GROUP)
    ]


def spread_heads(values, group):
    return jnp.concatenate([values * mask for mask in head_masks(group, bf16)], axis=0)


def gather_heads(values, group):
    masks = head_masks(group, f32)
    total = values[:SLOT] * masks[0]
    for h in range(1, GROUP):
        total = total + values[SLOT * h : SLOT * (h + 1)] * masks[h]
    return total


def standardize(values):
    centred = values - jnp.mean(values, axis=-1, keepdims=True)
    inv_std = lax.rsqrt(jnp.mean(centred * centred, axis=-1, keepdims=True) + 1e-05)
    return centred * inv_std, inv_std


def norm_back(d_normed, scaled, inv_std, gain):
    weighted = d_normed * gain
    inner_a = jnp.mean(weighted, axis=-1, keepdims=True)
    inner_b = jnp.mean(weighted * scaled, axis=-1, keepdims=True)
    return inv_std * (weighted - inner_a - scaled * inner_b)


def column_sum(values):
    return jnp.sum(values, axis=0, keepdims=True)


class Peers:
    def __init__(self):
        self.core, self.x, self.z, self.tp = place()
        mol = lax.axis_index("mol")
        self.over_core = {"mol": mol + 1 - 2 * self.core}
        self.over_x = {"mol": mol + 2 - 4 * self.x}
        self.over_tp = {"tp": 1 - self.tp}
        self.turn = [lax.rem(self.z + d, 4) for d in range(4)]
        self.over_z = [{"mol": self.turn[d] * 4 + self.x * 2 + self.core} for d in range(4)]

    def neighbour(self, k):
        core = self.core + (1 - 2 * self.core) * (k & 1)
        x = self.x + (1 - 2 * self.x) * (k >> 1 & 1)
        tp = self.tp + (1 - 2 * self.tp) * (k >> 2)
        return core * 4 + tp * 2 + x, {"mol": self.z * 4 + x * 2 + core, "tp": tp}

    def everyone(self):
        return [self.neighbour(k)[1] for k in range(1, 8)] + self.over_z[1:]


def span(start, size):
    return pl.ds(pl.multiple_of(start, size), size)


def add_rows(target, source, rows):
    step = 96 if rows % 96 == 0 else rows

    def piece(i, _):
        at = pl.ds(pl.multiple_of(i * step, step), step)
        target[at, :] = (target[at, :].astype(f32) + source[at, :].astype(f32)).astype(target.dtype)
        return 0

    lax.fori_loop(0, rows // step, piece, 0)


class Reduction:
    def __init__(self, peers, part, total, from_core, from_tp, from_x, from_z, sends, recvs):
        self.peers, self.part, self.total = peers, part, total
        self.from_core, self.from_tp, self.from_x, self.from_z = from_core, from_tp, from_x, from_z
        self.sends, self.recvs = sends, recvs
        p = peers
        self.at_core = p.core * 384
        self.at_x = self.at_core + p.x * 192

    def copy(self, b, kind):
        p = self.peers
        part, total = self.part, self.total
        if kind == 0:
            src, dst, peer = part.at[:, b, span((1 - p.core) * 384, 384)], self.from_core.at[:, b], p.over_core
        elif kind == 1:
            src, dst, peer = part.at[1 - p.tp, b, span(self.at_core, 384)], self.from_tp.at[b], p.over_tp
        elif kind == 2:
            src, dst, peer = part.at[p.tp, b, span(self.at_core + (1 - p.x) * 192, 192)], self.from_x.at[b], p.over_x
        elif kind < 6:
            d = kind - 2
            src, dst, peer = part.at[p.tp, b, span(self.at_x + p.turn[d] * 48, 48)], self.from_z.at[b, d - 1], p.over_z[d]
        elif kind < 9:
            src = dst = total.at[b, span(self.at_x + p.z * 48, 48)]
            peer = p.over_z[kind - 5]
        elif kind == 9:
            src = dst = total.at[b, span(self.at_x, 192)]
            peer = p.over_x
        else:
            src = dst = total.at[b, span(self.at_core, 384)]
            peer = p.over_core
        return pltpu.make_async_remote_copy(
            src_ref=src, dst_ref=dst, send_sem=self.sends.at[b, kind], recv_sem=self.recvs.at[b, kind],
            device_id=peer, device_id_type=MESH,
        )

    def act(self, b, stage):
        p = self.peers
        if stage == 0:
            self.copy(b, 0).start()
        elif stage == 1:
            self.copy(b, 0).wait_recv()
            add_rows(self.part.at[1 - p.tp, b, span(self.at_core, 384)], self.from_core.at[1 - p.tp, b], 384)
            self.copy(b, 1).start()
            add_rows(self.part.at[p.tp, b, span(self.at_core, 384)], self.from_core.at[p.tp, b], 384)
        elif stage == 2:
            self.copy(b, 1).wait_recv()
            away, mine = (1 - p.x) * 192, p.x * 192
            add_rows(self.part.at[p.tp, b, span(self.at_core + away, 192)], self.from_tp.at[b, span(away, 192)], 192)
            self.copy(b, 2).start()
            add_rows(self.part.at[p.tp, b, span(self.at_core + mine, 192)], self.from_tp.at[b, span(mine, 192)], 192)
        elif stage == 3:
            self.copy(b, 2).wait_recv()
            add_rows(self.part.at[p.tp, b, span(self.at_x, 192)], self.from_x.at[b], 192)
            for kind in (3, 4, 5):
                self.copy(b, kind).start()
        elif stage == 4:
            for kind in (3, 4, 5):
                self.copy(b, kind).wait_recv()
            mine = span(self.at_x + p.z * 48, 48)
            value = self.part[p.tp, b, mine, :].astype(f32)
            for d in range(3):
                value = value + self.from_z[b, d].astype(f32)
            self.total[b, mine, :] = value.astype(bf16)
            for kind in (6, 7, 8):
                self.copy(b, kind).start()
        elif stage == 5:
            for kind in (6, 7, 8):
                self.copy(b, kind).wait_recv()
            self.copy(b, 9).start()
        elif stage == 6:
            self.copy(b, 9).wait_recv()
            self.copy(b, 10).start()
        elif stage == 7:
            self.copy(b, 10).wait_recv()
        else:
            for kind in range(11):
                self.copy(b, kind).wait_send()


class SmallReduction:
    def __init__(self, peers, part, total, from_near, from_z, sends, recvs):
        self.peers, self.part, self.total, self.from_near, self.from_z = peers, part, total, from_near, from_z
        self.sends, self.recvs = sends, recvs
        p = peers
        self.near = [p.neighbour(k) for k in range(8)]
        self.at_near = self.near[0][0] * 32

    def copy(self, kind):
        p = self.peers
        part, total = self.part, self.total
        if kind < 7:
            index, peer = self.near[kind + 1]
            src, dst = part.at[span(index * 32, 32)], self.from_near.at[kind]
        elif kind < 10:
            d = kind - 6
            src, dst, peer = part.at[span(self.at_near + p.turn[d] * 8, 8)], self.from_z.at[d - 1], p.over_z[d]
        elif kind < 13:
            src = dst = total.at[span(self.at_near + p.z * 8, 8)]
            peer = p.over_z[kind - 9]
        else:
            src = dst = total.at[span(self.at_near, 32)]
            peer = self.near[kind - 12][1]
        return pltpu.make_async_remote_copy(
            src_ref=src, dst_ref=dst, send_sem=self.sends.at[kind], recv_sem=self.recvs.at[kind],
            device_id=peer, device_id_type=MESH,
        )

    def act(self, stage):
        p = self.peers
        hops = (range(0, 7), range(7, 10), range(10, 13), range(13, 20))
        if stage == 5:
            for kind in range(20):
                self.copy(kind).wait_send()
            return
        if stage > 0:
            for kind in hops[stage - 1]:
                self.copy(kind).wait_recv()
        if stage == 1:
            mine = span(self.at_near, 32)
            value = self.part[mine, :]
            for k in range(7):
                value = value + self.from_near[k]
            self.part[mine, :] = value
        elif stage == 2:
            mine = span(self.at_near + p.z * 8, 8)
            self.total[mine, :] = self.part[mine, :] + self.from_z[0] + self.from_z[1] + self.from_z[2]
        if stage < 4:
            for kind in hops[stage]:
                self.copy(kind).start()


def big_scratch():
    return [
        pltpu.VMEM((2, 3, 384, HALF_D), bf16), pltpu.VMEM((3, 384, HALF_D), bf16), pltpu.VMEM((3, 192, HALF_D), bf16),
        pltpu.VMEM((3, 3, 48, HALF_D), bf16), pltpu.SemaphoreType.DMA((3, 11)), pltpu.SemaphoreType.DMA((3, 11)),
    ]


def small_scratch():
    return [
        pltpu.VMEM((7, 32, 128), f32), pltpu.VMEM((3, 8, 128), f32),
        pltpu.SemaphoreType.DMA((20,)), pltpu.SemaphoreType.DMA((20,)),
    ]


class Gather:
    pieces = 6

    def __init__(self, peers, whole, sends, recvs):
        self.peers, self.whole, self.sends, self.recvs = peers, whole, sends, recvs
        self.quarter = peers.x * 2 + peers.core
        self.next_quarter = (1 - peers.x) * 2 + peers.core

    def rows(self, ref, quarter):
        count = ref.shape[0] // 4
        return ref.at[span(quarter * count, count), :]

    def copy(self, index, kind):
        p = self.peers
        if kind == 0:
            src = dst = self.rows(self.whole(index, p.tp), self.quarter)
            peer = p.over_tp
        elif kind == 1:
            src = dst = self.rows(self.whole(index, 1 - p.tp), self.quarter)
            peer = p.over_x
        else:
            src = dst = self.rows(self.whole(index, 1 - p.tp), self.quarter if kind == 2 else self.next_quarter)
            peer = p.over_core
        return pltpu.make_async_remote_copy(
            src_ref=src, dst_ref=dst, send_sem=self.sends.at[index, kind], recv_sem=self.recvs.at[index, kind],
            device_id=peer, device_id_type=MESH,
        )

    def start(self, indices):
        for index in indices:
            self.copy(index, 0).start()

    def onward_x(self, index):
        self.copy(index, 0).wait_recv()
        self.copy(index, 1).start()
        self.copy(index, 2).start()

    def onward_core(self, index):
        self.copy(index, 1).wait_recv()
        self.copy(index, 3).start()

    def arrive(self, index):
        self.copy(index, 2).wait_recv()
        self.copy(index, 3).wait_recv()

    def finish(self):
        for index in range(self.pieces):
            for kind in range(4):
                self.copy(index, kind).wait_send()


def widen(values):
    return jnp.concatenate([values] * (TILE // 128), axis=1)


def strips():
    return [slice(16 * i, 16 * (i + 1)) for i in range(K // 16)]


def four_rows(ref, slot, first):
    return jnp.concatenate([ref[slot, pl.ds(first + i, 1), :] for i in range(TILE // 128)], axis=1)


def hot_rows(values, count):
    return (values == iota((count, TILE), 0).astype(f32)).astype(f32)


def fold_lanes(values):
    total = values[:, :128]
    for i in range(1, TILE // 128):
        total = total + values[:, 128 * i : 128 * (i + 1)]
    return total


def prepare_pairs(r):
    spr = to_column(row_of(r.spreads))
    r.cols[0] = jnp.broadcast_to(to_column(row_of(r.centers)), (K, 128))
    r.cols[1] = jnp.broadcast_to(root_half / spr, (K, 128))
    r.cols[2] = jnp.broadcast_to(-jnp.log(root_tau * spr), (K, 128))
    r.cols[3] = jnp.broadcast_to(to_column(row_of(r.first_bias)), (K, 128))
    r.cols[4] = jnp.broadcast_to(1.0 / spr, (K, 128))
    r.w1t[...] = r.first_weight[...].astype(f32).T.astype(bf16)
    second = r.second_weight[...].astype(f32)
    r.w2[...] = jnp.concatenate([second, jnp.zeros((128 - H, K), f32)], axis=0).T.astype(bf16)
    table = jnp.concatenate([r.hop_table[...], r.edge_table[...], jnp.zeros((128 - HOPS - EDGES, H), f32)], axis=0)
    table = jnp.concatenate([table, jnp.zeros((128, 128 - H), f32)], axis=1).T[:H, :HOT]
    one = table.astype(bf16).astype(f32)
    r.base[...] = jnp.concatenate([second, one, table - one, jnp.zeros((H, 64), f32)], axis=1)


def pair_tables(r, slot):
    low = low_lanes(HALF)
    low_row = low_lanes(1)
    lanes = span(lax.div(slot, 2) * 128, 128)
    turn = lax.rem(slot, 2) * 64
    atoms = r.atoms[lanes].astype(f32).reshape(1, 128)
    rows = [pltpu.roll(row, turn, 1) for row in [r.positions[c : c + 1, lanes] for c in range(3)] + [atoms]]
    double = [jnp.where(low_row, row, half_swap(row)) for row in rows]
    columns = [to_column(row[:, :SLOT]) for row in rows]
    total = None
    for c in range(3):
        offset = jnp.where(low, columns[c][:HALF], columns[c][HALF:]) - double[c]
        total = offset * offset if total is None else total + offset * offset
    distance = jnp.sqrt(total)
    key_hot = (columns[3] == iota((SLOT, ATOMS), 1).astype(f32)).astype(f32)
    query_hot = (double[3] == iota((ATOMS, 128), 0).astype(f32)).astype(f32)
    picked = []
    for table in (r.kernel_scale, r.kernel_shift):
        both = dot_nn(dot_nt(key_hot, table[...], highest), query_hot, highest)
        picked.append(jnp.where(low, both[:HALF], both[HALF:]))
    r.argument[slot] = picked[0] * distance + picked[1]
    r.distance[slot] = distance
    for source, target in ((r.hops, r.hop_rows), (r.edges, r.edge_rows)):
        values = pltpu.roll(source[:, lanes].astype(f32), turn, 1)
        target[slot] = jnp.where(low, values[:HALF], half_swap(values[HALF:]))
    r.atom_rows[slot] = jnp.broadcast_to(double[3], (8, 128))


def pair_forward(r, slot):
    bank = lax.rem(slot, 2)
    graph_on = r.flags[0, slot].astype(f32)
    space_on = r.flags[1, slot].astype(f32)
    factor = jnp.where(iota((H, 256), 1) < K, space_on, graph_on)
    r.lhs[...] = (r.base[...] * factor).astype(bf16)

    def tile(t, _):
        for part in range(2):
            first_row = 8 * t + 4 * part
            where = span(t * 2 * TILE + part * TILE, TILE)
            arg = four_rows(r.argument, slot, first_row)
            pieces = []
            for rows in strips():
                u = (arg - widen(r.cols[0, rows])) * widen(r.cols[1, rows])
                pieces.append(jnp.exp(widen(r.cols[2, rows]) - u * u).astype(bf16))
                r.gauss[bank, rows, where] = pieces[-1]
            first = dot_nn(r.w1t[...], jnp.concatenate(pieces, axis=0))
            pieces = []
            for rows in strips():
                value, slope = gelu_parts(first[rows] + widen(r.cols[3, rows]))
                pieces.append(value.astype(bf16))
                r.second[bank, rows, where] = pieces[-1]
                r.slope[bank, rows, where] = slope.astype(bf16)
            hot = jnp.concatenate(
                [
                    hot_rows(four_rows(r.hop_rows, slot, first_row), HOPS),
                    hot_rows(four_rows(r.edge_rows, slot, first_row), HOT - HOPS),
                ],
                axis=0,
            ).astype(bf16)
            bias = dot_nn(r.lhs[:, : K + 2 * HOT], jnp.concatenate(pieces + [hot] * 2, axis=0))
            bias = bias.astype(bf16).astype(f32)
            for i in range(TILE // 128):
                r.bias[slot, pl.ds(first_row + i, H, stride=HALF), :] = bias[:, 128 * i : 128 * (i + 1)]
        return 0

    lax.fori_loop(0, PAIRS // (2 * TILE), tile, 0)


def pair_backward(r, slot, between):
    bank = lax.rem(slot, 2)
    graph_on = r.flags[0, slot].astype(f32)
    space_on = r.flags[1, slot].astype(f32)
    w2 = r.w2[:, :H] * space_on.astype(bf16)

    def tile(t, _):
        for part in range(2):
            first_row = 8 * t + 4 * part
            where = span(t * 2 * TILE + part * TILE, TILE)
            arg = four_rows(r.argument, slot, first_row)
            grad = jnp.concatenate(
                [r.bias[slot, pl.ds(first_row + i, H, stride=HALF), :] for i in range(TILE // 128)], axis=1
            )
            r.dspace[:, where] = jnp.concatenate([grad * space_on, grad * graph_on], axis=0).astype(bf16)
            d_second = dot_nn(w2, grad.astype(bf16))
            pieces = []
            for rows in strips():
                pieces.append((d_second[rows] * r.slope[bank, rows, where].astype(f32)).astype(bf16))
                r.dfirst[rows, where] = pieces[-1]
            d_gauss = dot_nn(r.first_weight[...], jnp.concatenate(pieces, axis=0))
            d_arg = None
            for rows in strips():
                inv = widen(r.cols[4, rows])
                u = (arg - widen(r.cols[0, rows])) * inv
                q = d_gauss[rows] * r.gauss[bank, rows, where].astype(f32)
                w = q * u
                r.sums[0, rows] += fold_lanes(w)
                r.sums[1, rows] += fold_lanes(w * u - q)
                w = w * inv
                w = w[:8] + w[8:]
                d_arg = w if d_arg is None else d_arg + w
            d_arg = -jnp.sum(d_arg, axis=0, keepdims=True)
            for i in range(TILE // 128):
                r.dargs[pl.ds(first_row + i, 1), :] = d_arg[:, 128 * i : 128 * (i + 1)]
            edge_hot = hot_rows(four_rows(r.edge_rows, slot, first_row), HOT - HOPS)
            edge_hot = jnp.where(iota((HOT - HOPS, TILE), 0) == EDGES, 1.0, edge_hot)
            r.hots[:, where] = jnp.concatenate(
                [hot_rows(four_rows(r.hop_rows, slot, first_row), HOPS), edge_hot], axis=0
            ).astype(bf16)
        return 0

    lax.fori_loop(0, PAIRS // (2 * TILE), tile, 0)
    between()
    left = jnp.concatenate([r.gauss[bank], r.second[bank], r.hots[...]], axis=0)
    r.acc_mixed[...] += dot_nt(left, jnp.concatenate([r.dfirst[...], r.dspace[...]], axis=0))
    query_hot = (r.atom_rows[slot, 0:1, :] == iota((ATOMS, 128), 0).astype(f32)).astype(f32)
    for index in range(2):
        values = r.dargs[...] * r.distance[slot] if index == 0 else r.dargs[...]
        part = jnp.where(
            low_lanes(ATOMS),
            dot_nn(query_hot[:, :HALF], values, highest),
            dot_nn(query_hot[:, HALF:SLOT], values, highest),
        )
        r.acc_table[index] += dot_nt(query_hot, part, highest)


def attend(r, s, first_slot):
    low = low_lanes(HALF)
    rows = span(s * SLOT, SLOT)
    valid = iota((SLOT, GROUP * SLOT), 0) < r.lengths[first_slot + s]
    r.work[0] = jnp.zeros((SLOT, D), f32)
    for g in range(GROUPS):
        start, width, _ = window(g)
        q = r.joined[rows, start : start + width]
        k = r.joined[rows, D + start : D + start + width]
        v = r.joined[rows, 2 * D + start : 2 * D + start + width]
        scores = dot_nt(k, spread_heads(q, g)) * head_scale
        parts = []
        for pair in range(GROUP // 2):
            head = GROUP * g + 2 * pair
            one = r.bias[s, head * HALF : (head + 1) * HALF, :]
            two = r.bias[s, (head + 1) * HALF : (head + 2) * HALF, :]
            top = jnp.where(low, one, half_swap(two))
            bottom = jnp.where(low, half_swap(one), two)
            parts.append(jnp.concatenate([top, bottom], axis=0))
        scores = jnp.where(valid, scores + jnp.concatenate(parts, axis=1), neg_large)
        weights = jnp.exp(scores - jnp.max(scores, axis=0, keepdims=True))
        prob = (weights * (1.0 / jnp.sum(weights, axis=0, keepdims=True))).astype(bf16)
        r.prob[s, :, g * GROUP * SLOT : (g + 1) * GROUP * SLOT] = prob
        r.work[0, :, start : start + width] += gather_heads(dot_tn(prob, v), g)
    r.attended[rows, :] = r.work[0].astype(bf16)


def attend_back(r, s):
    low = low_lanes(HALF)
    rows = span(s * SLOT, SLOT)
    r.work[...] = jnp.zeros((3, SLOT, D), f32)
    for g in range(GROUPS):
        start, width, _ = window(g)
        lanes = slice(start, start + width)
        k = r.joined[rows, D + start : D + start + width]
        v = r.joined[rows, 2 * D + start : 2 * D + start + width]
        q_heads = spread_heads(r.joined[rows, lanes], g)
        d_heads = spread_heads(r.d_attended[rows, lanes], g)
        prob = r.prob[s, :, g * GROUP * SLOT : (g + 1) * GROUP * SLOT]
        wide = prob.astype(f32)
        d_prob = dot_nt(v, d_heads)
        inner = jnp.sum(wide * d_prob, axis=0, keepdims=True)
        d_scores = (wide * (d_prob - inner)).astype(bf16)
        r.work[0, :, lanes] += gather_heads(dot_tn(d_scores, k), g)
        r.work[1, :, lanes] += dot_nn(d_scores, q_heads)
        r.work[2, :, lanes] += dot_nn(prob, d_heads)
        d_wide = d_scores.astype(f32)
        for pair in range(GROUP // 2):
            head = GROUP * g + 2 * pair
            top = d_wide[:HALF, 128 * pair : 128 * (pair + 1)]
            bottom = d_wide[HALF:, 128 * pair : 128 * (pair + 1)]
            r.bias[s, head * HALF : (head + 1) * HALF, :] = jnp.where(low, top, half_swap(bottom))
            r.bias[s, (head + 1) * HALF : (head + 2) * HALF, :] = jnp.where(low, half_swap(top), bottom)
    r.joined[rows, 0:D] = (r.work[0] * head_scale).astype(bf16)
    r.joined[rows, D : 2 * D] = (r.work[1] * head_scale).astype(bf16)
    r.joined[rows, 2 * D : 3 * D] = r.work[2].astype(bf16)


def project(r, rows):
    scaled, _ = standardize(r.hidden[rows, :].astype(f32))
    normed = (scaled * row_of(r.attn_gain) + row_of(r.attn_shift)).astype(bf16)
    r.normed_a[rows, :] = normed
    for m in range(3):
        for t in range(2):
            at = m * D + t * HALF_D
            r.joined[rows, at : at + HALF_D] = dot_nn(normed, r.wqkv[t, m]).astype(bf16)


def feed(r, rows):
    halves = [slice(0, HALF_D), slice(HALF_D, D)]
    resid = r.hidden[rows, :].astype(f32)
    for t in range(2):
        resid = resid + dot_nn(r.attended[rows, halves[t]], r.wproj[t])
    scaled, inv_std = standardize(resid)
    normed = (scaled * row_of(r.ffn_gain) + row_of(r.ffn_shift)).astype(bf16)
    r.normed_f[rows, :] = normed
    pre = jnp.concatenate([dot_nn(normed, r.wup[t]) for t in range(2)], axis=1)
    value, slope = gelu_parts(pre + row_of(r.up_bias))
    active = value.astype(bf16)
    r.activated[rows, :] = active
    result = resid + row_of(r.down_bias)
    for t in range(2):
        result = result + dot_nn(active[:, halves[t]], r.wdown[t])
    r.out_rows[rows, :] = result.astype(bf16)
    cot = r.cotangent[rows, :]
    cot_wide = cot.astype(f32)
    d_active = jnp.concatenate([dot_nt(cot, r.wdown[t]) for t in range(2)], axis=1)
    d_hidden = (d_active * slope).astype(bf16)
    r.d_pre[rows, :] = d_hidden
    d_normed = dot_nt(d_hidden[:, halves[0]], r.wup[0]) + dot_nt(d_hidden[:, halves[1]], r.wup[1])
    d_resid = cot_wide + norm_back(d_normed, scaled, inv_std, row_of(r.ffn_gain))
    r.d_resid[rows, :] = d_resid
    branch = d_resid.astype(bf16)
    r.d_branch[rows, :] = branch
    for t in range(2):
        r.d_attended[rows, halves[t]] = dot_nt(branch, r.wproj[t]).astype(bf16)
    r.vectors[2:3, :] += column_sum(d_normed * scaled)
    r.vectors[3:4, :] += column_sum(d_normed)
    r.vectors[4:5, :] += column_sum(d_hidden.astype(f32))
    r.vectors[5:6, :] += column_sum(cot_wide)


def feed_grads(r, block):
    for t in range(2):
        half = slice(t * HALF_D, (t + 1) * HALF_D)
        if block == 0:
            r.fpart[t, 0] = dot_tn(r.normed_f[...], r.d_pre[:, half]).astype(bf16)
        else:
            left, right = (r.attended, r.d_branch) if block == 1 else (r.activated, r.cotangent)
            grad = dot_tn(left[:, half], right[...]).astype(bf16)
            r.fpart[t, block, :HALF_D, :] = grad[:, :HALF_D]
            r.fpart[t, block, HALF_D:, :] = grad[:, HALF_D:]


def finish_input(r, rows):
    d_normed = None
    for m in range(3):
        for t in range(2):
            at = m * D + t * HALF_D
            term = dot_nt(r.joined[rows, at : at + HALF_D], r.wqkv[t, m])
            d_normed = term if d_normed is None else d_normed + term
    scaled, inv_std = standardize(r.hidden[rows, :].astype(f32))
    grad = r.d_resid[rows, :] + norm_back(d_normed, scaled, inv_std, row_of(r.attn_gain))
    r.in_rows[rows, :] = grad.astype(bf16)
    r.vectors[0:1, :] += column_sum(d_normed * scaled)
    r.vectors[1:2, :] += column_sum(d_normed)


def square_turn(values):
    rows, lanes = values.shape
    if lanes < 128:
        values = jnp.concatenate([values, jnp.zeros((rows, 128 - lanes), f32)], axis=1)
    if rows < 128:
        values = jnp.concatenate([values, jnp.zeros((128 - rows, 128), f32)], axis=0)
    return values.T


def pack_small(r):
    for v in range(6):
        for i in range(D // 128):
            at = VECTOR_ROWS + v * (D // 128) + i
            r.spart[at : at + 1, :] = r.vectors[v : v + 1, 128 * i : 128 * (i + 1)]
    r.spart[0:K, :] = r.acc_mixed[0:K, :K]
    r.spart[SECOND_ROWS : SECOND_ROWS + H, :] = square_turn(r.acc_mixed[K : 2 * K, K:])[:H]
    r.spart[TABLE_ROWS : TABLE_ROWS + H, :HOT] = square_turn(r.acc_mixed[2 * K :, K:])[H : 2 * H, :HOT]
    for index in range(2):
        rows = slice(TABLE_ROWS + ATOMS * index, TABLE_ROWS + ATOMS * (index + 1))
        r.spart[rows, HOT : HOT + ATOMS] = r.acc_table[index]
    ones = 2 * K + HOPS + EDGES
    r.spart[KERNEL_ROWS : KERNEL_ROWS + 1, :] = r.acc_mixed[ones : ones + 1, :K]
    for index in range(2):
        column = jnp.sum(r.sums[index] * r.cols[4], axis=1, keepdims=True)
        same = iota((K, K), 0) == iota((K, K), 1)
        at = KERNEL_ROWS + 1 + index
        r.spart[at : at + 1, :] = jnp.sum(jnp.where(same, column, 0.0), axis=0, keepdims=True)


def layer_kernel(remote, names, near_inputs, *refs):
    r = SimpleNamespace(**dict(zip(names, refs)))
    inputs = [
        pltpu.make_async_copy(getattr(r, "given_" + name), getattr(r, name), r.input_sems.at[i])
        for i, name in enumerate(near_inputs)
    ]
    for load in inputs:
        load.start()
    tokens = r.hidden.shape[0]
    slots = tokens // SLOT
    chunk = min(256, tokens)
    peers = Peers()
    whole = [r.wqkv, r.wup, r.wproj, r.wdown]
    given = [r.given_qkv, r.given_up, r.given_proj, r.given_down]
    targets = [w.at[peers.tp] for w in whole] if remote else whole
    loads = [
        pltpu.make_async_copy(src, dst, r.load_sems.at[i])
        for i, (src, dst) in enumerate(
            [(r.given_hidden, r.hidden), (r.given_cotangent, r.cotangent)] + list(zip(given, targets))
        )
    ]
    for load in loads[2:] + loads[:2]:
        load.start()

    def each_chunk(work):
        def one(c, _):
            work(r, span(c * chunk, chunk))
            return 0

        lax.fori_loop(0, tokens // chunk, one, 0)

    def move(slot, index, back):
        bank = lax.rem(slot, 2)
        far = (r.gauss_far, r.second_far, r.slope_far)[index].at[slot]
        near = (r.gauss, r.second, r.slope)[index].at[bank]
        pair = (far, near) if back else (near, far)
        return pltpu.make_async_copy(*pair, r.pair_sems.at[bank, index])

    def start_moves(slot, back):
        for index in range(3):
            move(slot, index, back).start()

    def wait_moves(slot, back):
        for index in range(3):
            move(slot, index, back).wait()

    if remote:
        def whole_piece(index, tp):
            return whole[0].at[tp, index] if index < 3 else whole[index - 2].at[tp]

        gather = Gather(peers, whole_piece, r.gather_sends, r.gather_recvs)
        ffn = Reduction(
            peers, r.fpart, r.ftotal, r.f_core, r.f_tp, r.f_x, r.f_z, r.f_sends, r.f_recvs
        )
        qkv = Reduction(
            peers, r.qpart, r.qtotal, r.q_core, r.q_tp, r.q_x, r.q_z, r.q_sends, r.q_recvs
        )
        small = SmallReduction(
            peers, r.spart, r.stotal, r.s_near, r.s_z, r.s_sends, r.s_recvs
        )
        greet(peers.everyone())
        for load, indices in zip(loads[2:], ((0, 1, 2), (3,), (4,), (5,))):
            load.wait()
            gather.start(indices)

    def at_time(index, plan):
        if remote:
            for k, steps in plan.items():

                @pl.when(index == k)
                def _(steps=steps):
                    run(steps)

    def run(steps):
        if remote:
            for act, *where in steps:
                act(*where)

    for load in inputs:
        load.wait()
    prepare_pairs(r)
    gather_plan = {}
    if remote:
        x, core = gather.onward_x, gather.onward_core
        gather_plan = {
            0: [(x, 0)], 1: [(x, 1), (core, 0)], 2: [(x, 2), (core, 1)], 3: [(x, 3), (core, 2)],
            4: [(x, 4), (core, 3), (x, 5)], 5: [(core, 4)], 6: [(core, 5)],
        }

    def pairs(slot, _):
        pair_tables(r, slot)
        pl.when(slot >= 2)(lambda: wait_moves(slot - 2, False))
        pair_forward(r, slot)
        start_moves(slot, False)
        at_time(slot, gather_plan)
        return 0

    lax.fori_loop(0, slots, pairs, 0)
    loads[0].wait()
    if not remote:
        for load in loads[2:]:
            load.wait()
    if remote:
        for index in range(3):
            gather.arrive(index)
    each_chunk(project)
    first_slot = peers.tp * slots

    def attend_one(s, _):
        attend(r, s, first_slot)
        return 0

    lax.fori_loop(0, slots, attend_one, 0)
    loads[1].wait()
    if remote:
        for index in range(3, 6):
            gather.arrive(index)
    r.vectors[...] = jnp.zeros_like(r.vectors)
    each_chunk(feed)
    store_out = pltpu.make_async_copy(r.out_rows, r.output, r.store_sems.at[0])
    store_out.start()
    for slot in (slots - 2, slots - 1):
        wait_moves(slot, False)
    start_moves(0, True)
    start_moves(1, True)
    f, q = (ffn.act, qkv.act) if remote else (None, None)
    for block in range(3):
        feed_grads(r, block)
        run([(f, block, 0)])
    run([(f, 0, 1)])

    back_plan = {
        0: [(f, 1, 1), (f, 2, 1)], 3: [(f, 0, 2)], 4: [(f, 0, 3)], 5: [(f, 0, 4), (f, 1, 2)],
        6: [(f, 0, 5), (f, 1, 3)], 7: [(f, 0, 6), (f, 1, 4)],
    }

    def back_one(s, _):
        attend_back(r, s)
        at_time(s, back_plan)
        return 0

    lax.fori_loop(0, slots, back_one, 0)
    for m in range(3):
        for t in range(2):
            at = m * D + t * HALF_D
            r.qpart[t, m] = dot_tn(r.normed_a[...], r.joined[:, at : at + HALF_D]).astype(bf16)
        run([(q, m, 0)])
    run([(q, 0, 1), (f, 2, 2), (f, 1, 5)])
    each_chunk(finish_input)
    store_in = pltpu.make_async_copy(r.in_rows, r.grad_input, r.store_sems.at[1])
    store_in.start()
    run([(q, 1, 1), (q, 2, 1), (f, 2, 3), (f, 1, 6)])
    for ref in (r.sums, r.acc_mixed, r.acc_table, r.spart):
        ref[...] = jnp.zeros_like(ref)
    pair_plan = {
        0: [(f, 2, 4), (q, 0, 2)], 1: [(f, 2, 5)], 2: [(q, 0, 3), (f, 2, 6)], 3: [(q, 1, 2)],
        4: [(q, 0, 4), (q, 1, 3)], 5: [(q, 0, 5)], 6: [(q, 2, 2), (q, 1, 4), (q, 0, 6)],
        7: [(q, 2, 3), (q, 1, 5)], 8: [(q, 2, 4), (q, 1, 6)], 9: [(q, 2, 5)], 10: [(q, 2, 6)],
    }

    def pairs_back(slot, _):
        wait_moves(slot, True)
        pair_backward(r, slot, lambda: at_time(2 * slot, pair_plan))
        pl.when(slot + 2 < slots)(lambda: start_moves(slot + 2, True))
        at_time(2 * slot + 1, pair_plan)
        return 0

    lax.fori_loop(0, slots, pairs_back, 0)
    pack_small(r)
    if remote:
        leave = [
            pltpu.make_async_copy(near.at[b], far.at[b], r.leave_sems.at[3 * i + b])
            for i, (near, far) in enumerate(((r.ftotal, r.ftotal_far), (r.qtotal, r.qtotal_far)))
            for b in range(3)
        ]
        small.act(0)
        for b in range(3):
            ffn.act(b, 7)
            leave[b].start()
        small.act(1)
        for b in range(3):
            qkv.act(b, 7)
            leave[3 + b].start()
        for stage in (2, 3, 4):
            small.act(stage)
        leave.append(pltpu.make_async_copy(r.stotal, r.stotal_far, r.leave_sems.at[6]))
        leave[6].start()
        for b in range(3):
            ffn.act(b, 8)
            qkv.act(b, 8)
        small.act(5)
        gather.finish()
    else:
        pairs_of = ((r.fpart, r.fpart_far), (r.qpart, r.qpart_far), (r.spart, r.spart_far))
        leave = [pltpu.make_async_copy(near, far, r.leave_sems.at[i]) for i, (near, far) in enumerate(pairs_of)]
        for copy in leave:
            copy.start()
    for copy in leave:
        copy.wait()
    store_out.wait()
    store_in.wait()


def layer(remote, group_slots, tokens, arrays):
    slots = tokens // SLOT
    part, total, rows = (2, 3, D, HALF_D), (3, D, HALF_D), (SMALL_ROWS, 128)
    whole = {"qkv": part, "up": (2, D, HALF_D), "proj": (2, HALF_D, D), "down": (2, HALF_D, D)}
    scalars = ("lengths", "flags")
    far = tuple("given_" + name for name in ("hidden", "cotangent", "qkv", "up", "proj", "down"))
    space = lambda name: pltpu.SMEM if name in scalars else pl.ANY
    near_inputs = {n: pltpu.VMEM(a.shape, a.dtype) for n, a in arrays.items() if n not in scalars + far}
    in_names = ["given_" + n if n in near_inputs else n for n in arrays]
    outs = {
        "output": ((tokens, D), bf16), "grad_input": ((tokens, D), bf16), "gauss_far": ((slots, K, PAIRS), bf16),
        "second_far": ((slots, K, PAIRS), bf16), "slope_far": ((slots, K, PAIRS), bf16),
    }
    near = (
        {"ftotal_far": (total, bf16), "qtotal_far": (total, bf16), "stotal_far": (rows, f32)}
        if remote
        else {"fpart_far": (part, bf16), "qpart_far": (part, bf16), "spart_far": (rows, f32)}
    )
    v = pltpu.VMEM
    sem = pltpu.SemaphoreType.DMA
    tokens_d = lambda kind: v((tokens, D), kind)
    scratch = {
        "hidden": tokens_d(bf16), "cotangent": tokens_d(bf16), "wqkv": v(whole["qkv"], bf16),
        "wup": v(whole["up"], bf16), "wproj": v(whole["proj"], bf16), "wdown": v(whole["down"], bf16),
        "load_sems": sem((6,)), "pair_sems": sem((2, 3)), "store_sems": sem((2,)),
        "cols": v((5, K, 128), f32), "w1t": v((K, K), bf16), "w2": v((K, 128), bf16), "base": v((H, 256), f32),
        "lhs": v((H, 256), bf16), "argument": v((slots, HALF, 128), f32), "distance": v((slots, HALF, 128), f32),
        "hop_rows": v((slots, HALF, 128), f32), "edge_rows": v((slots, HALF, 128), f32),
        "atom_rows": v((slots, 8, 128), f32), "bias": v((slots, H * HALF, 128), f32),
        "gauss": v((2, K, PAIRS), bf16), "second": v((2, K, PAIRS), bf16), "slope": v((2, K, PAIRS), bf16),
        "normed_a": tokens_d(bf16), "joined": v((tokens, 3 * D), bf16), "prob": v((slots, SLOT, H * SLOT), bf16),
        "work": v((3, SLOT, D), f32), "attended": tokens_d(bf16), "normed_f": tokens_d(bf16),
        "activated": tokens_d(bf16), "out_rows": tokens_d(bf16), "d_pre": tokens_d(bf16), "d_resid": tokens_d(f32),
        "d_branch": tokens_d(bf16), "d_attended": tokens_d(bf16), "in_rows": tokens_d(bf16), "vectors": v((8, D), f32),
        "dfirst": v((K, PAIRS), bf16), "dspace": v((2 * H, PAIRS), bf16), "hots": v((HOT, PAIRS), bf16),
        "dargs": v((HALF, 128), f32), "sums": v((2, K, 128), f32), "acc_mixed": v((2 * K + HOT, K + 2 * H), f32),
        "acc_table": v((2, ATOMS, ATOMS), f32),
    }
    scratch |= {"fpart": v(part, bf16), "qpart": v(part, bf16), "spart": v(rows, f32), "leave_sems": sem((7,))}
    if remote:
        scratch |= {"ftotal": v(total, bf16), "qtotal": v(total, bf16), "stotal": v(rows, f32)}
        for name in ("f", "q"):
            keys = ("_core", "_tp", "_x", "_z", "_sends", "_recvs")
            scratch |= {name + key: item for key, item in zip(keys, big_scratch())}
        keys = ("s_near", "s_z", "s_sends", "s_recvs")
        scratch |= dict(zip(keys, small_scratch()))
        scratch |= {"gather_sends": sem((6, 4)), "gather_recvs": sem((6, 4))}
    scratch |= near_inputs | {"input_sems": sem((len(near_inputs),))}
    names = in_names + list(outs) + list(near) + list(scratch)
    results = pl.pallas_call(
        functools.partial(layer_kernel, remote, names, list(near_inputs)),
        in_specs=[pl.BlockSpec(memory_space=space(name)) for name in in_names],
        out_specs=[pl.BlockSpec(memory_space=pl.ANY)] * (len(outs) + len(near)),
        out_shape=[jax.ShapeDtypeStruct(*item) for item in list(outs.values()) + list(near.values())],
        scratch_shapes=list(scratch.values()),
        compiler_params=pltpu.CompilerParams(
            vmem_limit_bytes=VMEM_BYTES, **(dict(collective_id=0, has_side_effects=True) if remote else {})
        ),
        name="layer",
    )(*arrays.values())
    return results[0], results[1], results[len(outs) :]


def unpack_kernel(
    qsum, up_sum, proj_low, proj_high, down_low, down_high, out_rows, in_rows, rows_ref,
    output, grad_input, again, ashift, qkv, proj, fgain, fshift, up, up_bias, down, down_bias, scale, shift, centers,
    spreads, first, first_bias, second, hop, edge,
):
    output[...] = out_rows[...]
    grad_input[...] = in_rows[...]
    qkv[...] = qsum[...].astype(f32)
    up[...] = up_sum[0].astype(f32)
    for low, high, ref in ((proj_low, proj_high, proj), (down_low, down_high, down)):
        ref[:, :HALF_D] = low[0].astype(f32)
        ref[:, HALF_D:] = high[0].astype(f32)

    @pl.when(pl.program_id(0) == 0)
    def _():
        for v, ref in enumerate((again, ashift, fgain, fshift, up_bias, down_bias)):
            for i in range(D // 128):
                ref[pl.ds(128 * i, 128)] = rows_ref[VECTOR_ROWS + v * (D // 128) + i, :]
        first[...] = rows_ref[0:K, :]
        second[...] = rows_ref[SECOND_ROWS : SECOND_ROWS + H, :]
        table = rows_ref[TABLE_ROWS : TABLE_ROWS + H, :]
        scale[...] = table[:ATOMS, HOT : HOT + ATOMS]
        shift[...] = table[ATOMS:, HOT : HOT + ATOMS]
        turned = square_turn(table)
        hop[...] = turned[:HOPS, :H]
        edge[...] = turned[HOPS : HOPS + EDGES, :H]
        for i, ref in enumerate((first_bias, centers, spreads)):
            ref[...] = rows_ref[KERNEL_ROWS + i, :]


def unpack(out_rows, in_rows, fsum, qsum, rows):
    steps = 4
    tokens = out_rows.shape[0]
    shape = jax.ShapeDtypeStruct
    vec, line = shape((D,), f32), shape((K,), f32)
    mat = lambda *dims: shape(dims, f32)
    whole = lambda item: pl.BlockSpec(item.shape, lambda i: (0,) * len(item.shape))
    by_rows = lambda count, lanes: pl.BlockSpec((count // steps, lanes), lambda i: (i, 0))
    piece = lambda block, count, skip: pl.BlockSpec((1, count, HALF_D), lambda i: (block, i + skip, 0))
    token_rows = by_rows(tokens, D)
    all_q = pl.BlockSpec((3, D // steps, HALF_D), lambda i: (0, i, 0))
    half = HALF_D // steps
    small = [mat(ATOMS, ATOMS), mat(ATOMS, ATOMS), line, line, mat(K, K), line, mat(H, K), mat(HOPS, H), mat(EDGES, H)]
    return pl.pallas_call(
        unpack_kernel,
        grid=(steps,),
        in_specs=[
            all_q, piece(0, D // steps, 0), piece(1, half, 0), piece(1, half, steps), piece(2, half, 0),
            piece(2, half, steps), token_rows, token_rows, whole(rows),
        ],
        out_specs=[
            token_rows, token_rows, whole(vec), whole(vec), all_q, by_rows(HALF_D, D), whole(vec), whole(vec),
            by_rows(D, HALF_D), whole(vec), by_rows(HALF_D, D), whole(vec),
        ] + [whole(item) for item in small],
        out_shape=[
            shape((tokens, D), bf16), shape((tokens, D), bf16), vec, vec, mat(3, D, HALF_D), mat(HALF_D, D), vec, vec,
            mat(D, HALF_D), vec, mat(HALF_D, D), vec,
        ] + small,
        compiler_params=pltpu.CompilerParams(vmem_limit_bytes=VMEM_BYTES),
        name="unpack",
    )(qsum, fsum, fsum, fsum, fsum, fsum, out_rows, in_rows, rows)


def whole_weights(qkv_weight, up_weight, proj_weight, down_weight):
    columns = lambda w: jnp.stack(jnp.split(w, 2, axis=-1))
    rows = lambda w: jnp.stack(jnp.split(w, 2, axis=0))
    gather = lambda w, dim: lax.all_gather(w, "tp", axis=dim, tiled=True)
    return (
        columns(gather(qkv_weight.transpose(1, 0, 2), 2)), columns(gather(up_weight, 1)),
        rows(gather(proj_weight, 0)), rows(gather(down_weight, 0)),
    )


def sum_grads(fgrads, qgrads, small):
    total_f, total_q, rows = lax.psum((fgrads, qgrads, small), ("mol", "tp"))
    share = D // lax.axis_size("tp")
    at = lax.axis_index("tp") * share
    columns = lambda w: lax.dynamic_slice_in_dim(jnp.concatenate([w[0], w[1]], axis=-1), at, share, w.ndim - 2)
    rows_of = lambda w: lax.dynamic_slice_in_dim(
        jnp.concatenate([jnp.concatenate([w[t, :HALF_D], w[t, HALF_D:]], axis=1) for t in range(2)]), at, share, 0
    )
    wide = lambda v: v.astype(f32)
    big = (wide(columns(total_q)), wide(columns(total_f[:, 0])), wide(rows_of(total_f[:, 1])), wide(rows_of(total_f[:, 2])))
    return big, rows


def body(
    mesh_shape,
    hidden_in, positions, atom_types, hop_counts, edge_types, lengths, branches,
    attn_gain, attn_shift, qkv_weight, proj_weight, ffn_gain, ffn_shift, up_weight, up_bias, down_weight, down_bias,
    kernel_scale, kernel_shift, centers, spreads, first_weight, first_bias, second_weight, hop_table, edge_table,
    cotangent,
):
    remote = mesh_shape["tp"] == 2 and mesh_shape["mol"] == 16 and branches.shape[0] == 8
    if remote:
        weights = (qkv_weight.transpose(1, 0, 2), up_weight, proj_weight, down_weight)
    else:
        weights = whole_weights(qkv_weight, up_weight, proj_weight, down_weight)
    arrays = dict(
        lengths=lengths, flags=branches.T, positions=positions, atoms=atom_types, hops=hop_counts.T,
        edges=edge_types.T, kernel_scale=kernel_scale, kernel_shift=kernel_shift, centers=centers, spreads=spreads,
        first_weight=first_weight, first_bias=first_bias, second_weight=second_weight.T, hop_table=hop_table,
        edge_table=edge_table, attn_gain=attn_gain, attn_shift=attn_shift, ffn_gain=ffn_gain, ffn_shift=ffn_shift,
        up_bias=up_bias, down_bias=down_bias, given_hidden=hidden_in, given_cotangent=cotangent,
        given_qkv=weights[0], given_up=weights[1], given_proj=weights[2], given_down=weights[3],
    )
    output, grad_input, sums = layer(remote, lengths.shape[0], hidden_in.shape[0], arrays)
    if remote:
        fsum, qsum, rows = sums
    else:
        big, rows = sum_grads(*sums)
        fsum = jnp.zeros((3, D, HALF_D), bf16)
        qsum = fsum
    output, grad_input, *grads = unpack(output, grad_input, fsum, qsum, rows)
    if not remote:
        grads[2], grads[6], grads[3], grads[8] = big
    grads[2] = grads[2].transpose(1, 0, 2)
    grads[16] = grads[16].T
    return (output, grad_input, *grads)


def solution(mesh):
    rows = P(("mol", "tp"), None)
    all_of = P()
    in_specs = (
        rows, P(None, ("mol", "tp")), P(("mol", "tp")), rows, rows, P("mol"), rows, all_of, all_of,
        P(None, None, "tp"), P("tp", None), all_of, all_of, P(None, "tp"), all_of, P("tp", None),
    ) + (all_of,) * 10 + (rows,)
    out_specs = (
        rows, rows, all_of, all_of, P(None, None, "tp"), P("tp", None), all_of, all_of, P(None, "tp"), all_of,
        P("tp", None),
    ) + (all_of,) * 10
    step = functools.partial(body, dict(mesh.shape))
    return jax.shard_map(step, mesh=mesh, in_specs=in_specs, out_specs=out_specs, check_vma=False)
```

```python
import functools
from types import SimpleNamespace

import jax
import jax.numpy as jnp
from jax import lax
from jax.experimental import pallas as pl
from jax.experimental.pallas import tpu as pltpu
from jax.sharding import PartitionSpec as P

D = 768
H = 32
HD = 24
FF = 768
K = 128
SLOT = 64
HALF = SLOT // 2
HALF_D = D // 2
PAIRS = SLOT * SLOT
HOPS = 16
EDGES = 8
ATOMS = 16
GROUP = 4
GROUPS = H // GROUP
HOT = 32

highest = lax.Precision.HIGHEST
neg_large = -1e30
root_tau = 2.5066282746310002
root_half = 0.7071067811865476
inv_root_tau = 0.3989422804014327
head_scale = HD ** (-0.5)
VMEM_BYTES = 62 * 1024 * 1024
TILE = 512

SECOND_ROWS = K
TABLE_ROWS = SECOND_ROWS + H
KERNEL_ROWS = TABLE_ROWS + H
VECTOR_ROWS = KERNEL_ROWS + 8
SMALL_ROWS = 256

MESH = pl.DeviceIdType.MESH
f32 = jnp.float32
bf16 = jnp.bfloat16


def dot_nn(left, right, precision=None):
    return lax.dot_general(left, right, (((1,), (0,)), ((), ())), precision=precision, preferred_element_type=f32)


def dot_nt(left, right, precision=None):
    return lax.dot_general(left, right, (((1,), (1,)), ((), ())), precision=precision, preferred_element_type=f32)


def dot_tn(left, right, precision=None):
    return lax.dot_general(left, right, (((0,), (0,)), ((), ())), precision=precision, preferred_element_type=f32)


def iota(shape, dim):
    return lax.broadcasted_iota(jnp.int32, shape, dim)


def gelu_parts(values):
    size = jnp.abs(values)
    bell = jnp.exp(values * values * -0.5)
    denominator = 1.0 + (0.3275911 * root_half) * size
    t = pl.reciprocal(denominator, approx=True)
    t = t * (2.0 - denominator * t)
    series = 0.5 * 1.061405429
    for factor in (-1.453152027, 1.421413741, -0.284496736, 0.254829592):
        series = series * t + 0.5 * factor
    tail = series * t * bell
    gelu = jnp.maximum(values, 0.0) - size * tail
    outer = tail - size * (bell * inv_root_tau)
    return gelu, jnp.where(values >= 0.0, 1.0 - outer, outer)


def to_column(row):
    size = row.shape[1]
    same = iota((size, size), 0) == iota((size, size), 1)
    return jnp.sum(jnp.where(same, row, 0.0), axis=1, keepdims=True)


def half_swap(values):
    return pltpu.roll(values, 64, 1)


def low_lanes(rows):
    return iota((rows, 128), 1) < 64


def vmem(count):
    return [pl.BlockSpec(memory_space=pltpu.VMEM)] * count


def row_of(ref):
    return ref[...].reshape(1, ref.shape[0])


def place():
    mol = lax.axis_index("mol")
    return mol % 2, (mol // 2) % 2, mol // 4, lax.axis_index("tp")


def greet(peers):
    barrier = pltpu.get_barrier_semaphore()
    for peer in peers:
        pl.semaphore_signal(barrier, inc=1, device_id=peer, device_id_type=MESH)
    pl.semaphore_wait(barrier, len(peers))


def window(group):
    first = GROUP * HD * group
    start = first // 128 * 128
    width = 128 if first - start + GROUP * HD <= 128 else 256
    return start, width, first - start


def head_masks(group, kind):
    _, width, offset = window(group)
    lane = iota((1, width), 1)
    return [
        ((lane >= offset + HD * h) & (lane < offset + HD * (h + 1))).astype(f32).astype(kind) for h in range(GROUP)
    ]


def spread_heads(values, group):
    return jnp.concatenate([values * mask for mask in head_masks(group, bf16)], axis=0)


def gather_heads(values, group):
    masks = head_masks(group, f32)
    total = values[:SLOT] * masks[0]
    for h in range(1, GROUP):
        total = total + values[SLOT * h : SLOT * (h + 1)] * masks[h]
    return total


def standardize(values):
    centred = values - jnp.mean(values, axis=-1, keepdims=True)
    inv_std = lax.rsqrt(jnp.mean(centred * centred, axis=-1, keepdims=True) + 1e-05)
    return centred * inv_std, inv_std


def norm_back(d_normed, scaled, inv_std, gain):
    weighted = d_normed * gain
    inner_a = jnp.mean(weighted, axis=-1, keepdims=True)
    inner_b = jnp.mean(weighted * scaled, axis=-1, keepdims=True)
    return inv_std * (weighted - inner_a - scaled * inner_b)


def column_sum(values):
    return jnp.sum(values, axis=0, keepdims=True)


class Peers:
    def __init__(self):
        self.core, self.x, self.z, self.tp = place()
        mol = lax.axis_index("mol")
        self.over_core = {"mol": mol + 1 - 2 * self.core}
        self.over_x = {"mol": mol + 2 - 4 * self.x}
        self.over_tp = {"tp": 1 - self.tp}
        self.turn = [lax.rem(self.z + d, 4) for d in range(4)]
        self.over_z = [{"mol": self.turn[d] * 4 + self.x * 2 + self.core} for d in range(4)]

    def neighbour(self, k):
        core = self.core + (1 - 2 * self.core) * (k & 1)
        x = self.x + (1 - 2 * self.x) * (k >> 1 & 1)
        tp = self.tp + (1 - 2 * self.tp) * (k >> 2)
        return core * 4 + tp * 2 + x, {"mol": self.z * 4 + x * 2 + core, "tp": tp}

    def everyone(self):
        return [self.neighbour(k)[1] for k in range(1, 8)] + self.over_z[1:]


def span(start, size):
    return pl.ds(pl.multiple_of(start, size), size)


def add_rows(target, source, rows):
    step = 96 if rows % 96 == 0 else rows

    def piece(i, _):
        at = pl.ds(pl.multiple_of(i * step, step), step)
        target[at, :] = (target[at, :].astype(f32) + source[at, :].astype(f32)).astype(target.dtype)
        return 0

    lax.fori_loop(0, rows // step, piece, 0)


class Reduction:
    def __init__(self, peers, part, total, from_core, from_tp, from_x, from_z, sends, recvs):
        self.peers, self.part, self.total = peers, part, total
        self.from_core, self.from_tp, self.from_x, self.from_z = from_core, from_tp, from_x, from_z
        self.sends, self.recvs = sends, recvs
        p = peers
        self.at_core = p.core * 384
        self.at_x = self.at_core + p.x * 192

    def copy(self, b, kind):
        p = self.peers
        part, total = self.part, self.total
        if kind == 0:
            src, dst, peer = part.at[:, b, span((1 - p.core) * 384, 384)], self.from_core.at[:, b], p.over_core
        elif kind == 1:
            src, dst, peer = part.at[1 - p.tp, b, span(self.at_core, 384)], self.from_tp.at[b], p.over_tp
        elif kind == 2:
            src, dst, peer = part.at[p.tp, b, span(self.at_core + (1 - p.x) * 192, 192)], self.from_x.at[b], p.over_x
        elif kind < 6:
            d = kind - 2
            src, dst, peer = part.at[p.tp, b, span(self.at_x + p.turn[d] * 48, 48)], self.from_z.at[b, d - 1], p.over_z[d]
        elif kind < 9:
            src = dst = total.at[b, span(self.at_x + p.z * 48, 48)]
            peer = p.over_z[kind - 5]
        elif kind == 9:
            src = dst = total.at[b, span(self.at_x, 192)]
            peer = p.over_x
        else:
            src = dst = total.at[b, span(self.at_core, 384)]
            peer = p.over_core
        return pltpu.make_async_remote_copy(
            src_ref=src, dst_ref=dst, send_sem=self.sends.at[b, kind], recv_sem=self.recvs.at[b, kind],
            device_id=peer, device_id_type=MESH,
        )

    def act(self, b, stage):
        p = self.peers
        if stage == 0:
            self.copy(b, 0).start()
        elif stage == 1:
            self.copy(b, 0).wait_recv()
            add_rows(self.part.at[1 - p.tp, b, span(self.at_core, 384)], self.from_core.at[1 - p.tp, b], 384)
            self.copy(b, 1).start()
            add_rows(self.part.at[p.tp, b, span(self.at_core, 384)], self.from_core.at[p.tp, b], 384)
        elif stage == 2:
            self.copy(b, 1).wait_recv()
            away, mine = (1 - p.x) * 192, p.x * 192
            add_rows(self.part.at[p.tp, b, span(self.at_core + away, 192)], self.from_tp.at[b, span(away, 192)], 192)
            self.copy(b, 2).start()
            add_rows(self.part.at[p.tp, b, span(self.at_core + mine, 192)], self.from_tp.at[b, span(mine, 192)], 192)
        elif stage == 3:
            self.copy(b, 2).wait_recv()
            add_rows(self.part.at[p.tp, b, span(self.at_x, 192)], self.from_x.at[b], 192)
            for kind in (3, 4, 5):
                self.copy(b, kind).start()
        elif stage == 4:
            for kind in (3, 4, 5):
                self.copy(b, kind).wait_recv()
            mine = span(self.at_x + p.z * 48, 48)
            value = self.part[p.tp, b, mine, :].astype(f32)
            for d in range(3):
                value = value + self.from_z[b, d].astype(f32)
            self.total[b, mine, :] = value.astype(bf16)
            for kind in (6, 7, 8):
                self.copy(b, kind).start()
        elif stage == 5:
            for kind in (6, 7, 8):
                self.copy(b, kind).wait_recv()
            self.copy(b, 9).start()
        elif stage == 6:
            self.copy(b, 9).wait_recv()
            self.copy(b, 10).start()
        elif stage == 7:
            self.copy(b, 10).wait_recv()
        else:
            for kind in range(11):
                self.copy(b, kind).wait_send()


class SmallReduction:
    def __init__(self, peers, part, total, from_near, from_z, sends, recvs):
        self.peers, self.part, self.total, self.from_near, self.from_z = peers, part, total, from_near, from_z
        self.sends, self.recvs = sends, recvs
        p = peers
        self.near = [p.neighbour(k) for k in range(8)]
        self.at_near = self.near[0][0] * 32

    def copy(self, kind):
        p = self.peers
        part, total = self.part, self.total
        if kind < 7:
            index, peer = self.near[kind + 1]
            src, dst = part.at[span(index * 32, 32)], self.from_near.at[kind]
        elif kind < 10:
            d = kind - 6
            src, dst, peer = part.at[span(self.at_near + p.turn[d] * 8, 8)], self.from_z.at[d - 1], p.over_z[d]
        elif kind < 13:
            src = dst = total.at[span(self.at_near + p.z * 8, 8)]
            peer = p.over_z[kind - 9]
        else:
            src = dst = total.at[span(self.at_near, 32)]
            peer = self.near[kind - 12][1]
        return pltpu.make_async_remote_copy(
            src_ref=src, dst_ref=dst, send_sem=self.sends.at[kind], recv_sem=self.recvs.at[kind],
            device_id=peer, device_id_type=MESH,
        )

    def act(self, stage):
        p = self.peers
        hops = (range(0, 7), range(7, 10), range(10, 13), range(13, 20))
        if stage == 5:
            for kind in range(20):
                self.copy(kind).wait_send()
            return
        if stage > 0:
            for kind in hops[stage - 1]:
                self.copy(kind).wait_recv()
        if stage == 1:
            mine = span(self.at_near, 32)
            value = self.part[mine, :]
            for k in range(7):
                value = value + self.from_near[k]
            self.part[mine, :] = value
        elif stage == 2:
            mine = span(self.at_near + p.z * 8, 8)
            self.total[mine, :] = self.part[mine, :] + self.from_z[0] + self.from_z[1] + self.from_z[2]
        if stage < 4:
            for kind in hops[stage]:
                self.copy(kind).start()


def big_scratch():
    return [
        pltpu.VMEM((2, 3, 384, HALF_D), bf16), pltpu.VMEM((3, 384, HALF_D), bf16), pltpu.VMEM((3, 192, HALF_D), bf16),
        pltpu.VMEM((3, 3, 48, HALF_D), bf16), pltpu.SemaphoreType.DMA((3, 11)), pltpu.SemaphoreType.DMA((3, 11)),
    ]


def small_scratch():
    return [
        pltpu.VMEM((7, 32, 128), f32), pltpu.VMEM((3, 8, 128), f32),
        pltpu.SemaphoreType.DMA((20,)), pltpu.SemaphoreType.DMA((20,)),
    ]


class Gather:
    pieces = 6

    def __init__(self, peers, whole, sends, recvs):
        self.peers, self.whole, self.sends, self.recvs = peers, whole, sends, recvs
        self.quarter = peers.x * 2 + peers.core
        self.next_quarter = (1 - peers.x) * 2 + peers.core

    def rows(self, ref, quarter):
        count = ref.shape[0] // 4
        return ref.at[span(quarter * count, count), :]

    def copy(self, index, kind):
        p = self.peers
        if kind == 0:
            src = dst = self.rows(self.whole(index, p.tp), self.quarter)
            peer = p.over_tp
        elif kind == 1:
            src = dst = self.rows(self.whole(index, 1 - p.tp), self.quarter)
            peer = p.over_x
        else:
            src = dst = self.rows(self.whole(index, 1 - p.tp), self.quarter if kind == 2 else self.next_quarter)
            peer = p.over_core
        return pltpu.make_async_remote_copy(
            src_ref=src, dst_ref=dst, send_sem=self.sends.at[index, kind], recv_sem=self.recvs.at[index, kind],
            device_id=peer, device_id_type=MESH,
        )

    def start(self, indices):
        for index in indices:
            self.copy(index, 0).start()

    def onward_x(self, index):
        self.copy(index, 0).wait_recv()
        self.copy(index, 1).start()
        self.copy(index, 2).start()

    def onward_core(self, index):
        self.copy(index, 1).wait_recv()
        self.copy(index, 3).start()

    def arrive(self, index):
        self.copy(index, 2).wait_recv()
        self.copy(index, 3).wait_recv()

    def finish(self):
        for index in range(self.pieces):
            for kind in range(4):
                self.copy(index, kind).wait_send()


def widen(values):
    return jnp.concatenate([values] * (TILE // 128), axis=1)


def strips():
    return [slice(16 * i, 16 * (i + 1)) for i in range(K // 16)]


def four_rows(ref, slot, first):
    return jnp.concatenate([ref[slot, pl.ds(first + i, 1), :] for i in range(TILE // 128)], axis=1)


def hot_rows(values, count):
    return (values == iota((count, TILE), 0).astype(f32)).astype(f32)


def fold_lanes(values):
    total = values[:, :128]
    for i in range(1, TILE // 128):
        total = total + values[:, 128 * i : 128 * (i + 1)]
    return total


def prepare_columns(r):
    spr = to_column(row_of(r.spreads))
    r.cols[0] = jnp.broadcast_to(to_column(row_of(r.centers)), (K, 128))
    r.cols[4] = jnp.broadcast_to(1.0 / spr, (K, 128))
    second = r.second_weight[...].astype(f32)
    r.w2[...] = jnp.concatenate([second, jnp.zeros((128 - H, K), f32)], axis=0).T.astype(bf16)


def prepare_pairs(r):
    spr = to_column(row_of(r.spreads))
    r.cols[0] = jnp.broadcast_to(to_column(row_of(r.centers)), (K, 128))
    r.cols[1] = jnp.broadcast_to(root_half / spr, (K, 128))
    r.cols[2] = jnp.broadcast_to(-jnp.log(root_tau * spr), (K, 128))
    r.cols[3] = jnp.broadcast_to(to_column(row_of(r.first_bias)), (K, 128))
    r.w1t[...] = r.first_weight[...].astype(f32).T.astype(bf16)
    table = jnp.concatenate([r.hop_table[...], r.edge_table[...], jnp.zeros((128 - HOPS - EDGES, H), f32)], axis=0)
    table = jnp.concatenate([table, jnp.zeros((128, 128 - H), f32)], axis=1).T[:H, :HOT]
    one = table.astype(bf16).astype(f32)
    r.base[...] = jnp.concatenate(
        [r.second_weight[...].astype(f32), one, table - one, jnp.zeros((H, 64), f32)], axis=1
    )


def pair_tables(r, slot):
    low = low_lanes(HALF)
    low_row = low_lanes(1)
    lanes = span(lax.div(slot, 2) * 128, 128)
    turn = lax.rem(slot, 2) * 64
    atoms = r.atoms[lanes].astype(f32).reshape(1, 128)
    rows = [pltpu.roll(row, turn, 1) for row in [r.positions[c : c + 1, lanes] for c in range(3)] + [atoms]]
    double = [jnp.where(low_row, row, half_swap(row)) for row in rows]
    columns = [to_column(row[:, :SLOT]) for row in rows]
    total = None
    for c in range(3):
        offset = jnp.where(low, columns[c][:HALF], columns[c][HALF:]) - double[c]
        total = offset * offset if total is None else total + offset * offset
    distance = jnp.sqrt(total)
    key_hot = (columns[3] == iota((SLOT, ATOMS), 1).astype(f32)).astype(f32)
    query_hot = (double[3] == iota((ATOMS, 128), 0).astype(f32)).astype(f32)
    picked = []
    for table in (r.kernel_scale, r.kernel_shift):
        both = dot_nn(dot_nt(key_hot, table[...], highest), query_hot, highest)
        picked.append(jnp.where(low, both[:HALF], both[HALF:]))
    r.argument[slot] = picked[0] * distance + picked[1]
    r.distance[slot] = distance
    for source, target in ((r.hops, r.hop_rows), (r.edges, r.edge_rows)):
        values = pltpu.roll(source[:, lanes].astype(f32), turn, 1)
        target[slot] = jnp.where(low, values[:HALF], half_swap(values[HALF:]))
    r.atom_rows[slot] = jnp.broadcast_to(double[3], (8, 128))


def pair_forward(r, slot):
    bank = lax.rem(slot, 2)
    graph_on = r.flags[0, slot].astype(f32)
    space_on = r.flags[1, slot].astype(f32)
    factor = jnp.where(iota((H, 256), 1) < K, space_on, graph_on)
    r.lhs[...] = (r.base[...] * factor).astype(bf16)

    def tile(t, _):
        for part in range(2):
            first_row = 8 * t + 4 * part
            where = span(t * 2 * TILE + part * TILE, TILE)
            arg = four_rows(r.argument, slot, first_row)
            pieces = []
            for rows in strips():
                u = (arg - widen(r.cols[0, rows])) * widen(r.cols[1, rows])
                pieces.append(jnp.exp(widen(r.cols[2, rows]) - u * u).astype(bf16))
                r.gauss[bank, rows, where] = pieces[-1]
            first = dot_nn(r.w1t[...], jnp.concatenate(pieces, axis=0))
            pieces = []
            for rows in strips():
                value, slope = gelu_parts(first[rows] + widen(r.cols[3, rows]))
                pieces.append(value.astype(bf16))
                r.second[bank, rows, where] = pieces[-1]
                r.slope[bank, rows, where] = slope.astype(bf16)
            hot = jnp.concatenate(
                [
                    hot_rows(four_rows(r.hop_rows, slot, first_row), HOPS),
                    hot_rows(four_rows(r.edge_rows, slot, first_row), HOT - HOPS),
                ],
                axis=0,
            ).astype(bf16)
            bias = dot_nn(r.lhs[:, : K + 2 * HOT], jnp.concatenate(pieces + [hot] * 2, axis=0))
            bias = bias.astype(bf16).astype(f32)
            for i in range(TILE // 128):
                r.bias[slot, pl.ds(first_row + i, H, stride=HALF), :] = bias[:, 128 * i : 128 * (i + 1)]
        return 0

    lax.fori_loop(0, PAIRS // (2 * TILE), tile, 0)


def pair_backward(r, slot, between):
    bank = lax.rem(slot, 2)
    graph_on = r.flags[0, slot].astype(f32)
    space_on = r.flags[1, slot].astype(f32)
    w2 = r.w2[:, :H] * space_on.astype(bf16)

    def tile(t, _):
        for part in range(2):
            first_row = 8 * t + 4 * part
            where = span(t * 2 * TILE + part * TILE, TILE)
            arg = four_rows(r.argument, slot, first_row)
            grad = jnp.concatenate(
                [r.bias[slot, pl.ds(first_row + i, H, stride=HALF), :] for i in range(TILE // 128)], axis=1
            )
            r.dspace[:, where] = jnp.concatenate([grad * space_on, grad * graph_on], axis=0).astype(bf16)
            d_second = dot_nn(w2, grad.astype(bf16))
            pieces = []
            for rows in strips():
                pieces.append((d_second[rows] * r.slope[bank, rows, where].astype(f32)).astype(bf16))
                r.dfirst[rows, where] = pieces[-1]
            d_gauss = dot_nn(r.first_weight[...], jnp.concatenate(pieces, axis=0))
            d_arg = None
            for rows in strips():
                inv = widen(r.cols[4, rows])
                u = (arg - widen(r.cols[0, rows])) * inv
                q = d_gauss[rows] * r.gauss[bank, rows, where].astype(f32)
                w = q * u
                r.sums[0, rows] += fold_lanes(w)
                r.sums[1, rows] += fold_lanes(w * u - q)
                w = w * inv
                w = w[:8] + w[8:]
                d_arg = w if d_arg is None else d_arg + w
            d_arg = -jnp.sum(d_arg, axis=0, keepdims=True)
            for i in range(TILE // 128):
                r.dargs[pl.ds(first_row + i, 1), :] = d_arg[:, 128 * i : 128 * (i + 1)]
            edge_hot = hot_rows(four_rows(r.edge_rows, slot, first_row), HOT - HOPS)
            edge_hot = jnp.where(iota((HOT - HOPS, TILE), 0) == EDGES, 1.0, edge_hot)
            r.hots[:, where] = jnp.concatenate(
                [hot_rows(four_rows(r.hop_rows, slot, first_row), HOPS), edge_hot], axis=0
            ).astype(bf16)
        return 0

    lax.fori_loop(0, PAIRS // (2 * TILE), tile, 0)
    between()
    left = jnp.concatenate([r.gauss[bank], r.second[bank], r.hots[...]], axis=0)
    r.acc_mixed[...] += dot_nt(left, jnp.concatenate([r.dfirst[...], r.dspace[...]], axis=0))
    query_hot = (r.atom_rows[slot, 0:1, :] == iota((ATOMS, 128), 0).astype(f32)).astype(f32)
    for index in range(2):
        values = r.dargs[...] * r.distance[slot] if index == 0 else r.dargs[...]
        part = jnp.where(
            low_lanes(ATOMS),
            dot_nn(query_hot[:, :HALF], values, highest),
            dot_nn(query_hot[:, HALF:SLOT], values, highest),
        )
        r.acc_table[index] += dot_nt(query_hot, part, highest)


def attend(r, s, first_slot):
    low = low_lanes(HALF)
    rows = span(s * SLOT, SLOT)
    valid = iota((SLOT, GROUP * SLOT), 0) < r.lengths[first_slot + s]
    r.work[0] = jnp.zeros((SLOT, D), f32)
    for g in range(GROUPS):
        start, width, _ = window(g)
        q = r.joined[rows, start : start + width]
        k = r.joined[rows, D + start : D + start + width]
        v = r.joined[rows, 2 * D + start : 2 * D + start + width]
        scores = dot_nt(k, spread_heads(q, g)) * head_scale
        parts = []
        for pair in range(GROUP // 2):
            head = GROUP * g + 2 * pair
            one = r.bias[s, head * HALF : (head + 1) * HALF, :]
            two = r.bias[s, (head + 1) * HALF : (head + 2) * HALF, :]
            top = jnp.where(low, one, half_swap(two))
            bottom = jnp.where(low, half_swap(one), two)
            parts.append(jnp.concatenate([top, bottom], axis=0))
        scores = jnp.where(valid, scores + jnp.concatenate(parts, axis=1), neg_large)
        weights = jnp.exp(scores - jnp.max(scores, axis=0, keepdims=True))
        prob = (weights * (1.0 / jnp.sum(weights, axis=0, keepdims=True))).astype(bf16)
        r.prob[s, :, g * GROUP * SLOT : (g + 1) * GROUP * SLOT] = prob
        r.work[0, :, start : start + width] += gather_heads(dot_tn(prob, v), g)
    r.attended[rows, :] = r.work[0].astype(bf16)


def attend_back(r, s):
    low = low_lanes(HALF)
    rows = span(s * SLOT, SLOT)
    r.work[...] = jnp.zeros((3, SLOT, D), f32)
    for g in range(GROUPS):
        start, width, _ = window(g)
        lanes = slice(start, start + width)
        k = r.joined[rows, D + start : D + start + width]
        v = r.joined[rows, 2 * D + start : 2 * D + start + width]
        q_heads = spread_heads(r.joined[rows, lanes], g)
        d_heads = spread_heads(r.d_attended[rows, lanes], g)
        prob = r.prob[s, :, g * GROUP * SLOT : (g + 1) * GROUP * SLOT]
        wide = prob.astype(f32)
        d_prob = dot_nt(v, d_heads)
        inner = jnp.sum(wide * d_prob, axis=0, keepdims=True)
        d_scores = (wide * (d_prob - inner)).astype(bf16)
        r.work[0, :, lanes] += gather_heads(dot_tn(d_scores, k), g)
        r.work[1, :, lanes] += dot_nn(d_scores, q_heads)
        r.work[2, :, lanes] += dot_nn(prob, d_heads)
        d_wide = d_scores.astype(f32)
        for pair in range(GROUP // 2):
            head = GROUP * g + 2 * pair
            top = d_wide[:HALF, 128 * pair : 128 * (pair + 1)]
            bottom = d_wide[HALF:, 128 * pair : 128 * (pair + 1)]
            r.bias[s, head * HALF : (head + 1) * HALF, :] = jnp.where(low, top, half_swap(bottom))
            r.bias[s, (head + 1) * HALF : (head + 2) * HALF, :] = jnp.where(low, half_swap(top), bottom)
    r.joined[rows, 0:D] = (r.work[0] * head_scale).astype(bf16)
    r.joined[rows, D : 2 * D] = (r.work[1] * head_scale).astype(bf16)
    r.joined[rows, 2 * D : 3 * D] = r.work[2].astype(bf16)


def project(r, rows):
    scaled, _ = standardize(r.hidden[rows, :].astype(f32))
    normed = (scaled * row_of(r.attn_gain) + row_of(r.attn_shift)).astype(bf16)
    r.normed_a[rows, :] = normed
    for m in range(3):
        for t in range(2):
            at = m * D + t * HALF_D
            r.joined[rows, at : at + HALF_D] = dot_nn(normed, r.wqkv[t, m]).astype(bf16)


def feed(r, rows):
    halves = [slice(0, HALF_D), slice(HALF_D, D)]
    resid = r.hidden[rows, :].astype(f32)
    for t in range(2):
        resid = resid + dot_nn(r.attended[rows, halves[t]], r.wproj[t])
    scaled, inv_std = standardize(resid)
    normed = (scaled * row_of(r.ffn_gain) + row_of(r.ffn_shift)).astype(bf16)
    r.normed_f[rows, :] = normed
    pre = jnp.concatenate([dot_nn(normed, r.wup[t]) for t in range(2)], axis=1)
    value, slope = gelu_parts(pre + row_of(r.up_bias))
    active = value.astype(bf16)
    r.activated[rows, :] = active
    result = resid + row_of(r.down_bias)
    for t in range(2):
        result = result + dot_nn(active[:, halves[t]], r.wdown[t])
    r.out_rows[rows, :] = result.astype(bf16)
    cot = r.cotangent[rows, :]
    cot_wide = cot.astype(f32)
    d_active = jnp.concatenate([dot_nt(cot, r.wdown[t]) for t in range(2)], axis=1)
    d_hidden = (d_active * slope).astype(bf16)
    r.d_pre[rows, :] = d_hidden
    d_normed = dot_nt(d_hidden[:, halves[0]], r.wup[0]) + dot_nt(d_hidden[:, halves[1]], r.wup[1])
    d_resid = cot_wide + norm_back(d_normed, scaled, inv_std, row_of(r.ffn_gain))
    r.d_resid[rows, :] = d_resid
    branch = d_resid.astype(bf16)
    r.d_branch[rows, :] = branch
    for t in range(2):
        r.d_attended[rows, halves[t]] = dot_nt(branch, r.wproj[t]).astype(bf16)
    r.vectors[2:3, :] += column_sum(d_normed * scaled)
    r.vectors[3:4, :] += column_sum(d_normed)
    r.vectors[4:5, :] += column_sum(d_hidden.astype(f32))
    r.vectors[5:6, :] += column_sum(cot_wide)


def feed_grads(r, block):
    for t in range(2):
        half = slice(t * HALF_D, (t + 1) * HALF_D)
        if block == 0:
            r.fpart[t, 0] = dot_tn(r.normed_f[...], r.d_pre[:, half]).astype(bf16)
        else:
            left, right = (r.attended, r.d_branch) if block == 1 else (r.activated, r.cotangent)
            grad = dot_tn(left[:, half], right[...]).astype(bf16)
            r.fpart[t, block, :HALF_D, :] = grad[:, :HALF_D]
            r.fpart[t, block, HALF_D:, :] = grad[:, HALF_D:]


def finish_input(r, rows):
    d_normed = None
    for m in range(3):
        for t in range(2):
            at = m * D + t * HALF_D
            term = dot_nt(r.joined[rows, at : at + HALF_D], r.wqkv[t, m])
            d_normed = term if d_normed is None else d_normed + term
    scaled, inv_std = standardize(r.hidden[rows, :].astype(f32))
    grad = r.d_resid[rows, :] + norm_back(d_normed, scaled, inv_std, row_of(r.attn_gain))
    r.in_rows[rows, :] = grad.astype(bf16)
    r.vectors[0:1, :] += column_sum(d_normed * scaled)
    r.vectors[1:2, :] += column_sum(d_normed)


def square_turn(values):
    rows, lanes = values.shape
    if lanes < 128:
        values = jnp.concatenate([values, jnp.zeros((rows, 128 - lanes), f32)], axis=1)
    if rows < 128:
        values = jnp.concatenate([values, jnp.zeros((128 - rows, 128), f32)], axis=0)
    return values.T


def pack_small(r):
    for v in range(6):
        for i in range(D // 128):
            at = VECTOR_ROWS + v * (D // 128) + i
            r.spart[at : at + 1, :] = r.vectors[v : v + 1, 128 * i : 128 * (i + 1)]
    r.spart[0:K, :] = r.acc_mixed[0:K, :K]
    r.spart[SECOND_ROWS : SECOND_ROWS + H, :] = square_turn(r.acc_mixed[K : 2 * K, K:])[:H]
    r.spart[TABLE_ROWS : TABLE_ROWS + H, :HOT] = square_turn(r.acc_mixed[2 * K :, K:])[H : 2 * H, :HOT]
    for index in range(2):
        rows = slice(TABLE_ROWS + ATOMS * index, TABLE_ROWS + ATOMS * (index + 1))
        r.spart[rows, HOT : HOT + ATOMS] = r.acc_table[index]
    ones = 2 * K + HOPS + EDGES
    r.spart[KERNEL_ROWS : KERNEL_ROWS + 1, :] = r.acc_mixed[ones : ones + 1, :K]
    for index in range(2):
        column = jnp.sum(r.sums[index] * r.cols[4], axis=1, keepdims=True)
        same = iota((K, K), 0) == iota((K, K), 1)
        at = KERNEL_ROWS + 1 + index
        r.spart[at : at + 1, :] = jnp.sum(jnp.where(same, column, 0.0), axis=0, keepdims=True)


class Stage:
    def __init__(self, names, near_inputs, carried, refs):
        self.r = SimpleNamespace(**dict(zip(names, refs)))
        r = self.r
        self.loads = {
            name: pltpu.make_async_copy(getattr(r, "given_" + name), getattr(r, name), r.input_sems.at[i])
            for i, name in enumerate(near_inputs)
        }
        self.stores = {
            name: pltpu.make_async_copy(getattr(r, name), getattr(r, name + "_far"), r.carry_sems.at[i])
            for i, name in enumerate(carried)
        }

    def load(self, *names):
        for name in names:
            self.loads[name].start()

    def need(self, *names):
        for name in names:
            self.loads[name].wait()

    def store(self, *names):
        for name in names:
            self.stores[name].start()

    def stored(self):
        for copy in self.stores.values():
            copy.wait()


def each_chunk(r, tokens, work):
    chunk = min(256, tokens)

    def one(c, _):
        work(r, span(c * chunk, chunk))
        return 0

    lax.fori_loop(0, tokens // chunk, one, 0)


def pair_moves(r, slot, back):
    bank = lax.rem(slot, 2)
    for index, name in enumerate(("gauss", "second", "slope")):
        far, near = getattr(r, name + "_far").at[slot], getattr(r, name).at[bank]
        yield pltpu.make_async_copy(*((far, near) if back else (near, far)), r.pair_sems.at[bank, index])


def start_moves(r, slot, back):
    for copy in pair_moves(r, slot, back):
        copy.start()


def wait_moves(r, slot, back):
    for copy in pair_moves(r, slot, back):
        copy.wait()


def run(steps):
    for act, *where in steps:
        act(*where)


def at_time(index, plan):
    for k, steps in plan.items():
        pl.when(index == k)(functools.partial(run, steps))


def forward_kernel(remote, names, near_inputs, carried, *refs):
    stage = Stage(names, near_inputs, carried, refs)
    r = stage.r
    weights = ("qkv", "up", "proj", "down")
    stage.load(*[name for name in near_inputs if name not in ("hidden", "cotangent")])
    tokens = r.hidden.shape[0]
    slots = tokens // SLOT
    peers = Peers()
    whole = [r.wqkv, r.wup, r.wproj, r.wdown]
    given = [r.given_qkv, r.given_up, r.given_proj, r.given_down]
    targets = [w.at[peers.tp] for w in whole] if remote else whole
    loads = [
        pltpu.make_async_copy(src, dst, r.load_sems.at[i]) for i, (src, dst) in enumerate(zip(given, targets))
    ]
    for load in loads:
        load.start()
    stage.load("hidden", "cotangent")
    gather_plan = {}
    if remote:

        def whole_piece(index, tp):
            return whole[0].at[tp, index] if index < 3 else whole[index - 2].at[tp]

        gather = Gather(peers, whole_piece, r.gather_sends, r.gather_recvs)
        greet([peers.over_tp, peers.over_x, peers.over_core])
        for load, indices in zip(loads, ((0, 1, 2), (3,), (4,), (5,))):
            load.wait()
            gather.start(indices)
        x, core = gather.onward_x, gather.onward_core
        gather_plan = {
            0: [(x, 0)], 1: [(x, 1), (core, 0)], 2: [(x, 2), (core, 1)], 3: [(x, 3), (core, 2)],
            4: [(x, 4), (core, 3), (x, 5)], 5: [(core, 4)], 6: [(core, 5)],
        }
    stage.need(*[name for name in near_inputs if name not in ("hidden", "cotangent")])
    prepare_pairs(r)

    def pairs(slot, _):
        pair_tables(r, slot)
        pl.when(slot >= 2)(lambda: wait_moves(r, slot - 2, False))
        pair_forward(r, slot)
        start_moves(r, slot, False)
        at_time(slot, gather_plan)
        return 0

    lax.fori_loop(0, slots, pairs, 0)
    stage.store("argument", "distance", "hop_rows", "edge_rows", "atom_rows")
    stage.need("hidden")
    if remote:
        for index in range(3):
            gather.arrive(index)
    else:
        for load in loads:
            load.wait()
    stage.store("wqkv")
    each_chunk(r, tokens, project)
    stage.store("normed_a", "joined")
    first_slot = peers.tp * slots

    def attend_one(s, _):
        attend(r, s, first_slot)
        return 0

    lax.fori_loop(0, slots, attend_one, 0)
    stage.store("prob")
    stage.need("cotangent")
    if remote:
        for index in range(3, 6):
            gather.arrive(index)
    r.vectors[...] = jnp.zeros_like(r.vectors)
    each_chunk(r, tokens, feed)
    stage.store("out_rows", "d_resid", "d_attended", "vectors")
    for block in range(3):
        feed_grads(r, block)
    stage.store("fpart")
    for slot in (slots - 2, slots - 1):
        wait_moves(r, slot, False)
    if remote:
        gather.finish()
    stage.stored()


def backward_kernel(remote, names, near_inputs, carried, *refs):
    stage = Stage(names, near_inputs, carried, refs)
    r = stage.r
    first = ["fpart"] if remote else []
    first += ["joined", "prob", "d_attended"]
    stage.load(*first)
    stage.load(*[name for name in near_inputs if name not in first])
    tokens = r.hidden.shape[0]
    slots = tokens // SLOT
    start_moves(r, 0, True)
    start_moves(r, 1, True)
    plans = [{}, {}]
    if remote:
        peers = Peers()
        ffn = Reduction(peers, r.fpart, r.ftotal, r.f_core, r.f_tp, r.f_x, r.f_z, r.f_sends, r.f_recvs)
        qkv = Reduction(peers, r.qpart, r.qtotal, r.q_core, r.q_tp, r.q_x, r.q_z, r.q_sends, r.q_recvs)
        small = SmallReduction(peers, r.spart, r.stotal, r.s_near, r.s_z, r.s_sends, r.s_recvs)
        f, q = ffn.act, qkv.act
        plans = [
            {
                0: [(f, 1, 1), (f, 2, 1)], 3: [(f, 0, 2)], 4: [(f, 0, 3)], 5: [(f, 0, 4), (f, 1, 2)],
                6: [(f, 0, 5), (f, 1, 3)], 7: [(f, 0, 6), (f, 1, 4)],
            },
            {
                0: [(f, 2, 4), (q, 0, 2)], 1: [(f, 2, 5)], 2: [(q, 0, 3), (f, 2, 6)], 3: [(q, 1, 2)],
                4: [(q, 0, 4), (q, 1, 3)], 5: [(q, 0, 5)], 6: [(q, 2, 2), (q, 1, 4), (q, 0, 6)],
                7: [(q, 2, 3), (q, 1, 5)], 8: [(q, 2, 4), (q, 1, 6)], 9: [(q, 2, 5)], 10: [(q, 2, 6)],
            },
        ]
        greet(peers.everyone())
        stage.need("fpart")
        run([(f, 0, 0), (f, 1, 0), (f, 2, 0)])
    stage.need(*[name for name in near_inputs if name != "fpart"])
    if remote:
        run([(f, 0, 1)])

    def back_one(s, _):
        attend_back(r, s)
        at_time(s, plans[0])
        return 0

    lax.fori_loop(0, slots, back_one, 0)
    for m in range(3):
        for t in range(2):
            at = m * D + t * HALF_D
            r.qpart[t, m] = dot_tn(r.normed_a[...], r.joined[:, at : at + HALF_D]).astype(bf16)
        if remote:
            q(m, 0)
    if remote:
        run([(q, 0, 1), (f, 2, 2), (f, 1, 5)])
    each_chunk(r, tokens, finish_input)
    stage.store("in_rows")
    if remote:
        run([(q, 1, 1), (q, 2, 1), (f, 2, 3), (f, 1, 6)])
    for ref in (r.sums, r.acc_mixed, r.acc_table, r.spart):
        ref[...] = jnp.zeros_like(ref)
    prepare_columns(r)

    def pairs_back(slot, _):
        wait_moves(r, slot, True)
        pair_backward(r, slot, lambda: at_time(2 * slot, plans[1]))
        pl.when(slot + 2 < slots)(lambda: start_moves(r, slot + 2, True))
        at_time(2 * slot + 1, plans[1])
        return 0

    lax.fori_loop(0, slots, pairs_back, 0)
    pack_small(r)
    if remote:
        leave = [
            pltpu.make_async_copy(near.at[b], far.at[b], r.leave_sems.at[3 * i + b])
            for i, (near, far) in enumerate(((r.ftotal, r.ftotal_far), (r.qtotal, r.qtotal_far)))
            for b in range(3)
        ]
        small.act(0)
        for b in range(3):
            f(b, 7)
            leave[b].start()
        small.act(1)
        for b in range(3):
            q(b, 7)
            leave[3 + b].start()
        for step in (2, 3, 4):
            small.act(step)
        leave.append(pltpu.make_async_copy(r.stotal, r.stotal_far, r.leave_sems.at[6]))
        leave[6].start()
        for b in range(3):
            f(b, 8)
            q(b, 8)
        small.act(5)
        for copy in leave:
            copy.wait()
    else:
        stage.store("qpart", "spart")
    stage.stored()


def call_stage(kernel, name, remote, collective, arrays, scalars, far, outs, carried, scratch):
    vm, sem = pltpu.VMEM, pltpu.SemaphoreType.DMA
    near = {n: vm(a.shape, a.dtype) for n, a in arrays.items() if n not in scalars + far}
    in_names = [n if n in scalars or n.endswith("_far") else "given_" + n for n in arrays]
    results = outs | {n + "_far": item for n, item in carried.items()}
    scratch = near | {n: vm(*item) for n, item in carried.items()} | scratch
    scratch |= {"input_sems": sem((len(near),)), "carry_sems": sem((len(carried),))}
    names = in_names + list(results) + list(scratch)
    values = pl.pallas_call(
        functools.partial(kernel, remote, names, list(near), list(carried)),
        in_specs=[pl.BlockSpec(memory_space=pltpu.SMEM if n in scalars else pl.ANY) for n in arrays],
        out_specs=[pl.BlockSpec(memory_space=pl.ANY)] * len(results),
        out_shape=[jax.ShapeDtypeStruct(*item) for item in results.values()],
        scratch_shapes=list(scratch.values()),
        compiler_params=pltpu.CompilerParams(
            vmem_limit_bytes=VMEM_BYTES, **(dict(collective_id=collective, has_side_effects=True) if remote else {})
        ),
        name=name,
    )(*arrays.values())
    return dict(zip(results, values))


def layer(remote, arrays):
    tokens = arrays["hidden"].shape[0]
    slots = tokens // SLOT
    part, total, rows = (2, 3, D, HALF_D), (3, D, HALF_D), (SMALL_ROWS, 128)
    v, sem = pltpu.VMEM, pltpu.SemaphoreType.DMA
    of_tokens = (tokens, D)
    table = (slots, HALF, 128)
    far_pairs = {n + "_far": ((slots, K, PAIRS), bf16) for n in ("gauss", "second", "slope")}
    pair_banks = {n: v((2, K, PAIRS), bf16) for n in ("gauss", "second", "slope")} | {"pair_sems": sem((2, 3))}
    carried = {
        "argument": (table, f32), "distance": (table, f32), "hop_rows": (table, f32), "edge_rows": (table, f32),
        "atom_rows": ((slots, 8, 128), f32), "wqkv": (part, bf16), "normed_a": (of_tokens, bf16),
        "joined": ((tokens, 3 * D), bf16), "prob": ((slots, SLOT, H * SLOT), bf16), "d_resid": (of_tokens, f32),
        "d_attended": (of_tokens, bf16), "vectors": ((8, D), f32), "fpart": (part, bf16),
    }
    first = call_stage(
        forward_kernel, "layer_forward", remote, 0, arrays, ("lengths", "flags"), ("qkv", "up", "proj", "down"),
        far_pairs, carried | {"out_rows": (of_tokens, bf16)},
        pair_banks | {
            "wup": v((2, D, HALF_D), bf16), "wproj": v((2, HALF_D, D), bf16), "wdown": v((2, HALF_D, D), bf16),
            "load_sems": sem((4,)), "cols": v((5, K, 128), f32), "w1t": v((K, K), bf16), "base": v((H, 256), f32),
            "lhs": v((H, 256), bf16), "bias": v((slots, H * HALF, 128), f32), "work": v((3, SLOT, D), f32),
            "attended": v(of_tokens, bf16), "normed_f": v(of_tokens, bf16), "activated": v(of_tokens, bf16),
            "d_pre": v(of_tokens, bf16), "d_branch": v(of_tokens, bf16),
        } | ({"gather_sends": sem((6, 4)), "gather_recvs": sem((6, 4))} if remote else {}),
    )
    again = ("flags", "centers", "spreads", "first_weight", "second_weight", "attn_gain", "hidden")
    inputs = {n: arrays[n] for n in again} | {n: first[n + "_far"] for n in carried if remote or n != "fpart"}
    inputs |= {n: first[n] for n in far_pairs}
    scratch = pair_banks | {
        "cols": v((5, K, 128), f32), "w2": v((K, 128), bf16), "bias": v((slots, H * HALF, 128), f32),
        "work": v((3, SLOT, D), f32), "dfirst": v((K, PAIRS), bf16), "dspace": v((2 * H, PAIRS), bf16),
        "hots": v((HOT, PAIRS), bf16), "dargs": v((HALF, 128), f32), "sums": v((2, K, 128), f32),
        "acc_mixed": v((2 * K + HOT, K + 2 * H), f32), "acc_table": v((2, ATOMS, ATOMS), f32),
    }
    leaving = {"in_rows": (of_tokens, bf16)}
    outs = {}
    if remote:
        outs = {"ftotal_far": (total, bf16), "qtotal_far": (total, bf16), "stotal_far": (rows, f32)}
        scratch |= {
            "qpart": v(part, bf16), "spart": v(rows, f32), "ftotal": v(total, bf16), "qtotal": v(total, bf16),
            "stotal": v(rows, f32), "leave_sems": sem((7,)),
        }
        for name in ("f", "q"):
            keys = ("_core", "_tp", "_x", "_z", "_sends", "_recvs")
            scratch |= {name + key: item for key, item in zip(keys, big_scratch())}
        scratch |= dict(zip(("s_near", "s_z", "s_sends", "s_recvs"), small_scratch()))
    else:
        leaving |= {"qpart": (part, bf16), "spart": (rows, f32)}
    second = call_stage(
        backward_kernel, "layer_backward", remote, 1, inputs, ("flags",), tuple(far_pairs), outs, leaving, scratch
    )
    if remote:
        sums = [second[n] for n in outs]
    else:
        sums = [first["fpart_far"], second["qpart_far"], second["spart_far"]]
    return first["out_rows_far"], second["in_rows_far"], sums


def unpack_kernel(
    qsum, up_sum, proj_low, proj_high, down_low, down_high, out_rows, in_rows, rows_ref,
    output, grad_input, again, ashift, qkv, proj, fgain, fshift, up, up_bias, down, down_bias, scale, shift, centers,
    spreads, first, first_bias, second, hop, edge,
):
    output[...] = out_rows[...]
    grad_input[...] = in_rows[...]
    qkv[...] = qsum[...].astype(f32)
    up[...] = up_sum[0].astype(f32)
    for low, high, ref in ((proj_low, proj_high, proj), (down_low, down_high, down)):
        ref[:, :HALF_D] = low[0].astype(f32)
        ref[:, HALF_D:] = high[0].astype(f32)

    @pl.when(pl.program_id(0) == 0)
    def _():
        for v, ref in enumerate((again, ashift, fgain, fshift, up_bias, down_bias)):
            for i in range(D // 128):
                ref[pl.ds(128 * i, 128)] = rows_ref[VECTOR_ROWS + v * (D // 128) + i, :]
        first[...] = rows_ref[0:K, :]
        second[...] = rows_ref[SECOND_ROWS : SECOND_ROWS + H, :]
        table = rows_ref[TABLE_ROWS : TABLE_ROWS + H, :]
        scale[...] = table[:ATOMS, HOT : HOT + ATOMS]
        shift[...] = table[ATOMS:, HOT : HOT + ATOMS]
        turned = square_turn(table)
        hop[...] = turned[:HOPS, :H]
        edge[...] = turned[HOPS : HOPS + EDGES, :H]
        for i, ref in enumerate((first_bias, centers, spreads)):
            ref[...] = rows_ref[KERNEL_ROWS + i, :]


def unpack(out_rows, in_rows, fsum, qsum, rows):
    steps = 4
    tokens = out_rows.shape[0]
    shape = jax.ShapeDtypeStruct
    vec, line = shape((D,), f32), shape((K,), f32)
    mat = lambda *dims: shape(dims, f32)
    whole = lambda item: pl.BlockSpec(item.shape, lambda i: (0,) * len(item.shape))
    by_rows = lambda count, lanes: pl.BlockSpec((count // steps, lanes), lambda i: (i, 0))
    piece = lambda block, count, skip: pl.BlockSpec((1, count, HALF_D), lambda i: (block, i + skip, 0))
    token_rows = by_rows(tokens, D)
    all_q = pl.BlockSpec((3, D // steps, HALF_D), lambda i: (0, i, 0))
    half = HALF_D // steps
    small = [mat(ATOMS, ATOMS), mat(ATOMS, ATOMS), line, line, mat(K, K), line, mat(H, K), mat(HOPS, H), mat(EDGES, H)]
    return pl.pallas_call(
        unpack_kernel,
        grid=(steps,),
        in_specs=[
            all_q, piece(0, D // steps, 0), piece(1, half, 0), piece(1, half, steps), piece(2, half, 0),
            piece(2, half, steps), token_rows, token_rows, whole(rows),
        ],
        out_specs=[
            token_rows, token_rows, whole(vec), whole(vec), all_q, by_rows(HALF_D, D), whole(vec), whole(vec),
            by_rows(D, HALF_D), whole(vec), by_rows(HALF_D, D), whole(vec),
        ] + [whole(item) for item in small],
        out_shape=[
            shape((tokens, D), bf16), shape((tokens, D), bf16), vec, vec, mat(3, D, HALF_D), mat(HALF_D, D), vec, vec,
            mat(D, HALF_D), vec, mat(HALF_D, D), vec,
        ] + small,
        compiler_params=pltpu.CompilerParams(vmem_limit_bytes=VMEM_BYTES),
        name="unpack",
    )(qsum, fsum, fsum, fsum, fsum, fsum, out_rows, in_rows, rows)


def whole_weights(qkv_weight, up_weight, proj_weight, down_weight):
    columns = lambda w: jnp.stack(jnp.split(w, 2, axis=-1))
    rows = lambda w: jnp.stack(jnp.split(w, 2, axis=0))
    gather = lambda w, dim: lax.all_gather(w, "tp", axis=dim, tiled=True)
    return (
        columns(gather(qkv_weight.transpose(1, 0, 2), 2)), columns(gather(up_weight, 1)),
        rows(gather(proj_weight, 0)), rows(gather(down_weight, 0)),
    )


def sum_grads(fgrads, qgrads, small):
    total_f, total_q, rows = lax.psum((fgrads, qgrads, small), ("mol", "tp"))
    share = D // lax.axis_size("tp")
    at = lax.axis_index("tp") * share
    columns = lambda w: lax.dynamic_slice_in_dim(jnp.concatenate([w[0], w[1]], axis=-1), at, share, w.ndim - 2)
    rows_of = lambda w: lax.dynamic_slice_in_dim(
        jnp.concatenate([jnp.concatenate([w[t, :HALF_D], w[t, HALF_D:]], axis=1) for t in range(2)]), at, share, 0
    )
    wide = lambda v: v.astype(f32)
    big = (wide(columns(total_q)), wide(columns(total_f[:, 0])), wide(rows_of(total_f[:, 1])), wide(rows_of(total_f[:, 2])))
    return big, rows


def body(
    mesh_shape,
    hidden_in, positions, atom_types, hop_counts, edge_types, lengths, branches,
    attn_gain, attn_shift, qkv_weight, proj_weight, ffn_gain, ffn_shift, up_weight, up_bias, down_weight, down_bias,
    kernel_scale, kernel_shift, centers, spreads, first_weight, first_bias, second_weight, hop_table, edge_table,
    cotangent,
):
    remote = mesh_shape["tp"] == 2 and mesh_shape["mol"] == 16 and branches.shape[0] == 8
    if remote:
        weights = (qkv_weight.transpose(1, 0, 2), up_weight, proj_weight, down_weight)
    else:
        weights = whole_weights(qkv_weight, up_weight, proj_weight, down_weight)
    arrays = dict(
        lengths=lengths, flags=branches.T, positions=positions, atoms=atom_types, hops=hop_counts.T,
        edges=edge_types.T, kernel_scale=kernel_scale, kernel_shift=kernel_shift, centers=centers, spreads=spreads,
        first_weight=first_weight, first_bias=first_bias, second_weight=second_weight.T, hop_table=hop_table,
        edge_table=edge_table, attn_gain=attn_gain, attn_shift=attn_shift, ffn_gain=ffn_gain, ffn_shift=ffn_shift,
        up_bias=up_bias, down_bias=down_bias, hidden=hidden_in, cotangent=cotangent,
        qkv=weights[0], up=weights[1], proj=weights[2], down=weights[3],
    )
    output, grad_input, sums = layer(remote, arrays)
    if remote:
        fsum, qsum, rows = sums
    else:
        big, rows = sum_grads(*sums)
        fsum = jnp.zeros((3, D, HALF_D), bf16)
        qsum = fsum
    output, grad_input, *grads = unpack(output, grad_input, fsum, qsum, rows)
    if not remote:
        grads[2], grads[6], grads[3], grads[8] = big
    grads[2] = grads[2].transpose(1, 0, 2)
    grads[16] = grads[16].T
    return (output, grad_input, *grads)


def solution(mesh):
    rows = P(("mol", "tp"), None)
    all_of = P()
    in_specs = (
        rows, P(None, ("mol", "tp")), P(("mol", "tp")), rows, rows, P("mol"), rows, all_of, all_of,
        P(None, None, "tp"), P("tp", None), all_of, all_of, P(None, "tp"), all_of, P("tp", None),
    ) + (all_of,) * 10 + (rows,)
    out_specs = (
        rows, rows, all_of, all_of, P(None, None, "tp"), P("tp", None), all_of, all_of, P(None, "tp"), all_of,
        P("tp", None),
    ) + (all_of,) * 10
    step = functools.partial(body, dict(mesh.shape))
    return jax.shard_map(step, mesh=mesh, in_specs=in_specs, out_specs=out_specs, check_vma=False)
```

```python
import functools
from types import SimpleNamespace

import jax
import jax.numpy as jnp
from jax import lax
from jax.experimental import pallas as pl
from jax.experimental.pallas import tpu as pltpu
from jax.sharding import PartitionSpec as P

D = 768
H = 32
HD = 24
FF = 768
K = 128
SLOT = 64
HALF = SLOT // 2
HALF_D = D // 2
PAIRS = SLOT * SLOT
HOPS = 16
EDGES = 8
ATOMS = 16
GROUP = 4
GROUPS = H // GROUP
HOT = 32

highest = lax.Precision.HIGHEST
neg_large = -1e30
root_tau = 2.5066282746310002
root_half = 0.7071067811865476
inv_root_tau = 0.3989422804014327
head_scale = HD ** (-0.5)
VMEM_BYTES = 62 * 1024 * 1024
TILE = 512

SECOND_ROWS = K
TABLE_ROWS = SECOND_ROWS + H
KERNEL_ROWS = TABLE_ROWS + H
VECTOR_ROWS = KERNEL_ROWS + 8
SMALL_ROWS = 256

MESH = pl.DeviceIdType.MESH
f32 = jnp.float32
bf16 = jnp.bfloat16


def dot_nn(left, right, precision=None):
    return lax.dot_general(left, right, (((1,), (0,)), ((), ())), precision=precision, preferred_element_type=f32)


def dot_nt(left, right, precision=None):
    return lax.dot_general(left, right, (((1,), (1,)), ((), ())), precision=precision, preferred_element_type=f32)


def dot_tn(left, right, precision=None):
    return lax.dot_general(left, right, (((0,), (0,)), ((), ())), precision=precision, preferred_element_type=f32)


def iota(shape, dim):
    return lax.broadcasted_iota(jnp.int32, shape, dim)


def gelu_parts(values):
    size = jnp.abs(values)
    bell = jnp.exp(values * values * -0.5)
    denominator = 1.0 + (0.3275911 * root_half) * size
    t = pl.reciprocal(denominator, approx=True)
    t = t * (2.0 - denominator * t)
    series = 0.5 * 1.061405429
    for factor in (-1.453152027, 1.421413741, -0.284496736, 0.254829592):
        series = series * t + 0.5 * factor
    tail = series * t * bell
    gelu = jnp.maximum(values, 0.0) - size * tail
    outer = tail - size * (bell * inv_root_tau)
    return gelu, jnp.where(values >= 0.0, 1.0 - outer, outer)


def to_column(row):
    size = row.shape[1]
    same = iota((size, size), 0) == iota((size, size), 1)
    return jnp.sum(jnp.where(same, row, 0.0), axis=1, keepdims=True)


def half_swap(values):
    return pltpu.roll(values, 64, 1)


def low_lanes(rows):
    return iota((rows, 128), 1) < 64


def vmem(count):
    return [pl.BlockSpec(memory_space=pltpu.VMEM)] * count


def row_of(ref):
    return ref[...].reshape(1, ref.shape[0])


def place():
    mol = lax.axis_index("mol")
    return mol % 2, (mol // 2) % 2, mol // 4, lax.axis_index("tp")


def greet(peers):
    barrier = pltpu.get_barrier_semaphore()
    for peer in peers:
        pl.semaphore_signal(barrier, inc=1, device_id=peer, device_id_type=MESH)
    pl.semaphore_wait(barrier, len(peers))


def window(group):
    first = GROUP * HD * group
    start = first // 128 * 128
    width = 128 if first - start + GROUP * HD <= 128 else 256
    return start, width, first - start


def head_masks(group, kind):
    _, width, offset = window(group)
    lane = iota((1, width), 1)
    return [
        ((lane >= offset + HD * h) & (lane < offset + HD * (h + 1))).astype(f32).astype(kind) for h in range(GROUP)
    ]


def spread_heads(values, group):
    return jnp.concatenate([values * mask for mask in head_masks(group, bf16)], axis=0)


def gather_heads(values, group):
    masks = head_masks(group, f32)
    total = values[:SLOT] * masks[0]
    for h in range(1, GROUP):
        total = total + values[SLOT * h : SLOT * (h + 1)] * masks[h]
    return total


def standardize(values):
    centred = values - jnp.mean(values, axis=-1, keepdims=True)
    inv_std = lax.rsqrt(jnp.mean(centred * centred, axis=-1, keepdims=True) + 1e-05)
    return centred * inv_std, inv_std


def norm_back(d_normed, scaled, inv_std, gain):
    weighted = d_normed * gain
    inner_a = jnp.mean(weighted, axis=-1, keepdims=True)
    inner_b = jnp.mean(weighted * scaled, axis=-1, keepdims=True)
    return inv_std * (weighted - inner_a - scaled * inner_b)


def column_sum(values):
    return jnp.sum(values, axis=0, keepdims=True)


class Peers:
    def __init__(self):
        self.core, self.x, self.z, self.tp = place()
        mol = lax.axis_index("mol")
        self.over_core = {"mol": mol + 1 - 2 * self.core}
        self.over_x = {"mol": mol + 2 - 4 * self.x}
        self.over_tp = {"tp": 1 - self.tp}
        self.turn = [lax.rem(self.z + d, 4) for d in range(4)]
        self.over_z = [{"mol": self.turn[d] * 4 + self.x * 2 + self.core} for d in range(4)]

    def neighbour(self, k):
        core = self.core + (1 - 2 * self.core) * (k & 1)
        x = self.x + (1 - 2 * self.x) * (k >> 1 & 1)
        tp = self.tp + (1 - 2 * self.tp) * (k >> 2)
        return core * 4 + tp * 2 + x, {"mol": self.z * 4 + x * 2 + core, "tp": tp}

    def everyone(self):
        return [self.neighbour(k)[1] for k in range(1, 8)] + self.over_z[1:]


def span(start, size):
    return pl.ds(pl.multiple_of(start, size), size)


def add_rows(target, source, rows):
    step = 96 if rows % 96 == 0 else rows

    def piece(i, _):
        at = pl.ds(pl.multiple_of(i * step, step), step)
        target[at, :] = (target[at, :].astype(f32) + source[at, :].astype(f32)).astype(target.dtype)
        return 0

    lax.fori_loop(0, rows // step, piece, 0)


class Reduction:
    kinds = 12

    def __init__(self, peers, part, total, from_core, from_one, from_two, from_z, sends, recvs):
        self.peers, self.part, self.total = peers, part, total
        self.from_core, self.from_one, self.from_two, self.from_z = from_core, from_one, from_two, from_z
        self.sends, self.recvs = sends, recvs
        p = peers
        mol = lax.axis_index("mol")
        turn_tp, turn_x = 1 - 2 * p.tp, 1 - 2 * p.x
        self.one = {"mol": mol + p.core * 2 * turn_x, "tp": p.tp + (1 - p.core) * turn_tp}
        self.two = {"mol": mol + (1 - p.core) * 2 * turn_x, "tp": p.tp + p.core * turn_tp}
        self.at_core = p.core * 384
        self.at_x = self.at_core + p.x * 192
        self.first = ((1 - p.tp, 1 - p.x), (p.tp + (1 - p.core) * turn_tp, p.x + p.core * turn_x))
        self.second = (p.tp + p.core * turn_tp, p.x + (1 - p.core) * turn_x)
        self.kept = (p.tp, p.x)

    def quarter(self, b, where):
        return self.part.at[where[0], b, span(self.at_core + where[1] * 192, 192)]

    def copy(self, b, kind):
        p = self.peers
        total = self.total
        if kind == 0:
            src, dst, peer = self.part.at[:, b, span((1 - p.core) * 384, 384)], self.from_core.at[:, b], p.over_core
        elif kind < 3:
            src, dst, peer = self.quarter(b, self.first[kind - 1]), self.from_one.at[b, kind - 1], self.one
        elif kind == 3:
            src, dst, peer = self.quarter(b, self.second), self.from_two.at[b], self.two
        elif kind < 7:
            d = kind - 3
            src = self.part.at[p.tp, b, span(self.at_x + p.turn[d] * 48, 48)]
            dst, peer = self.from_z.at[b, d - 1], p.over_z[d]
        elif kind < 10:
            src = dst = total.at[b, span(self.at_x + p.z * 48, 48)]
            peer = p.over_z[kind - 6]
        elif kind == 10:
            src = dst = total.at[b, span(self.at_x, 192)]
            peer = p.over_x
        else:
            src = dst = total.at[b, span(self.at_core, 384)]
            peer = p.over_core
        return pltpu.make_async_remote_copy(
            src_ref=src, dst_ref=dst, send_sem=self.sends.at[b, kind], recv_sem=self.recvs.at[b, kind],
            device_id=peer, device_id_type=MESH,
        )

    def add_core(self, b, where):
        add_rows(self.quarter(b, where), self.from_core.at[where[0], b, span(where[1] * 192, 192)], 192)

    def act(self, b, stage):
        p = self.peers
        if stage == 0:
            self.copy(b, 0).start()
        elif stage == 1:
            self.copy(b, 0).wait_recv()
            for k in range(2):
                self.add_core(b, self.first[k])
                self.copy(b, 1 + k).start()
            self.add_core(b, self.second)
            self.add_core(b, self.kept)
        elif stage == 2:
            self.copy(b, 1).wait_recv()
            add_rows(self.quarter(b, self.second), self.from_one.at[b, 0], 192)
            self.copy(b, 3).start()
            self.copy(b, 2).wait_recv()
            add_rows(self.quarter(b, self.kept), self.from_one.at[b, 1], 192)
        elif stage == 3:
            self.copy(b, 3).wait_recv()
            add_rows(self.quarter(b, self.kept), self.from_two.at[b], 192)
            for kind in (4, 5, 6):
                self.copy(b, kind).start()
        elif stage == 4:
            for kind in (4, 5, 6):
                self.copy(b, kind).wait_recv()
            mine = span(self.at_x + p.z * 48, 48)
            value = self.part[p.tp, b, mine, :].astype(f32)
            for d in range(3):
                value = value + self.from_z[b, d].astype(f32)
            self.total[b, mine, :] = value.astype(bf16)
            for kind in (7, 8, 9):
                self.copy(b, kind).start()
        elif stage == 5:
            for kind in (7, 8, 9):
                self.copy(b, kind).wait_recv()
            self.copy(b, 10).start()
        elif stage == 6:
            self.copy(b, 10).wait_recv()
            self.copy(b, 11).start()
        elif stage == 7:
            self.copy(b, 11).wait_recv()
        else:
            for kind in range(self.kinds):
                self.copy(b, kind).wait_send()


class SmallReduction:
    def __init__(self, peers, part, total, from_near, from_z, sends, recvs):
        self.peers, self.part, self.total, self.from_near, self.from_z = peers, part, total, from_near, from_z
        self.sends, self.recvs = sends, recvs
        p = peers
        self.near = [p.neighbour(k) for k in range(8)]
        self.at_near = self.near[0][0] * 32

    def copy(self, kind):
        p = self.peers
        part, total = self.part, self.total
        if kind < 7:
            index, peer = self.near[kind + 1]
            src, dst = part.at[span(index * 32, 32)], self.from_near.at[kind]
        elif kind < 10:
            d = kind - 6
            src, dst, peer = part.at[span(self.at_near + p.turn[d] * 8, 8)], self.from_z.at[d - 1], p.over_z[d]
        elif kind < 13:
            src = dst = total.at[span(self.at_near + p.z * 8, 8)]
            peer = p.over_z[kind - 9]
        else:
            src = dst = total.at[span(self.at_near, 32)]
            peer = self.near[kind - 12][1]
        return pltpu.make_async_remote_copy(
            src_ref=src, dst_ref=dst, send_sem=self.sends.at[kind], recv_sem=self.recvs.at[kind],
            device_id=peer, device_id_type=MESH,
        )

    def act(self, stage):
        p = self.peers
        hops = (range(0, 7), range(7, 10), range(10, 13), range(13, 20))
        if stage == 5:
            for kind in range(20):
                self.copy(kind).wait_send()
            return
        if stage > 0:
            for kind in hops[stage - 1]:
                self.copy(kind).wait_recv()
        if stage == 1:
            mine = span(self.at_near, 32)
            value = self.part[mine, :]
            for k in range(7):
                value = value + self.from_near[k]
            self.part[mine, :] = value
        elif stage == 2:
            mine = span(self.at_near + p.z * 8, 8)
            self.total[mine, :] = self.part[mine, :] + self.from_z[0] + self.from_z[1] + self.from_z[2]
        if stage < 4:
            for kind in hops[stage]:
                self.copy(kind).start()


def big_scratch():
    return [
        pltpu.VMEM((2, 3, 384, HALF_D), bf16), pltpu.VMEM((3, 2, 192, HALF_D), bf16),
        pltpu.VMEM((3, 192, HALF_D), bf16), pltpu.VMEM((3, 3, 48, HALF_D), bf16),
        pltpu.SemaphoreType.DMA((3, Reduction.kinds)), pltpu.SemaphoreType.DMA((3, Reduction.kinds)),
    ]


def small_scratch():
    return [
        pltpu.VMEM((7, 32, 128), f32), pltpu.VMEM((3, 8, 128), f32),
        pltpu.SemaphoreType.DMA((20,)), pltpu.SemaphoreType.DMA((20,)),
    ]


class Gather:
    pieces = 6

    def __init__(self, peers, whole, sends, recvs):
        self.peers, self.whole, self.sends, self.recvs = peers, whole, sends, recvs
        mol = lax.axis_index("mol")
        self.over_tp = {"mol": mol + 1 - 2 * peers.core, "tp": 1 - peers.tp}
        self.over_x = {"mol": mol + (2 - 4 * peers.x) + 1 - 2 * peers.core}
        self.greeted = [self.over_tp, self.over_x, peers.over_core]

    def copy(self, index, kind):
        p = self.peers
        ref = self.whole(index, p.tp if kind == 0 else 1 - p.tp)
        count = ref.shape[0] // 2
        place = ref.at[span((1 - p.x if kind == 3 else p.x) * count, count), :]
        return pltpu.make_async_remote_copy(
            src_ref=place, dst_ref=place, send_sem=self.sends.at[index, kind], recv_sem=self.recvs.at[index, kind],
            device_id=(self.over_tp, self.over_x, p.over_core, p.over_core)[kind], device_id_type=MESH,
        )

    def on_core(self, core, work):
        pl.when(self.peers.core == core)(work)

    def start(self, indices):
        @functools.partial(self.on_core, 0)
        def _():
            for index in indices:
                self.copy(index, 0).start()

    def onward_x(self, index):
        @functools.partial(self.on_core, 1)
        def _():
            self.copy(index, 0).wait_recv()
            self.copy(index, 1).start()
            self.copy(index, 2).start()

    def onward_core(self, index):
        @functools.partial(self.on_core, 0)
        def _():
            self.copy(index, 1).wait_recv()
            self.copy(index, 3).start()

    def arrive(self, index):
        self.on_core(0, lambda: self.copy(index, 2).wait_recv())
        self.on_core(1, lambda: self.copy(index, 3).wait_recv())

    def finish(self):
        for core, kinds in ((0, (0, 3)), (1, (1, 2))):

            @functools.partial(self.on_core, core)
            def _(kinds=kinds):
                for index in range(self.pieces):
                    for kind in kinds:
                        self.copy(index, kind).wait_send()


def widen(values):
    return jnp.concatenate([values] * (TILE // 128), axis=1)


def strips():
    return [slice(16 * i, 16 * (i + 1)) for i in range(K // 16)]


def four_rows(ref, slot, first):
    return jnp.concatenate([ref[slot, pl.ds(first + i, 1), :] for i in range(TILE // 128)], axis=1)


def hot_rows(values, count):
    return (values == iota((count, TILE), 0).astype(f32)).astype(f32)


def fold_lanes(values):
    total = values[:, :128]
    for i in range(1, TILE // 128):
        total = total + values[:, 128 * i : 128 * (i + 1)]
    return total


def prepare_columns(r):
    spr = to_column(row_of(r.spreads))
    r.cols[0] = jnp.broadcast_to(to_column(row_of(r.centers)), (K, 128))
    r.cols[4] = jnp.broadcast_to(1.0 / spr, (K, 128))
    second = r.second_weight[...].astype(f32)
    r.w2[...] = jnp.concatenate([second, jnp.zeros((128 - H, K), f32)], axis=0).T.astype(bf16)


def prepare_pairs(r):
    spr = to_column(row_of(r.spreads))
    r.cols[0] = jnp.broadcast_to(to_column(row_of(r.centers)), (K, 128))
    r.cols[1] = jnp.broadcast_to(root_half / spr, (K, 128))
    r.cols[2] = jnp.broadcast_to(-jnp.log(root_tau * spr), (K, 128))
    r.cols[3] = jnp.broadcast_to(to_column(row_of(r.first_bias)), (K, 128))
    r.w1t[...] = r.first_weight[...].astype(f32).T.astype(bf16)
    table = jnp.concatenate([r.hop_table[...], r.edge_table[...], jnp.zeros((128 - HOPS - EDGES, H), f32)], axis=0)
    table = jnp.concatenate([table, jnp.zeros((128, 128 - H), f32)], axis=1).T[:H, :HOT]
    one = table.astype(bf16).astype(f32)
    r.base[...] = jnp.concatenate(
        [r.second_weight[...].astype(f32), one, table - one, jnp.zeros((H, 64), f32)], axis=1
    )


def pair_tables(r, slot):
    low = low_lanes(HALF)
    low_row = low_lanes(1)
    lanes = span(lax.div(slot, 2) * 128, 128)
    turn = lax.rem(slot, 2) * 64
    atoms = r.atoms[lanes].astype(f32).reshape(1, 128)
    rows = [pltpu.roll(row, turn, 1) for row in [r.positions[c : c + 1, lanes] for c in range(3)] + [atoms]]
    double = [jnp.where(low_row, row, half_swap(row)) for row in rows]
    columns = [to_column(row[:, :SLOT]) for row in rows]
    total = None
    for c in range(3):
        offset = jnp.where(low, columns[c][:HALF], columns[c][HALF:]) - double[c]
        total = offset * offset if total is None else total + offset * offset
    distance = jnp.sqrt(total)
    key_hot = (columns[3] == iota((SLOT, ATOMS), 1).astype(f32)).astype(f32)
    query_hot = (double[3] == iota((ATOMS, 128), 0).astype(f32)).astype(f32)
    picked = []
    for table in (r.kernel_scale, r.kernel_shift):
        both = dot_nn(dot_nt(key_hot, table[...], highest), query_hot, highest)
        picked.append(jnp.where(low, both[:HALF], both[HALF:]))
    r.argument[slot] = picked[0] * distance + picked[1]
    r.distance[slot] = distance
    for source, target in ((r.hops, r.hop_rows), (r.edges, r.edge_rows)):
        values = pltpu.roll(source[:, lanes].astype(f32), turn, 1)
        target[slot] = jnp.where(low, values[:HALF], half_swap(values[HALF:]))
    r.atom_rows[slot] = jnp.broadcast_to(double[3], (8, 128))


def pair_forward(r, slot):
    bank = lax.rem(slot, 2)
    graph_on = r.flags[0, slot].astype(f32)
    space_on = r.flags[1, slot].astype(f32)
    factor = jnp.where(iota((H, 256), 1) < K, space_on, graph_on)
    r.lhs[...] = (r.base[...] * factor).astype(bf16)

    def tile(t, _):
        for part in range(2):
            first_row = 8 * t + 4 * part
            where = span(t * 2 * TILE + part * TILE, TILE)
            arg = four_rows(r.argument, slot, first_row)
            pieces = []
            for rows in strips():
                u = (arg - widen(r.cols[0, rows])) * widen(r.cols[1, rows])
                pieces.append(jnp.exp(widen(r.cols[2, rows]) - u * u).astype(bf16))
                r.gauss[bank, rows, where] = pieces[-1]
            first = dot_nn(r.w1t[...], jnp.concatenate(pieces, axis=0))
            pieces = []
            for rows in strips():
                value, slope = gelu_parts(first[rows] + widen(r.cols[3, rows]))
                pieces.append(value.astype(bf16))
                r.second[bank, rows, where] = pieces[-1]
                r.slope[bank, rows, where] = slope.astype(bf16)
            hot = jnp.concatenate(
                [
                    hot_rows(four_rows(r.hop_rows, slot, first_row), HOPS),
                    hot_rows(four_rows(r.edge_rows, slot, first_row), HOT - HOPS),
                ],
                axis=0,
            ).astype(bf16)
            bias = dot_nn(r.lhs[:, : K + 2 * HOT], jnp.concatenate(pieces + [hot] * 2, axis=0))
            bias = bias.astype(bf16).astype(f32)
            for i in range(TILE // 128):
                r.bias[slot, pl.ds(first_row + i, H, stride=HALF), :] = bias[:, 128 * i : 128 * (i + 1)]
        return 0

    lax.fori_loop(0, PAIRS // (2 * TILE), tile, 0)


def pair_backward(r, slot, between):
    bank = lax.rem(slot, 2)
    graph_on = r.flags[0, slot].astype(f32)
    space_on = r.flags[1, slot].astype(f32)
    w2 = r.w2[:, :H] * space_on.astype(bf16)

    def tile(t, _):
        for part in range(2):
            first_row = 8 * t + 4 * part
            where = span(t * 2 * TILE + part * TILE, TILE)
            arg = four_rows(r.argument, slot, first_row)
            grad = jnp.concatenate(
                [r.bias[slot, pl.ds(first_row + i, H, stride=HALF), :] for i in range(TILE // 128)], axis=1
            )
            r.dspace[:, where] = jnp.concatenate([grad * space_on, grad * graph_on], axis=0).astype(bf16)
            d_second = dot_nn(w2, grad.astype(bf16))
            pieces = []
            for rows in strips():
                pieces.append((d_second[rows] * r.slope[bank, rows, where].astype(f32)).astype(bf16))
                r.dfirst[rows, where] = pieces[-1]
            d_gauss = dot_nn(r.first_weight[...], jnp.concatenate(pieces, axis=0))
            d_arg = None
            for rows in strips():
                inv = widen(r.cols[4, rows])
                u = (arg - widen(r.cols[0, rows])) * inv
                q = d_gauss[rows] * r.gauss[bank, rows, where].astype(f32)
                w = q * u
                r.sums[0, rows] += fold_lanes(w)
                r.sums[1, rows] += fold_lanes(w * u - q)
                w = w * inv
                w = w[:8] + w[8:]
                d_arg = w if d_arg is None else d_arg + w
            d_arg = -jnp.sum(d_arg, axis=0, keepdims=True)
            for i in range(TILE // 128):
                r.dargs[pl.ds(first_row + i, 1), :] = d_arg[:, 128 * i : 128 * (i + 1)]
            edge_hot = hot_rows(four_rows(r.edge_rows, slot, first_row), HOT - HOPS)
            edge_hot = jnp.where(iota((HOT - HOPS, TILE), 0) == EDGES, 1.0, edge_hot)
            r.hots[:, where] = jnp.concatenate(
                [hot_rows(four_rows(r.hop_rows, slot, first_row), HOPS), edge_hot], axis=0
            ).astype(bf16)
        return 0

    lax.fori_loop(0, PAIRS // (2 * TILE), tile, 0)
    between()
    left = jnp.concatenate([r.gauss[bank], r.second[bank], r.hots[...]], axis=0)
    r.acc_mixed[...] += dot_nt(left, jnp.concatenate([r.dfirst[...], r.dspace[...]], axis=0))
    query_hot = (r.atom_rows[slot, 0:1, :] == iota((ATOMS, 128), 0).astype(f32)).astype(f32)
    for index in range(2):
        values = r.dargs[...] * r.distance[slot] if index == 0 else r.dargs[...]
        part = jnp.where(
            low_lanes(ATOMS),
            dot_nn(query_hot[:, :HALF], values, highest),
            dot_nn(query_hot[:, HALF:SLOT], values, highest),
        )
        r.acc_table[index] += dot_nt(query_hot, part, highest)


def attend(r, s, first_slot):
    low = low_lanes(HALF)
    rows = span(s * SLOT, SLOT)
    valid = iota((SLOT, GROUP * SLOT), 0) < r.lengths[first_slot + s]
    r.work[0] = jnp.zeros((SLOT, D), f32)
    for g in range(GROUPS):
        start, width, _ = window(g)
        q = r.joined[rows, start : start + width]
        k = r.joined[rows, D + start : D + start + width]
        v = r.joined[rows, 2 * D + start : 2 * D + start + width]
        scores = dot_nt(k, spread_heads(q, g)) * head_scale
        parts = []
        for pair in range(GROUP // 2):
            head = GROUP * g + 2 * pair
            one = r.bias[s, head * HALF : (head + 1) * HALF, :]
            two = r.bias[s, (head + 1) * HALF : (head + 2) * HALF, :]
            top = jnp.where(low, one, half_swap(two))
            bottom = jnp.where(low, half_swap(one), two)
            parts.append(jnp.concatenate([top, bottom], axis=0))
        scores = jnp.where(valid, scores + jnp.concatenate(parts, axis=1), neg_large)
        weights = jnp.exp(scores - jnp.max(scores, axis=0, keepdims=True))
        prob = (weights * (1.0 / jnp.sum(weights, axis=0, keepdims=True))).astype(bf16)
        r.prob[s, :, g * GROUP * SLOT : (g + 1) * GROUP * SLOT] = prob
        r.work[0, :, start : start + width] += gather_heads(dot_tn(prob, v), g)
    r.attended[rows, :] = r.work[0].astype(bf16)


def attend_back(r, s):
    low = low_lanes(HALF)
    rows = span(s * SLOT, SLOT)
    r.work[...] = jnp.zeros((3, SLOT, D), f32)
    for g in range(GROUPS):
        start, width, _ = window(g)
        lanes = slice(start, start + width)
        k = r.joined[rows, D + start : D + start + width]
        v = r.joined[rows, 2 * D + start : 2 * D + start + width]
        q_heads = spread_heads(r.joined[rows, lanes], g)
        d_heads = spread_heads(r.d_attended[rows, lanes], g)
        prob = r.prob[s, :, g * GROUP * SLOT : (g + 1) * GROUP * SLOT]
        wide = prob.astype(f32)
        d_prob = dot_nt(v, d_heads)
        inner = jnp.sum(wide * d_prob, axis=0, keepdims=True)
        d_scores = (wide * (d_prob - inner)).astype(bf16)
        r.work[0, :, lanes] += gather_heads(dot_tn(d_scores, k), g)
        r.work[1, :, lanes] += dot_nn(d_scores, q_heads)
        r.work[2, :, lanes] += dot_nn(prob, d_heads)
        d_wide = d_scores.astype(f32)
        for pair in range(GROUP // 2):
            head = GROUP * g + 2 * pair
            top = d_wide[:HALF, 128 * pair : 128 * (pair + 1)]
            bottom = d_wide[HALF:, 128 * pair : 128 * (pair + 1)]
            r.bias[s, head * HALF : (head + 1) * HALF, :] = jnp.where(low, top, half_swap(bottom))
            r.bias[s, (head + 1) * HALF : (head + 2) * HALF, :] = jnp.where(low, half_swap(top), bottom)
    r.joined[rows, 0:D] = (r.work[0] * head_scale).astype(bf16)
    r.joined[rows, D : 2 * D] = (r.work[1] * head_scale).astype(bf16)
    r.joined[rows, 2 * D : 3 * D] = r.work[2].astype(bf16)


def project(r, rows):
    scaled, _ = standardize(r.hidden[rows, :].astype(f32))
    normed = (scaled * row_of(r.attn_gain) + row_of(r.attn_shift)).astype(bf16)
    r.normed_a[rows, :] = normed
    for m in range(3):
        for t in range(2):
            at = m * D + t * HALF_D
            r.joined[rows, at : at + HALF_D] = dot_nn(normed, r.wqkv[t, m]).astype(bf16)


def feed(r, rows):
    halves = [slice(0, HALF_D), slice(HALF_D, D)]
    resid = r.hidden[rows, :].astype(f32)
    for t in range(2):
        resid = resid + dot_nn(r.attended[rows, halves[t]], r.wproj[t])
    scaled, inv_std = standardize(resid)
    normed = (scaled * row_of(r.ffn_gain) + row_of(r.ffn_shift)).astype(bf16)
    r.normed_f[rows, :] = normed
    pre = jnp.concatenate([dot_nn(normed, r.wup[t]) for t in range(2)], axis=1)
    value, slope = gelu_parts(pre + row_of(r.up_bias))
    active = value.astype(bf16)
    r.activated[rows, :] = active
    result = resid + row_of(r.down_bias)
    for t in range(2):
        result = result + dot_nn(active[:, halves[t]], r.wdown[t])
    r.out_rows[rows, :] = result.astype(bf16)
    cot = r.cotangent[rows, :]
    cot_wide = cot.astype(f32)
    d_active = jnp.concatenate([dot_nt(cot, r.wdown[t]) for t in range(2)], axis=1)
    d_hidden = (d_active * slope).astype(bf16)
    r.d_pre[rows, :] = d_hidden
    d_normed = dot_nt(d_hidden[:, halves[0]], r.wup[0]) + dot_nt(d_hidden[:, halves[1]], r.wup[1])
    d_resid = cot_wide + norm_back(d_normed, scaled, inv_std, row_of(r.ffn_gain))
    r.d_resid[rows, :] = d_resid
    branch = d_resid.astype(bf16)
    r.d_branch[rows, :] = branch
    for t in range(2):
        r.d_attended[rows, halves[t]] = dot_nt(branch, r.wproj[t]).astype(bf16)
    r.vectors[2:3, :] += column_sum(d_normed * scaled)
    r.vectors[3:4, :] += column_sum(d_normed)
    r.vectors[4:5, :] += column_sum(d_hidden.astype(f32))
    r.vectors[5:6, :] += column_sum(cot_wide)


def feed_grads(r, block):
    for t in range(2):
        half = slice(t * HALF_D, (t + 1) * HALF_D)
        if block == 0:
            r.fpart[t, 0] = dot_tn(r.normed_f[...], r.d_pre[:, half]).astype(bf16)
        else:
            left, right = (r.attended, r.d_branch) if block == 1 else (r.activated, r.cotangent)
            grad = dot_tn(left[:, half], right[...]).astype(bf16)
            r.fpart[t, block, :HALF_D, :] = grad[:, :HALF_D]
            r.fpart[t, block, HALF_D:, :] = grad[:, HALF_D:]


def finish_input(r, rows):
    d_normed = None
    for m in range(3):
        for t in range(2):
            at = m * D + t * HALF_D
            term = dot_nt(r.joined[rows, at : at + HALF_D], r.wqkv[t, m])
            d_normed = term if d_normed is None else d_normed + term
    scaled, inv_std = standardize(r.hidden[rows, :].astype(f32))
    grad = r.d_resid[rows, :] + norm_back(d_normed, scaled, inv_std, row_of(r.attn_gain))
    r.in_rows[rows, :] = grad.astype(bf16)
    r.vectors[0:1, :] += column_sum(d_normed * scaled)
    r.vectors[1:2, :] += column_sum(d_normed)


def square_turn(values):
    rows, lanes = values.shape
    if lanes < 128:
        values = jnp.concatenate([values, jnp.zeros((rows, 128 - lanes), f32)], axis=1)
    if rows < 128:
        values = jnp.concatenate([values, jnp.zeros((128 - rows, 128), f32)], axis=0)
    return values.T


def pack_small(r):
    for v in range(6):
        for i in range(D // 128):
            at = VECTOR_ROWS + v * (D // 128) + i
            r.spart[at : at + 1, :] = r.vectors[v : v + 1, 128 * i : 128 * (i + 1)]
    r.spart[0:K, :] = r.acc_mixed[0:K, :K]
    r.spart[SECOND_ROWS : SECOND_ROWS + H, :] = square_turn(r.acc_mixed[K : 2 * K, K:])[:H]
    r.spart[TABLE_ROWS : TABLE_ROWS + H, :HOT] = square_turn(r.acc_mixed[2 * K :, K:])[H : 2 * H, :HOT]
    for index in range(2):
        rows = slice(TABLE_ROWS + ATOMS * index, TABLE_ROWS + ATOMS * (index + 1))
        r.spart[rows, HOT : HOT + ATOMS] = r.acc_table[index]
    ones = 2 * K + HOPS + EDGES
    r.spart[KERNEL_ROWS : KERNEL_ROWS + 1, :] = r.acc_mixed[ones : ones + 1, :K]
    for index in range(2):
        column = jnp.sum(r.sums[index] * r.cols[4], axis=1, keepdims=True)
        same = iota((K, K), 0) == iota((K, K), 1)
        at = KERNEL_ROWS + 1 + index
        r.spart[at : at + 1, :] = jnp.sum(jnp.where(same, column, 0.0), axis=0, keepdims=True)


class Stage:
    def __init__(self, names, near_inputs, carried, refs):
        self.r = SimpleNamespace(**dict(zip(names, refs)))
        r = self.r
        self.loads = {
            name: pltpu.make_async_copy(getattr(r, "given_" + name), getattr(r, name), r.input_sems.at[i])
            for i, name in enumerate(near_inputs)
        }
        self.stores = {
            name: pltpu.make_async_copy(getattr(r, name), getattr(r, name + "_far"), r.carry_sems.at[i])
            for i, name in enumerate(carried)
        }

    def load(self, *names):
        for name in names:
            self.loads[name].start()

    def need(self, *names):
        for name in names:
            self.loads[name].wait()

    def store(self, *names):
        for name in names:
            self.stores[name].start()

    def stored(self):
        for copy in self.stores.values():
            copy.wait()


def each_chunk(r, tokens, work):
    chunk = min(256, tokens)

    def one(c, _):
        work(r, span(c * chunk, chunk))
        return 0

    lax.fori_loop(0, tokens // chunk, one, 0)


def pair_moves(r, slot, back):
    bank = lax.rem(slot, 2)
    for index, name in enumerate(("gauss", "second", "slope")):
        far, near = getattr(r, name + "_far").at[slot], getattr(r, name).at[bank]
        yield pltpu.make_async_copy(*((far, near) if back else (near, far)), r.pair_sems.at[bank, index])


def start_moves(r, slot, back):
    for copy in pair_moves(r, slot, back):
        copy.start()


def wait_moves(r, slot, back):
    for copy in pair_moves(r, slot, back):
        copy.wait()


def run(steps):
    for act, *where in steps:
        act(*where)


def at_time(index, plan):
    for k, steps in plan.items():
        pl.when(index == k)(functools.partial(run, steps))


def forward_kernel(remote, names, near_inputs, carried, *refs):
    stage = Stage(names, near_inputs, carried, refs)
    r = stage.r
    weights = ("qkv", "up", "proj", "down")
    stage.load(*[name for name in near_inputs if name not in ("hidden", "cotangent")])
    tokens = r.hidden.shape[0]
    slots = tokens // SLOT
    peers = Peers()
    whole = [r.wqkv, r.wup, r.wproj, r.wdown]
    given = [r.given_qkv, r.given_up, r.given_proj, r.given_down]
    targets = [w.at[peers.tp] for w in whole] if remote else whole
    loads = [
        pltpu.make_async_copy(src, dst, r.load_sems.at[i]) for i, (src, dst) in enumerate(zip(given, targets))
    ]
    for load in loads:
        load.start()
    stage.load("hidden", "cotangent")
    gather_plan = {}
    if remote:

        def whole_piece(index, tp):
            return whole[0].at[tp, index] if index < 3 else whole[index - 2].at[tp]

        gather = Gather(peers, whole_piece, r.gather_sends, r.gather_recvs)
        greet(gather.greeted)
        for load, indices in zip(loads, ((0, 1, 2), (3,), (4,), (5,))):
            load.wait()
            gather.start(indices)
        x, core = gather.onward_x, gather.onward_core
        gather_plan = {
            0: [(x, 0)], 1: [(x, 1), (core, 0)], 2: [(x, 2), (core, 1)], 3: [(x, 3), (core, 2)],
            4: [(x, 4), (core, 3), (x, 5)], 5: [(core, 4)], 6: [(core, 5)],
        }
    stage.need(*[name for name in near_inputs if name not in ("hidden", "cotangent")])
    prepare_pairs(r)

    def pairs(slot, _):
        pair_tables(r, slot)
        pl.when(slot >= 2)(lambda: wait_moves(r, slot - 2, False))
        pair_forward(r, slot)
        start_moves(r, slot, False)
        at_time(slot, gather_plan)
        return 0

    lax.fori_loop(0, slots, pairs, 0)
    stage.store("argument", "distance", "hop_rows", "edge_rows", "atom_rows")
    stage.need("hidden")
    if remote:
        for index in range(3):
            gather.arrive(index)
    else:
        for load in loads:
            load.wait()
    stage.store("wqkv")
    each_chunk(r, tokens, project)
    stage.store("normed_a", "joined")
    first_slot = peers.tp * slots

    def attend_one(s, _):
        attend(r, s, first_slot)
        return 0

    lax.fori_loop(0, slots, attend_one, 0)
    stage.store("prob")
    stage.need("cotangent")
    if remote:
        for index in range(3, 6):
            gather.arrive(index)
    r.vectors[...] = jnp.zeros_like(r.vectors)
    each_chunk(r, tokens, feed)
    stage.store("out_rows", "d_resid", "d_attended", "vectors")
    for block in range(3):
        feed_grads(r, block)
    stage.store("fpart")
    for slot in (slots - 2, slots - 1):
        wait_moves(r, slot, False)
    if remote:
        gather.finish()
    stage.stored()


def backward_kernel(remote, names, near_inputs, carried, *refs):
    stage = Stage(names, near_inputs, carried, refs)
    r = stage.r
    first = ["fpart"] if remote else []
    first += ["joined", "prob", "d_attended"]
    stage.load(*first)
    stage.load(*[name for name in near_inputs if name not in first])
    tokens = r.hidden.shape[0]
    slots = tokens // SLOT
    start_moves(r, 0, True)
    start_moves(r, 1, True)
    plans = [{}, {}]
    if remote:
        peers = Peers()
        ffn = Reduction(peers, r.fpart, r.ftotal, r.f_core, r.f_one, r.f_two, r.f_z, r.f_sends, r.f_recvs)
        qkv = Reduction(peers, r.qpart, r.qtotal, r.q_core, r.q_one, r.q_two, r.q_z, r.q_sends, r.q_recvs)
        small = SmallReduction(peers, r.spart, r.stotal, r.s_near, r.s_z, r.s_sends, r.s_recvs)
        f, q = ffn.act, qkv.act
        plans = [
            {
                0: [(f, 1, 1), (f, 2, 1)], 3: [(f, 0, 2)], 4: [(f, 0, 3)], 5: [(f, 0, 4), (f, 1, 2)],
                6: [(f, 0, 5), (f, 1, 3)], 7: [(f, 0, 6), (f, 1, 4)],
            },
            {
                0: [(f, 2, 4), (q, 0, 2)], 1: [(f, 2, 5)], 2: [(q, 0, 3), (f, 2, 6)], 3: [(q, 1, 2)],
                4: [(q, 0, 4), (q, 1, 3)], 5: [(q, 0, 5)], 6: [(q, 2, 2), (q, 1, 4), (q, 0, 6)],
                7: [(q, 2, 3), (q, 1, 5)], 8: [(q, 2, 4), (q, 1, 6)], 9: [(q, 2, 5)], 10: [(q, 2, 6)],
            },
        ]
        greet(peers.everyone())
        stage.need("fpart")
        run([(f, 0, 0), (f, 1, 0), (f, 2, 0)])
    stage.need(*[name for name in near_inputs if name != "fpart"])
    if remote:
        run([(f, 0, 1)])

    def back_one(s, _):
        attend_back(r, s)
        at_time(s, plans[0])
        return 0

    lax.fori_loop(0, slots, back_one, 0)
    for m in range(3):
        for t in range(2):
            at = m * D + t * HALF_D
            r.qpart[t, m] = dot_tn(r.normed_a[...], r.joined[:, at : at + HALF_D]).astype(bf16)
        if remote:
            q(m, 0)
    if remote:
        run([(q, 0, 1), (f, 2, 2), (f, 1, 5)])
    each_chunk(r, tokens, finish_input)
    stage.store("in_rows")
    if remote:
        run([(q, 1, 1), (q, 2, 1), (f, 2, 3), (f, 1, 6)])
    for ref in (r.sums, r.acc_mixed, r.acc_table, r.spart):
        ref[...] = jnp.zeros_like(ref)
    prepare_columns(r)

    def pairs_back(slot, _):
        wait_moves(r, slot, True)
        pair_backward(r, slot, lambda: at_time(2 * slot, plans[1]))
        pl.when(slot + 2 < slots)(lambda: start_moves(r, slot + 2, True))
        at_time(2 * slot + 1, plans[1])
        return 0

    lax.fori_loop(0, slots, pairs_back, 0)
    pack_small(r)
    if remote:
        leave = [
            pltpu.make_async_copy(near.at[b], far.at[b], r.leave_sems.at[3 * i + b])
            for i, (near, far) in enumerate(((r.ftotal, r.ftotal_far), (r.qtotal, r.qtotal_far)))
            for b in range(3)
        ]
        small.act(0)
        for b in range(3):
            f(b, 7)
            leave[b].start()
        small.act(1)
        for b in range(3):
            q(b, 7)
            leave[3 + b].start()
        for step in (2, 3, 4):
            small.act(step)
        leave.append(pltpu.make_async_copy(r.stotal, r.stotal_far, r.leave_sems.at[6]))
        leave[6].start()
        for b in range(3):
            f(b, 8)
            q(b, 8)
        small.act(5)
        for copy in leave:
            copy.wait()
    else:
        stage.store("qpart", "spart")
    stage.stored()


def call_stage(kernel, name, remote, collective, arrays, scalars, far, outs, carried, scratch):
    vm, sem = pltpu.VMEM, pltpu.SemaphoreType.DMA
    near = {n: vm(a.shape, a.dtype) for n, a in arrays.items() if n not in scalars + far}
    in_names = [n if n in scalars or n.endswith("_far") else "given_" + n for n in arrays]
    results = outs | {n + "_far": item for n, item in carried.items()}
    scratch = near | {n: vm(*item) for n, item in carried.items()} | scratch
    scratch |= {"input_sems": sem((len(near),)), "carry_sems": sem((len(carried),))}
    names = in_names + list(results) + list(scratch)
    values = pl.pallas_call(
        functools.partial(kernel, remote, names, list(near), list(carried)),
        in_specs=[pl.BlockSpec(memory_space=pltpu.SMEM if n in scalars else pl.ANY) for n in arrays],
        out_specs=[pl.BlockSpec(memory_space=pl.ANY)] * len(results),
        out_shape=[jax.ShapeDtypeStruct(*item) for item in results.values()],
        scratch_shapes=list(scratch.values()),
        compiler_params=pltpu.CompilerParams(
            vmem_limit_bytes=VMEM_BYTES, **(dict(collective_id=collective, has_side_effects=True) if remote else {})
        ),
        name=name,
    )(*arrays.values())
    return dict(zip(results, values))


def layer(remote, arrays):
    tokens = arrays["hidden"].shape[0]
    slots = tokens // SLOT
    part, total, rows = (2, 3, D, HALF_D), (3, D, HALF_D), (SMALL_ROWS, 128)
    v, sem = pltpu.VMEM, pltpu.SemaphoreType.DMA
    of_tokens = (tokens, D)
    table = (slots, HALF, 128)
    far_pairs = {n + "_far": ((slots, K, PAIRS), bf16) for n in ("gauss", "second", "slope")}
    pair_banks = {n: v((2, K, PAIRS), bf16) for n in ("gauss", "second", "slope")} | {"pair_sems": sem((2, 3))}
    carried = {
        "argument": (table, f32), "distance": (table, f32), "hop_rows": (table, f32), "edge_rows": (table, f32),
        "atom_rows": ((slots, 8, 128), f32), "wqkv": (part, bf16), "normed_a": (of_tokens, bf16),
        "joined": ((tokens, 3 * D), bf16), "prob": ((slots, SLOT, H * SLOT), bf16), "d_resid": (of_tokens, f32),
        "d_attended": (of_tokens, bf16), "vectors": ((8, D), f32), "fpart": (part, bf16),
    }
    first = call_stage(
        forward_kernel, "layer_forward", remote, 0, arrays, ("lengths", "flags"), ("qkv", "up", "proj", "down"),
        far_pairs, carried | {"out_rows": (of_tokens, bf16)},
        pair_banks | {
            "wup": v((2, D, HALF_D), bf16), "wproj": v((2, HALF_D, D), bf16), "wdown": v((2, HALF_D, D), bf16),
            "load_sems": sem((4,)), "cols": v((5, K, 128), f32), "w1t": v((K, K), bf16), "base": v((H, 256), f32),
            "lhs": v((H, 256), bf16), "bias": v((slots, H * HALF, 128), f32), "work": v((3, SLOT, D), f32),
            "attended": v(of_tokens, bf16), "normed_f": v(of_tokens, bf16), "activated": v(of_tokens, bf16),
            "d_pre": v(of_tokens, bf16), "d_branch": v(of_tokens, bf16),
        } | ({"gather_sends": sem((6, 4)), "gather_recvs": sem((6, 4))} if remote else {}),
    )
    again = ("flags", "centers", "spreads", "first_weight", "second_weight", "attn_gain", "hidden")
    inputs = {n: arrays[n] for n in again} | {n: first[n + "_far"] for n in carried if remote or n != "fpart"}
    inputs |= {n: first[n] for n in far_pairs}
    scratch = pair_banks | {
        "cols": v((5, K, 128), f32), "w2": v((K, 128), bf16), "bias": v((slots, H * HALF, 128), f32),
        "work": v((3, SLOT, D), f32), "dfirst": v((K, PAIRS), bf16), "dspace": v((2 * H, PAIRS), bf16),
        "hots": v((HOT, PAIRS), bf16), "dargs": v((HALF, 128), f32), "sums": v((2, K, 128), f32),
        "acc_mixed": v((2 * K + HOT, K + 2 * H), f32), "acc_table": v((2, ATOMS, ATOMS), f32),
    }
    leaving = {"in_rows": (of_tokens, bf16)}
    outs = {}
    if remote:
        outs = {"ftotal_far": (total, bf16), "qtotal_far": (total, bf16), "stotal_far": (rows, f32)}
        scratch |= {
            "qpart": v(part, bf16), "spart": v(rows, f32), "ftotal": v(total, bf16), "qtotal": v(total, bf16),
            "stotal": v(rows, f32), "leave_sems": sem((7,)),
        }
        for name in ("f", "q"):
            keys = ("_core", "_one", "_two", "_z", "_sends", "_recvs")
            scratch |= {name + key: item for key, item in zip(keys, big_scratch())}
        scratch |= dict(zip(("s_near", "s_z", "s_sends", "s_recvs"), small_scratch()))
    else:
        leaving |= {"qpart": (part, bf16), "spart": (rows, f32)}
    second = call_stage(
        backward_kernel, "layer_backward", remote, 1, inputs, ("flags",), tuple(far_pairs), outs, leaving, scratch
    )
    if remote:
        sums = [second[n] for n in outs]
    else:
        sums = [first["fpart_far"], second["qpart_far"], second["spart_far"]]
    return first["out_rows_far"], second["in_rows_far"], sums


def unpack_kernel(
    qsum, up_sum, proj_low, proj_high, down_low, down_high, out_rows, in_rows, rows_ref,
    output, grad_input, again, ashift, qkv, proj, fgain, fshift, up, up_bias, down, down_bias, scale, shift, centers,
    spreads, first, first_bias, second, hop, edge,
):
    output[...] = out_rows[...]
    grad_input[...] = in_rows[...]
    qkv[...] = qsum[...].astype(f32)
    up[...] = up_sum[0].astype(f32)
    for low, high, ref in ((proj_low, proj_high, proj), (down_low, down_high, down)):
        ref[:, :HALF_D] = low[0].astype(f32)
        ref[:, HALF_D:] = high[0].astype(f32)

    @pl.when(pl.program_id(0) == 0)
    def _():
        for v, ref in enumerate((again, ashift, fgain, fshift, up_bias, down_bias)):
            for i in range(D // 128):
                ref[pl.ds(128 * i, 128)] = rows_ref[VECTOR_ROWS + v * (D // 128) + i, :]
        first[...] = rows_ref[0:K, :]
        second[...] = rows_ref[SECOND_ROWS : SECOND_ROWS + H, :]
        table = rows_ref[TABLE_ROWS : TABLE_ROWS + H, :]
        scale[...] = table[:ATOMS, HOT : HOT + ATOMS]
        shift[...] = table[ATOMS:, HOT : HOT + ATOMS]
        turned = square_turn(table)
        hop[...] = turned[:HOPS, :H]
        edge[...] = turned[HOPS : HOPS + EDGES, :H]
        for i, ref in enumerate((first_bias, centers, spreads)):
            ref[...] = rows_ref[KERNEL_ROWS + i, :]


def unpack(out_rows, in_rows, fsum, qsum, rows):
    steps = 4
    tokens = out_rows.shape[0]
    shape = jax.ShapeDtypeStruct
    vec, line = shape((D,), f32), shape((K,), f32)
    mat = lambda *dims: shape(dims, f32)
    whole = lambda item: pl.BlockSpec(item.shape, lambda i: (0,) * len(item.shape))
    by_rows = lambda count, lanes: pl.BlockSpec((count // steps, lanes), lambda i: (i, 0))
    piece = lambda block, count, skip: pl.BlockSpec((1, count, HALF_D), lambda i: (block, i + skip, 0))
    token_rows = by_rows(tokens, D)
    all_q = pl.BlockSpec((3, D // steps, HALF_D), lambda i: (0, i, 0))
    half = HALF_D // steps
    small = [mat(ATOMS, ATOMS), mat(ATOMS, ATOMS), line, line, mat(K, K), line, mat(H, K), mat(HOPS, H), mat(EDGES, H)]
    return pl.pallas_call(
        unpack_kernel,
        grid=(steps,),
        in_specs=[
            all_q, piece(0, D // steps, 0), piece(1, half, 0), piece(1, half, steps), piece(2, half, 0),
            piece(2, half, steps), token_rows, token_rows, whole(rows),
        ],
        out_specs=[
            token_rows, token_rows, whole(vec), whole(vec), all_q, by_rows(HALF_D, D), whole(vec), whole(vec),
            by_rows(D, HALF_D), whole(vec), by_rows(HALF_D, D), whole(vec),
        ] + [whole(item) for item in small],
        out_shape=[
            shape((tokens, D), bf16), shape((tokens, D), bf16), vec, vec, mat(3, D, HALF_D), mat(HALF_D, D), vec, vec,
            mat(D, HALF_D), vec, mat(HALF_D, D), vec,
        ] + small,
        compiler_params=pltpu.CompilerParams(vmem_limit_bytes=VMEM_BYTES),
        name="unpack",
    )(qsum, fsum, fsum, fsum, fsum, fsum, out_rows, in_rows, rows)


def whole_weights(qkv_weight, up_weight, proj_weight, down_weight):
    columns = lambda w: jnp.stack(jnp.split(w, 2, axis=-1))
    rows = lambda w: jnp.stack(jnp.split(w, 2, axis=0))
    gather = lambda w, dim: lax.all_gather(w, "tp", axis=dim, tiled=True)
    return (
        columns(gather(qkv_weight.transpose(1, 0, 2), 2)), columns(gather(up_weight, 1)),
        rows(gather(proj_weight, 0)), rows(gather(down_weight, 0)),
    )


def sum_grads(fgrads, qgrads, small):
    total_f, total_q, rows = lax.psum((fgrads, qgrads, small), ("mol", "tp"))
    share = D // lax.axis_size("tp")
    at = lax.axis_index("tp") * share
    columns = lambda w: lax.dynamic_slice_in_dim(jnp.concatenate([w[0], w[1]], axis=-1), at, share, w.ndim - 2)
    rows_of = lambda w: lax.dynamic_slice_in_dim(
        jnp.concatenate([jnp.concatenate([w[t, :HALF_D], w[t, HALF_D:]], axis=1) for t in range(2)]), at, share, 0
    )
    wide = lambda v: v.astype(f32)
    big = (wide(columns(total_q)), wide(columns(total_f[:, 0])), wide(rows_of(total_f[:, 1])), wide(rows_of(total_f[:, 2])))
    return big, rows


def body(
    mesh_shape,
    hidden_in, positions, atom_types, hop_counts, edge_types, lengths, branches,
    attn_gain, attn_shift, qkv_weight, proj_weight, ffn_gain, ffn_shift, up_weight, up_bias, down_weight, down_bias,
    kernel_scale, kernel_shift, centers, spreads, first_weight, first_bias, second_weight, hop_table, edge_table,
    cotangent,
):
    remote = mesh_shape["tp"] == 2 and mesh_shape["mol"] == 16 and branches.shape[0] == 8
    if remote:
        weights = (qkv_weight.transpose(1, 0, 2), up_weight, proj_weight, down_weight)
    else:
        weights = whole_weights(qkv_weight, up_weight, proj_weight, down_weight)
    arrays = dict(
        lengths=lengths, flags=branches.T, positions=positions, atoms=atom_types, hops=hop_counts.T,
        edges=edge_types.T, kernel_scale=kernel_scale, kernel_shift=kernel_shift, centers=centers, spreads=spreads,
        first_weight=first_weight, first_bias=first_bias, second_weight=second_weight.T, hop_table=hop_table,
        edge_table=edge_table, attn_gain=attn_gain, attn_shift=attn_shift, ffn_gain=ffn_gain, ffn_shift=ffn_shift,
        up_bias=up_bias, down_bias=down_bias, hidden=hidden_in, cotangent=cotangent,
        qkv=weights[0], up=weights[1], proj=weights[2], down=weights[3],
    )
    output, grad_input, sums = layer(remote, arrays)
    if remote:
        fsum, qsum, rows = sums
    else:
        big, rows = sum_grads(*sums)
        fsum = jnp.zeros((3, D, HALF_D), bf16)
        qsum = fsum
    output, grad_input, *grads = unpack(output, grad_input, fsum, qsum, rows)
    if not remote:
        grads[2], grads[6], grads[3], grads[8] = big
    grads[2] = grads[2].transpose(1, 0, 2)
    grads[16] = grads[16].T
    return (output, grad_input, *grads)


def solution(mesh):
    rows = P(("mol", "tp"), None)
    all_of = P()
    in_specs = (
        rows, P(None, ("mol", "tp")), P(("mol", "tp")), rows, rows, P("mol"), rows, all_of, all_of,
        P(None, None, "tp"), P("tp", None), all_of, all_of, P(None, "tp"), all_of, P("tp", None),
    ) + (all_of,) * 10 + (rows,)
    out_specs = (
        rows, rows, all_of, all_of, P(None, None, "tp"), P("tp", None), all_of, all_of, P(None, "tp"), all_of,
        P("tp", None),
    ) + (all_of,) * 10
    step = functools.partial(body, dict(mesh.shape))
    return jax.shard_map(step, mesh=mesh, in_specs=in_specs, out_specs=out_specs, check_vma=False)
```

```python
import functools
from types import SimpleNamespace

import jax
import jax.numpy as jnp
from jax import lax
from jax.experimental import pallas as pl
from jax.experimental.pallas import tpu as pltpu
from jax.sharding import PartitionSpec as P

D = 768
H = 32
HD = 24
FF = 768
K = 128
SLOT = 64
HALF = SLOT // 2
HALF_D = D // 2
PAIRS = SLOT * SLOT
HOPS = 16
EDGES = 8
ATOMS = 16
GROUP = 4
GROUPS = H // GROUP
HOT = 32

highest = lax.Precision.HIGHEST
neg_large = -1e30
root_tau = 2.5066282746310002
root_half = 0.7071067811865476
inv_root_tau = 0.3989422804014327
head_scale = HD ** (-0.5)
VMEM_BYTES = 62 * 1024 * 1024
TILE = 512

SECOND_ROWS = K
TABLE_ROWS = SECOND_ROWS + H
KERNEL_ROWS = TABLE_ROWS + H
VECTOR_ROWS = KERNEL_ROWS + 8
SMALL_ROWS = 256

MESH = pl.DeviceIdType.MESH
f32 = jnp.float32
bf16 = jnp.bfloat16


def dot_nn(left, right, precision=None):
    return lax.dot_general(left, right, (((1,), (0,)), ((), ())), precision=precision, preferred_element_type=f32)


def dot_nt(left, right, precision=None):
    return lax.dot_general(left, right, (((1,), (1,)), ((), ())), precision=precision, preferred_element_type=f32)


def dot_tn(left, right, precision=None):
    return lax.dot_general(left, right, (((0,), (0,)), ((), ())), precision=precision, preferred_element_type=f32)


def iota(shape, dim):
    return lax.broadcasted_iota(jnp.int32, shape, dim)


def gelu_parts(values):
    size = jnp.abs(values)
    bell = jnp.exp(values * values * -0.5)
    denominator = 1.0 + (0.3275911 * root_half) * size
    t = pl.reciprocal(denominator, approx=True)
    series = 0.5 * 1.061405429
    for factor in (-1.453152027, 1.421413741, -0.284496736, 0.254829592):
        series = series * t + 0.5 * factor
    tail = series * t * bell
    gelu = jnp.maximum(values, 0.0) - size * tail
    outer = tail - size * (bell * inv_root_tau)
    return gelu, jnp.where(values >= 0.0, 1.0 - outer, outer)


def to_column(row):
    size = row.shape[1]
    same = iota((size, size), 0) == iota((size, size), 1)
    return jnp.sum(jnp.where(same, row, 0.0), axis=1, keepdims=True)


def half_swap(values):
    return pltpu.roll(values, 64, 1)


def low_lanes(rows):
    return iota((rows, 128), 1) < 64


def vmem(count):
    return [pl.BlockSpec(memory_space=pltpu.VMEM)] * count


def row_of(ref):
    return ref[...].reshape(1, ref.shape[0])


def place():
    mol = lax.axis_index("mol")
    return mol % 2, (mol // 2) % 2, mol // 4, lax.axis_index("tp")


def greet(peers):
    barrier = pltpu.get_barrier_semaphore()
    for peer in peers:
        pl.semaphore_signal(barrier, inc=1, device_id=peer, device_id_type=MESH)
    pl.semaphore_wait(barrier, len(peers))


def window(group):
    first = GROUP * HD * group
    start = first // 128 * 128
    width = 128 if first - start + GROUP * HD <= 128 else 256
    return start, width, first - start


def head_masks(group, kind):
    _, width, offset = window(group)
    lane = iota((1, width), 1)
    return [
        ((lane >= offset + HD * h) & (lane < offset + HD * (h + 1))).astype(f32).astype(kind) for h in range(GROUP)
    ]


def spread_heads(values, group):
    return jnp.concatenate([values * mask for mask in head_masks(group, bf16)], axis=0)


def gather_heads(values, group):
    masks = head_masks(group, f32)
    total = values[:SLOT] * masks[0]
    for h in range(1, GROUP):
        total = total + values[SLOT * h : SLOT * (h + 1)] * masks[h]
    return total


def standardize(values):
    centred = values - jnp.mean(values, axis=-1, keepdims=True)
    inv_std = lax.rsqrt(jnp.mean(centred * centred, axis=-1, keepdims=True) + 1e-05)
    return centred * inv_std, inv_std


def norm_back(d_normed, scaled, inv_std, gain):
    weighted = d_normed * gain
    inner_a = jnp.mean(weighted, axis=-1, keepdims=True)
    inner_b = jnp.mean(weighted * scaled, axis=-1, keepdims=True)
    return inv_std * (weighted - inner_a - scaled * inner_b)


def column_sum(values):
    return jnp.sum(values, axis=0, keepdims=True)


class Peers:
    def __init__(self):
        self.core, self.x, self.z, self.tp = place()
        mol = lax.axis_index("mol")
        self.over_core = {"mol": mol + 1 - 2 * self.core}
        self.over_x = {"mol": mol + 2 - 4 * self.x}
        self.over_tp = {"tp": 1 - self.tp}
        self.turn = [lax.rem(self.z + d, 4) for d in range(4)]
        self.over_z = [{"mol": self.turn[d] * 4 + self.x * 2 + self.core} for d in range(4)]

    def neighbour(self, k):
        core = self.core + (1 - 2 * self.core) * (k & 1)
        x = self.x + (1 - 2 * self.x) * (k >> 1 & 1)
        tp = self.tp + (1 - 2 * self.tp) * (k >> 2)
        return core * 4 + tp * 2 + x, {"mol": self.z * 4 + x * 2 + core, "tp": tp}

    def everyone(self):
        return [self.neighbour(k)[1] for k in range(1, 8)] + self.over_z[1:]


def span(start, size):
    return pl.ds(pl.multiple_of(start, size), size)


def add_rows(target, source, rows):
    step = 96 if rows % 96 == 0 else rows

    def piece(i, _):
        at = pl.ds(pl.multiple_of(i * step, step), step)
        target[at, :] = (target[at, :].astype(f32) + source[at, :].astype(f32)).astype(target.dtype)
        return 0

    lax.fori_loop(0, rows // step, piece, 0)


class Reduction:
    def __init__(self, peers, part, total, from_core, from_tp, from_x, from_z, sends, recvs):
        self.peers, self.part, self.total = peers, part, total
        self.from_core, self.from_tp, self.from_x, self.from_z = from_core, from_tp, from_x, from_z
        self.sends, self.recvs = sends, recvs
        p = peers
        self.at_core = p.core * 384
        self.at_x = self.at_core + p.x * 192

    def copy(self, b, kind):
        p = self.peers
        part, total = self.part, self.total
        if kind == 0:
            src, dst, peer = part.at[:, b, span((1 - p.core) * 384, 384)], self.from_core.at[:, b], p.over_core
        elif kind == 1:
            src, dst, peer = part.at[1 - p.tp, b, span(self.at_core, 384)], self.from_tp.at[b], p.over_tp
        elif kind == 2:
            src, dst, peer = part.at[p.tp, b, span(self.at_core + (1 - p.x) * 192, 192)], self.from_x.at[b], p.over_x
        elif kind < 6:
            d = kind - 2
            src, dst, peer = part.at[p.tp, b, span(self.at_x + p.turn[d] * 48, 48)], self.from_z.at[b, d - 1], p.over_z[d]
        elif kind < 9:
            src = dst = total.at[b, span(self.at_x + p.z * 48, 48)]
            peer = p.over_z[kind - 5]
        elif kind == 9:
            src = dst = total.at[b, span(self.at_x, 192)]
            peer = p.over_x
        else:
            src = dst = total.at[b, span(self.at_core, 384)]
            peer = p.over_core
        return pltpu.make_async_remote_copy(
            src_ref=src, dst_ref=dst, send_sem=self.sends.at[b, kind], recv_sem=self.recvs.at[b, kind],
            device_id=peer, device_id_type=MESH,
        )

    def act(self, b, stage):
        p = self.peers
        if stage == 0:
            self.copy(b, 0).start()
        elif stage == 1:
            self.copy(b, 0).wait_recv()
            add_rows(self.part.at[1 - p.tp, b, span(self.at_core, 384)], self.from_core.at[1 - p.tp, b], 384)
            self.copy(b, 1).start()
            add_rows(self.part.at[p.tp, b, span(self.at_core, 384)], self.from_core.at[p.tp, b], 384)
        elif stage == 2:
            self.copy(b, 1).wait_recv()
            away, mine = (1 - p.x) * 192, p.x * 192
            add_rows(self.part.at[p.tp, b, span(self.at_core + away, 192)], self.from_tp.at[b, span(away, 192)], 192)
            self.copy(b, 2).start()
            add_rows(self.part.at[p.tp, b, span(self.at_core + mine, 192)], self.from_tp.at[b, span(mine, 192)], 192)
        elif stage == 3:
            self.copy(b, 2).wait_recv()
            add_rows(self.part.at[p.tp, b, span(self.at_x, 192)], self.from_x.at[b], 192)
            for kind in (3, 4, 5):
                self.copy(b, kind).start()
        elif stage == 4:
            for kind in (3, 4, 5):
                self.copy(b, kind).wait_recv()
            mine = span(self.at_x + p.z * 48, 48)
            value = self.part[p.tp, b, mine, :].astype(f32)
            for d in range(3):
                value = value + self.from_z[b, d].astype(f32)
            self.total[b, mine, :] = value.astype(bf16)
            for kind in (6, 7, 8):
                self.copy(b, kind).start()
        elif stage == 5:
            for kind in (6, 7, 8):
                self.copy(b, kind).wait_recv()
            self.copy(b, 9).start()
        elif stage == 6:
            self.copy(b, 9).wait_recv()
            self.copy(b, 10).start()
        elif stage == 7:
            self.copy(b, 10).wait_recv()
        else:
            for kind in range(11):
                self.copy(b, kind).wait_send()


class SmallReduction:
    def __init__(self, peers, part, total, from_near, from_z, sends, recvs):
        self.peers, self.part, self.total, self.from_near, self.from_z = peers, part, total, from_near, from_z
        self.sends, self.recvs = sends, recvs
        p = peers
        self.near = [p.neighbour(k) for k in range(8)]
        self.at_near = self.near[0][0] * 32

    def copy(self, kind):
        p = self.peers
        part, total = self.part, self.total
        if kind < 7:
            index, peer = self.near[kind + 1]
            src, dst = part.at[span(index * 32, 32)], self.from_near.at[kind]
        elif kind < 10:
            d = kind - 6
            src, dst, peer = part.at[span(self.at_near + p.turn[d] * 8, 8)], self.from_z.at[d - 1], p.over_z[d]
        elif kind < 13:
            src = dst = total.at[span(self.at_near + p.z * 8, 8)]
            peer = p.over_z[kind - 9]
        else:
            src = dst = total.at[span(self.at_near, 32)]
            peer = self.near[kind - 12][1]
        return pltpu.make_async_remote_copy(
            src_ref=src, dst_ref=dst, send_sem=self.sends.at[kind], recv_sem=self.recvs.at[kind],
            device_id=peer, device_id_type=MESH,
        )

    def act(self, stage):
        p = self.peers
        hops = (range(0, 7), range(7, 10), range(10, 13), range(13, 20))
        if stage == 5:
            for kind in range(20):
                self.copy(kind).wait_send()
            return
        if stage > 0:
            for kind in hops[stage - 1]:
                self.copy(kind).wait_recv()
        if stage == 1:
            mine = span(self.at_near, 32)
            value = self.part[mine, :]
            for k in range(7):
                value = value + self.from_near[k]
            self.part[mine, :] = value
        elif stage == 2:
            mine = span(self.at_near + p.z * 8, 8)
            self.total[mine, :] = self.part[mine, :] + self.from_z[0] + self.from_z[1] + self.from_z[2]
        if stage < 4:
            for kind in hops[stage]:
                self.copy(kind).start()


def big_scratch():
    return [
        pltpu.VMEM((2, 3, 384, HALF_D), bf16), pltpu.VMEM((3, 384, HALF_D), bf16), pltpu.VMEM((3, 192, HALF_D), bf16),
        pltpu.VMEM((3, 3, 48, HALF_D), bf16), pltpu.SemaphoreType.DMA((3, 11)), pltpu.SemaphoreType.DMA((3, 11)),
    ]


def small_scratch():
    return [
        pltpu.VMEM((7, 32, 128), f32), pltpu.VMEM((3, 8, 128), f32),
        pltpu.SemaphoreType.DMA((20,)), pltpu.SemaphoreType.DMA((20,)),
    ]


class Gather:
    pieces = 6

    def __init__(self, peers, whole, sends, recvs):
        self.peers, self.whole, self.sends, self.recvs = peers, whole, sends, recvs
        self.quarter = peers.x * 2 + peers.core
        self.next_quarter = (1 - peers.x) * 2 + peers.core

    def rows(self, ref, quarter):
        count = ref.shape[0] // 4
        return ref.at[span(quarter * count, count), :]

    def copy(self, index, kind):
        p = self.peers
        if kind == 0:
            src = dst = self.rows(self.whole(index, p.tp), self.quarter)
            peer = p.over_tp
        elif kind == 1:
            src = dst = self.rows(self.whole(index, 1 - p.tp), self.quarter)
            peer = p.over_x
        else:
            src = dst = self.rows(self.whole(index, 1 - p.tp), self.quarter if kind == 2 else self.next_quarter)
            peer = p.over_core
        return pltpu.make_async_remote_copy(
            src_ref=src, dst_ref=dst, send_sem=self.sends.at[index, kind], recv_sem=self.recvs.at[index, kind],
            device_id=peer, device_id_type=MESH,
        )

    def start(self, indices):
        for index in indices:
            self.copy(index, 0).start()

    def onward_x(self, index):
        self.copy(index, 0).wait_recv()
        self.copy(index, 1).start()
        self.copy(index, 2).start()

    def onward_core(self, index):
        self.copy(index, 1).wait_recv()
        self.copy(index, 3).start()

    def arrive(self, index):
        self.copy(index, 2).wait_recv()
        self.copy(index, 3).wait_recv()

    def finish(self):
        for index in range(self.pieces):
            for kind in range(4):
                self.copy(index, kind).wait_send()


def square_turn(values):
    rows, lanes = values.shape
    if lanes < 128:
        values = jnp.concatenate([values, jnp.zeros((rows, 128 - lanes), f32)], axis=1)
    if rows < 128:
        values = jnp.concatenate([values, jnp.zeros((128 - rows, 128), f32)], axis=0)
    return values.T


def widen(values):
    return jnp.concatenate([values] * (TILE // 128), axis=1)


def strips():
    return [slice(16 * i, 16 * (i + 1)) for i in range(K // 16)]


def four_rows(ref, slot, first):
    return jnp.concatenate([ref[slot, pl.ds(first + i, 1), :] for i in range(TILE // 128)], axis=1)


def hot_rows(values, count):
    return (values == iota((count, TILE), 0).astype(f32)).astype(f32)


def fold_lanes(values):
    total = values[:, :128]
    for i in range(1, TILE // 128):
        total = total + values[:, 128 * i : 128 * (i + 1)]
    return total


def prepare_columns(r):
    spr = to_column(row_of(r.spreads))
    r.cols[0] = jnp.broadcast_to(to_column(row_of(r.centers)), (K, 128))
    r.cols[4] = jnp.broadcast_to(1.0 / spr, (K, 128))
    second = r.second_weight[...].astype(f32)
    r.w2[...] = jnp.concatenate([second, jnp.zeros((128 - H, K), f32)], axis=0).T.astype(bf16)


def prepare_pairs(r):
    spr = to_column(row_of(r.spreads))
    r.cols[0] = jnp.broadcast_to(to_column(row_of(r.centers)), (K, 128))
    r.cols[1] = jnp.broadcast_to(root_half / spr, (K, 128))
    r.cols[2] = jnp.broadcast_to(-jnp.log(root_tau * spr), (K, 128))
    r.cols[3] = jnp.broadcast_to(to_column(row_of(r.first_bias)), (K, 128))
    r.w1t[...] = r.first_weight[...].astype(f32).T.astype(bf16)
    table = jnp.concatenate([r.hop_table[...], r.edge_table[...], jnp.zeros((128 - HOPS - EDGES, H), f32)], axis=0)
    table = jnp.concatenate([table, jnp.zeros((128, 128 - H), f32)], axis=1).T[:H, :HOT]
    one = table.astype(bf16).astype(f32)
    r.base[...] = jnp.concatenate(
        [r.second_weight[...].astype(f32), one, table - one, jnp.zeros((H, 64), f32)], axis=1
    )


def bf16_parts(values, count):
    parts = []
    for _ in range(count):
        parts.append(values.astype(bf16))
        values = values - parts[-1].astype(f32)
    return parts


def pair_tables(r, slots):
    low = low_lanes(HALF)
    low_row = low_lanes(1)
    tables = [part.astype(f32) for ref in (r.kernel_scale, r.kernel_shift) for part in bf16_parts(ref[...], 3)]
    tables = jnp.concatenate([square_turn(part)[:ATOMS, :ATOMS] for part in tables], axis=1)
    tables = jnp.concatenate([tables, jnp.zeros((ATOMS, 128 - 6 * ATOMS), f32)], axis=1).astype(bf16)
    for group in range(slots // 2):
        lanes = slice(128 * group, 128 * (group + 1))
        atoms = r.atoms[lanes].astype(f32).reshape(1, 128)
        rows = jnp.concatenate([r.positions[:, lanes], atoms, jnp.zeros((4, 128), f32)], axis=0)
        columns = square_turn(rows)
        key_hot = (columns[:, 3:4] == iota((128, ATOMS), 1).astype(f32)).astype(f32).astype(bf16)
        picks = dot_nn(key_hot, tables).astype(bf16)
        turned = half_swap(rows)
        for s in range(2):
            slot = 2 * group + s
            tokens = slice(SLOT * s, SLOT * (s + 1))
            double = jnp.where(low_lanes(8), *((rows, turned) if s == 0 else (turned, rows)))
            total = None
            for c in range(3):
                column = columns[tokens, c : c + 1]
                offset = jnp.where(low, column[:HALF], column[HALF:]) - double[c : c + 1]
                total = offset * offset if total is None else total + offset * offset
            distance = jnp.sqrt(total)
            query_hot = (double[3:4] == iota((ATOMS, 128), 0).astype(f32)).astype(f32)
            three, none = [query_hot] * 3, [jnp.zeros((3 * ATOMS, 128), f32)]
            rest = [jnp.zeros((128 - 6 * ATOMS, 128), f32)]
            spread = jnp.concatenate(
                [jnp.concatenate(three + none + rest, axis=0), jnp.concatenate(none + three + rest, axis=0)], axis=1
            )
            both = dot_nn(picks[tokens], spread.astype(bf16))
            scale = jnp.where(low, both[:HALF, :128], both[HALF:, :128])
            shift = jnp.where(low, both[:HALF, 128:], both[HALF:, 128:])
            r.argument[slot] = scale * distance + shift
            r.distance[slot] = distance
            for source, target in ((r.hops, r.hop_rows), (r.edges, r.edge_rows)):
                values = source[:, lanes].astype(f32)
                top, bottom = values[:HALF], values[HALF:]
                if s == 0:
                    target[slot] = jnp.where(low, top, half_swap(bottom))
                else:
                    target[slot] = jnp.where(low, half_swap(top), bottom)
            r.atom_rows[slot] = jnp.broadcast_to(double[3:4], (8, 128))


def table_grads(r, slots):
    lefts, rights = [], []
    for slot in range(slots):
        query_hot = (r.atom_rows[slot, 0:1, :] == iota((ATOMS, 128), 0).astype(f32)).astype(f32)
        keys = jnp.concatenate([query_hot[:, :HALF], query_hot[:, HALF:SLOT]], axis=0)
        keys = jnp.concatenate([keys, keys], axis=1).astype(bf16)
        values = jnp.concatenate([r.dargs[slot] * r.distance[slot], r.dargs[slot]], axis=1)
        both = dot_nn(keys, jnp.concatenate(bf16_parts(values, 2), axis=0))
        low = low_lanes(ATOMS)
        for index in range(2):
            lanes = slice(128 * index, 128 * (index + 1))
            rights.append(bf16_parts(jnp.where(low, both[:ATOMS, lanes], both[ATOMS:, lanes]), 2))
        lefts.append(query_hot.astype(bf16))
    left = jnp.concatenate(lefts, axis=1)
    right = jnp.concatenate(
        [jnp.concatenate([rights[2 * s + index][part] for s in range(slots)], axis=1) for index in range(2) for part in range(2)],
        axis=0,
    )
    result = dot_nt(left, right)
    return [
        result[:, 2 * ATOMS * index : 2 * ATOMS * index + ATOMS] + result[:, 2 * ATOMS * index + ATOMS : 2 * ATOMS * (index + 1)]
        for index in range(2)
    ]


def in_stages(stages, count):
    held = {}
    for time in range(count + len(stages) - 1):
        for k, stage in reversed(list(enumerate(stages))):
            if 0 <= time - k < count:
                held[time - k] = stage(time - k, held.get(time - k))


TILES = PAIRS // TILE
ROWS = TILE // 128


def pair_forward(r, slot):
    bank = lax.rem(slot, 2)
    graph_on = r.flags[0, slot].astype(f32)
    space_on = r.flags[1, slot].astype(f32)
    factor = jnp.where(iota((H, 256), 1) < K, space_on, graph_on)
    r.lhs[...] = (r.base[...] * factor).astype(bf16)

    def kernels(tile, _):
        where = slice(tile * TILE, (tile + 1) * TILE)
        arg = four_rows(r.argument, slot, tile * ROWS)
        pieces = []
        for rows in strips():
            u = (arg - widen(r.cols[0, rows])) * widen(r.cols[1, rows])
            pieces.append(jnp.exp(widen(r.cols[2, rows]) - u * u).astype(bf16))
            r.gauss[bank, rows, where] = pieces[-1]
        return dot_nn(r.w1t[...], jnp.concatenate(pieces, axis=0))

    def hidden(tile, first):
        where = slice(tile * TILE, (tile + 1) * TILE)
        pieces = []
        for rows in strips():
            value, slope = gelu_parts(first[rows] + widen(r.cols[3, rows]))
            pieces.append(value.astype(bf16))
            r.second[bank, rows, where] = pieces[-1]
            r.slope[bank, rows, where] = slope.astype(bf16)
        hot = jnp.concatenate(
            [
                hot_rows(four_rows(r.hop_rows, slot, tile * ROWS), HOPS),
                hot_rows(four_rows(r.edge_rows, slot, tile * ROWS), HOT - HOPS),
            ],
            axis=0,
        ).astype(bf16)
        return dot_nn(r.lhs[:, : K + 2 * HOT], jnp.concatenate(pieces + [hot] * 2, axis=0))

    def biases(tile, bias):
        bias = bias.astype(bf16).astype(f32)
        for i in range(ROWS):
            r.bias[slot, pl.ds(tile * ROWS + i, H, stride=HALF), :] = bias[:, 128 * i : 128 * (i + 1)]

    in_stages([kernels, hidden, biases], TILES)


def pair_backward(r, slot, between):
    bank = lax.rem(slot, 2)
    graph_on = r.flags[0, slot].astype(f32)
    space_on = r.flags[1, slot].astype(f32)
    w2 = r.w2[:, :H] * space_on.astype(bf16)

    def scores(tile, _):
        where = slice(tile * TILE, (tile + 1) * TILE)
        grad = jnp.concatenate(
            [r.bias[slot, pl.ds(tile * ROWS + i, H, stride=HALF), :] for i in range(ROWS)], axis=1
        )
        r.dspace[:, where] = jnp.concatenate([grad * space_on, grad * graph_on], axis=0).astype(bf16)
        edge_hot = hot_rows(four_rows(r.edge_rows, slot, tile * ROWS), HOT - HOPS)
        edge_hot = jnp.where(iota((HOT - HOPS, TILE), 0) == EDGES, 1.0, edge_hot)
        r.hots[:, where] = jnp.concatenate(
            [hot_rows(four_rows(r.hop_rows, slot, tile * ROWS), HOPS), edge_hot], axis=0
        ).astype(bf16)
        return dot_nn(w2, grad.astype(bf16))

    def hidden(tile, d_second):
        where = slice(tile * TILE, (tile + 1) * TILE)
        pieces = []
        for rows in strips():
            pieces.append((d_second[rows] * r.slope[bank, rows, where].astype(f32)).astype(bf16))
            r.dfirst[rows, where] = pieces[-1]
        return dot_nn(r.first_weight[...], jnp.concatenate(pieces, axis=0))

    def kernels(tile, d_gauss):
        where = slice(tile * TILE, (tile + 1) * TILE)
        arg = four_rows(r.argument, slot, tile * ROWS)
        d_arg = None
        for rows in strips():
            inv = widen(r.cols[4, rows])
            u = (arg - widen(r.cols[0, rows])) * inv
            q = d_gauss[rows] * r.gauss[bank, rows, where].astype(f32)
            w = q * u
            r.sums[0, rows] += fold_lanes(w)
            r.sums[1, rows] += fold_lanes(w * u - q)
            w = w * inv
            w = w[:8] + w[8:]
            d_arg = w if d_arg is None else d_arg + w
        d_arg = -jnp.sum(d_arg, axis=0, keepdims=True)
        for i in range(ROWS):
            at = tile * ROWS + i
            r.dargs[slot, at : at + 1, :] = d_arg[:, 128 * i : 128 * (i + 1)]

    in_stages([scores, hidden, kernels], TILES)
    between()
    left = jnp.concatenate([r.gauss[bank], r.second[bank], r.hots[...]], axis=0)
    r.acc_mixed[...] += dot_nt(left, jnp.concatenate([r.dfirst[...], r.dspace[...]], axis=0))


def attend(r, s, first_slot):
    low = low_lanes(HALF)
    rows = span(s * SLOT, SLOT)
    valid = iota((SLOT, GROUP * SLOT), 0) < r.lengths[first_slot + s]
    r.work[0] = jnp.zeros((SLOT, D), f32)
    for g in range(GROUPS):
        start, width, _ = window(g)
        q = r.joined[rows, start : start + width]
        k = r.joined[rows, D + start : D + start + width]
        v = r.joined[rows, 2 * D + start : 2 * D + start + width]
        scores = dot_nt(k, spread_heads(q, g)) * head_scale
        parts = []
        for pair in range(GROUP // 2):
            head = GROUP * g + 2 * pair
            one = r.bias[s, head * HALF : (head + 1) * HALF, :]
            two = r.bias[s, (head + 1) * HALF : (head + 2) * HALF, :]
            top = jnp.where(low, one, half_swap(two))
            bottom = jnp.where(low, half_swap(one), two)
            parts.append(jnp.concatenate([top, bottom], axis=0))
        scores = jnp.where(valid, scores + jnp.concatenate(parts, axis=1), neg_large)
        weights = jnp.exp(scores - jnp.max(scores, axis=0, keepdims=True))
        prob = (weights * (1.0 / jnp.sum(weights, axis=0, keepdims=True))).astype(bf16)
        r.prob[s, :, g * GROUP * SLOT : (g + 1) * GROUP * SLOT] = prob
        r.work[0, :, start : start + width] += gather_heads(dot_tn(prob, v), g)
    r.attended[rows, :] = r.work[0].astype(bf16)


def attend_back(r, s):
    low = low_lanes(HALF)
    rows = span(s * SLOT, SLOT)
    r.work[...] = jnp.zeros((3, SLOT, D), f32)
    for g in range(GROUPS):
        start, width, _ = window(g)
        lanes = slice(start, start + width)
        k = r.joined[rows, D + start : D + start + width]
        v = r.joined[rows, 2 * D + start : 2 * D + start + width]
        q_heads = spread_heads(r.joined[rows, lanes], g)
        d_heads = spread_heads(r.d_attended[rows, lanes], g)
        prob = r.prob[s, :, g * GROUP * SLOT : (g + 1) * GROUP * SLOT]
        wide = prob.astype(f32)
        d_prob = dot_nt(v, d_heads)
        inner = jnp.sum(wide * d_prob, axis=0, keepdims=True)
        d_scores = (wide * (d_prob - inner)).astype(bf16)
        r.work[0, :, lanes] += gather_heads(dot_tn(d_scores, k), g)
        r.work[1, :, lanes] += dot_nn(d_scores, q_heads)
        r.work[2, :, lanes] += dot_nn(prob, d_heads)
        d_wide = d_scores.astype(f32)
        for pair in range(GROUP // 2):
            head = GROUP * g + 2 * pair
            top = d_wide[:HALF, 128 * pair : 128 * (pair + 1)]
            bottom = d_wide[HALF:, 128 * pair : 128 * (pair + 1)]
            r.bias[s, head * HALF : (head + 1) * HALF, :] = jnp.where(low, top, half_swap(bottom))
            r.bias[s, (head + 1) * HALF : (head + 2) * HALF, :] = jnp.where(low, half_swap(top), bottom)
    r.joined[rows, 0:D] = (r.work[0] * head_scale).astype(bf16)
    r.joined[rows, D : 2 * D] = (r.work[1] * head_scale).astype(bf16)
    r.joined[rows, 2 * D : 3 * D] = r.work[2].astype(bf16)


def project(r, rows):
    scaled, _ = standardize(r.hidden[rows, :].astype(f32))
    normed = (scaled * row_of(r.attn_gain) + row_of(r.attn_shift)).astype(bf16)
    r.normed_a[rows, :] = normed
    for m in range(3):
        for t in range(2):
            at = m * D + t * HALF_D
            r.joined[rows, at : at + HALF_D] = dot_nn(normed, r.wqkv[t, m]).astype(bf16)


def feed(r, rows):
    halves = [slice(0, HALF_D), slice(HALF_D, D)]
    resid = r.hidden[rows, :].astype(f32)
    for t in range(2):
        resid = resid + dot_nn(r.attended[rows, halves[t]], r.wproj[t])
    scaled, inv_std = standardize(resid)
    normed = (scaled * row_of(r.ffn_gain) + row_of(r.ffn_shift)).astype(bf16)
    r.normed_f[rows, :] = normed
    pre = jnp.concatenate([dot_nn(normed, r.wup[t]) for t in range(2)], axis=1)
    value, slope = gelu_parts(pre + row_of(r.up_bias))
    active = value.astype(bf16)
    r.activated[rows, :] = active
    result = resid + row_of(r.down_bias)
    for t in range(2):
        result = result + dot_nn(active[:, halves[t]], r.wdown[t])
    r.out_rows[rows, :] = result.astype(bf16)
    cot = r.cotangent[rows, :]
    cot_wide = cot.astype(f32)
    d_active = jnp.concatenate([dot_nt(cot, r.wdown[t]) for t in range(2)], axis=1)
    d_hidden = (d_active * slope).astype(bf16)
    r.d_pre[rows, :] = d_hidden
    d_normed = dot_nt(d_hidden[:, halves[0]], r.wup[0]) + dot_nt(d_hidden[:, halves[1]], r.wup[1])
    d_resid = cot_wide + norm_back(d_normed, scaled, inv_std, row_of(r.ffn_gain))
    r.d_resid[rows, :] = d_resid
    branch = d_resid.astype(bf16)
    r.d_branch[rows, :] = branch
    for t in range(2):
        r.d_attended[rows, halves[t]] = dot_nt(branch, r.wproj[t]).astype(bf16)
    r.vectors[2:3, :] += column_sum(d_normed * scaled)
    r.vectors[3:4, :] += column_sum(d_normed)
    r.vectors[4:5, :] += column_sum(d_hidden.astype(f32))
    r.vectors[5:6, :] += column_sum(cot_wide)


def feed_grads(r, block):
    for t in range(2):
        half = slice(t * HALF_D, (t + 1) * HALF_D)
        if block == 0:
            r.fpart[t, 0] = dot_tn(r.normed_f[...], r.d_pre[:, half]).astype(bf16)
        else:
            left, right = (r.attended, r.d_branch) if block == 1 else (r.activated, r.cotangent)
            grad = dot_tn(left[:, half], right[...]).astype(bf16)
            r.fpart[t, block, :HALF_D, :] = grad[:, :HALF_D]
            r.fpart[t, block, HALF_D:, :] = grad[:, HALF_D:]


def finish_input(r, rows):
    d_normed = None
    for m in range(3):
        for t in range(2):
            at = m * D + t * HALF_D
            term = dot_nt(r.joined[rows, at : at + HALF_D], r.wqkv[t, m])
            d_normed = term if d_normed is None else d_normed + term
    scaled, inv_std = standardize(r.hidden[rows, :].astype(f32))
    grad = r.d_resid[rows, :] + norm_back(d_normed, scaled, inv_std, row_of(r.attn_gain))
    r.in_rows[rows, :] = grad.astype(bf16)
    r.vectors[0:1, :] += column_sum(d_normed * scaled)
    r.vectors[1:2, :] += column_sum(d_normed)


def pack_small(r, slots):
    tables = table_grads(r, slots)
    for v in range(6):
        for i in range(D // 128):
            at = VECTOR_ROWS + v * (D // 128) + i
            r.spart[at : at + 1, :] = r.vectors[v : v + 1, 128 * i : 128 * (i + 1)]
    r.spart[0:K, :] = r.acc_mixed[0:K, :K]
    r.spart[SECOND_ROWS : SECOND_ROWS + H, :] = square_turn(r.acc_mixed[K : 2 * K, K:])[:H]
    r.spart[TABLE_ROWS : TABLE_ROWS + H, :HOT] = square_turn(r.acc_mixed[2 * K :, K:])[H : 2 * H, :HOT]
    for index in range(2):
        rows = slice(TABLE_ROWS + ATOMS * index, TABLE_ROWS + ATOMS * (index + 1))
        r.spart[rows, HOT : HOT + ATOMS] = tables[index]
    ones = 2 * K + HOPS + EDGES
    r.spart[KERNEL_ROWS : KERNEL_ROWS + 1, :] = r.acc_mixed[ones : ones + 1, :K]
    for index in range(2):
        column = jnp.sum(r.sums[index] * r.cols[4], axis=1, keepdims=True)
        same = iota((K, K), 0) == iota((K, K), 1)
        at = KERNEL_ROWS + 1 + index
        r.spart[at : at + 1, :] = jnp.sum(jnp.where(same, column, 0.0), axis=0, keepdims=True)


class Stage:
    def __init__(self, names, near_inputs, carried, refs):
        self.r = SimpleNamespace(**dict(zip(names, refs)))
        r = self.r
        self.loads = {
            name: pltpu.make_async_copy(getattr(r, "given_" + name), getattr(r, name), r.input_sems.at[i])
            for i, name in enumerate(near_inputs)
        }
        self.stores = {
            name: pltpu.make_async_copy(getattr(r, name), getattr(r, name + "_far"), r.carry_sems.at[i])
            for i, name in enumerate(carried)
        }

    def load(self, *names):
        for name in names:
            self.loads[name].start()

    def need(self, *names):
        for name in names:
            self.loads[name].wait()

    def store(self, *names):
        for name in names:
            self.stores[name].start()

    def stored(self):
        for copy in self.stores.values():
            copy.wait()


def each_chunk(r, tokens, work):
    chunk = min(256, tokens)

    def one(c, _):
        work(r, span(c * chunk, chunk))
        return 0

    lax.fori_loop(0, tokens // chunk, one, 0)


def pair_moves(r, slot, back):
    bank = lax.rem(slot, 2)
    for index, name in enumerate(("gauss", "second", "slope")):
        far, near = getattr(r, name + "_far").at[slot], getattr(r, name).at[bank]
        yield pltpu.make_async_copy(*((far, near) if back else (near, far)), r.pair_sems.at[bank, index])


def start_moves(r, slot, back):
    for copy in pair_moves(r, slot, back):
        copy.start()


def wait_moves(r, slot, back):
    for copy in pair_moves(r, slot, back):
        copy.wait()


def run(steps):
    for act, *where in steps:
        act(*where)


def at_time(index, plan):
    for k, steps in plan.items():
        pl.when(index == k)(functools.partial(run, steps))


def forward_kernel(remote, names, near_inputs, carried, *refs):
    stage = Stage(names, near_inputs, carried, refs)
    r = stage.r
    weights = ("qkv", "up", "proj", "down")
    stage.load(*[name for name in near_inputs if name not in ("hidden", "cotangent")])
    tokens = r.hidden.shape[0]
    slots = tokens // SLOT
    peers = Peers()
    whole = [r.wqkv, r.wup, r.wproj, r.wdown]
    given = [r.given_qkv, r.given_up, r.given_proj, r.given_down]
    targets = [w.at[peers.tp] for w in whole] if remote else whole
    loads = [
        pltpu.make_async_copy(src, dst, r.load_sems.at[i]) for i, (src, dst) in enumerate(zip(given, targets))
    ]
    for load in loads:
        load.start()
    stage.load("hidden", "cotangent")
    gather_plan = {}
    if remote:

        def whole_piece(index, tp):
            return whole[0].at[tp, index] if index < 3 else whole[index - 2].at[tp]

        gather = Gather(peers, whole_piece, r.gather_sends, r.gather_recvs)
        greet([peers.over_tp, peers.over_x, peers.over_core])
        for load, indices in zip(loads, ((0, 1, 2), (3,), (4,), (5,))):
            load.wait()
            gather.start(indices)
        x, core = gather.onward_x, gather.onward_core
        gather_plan = {
            0: [(x, 0)], 1: [(x, 1), (core, 0)], 2: [(x, 2), (core, 1)], 3: [(x, 3), (core, 2)],
            4: [(x, 4), (core, 3), (x, 5)], 5: [(core, 4)], 6: [(core, 5)],
        }
    stage.need(*[name for name in near_inputs if name not in ("hidden", "cotangent")])
    prepare_pairs(r)
    pair_tables(r, slots)

    def pairs(slot, _):
        pl.when(slot >= 2)(lambda: wait_moves(r, slot - 2, False))
        pair_forward(r, slot)
        start_moves(r, slot, False)
        at_time(slot, gather_plan)
        return 0

    lax.fori_loop(0, slots, pairs, 0)
    stage.store("argument", "distance", "hop_rows", "edge_rows", "atom_rows")
    stage.need("hidden")
    if remote:
        for index in range(3):
            gather.arrive(index)
    else:
        for load in loads:
            load.wait()
    stage.store("wqkv")
    each_chunk(r, tokens, project)
    stage.store("normed_a", "joined")
    first_slot = peers.tp * slots

    def attend_one(s, _):
        attend(r, s, first_slot)
        return 0

    lax.fori_loop(0, slots, attend_one, 0)
    stage.store("prob")
    stage.need("cotangent")
    if remote:
        for index in range(3, 6):
            gather.arrive(index)
    r.vectors[...] = jnp.zeros_like(r.vectors)
    each_chunk(r, tokens, feed)
    stage.store("out_rows", "d_resid", "d_attended", "vectors")
    for block in range(3):
        feed_grads(r, block)
    stage.store("fpart")
    for slot in (slots - 2, slots - 1):
        wait_moves(r, slot, False)
    if remote:
        gather.finish()
    stage.stored()


def backward_kernel(remote, names, near_inputs, carried, *refs):
    stage = Stage(names, near_inputs, carried, refs)
    r = stage.r
    first = ["fpart"] if remote else []
    first += ["joined", "prob", "d_attended"]
    stage.load(*first)
    stage.load(*[name for name in near_inputs if name not in first])
    tokens = r.hidden.shape[0]
    slots = tokens // SLOT
    start_moves(r, 0, True)
    start_moves(r, 1, True)
    plans = [{}, {}]
    if remote:
        peers = Peers()
        ffn = Reduction(peers, r.fpart, r.ftotal, r.f_core, r.f_tp, r.f_x, r.f_z, r.f_sends, r.f_recvs)
        qkv = Reduction(peers, r.qpart, r.qtotal, r.q_core, r.q_tp, r.q_x, r.q_z, r.q_sends, r.q_recvs)
        small = SmallReduction(peers, r.spart, r.stotal, r.s_near, r.s_z, r.s_sends, r.s_recvs)
        f, q = ffn.act, qkv.act
        plans = [
            {
                0: [(f, 1, 1), (f, 2, 1)], 3: [(f, 0, 2)], 4: [(f, 0, 3)], 5: [(f, 0, 4), (f, 1, 2)],
                6: [(f, 0, 5), (f, 1, 3)], 7: [(f, 0, 6), (f, 1, 4)],
            },
            {
                0: [(f, 2, 4), (q, 0, 2)], 1: [(f, 2, 5)], 2: [(q, 0, 3), (f, 2, 6)], 3: [(q, 1, 2)],
                4: [(q, 0, 4), (q, 1, 3)], 5: [(q, 0, 5)], 6: [(q, 2, 2), (q, 1, 4), (q, 0, 6)],
                7: [(q, 2, 3), (q, 1, 5)], 8: [(q, 2, 4), (q, 1, 6)], 9: [(q, 2, 5)], 10: [(q, 2, 6)],
            },
        ]
        greet(peers.everyone())
        stage.need("fpart")
        run([(f, 0, 0), (f, 1, 0), (f, 2, 0)])
    stage.need(*[name for name in near_inputs if name != "fpart"])
    if remote:
        run([(f, 0, 1)])

    def back_one(s, _):
        attend_back(r, s)
        at_time(s, plans[0])
        return 0

    lax.fori_loop(0, slots, back_one, 0)
    for m in range(3):
        for t in range(2):
            at = m * D + t * HALF_D
            r.qpart[t, m] = dot_tn(r.normed_a[...], r.joined[:, at : at + HALF_D]).astype(bf16)
        if remote:
            q(m, 0)
    if remote:
        run([(q, 0, 1), (f, 2, 2), (f, 1, 5)])
    each_chunk(r, tokens, finish_input)
    stage.store("in_rows")
    if remote:
        run([(q, 1, 1), (q, 2, 1), (f, 2, 3), (f, 1, 6)])
    for ref in (r.sums, r.acc_mixed, r.spart):
        ref[...] = jnp.zeros_like(ref)
    prepare_columns(r)

    def pairs_back(slot, _):
        wait_moves(r, slot, True)
        pair_backward(r, slot, lambda: at_time(2 * slot, plans[1]))
        pl.when(slot + 2 < slots)(lambda: start_moves(r, slot + 2, True))
        at_time(2 * slot + 1, plans[1])
        return 0

    lax.fori_loop(0, slots, pairs_back, 0)
    pack_small(r, slots)
    if remote:
        leave = [
            pltpu.make_async_copy(near.at[b], far.at[b], r.leave_sems.at[3 * i + b])
            for i, (near, far) in enumerate(((r.ftotal, r.ftotal_far), (r.qtotal, r.qtotal_far)))
            for b in range(3)
        ]
        small.act(0)
        for b in range(3):
            f(b, 7)
            leave[b].start()
        small.act(1)
        for b in range(3):
            q(b, 7)
            leave[3 + b].start()
        for step in (2, 3, 4):
            small.act(step)
        leave.append(pltpu.make_async_copy(r.stotal, r.stotal_far, r.leave_sems.at[6]))
        leave[6].start()
        for b in range(3):
            f(b, 8)
            q(b, 8)
        small.act(5)
        for copy in leave:
            copy.wait()
    else:
        stage.store("qpart", "spart")
    stage.stored()


def call_stage(kernel, name, remote, collective, arrays, scalars, far, outs, carried, scratch):
    vm, sem = pltpu.VMEM, pltpu.SemaphoreType.DMA
    near = {n: vm(a.shape, a.dtype) for n, a in arrays.items() if n not in scalars + far}
    in_names = [n if n in scalars or n.endswith("_far") else "given_" + n for n in arrays]
    results = outs | {n + "_far": item for n, item in carried.items()}
    scratch = near | {n: vm(*item) for n, item in carried.items()} | scratch
    scratch |= {"input_sems": sem((len(near),)), "carry_sems": sem((len(carried),))}
    names = in_names + list(results) + list(scratch)
    values = pl.pallas_call(
        functools.partial(kernel, remote, names, list(near), list(carried)),
        in_specs=[pl.BlockSpec(memory_space=pltpu.SMEM if n in scalars else pl.ANY) for n in arrays],
        out_specs=[pl.BlockSpec(memory_space=pl.ANY)] * len(results),
        out_shape=[jax.ShapeDtypeStruct(*item) for item in results.values()],
        scratch_shapes=list(scratch.values()),
        compiler_params=pltpu.CompilerParams(
            vmem_limit_bytes=VMEM_BYTES, **(dict(collective_id=collective, has_side_effects=True) if remote else {})
        ),
        name=name,
    )(*arrays.values())
    return dict(zip(results, values))


def layer(remote, arrays):
    tokens = arrays["hidden"].shape[0]
    slots = tokens // SLOT
    part, total, rows = (2, 3, D, HALF_D), (3, D, HALF_D), (SMALL_ROWS, 128)
    v, sem = pltpu.VMEM, pltpu.SemaphoreType.DMA
    of_tokens = (tokens, D)
    table = (slots, HALF, 128)
    far_pairs = {n + "_far": ((slots, K, PAIRS), bf16) for n in ("gauss", "second", "slope")}
    pair_banks = {n: v((2, K, PAIRS), bf16) for n in ("gauss", "second", "slope")} | {"pair_sems": sem((2, 3))}
    carried = {
        "argument": (table, f32), "distance": (table, f32), "hop_rows": (table, f32), "edge_rows": (table, f32),
        "atom_rows": ((slots, 8, 128), f32), "wqkv": (part, bf16), "normed_a": (of_tokens, bf16),
        "joined": ((tokens, 3 * D), bf16), "prob": ((slots, SLOT, H * SLOT), bf16), "d_resid": (of_tokens, f32),
        "d_attended": (of_tokens, bf16), "vectors": ((8, D), f32), "fpart": (part, bf16),
    }
    first = call_stage(
        forward_kernel, "layer_forward", remote, 0, arrays, ("lengths", "flags"), ("qkv", "up", "proj", "down"),
        far_pairs, carried | {"out_rows": (of_tokens, bf16)},
        pair_banks | {
            "wup": v((2, D, HALF_D), bf16), "wproj": v((2, HALF_D, D), bf16), "wdown": v((2, HALF_D, D), bf16),
            "load_sems": sem((4,)), "cols": v((5, K, 128), f32), "w1t": v((K, K), bf16), "base": v((H, 256), f32),
            "lhs": v((H, 256), bf16), "bias": v((slots, H * HALF, 128), f32), "work": v((3, SLOT, D), f32),
            "attended": v(of_tokens, bf16), "normed_f": v(of_tokens, bf16), "activated": v(of_tokens, bf16),
            "d_pre": v(of_tokens, bf16), "d_branch": v(of_tokens, bf16),
        } | ({"gather_sends": sem((6, 4)), "gather_recvs": sem((6, 4))} if remote else {}),
    )
    again = ("flags", "centers", "spreads", "first_weight", "second_weight", "attn_gain", "hidden")
    inputs = {n: arrays[n] for n in again} | {n: first[n + "_far"] for n in carried if remote or n != "fpart"}
    inputs |= {n: first[n] for n in far_pairs}
    scratch = pair_banks | {
        "cols": v((5, K, 128), f32), "w2": v((K, 128), bf16), "bias": v((slots, H * HALF, 128), f32),
        "work": v((3, SLOT, D), f32), "dfirst": v((K, PAIRS), bf16), "dspace": v((2 * H, PAIRS), bf16),
        "hots": v((HOT, PAIRS), bf16), "dargs": v(table, f32), "sums": v((2, K, 128), f32),
        "acc_mixed": v((2 * K + HOT, K + 2 * H), f32),
    }
    leaving = {"in_rows": (of_tokens, bf16)}
    outs = {}
    if remote:
        outs = {"ftotal_far": (total, bf16), "qtotal_far": (total, bf16), "stotal_far": (rows, f32)}
        scratch |= {
            "qpart": v(part, bf16), "spart": v(rows, f32), "ftotal": v(total, bf16), "qtotal": v(total, bf16),
            "stotal": v(rows, f32), "leave_sems": sem((7,)),
        }
        for name in ("f", "q"):
            keys = ("_core", "_tp", "_x", "_z", "_sends", "_recvs")
            scratch |= {name + key: item for key, item in zip(keys, big_scratch())}
        scratch |= dict(zip(("s_near", "s_z", "s_sends", "s_recvs"), small_scratch()))
    else:
        leaving |= {"qpart": (part, bf16), "spart": (rows, f32)}
    second = call_stage(
        backward_kernel, "layer_backward", remote, 1, inputs, ("flags",), tuple(far_pairs), outs, leaving, scratch
    )
    if remote:
        sums = [second[n] for n in outs]
    else:
        sums = [first["fpart_far"], second["qpart_far"], second["spart_far"]]
    return first["out_rows_far"], second["in_rows_far"], sums


def unpack_kernel(
    qsum, up_sum, proj_low, proj_high, down_low, down_high, out_rows, in_rows, rows_ref,
    output, grad_input, again, ashift, qkv, proj, fgain, fshift, up, up_bias, down, down_bias, scale, shift, centers,
    spreads, first, first_bias, second, hop, edge,
):
    output[...] = out_rows[...]
    grad_input[...] = in_rows[...]
    qkv[...] = qsum[...].astype(f32)
    up[...] = up_sum[0].astype(f32)
    for low, high, ref in ((proj_low, proj_high, proj), (down_low, down_high, down)):
        ref[:, :HALF_D] = low[0].astype(f32)
        ref[:, HALF_D:] = high[0].astype(f32)

    @pl.when(pl.program_id(0) == 0)
    def _():
        for v, ref in enumerate((again, ashift, fgain, fshift, up_bias, down_bias)):
            for i in range(D // 128):
                ref[pl.ds(128 * i, 128)] = rows_ref[VECTOR_ROWS + v * (D // 128) + i, :]
        first[...] = rows_ref[0:K, :]
        second[...] = rows_ref[SECOND_ROWS : SECOND_ROWS + H, :]
        table = rows_ref[TABLE_ROWS : TABLE_ROWS + H, :]
        scale[...] = table[:ATOMS, HOT : HOT + ATOMS]
        shift[...] = table[ATOMS:, HOT : HOT + ATOMS]
        turned = square_turn(table)
        hop[...] = turned[:HOPS, :H]
        edge[...] = turned[HOPS : HOPS + EDGES, :H]
        for i, ref in enumerate((first_bias, centers, spreads)):
            ref[...] = rows_ref[KERNEL_ROWS + i, :]


def unpack(out_rows, in_rows, fsum, qsum, rows):
    steps = 4
    tokens = out_rows.shape[0]
    shape = jax.ShapeDtypeStruct
    vec, line = shape((D,), f32), shape((K,), f32)
    mat = lambda *dims: shape(dims, f32)
    whole = lambda item: pl.BlockSpec(item.shape, lambda i: (0,) * len(item.shape))
    by_rows = lambda count, lanes: pl.BlockSpec((count // steps, lanes), lambda i: (i, 0))
    piece = lambda block, count, skip: pl.BlockSpec((1, count, HALF_D), lambda i: (block, i + skip, 0))
    token_rows = by_rows(tokens, D)
    all_q = pl.BlockSpec((3, D // steps, HALF_D), lambda i: (0, i, 0))
    half = HALF_D // steps
    small = [mat(ATOMS, ATOMS), mat(ATOMS, ATOMS), line, line, mat(K, K), line, mat(H, K), mat(HOPS, H), mat(EDGES, H)]
    return pl.pallas_call(
        unpack_kernel,
        grid=(steps,),
        in_specs=[
            all_q, piece(0, D // steps, 0), piece(1, half, 0), piece(1, half, steps), piece(2, half, 0),
            piece(2, half, steps), token_rows, token_rows, whole(rows),
        ],
        out_specs=[
            token_rows, token_rows, whole(vec), whole(vec), all_q, by_rows(HALF_D, D), whole(vec), whole(vec),
            by_rows(D, HALF_D), whole(vec), by_rows(HALF_D, D), whole(vec),
        ] + [whole(item) for item in small],
        out_shape=[
            shape((tokens, D), bf16), shape((tokens, D), bf16), vec, vec, mat(3, D, HALF_D), mat(HALF_D, D), vec, vec,
            mat(D, HALF_D), vec, mat(HALF_D, D), vec,
        ] + small,
        compiler_params=pltpu.CompilerParams(vmem_limit_bytes=VMEM_BYTES),
        name="unpack",
    )(qsum, fsum, fsum, fsum, fsum, fsum, out_rows, in_rows, rows)


def whole_weights(qkv_weight, up_weight, proj_weight, down_weight):
    columns = lambda w: jnp.stack(jnp.split(w, 2, axis=-1))
    rows = lambda w: jnp.stack(jnp.split(w, 2, axis=0))
    gather = lambda w, dim: lax.all_gather(w, "tp", axis=dim, tiled=True)
    return (
        columns(gather(qkv_weight.transpose(1, 0, 2), 2)), columns(gather(up_weight, 1)),
        rows(gather(proj_weight, 0)), rows(gather(down_weight, 0)),
    )


def sum_grads(fgrads, qgrads, small):
    total_f, total_q, rows = lax.psum((fgrads, qgrads, small), ("mol", "tp"))
    share = D // lax.axis_size("tp")
    at = lax.axis_index("tp") * share
    columns = lambda w: lax.dynamic_slice_in_dim(jnp.concatenate([w[0], w[1]], axis=-1), at, share, w.ndim - 2)
    rows_of = lambda w: lax.dynamic_slice_in_dim(
        jnp.concatenate([jnp.concatenate([w[t, :HALF_D], w[t, HALF_D:]], axis=1) for t in range(2)]), at, share, 0
    )
    wide = lambda v: v.astype(f32)
    big = (wide(columns(total_q)), wide(columns(total_f[:, 0])), wide(rows_of(total_f[:, 1])), wide(rows_of(total_f[:, 2])))
    return big, rows


def body(
    mesh_shape,
    hidden_in, positions, atom_types, hop_counts, edge_types, lengths, branches,
    attn_gain, attn_shift, qkv_weight, proj_weight, ffn_gain, ffn_shift, up_weight, up_bias, down_weight, down_bias,
    kernel_scale, kernel_shift, centers, spreads, first_weight, first_bias, second_weight, hop_table, edge_table,
    cotangent,
):
    remote = mesh_shape["tp"] == 2 and mesh_shape["mol"] == 16 and branches.shape[0] == 8
    if remote:
        weights = (qkv_weight.transpose(1, 0, 2), up_weight, proj_weight, down_weight)
    else:
        weights = whole_weights(qkv_weight, up_weight, proj_weight, down_weight)
    arrays = dict(
        lengths=lengths, flags=branches.T, positions=positions, atoms=atom_types, hops=hop_counts.T,
        edges=edge_types.T, kernel_scale=kernel_scale, kernel_shift=kernel_shift, centers=centers, spreads=spreads,
        first_weight=first_weight, first_bias=first_bias, second_weight=second_weight.T, hop_table=hop_table,
        edge_table=edge_table, attn_gain=attn_gain, attn_shift=attn_shift, ffn_gain=ffn_gain, ffn_shift=ffn_shift,
        up_bias=up_bias, down_bias=down_bias, hidden=hidden_in, cotangent=cotangent,
        qkv=weights[0], up=weights[1], proj=weights[2], down=weights[3],
    )
    output, grad_input, sums = layer(remote, arrays)
    if remote:
        fsum, qsum, rows = sums
    else:
        big, rows = sum_grads(*sums)
        fsum = jnp.zeros((3, D, HALF_D), bf16)
        qsum = fsum
    output, grad_input, *grads = unpack(output, grad_input, fsum, qsum, rows)
    if not remote:
        grads[2], grads[6], grads[3], grads[8] = big
    grads[2] = grads[2].transpose(1, 0, 2)
    grads[16] = grads[16].T
    return (output, grad_input, *grads)


def solution(mesh):
    rows = P(("mol", "tp"), None)
    all_of = P()
    in_specs = (
        rows, P(None, ("mol", "tp")), P(("mol", "tp")), rows, rows, P("mol"), rows, all_of, all_of,
        P(None, None, "tp"), P("tp", None), all_of, all_of, P(None, "tp"), all_of, P("tp", None),
    ) + (all_of,) * 10 + (rows,)
    out_specs = (
        rows, rows, all_of, all_of, P(None, None, "tp"), P("tp", None), all_of, all_of, P(None, "tp"), all_of,
        P("tp", None),
    ) + (all_of,) * 10
    step = functools.partial(body, dict(mesh.shape))
    return jax.shard_map(step, mesh=mesh, in_specs=in_specs, out_specs=out_specs, check_vma=False)
```

```python
import functools
from types import SimpleNamespace

import jax
import jax.numpy as jnp
from jax import lax
from jax.experimental import pallas as pl
from jax.experimental.pallas import tpu as pltpu
from jax.sharding import PartitionSpec as P

D = 768
H = 32
HD = 24
FF = 768
K = 128
SLOT = 64
HALF = SLOT // 2
HALF_D = D // 2
PAIRS = SLOT * SLOT
HOPS = 16
EDGES = 8
ATOMS = 16
GROUP = 4
GROUPS = H // GROUP
HOT = 32

highest = lax.Precision.HIGHEST
neg_large = -1e30
root_tau = 2.5066282746310002
root_half = 0.7071067811865476
inv_root_tau = 0.3989422804014327
head_scale = HD ** (-0.5)
VMEM_BYTES = 62 * 1024 * 1024
TILE = 512

SECOND_ROWS = K
TABLE_ROWS = SECOND_ROWS + H
KERNEL_ROWS = TABLE_ROWS + H
VECTOR_ROWS = KERNEL_ROWS + 8
SMALL_ROWS = 256

MESH = pl.DeviceIdType.MESH
f32 = jnp.float32
bf16 = jnp.bfloat16


def dot_nn(left, right, precision=None):
    return lax.dot_general(left, right, (((1,), (0,)), ((), ())), precision=precision, preferred_element_type=f32)


def dot_nt(left, right, precision=None):
    return lax.dot_general(left, right, (((1,), (1,)), ((), ())), precision=precision, preferred_element_type=f32)


def dot_tn(left, right, precision=None):
    return lax.dot_general(left, right, (((0,), (0,)), ((), ())), precision=precision, preferred_element_type=f32)


def iota(shape, dim):
    return lax.broadcasted_iota(jnp.int32, shape, dim)


def gelu_parts(values):
    size = jnp.abs(values)
    bell = jnp.exp(values * values * -0.5)
    denominator = 1.0 + (0.3275911 * root_half) * size
    t = pl.reciprocal(denominator, approx=True)
    series = 0.5 * 1.061405429
    for factor in (-1.453152027, 1.421413741, -0.284496736, 0.254829592):
        series = series * t + 0.5 * factor
    tail = series * t * bell
    gelu = jnp.maximum(values, 0.0) - size * tail
    outer = tail - size * (bell * inv_root_tau)
    return gelu, jnp.where(values >= 0.0, 1.0 - outer, outer)


def to_column(row):
    size = row.shape[1]
    same = iota((size, size), 0) == iota((size, size), 1)
    return jnp.sum(jnp.where(same, row, 0.0), axis=1, keepdims=True)


def half_swap(values):
    return pltpu.roll(values, 64, 1)


def low_lanes(rows):
    return iota((rows, 128), 1) < 64


def vmem(count):
    return [pl.BlockSpec(memory_space=pltpu.VMEM)] * count


def row_of(ref):
    return ref[...].reshape(1, ref.shape[0])


def place():
    mol = lax.axis_index("mol")
    return mol % 2, (mol // 2) % 2, mol // 4, lax.axis_index("tp")


def greet(peers):
    barrier = pltpu.get_barrier_semaphore()
    for peer in peers:
        pl.semaphore_signal(barrier, inc=1, device_id=peer, device_id_type=MESH)
    pl.semaphore_wait(barrier, len(peers))


def window(group):
    first = GROUP * HD * group
    start = first // 128 * 128
    width = 128 if first - start + GROUP * HD <= 128 else 256
    return start, width, first - start


def head_masks(group, kind):
    _, width, offset = window(group)
    lane = iota((1, width), 1)
    return [
        ((lane >= offset + HD * h) & (lane < offset + HD * (h + 1))).astype(f32).astype(kind) for h in range(GROUP)
    ]


def spread_heads(values, group):
    return jnp.concatenate([values * mask for mask in head_masks(group, bf16)], axis=0)


def gather_heads(values, group):
    masks = head_masks(group, f32)
    total = values[:SLOT] * masks[0]
    for h in range(1, GROUP):
        total = total + values[SLOT * h : SLOT * (h + 1)] * masks[h]
    return total


def standardize(values):
    centred = values - jnp.mean(values, axis=-1, keepdims=True)
    inv_std = lax.rsqrt(jnp.mean(centred * centred, axis=-1, keepdims=True) + 1e-05)
    return centred * inv_std, inv_std


def norm_back(d_normed, scaled, inv_std, gain):
    weighted = d_normed * gain
    inner_a = jnp.mean(weighted, axis=-1, keepdims=True)
    inner_b = jnp.mean(weighted * scaled, axis=-1, keepdims=True)
    return inv_std * (weighted - inner_a - scaled * inner_b)


def column_sum(values):
    return jnp.sum(values, axis=0, keepdims=True)


class Peers:
    def __init__(self):
        self.core, self.x, self.z, self.tp = place()
        mol = lax.axis_index("mol")
        self.over_core = {"mol": mol + 1 - 2 * self.core}
        self.over_x = {"mol": mol + 2 - 4 * self.x}
        self.over_tp = {"tp": 1 - self.tp}
        self.turn = [lax.rem(self.z + d, 4) for d in range(4)]
        self.over_z = [{"mol": self.turn[d] * 4 + self.x * 2 + self.core} for d in range(4)]

    def neighbour(self, k):
        core = self.core + (1 - 2 * self.core) * (k & 1)
        x = self.x + (1 - 2 * self.x) * (k >> 1 & 1)
        tp = self.tp + (1 - 2 * self.tp) * (k >> 2)
        return core * 4 + tp * 2 + x, {"mol": self.z * 4 + x * 2 + core, "tp": tp}

    def everyone(self):
        return [self.neighbour(k)[1] for k in range(1, 8)] + self.over_z[1:]


def span(start, size):
    return pl.ds(pl.multiple_of(start, size), size)


def add_rows(target, source, rows):
    step = 96 if rows % 96 == 0 else min(rows, 32)

    def piece(i, _):
        at = pl.ds(pl.multiple_of(i * step, step), step)
        target[at, :] = (target[at, :].astype(f32) + source[at, :].astype(f32)).astype(target.dtype)
        return 0

    lax.fori_loop(0, rows // step, piece, 0)


class Reduction:
    kinds = 11

    def __init__(self, peers, part, total, from_core, from_tp, from_x, from_z, sends, recvs):
        self.peers, self.part, self.total = peers, part, total
        self.from_core, self.from_tp, self.from_x, self.from_z = from_core, from_tp, from_x, from_z
        self.sends, self.recvs = sends, recvs
        self.half = from_core.shape[2]
        self.quarter, self.least = self.half // 2, self.half // 8

    def rows(self, b, level):
        p = self.peers
        at = b * 2 * self.half + p.core * self.half
        if level > 0:
            at = at + p.x * self.quarter
        return at + p.z * self.least if level > 1 else at

    def copy(self, b, kind):
        p = self.peers
        part, total = self.part, self.total
        half, quarter, least = self.half, self.quarter, self.least
        if kind == 0:
            src = part.at[:, span(b * 2 * half + (1 - p.core) * half, half)]
            dst, peer = self.from_core.at[b], p.over_core
        elif kind == 1:
            src, dst, peer = part.at[1 - p.tp, span(self.rows(b, 0), half)], self.from_tp.at[b], p.over_tp
        elif kind == 2:
            src = part.at[p.tp, span(self.rows(b, 0) + (1 - p.x) * quarter, quarter)]
            dst, peer = self.from_x.at[b], p.over_x
        elif kind < 6:
            d = kind - 2
            src = part.at[p.tp, span(self.rows(b, 1) + p.turn[d] * least, least)]
            dst, peer = self.from_z.at[b, d - 1], p.over_z[d]
        elif kind < 9:
            src = dst = total.at[span(self.rows(b, 2), least)]
            peer = p.over_z[kind - 5]
        elif kind == 9:
            src = dst = total.at[span(self.rows(b, 1), quarter)]
            peer = p.over_x
        else:
            src = dst = total.at[span(self.rows(b, 0), half)]
            peer = p.over_core
        return pltpu.make_async_remote_copy(
            src_ref=src, dst_ref=dst, send_sem=self.sends.at[b, kind], recv_sem=self.recvs.at[b, kind],
            device_id=peer, device_id_type=MESH,
        )

    def act(self, b, stage):
        p = self.peers
        half, quarter, least = self.half, self.quarter, self.least
        part = self.part
        if stage == 0:
            self.copy(b, 0).start()
        elif stage == 1:
            self.copy(b, 0).wait_recv()
            at = span(self.rows(b, 0), half)
            add_rows(part.at[1 - p.tp, at], self.from_core.at[b, 1 - p.tp], half)
            self.copy(b, 1).start()
            add_rows(part.at[p.tp, at], self.from_core.at[b, p.tp], half)
        elif stage == 2:
            self.copy(b, 1).wait_recv()
            away, mine = (1 - p.x) * quarter, p.x * quarter
            at = self.rows(b, 0)
            add_rows(part.at[p.tp, span(at + away, quarter)], self.from_tp.at[b, span(away, quarter)], quarter)
            self.copy(b, 2).start()
            add_rows(part.at[p.tp, span(at + mine, quarter)], self.from_tp.at[b, span(mine, quarter)], quarter)
        elif stage == 3:
            self.copy(b, 2).wait_recv()
            add_rows(part.at[p.tp, span(self.rows(b, 1), quarter)], self.from_x.at[b], quarter)
            for kind in (3, 4, 5):
                self.copy(b, kind).start()
        elif stage == 4:
            for kind in (3, 4, 5):
                self.copy(b, kind).wait_recv()
            mine = span(self.rows(b, 2), least)
            value = part[p.tp, mine, :].astype(f32)
            for d in range(3):
                value = value + self.from_z[b, d].astype(f32)
            self.total[mine, :] = value.astype(bf16)
            for kind in (6, 7, 8):
                self.copy(b, kind).start()
        elif stage == 5:
            for kind in (6, 7, 8):
                self.copy(b, kind).wait_recv()
            self.copy(b, 9).start()
        elif stage == 6:
            self.copy(b, 9).wait_recv()
            self.copy(b, 10).start()
        elif stage == 7:
            self.copy(b, 10).wait_recv()
        else:
            for kind in range(self.kinds):
                self.copy(b, kind).wait_send()


class SmallReduction:
    def __init__(self, peers, part, total, from_near, from_z, sends, recvs):
        self.peers, self.part, self.total, self.from_near, self.from_z = peers, part, total, from_near, from_z
        self.sends, self.recvs = sends, recvs
        p = peers
        self.near = [p.neighbour(k) for k in range(8)]
        self.at_near = self.near[0][0] * 32

    def copy(self, kind):
        p = self.peers
        part, total = self.part, self.total
        if kind < 7:
            index, peer = self.near[kind + 1]
            src, dst = part.at[span(index * 32, 32)], self.from_near.at[kind]
        elif kind < 10:
            d = kind - 6
            src, dst, peer = part.at[span(self.at_near + p.turn[d] * 8, 8)], self.from_z.at[d - 1], p.over_z[d]
        elif kind < 13:
            src = dst = total.at[span(self.at_near + p.z * 8, 8)]
            peer = p.over_z[kind - 9]
        else:
            src = dst = total.at[span(self.at_near, 32)]
            peer = self.near[kind - 12][1]
        return pltpu.make_async_remote_copy(
            src_ref=src, dst_ref=dst, send_sem=self.sends.at[kind], recv_sem=self.recvs.at[kind],
            device_id=peer, device_id_type=MESH,
        )

    def act(self, stage):
        p = self.peers
        hops = (range(0, 7), range(7, 10), range(10, 13), range(13, 20))
        if stage == 5:
            for kind in range(20):
                self.copy(kind).wait_send()
            return
        if stage > 0:
            for kind in hops[stage - 1]:
                self.copy(kind).wait_recv()
        if stage == 1:
            mine = span(self.at_near, 32)
            value = self.part[mine, :]
            for k in range(7):
                value = value + self.from_near[k]
            self.part[mine, :] = value
        elif stage == 2:
            mine = span(self.at_near + p.z * 8, 8)
            self.total[mine, :] = self.part[mine, :] + self.from_z[0] + self.from_z[1] + self.from_z[2]
        if stage < 4:
            for kind in hops[stage]:
                self.copy(kind).start()


def big_scratch(rows, lanes):
    half = rows // 2
    sems = pltpu.SemaphoreType.DMA((3, Reduction.kinds))
    return [
        pltpu.VMEM((3, 2, half, lanes), bf16), pltpu.VMEM((3, half, lanes), bf16),
        pltpu.VMEM((3, half // 2, lanes), bf16), pltpu.VMEM((3, 3, half // 8, lanes), bf16), sems, sems,
    ]


def small_scratch():
    return [
        pltpu.VMEM((7, 32, 128), f32), pltpu.VMEM((3, 8, 128), f32),
        pltpu.SemaphoreType.DMA((20,)), pltpu.SemaphoreType.DMA((20,)),
    ]


class Gather:
    pieces = 6

    def __init__(self, peers, whole, sends, recvs):
        self.peers, self.whole, self.sends, self.recvs = peers, whole, sends, recvs
        self.quarter = peers.x * 2 + peers.core
        self.next_quarter = (1 - peers.x) * 2 + peers.core

    def rows(self, ref, quarter):
        count = ref.shape[0] // 4
        return ref.at[span(quarter * count, count), :]

    def copy(self, index, kind):
        p = self.peers
        if kind == 0:
            src = dst = self.rows(self.whole(index, p.tp), self.quarter)
            peer = p.over_tp
        elif kind == 1:
            src = dst = self.rows(self.whole(index, 1 - p.tp), self.quarter)
            peer = p.over_x
        else:
            src = dst = self.rows(self.whole(index, 1 - p.tp), self.quarter if kind == 2 else self.next_quarter)
            peer = p.over_core
        return pltpu.make_async_remote_copy(
            src_ref=src, dst_ref=dst, send_sem=self.sends.at[index, kind], recv_sem=self.recvs.at[index, kind],
            device_id=peer, device_id_type=MESH,
        )

    def start(self, indices):
        for index in indices:
            self.copy(index, 0).start()

    def onward_x(self, index):
        self.copy(index, 0).wait_recv()
        self.copy(index, 1).start()
        self.copy(index, 2).start()

    def onward_core(self, index):
        self.copy(index, 1).wait_recv()
        self.copy(index, 3).start()

    def arrive(self, index):
        self.copy(index, 2).wait_recv()
        self.copy(index, 3).wait_recv()

    def finish(self):
        for index in range(self.pieces):
            for kind in range(4):
                self.copy(index, kind).wait_send()


def square_turn(values):
    rows, lanes = values.shape
    if lanes < 128:
        values = jnp.concatenate([values, jnp.zeros((rows, 128 - lanes), f32)], axis=1)
    if rows < 128:
        values = jnp.concatenate([values, jnp.zeros((128 - rows, 128), f32)], axis=0)
    return values.T


def widen(values):
    return jnp.concatenate([values] * (TILE // 128), axis=1)


def strips():
    return [slice(16 * i, 16 * (i + 1)) for i in range(K // 16)]


def four_rows(ref, slot, first):
    return jnp.concatenate([ref[slot, pl.ds(first + i, 1), :] for i in range(TILE // 128)], axis=1)


def hot_rows(values, count):
    return (values == iota((count, TILE), 0).astype(f32)).astype(f32)


def fold_lanes(values):
    total = values[:, :128]
    for i in range(1, TILE // 128):
        total = total + values[:, 128 * i : 128 * (i + 1)]
    return total


def prepare_pairs(r):
    spr = to_column(row_of(r.spreads))
    r.cols[0] = jnp.broadcast_to(to_column(row_of(r.centers)), (K, 128))
    r.cols[1] = jnp.broadcast_to(root_half / spr, (K, 128))
    r.cols[2] = jnp.broadcast_to(-jnp.log(root_tau * spr), (K, 128))
    r.cols[3] = jnp.broadcast_to(to_column(row_of(r.first_bias)), (K, 128))
    r.cols[4] = jnp.broadcast_to(1.0 / spr, (K, 128))
    r.w1t[...] = r.first_weight[...].astype(f32).T.astype(bf16)
    r.w2[...] = square_turn(r.second_weight[...].astype(f32)).astype(bf16)
    table = jnp.concatenate([r.hop_table[...], r.edge_table[...], jnp.zeros((128 - HOPS - EDGES, H), f32)], axis=0)
    table = jnp.concatenate([table, jnp.zeros((128, 128 - H), f32)], axis=1).T[:H, :HOT]
    one = table.astype(bf16).astype(f32)
    r.base[...] = jnp.concatenate(
        [r.second_weight[...].astype(f32), one, table - one, jnp.zeros((H, 64), f32)], axis=1
    )


def bf16_parts(values, count):
    parts = []
    for _ in range(count):
        parts.append(values.astype(bf16))
        values = values - parts[-1].astype(f32)
    return parts


def pair_tables(r, slots):
    low = low_lanes(HALF)
    low_row = low_lanes(1)
    tables = [part.astype(f32) for ref in (r.kernel_scale, r.kernel_shift) for part in bf16_parts(ref[...], 3)]
    tables = jnp.concatenate([square_turn(part)[:ATOMS, :ATOMS] for part in tables], axis=1)
    tables = jnp.concatenate([tables, jnp.zeros((ATOMS, 128 - 6 * ATOMS), f32)], axis=1).astype(bf16)
    for group in range(slots // 2):
        lanes = slice(128 * group, 128 * (group + 1))
        atoms = r.atoms[lanes].astype(f32).reshape(1, 128)
        rows = jnp.concatenate([r.positions[:, lanes], atoms, jnp.zeros((4, 128), f32)], axis=0)
        columns = square_turn(rows)
        key_hot = (columns[:, 3:4] == iota((128, ATOMS), 1).astype(f32)).astype(f32).astype(bf16)
        picks = dot_nn(key_hot, tables).astype(bf16)
        turned = half_swap(rows)
        for s in range(2):
            slot = 2 * group + s
            tokens = slice(SLOT * s, SLOT * (s + 1))
            double = jnp.where(low_lanes(8), *((rows, turned) if s == 0 else (turned, rows)))
            total = None
            for c in range(3):
                column = columns[tokens, c : c + 1]
                offset = jnp.where(low, column[:HALF], column[HALF:]) - double[c : c + 1]
                total = offset * offset if total is None else total + offset * offset
            distance = jnp.sqrt(total)
            query_hot = (double[3:4] == iota((ATOMS, 128), 0).astype(f32)).astype(f32)
            three, none = [query_hot] * 3, [jnp.zeros((3 * ATOMS, 128), f32)]
            rest = [jnp.zeros((128 - 6 * ATOMS, 128), f32)]
            spread = jnp.concatenate(
                [jnp.concatenate(three + none + rest, axis=0), jnp.concatenate(none + three + rest, axis=0)], axis=1
            )
            both = dot_nn(picks[tokens], spread.astype(bf16))
            scale = jnp.where(low, both[:HALF, :128], both[HALF:, :128])
            shift = jnp.where(low, both[:HALF, 128:], both[HALF:, 128:])
            r.argument[slot] = scale * distance + shift
            r.distance[slot] = distance
            for source, target in ((r.hops, r.hop_rows), (r.edges, r.edge_rows)):
                values = source[:, lanes].astype(f32)
                top, bottom = values[:HALF], values[HALF:]
                if s == 0:
                    target[slot] = jnp.where(low, top, half_swap(bottom))
                else:
                    target[slot] = jnp.where(low, half_swap(top), bottom)
            r.atom_rows[slot] = jnp.broadcast_to(double[3:4], (8, 128))


def table_grads(r, slots):
    lefts, rights = [], []
    for slot in range(slots):
        query_hot = (r.atom_rows[slot, 0:1, :] == iota((ATOMS, 128), 0).astype(f32)).astype(f32)
        keys = jnp.concatenate([query_hot[:, :HALF], query_hot[:, HALF:SLOT]], axis=0)
        keys = jnp.concatenate([keys, keys], axis=1).astype(bf16)
        values = jnp.concatenate([r.dargs[slot] * r.distance[slot], r.dargs[slot]], axis=1)
        both = dot_nn(keys, jnp.concatenate(bf16_parts(values, 2), axis=0))
        low = low_lanes(ATOMS)
        for index in range(2):
            lanes = slice(128 * index, 128 * (index + 1))
            rights.append(bf16_parts(jnp.where(low, both[:ATOMS, lanes], both[ATOMS:, lanes]), 2))
        lefts.append(query_hot.astype(bf16))
    left = jnp.concatenate(lefts, axis=1)
    right = jnp.concatenate(
        [jnp.concatenate([rights[2 * s + index][part] for s in range(slots)], axis=1) for index in range(2) for part in range(2)],
        axis=0,
    )
    result = dot_nt(left, right)
    return [
        result[:, 2 * ATOMS * index : 2 * ATOMS * index + ATOMS] + result[:, 2 * ATOMS * index + ATOMS : 2 * ATOMS * (index + 1)]
        for index in range(2)
    ]


def in_stages(stages, count):
    held = {}
    for time in range(count + len(stages) - 1):
        for k, stage in reversed(list(enumerate(stages))):
            if 0 <= time - k < count:
                held[time - k] = stage(time - k, held.get(time - k))


TILES = PAIRS // TILE
ROWS = TILE // 128


def pair_forward(r, slot):
    bank = lax.rem(slot, 2)
    graph_on = r.flags[0, slot].astype(f32)
    space_on = r.flags[1, slot].astype(f32)
    factor = jnp.where(iota((H, 256), 1) < K, space_on, graph_on)
    r.lhs[...] = (r.base[...] * factor).astype(bf16)

    def kernels(tile, _):
        where = slice(tile * TILE, (tile + 1) * TILE)
        arg = four_rows(r.argument, slot, tile * ROWS)
        pieces = []
        for rows in strips():
            u = (arg - widen(r.cols[0, rows])) * widen(r.cols[1, rows])
            pieces.append(jnp.exp(widen(r.cols[2, rows]) - u * u).astype(bf16))
            r.left[bank, rows, where] = pieces[-1]
        return dot_nn(r.w1t[...], jnp.concatenate(pieces, axis=0))

    def hidden(tile, first):
        where = slice(tile * TILE, (tile + 1) * TILE)
        pieces = []
        for rows in strips():
            value, slope = gelu_parts(first[rows] + widen(r.cols[3, rows]))
            pieces.append(value.astype(bf16))
            r.left[bank, slice(K + rows.start, K + rows.stop), where] = pieces[-1]
            r.slope[bank, rows, where] = slope.astype(bf16)
        hot = jnp.concatenate(
            [
                hot_rows(four_rows(r.hop_rows, slot, tile * ROWS), HOPS),
                hot_rows(four_rows(r.edge_rows, slot, tile * ROWS), HOT - HOPS),
            ],
            axis=0,
        ).astype(bf16)
        return dot_nn(r.lhs[:, : K + 2 * HOT], jnp.concatenate(pieces + [hot] * 2, axis=0))

    def biases(tile, bias):
        bias = bias.astype(bf16).astype(f32)
        for i in range(ROWS):
            r.bias[slot, pl.ds(tile * ROWS + i, H, stride=HALF), :] = bias[:, 128 * i : 128 * (i + 1)]

    in_stages([kernels, hidden, biases], TILES)


def pair_backward(r, slot, between):
    bank = lax.rem(slot, 2)
    graph_on = r.flags[0, slot].astype(f32)
    space_on = r.flags[1, slot].astype(f32)
    w2 = r.w2[:, :H] * space_on.astype(bf16)

    def scores(tile, _):
        where = slice(tile * TILE, (tile + 1) * TILE)
        grad = jnp.concatenate(
            [r.bias[slot, pl.ds(tile * ROWS + i, H, stride=HALF), :] for i in range(ROWS)], axis=1
        )
        r.right[K:, where] = jnp.concatenate([grad * space_on, grad * graph_on], axis=0).astype(bf16)
        edge_hot = hot_rows(four_rows(r.edge_rows, slot, tile * ROWS), HOT - HOPS)
        edge_hot = jnp.where(iota((HOT - HOPS, TILE), 0) == EDGES, 1.0, edge_hot)
        r.left[bank, 2 * K :, where] = jnp.concatenate(
            [hot_rows(four_rows(r.hop_rows, slot, tile * ROWS), HOPS), edge_hot], axis=0
        ).astype(bf16)
        return dot_nn(w2, grad.astype(bf16))

    def hidden(tile, d_second):
        where = slice(tile * TILE, (tile + 1) * TILE)
        pieces = []
        for rows in strips():
            pieces.append((d_second[rows] * r.slope[bank, rows, where].astype(f32)).astype(bf16))
            r.right[rows, where] = pieces[-1]
        return dot_nn(r.first_weight[...], jnp.concatenate(pieces, axis=0))

    def kernels(tile, d_gauss):
        where = slice(tile * TILE, (tile + 1) * TILE)
        arg = four_rows(r.argument, slot, tile * ROWS)
        d_arg = None
        for rows in strips():
            inv = widen(r.cols[4, rows])
            u = (arg - widen(r.cols[0, rows])) * inv
            q = d_gauss[rows] * r.left[bank, rows, where].astype(f32)
            w = q * u
            r.sums[0, rows] += fold_lanes(w)
            r.sums[1, rows] += fold_lanes(w * u - q)
            w = w * inv
            w = w[:8] + w[8:]
            d_arg = w if d_arg is None else d_arg + w
        d_arg = -jnp.sum(d_arg, axis=0, keepdims=True)
        for i in range(ROWS):
            at = tile * ROWS + i
            r.dargs[slot, at : at + 1, :] = d_arg[:, 128 * i : 128 * (i + 1)]

    in_stages([scores, hidden, kernels], TILES)
    between()
    r.acc_mixed[...] += dot_nt(r.left[bank], r.right[...])


def attend(r, s, first_slot):
    low = low_lanes(HALF)
    rows = span(s * SLOT, SLOT)
    valid = iota((SLOT, GROUP * SLOT), 0) < r.lengths[first_slot + s]
    r.work[0] = jnp.zeros((SLOT, D), f32)
    for g in range(GROUPS):
        start, width, _ = window(g)
        q = r.joined[rows, start : start + width]
        k = r.joined[rows, D + start : D + start + width]
        v = r.joined[rows, 2 * D + start : 2 * D + start + width]
        scores = dot_nt(k, spread_heads(q, g)) * head_scale
        parts = []
        for pair in range(GROUP // 2):
            head = GROUP * g + 2 * pair
            one = r.bias[s, head * HALF : (head + 1) * HALF, :]
            two = r.bias[s, (head + 1) * HALF : (head + 2) * HALF, :]
            top = jnp.where(low, one, half_swap(two))
            bottom = jnp.where(low, half_swap(one), two)
            parts.append(jnp.concatenate([top, bottom], axis=0))
        scores = jnp.where(valid, scores + jnp.concatenate(parts, axis=1), neg_large)
        weights = jnp.exp(scores - jnp.max(scores, axis=0, keepdims=True))
        prob = (weights * (1.0 / jnp.sum(weights, axis=0, keepdims=True))).astype(bf16)
        r.prob[s, :, g * GROUP * SLOT : (g + 1) * GROUP * SLOT] = prob
        r.work[0, :, start : start + width] += gather_heads(dot_tn(prob, v), g)
    r.attended[rows, :] = r.work[0].astype(bf16)


def attend_back(r, s):
    low = low_lanes(HALF)
    rows = span(s * SLOT, SLOT)
    r.work[...] = jnp.zeros((3, SLOT, D), f32)
    for g in range(GROUPS):
        start, width, _ = window(g)
        lanes = slice(start, start + width)
        k = r.joined[rows, D + start : D + start + width]
        v = r.joined[rows, 2 * D + start : 2 * D + start + width]
        q_heads = spread_heads(r.joined[rows, lanes], g)
        d_heads = spread_heads(r.d_attended[rows, lanes], g)
        prob = r.prob[s, :, g * GROUP * SLOT : (g + 1) * GROUP * SLOT]
        wide = prob.astype(f32)
        d_prob = dot_nt(v, d_heads)
        inner = jnp.sum(wide * d_prob, axis=0, keepdims=True)
        d_scores = (wide * (d_prob - inner)).astype(bf16)
        r.work[0, :, lanes] += gather_heads(dot_tn(d_scores, k), g)
        r.work[1, :, lanes] += dot_nn(d_scores, q_heads)
        r.work[2, :, lanes] += dot_nn(prob, d_heads)
        d_wide = d_scores.astype(f32)
        for pair in range(GROUP // 2):
            head = GROUP * g + 2 * pair
            top = d_wide[:HALF, 128 * pair : 128 * (pair + 1)]
            bottom = d_wide[HALF:, 128 * pair : 128 * (pair + 1)]
            r.bias[s, head * HALF : (head + 1) * HALF, :] = jnp.where(low, top, half_swap(bottom))
            r.bias[s, (head + 1) * HALF : (head + 2) * HALF, :] = jnp.where(low, half_swap(top), bottom)
    r.joined[rows, 0:D] = (r.work[0] * head_scale).astype(bf16)
    r.joined[rows, D : 2 * D] = (r.work[1] * head_scale).astype(bf16)
    r.joined[rows, 2 * D : 3 * D] = r.work[2].astype(bf16)


def project(r, rows):
    scaled, _ = standardize(r.hidden[rows, :].astype(f32))
    normed = (scaled * row_of(r.attn_gain) + row_of(r.attn_shift)).astype(bf16)
    r.normed_a[rows, :] = normed
    for m in range(3):
        for t in range(2):
            at = m * D + t * HALF_D
            r.joined[rows, at : at + HALF_D] = dot_nn(normed, r.wqkv[t, m]).astype(bf16)


def feed(r, rows):
    halves = [slice(0, HALF_D), slice(HALF_D, D)]
    resid = r.hidden[rows, :].astype(f32)
    for t in range(2):
        resid = resid + dot_nn(r.attended[rows, halves[t]], r.wproj[t])
    scaled, inv_std = standardize(resid)
    normed = (scaled * row_of(r.ffn_gain) + row_of(r.ffn_shift)).astype(bf16)
    r.normed_f[rows, :] = normed
    pre = jnp.concatenate([dot_nn(normed, r.wup[t]) for t in range(2)], axis=1)
    value, slope = gelu_parts(pre + row_of(r.up_bias))
    active = value.astype(bf16)
    r.activated[rows, :] = active
    result = resid + row_of(r.down_bias)
    for t in range(2):
        result = result + dot_nn(active[:, halves[t]], r.wdown[t])
    r.out_rows[rows, :] = result.astype(bf16)
    cot = r.cotangent[rows, :]
    cot_wide = cot.astype(f32)
    d_active = jnp.concatenate([dot_nt(cot, r.wdown[t]) for t in range(2)], axis=1)
    d_hidden = (d_active * slope).astype(bf16)
    r.d_pre[rows, :] = d_hidden
    d_normed = dot_nt(d_hidden[:, halves[0]], r.wup[0]) + dot_nt(d_hidden[:, halves[1]], r.wup[1])
    d_resid = cot_wide + norm_back(d_normed, scaled, inv_std, row_of(r.ffn_gain))
    r.d_resid[rows, :] = d_resid
    branch = d_resid.astype(bf16)
    r.d_branch[rows, :] = branch
    for t in range(2):
        r.d_attended[rows, halves[t]] = dot_nt(branch, r.wproj[t]).astype(bf16)
    r.vectors[2:3, :] += column_sum(d_normed * scaled)
    r.vectors[3:4, :] += column_sum(d_normed)
    r.vectors[4:5, :] += column_sum(d_hidden.astype(f32))
    r.vectors[5:6, :] += column_sum(cot_wide)


def feed_grads(r, block):
    halves = [slice(0, HALF_D), slice(HALF_D, D)]
    if block == 0:
        grad = dot_tn(r.normed_f[...], r.d_pre[...]).astype(bf16)
        for t in range(2):
            r.fpart[t, :D, :] = grad[:, halves[t]]
        return
    left, right = (r.attended, r.d_branch) if block == 1 else (r.activated, r.cotangent)
    for t in range(2):
        grad = dot_tn(left[:, halves[t]], right[...]).astype(bf16)
        for side in range(2):
            r.fpart[t, D * block + HALF_D * side : D * block + HALF_D * (side + 1), :] = grad[:, halves[side]]


def qkv_grads(r, block):
    rows = slice(256 * block, 256 * (block + 1))
    for m in range(3):
        grad = dot_tn(r.normed_a[:, rows], r.joined[:, m * D : (m + 1) * D]).astype(bf16)
        for t in range(2):
            r.qpart[t, rows, m * HALF_D : (m + 1) * HALF_D] = grad[:, t * HALF_D : (t + 1) * HALF_D]


def finish_input(r, rows):
    d_normed = None
    for m in range(3):
        for t in range(2):
            at = m * D + t * HALF_D
            term = dot_nt(r.joined[rows, at : at + HALF_D], r.wqkv[t, m])
            d_normed = term if d_normed is None else d_normed + term
    scaled, inv_std = standardize(r.hidden[rows, :].astype(f32))
    grad = r.d_resid[rows, :] + norm_back(d_normed, scaled, inv_std, row_of(r.attn_gain))
    r.in_rows[rows, :] = grad.astype(bf16)
    r.vectors[0:1, :] += column_sum(d_normed * scaled)
    r.vectors[1:2, :] += column_sum(d_normed)


def pack_small(r, slots):
    tables = table_grads(r, slots)
    for v in range(6):
        for i in range(D // 128):
            at = VECTOR_ROWS + v * (D // 128) + i
            r.spart[at : at + 1, :] = r.vectors[v : v + 1, 128 * i : 128 * (i + 1)]
    r.spart[0:K, :] = r.acc_mixed[0:K, :K]
    r.spart[SECOND_ROWS : SECOND_ROWS + H, :] = square_turn(r.acc_mixed[K : 2 * K, K:])[:H]
    r.spart[TABLE_ROWS : TABLE_ROWS + H, :HOT] = square_turn(r.acc_mixed[2 * K :, K:])[H : 2 * H, :HOT]
    for index in range(2):
        rows = slice(TABLE_ROWS + ATOMS * index, TABLE_ROWS + ATOMS * (index + 1))
        r.spart[rows, HOT : HOT + ATOMS] = tables[index]
    ones = 2 * K + HOPS + EDGES
    r.spart[KERNEL_ROWS : KERNEL_ROWS + 1, :] = r.acc_mixed[ones : ones + 1, :K]
    for index in range(2):
        column = jnp.sum(r.sums[index] * r.cols[4], axis=1, keepdims=True)
        same = iota((K, K), 0) == iota((K, K), 1)
        at = KERNEL_ROWS + 1 + index
        r.spart[at : at + 1, :] = jnp.sum(jnp.where(same, column, 0.0), axis=0, keepdims=True)


class Stage:
    def __init__(self, names, near_inputs, carried, refs):
        self.r = SimpleNamespace(**dict(zip(names, refs)))
        r = self.r
        self.loads = {
            name: pltpu.make_async_copy(getattr(r, "given_" + name), getattr(r, name), r.input_sems.at[i])
            for i, name in enumerate(near_inputs)
        }
        self.stores = {
            name: pltpu.make_async_copy(getattr(r, name), getattr(r, name + "_far"), r.carry_sems.at[i])
            for i, name in enumerate(carried)
        }

    def load(self, *names):
        for name in names:
            self.loads[name].start()

    def need(self, *names):
        for name in names:
            self.loads[name].wait()

    def store(self, *names):
        for name in names:
            self.stores[name].start()

    def stored(self):
        for copy in self.stores.values():
            copy.wait()


def each_chunk(r, tokens, work):
    chunk = min(256, tokens)

    def one(c, _):
        work(r, span(c * chunk, chunk))
        return 0

    lax.fori_loop(0, tokens // chunk, one, 0)


def pair_moves(r, slot, back):
    bank = lax.rem(slot, 2)
    both = (r.left_far.at[slot], r.left.at[bank, : 2 * K]), (r.slope_far.at[slot], r.slope.at[bank])
    for index, (far, near) in enumerate(both):
        yield pltpu.make_async_copy(*((far, near) if back else (near, far)), r.pair_sems.at[bank, index])


def start_moves(r, slot, back):
    for copy in pair_moves(r, slot, back):
        copy.start()


def wait_moves(r, slot, back):
    for copy in pair_moves(r, slot, back):
        copy.wait()


def run(steps):
    for act, *where in steps:
        act(*where)


def at_time(index, plan):
    for k, steps in plan.items():
        pl.when(index == k)(functools.partial(run, steps))


FFN_BACK = {0: [(1, 1), (2, 1)], 3: [(0, 2)], 7: [(0, 3), (1, 2)]}
AFTER_GRADS = ([(0, 4), (1, 3), (2, 2)], [(0, 1), (1, 1), (2, 1)])
AFTER_HALF = ([(0, 5)], [])
AFTER_INPUT = ([(2, 3), (1, 4)], [(0, 2)])
FFN_PAIRS = {
    0: [(0, 6)], 2: [(2, 4)], 3: [(1, 5), (0, 7)], 5: [(2, 5)], 7: [(1, 6)], 9: [(2, 6)], 10: [(1, 7)], 12: [(2, 7)],
}
QKV_PAIRS = {
    2: [(0, 3)], 3: [(1, 2)], 6: [(1, 3), (2, 2), (0, 4)], 9: [(1, 4)], 10: [(0, 5)], 11: [(2, 3)], 12: [(1, 5)],
    13: [(0, 6)], 14: [(2, 4)], 15: [(1, 6)],
}


def layer_kernel(remote, names, near_inputs, carried, *refs):
    stage = Stage(names, near_inputs, carried, refs)
    r = stage.r
    stage.load(*[name for name in near_inputs if name not in ("hidden", "cotangent")])
    tokens = r.hidden.shape[0]
    slots = tokens // SLOT
    peers = Peers()
    whole = [r.wqkv, r.wup, r.wproj, r.wdown]
    given = [r.given_qkv, r.given_up, r.given_proj, r.given_down]
    targets = [w.at[peers.tp] for w in whole] if remote else whole
    loads = [
        pltpu.make_async_copy(src, dst, r.load_sems.at[i]) for i, (src, dst) in enumerate(zip(given, targets))
    ]
    for load in loads:
        load.start()
    stage.load("hidden", "cotangent")
    gather_plan = {}
    if remote:

        def whole_piece(index, tp):
            return whole[0].at[tp, index] if index < 3 else whole[index - 2].at[tp]

        gather = Gather(peers, whole_piece, r.gather_sends, r.gather_recvs)
        ffn = Reduction(peers, r.fpart, r.ftotal, r.f_core, r.f_tp, r.f_x, r.f_z, r.f_sends, r.f_recvs)
        qkv = Reduction(peers, r.qpart, r.qtotal, r.q_core, r.q_tp, r.q_x, r.q_z, r.q_sends, r.q_recvs)
        small = SmallReduction(peers, r.spart, r.stotal, r.s_near, r.s_z, r.s_sends, r.s_recvs)
        greet(peers.everyone())
        for load, indices in zip(loads, ((0, 1, 2), (3,), (4,), (5,))):
            load.wait()
            gather.start(indices)
        x, core = gather.onward_x, gather.onward_core
        gather_plan = {
            0: [(x, 0)], 1: [(x, 1), (core, 0)], 2: [(x, 2), (core, 1)], 3: [(x, 3), (core, 2)],
            4: [(x, 4), (core, 3), (x, 5)], 5: [(core, 4)], 6: [(core, 5)],
        }

    def leave(which, block):
        near, far = ((r.ftotal, r.ftotal_far), (r.qtotal, r.qtotal_far))[which]
        rows = near.shape[0] // 3
        at = slice(block * rows, (block + 1) * rows)
        return pltpu.make_async_copy(near.at[at], far.at[at], r.leave_sems.at[3 * which + block])

    def advance(which, actions):
        if remote:
            for block, step in actions:
                (ffn, qkv)[which].act(block, step)
                if step == 7:
                    leave(which, block).start()

    def plan_of(*plans):
        times = sorted(set().union(*plans)) if remote else []
        return {
            k: [(advance, which, plan[k]) for which, plan in enumerate(plans) if k in plan] for k in times
        }

    stage.need(*[name for name in near_inputs if name not in ("hidden", "cotangent")])
    prepare_pairs(r)
    pair_tables(r, slots)

    def pairs(slot, _):
        pl.when(slot >= 2)(lambda: wait_moves(r, slot - 2, False))
        pair_forward(r, slot)
        start_moves(r, slot, False)
        at_time(slot, gather_plan)
        return 0

    lax.fori_loop(0, slots, pairs, 0)
    stage.need("hidden")
    if remote:
        for index in range(3):
            gather.arrive(index)
    else:
        for load in loads:
            load.wait()
    each_chunk(r, tokens, project)
    first_slot = peers.tp * slots

    def attend_one(s, _):
        attend(r, s, first_slot)
        return 0

    lax.fori_loop(0, slots, attend_one, 0)
    stage.need("cotangent")
    if remote:
        for index in range(3, 6):
            gather.arrive(index)
    r.vectors[...] = jnp.zeros_like(r.vectors)
    each_chunk(r, tokens, feed)
    stage.store("out_rows")
    for slot in (slots - 2, slots - 1):
        wait_moves(r, slot, False)
    start_moves(r, 0, True)
    start_moves(r, 1, True)
    for block in range(3):
        feed_grads(r, block)
        advance(0, [(block, 0)])
    advance(0, [(0, 1)])

    back_plan, pair_plan = plan_of(FFN_BACK), plan_of(FFN_PAIRS, QKV_PAIRS)

    def back_one(s, _):
        attend_back(r, s)
        at_time(s, back_plan)
        return 0

    lax.fori_loop(0, slots, back_one, 0)
    for block in range(3):
        qkv_grads(r, block)
        advance(1, [(block, 0)])
    for which in range(2):
        advance(which, AFTER_GRADS[which])
    each_chunk(r, tokens, finish_input)
    stage.store("in_rows")
    for which in range(2):
        advance(which, AFTER_HALF[which] + AFTER_INPUT[which])
    for ref in (r.sums, r.acc_mixed, r.spart):
        ref[...] = jnp.zeros_like(ref)

    def pairs_back(slot, _):
        wait_moves(r, slot, True)
        pair_backward(r, slot, lambda: at_time(2 * slot, pair_plan))
        pl.when(slot + 2 < slots)(lambda: start_moves(r, slot + 2, True))
        at_time(2 * slot + 1, pair_plan)
        return 0

    lax.fori_loop(0, slots, pairs_back, 0)
    pack_small(r, slots)
    if remote:
        small.act(0)
        advance(1, [(2, 5), (0, 7)])
        small.act(1)
        advance(1, [(1, 7)])
        small.act(2)
        advance(1, [(2, 6)])
        small.act(3)
        advance(1, [(2, 7)])
        small.act(4)
        rows = pltpu.make_async_copy(r.stotal, r.stotal_far, r.leave_sems.at[6])
        rows.start()
        for which in range(2):
            advance(which, [(b, 8) for b in range(3)])
        small.act(5)
        gather.finish()
        for which in range(2):
            for block in range(3):
                leave(which, block).wait()
        rows.wait()
    else:
        stage.store("fpart", "qpart", "spart")
    stage.stored()


def call_stage(kernel, name, remote, collective, arrays, scalars, far, outs, carried, scratch):
    vm, sem = pltpu.VMEM, pltpu.SemaphoreType.DMA
    near = {n: vm(a.shape, a.dtype) for n, a in arrays.items() if n not in scalars + far}
    in_names = [n if n in scalars or n.endswith("_far") else "given_" + n for n in arrays]
    results = outs | {n + "_far": item for n, item in carried.items()}
    scratch = near | {n: vm(*item) for n, item in carried.items()} | scratch
    scratch |= {"input_sems": sem((len(near),)), "carry_sems": sem((len(carried),))}
    names = in_names + list(results) + list(scratch)
    values = pl.pallas_call(
        functools.partial(kernel, remote, names, list(near), list(carried)),
        in_specs=[pl.BlockSpec(memory_space=pltpu.SMEM if n in scalars else pl.ANY) for n in arrays],
        out_specs=[pl.BlockSpec(memory_space=pl.ANY)] * len(results),
        out_shape=[jax.ShapeDtypeStruct(*item) for item in results.values()],
        scratch_shapes=list(scratch.values()),
        compiler_params=pltpu.CompilerParams(
            vmem_limit_bytes=VMEM_BYTES, **(dict(collective_id=collective, has_side_effects=True) if remote else {})
        ),
        name=name,
    )(*arrays.values())
    return dict(zip(results, values))


def layer(remote, arrays):
    tokens = arrays["hidden"].shape[0]
    slots = tokens // SLOT
    v, sem = pltpu.VMEM, pltpu.SemaphoreType.DMA
    of_tokens = (tokens, D)
    table = (slots, HALF, 128)
    fshape, qshape, sshape = (3 * D, HALF_D), (D, 3 * HALF_D), (SMALL_ROWS, 128)
    outs = {"left_far": ((slots, 2 * K, PAIRS), bf16), "slope_far": ((slots, K, PAIRS), bf16)}
    carried = {"out_rows": (of_tokens, bf16), "in_rows": (of_tokens, bf16)}
    scratch = {
        "wqkv": v((2, 3, D, HALF_D), bf16), "wup": v((2, D, HALF_D), bf16), "wproj": v((2, HALF_D, D), bf16),
        "wdown": v((2, HALF_D, D), bf16), "load_sems": sem((4,)), "pair_sems": sem((2, 2)),
        "left": v((2, 2 * K + HOT, PAIRS), bf16), "slope": v((2, K, PAIRS), bf16),
        "right": v((K + 2 * H, PAIRS), bf16), "cols": v((5, K, 128), f32), "w1t": v((K, K), bf16),
        "w2": v((K, 128), bf16), "base": v((H, 256), f32), "lhs": v((H, 256), bf16),
        "argument": v(table, f32), "distance": v(table, f32), "hop_rows": v(table, f32), "edge_rows": v(table, f32),
        "atom_rows": v((slots, 8, 128), f32), "dargs": v(table, f32), "bias": v((slots, H * HALF, 128), f32),
        "work": v((3, SLOT, D), f32), "normed_a": v(of_tokens, bf16), "joined": v((tokens, 3 * D), bf16),
        "prob": v((slots, SLOT, H * SLOT), bf16), "attended": v(of_tokens, bf16), "normed_f": v(of_tokens, bf16),
        "activated": v(of_tokens, bf16), "d_pre": v(of_tokens, bf16), "d_branch": v(of_tokens, bf16),
        "d_attended": v(of_tokens, bf16), "d_resid": v(of_tokens, f32), "vectors": v((8, D), f32),
        "sums": v((2, K, 128), f32), "acc_mixed": v((2 * K + HOT, K + 2 * H), f32),
    }
    parts = {"fpart": ((2,) + fshape, bf16), "qpart": ((2,) + qshape, bf16), "spart": (sshape, f32)}
    totals = {"ftotal": (fshape, bf16), "qtotal": (qshape, bf16), "stotal": (sshape, f32)}
    if remote:
        outs |= {n + "_far": item for n, item in totals.items()}
        scratch |= {n: v(*item) for n, item in (parts | totals).items()}
        scratch |= {"leave_sems": sem((7,)), "gather_sends": sem((6, 4)), "gather_recvs": sem((6, 4))}
        for name, shape in (("f", (D, HALF_D)), ("q", (D // 3, 3 * HALF_D))):
            keys = ("_core", "_tp", "_x", "_z", "_sends", "_recvs")
            scratch |= {name + key: item for key, item in zip(keys, big_scratch(*shape))}
        scratch |= dict(zip(("s_near", "s_z", "s_sends", "s_recvs"), small_scratch()))
    else:
        carried |= parts
    results = call_stage(
        layer_kernel, "layer", remote, 0, arrays, ("lengths", "flags"), ("qkv", "up", "proj", "down"), outs, carried,
        scratch,
    )
    sums = [results[n + "_far"] for n in (totals if remote else parts)]
    return results["out_rows_far"], results["in_rows_far"], sums


def unpack_kernel(
    qsum, up_sum, proj_low, proj_high, down_low, down_high, out_rows, in_rows, rows_ref,
    output, grad_input, again, ashift, qkv, proj, fgain, fshift, up, up_bias, down, down_bias, scale, shift, centers,
    spreads, first, first_bias, second, hop, edge,
):
    output[...] = out_rows[...]
    grad_input[...] = in_rows[...]
    for m in range(3):
        qkv[m] = qsum[:, m * HALF_D : (m + 1) * HALF_D].astype(f32)
    up[...] = up_sum[...].astype(f32)
    for low, high, ref in ((proj_low, proj_high, proj), (down_low, down_high, down)):
        ref[:, :HALF_D] = low[...].astype(f32)
        ref[:, HALF_D:] = high[...].astype(f32)

    @pl.when(pl.program_id(0) == 0)
    def _():
        for v, ref in enumerate((again, ashift, fgain, fshift, up_bias, down_bias)):
            for i in range(D // 128):
                ref[pl.ds(128 * i, 128)] = rows_ref[VECTOR_ROWS + v * (D // 128) + i, :]
        first[...] = rows_ref[0:K, :]
        second[...] = rows_ref[SECOND_ROWS : SECOND_ROWS + H, :]
        table = rows_ref[TABLE_ROWS : TABLE_ROWS + H, :]
        scale[...] = table[:ATOMS, HOT : HOT + ATOMS]
        shift[...] = table[ATOMS:, HOT : HOT + ATOMS]
        turned = square_turn(table)
        hop[...] = turned[:HOPS, :H]
        edge[...] = turned[HOPS : HOPS + EDGES, :H]
        for i, ref in enumerate((first_bias, centers, spreads)):
            ref[...] = rows_ref[KERNEL_ROWS + i, :]


def unpack(out_rows, in_rows, fsum, qsum, rows):
    steps = 4
    tokens = out_rows.shape[0]
    shape = jax.ShapeDtypeStruct
    vec, line = shape((D,), f32), shape((K,), f32)
    mat = lambda *dims: shape(dims, f32)
    whole = lambda item: pl.BlockSpec(item.shape, lambda i: (0,) * len(item.shape))
    by_rows = lambda count, lanes: pl.BlockSpec((count // steps, lanes), lambda i: (i, 0))
    piece = lambda first, count: pl.BlockSpec((count, HALF_D), lambda i: (first // count + i, 0))
    token_rows = by_rows(tokens, D)
    all_q = pl.BlockSpec((3, D // steps, HALF_D), lambda i: (0, i, 0))
    half = HALF_D // steps
    small = [mat(ATOMS, ATOMS), mat(ATOMS, ATOMS), line, line, mat(K, K), line, mat(H, K), mat(HOPS, H), mat(EDGES, H)]
    return pl.pallas_call(
        unpack_kernel,
        grid=(steps,),
        in_specs=[
            by_rows(D, 3 * HALF_D), piece(0, D // steps), piece(D, half), piece(D + HALF_D, half), piece(2 * D, half),
            piece(2 * D + HALF_D, half), token_rows, token_rows, whole(rows),
        ],
        out_specs=[
            token_rows, token_rows, whole(vec), whole(vec), all_q, by_rows(HALF_D, D), whole(vec), whole(vec),
            by_rows(D, HALF_D), whole(vec), by_rows(HALF_D, D), whole(vec),
        ] + [whole(item) for item in small],
        out_shape=[
            shape((tokens, D), bf16), shape((tokens, D), bf16), vec, vec, mat(3, D, HALF_D), mat(HALF_D, D), vec, vec,
            mat(D, HALF_D), vec, mat(HALF_D, D), vec,
        ] + small,
        compiler_params=pltpu.CompilerParams(vmem_limit_bytes=VMEM_BYTES),
        name="unpack",
    )(qsum, fsum, fsum, fsum, fsum, fsum, out_rows, in_rows, rows)


def whole_weights(qkv_weight, up_weight, proj_weight, down_weight):
    columns = lambda w: jnp.stack(jnp.split(w, 2, axis=-1))
    rows = lambda w: jnp.stack(jnp.split(w, 2, axis=0))
    gather = lambda w, dim: lax.all_gather(w, "tp", axis=dim, tiled=True)
    return (
        columns(gather(qkv_weight.transpose(1, 0, 2), 2)), columns(gather(up_weight, 1)),
        rows(gather(proj_weight, 0)), rows(gather(down_weight, 0)),
    )


def sum_grads(fgrads, qgrads, small):
    total_f, total_q, rows = lax.psum((fgrads, qgrads, small), ("mol", "tp"))
    share = D // lax.axis_size("tp")
    at = lax.axis_index("tp") * share

    def columns(halves):
        return lax.dynamic_slice_in_dim(jnp.concatenate(list(halves), axis=-1), at, share, halves.ndim - 2)

    def rows_of(block):
        part = total_f[:, D * block : D * (block + 1)]
        sides = jnp.concatenate([part[:, :HALF_D], part[:, HALF_D:]], axis=2).reshape(D, D)
        return lax.dynamic_slice_in_dim(sides, at, share, 0)

    qkv = columns(total_q.reshape(2, D, 3, HALF_D)).transpose(1, 0, 2)
    return [v.astype(f32) for v in (qkv, columns(total_f[:, :D]), rows_of(1), rows_of(2))], rows


def body(
    mesh_shape,
    hidden_in, positions, atom_types, hop_counts, edge_types, lengths, branches,
    attn_gain, attn_shift, qkv_weight, proj_weight, ffn_gain, ffn_shift, up_weight, up_bias, down_weight, down_bias,
    kernel_scale, kernel_shift, centers, spreads, first_weight, first_bias, second_weight, hop_table, edge_table,
    cotangent,
):
    remote = mesh_shape["tp"] == 2 and mesh_shape["mol"] == 16 and branches.shape[0] == 8
    if remote:
        weights = (qkv_weight.transpose(1, 0, 2), up_weight, proj_weight, down_weight)
    else:
        weights = whole_weights(qkv_weight, up_weight, proj_weight, down_weight)
    arrays = dict(
        lengths=lengths, flags=branches.T, positions=positions, atoms=atom_types, hops=hop_counts.T,
        edges=edge_types.T, kernel_scale=kernel_scale, kernel_shift=kernel_shift, centers=centers, spreads=spreads,
        first_weight=first_weight, first_bias=first_bias, second_weight=second_weight.T, hop_table=hop_table,
        edge_table=edge_table, attn_gain=attn_gain, attn_shift=attn_shift, ffn_gain=ffn_gain, ffn_shift=ffn_shift,
        up_bias=up_bias, down_bias=down_bias, hidden=hidden_in, cotangent=cotangent,
        qkv=weights[0], up=weights[1], proj=weights[2], down=weights[3],
    )
    output, grad_input, sums = layer(remote, arrays)
    if remote:
        fsum, qsum, rows = sums
    else:
        big, rows = sum_grads(*sums)
        fsum, qsum = jnp.zeros((3 * D, HALF_D), bf16), jnp.zeros((D, 3 * HALF_D), bf16)
    output, grad_input, *grads = unpack(output, grad_input, fsum, qsum, rows)
    if not remote:
        grads[2], grads[6], grads[3], grads[8] = big
    grads[2] = grads[2].transpose(1, 0, 2)
    grads[16] = grads[16].T
    return (output, grad_input, *grads)


def solution(mesh):
    rows = P(("mol", "tp"), None)
    all_of = P()
    in_specs = (
        rows, P(None, ("mol", "tp")), P(("mol", "tp")), rows, rows, P("mol"), rows, all_of, all_of,
        P(None, None, "tp"), P("tp", None), all_of, all_of, P(None, "tp"), all_of, P("tp", None),
    ) + (all_of,) * 10 + (rows,)
    out_specs = (
        rows, rows, all_of, all_of, P(None, None, "tp"), P("tp", None), all_of, all_of, P(None, "tp"), all_of,
        P("tp", None),
    ) + (all_of,) * 10
    step = functools.partial(body, dict(mesh.shape))
    return jax.shard_map(step, mesh=mesh, in_specs=in_specs, out_specs=out_specs, check_vma=False)
```

```python
import functools
from types import SimpleNamespace

import jax
import jax.numpy as jnp
from jax import lax
from jax.experimental import pallas as pl
from jax.experimental.pallas import tpu as pltpu
from jax.sharding import PartitionSpec as P

D = 768
H = 32
HD = 24
FF = 768
K = 128
SLOT = 64
HALF = SLOT // 2
HALF_D = D // 2
PAIRS = SLOT * SLOT
HOPS = 16
EDGES = 8
ATOMS = 16
GROUP = 4
GROUPS = H // GROUP
HOT = 32

highest = lax.Precision.HIGHEST
neg_large = -1e30
root_tau = 2.5066282746310002
root_half = 0.7071067811865476
inv_root_tau = 0.3989422804014327
head_scale = HD ** (-0.5)
VMEM_BYTES = 62 * 1024 * 1024
TILE = 256

SECOND_ROWS = K
TABLE_ROWS = SECOND_ROWS + H
KERNEL_ROWS = TABLE_ROWS + H
VECTOR_ROWS = KERNEL_ROWS + 8
SMALL_ROWS = 256

MESH = pl.DeviceIdType.MESH
f32 = jnp.float32
bf16 = jnp.bfloat16


def dot_nn(left, right, precision=None):
    return lax.dot_general(left, right, (((1,), (0,)), ((), ())), precision=precision, preferred_element_type=f32)


def dot_nt(left, right, precision=None):
    return lax.dot_general(left, right, (((1,), (1,)), ((), ())), precision=precision, preferred_element_type=f32)


def dot_tn(left, right, precision=None):
    return lax.dot_general(left, right, (((0,), (0,)), ((), ())), precision=precision, preferred_element_type=f32)


def iota(shape, dim):
    return lax.broadcasted_iota(jnp.int32, shape, dim)


def gelu_parts(values):
    size = jnp.abs(values)
    bell = jnp.exp(values * values * -0.5)
    denominator = 1.0 + (0.3275911 * root_half) * size
    t = pl.reciprocal(denominator, approx=True)
    series = 0.5 * 1.061405429
    for factor in (-1.453152027, 1.421413741, -0.284496736, 0.254829592):
        series = series * t + 0.5 * factor
    tail = series * t * bell
    gelu = jnp.maximum(values, 0.0) - size * tail
    outer = tail - size * (bell * inv_root_tau)
    return gelu, jnp.where(values >= 0.0, 1.0 - outer, outer)


def to_column(row):
    size = row.shape[1]
    same = iota((size, size), 0) == iota((size, size), 1)
    return jnp.sum(jnp.where(same, row, 0.0), axis=1, keepdims=True)


def half_swap(values):
    return pltpu.roll(values, 64, 1)


def low_lanes(rows):
    return iota((rows, 128), 1) < 64


def vmem(count):
    return [pl.BlockSpec(memory_space=pltpu.VMEM)] * count


def row_of(ref):
    return ref[...].reshape(1, ref.shape[0])


def place():
    mol = lax.axis_index("mol")
    return mol % 2, (mol // 2) % 2, mol // 4, lax.axis_index("tp")


def greet(peers):
    barrier = pltpu.get_barrier_semaphore()
    for peer in peers:
        pl.semaphore_signal(barrier, inc=1, device_id=peer, device_id_type=MESH)
    pl.semaphore_wait(barrier, len(peers))


def window(group):
    first = GROUP * HD * group
    start = first // 128 * 128
    width = 128 if first - start + GROUP * HD <= 128 else 256
    return start, width, first - start


def head_masks(group, kind):
    _, width, offset = window(group)
    lane = iota((1, width), 1)
    return [
        ((lane >= offset + HD * h) & (lane < offset + HD * (h + 1))).astype(f32).astype(kind) for h in range(GROUP)
    ]


def spread_heads(values, group):
    return jnp.concatenate([values * mask for mask in head_masks(group, bf16)], axis=0)


def gather_heads(values, group):
    masks = head_masks(group, f32)
    total = values[:SLOT] * masks[0]
    for h in range(1, GROUP):
        total = total + values[SLOT * h : SLOT * (h + 1)] * masks[h]
    return total


def standardize(values):
    centred = values - jnp.mean(values, axis=-1, keepdims=True)
    inv_std = lax.rsqrt(jnp.mean(centred * centred, axis=-1, keepdims=True) + 1e-05)
    return centred * inv_std, inv_std


def norm_back(d_normed, scaled, inv_std, gain):
    weighted = d_normed * gain
    inner_a = jnp.mean(weighted, axis=-1, keepdims=True)
    inner_b = jnp.mean(weighted * scaled, axis=-1, keepdims=True)
    return inv_std * (weighted - inner_a - scaled * inner_b)


def column_sum(values):
    return jnp.sum(values, axis=0, keepdims=True)


class Peers:
    def __init__(self):
        self.core, self.x, self.z, self.tp = place()
        mol = lax.axis_index("mol")
        self.over_core = {"mol": mol + 1 - 2 * self.core}
        self.over_x = {"mol": mol + 2 - 4 * self.x}
        self.over_tp = {"tp": 1 - self.tp}
        self.turn = [lax.rem(self.z + d, 4) for d in range(4)]
        self.over_z = [{"mol": self.turn[d] * 4 + self.x * 2 + self.core} for d in range(4)]

    def neighbour(self, k):
        core = self.core + (1 - 2 * self.core) * (k & 1)
        x = self.x + (1 - 2 * self.x) * (k >> 1 & 1)
        tp = self.tp + (1 - 2 * self.tp) * (k >> 2)
        return core * 4 + tp * 2 + x, {"mol": self.z * 4 + x * 2 + core, "tp": tp}

    def everyone(self):
        return [self.neighbour(k)[1] for k in range(1, 8)] + self.over_z[1:]


def span(start, size):
    return pl.ds(pl.multiple_of(start, size), size)


def add_rows(target, source, rows):
    step = 96 if rows % 96 == 0 else min(rows, 32)

    def piece(i, _):
        at = pl.ds(pl.multiple_of(i * step, step), step)
        target[at, :] = (target[at, :].astype(f32) + source[at, :].astype(f32)).astype(target.dtype)
        return 0

    lax.fori_loop(0, rows // step, piece, 0)


class Reduction:
    kinds = 11

    def __init__(self, peers, part, total, from_core, from_tp, from_x, from_z, sends, recvs):
        self.peers, self.part, self.total = peers, part, total
        self.from_core, self.from_tp, self.from_x, self.from_z = from_core, from_tp, from_x, from_z
        self.sends, self.recvs = sends, recvs
        self.half = from_core.shape[2]
        self.quarter, self.least = self.half // 2, self.half // 8

    def rows(self, b, level):
        p = self.peers
        at = b * 2 * self.half + p.core * self.half
        if level > 0:
            at = at + p.x * self.quarter
        return at + p.z * self.least if level > 1 else at

    def copy(self, b, kind):
        p = self.peers
        part, total = self.part, self.total
        half, quarter, least = self.half, self.quarter, self.least
        if kind == 0:
            src = part.at[:, span(b * 2 * half + (1 - p.core) * half, half)]
            dst, peer = self.from_core.at[b], p.over_core
        elif kind == 1:
            src, dst, peer = part.at[1 - p.tp, span(self.rows(b, 0), half)], self.from_tp.at[b], p.over_tp
        elif kind == 2:
            src = part.at[p.tp, span(self.rows(b, 0) + (1 - p.x) * quarter, quarter)]
            dst, peer = self.from_x.at[b], p.over_x
        elif kind < 6:
            d = kind - 2
            src = part.at[p.tp, span(self.rows(b, 1) + p.turn[d] * least, least)]
            dst, peer = self.from_z.at[b, d - 1], p.over_z[d]
        elif kind < 9:
            src = dst = total.at[span(self.rows(b, 2), least)]
            peer = p.over_z[kind - 5]
        elif kind == 9:
            src = dst = total.at[span(self.rows(b, 1), quarter)]
            peer = p.over_x
        else:
            src = dst = total.at[span(self.rows(b, 0), half)]
            peer = p.over_core
        return pltpu.make_async_remote_copy(
            src_ref=src, dst_ref=dst, send_sem=self.sends.at[b, kind], recv_sem=self.recvs.at[b, kind],
            device_id=peer, device_id_type=MESH,
        )

    def act(self, b, stage):
        p = self.peers
        half, quarter, least = self.half, self.quarter, self.least
        part = self.part
        if stage == 0:
            self.copy(b, 0).start()
        elif stage == 1:
            self.copy(b, 0).wait_recv()
            at = span(self.rows(b, 0), half)
            add_rows(part.at[1 - p.tp, at], self.from_core.at[b, 1 - p.tp], half)
            self.copy(b, 1).start()
            add_rows(part.at[p.tp, at], self.from_core.at[b, p.tp], half)
        elif stage == 2:
            self.copy(b, 1).wait_recv()
            away, mine = (1 - p.x) * quarter, p.x * quarter
            at = self.rows(b, 0)
            add_rows(part.at[p.tp, span(at + away, quarter)], self.from_tp.at[b, span(away, quarter)], quarter)
            self.copy(b, 2).start()
            add_rows(part.at[p.tp, span(at + mine, quarter)], self.from_tp.at[b, span(mine, quarter)], quarter)
        elif stage == 3:
            self.copy(b, 2).wait_recv()
            add_rows(part.at[p.tp, span(self.rows(b, 1), quarter)], self.from_x.at[b], quarter)
            for kind in (3, 4, 5):
                self.copy(b, kind).start()
        elif stage == 4:
            for kind in (3, 4, 5):
                self.copy(b, kind).wait_recv()
            mine = span(self.rows(b, 2), least)
            value = part[p.tp, mine, :].astype(f32)
            for d in range(3):
                value = value + self.from_z[b, d].astype(f32)
            self.total[mine, :] = value.astype(bf16)
            for kind in (6, 7, 8):
                self.copy(b, kind).start()
        elif stage == 5:
            for kind in (6, 7, 8):
                self.copy(b, kind).wait_recv()
            self.copy(b, 9).start()
        elif stage == 6:
            self.copy(b, 9).wait_recv()
            self.copy(b, 10).start()
        elif stage == 7:
            self.copy(b, 10).wait_recv()
        else:
            for kind in range(self.kinds):
                self.copy(b, kind).wait_send()


class SmallReduction:
    def __init__(self, peers, part, total, from_near, from_z, sends, recvs):
        self.peers, self.part, self.total, self.from_near, self.from_z = peers, part, total, from_near, from_z
        self.sends, self.recvs = sends, recvs
        p = peers
        self.near = [p.neighbour(k) for k in range(8)]
        self.at_near = self.near[0][0] * 32

    def copy(self, kind):
        p = self.peers
        part, total = self.part, self.total
        if kind < 7:
            index, peer = self.near[kind + 1]
            src, dst = part.at[span(index * 32, 32)], self.from_near.at[kind]
        elif kind < 10:
            d = kind - 6
            src, dst, peer = part.at[span(self.at_near + p.turn[d] * 8, 8)], self.from_z.at[d - 1], p.over_z[d]
        elif kind < 13:
            src = dst = total.at[span(self.at_near + p.z * 8, 8)]
            peer = p.over_z[kind - 9]
        else:
            src = dst = total.at[span(self.at_near, 32)]
            peer = self.near[kind - 12][1]
        return pltpu.make_async_remote_copy(
            src_ref=src, dst_ref=dst, send_sem=self.sends.at[kind], recv_sem=self.recvs.at[kind],
            device_id=peer, device_id_type=MESH,
        )

    def act(self, stage):
        p = self.peers
        hops = (range(0, 7), range(7, 10), range(10, 13), range(13, 20))
        if stage == 5:
            for kind in range(20):
                self.copy(kind).wait_send()
            return
        if stage > 0:
            for kind in hops[stage - 1]:
                self.copy(kind).wait_recv()
        if stage == 1:
            mine = span(self.at_near, 32)
            value = self.part[mine, :]
            for k in range(7):
                value = value + self.from_near[k]
            self.part[mine, :] = value
        elif stage == 2:
            mine = span(self.at_near + p.z * 8, 8)
            self.total[mine, :] = self.part[mine, :] + self.from_z[0] + self.from_z[1] + self.from_z[2]
        if stage < 4:
            for kind in hops[stage]:
                self.copy(kind).start()


def big_scratch(rows, lanes):
    half = rows // 2
    sems = pltpu.SemaphoreType.DMA((3, Reduction.kinds))
    return [
        pltpu.VMEM((3, 2, half, lanes), bf16), pltpu.VMEM((3, half, lanes), bf16),
        pltpu.VMEM((3, half // 2, lanes), bf16), pltpu.VMEM((3, 3, half // 8, lanes), bf16), sems, sems,
    ]


def small_scratch():
    return [
        pltpu.VMEM((7, 32, 128), f32), pltpu.VMEM((3, 8, 128), f32),
        pltpu.SemaphoreType.DMA((20,)), pltpu.SemaphoreType.DMA((20,)),
    ]


class Gather:
    pieces = 6

    def __init__(self, peers, whole, sends, recvs):
        self.peers, self.whole, self.sends, self.recvs = peers, whole, sends, recvs
        self.quarter = peers.x * 2 + peers.core
        self.next_quarter = (1 - peers.x) * 2 + peers.core

    def rows(self, ref, quarter):
        count = ref.shape[0] // 4
        return ref.at[span(quarter * count, count), :]

    def copy(self, index, kind):
        p = self.peers
        if kind == 0:
            src = dst = self.rows(self.whole(index, p.tp), self.quarter)
            peer = p.over_tp
        elif kind == 1:
            src = dst = self.rows(self.whole(index, 1 - p.tp), self.quarter)
            peer = p.over_x
        else:
            src = dst = self.rows(self.whole(index, 1 - p.tp), self.quarter if kind == 2 else self.next_quarter)
            peer = p.over_core
        return pltpu.make_async_remote_copy(
            src_ref=src, dst_ref=dst, send_sem=self.sends.at[index, kind], recv_sem=self.recvs.at[index, kind],
            device_id=peer, device_id_type=MESH,
        )

    def start(self, indices):
        for index in indices:
            self.copy(index, 0).start()

    def onward_x(self, index):
        self.copy(index, 0).wait_recv()
        self.copy(index, 1).start()
        self.copy(index, 2).start()

    def onward_core(self, index):
        self.copy(index, 1).wait_recv()
        self.copy(index, 3).start()

    def arrive(self, index):
        self.copy(index, 2).wait_recv()
        self.copy(index, 3).wait_recv()

    def finish(self):
        for index in range(self.pieces):
            for kind in range(4):
                self.copy(index, kind).wait_send()


def square_turn(values):
    rows, lanes = values.shape
    if lanes < 128:
        values = jnp.concatenate([values, jnp.zeros((rows, 128 - lanes), f32)], axis=1)
    if rows < 128:
        values = jnp.concatenate([values, jnp.zeros((128 - rows, 128), f32)], axis=0)
    return values.T


def widen(values):
    return jnp.concatenate([values] * (TILE // 128), axis=1)


def strips():
    return [slice(16 * i, 16 * (i + 1)) for i in range(K // 16)]


def four_rows(ref, slot, first):
    return jnp.concatenate([ref[slot, pl.ds(first + i, 1), :] for i in range(TILE // 128)], axis=1)


def hot_rows(values, count):
    return (values == iota((count, TILE), 0).astype(f32)).astype(f32)


def fold_lanes(values):
    total = values[:, :128]
    for i in range(1, TILE // 128):
        total = total + values[:, 128 * i : 128 * (i + 1)]
    return total


def prepare_pairs(r):
    spr = to_column(row_of(r.spreads))
    r.cols[0] = jnp.broadcast_to(to_column(row_of(r.centers)), (K, 128))
    r.cols[1] = jnp.broadcast_to(root_half / spr, (K, 128))
    r.cols[2] = jnp.broadcast_to(-jnp.log(root_tau * spr), (K, 128))
    r.cols[3] = jnp.broadcast_to(to_column(row_of(r.first_bias)), (K, 128))
    r.cols[4] = jnp.broadcast_to(1.0 / spr, (K, 128))
    r.w1t[...] = r.first_weight[...].astype(f32).T.astype(bf16)
    r.w2[...] = square_turn(r.second_weight[...].astype(f32)).astype(bf16)
    table = jnp.concatenate([r.hop_table[...], r.edge_table[...], jnp.zeros((128 - HOPS - EDGES, H), f32)], axis=0)
    table = jnp.concatenate([table, jnp.zeros((128, 128 - H), f32)], axis=1).T[:H, :HOT]
    one = table.astype(bf16).astype(f32)
    r.base[...] = jnp.concatenate(
        [r.second_weight[...].astype(f32), one, table - one, jnp.zeros((H, 64), f32)], axis=1
    )


def bf16_parts(values, count):
    parts = []
    for _ in range(count):
        parts.append(values.astype(bf16))
        values = values - parts[-1].astype(f32)
    return parts


def pair_tables(r, slots):
    low = low_lanes(HALF)
    low_row = low_lanes(1)
    tables = [part.astype(f32) for ref in (r.kernel_scale, r.kernel_shift) for part in bf16_parts(ref[...], 3)]
    tables = jnp.concatenate([square_turn(part)[:ATOMS, :ATOMS] for part in tables], axis=1)
    tables = jnp.concatenate([tables, jnp.zeros((ATOMS, 128 - 6 * ATOMS), f32)], axis=1).astype(bf16)
    for group in range(slots // 2):
        lanes = slice(128 * group, 128 * (group + 1))
        atoms = r.atoms[lanes].astype(f32).reshape(1, 128)
        rows = jnp.concatenate([r.positions[:, lanes], atoms, jnp.zeros((4, 128), f32)], axis=0)
        columns = square_turn(rows)
        key_hot = (columns[:, 3:4] == iota((128, ATOMS), 1).astype(f32)).astype(f32).astype(bf16)
        picks = dot_nn(key_hot, tables).astype(bf16)
        turned = half_swap(rows)
        for s in range(2):
            slot = 2 * group + s
            tokens = slice(SLOT * s, SLOT * (s + 1))
            double = jnp.where(low_lanes(8), *((rows, turned) if s == 0 else (turned, rows)))
            total = None
            for c in range(3):
                column = columns[tokens, c : c + 1]
                offset = jnp.where(low, column[:HALF], column[HALF:]) - double[c : c + 1]
                total = offset * offset if total is None else total + offset * offset
            distance = jnp.sqrt(total)
            query_hot = (double[3:4] == iota((ATOMS, 128), 0).astype(f32)).astype(f32)
            three, none = [query_hot] * 3, [jnp.zeros((3 * ATOMS, 128), f32)]
            rest = [jnp.zeros((128 - 6 * ATOMS, 128), f32)]
            spread = jnp.concatenate(
                [jnp.concatenate(three + none + rest, axis=0), jnp.concatenate(none + three + rest, axis=0)], axis=1
            )
            both = dot_nn(picks[tokens], spread.astype(bf16))
            scale = jnp.where(low, both[:HALF, :128], both[HALF:, :128])
            shift = jnp.where(low, both[:HALF, 128:], both[HALF:, 128:])
            r.argument[slot] = scale * distance + shift
            r.distance[slot] = distance
            for source, target in ((r.hops, r.hop_rows), (r.edges, r.edge_rows)):
                values = source[:, lanes].astype(f32)
                top, bottom = values[:HALF], values[HALF:]
                if s == 0:
                    target[slot] = jnp.where(low, top, half_swap(bottom))
                else:
                    target[slot] = jnp.where(low, half_swap(top), bottom)
            r.atom_rows[slot] = jnp.broadcast_to(double[3:4], (8, 128))


def table_grads(r, slots):
    lefts, rights = [], []
    for slot in range(slots):
        query_hot = (r.atom_rows[slot, 0:1, :] == iota((ATOMS, 128), 0).astype(f32)).astype(f32)
        keys = jnp.concatenate([query_hot[:, :HALF], query_hot[:, HALF:SLOT]], axis=0)
        keys = jnp.concatenate([keys, keys], axis=1).astype(bf16)
        values = jnp.concatenate([r.dargs[slot] * r.distance[slot], r.dargs[slot]], axis=1)
        both = dot_nn(keys, jnp.concatenate(bf16_parts(values, 2), axis=0))
        low = low_lanes(ATOMS)
        for index in range(2):
            lanes = slice(128 * index, 128 * (index + 1))
            rights.append(bf16_parts(jnp.where(low, both[:ATOMS, lanes], both[ATOMS:, lanes]), 2))
        lefts.append(query_hot.astype(bf16))
    left = jnp.concatenate(lefts, axis=1)
    right = jnp.concatenate(
        [jnp.concatenate([rights[2 * s + index][part] for s in range(slots)], axis=1) for index in range(2) for part in range(2)],
        axis=0,
    )
    result = dot_nt(left, right)
    return [
        result[:, 2 * ATOMS * index : 2 * ATOMS * index + ATOMS] + result[:, 2 * ATOMS * index + ATOMS : 2 * ATOMS * (index + 1)]
        for index in range(2)
    ]


def in_stages(stages, count):
    held = {}
    for time in range(count + len(stages) - 1):
        for k, stage in reversed(list(enumerate(stages))):
            if 0 <= time - k < count:
                held[time - k] = stage(time - k, held.get(time - k))


TILES = PAIRS // TILE
ROWS = TILE // 128


def pair_forward(r, slot):
    bank = lax.rem(slot, 2)
    graph_on = r.flags[0, slot].astype(f32)
    space_on = r.flags[1, slot].astype(f32)
    factor = jnp.where(iota((H, 256), 1) < K, space_on, graph_on)
    r.lhs[...] = (r.base[...] * factor).astype(bf16)

    def kernels(tile, _):
        where = slice(tile * TILE, (tile + 1) * TILE)
        arg = four_rows(r.argument, slot, tile * ROWS)
        pieces = []
        for rows in strips():
            u = (arg - widen(r.cols[0, rows])) * widen(r.cols[1, rows])
            pieces.append(jnp.exp(widen(r.cols[2, rows]) - u * u).astype(bf16))
            r.left[bank, rows, where] = pieces[-1]
        return dot_nn(r.w1t[...], jnp.concatenate(pieces, axis=0))

    def hidden(tile, first):
        where = slice(tile * TILE, (tile + 1) * TILE)
        pieces = []
        for rows in strips():
            value, slope = gelu_parts(first[rows] + widen(r.cols[3, rows]))
            pieces.append(value.astype(bf16))
            r.left[bank, slice(K + rows.start, K + rows.stop), where] = pieces[-1]
            r.slope[bank, rows, where] = slope.astype(bf16)
        hot = jnp.concatenate(
            [
                hot_rows(four_rows(r.hop_rows, slot, tile * ROWS), HOPS),
                hot_rows(four_rows(r.edge_rows, slot, tile * ROWS), HOT - HOPS),
            ],
            axis=0,
        ).astype(bf16)
        return dot_nn(r.lhs[:, : K + 2 * HOT], jnp.concatenate(pieces + [hot] * 2, axis=0))

    def biases(tile, bias):
        bias = bias.astype(bf16).astype(f32)
        for i in range(ROWS):
            r.bias[slot, pl.ds(tile * ROWS + i, H, stride=HALF), :] = bias[:, 128 * i : 128 * (i + 1)]

    in_stages([kernels, hidden, biases], TILES)


def pair_backward(r, slot, between):
    bank = lax.rem(slot, 2)
    graph_on = r.flags[0, slot].astype(f32)
    space_on = r.flags[1, slot].astype(f32)
    w2 = r.w2[:, :H] * space_on.astype(bf16)

    def scores(tile, _):
        where = slice(tile * TILE, (tile + 1) * TILE)
        grad = jnp.concatenate(
            [r.bias[slot, pl.ds(tile * ROWS + i, H, stride=HALF), :] for i in range(ROWS)], axis=1
        )
        r.right[K:, where] = jnp.concatenate([grad * space_on, grad * graph_on], axis=0).astype(bf16)
        edge_hot = hot_rows(four_rows(r.edge_rows, slot, tile * ROWS), HOT - HOPS)
        edge_hot = jnp.where(iota((HOT - HOPS, TILE), 0) == EDGES, 1.0, edge_hot)
        r.left[bank, 2 * K :, where] = jnp.concatenate(
            [hot_rows(four_rows(r.hop_rows, slot, tile * ROWS), HOPS), edge_hot], axis=0
        ).astype(bf16)
        return dot_nn(w2, grad.astype(bf16))

    def hidden(tile, d_second):
        where = slice(tile * TILE, (tile + 1) * TILE)
        pieces = []
        for rows in strips():
            pieces.append((d_second[rows] * r.slope[bank, rows, where].astype(f32)).astype(bf16))
            r.right[rows, where] = pieces[-1]
        return dot_nn(r.first_weight[...], jnp.concatenate(pieces, axis=0))

    def kernels(tile, d_gauss):
        where = slice(tile * TILE, (tile + 1) * TILE)
        arg = four_rows(r.argument, slot, tile * ROWS)
        d_arg = None
        for rows in strips():
            inv = widen(r.cols[4, rows])
            u = (arg - widen(r.cols[0, rows])) * inv
            q = d_gauss[rows] * r.left[bank, rows, where].astype(f32)
            w = q * u
            r.sums[0, rows] += fold_lanes(w)
            r.sums[1, rows] += fold_lanes(w * u - q)
            w = w * inv
            w = w[:8] + w[8:]
            d_arg = w if d_arg is None else d_arg + w
        d_arg = -jnp.sum(d_arg, axis=0, keepdims=True)
        for i in range(ROWS):
            at = tile * ROWS + i
            r.dargs[slot, at : at + 1, :] = d_arg[:, 128 * i : 128 * (i + 1)]

    in_stages([scores, hidden, kernels], TILES)
    between()
    r.acc_mixed[...] += dot_nt(r.left[bank], r.right[...])


def attend(r, s, first_slot):
    low = low_lanes(HALF)
    rows = span(s * SLOT, SLOT)
    valid = iota((SLOT, GROUP * SLOT), 0) < r.lengths[first_slot + s]
    r.work[0] = jnp.zeros((SLOT, D), f32)
    for g in range(GROUPS):
        start, width, _ = window(g)
        q = r.joined[rows, start : start + width]
        k = r.joined[rows, D + start : D + start + width]
        v = r.joined[rows, 2 * D + start : 2 * D + start + width]
        scores = dot_nt(k, spread_heads(q, g)) * head_scale
        parts = []
        for pair in range(GROUP // 2):
            head = GROUP * g + 2 * pair
            one = r.bias[s, head * HALF : (head + 1) * HALF, :]
            two = r.bias[s, (head + 1) * HALF : (head + 2) * HALF, :]
            top = jnp.where(low, one, half_swap(two))
            bottom = jnp.where(low, half_swap(one), two)
            parts.append(jnp.concatenate([top, bottom], axis=0))
        scores = jnp.where(valid, scores + jnp.concatenate(parts, axis=1), neg_large)
        weights = jnp.exp(scores - jnp.max(scores, axis=0, keepdims=True))
        prob = (weights * (1.0 / jnp.sum(weights, axis=0, keepdims=True))).astype(bf16)
        r.prob[s, :, g * GROUP * SLOT : (g + 1) * GROUP * SLOT] = prob
        r.work[0, :, start : start + width] += gather_heads(dot_tn(prob, v), g)
    r.attended[rows, :] = r.work[0].astype(bf16)


def attend_back(r, s):
    low = low_lanes(HALF)
    rows = span(s * SLOT, SLOT)
    r.work[...] = jnp.zeros((3, SLOT, D), f32)
    for g in range(GROUPS):
        start, width, _ = window(g)
        lanes = slice(start, start + width)
        k = r.joined[rows, D + start : D + start + width]
        v = r.joined[rows, 2 * D + start : 2 * D + start + width]
        q_heads = spread_heads(r.joined[rows, lanes], g)
        d_heads = spread_heads(r.d_attended[rows, lanes], g)
        prob = r.prob[s, :, g * GROUP * SLOT : (g + 1) * GROUP * SLOT]
        wide = prob.astype(f32)
        d_prob = dot_nt(v, d_heads)
        inner = jnp.sum(wide * d_prob, axis=0, keepdims=True)
        d_scores = (wide * (d_prob - inner)).astype(bf16)
        r.work[0, :, lanes] += gather_heads(dot_tn(d_scores, k), g)
        r.work[1, :, lanes] += dot_nn(d_scores, q_heads)
        r.work[2, :, lanes] += dot_nn(prob, d_heads)
        d_wide = d_scores.astype(f32)
        for pair in range(GROUP // 2):
            head = GROUP * g + 2 * pair
            top = d_wide[:HALF, 128 * pair : 128 * (pair + 1)]
            bottom = d_wide[HALF:, 128 * pair : 128 * (pair + 1)]
            r.bias[s, head * HALF : (head + 1) * HALF, :] = jnp.where(low, top, half_swap(bottom))
            r.bias[s, (head + 1) * HALF : (head + 2) * HALF, :] = jnp.where(low, half_swap(top), bottom)
    r.joined[rows, 0:D] = (r.work[0] * head_scale).astype(bf16)
    r.joined[rows, D : 2 * D] = (r.work[1] * head_scale).astype(bf16)
    r.joined[rows, 2 * D : 3 * D] = r.work[2].astype(bf16)


def project(r, rows):
    scaled, _ = standardize(r.hidden[rows, :].astype(f32))
    normed = (scaled * row_of(r.attn_gain) + row_of(r.attn_shift)).astype(bf16)
    r.normed_a[rows, :] = normed
    for m in range(3):
        for t in range(2):
            at = m * D + t * HALF_D
            r.joined[rows, at : at + HALF_D] = dot_nn(normed, r.wqkv[t, m]).astype(bf16)


def feed(r, rows):
    halves = [slice(0, HALF_D), slice(HALF_D, D)]
    resid = r.hidden[rows, :].astype(f32)
    for t in range(2):
        resid = resid + dot_nn(r.attended[rows, halves[t]], r.wproj[t])
    scaled, inv_std = standardize(resid)
    normed = (scaled * row_of(r.ffn_gain) + row_of(r.ffn_shift)).astype(bf16)
    r.normed_f[rows, :] = normed
    pre = jnp.concatenate([dot_nn(normed, r.wup[t]) for t in range(2)], axis=1)
    value, slope = gelu_parts(pre + row_of(r.up_bias))
    active = value.astype(bf16)
    r.activated[rows, :] = active
    result = resid + row_of(r.down_bias)
    for t in range(2):
        result = result + dot_nn(active[:, halves[t]], r.wdown[t])
    r.out_rows[rows, :] = result.astype(bf16)
    cot = r.cotangent[rows, :]
    cot_wide = cot.astype(f32)
    d_active = jnp.concatenate([dot_nt(cot, r.wdown[t]) for t in range(2)], axis=1)
    d_hidden = (d_active * slope).astype(bf16)
    r.d_pre[rows, :] = d_hidden
    d_normed = dot_nt(d_hidden[:, halves[0]], r.wup[0]) + dot_nt(d_hidden[:, halves[1]], r.wup[1])
    d_resid = cot_wide + norm_back(d_normed, scaled, inv_std, row_of(r.ffn_gain))
    r.d_resid[rows, :] = d_resid
    branch = d_resid.astype(bf16)
    r.d_branch[rows, :] = branch
    for t in range(2):
        r.d_attended[rows, halves[t]] = dot_nt(branch, r.wproj[t]).astype(bf16)
    r.vectors[2:3, :] += column_sum(d_normed * scaled)
    r.vectors[3:4, :] += column_sum(d_normed)
    r.vectors[4:5, :] += column_sum(d_hidden.astype(f32))
    r.vectors[5:6, :] += column_sum(cot_wide)


def feed_grads(r, block):
    halves = [slice(0, HALF_D), slice(HALF_D, D)]
    if block == 0:
        grad = dot_tn(r.normed_f[...], r.d_pre[...]).astype(bf16)
        for t in range(2):
            r.fpart[t, :D, :] = grad[:, halves[t]]
        return
    left, right = (r.attended, r.d_branch) if block == 1 else (r.activated, r.cotangent)
    for t in range(2):
        grad = dot_tn(left[:, halves[t]], right[...]).astype(bf16)
        for side in range(2):
            r.fpart[t, D * block + HALF_D * side : D * block + HALF_D * (side + 1), :] = grad[:, halves[side]]


def qkv_grads(r, block):
    rows = slice(256 * block, 256 * (block + 1))
    for m in range(3):
        grad = dot_tn(r.normed_a[:, rows], r.joined[:, m * D : (m + 1) * D]).astype(bf16)
        for t in range(2):
            r.qpart[t, rows, m * HALF_D : (m + 1) * HALF_D] = grad[:, t * HALF_D : (t + 1) * HALF_D]


def finish_input(r, rows):
    d_normed = None
    for m in range(3):
        for t in range(2):
            at = m * D + t * HALF_D
            term = dot_nt(r.joined[rows, at : at + HALF_D], r.wqkv[t, m])
            d_normed = term if d_normed is None else d_normed + term
    scaled, inv_std = standardize(r.hidden[rows, :].astype(f32))
    grad = r.d_resid[rows, :] + norm_back(d_normed, scaled, inv_std, row_of(r.attn_gain))
    r.in_rows[rows, :] = grad.astype(bf16)
    r.vectors[0:1, :] += column_sum(d_normed * scaled)
    r.vectors[1:2, :] += column_sum(d_normed)


def pack_small(r, slots):
    tables = table_grads(r, slots)
    for v in range(6):
        for i in range(D // 128):
            at = VECTOR_ROWS + v * (D // 128) + i
            r.spart[at : at + 1, :] = r.vectors[v : v + 1, 128 * i : 128 * (i + 1)]
    r.spart[0:K, :] = r.acc_mixed[0:K, :K]
    r.spart[SECOND_ROWS : SECOND_ROWS + H, :] = square_turn(r.acc_mixed[K : 2 * K, K:])[:H]
    r.spart[TABLE_ROWS : TABLE_ROWS + H, :HOT] = square_turn(r.acc_mixed[2 * K :, K:])[H : 2 * H, :HOT]
    for index in range(2):
        rows = slice(TABLE_ROWS + ATOMS * index, TABLE_ROWS + ATOMS * (index + 1))
        r.spart[rows, HOT : HOT + ATOMS] = tables[index]
    ones = 2 * K + HOPS + EDGES
    r.spart[KERNEL_ROWS : KERNEL_ROWS + 1, :] = r.acc_mixed[ones : ones + 1, :K]
    for index in range(2):
        column = jnp.sum(r.sums[index] * r.cols[4], axis=1, keepdims=True)
        same = iota((K, K), 0) == iota((K, K), 1)
        at = KERNEL_ROWS + 1 + index
        r.spart[at : at + 1, :] = jnp.sum(jnp.where(same, column, 0.0), axis=0, keepdims=True)


class Stage:
    def __init__(self, names, near_inputs, carried, refs):
        self.r = SimpleNamespace(**dict(zip(names, refs)))
        r = self.r
        self.loads = {
            name: pltpu.make_async_copy(getattr(r, "given_" + name), getattr(r, name), r.input_sems.at[i])
            for i, name in enumerate(near_inputs)
        }
        self.stores = {
            name: pltpu.make_async_copy(getattr(r, name), getattr(r, name + "_far"), r.carry_sems.at[i])
            for i, name in enumerate(carried)
        }

    def load(self, *names):
        for name in names:
            self.loads[name].start()

    def need(self, *names):
        for name in names:
            self.loads[name].wait()

    def store(self, *names):
        for name in names:
            self.stores[name].start()

    def stored(self):
        for copy in self.stores.values():
            copy.wait()


def each_chunk(r, tokens, work):
    chunk = min(256, tokens)

    def one(c, _):
        work(r, span(c * chunk, chunk))
        return 0

    lax.fori_loop(0, tokens // chunk, one, 0)


def pair_moves(r, slot, back):
    bank = lax.rem(slot, 2)
    both = (r.left_far.at[slot], r.left.at[bank, : 2 * K]), (r.slope_far.at[slot], r.slope.at[bank])
    for index, (far, near) in enumerate(both):
        yield pltpu.make_async_copy(*((far, near) if back else (near, far)), r.pair_sems.at[bank, index])


def start_moves(r, slot, back):
    for copy in pair_moves(r, slot, back):
        copy.start()


def wait_moves(r, slot, back):
    for copy in pair_moves(r, slot, back):
        copy.wait()


def run(steps):
    for act, *where in steps:
        act(*where)


def at_time(index, plan):
    for k, steps in plan.items():
        pl.when(index == k)(functools.partial(run, steps))


FFN_BACK = {0: [(1, 1), (2, 1)], 3: [(0, 2)], 7: [(0, 3), (1, 2)]}
AFTER_GRADS = ([(0, 4), (1, 3), (2, 2)], [(0, 1), (1, 1), (2, 1)])
AFTER_HALF = ([(0, 5)], [])
AFTER_INPUT = ([(2, 3), (1, 4)], [(0, 2)])
FFN_PAIRS = {
    0: [(0, 6)], 2: [(2, 4)], 3: [(1, 5), (0, 7)], 5: [(2, 5)], 7: [(1, 6)], 9: [(2, 6)], 10: [(1, 7)], 12: [(2, 7)],
}
QKV_PAIRS = {
    2: [(0, 3)], 3: [(1, 2)], 6: [(1, 3), (2, 2), (0, 4)], 9: [(1, 4)], 10: [(0, 5)], 11: [(2, 3)], 12: [(1, 5)],
    13: [(0, 6)], 14: [(2, 4)], 15: [(1, 6)],
}


def layer_kernel(remote, names, near_inputs, carried, *refs):
    stage = Stage(names, near_inputs, carried, refs)
    r = stage.r
    stage.load(*[name for name in near_inputs if name not in ("hidden", "cotangent")])
    tokens = r.hidden.shape[0]
    slots = tokens // SLOT
    peers = Peers()
    whole = [r.wqkv, r.wup, r.wproj, r.wdown]
    given = [r.given_qkv, r.given_up, r.given_proj, r.given_down]
    targets = [w.at[peers.tp] for w in whole] if remote else whole
    loads = [
        pltpu.make_async_copy(src, dst, r.load_sems.at[i]) for i, (src, dst) in enumerate(zip(given, targets))
    ]
    for load in loads:
        load.start()
    stage.load("hidden", "cotangent")
    gather_plan = {}
    if remote:

        def whole_piece(index, tp):
            return whole[0].at[tp, index] if index < 3 else whole[index - 2].at[tp]

        gather = Gather(peers, whole_piece, r.gather_sends, r.gather_recvs)
        ffn = Reduction(peers, r.fpart, r.ftotal, r.f_core, r.f_tp, r.f_x, r.f_z, r.f_sends, r.f_recvs)
        qkv = Reduction(peers, r.qpart, r.qtotal, r.q_core, r.q_tp, r.q_x, r.q_z, r.q_sends, r.q_recvs)
        small = SmallReduction(peers, r.spart, r.stotal, r.s_near, r.s_z, r.s_sends, r.s_recvs)
        greet(peers.everyone())
        for load, indices in zip(loads, ((0, 1, 2), (3,), (4,), (5,))):
            load.wait()
            gather.start(indices)
        x, core = gather.onward_x, gather.onward_core
        gather_plan = {
            0: [(x, 0)], 1: [(x, 1), (core, 0)], 2: [(x, 2), (core, 1)], 3: [(x, 3), (core, 2)],
            4: [(x, 4), (core, 3), (x, 5)], 5: [(core, 4)], 6: [(core, 5)],
        }

    def leave(which, block):
        near, far = ((r.ftotal, r.ftotal_far), (r.qtotal, r.qtotal_far))[which]
        rows = near.shape[0] // 3
        at = slice(block * rows, (block + 1) * rows)
        return pltpu.make_async_copy(near.at[at], far.at[at], r.leave_sems.at[3 * which + block])

    def advance(which, actions):
        if remote:
            for block, step in actions:
                (ffn, qkv)[which].act(block, step)
                if step == 7:
                    leave(which, block).start()

    def plan_of(*plans):
        times = sorted(set().union(*plans)) if remote else []
        return {
            k: [(advance, which, plan[k]) for which, plan in enumerate(plans) if k in plan] for k in times
        }

    stage.need(*[name for name in near_inputs if name not in ("hidden", "cotangent")])
    prepare_pairs(r)
    pair_tables(r, slots)

    def pairs(slot, _):
        pl.when(slot >= 2)(lambda: wait_moves(r, slot - 2, False))
        pair_forward(r, slot)
        start_moves(r, slot, False)
        at_time(slot, gather_plan)
        return 0

    lax.fori_loop(0, slots, pairs, 0)
    stage.need("hidden")
    if remote:
        for index in range(3):
            gather.arrive(index)
    else:
        for load in loads:
            load.wait()
    each_chunk(r, tokens, project)
    first_slot = peers.tp * slots

    def attend_one(s, _):
        attend(r, s, first_slot)
        return 0

    lax.fori_loop(0, slots, attend_one, 0)
    stage.need("cotangent")
    if remote:
        for index in range(3, 6):
            gather.arrive(index)
    r.vectors[...] = jnp.zeros_like(r.vectors)
    each_chunk(r, tokens, feed)
    stage.store("out_rows")
    for slot in (slots - 2, slots - 1):
        wait_moves(r, slot, False)
    start_moves(r, 0, True)
    start_moves(r, 1, True)
    for block in range(3):
        feed_grads(r, block)
        advance(0, [(block, 0)])
    advance(0, [(0, 1)])

    back_plan, pair_plan = plan_of(FFN_BACK), plan_of(FFN_PAIRS, QKV_PAIRS)

    def back_one(s, _):
        attend_back(r, s)
        at_time(s, back_plan)
        return 0

    lax.fori_loop(0, slots, back_one, 0)
    for block in range(3):
        qkv_grads(r, block)
        advance(1, [(block, 0)])
    for which in range(2):
        advance(which, AFTER_GRADS[which])
    each_chunk(r, tokens, finish_input)
    stage.store("in_rows")
    for which in range(2):
        advance(which, AFTER_HALF[which] + AFTER_INPUT[which])
    for ref in (r.sums, r.acc_mixed, r.spart):
        ref[...] = jnp.zeros_like(ref)

    def pairs_back(slot, _):
        wait_moves(r, slot, True)
        pair_backward(r, slot, lambda: at_time(2 * slot, pair_plan))
        pl.when(slot + 2 < slots)(lambda: start_moves(r, slot + 2, True))
        at_time(2 * slot + 1, pair_plan)
        return 0

    lax.fori_loop(0, slots, pairs_back, 0)
    pack_small(r, slots)
    if remote:
        small.act(0)
        advance(1, [(2, 5), (0, 7)])
        small.act(1)
        advance(1, [(1, 7)])
        small.act(2)
        advance(1, [(2, 6)])
        small.act(3)
        advance(1, [(2, 7)])
        small.act(4)
        rows = pltpu.make_async_copy(r.stotal, r.stotal_far, r.leave_sems.at[6])
        rows.start()
        for which in range(2):
            advance(which, [(b, 8) for b in range(3)])
        small.act(5)
        gather.finish()
        for which in range(2):
            for block in range(3):
                leave(which, block).wait()
        rows.wait()
    else:
        stage.store("fpart", "qpart", "spart")
    stage.stored()


def call_stage(kernel, name, remote, collective, arrays, scalars, far, outs, carried, scratch):
    vm, sem = pltpu.VMEM, pltpu.SemaphoreType.DMA
    near = {n: vm(a.shape, a.dtype) for n, a in arrays.items() if n not in scalars + far}
    in_names = [n if n in scalars or n.endswith("_far") else "given_" + n for n in arrays]
    results = outs | {n + "_far": item for n, item in carried.items()}
    scratch = near | {n: vm(*item) for n, item in carried.items()} | scratch
    scratch |= {"input_sems": sem((len(near),)), "carry_sems": sem((len(carried),))}
    names = in_names + list(results) + list(scratch)
    values = pl.pallas_call(
        functools.partial(kernel, remote, names, list(near), list(carried)),
        in_specs=[pl.BlockSpec(memory_space=pltpu.SMEM if n in scalars else pl.ANY) for n in arrays],
        out_specs=[pl.BlockSpec(memory_space=pl.ANY)] * len(results),
        out_shape=[jax.ShapeDtypeStruct(*item) for item in results.values()],
        scratch_shapes=list(scratch.values()),
        compiler_params=pltpu.CompilerParams(
            vmem_limit_bytes=VMEM_BYTES, **(dict(collective_id=collective, has_side_effects=True) if remote else {})
        ),
        name=name,
    )(*arrays.values())
    return dict(zip(results, values))


def layer(remote, arrays):
    tokens = arrays["hidden"].shape[0]
    slots = tokens // SLOT
    v, sem = pltpu.VMEM, pltpu.SemaphoreType.DMA
    of_tokens = (tokens, D)
    table = (slots, HALF, 128)
    fshape, qshape, sshape = (3 * D, HALF_D), (D, 3 * HALF_D), (SMALL_ROWS, 128)
    outs = {"left_far": ((slots, 2 * K, PAIRS), bf16), "slope_far": ((slots, K, PAIRS), bf16)}
    carried = {"out_rows": (of_tokens, bf16), "in_rows": (of_tokens, bf16)}
    scratch = {
        "wqkv": v((2, 3, D, HALF_D), bf16), "wup": v((2, D, HALF_D), bf16), "wproj": v((2, HALF_D, D), bf16),
        "wdown": v((2, HALF_D, D), bf16), "load_sems": sem((4,)), "pair_sems": sem((2, 2)),
        "left": v((2, 2 * K + HOT, PAIRS), bf16), "slope": v((2, K, PAIRS), bf16),
        "right": v((K + 2 * H, PAIRS), bf16), "cols": v((5, K, 128), f32), "w1t": v((K, K), bf16),
        "w2": v((K, 128), bf16), "base": v((H, 256), f32), "lhs": v((H, 256), bf16),
        "argument": v(table, f32), "distance": v(table, f32), "hop_rows": v(table, f32), "edge_rows": v(table, f32),
        "atom_rows": v((slots, 8, 128), f32), "dargs": v(table, f32), "bias": v((slots, H * HALF, 128), f32),
        "work": v((3, SLOT, D), f32), "normed_a": v(of_tokens, bf16), "joined": v((tokens, 3 * D), bf16),
        "prob": v((slots, SLOT, H * SLOT), bf16), "attended": v(of_tokens, bf16), "normed_f": v(of_tokens, bf16),
        "activated": v(of_tokens, bf16), "d_pre": v(of_tokens, bf16), "d_branch": v(of_tokens, bf16),
        "d_attended": v(of_tokens, bf16), "d_resid": v(of_tokens, f32), "vectors": v((8, D), f32),
        "sums": v((2, K, 128), f32), "acc_mixed": v((2 * K + HOT, K + 2 * H), f32),
    }
    parts = {"fpart": ((2,) + fshape, bf16), "qpart": ((2,) + qshape, bf16), "spart": (sshape, f32)}
    totals = {"ftotal": (fshape, bf16), "qtotal": (qshape, bf16), "stotal": (sshape, f32)}
    if remote:
        outs |= {n + "_far": item for n, item in totals.items()}
        scratch |= {n: v(*item) for n, item in (parts | totals).items()}
        scratch |= {"leave_sems": sem((7,)), "gather_sends": sem((6, 4)), "gather_recvs": sem((6, 4))}
        for name, shape in (("f", (D, HALF_D)), ("q", (D // 3, 3 * HALF_D))):
            keys = ("_core", "_tp", "_x", "_z", "_sends", "_recvs")
            scratch |= {name + key: item for key, item in zip(keys, big_scratch(*shape))}
        scratch |= dict(zip(("s_near", "s_z", "s_sends", "s_recvs"), small_scratch()))
    else:
        carried |= parts
    results = call_stage(
        layer_kernel, "layer", remote, 0, arrays, ("lengths", "flags"), ("qkv", "up", "proj", "down"), outs, carried,
        scratch,
    )
    sums = [results[n + "_far"] for n in (totals if remote else parts)]
    return results["out_rows_far"], results["in_rows_far"], sums


def unpack_kernel(
    qsum, up_sum, proj_low, proj_high, down_low, down_high, out_rows, in_rows, rows_ref,
    output, grad_input, again, ashift, qkv, proj, fgain, fshift, up, up_bias, down, down_bias, scale, shift, centers,
    spreads, first, first_bias, second, hop, edge,
):
    output[...] = out_rows[...]
    grad_input[...] = in_rows[...]
    for m in range(3):
        qkv[m] = qsum[:, m * HALF_D : (m + 1) * HALF_D].astype(f32)
    up[...] = up_sum[...].astype(f32)
    for low, high, ref in ((proj_low, proj_high, proj), (down_low, down_high, down)):
        ref[:, :HALF_D] = low[...].astype(f32)
        ref[:, HALF_D:] = high[...].astype(f32)

    @pl.when(pl.program_id(0) == 0)
    def _():
        for v, ref in enumerate((again, ashift, fgain, fshift, up_bias, down_bias)):
            for i in range(D // 128):
                ref[pl.ds(128 * i, 128)] = rows_ref[VECTOR_ROWS + v * (D // 128) + i, :]
        first[...] = rows_ref[0:K, :]
        second[...] = rows_ref[SECOND_ROWS : SECOND_ROWS + H, :]
        table = rows_ref[TABLE_ROWS : TABLE_ROWS + H, :]
        scale[...] = table[:ATOMS, HOT : HOT + ATOMS]
        shift[...] = table[ATOMS:, HOT : HOT + ATOMS]
        turned = square_turn(table)
        hop[...] = turned[:HOPS, :H]
        edge[...] = turned[HOPS : HOPS + EDGES, :H]
        for i, ref in enumerate((first_bias, centers, spreads)):
            ref[...] = rows_ref[KERNEL_ROWS + i, :]


def unpack(out_rows, in_rows, fsum, qsum, rows):
    steps = 8
    tokens = out_rows.shape[0]
    shape = jax.ShapeDtypeStruct
    vec, line = shape((D,), f32), shape((K,), f32)
    mat = lambda *dims: shape(dims, f32)
    whole = lambda item: pl.BlockSpec(item.shape, lambda i: (0,) * len(item.shape))
    by_rows = lambda count, lanes: pl.BlockSpec((count // steps, lanes), lambda i: (i, 0))
    piece = lambda first, count: pl.BlockSpec((count, HALF_D), lambda i: (first // count + i, 0))
    token_rows = by_rows(tokens, D)
    all_q = pl.BlockSpec((3, D // steps, HALF_D), lambda i: (0, i, 0))
    half = HALF_D // steps
    small = [mat(ATOMS, ATOMS), mat(ATOMS, ATOMS), line, line, mat(K, K), line, mat(H, K), mat(HOPS, H), mat(EDGES, H)]
    return pl.pallas_call(
        unpack_kernel,
        grid=(steps,),
        in_specs=[
            by_rows(D, 3 * HALF_D), piece(0, D // steps), piece(D, half), piece(D + HALF_D, half), piece(2 * D, half),
            piece(2 * D + HALF_D, half), token_rows, token_rows, whole(rows),
        ],
        out_specs=[
            token_rows, token_rows, whole(vec), whole(vec), all_q, by_rows(HALF_D, D), whole(vec), whole(vec),
            by_rows(D, HALF_D), whole(vec), by_rows(HALF_D, D), whole(vec),
        ] + [whole(item) for item in small],
        out_shape=[
            shape((tokens, D), bf16), shape((tokens, D), bf16), vec, vec, mat(3, D, HALF_D), mat(HALF_D, D), vec, vec,
            mat(D, HALF_D), vec, mat(HALF_D, D), vec,
        ] + small,
        compiler_params=pltpu.CompilerParams(vmem_limit_bytes=VMEM_BYTES),
        name="unpack",
    )(qsum, fsum, fsum, fsum, fsum, fsum, out_rows, in_rows, rows)


def whole_weights(qkv_weight, up_weight, proj_weight, down_weight):
    columns = lambda w: jnp.stack(jnp.split(w, 2, axis=-1))
    rows = lambda w: jnp.stack(jnp.split(w, 2, axis=0))
    gather = lambda w, dim: lax.all_gather(w, "tp", axis=dim, tiled=True)
    return (
        columns(gather(qkv_weight.transpose(1, 0, 2), 2)), columns(gather(up_weight, 1)),
        rows(gather(proj_weight, 0)), rows(gather(down_weight, 0)),
    )


def sum_grads(fgrads, qgrads, small):
    total_f, total_q, rows = lax.psum((fgrads, qgrads, small), ("mol", "tp"))
    share = D // lax.axis_size("tp")
    at = lax.axis_index("tp") * share

    def columns(halves):
        return lax.dynamic_slice_in_dim(jnp.concatenate(list(halves), axis=-1), at, share, halves.ndim - 2)

    def rows_of(block):
        part = total_f[:, D * block : D * (block + 1)]
        sides = jnp.concatenate([part[:, :HALF_D], part[:, HALF_D:]], axis=2).reshape(D, D)
        return lax.dynamic_slice_in_dim(sides, at, share, 0)

    qkv = columns(total_q.reshape(2, D, 3, HALF_D)).transpose(1, 0, 2)
    return [v.astype(f32) for v in (qkv, columns(total_f[:, :D]), rows_of(1), rows_of(2))], rows


def body(
    mesh_shape,
    hidden_in, positions, atom_types, hop_counts, edge_types, lengths, branches,
    attn_gain, attn_shift, qkv_weight, proj_weight, ffn_gain, ffn_shift, up_weight, up_bias, down_weight, down_bias,
    kernel_scale, kernel_shift, centers, spreads, first_weight, first_bias, second_weight, hop_table, edge_table,
    cotangent,
):
    remote = mesh_shape["tp"] == 2 and mesh_shape["mol"] == 16 and branches.shape[0] == 8
    if remote:
        weights = (qkv_weight.transpose(1, 0, 2), up_weight, proj_weight, down_weight)
    else:
        weights = whole_weights(qkv_weight, up_weight, proj_weight, down_weight)
    arrays = dict(
        lengths=lengths, flags=branches.T, positions=positions, atoms=atom_types, hops=hop_counts.T,
        edges=edge_types.T, kernel_scale=kernel_scale, kernel_shift=kernel_shift, centers=centers, spreads=spreads,
        first_weight=first_weight, first_bias=first_bias, second_weight=second_weight.T, hop_table=hop_table,
        edge_table=edge_table, attn_gain=attn_gain, attn_shift=attn_shift, ffn_gain=ffn_gain, ffn_shift=ffn_shift,
        up_bias=up_bias, down_bias=down_bias, hidden=hidden_in, cotangent=cotangent,
        qkv=weights[0], up=weights[1], proj=weights[2], down=weights[3],
    )
    output, grad_input, sums = layer(remote, arrays)
    if remote:
        fsum, qsum, rows = sums
    else:
        big, rows = sum_grads(*sums)
        fsum, qsum = jnp.zeros((3 * D, HALF_D), bf16), jnp.zeros((D, 3 * HALF_D), bf16)
    output, grad_input, *grads = unpack(output, grad_input, fsum, qsum, rows)
    if not remote:
        grads[2], grads[6], grads[3], grads[8] = big
    grads[2] = grads[2].transpose(1, 0, 2)
    grads[16] = grads[16].T
    return (output, grad_input, *grads)


def solution(mesh):
    rows = P(("mol", "tp"), None)
    all_of = P()
    in_specs = (
        rows, P(None, ("mol", "tp")), P(("mol", "tp")), rows, rows, P("mol"), rows, all_of, all_of,
        P(None, None, "tp"), P("tp", None), all_of, all_of, P(None, "tp"), all_of, P("tp", None),
    ) + (all_of,) * 10 + (rows,)
    out_specs = (
        rows, rows, all_of, all_of, P(None, None, "tp"), P("tp", None), all_of, all_of, P(None, "tp"), all_of,
        P("tp", None),
    ) + (all_of,) * 10
    step = functools.partial(body, dict(mesh.shape))
    return jax.shard_map(step, mesh=mesh, in_specs=in_specs, out_specs=out_specs, check_vma=False)
```

```python
import functools
from types import SimpleNamespace

import jax
import jax.numpy as jnp
from jax import lax
from jax.experimental import pallas as pl
from jax.experimental.pallas import tpu as pltpu
from jax.sharding import PartitionSpec as P

D = 768
H = 32
HD = 24
FF = 768
K = 128
SLOT = 64
HALF = SLOT // 2
HALF_D = D // 2
PAIRS = SLOT * SLOT
HOPS = 16
EDGES = 8
ATOMS = 16
GROUP = 4
GROUPS = H // GROUP
HOT = 32

highest = lax.Precision.HIGHEST
neg_large = -1e30
root_tau = 2.5066282746310002
root_half = 0.7071067811865476
inv_root_tau = 0.3989422804014327
head_scale = HD ** (-0.5)
VMEM_BYTES = 62 * 1024 * 1024
TILE = 512

SECOND_ROWS = K
TABLE_ROWS = SECOND_ROWS + H
KERNEL_ROWS = TABLE_ROWS + H
VECTOR_ROWS = KERNEL_ROWS + 8
SMALL_ROWS = 256

MESH = pl.DeviceIdType.MESH
f32 = jnp.float32
bf16 = jnp.bfloat16


def dot_nn(left, right, precision=None):
    return lax.dot_general(left, right, (((1,), (0,)), ((), ())), precision=precision, preferred_element_type=f32)


def dot_nt(left, right, precision=None):
    return lax.dot_general(left, right, (((1,), (1,)), ((), ())), precision=precision, preferred_element_type=f32)


def dot_tn(left, right, precision=None):
    return lax.dot_general(left, right, (((0,), (0,)), ((), ())), precision=precision, preferred_element_type=f32)


def iota(shape, dim):
    return lax.broadcasted_iota(jnp.int32, shape, dim)


def gelu_parts(values):
    size = jnp.abs(values)
    bell = jnp.exp(values * values * -0.5)
    denominator = 1.0 + (0.3275911 * root_half) * size
    t = pl.reciprocal(denominator, approx=True)
    series = 0.5 * 1.061405429
    for factor in (-1.453152027, 1.421413741, -0.284496736, 0.254829592):
        series = series * t + 0.5 * factor
    tail = series * t * bell
    gelu = jnp.maximum(values, 0.0) - size * tail
    outer = tail - size * (bell * inv_root_tau)
    return gelu, jnp.where(values >= 0.0, 1.0 - outer, outer)


def to_column(row):
    size = row.shape[1]
    same = iota((size, size), 0) == iota((size, size), 1)
    return jnp.sum(jnp.where(same, row, 0.0), axis=1, keepdims=True)


def half_swap(values):
    return pltpu.roll(values, 64, 1)


def low_lanes(rows):
    return iota((rows, 128), 1) < 64


def vmem(count):
    return [pl.BlockSpec(memory_space=pltpu.VMEM)] * count


def row_of(ref):
    return ref[...].reshape(1, ref.shape[0])


def place():
    mol = lax.axis_index("mol")
    return mol % 2, (mol // 2) % 2, mol // 4, lax.axis_index("tp")


def greet(peers):
    barrier = pltpu.get_barrier_semaphore()
    for peer in peers:
        pl.semaphore_signal(barrier, inc=1, device_id=peer, device_id_type=MESH)
    pl.semaphore_wait(barrier, len(peers))


def window(group):
    first = GROUP * HD * group
    start = first // 128 * 128
    width = 128 if first - start + GROUP * HD <= 128 else 256
    return start, width, first - start


def head_masks(group, kind):
    _, width, offset = window(group)
    lane = iota((1, width), 1)
    return [
        ((lane >= offset + HD * h) & (lane < offset + HD * (h + 1))).astype(f32).astype(kind) for h in range(GROUP)
    ]


def spread_heads(values, group):
    return jnp.concatenate([values * mask for mask in head_masks(group, bf16)], axis=0)


def gather_heads(values, group):
    masks = head_masks(group, f32)
    total = values[:SLOT] * masks[0]
    for h in range(1, GROUP):
        total = total + values[SLOT * h : SLOT * (h + 1)] * masks[h]
    return total


def standardize(values):
    centred = values - jnp.mean(values, axis=-1, keepdims=True)
    inv_std = lax.rsqrt(jnp.mean(centred * centred, axis=-1, keepdims=True) + 1e-05)
    return centred * inv_std, inv_std


def norm_back(d_normed, scaled, inv_std, gain):
    weighted = d_normed * gain
    inner_a = jnp.mean(weighted, axis=-1, keepdims=True)
    inner_b = jnp.mean(weighted * scaled, axis=-1, keepdims=True)
    return inv_std * (weighted - inner_a - scaled * inner_b)


def column_sum(values):
    return jnp.sum(values, axis=0, keepdims=True)


class Peers:
    def __init__(self):
        self.core, self.x, self.z, self.tp = place()
        mol = lax.axis_index("mol")
        self.over_core = {"mol": mol + 1 - 2 * self.core}
        self.over_x = {"mol": mol + 2 - 4 * self.x}
        self.over_tp = {"tp": 1 - self.tp}
        self.turn = [lax.rem(self.z + d, 4) for d in range(4)]
        self.over_z = [{"mol": self.turn[d] * 4 + self.x * 2 + self.core} for d in range(4)]

    def neighbour(self, k):
        core = self.core + (1 - 2 * self.core) * (k & 1)
        x = self.x + (1 - 2 * self.x) * (k >> 1 & 1)
        tp = self.tp + (1 - 2 * self.tp) * (k >> 2)
        return core * 4 + tp * 2 + x, {"mol": self.z * 4 + x * 2 + core, "tp": tp}

    def everyone(self):
        return [self.neighbour(k)[1] for k in range(1, 8)] + self.over_z[1:]


def span(start, size):
    return pl.ds(pl.multiple_of(start, size), size)


def add_rows(target, source, rows):
    step = 96 if rows % 96 == 0 else min(rows, 32)

    def piece(i, _):
        at = pl.ds(pl.multiple_of(i * step, step), step)
        target[at, :] = (target[at, :].astype(f32) + source[at, :].astype(f32)).astype(target.dtype)
        return 0

    lax.fori_loop(0, rows // step, piece, 0)


class Reduction:
    kinds = 11

    def __init__(self, peers, part, total, from_core, from_tp, from_x, from_z, sends, recvs):
        self.peers, self.part, self.total = peers, part, total
        self.from_core, self.from_tp, self.from_x, self.from_z = from_core, from_tp, from_x, from_z
        self.sends, self.recvs = sends, recvs
        self.half = from_core.shape[2]
        self.quarter, self.least = self.half // 2, self.half // 8

    def rows(self, b, level):
        p = self.peers
        at = b * 2 * self.half + p.core * self.half
        if level > 0:
            at = at + p.x * self.quarter
        return at + p.z * self.least if level > 1 else at

    def copy(self, b, kind):
        p = self.peers
        part, total = self.part, self.total
        half, quarter, least = self.half, self.quarter, self.least
        if kind == 0:
            src = part.at[:, span(b * 2 * half + (1 - p.core) * half, half)]
            dst, peer = self.from_core.at[b], p.over_core
        elif kind == 1:
            src, dst, peer = part.at[1 - p.tp, span(self.rows(b, 0), half)], self.from_tp.at[b], p.over_tp
        elif kind == 2:
            src = part.at[p.tp, span(self.rows(b, 0) + (1 - p.x) * quarter, quarter)]
            dst, peer = self.from_x.at[b], p.over_x
        elif kind < 6:
            d = kind - 2
            src = part.at[p.tp, span(self.rows(b, 1) + p.turn[d] * least, least)]
            dst, peer = self.from_z.at[b, d - 1], p.over_z[d]
        elif kind < 9:
            src = dst = total.at[span(self.rows(b, 2), least)]
            peer = p.over_z[kind - 5]
        elif kind == 9:
            src = dst = total.at[span(self.rows(b, 1), quarter)]
            peer = p.over_x
        else:
            src = dst = total.at[span(self.rows(b, 0), half)]
            peer = p.over_core
        return pltpu.make_async_remote_copy(
            src_ref=src, dst_ref=dst, send_sem=self.sends.at[b, kind], recv_sem=self.recvs.at[b, kind],
            device_id=peer, device_id_type=MESH,
        )

    def act(self, b, stage):
        p = self.peers
        half, quarter, least = self.half, self.quarter, self.least
        part = self.part
        if stage == 0:
            self.copy(b, 0).start()
        elif stage == 1:
            self.copy(b, 0).wait_recv()
            at = span(self.rows(b, 0), half)
            add_rows(part.at[1 - p.tp, at], self.from_core.at[b, 1 - p.tp], half)
            self.copy(b, 1).start()
            add_rows(part.at[p.tp, at], self.from_core.at[b, p.tp], half)
        elif stage == 2:
            self.copy(b, 1).wait_recv()
            away, mine = (1 - p.x) * quarter, p.x * quarter
            at = self.rows(b, 0)
            add_rows(part.at[p.tp, span(at + away, quarter)], self.from_tp.at[b, span(away, quarter)], quarter)
            self.copy(b, 2).start()
            add_rows(part.at[p.tp, span(at + mine, quarter)], self.from_tp.at[b, span(mine, quarter)], quarter)
        elif stage == 3:
            self.copy(b, 2).wait_recv()
            add_rows(part.at[p.tp, span(self.rows(b, 1), quarter)], self.from_x.at[b], quarter)
            for kind in (3, 4, 5):
                self.copy(b, kind).start()
        elif stage == 4:
            for kind in (3, 4, 5):
                self.copy(b, kind).wait_recv()
            mine = span(self.rows(b, 2), least)
            value = part[p.tp, mine, :].astype(f32)
            for d in range(3):
                value = value + self.from_z[b, d].astype(f32)
            self.total[mine, :] = value.astype(bf16)
            for kind in (6, 7, 8):
                self.copy(b, kind).start()
        elif stage == 5:
            for kind in (6, 7, 8):
                self.copy(b, kind).wait_recv()
            self.copy(b, 9).start()
        elif stage == 6:
            self.copy(b, 9).wait_recv()
            self.copy(b, 10).start()
        elif stage == 7:
            self.copy(b, 10).wait_recv()
        else:
            for kind in range(self.kinds):
                self.copy(b, kind).wait_send()


class SmallReduction:
    def __init__(self, peers, part, total, from_near, from_z, sends, recvs):
        self.peers, self.part, self.total, self.from_near, self.from_z = peers, part, total, from_near, from_z
        self.sends, self.recvs = sends, recvs
        p = peers
        self.near = [p.neighbour(k) for k in range(8)]
        self.mine = span(self.near[0][0] * 32, 32)

    def copy(self, kind):
        p = self.peers
        if kind < 7:
            index, peer = self.near[kind + 1]
            src, dst = self.part.at[span(index * 32, 32)], self.from_near.at[kind]
        elif kind < 10:
            src = dst = self.from_z.at[p.z]
            peer = p.over_z[kind - 6]
        else:
            src = dst = self.total.at[self.mine]
            peer = self.near[kind - 9][1]
        return pltpu.make_async_remote_copy(
            src_ref=src, dst_ref=dst, send_sem=self.sends.at[kind], recv_sem=self.recvs.at[kind],
            device_id=peer, device_id_type=MESH,
        )

    def act(self, stage):
        hops = (range(0, 7), range(7, 10), range(10, 17))
        if stage == 4:
            for kind in range(17):
                self.copy(kind).wait_send()
            return
        if stage > 0:
            for kind in hops[stage - 1]:
                self.copy(kind).wait_recv()
        if stage == 1:
            value = self.part[self.mine, :]
            for k in range(7):
                value = value + self.from_near[k]
            self.from_z[self.peers.z] = value
        elif stage == 2:
            self.total[self.mine, :] = (self.from_z[0] + self.from_z[1]) + (self.from_z[2] + self.from_z[3])
        if stage < 3:
            for kind in hops[stage]:
                self.copy(kind).start()


def big_scratch(rows, lanes):
    half = rows // 2
    sems = pltpu.SemaphoreType.DMA((3, Reduction.kinds))
    return [
        pltpu.VMEM((3, 2, half, lanes), bf16), pltpu.VMEM((3, half, lanes), bf16),
        pltpu.VMEM((3, half // 2, lanes), bf16), pltpu.VMEM((3, 3, half // 8, lanes), bf16), sems, sems,
    ]


def small_scratch():
    return [
        pltpu.VMEM((7, 32, 128), f32), pltpu.VMEM((4, 32, 128), f32),
        pltpu.SemaphoreType.DMA((17,)), pltpu.SemaphoreType.DMA((17,)),
    ]


class Gather:
    pieces = 6

    def __init__(self, peers, whole, sends, recvs):
        self.peers, self.whole, self.sends, self.recvs = peers, whole, sends, recvs
        self.quarter = peers.x * 2 + peers.core
        self.next_quarter = (1 - peers.x) * 2 + peers.core

    def rows(self, ref, quarter):
        count = ref.shape[0] // 4
        return ref.at[span(quarter * count, count), :]

    def copy(self, index, kind):
        p = self.peers
        if kind == 0:
            src = dst = self.rows(self.whole(index, p.tp), self.quarter)
            peer = p.over_tp
        elif kind == 1:
            src = dst = self.rows(self.whole(index, 1 - p.tp), self.quarter)
            peer = p.over_x
        else:
            src = dst = self.rows(self.whole(index, 1 - p.tp), self.quarter if kind == 2 else self.next_quarter)
            peer = p.over_core
        return pltpu.make_async_remote_copy(
            src_ref=src, dst_ref=dst, send_sem=self.sends.at[index, kind], recv_sem=self.recvs.at[index, kind],
            device_id=peer, device_id_type=MESH,
        )

    def start(self, indices):
        for index in indices:
            self.copy(index, 0).start()

    def onward_x(self, index):
        self.copy(index, 0).wait_recv()
        self.copy(index, 1).start()
        self.copy(index, 2).start()

    def onward_core(self, index):
        self.copy(index, 1).wait_recv()
        self.copy(index, 3).start()

    def arrive(self, index):
        self.copy(index, 2).wait_recv()
        self.copy(index, 3).wait_recv()

    def finish(self):
        for index in range(self.pieces):
            for kind in range(4):
                self.copy(index, kind).wait_send()


def square_turn(values):
    rows, lanes = values.shape
    if lanes < 128:
        values = jnp.concatenate([values, jnp.zeros((rows, 128 - lanes), f32)], axis=1)
    if rows < 128:
        values = jnp.concatenate([values, jnp.zeros((128 - rows, 128), f32)], axis=0)
    return values.T


def widen(values):
    return jnp.concatenate([values] * (TILE // 128), axis=1)


def strips():
    return [slice(16 * i, 16 * (i + 1)) for i in range(K // 16)]


def four_rows(ref, slot, first):
    return jnp.concatenate([ref[slot, pl.ds(first + i, 1), :] for i in range(TILE // 128)], axis=1)


def hot_rows(values, count):
    return (values == iota((count, TILE), 0).astype(f32)).astype(f32)


def fold_lanes(values):
    total = values[:, :128]
    for i in range(1, TILE // 128):
        total = total + values[:, 128 * i : 128 * (i + 1)]
    return total


def twice(ref, values):
    none = jnp.zeros_like(values)
    ref[...] = jnp.concatenate(
        [jnp.concatenate([values, none], axis=1), jnp.concatenate([none, values], axis=1)], axis=0
    ).astype(bf16)


def dot_halves(weights, pieces):
    values = jnp.concatenate(pieces, axis=0)
    half = TILE // 2
    both = dot_nn(weights, jnp.concatenate([values[:, :half], values[:, half:]], axis=0))
    rows = both.shape[0] // 2
    return jnp.concatenate([both[:rows], both[rows:]], axis=1)


def prepare_pairs(r):
    spr = to_column(row_of(r.spreads))
    r.cols[0] = jnp.broadcast_to(to_column(row_of(r.centers)), (K, 128))
    r.cols[1] = jnp.broadcast_to(root_half / spr, (K, 128))
    r.cols[2] = jnp.broadcast_to(-jnp.log(root_tau * spr), (K, 128))
    r.cols[3] = jnp.broadcast_to(to_column(row_of(r.first_bias)), (K, 128))
    r.cols[4] = jnp.broadcast_to(1.0 / spr, (K, 128))
    twice(r.w1, r.first_weight[...].astype(f32))
    twice(r.w1t, r.first_weight[...].astype(f32).T)
    r.w2[...] = square_turn(r.second_weight[...].astype(f32))
    table = jnp.concatenate([r.hop_table[...], r.edge_table[...], jnp.zeros((128 - HOPS - EDGES, H), f32)], axis=0)
    table = jnp.concatenate([table, jnp.zeros((128, 128 - H), f32)], axis=1).T[:H, :HOT]
    one = table.astype(bf16).astype(f32)
    r.base[...] = jnp.concatenate(
        [r.second_weight[...].astype(f32), one, table - one, jnp.zeros((H, 64), f32)], axis=1
    )


def bf16_parts(values, count):
    parts = []
    for _ in range(count):
        parts.append(values.astype(bf16))
        values = values - parts[-1].astype(f32)
    return parts


def pair_tables(r, slots):
    low = low_lanes(HALF)
    low_row = low_lanes(1)
    tables = [part.astype(f32) for ref in (r.kernel_scale, r.kernel_shift) for part in bf16_parts(ref[...], 3)]
    tables = jnp.concatenate([square_turn(part)[:ATOMS, :ATOMS] for part in tables], axis=1)
    tables = jnp.concatenate([tables, jnp.zeros((ATOMS, 128 - 6 * ATOMS), f32)], axis=1).astype(bf16)
    for group in range(slots // 2):
        lanes = slice(128 * group, 128 * (group + 1))
        atoms = r.atoms[lanes].astype(f32).reshape(1, 128)
        rows = jnp.concatenate([r.positions[:, lanes], atoms, jnp.zeros((4, 128), f32)], axis=0)
        columns = square_turn(rows)
        key_hot = (columns[:, 3:4] == iota((128, ATOMS), 1).astype(f32)).astype(f32).astype(bf16)
        picks = dot_nn(key_hot, tables).astype(bf16)
        turned = half_swap(rows)
        for s in range(2):
            slot = 2 * group + s
            tokens = slice(SLOT * s, SLOT * (s + 1))
            double = jnp.where(low_lanes(8), *((rows, turned) if s == 0 else (turned, rows)))
            total = None
            for c in range(3):
                column = columns[tokens, c : c + 1]
                offset = jnp.where(low, column[:HALF], column[HALF:]) - double[c : c + 1]
                total = offset * offset if total is None else total + offset * offset
            distance = jnp.sqrt(total)
            query_hot = (double[3:4] == iota((ATOMS, 128), 0).astype(f32)).astype(f32)
            three, none = [query_hot] * 3, [jnp.zeros((3 * ATOMS, 128), f32)]
            rest = [jnp.zeros((128 - 6 * ATOMS, 128), f32)]
            spread = jnp.concatenate(
                [jnp.concatenate(three + none + rest, axis=0), jnp.concatenate(none + three + rest, axis=0)], axis=1
            )
            both = dot_nn(picks[tokens], spread.astype(bf16))
            scale = jnp.where(low, both[:HALF, :128], both[HALF:, :128])
            shift = jnp.where(low, both[:HALF, 128:], both[HALF:, 128:])
            r.argument[slot] = scale * distance + shift
            r.distance[slot] = distance
            for source, target in ((r.hops, r.hop_rows), (r.edges, r.edge_rows)):
                values = source[:, lanes].astype(f32)
                top, bottom = values[:HALF], values[HALF:]
                if s == 0:
                    target[slot] = jnp.where(low, top, half_swap(bottom))
                else:
                    target[slot] = jnp.where(low, half_swap(top), bottom)
            r.atom_rows[slot] = jnp.broadcast_to(double[3:4], (8, 128))


def table_grads(r, slots):
    lefts, rights = [], []
    for slot in range(slots):
        query_hot = (r.atom_rows[slot, 0:1, :] == iota((ATOMS, 128), 0).astype(f32)).astype(f32)
        keys = jnp.concatenate([query_hot[:, :HALF], query_hot[:, HALF:SLOT]], axis=0)
        keys = jnp.concatenate([keys, keys], axis=1).astype(bf16)
        values = jnp.concatenate([r.dargs[slot] * r.distance[slot], r.dargs[slot]], axis=1)
        both = dot_nn(keys, jnp.concatenate(bf16_parts(values, 2), axis=0))
        low = low_lanes(ATOMS)
        for index in range(2):
            lanes = slice(128 * index, 128 * (index + 1))
            rights.append(bf16_parts(jnp.where(low, both[:ATOMS, lanes], both[ATOMS:, lanes]), 2))
        lefts.append(query_hot.astype(bf16))
    left = jnp.concatenate(lefts, axis=1)
    right = jnp.concatenate(
        [jnp.concatenate([rights[2 * s + index][part] for s in range(slots)], axis=1) for index in range(2) for part in range(2)],
        axis=0,
    )
    result = dot_nt(left, right)
    return [
        result[:, 2 * ATOMS * index : 2 * ATOMS * index + ATOMS] + result[:, 2 * ATOMS * index + ATOMS : 2 * ATOMS * (index + 1)]
        for index in range(2)
    ]


def in_stages(stages, count):
    held = {}
    for time in range(count + len(stages) - 1):
        for k, stage in reversed(list(enumerate(stages))):
            if 0 <= time - k < count:
                held[time - k] = stage(time - k, held.get(time - k))


TILES = PAIRS // TILE
ROWS = TILE // 128


def pair_forward(r, slot):
    bank = lax.rem(slot, 2)
    graph_on = r.flags[0, slot].astype(f32)
    space_on = r.flags[1, slot].astype(f32)
    factor = jnp.where(iota((H, 256), 1) < K, space_on, graph_on)
    r.lhs[...] = (r.base[...] * factor).astype(bf16)

    def kernels(tile, _):
        where = slice(tile * TILE, (tile + 1) * TILE)
        arg = four_rows(r.argument, slot, tile * ROWS)
        pieces = []
        for rows in strips():
            u = (arg - widen(r.cols[0, rows])) * widen(r.cols[1, rows])
            pieces.append(jnp.exp(widen(r.cols[2, rows]) - u * u).astype(bf16))
            r.left[bank, rows, where] = pieces[-1]
        return dot_halves(r.w1t[...], pieces)

    def hidden(tile, first):
        where = slice(tile * TILE, (tile + 1) * TILE)
        pieces = []
        for rows in strips():
            value, slope = gelu_parts(first[rows] + widen(r.cols[3, rows]))
            pieces.append(value.astype(bf16))
            r.left[bank, slice(K + rows.start, K + rows.stop), where] = pieces[-1]
            r.slope[bank, rows, where] = slope.astype(bf16)
        hot = jnp.concatenate(
            [
                hot_rows(four_rows(r.hop_rows, slot, tile * ROWS), HOPS),
                hot_rows(four_rows(r.edge_rows, slot, tile * ROWS), HOT - HOPS),
            ],
            axis=0,
        ).astype(bf16)
        return dot_nn(r.lhs[:, : K + 2 * HOT], jnp.concatenate(pieces + [hot] * 2, axis=0))

    def biases(tile, bias):
        bias = bias.astype(bf16).astype(f32)
        for i in range(ROWS):
            r.bias[slot, pl.ds(tile * ROWS + i, H, stride=HALF), :] = bias[:, 128 * i : 128 * (i + 1)]

    in_stages([kernels, hidden, biases], TILES)


def pair_backward(r, slot, between):
    bank = lax.rem(slot, 2)
    graph_on = r.flags[0, slot].astype(f32)
    space_on = r.flags[1, slot].astype(f32)
    twice(r.w2_twice, r.w2[:, :H] * space_on)

    def scores(tile, _):
        where = slice(tile * TILE, (tile + 1) * TILE)
        grad = jnp.concatenate(
            [r.bias[slot, pl.ds(tile * ROWS + i, H, stride=HALF), :] for i in range(ROWS)], axis=1
        )
        r.right[K:, where] = jnp.concatenate([grad * space_on, grad * graph_on], axis=0).astype(bf16)
        edge_hot = hot_rows(four_rows(r.edge_rows, slot, tile * ROWS), HOT - HOPS)
        edge_hot = jnp.where(iota((HOT - HOPS, TILE), 0) == EDGES, 1.0, edge_hot)
        r.left[bank, 2 * K :, where] = jnp.concatenate(
            [hot_rows(four_rows(r.hop_rows, slot, tile * ROWS), HOPS), edge_hot], axis=0
        ).astype(bf16)
        return dot_halves(r.w2_twice[...], [grad.astype(bf16)])

    def hidden(tile, d_second):
        where = slice(tile * TILE, (tile + 1) * TILE)
        pieces = []
        for rows in strips():
            pieces.append((d_second[rows] * r.slope[bank, rows, where].astype(f32)).astype(bf16))
            r.right[rows, where] = pieces[-1]
        return dot_halves(r.w1[...], pieces)

    def kernels(tile, d_gauss):
        where = slice(tile * TILE, (tile + 1) * TILE)
        arg = four_rows(r.argument, slot, tile * ROWS)
        d_arg = None
        for rows in strips():
            inv = widen(r.cols[4, rows])
            u = (arg - widen(r.cols[0, rows])) * inv
            q = d_gauss[rows] * r.left[bank, rows, where].astype(f32)
            w = q * u
            r.sums[0, rows] += fold_lanes(w)
            r.sums[1, rows] += fold_lanes(w * u - q)
            w = w * inv
            w = w[:8] + w[8:]
            d_arg = w if d_arg is None else d_arg + w
        d_arg = -jnp.sum(d_arg, axis=0, keepdims=True)
        for i in range(ROWS):
            at = tile * ROWS + i
            r.dargs[slot, at : at + 1, :] = d_arg[:, 128 * i : 128 * (i + 1)]

    in_stages([scores, hidden, kernels], TILES)
    between()
    r.acc_mixed[...] += dot_nt(r.left[bank], r.right[...])


def attend(r, s, first_slot):
    low = low_lanes(HALF)
    rows = span(s * SLOT, SLOT)
    valid = iota((SLOT, GROUP * SLOT), 0) < r.lengths[first_slot + s]
    r.work[0] = jnp.zeros((SLOT, D), f32)
    for g in range(GROUPS):
        start, width, _ = window(g)
        q = r.joined[rows, start : start + width]
        k = r.joined[rows, D + start : D + start + width]
        v = r.joined[rows, 2 * D + start : 2 * D + start + width]
        scores = dot_nt(k, spread_heads(q, g)) * head_scale
        parts = []
        for pair in range(GROUP // 2):
            head = GROUP * g + 2 * pair
            one = r.bias[s, head * HALF : (head + 1) * HALF, :]
            two = r.bias[s, (head + 1) * HALF : (head + 2) * HALF, :]
            top = jnp.where(low, one, half_swap(two))
            bottom = jnp.where(low, half_swap(one), two)
            parts.append(jnp.concatenate([top, bottom], axis=0))
        scores = jnp.where(valid, scores + jnp.concatenate(parts, axis=1), neg_large)
        weights = jnp.exp(scores - jnp.max(scores, axis=0, keepdims=True))
        prob = (weights * (1.0 / jnp.sum(weights, axis=0, keepdims=True))).astype(bf16)
        r.prob[s, :, g * GROUP * SLOT : (g + 1) * GROUP * SLOT] = prob
        r.work[0, :, start : start + width] += gather_heads(dot_tn(prob, v), g)
    r.attended[rows, :] = r.work[0].astype(bf16)


def attend_back(r, s):
    low = low_lanes(HALF)
    rows = span(s * SLOT, SLOT)
    r.work[...] = jnp.zeros((3, SLOT, D), f32)
    for g in range(GROUPS):
        start, width, _ = window(g)
        lanes = slice(start, start + width)
        k = r.joined[rows, D + start : D + start + width]
        v = r.joined[rows, 2 * D + start : 2 * D + start + width]
        q_heads = spread_heads(r.joined[rows, lanes], g)
        d_heads = spread_heads(r.d_attended[rows, lanes], g)
        prob = r.prob[s, :, g * GROUP * SLOT : (g + 1) * GROUP * SLOT]
        wide = prob.astype(f32)
        d_prob = dot_nt(v, d_heads)
        inner = jnp.sum(wide * d_prob, axis=0, keepdims=True)
        d_scores = (wide * (d_prob - inner)).astype(bf16)
        r.work[0, :, lanes] += gather_heads(dot_tn(d_scores, k), g)
        r.work[1, :, lanes] += dot_nn(d_scores, q_heads)
        r.work[2, :, lanes] += dot_nn(prob, d_heads)
        d_wide = d_scores.astype(f32)
        for pair in range(GROUP // 2):
            head = GROUP * g + 2 * pair
            top = d_wide[:HALF, 128 * pair : 128 * (pair + 1)]
            bottom = d_wide[HALF:, 128 * pair : 128 * (pair + 1)]
            r.bias[s, head * HALF : (head + 1) * HALF, :] = jnp.where(low, top, half_swap(bottom))
            r.bias[s, (head + 1) * HALF : (head + 2) * HALF, :] = jnp.where(low, half_swap(top), bottom)
    r.joined[rows, 0:D] = (r.work[0] * head_scale).astype(bf16)
    r.joined[rows, D : 2 * D] = (r.work[1] * head_scale).astype(bf16)
    r.joined[rows, 2 * D : 3 * D] = r.work[2].astype(bf16)


def project(r, rows):
    scaled, _ = standardize(r.hidden[rows, :].astype(f32))
    normed = (scaled * row_of(r.attn_gain) + row_of(r.attn_shift)).astype(bf16)
    r.normed_a[rows, :] = normed
    for m in range(3):
        for t in range(2):
            at = m * D + t * HALF_D
            r.joined[rows, at : at + HALF_D] = dot_nn(normed, r.wqkv[t, m]).astype(bf16)


def feed(r, rows):
    halves = [slice(0, HALF_D), slice(HALF_D, D)]
    resid = r.hidden[rows, :].astype(f32)
    for t in range(2):
        resid = resid + dot_nn(r.attended[rows, halves[t]], r.wproj[t])
    scaled, inv_std = standardize(resid)
    normed = (scaled * row_of(r.ffn_gain) + row_of(r.ffn_shift)).astype(bf16)
    r.normed_f[rows, :] = normed
    pre = jnp.concatenate([dot_nn(normed, r.wup[t]) for t in range(2)], axis=1)
    value, slope = gelu_parts(pre + row_of(r.up_bias))
    active = value.astype(bf16)
    r.activated[rows, :] = active
    result = resid + row_of(r.down_bias)
    for t in range(2):
        result = result + dot_nn(active[:, halves[t]], r.wdown[t])
    r.out_rows[rows, :] = result.astype(bf16)
    cot = r.cotangent[rows, :]
    cot_wide = cot.astype(f32)
    d_active = jnp.concatenate([dot_nt(cot, r.wdown[t]) for t in range(2)], axis=1)
    d_hidden = (d_active * slope).astype(bf16)
    r.d_pre[rows, :] = d_hidden
    d_normed = dot_nt(d_hidden[:, halves[0]], r.wup[0]) + dot_nt(d_hidden[:, halves[1]], r.wup[1])
    d_resid = cot_wide + norm_back(d_normed, scaled, inv_std, row_of(r.ffn_gain))
    r.d_resid[rows, :] = d_resid
    branch = d_resid.astype(bf16)
    r.d_branch[rows, :] = branch
    for t in range(2):
        r.d_attended[rows, halves[t]] = dot_nt(branch, r.wproj[t]).astype(bf16)
    r.vectors[2:3, :] += column_sum(d_normed * scaled)
    r.vectors[3:4, :] += column_sum(d_normed)
    r.vectors[4:5, :] += column_sum(d_hidden.astype(f32))
    r.vectors[5:6, :] += column_sum(cot_wide)


def feed_grads(r, block):
    halves = [slice(0, HALF_D), slice(HALF_D, D)]
    if block == 0:
        grad = dot_tn(r.normed_f[...], r.d_pre[...]).astype(bf16)
        for t in range(2):
            r.fpart[t, :D, :] = grad[:, halves[t]]
        return
    left, right = (r.attended, r.d_branch) if block == 1 else (r.activated, r.cotangent)
    for t in range(2):
        grad = dot_tn(left[:, halves[t]], right[...]).astype(bf16)
        for side in range(2):
            r.fpart[t, D * block + HALF_D * side : D * block + HALF_D * (side + 1), :] = grad[:, halves[side]]


def qkv_grads(r, block):
    rows = slice(256 * block, 256 * (block + 1))
    for m in range(3):
        grad = dot_tn(r.normed_a[:, rows], r.joined[:, m * D : (m + 1) * D]).astype(bf16)
        for t in range(2):
            r.qpart[t, rows, m * HALF_D : (m + 1) * HALF_D] = grad[:, t * HALF_D : (t + 1) * HALF_D]


def finish_input(r, rows):
    d_normed = None
    for m in range(3):
        for t in range(2):
            at = m * D + t * HALF_D
            term = dot_nt(r.joined[rows, at : at + HALF_D], r.wqkv[t, m])
            d_normed = term if d_normed is None else d_normed + term
    scaled, inv_std = standardize(r.hidden[rows, :].astype(f32))
    grad = r.d_resid[rows, :] + norm_back(d_normed, scaled, inv_std, row_of(r.attn_gain))
    r.in_rows[rows, :] = grad.astype(bf16)
    r.vectors[0:1, :] += column_sum(d_normed * scaled)
    r.vectors[1:2, :] += column_sum(d_normed)


def pack_small(r, slots):
    tables = table_grads(r, slots)
    for v in range(6):
        for i in range(D // 128):
            at = VECTOR_ROWS + v * (D // 128) + i
            r.spart[at : at + 1, :] = r.vectors[v : v + 1, 128 * i : 128 * (i + 1)]
    r.spart[0:K, :] = r.acc_mixed[0:K, :K]
    r.spart[SECOND_ROWS : SECOND_ROWS + H, :] = square_turn(r.acc_mixed[K : 2 * K, K:])[:H]
    r.spart[TABLE_ROWS : TABLE_ROWS + H, :HOT] = square_turn(r.acc_mixed[2 * K :, K:])[H : 2 * H, :HOT]
    for index in range(2):
        rows = slice(TABLE_ROWS + ATOMS * index, TABLE_ROWS + ATOMS * (index + 1))
        r.spart[rows, HOT : HOT + ATOMS] = tables[index]
    ones = 2 * K + HOPS + EDGES
    r.spart[KERNEL_ROWS : KERNEL_ROWS + 1, :] = r.acc_mixed[ones : ones + 1, :K]
    for index in range(2):
        column = jnp.sum(r.sums[index] * r.cols[4], axis=1, keepdims=True)
        same = iota((K, K), 0) == iota((K, K), 1)
        at = KERNEL_ROWS + 1 + index
        r.spart[at : at + 1, :] = jnp.sum(jnp.where(same, column, 0.0), axis=0, keepdims=True)


class Stage:
    def __init__(self, names, near_inputs, carried, refs):
        self.r = SimpleNamespace(**dict(zip(names, refs)))
        r = self.r
        self.loads = {
            name: pltpu.make_async_copy(getattr(r, "given_" + name), getattr(r, name), r.input_sems.at[i])
            for i, name in enumerate(near_inputs)
        }
        self.stores = {
            name: pltpu.make_async_copy(getattr(r, name), getattr(r, name + "_far"), r.carry_sems.at[i])
            for i, name in enumerate(carried)
        }

    def load(self, *names):
        for name in names:
            self.loads[name].start()

    def need(self, *names):
        for name in names:
            self.loads[name].wait()

    def store(self, *names):
        for name in names:
            self.stores[name].start()

    def stored(self):
        for copy in self.stores.values():
            copy.wait()


def each_chunk(r, tokens, work):
    chunk = min(256, tokens)

    def one(c, _):
        work(r, span(c * chunk, chunk))
        return 0

    lax.fori_loop(0, tokens // chunk, one, 0)


def pair_moves(r, slot, back):
    bank = lax.rem(slot, 2)
    both = (r.left_far.at[slot], r.left.at[bank, : 2 * K]), (r.slope_far.at[slot], r.slope.at[bank])
    for index, (far, near) in enumerate(both):
        yield pltpu.make_async_copy(*((far, near) if back else (near, far)), r.pair_sems.at[bank, index])


def start_moves(r, slot, back):
    for copy in pair_moves(r, slot, back):
        copy.start()


def wait_moves(r, slot, back):
    for copy in pair_moves(r, slot, back):
        copy.wait()


def run(steps):
    for act, *where in steps:
        act(*where)


def at_time(index, plan):
    for k, steps in plan.items():
        pl.when(index == k)(functools.partial(run, steps))


FFN_BACK = {0: [(1, 1), (2, 1)], 3: [(0, 2)], 7: [(0, 3), (1, 2)]}
AFTER_GRADS = ([(0, 4), (1, 3), (2, 2)], [(0, 1), (1, 1), (2, 1)])
AFTER_HALF = ([(0, 5)], [])
AFTER_INPUT = ([(2, 3), (1, 4)], [(0, 2)])
FFN_PAIRS = {
    0: [(0, 6)], 2: [(2, 4)], 3: [(1, 5), (0, 7)], 5: [(2, 5)], 7: [(1, 6)], 9: [(2, 6)], 10: [(1, 7)], 12: [(2, 7)],
}
QKV_PAIRS = {
    2: [(0, 3)], 3: [(1, 2)], 6: [(1, 3), (2, 2), (0, 4)], 9: [(1, 4)], 10: [(0, 5)], 11: [(2, 3)], 12: [(1, 5)],
    13: [(0, 6)], 14: [(2, 4)], 15: [(1, 6)],
}


def layer_kernel(remote, names, near_inputs, carried, *refs):
    stage = Stage(names, near_inputs, carried, refs)
    r = stage.r
    stage.load(*[name for name in near_inputs if name not in ("hidden", "cotangent")])
    tokens = r.hidden.shape[0]
    slots = tokens // SLOT
    peers = Peers()
    whole = [r.wqkv, r.wup, r.wproj, r.wdown]
    given = [r.given_qkv, r.given_up, r.given_proj, r.given_down]
    targets = [w.at[peers.tp] for w in whole] if remote else whole
    loads = [
        pltpu.make_async_copy(src, dst, r.load_sems.at[i]) for i, (src, dst) in enumerate(zip(given, targets))
    ]
    for load in loads:
        load.start()
    stage.load("hidden", "cotangent")
    gather_plan = {}
    if remote:

        def whole_piece(index, tp):
            return whole[0].at[tp, index] if index < 3 else whole[index - 2].at[tp]

        gather = Gather(peers, whole_piece, r.gather_sends, r.gather_recvs)
        ffn = Reduction(peers, r.fpart, r.ftotal, r.f_core, r.f_tp, r.f_x, r.f_z, r.f_sends, r.f_recvs)
        qkv = Reduction(peers, r.qpart, r.qtotal, r.q_core, r.q_tp, r.q_x, r.q_z, r.q_sends, r.q_recvs)
        small = SmallReduction(peers, r.spart, r.stotal, r.s_near, r.s_z, r.s_sends, r.s_recvs)
        greet(peers.everyone())
        for load, indices in zip(loads, ((0, 1, 2), (3,), (4,), (5,))):
            load.wait()
            gather.start(indices)
        x, core = gather.onward_x, gather.onward_core
        gather_plan = {
            0: [(x, 0)], 1: [(x, 1), (core, 0)], 2: [(x, 2), (core, 1)], 3: [(x, 3), (core, 2)],
            4: [(x, 4), (core, 3), (x, 5)], 5: [(core, 4)], 6: [(core, 5)],
        }

    def leave(which, block):
        near, far = ((r.ftotal, r.ftotal_far), (r.qtotal, r.qtotal_far))[which]
        rows = near.shape[0] // 3
        at = slice(block * rows, (block + 1) * rows)
        return pltpu.make_async_copy(near.at[at], far.at[at], r.leave_sems.at[3 * which + block])

    def advance(which, actions):
        if remote:
            for block, step in actions:
                (ffn, qkv)[which].act(block, step)
                if step == 7:
                    leave(which, block).start()

    def plan_of(*plans):
        times = sorted(set().union(*plans)) if remote else []
        return {
            k: [(advance, which, plan[k]) for which, plan in enumerate(plans) if k in plan] for k in times
        }

    stage.need(*[name for name in near_inputs if name not in ("hidden", "cotangent")])
    prepare_pairs(r)
    pair_tables(r, slots)

    def pairs(slot, _):
        pl.when(slot >= 2)(lambda: wait_moves(r, slot - 2, False))
        pair_forward(r, slot)
        start_moves(r, slot, False)
        at_time(slot, gather_plan)
        return 0

    lax.fori_loop(0, slots, pairs, 0)
    stage.need("hidden")
    if remote:
        for index in range(3):
            gather.arrive(index)
    else:
        for load in loads:
            load.wait()
    each_chunk(r, tokens, project)
    first_slot = peers.tp * slots

    def attend_one(s, _):
        attend(r, s, first_slot)
        return 0

    lax.fori_loop(0, slots, attend_one, 0)
    stage.need("cotangent")
    if remote:
        for index in range(3, 6):
            gather.arrive(index)
    r.vectors[...] = jnp.zeros_like(r.vectors)
    each_chunk(r, tokens, feed)
    stage.store("out_rows")
    for slot in (slots - 2, slots - 1):
        wait_moves(r, slot, False)
    start_moves(r, 0, True)
    start_moves(r, 1, True)
    for block in range(3):
        feed_grads(r, block)
        advance(0, [(block, 0)])
    advance(0, [(0, 1)])

    back_plan, pair_plan = plan_of(FFN_BACK), plan_of(FFN_PAIRS, QKV_PAIRS)

    def back_one(s, _):
        attend_back(r, s)
        at_time(s, back_plan)
        return 0

    lax.fori_loop(0, slots, back_one, 0)
    for block in range(3):
        qkv_grads(r, block)
        advance(1, [(block, 0)])
    for which in range(2):
        advance(which, AFTER_GRADS[which])
    each_chunk(r, tokens, finish_input)
    stage.store("in_rows")
    for which in range(2):
        advance(which, AFTER_HALF[which] + AFTER_INPUT[which])
    for ref in (r.sums, r.acc_mixed, r.spart):
        ref[...] = jnp.zeros_like(ref)

    def pairs_back(slot, _):
        wait_moves(r, slot, True)
        pair_backward(r, slot, lambda: at_time(2 * slot, pair_plan))
        pl.when(slot + 2 < slots)(lambda: start_moves(r, slot + 2, True))
        at_time(2 * slot + 1, pair_plan)
        return 0

    lax.fori_loop(0, slots, pairs_back, 0)
    pack_small(r, slots)
    if remote:
        small.act(0)
        advance(1, [(2, 5), (0, 7)])
        small.act(1)
        advance(1, [(1, 7)])
        advance(1, [(2, 6)])
        small.act(2)
        advance(1, [(2, 7)])
        small.act(3)
        rows = pltpu.make_async_copy(r.stotal, r.stotal_far, r.leave_sems.at[6])
        rows.start()
        for which in range(2):
            advance(which, [(b, 8) for b in range(3)])
        small.act(4)
        gather.finish()
        for which in range(2):
            for block in range(3):
                leave(which, block).wait()
        rows.wait()
    else:
        stage.store("fpart", "qpart", "spart")
    stage.stored()


def call_stage(kernel, name, remote, collective, arrays, scalars, far, outs, carried, scratch):
    vm, sem = pltpu.VMEM, pltpu.SemaphoreType.DMA
    near = {n: vm(a.shape, a.dtype) for n, a in arrays.items() if n not in scalars + far}
    in_names = [n if n in scalars or n.endswith("_far") else "given_" + n for n in arrays]
    results = outs | {n + "_far": item for n, item in carried.items()}
    scratch = near | {n: vm(*item) for n, item in carried.items()} | scratch
    scratch |= {"input_sems": sem((len(near),)), "carry_sems": sem((len(carried),))}
    names = in_names + list(results) + list(scratch)
    values = pl.pallas_call(
        functools.partial(kernel, remote, names, list(near), list(carried)),
        in_specs=[pl.BlockSpec(memory_space=pltpu.SMEM if n in scalars else pl.ANY) for n in arrays],
        out_specs=[pl.BlockSpec(memory_space=pl.ANY)] * len(results),
        out_shape=[jax.ShapeDtypeStruct(*item) for item in results.values()],
        scratch_shapes=list(scratch.values()),
        compiler_params=pltpu.CompilerParams(
            vmem_limit_bytes=VMEM_BYTES, **(dict(collective_id=collective, has_side_effects=True) if remote else {})
        ),
        name=name,
    )(*arrays.values())
    return dict(zip(results, values))


def layer(remote, arrays):
    tokens = arrays["hidden"].shape[0]
    slots = tokens // SLOT
    v, sem = pltpu.VMEM, pltpu.SemaphoreType.DMA
    of_tokens = (tokens, D)
    table = (slots, HALF, 128)
    fshape, qshape, sshape = (3 * D, HALF_D), (D, 3 * HALF_D), (SMALL_ROWS, 128)
    outs = {"left_far": ((slots, 2 * K, PAIRS), bf16), "slope_far": ((slots, K, PAIRS), bf16)}
    carried = {"out_rows": (of_tokens, bf16), "in_rows": (of_tokens, bf16)}
    scratch = {
        "wqkv": v((2, 3, D, HALF_D), bf16), "wup": v((2, D, HALF_D), bf16), "wproj": v((2, HALF_D, D), bf16),
        "wdown": v((2, HALF_D, D), bf16), "load_sems": sem((4,)), "pair_sems": sem((2, 2)),
        "left": v((2, 2 * K + HOT, PAIRS), bf16), "slope": v((2, K, PAIRS), bf16),
        "right": v((K + 2 * H, PAIRS), bf16), "cols": v((5, K, 128), f32), "w1": v((2 * K, 2 * K), bf16), "w1t": v((2 * K, 2 * K), bf16),
        "w2": v((K, 128), f32), "w2_twice": v((2 * K, 2 * H), bf16), "base": v((H, 256), f32), "lhs": v((H, 256), bf16),
        "argument": v(table, f32), "distance": v(table, f32), "hop_rows": v(table, f32), "edge_rows": v(table, f32),
        "atom_rows": v((slots, 8, 128), f32), "dargs": v(table, f32), "bias": v((slots, H * HALF, 128), f32),
        "work": v((3, SLOT, D), f32), "normed_a": v(of_tokens, bf16), "joined": v((tokens, 3 * D), bf16),
        "prob": v((slots, SLOT, H * SLOT), bf16), "attended": v(of_tokens, bf16), "normed_f": v(of_tokens, bf16),
        "activated": v(of_tokens, bf16), "d_pre": v(of_tokens, bf16), "d_branch": v(of_tokens, bf16),
        "d_attended": v(of_tokens, bf16), "d_resid": v(of_tokens, f32), "vectors": v((8, D), f32),
        "sums": v((2, K, 128), f32), "acc_mixed": v((2 * K + HOT, K + 2 * H), f32),
    }
    parts = {"fpart": ((2,) + fshape, bf16), "qpart": ((2,) + qshape, bf16), "spart": (sshape, f32)}
    totals = {"ftotal": (fshape, bf16), "qtotal": (qshape, bf16), "stotal": (sshape, f32)}
    if remote:
        outs |= {n + "_far": item for n, item in totals.items()}
        scratch |= {n: v(*item) for n, item in (parts | totals).items()}
        scratch |= {"leave_sems": sem((7,)), "gather_sends": sem((6, 4)), "gather_recvs": sem((6, 4))}
        for name, shape in (("f", (D, HALF_D)), ("q", (D // 3, 3 * HALF_D))):
            keys = ("_core", "_tp", "_x", "_z", "_sends", "_recvs")
            scratch |= {name + key: item for key, item in zip(keys, big_scratch(*shape))}
        scratch |= dict(zip(("s_near", "s_z", "s_sends", "s_recvs"), small_scratch()))
    else:
        carried |= parts
    results = call_stage(
        layer_kernel, "layer", remote, 0, arrays, ("lengths", "flags"), ("qkv", "up", "proj", "down"), outs, carried,
        scratch,
    )
    sums = [results[n + "_far"] for n in (totals if remote else parts)]
    return results["out_rows_far"], results["in_rows_far"], sums


RESULTS = (
    "output", "grad_input", "attn_gain", "attn_shift", "qkv", "proj", "ffn_gain", "ffn_shift", "up", "up_bias", "down",
    "down_bias", "scale", "shift", "centers", "spreads", "first", "first_bias", "second", "hop", "edge",
)


def unpack_kernel(*refs):
    given = SimpleNamespace(**dict(zip(("out_rows", "in_rows", "fsum", "qsum", "rows"), refs)))
    far = SimpleNamespace(**dict(zip(RESULTS, refs[5:])))
    count = len(RESULTS)
    near = SimpleNamespace(**dict(zip(RESULTS, refs[5 + count : 5 + 2 * count])))
    fsum, qsum, rows, load_sems, store_sems = refs[5 + 2 * count :]
    moves = [(given.rows, rows)]
    sources = ((given.qsum, qsum, 3), (given.fsum, fsum, 9), (given.out_rows, near.output, 1), (given.in_rows, near.grad_input, 1))
    for src, dst, pieces in sources:
        height = src.shape[0] // pieces
        for i in range(pieces):
            at = slice(i * height, (i + 1) * height)
            moves.append((src.at[at], dst.at[at]))
    loads = [pltpu.make_async_copy(src, dst, load_sems.at[i]) for i, (src, dst) in enumerate(moves)]
    for load in loads:
        load.start()
    stores = []

    def store(src, dst):
        stores.append(pltpu.make_async_copy(src, dst, store_sems.at[len(stores)]))
        stores[-1].start()

    for i in range(3):
        loads[1 + i].wait()
        at = slice(256 * i, 256 * (i + 1))
        for m in range(3):
            near.qkv[m, at] = qsum[at, m * HALF_D : (m + 1) * HALF_D].astype(f32)
        store(near.qkv.at[:, at], far.qkv.at[:, at])
    for i in range(3):
        loads[4 + i].wait()
        at = slice(256 * i, 256 * (i + 1))
        near.up[at, :] = fsum[at, :].astype(f32)
        store(near.up.at[at], far.up.at[at])
    for block, name in ((1, "proj"), (2, "down")):
        for i in range(3):
            loads[4 + 3 * block + i].wait()
        ref = getattr(near, name)
        at = D * block
        ref[:, :HALF_D] = fsum[at : at + HALF_D, :].astype(f32)
        ref[:, HALF_D:] = fsum[at + HALF_D : at + D, :].astype(f32)
        store(ref, getattr(far, name))
    loads[13].wait()
    store(near.output, far.output)
    loads[14].wait()
    store(near.grad_input, far.grad_input)
    loads[0].wait()
    names = ("attn_gain", "attn_shift", "ffn_gain", "ffn_shift", "up_bias", "down_bias")
    for v, name in enumerate(names):
        for i in range(D // 128):
            getattr(near, name)[pl.ds(128 * i, 128)] = rows[VECTOR_ROWS + v * (D // 128) + i, :]
    near.first[...] = rows[0:K, :]
    near.second[...] = rows[SECOND_ROWS : SECOND_ROWS + H, :]
    table = rows[TABLE_ROWS : TABLE_ROWS + H, :]
    near.scale[...] = table[:ATOMS, HOT : HOT + ATOMS]
    near.shift[...] = table[ATOMS:, HOT : HOT + ATOMS]
    turned = square_turn(table)
    near.hop[...] = turned[:HOPS, :H]
    near.edge[...] = turned[HOPS : HOPS + EDGES, :H]
    lines = ("first_bias", "centers", "spreads")
    for i, name in enumerate(lines):
        getattr(near, name)[...] = rows[KERNEL_ROWS + i, :]
    for name in names + ("first", "second", "scale", "shift", "hop", "edge") + lines:
        store(getattr(near, name), getattr(far, name))
    for copy in stores:
        copy.wait()


def unpack(out_rows, in_rows, fsum, qsum, rows):
    tokens = out_rows.shape[0]
    vec, line, types = ((D,), f32), ((K,), f32), ((ATOMS, ATOMS), f32)
    shapes = (
        ((tokens, D), bf16), ((tokens, D), bf16), vec, vec, ((3, D, HALF_D), f32), ((HALF_D, D), f32), vec, vec,
        ((D, HALF_D), f32), vec, ((HALF_D, D), f32), vec, types, types, line, line, ((K, K), f32), line, ((H, K), f32),
        ((HOPS, H), f32), ((EDGES, H), f32),
    )
    anywhere = pl.BlockSpec(memory_space=pl.ANY)
    return pl.pallas_call(
        unpack_kernel,
        in_specs=[anywhere] * 5,
        out_specs=[anywhere] * len(shapes),
        out_shape=[jax.ShapeDtypeStruct(*item) for item in shapes],
        scratch_shapes=[pltpu.VMEM(*item) for item in shapes] + [
            pltpu.VMEM(fsum.shape, bf16), pltpu.VMEM(qsum.shape, bf16), pltpu.VMEM(rows.shape, f32),
            pltpu.SemaphoreType.DMA((15,)), pltpu.SemaphoreType.DMA((25,)),
        ],
        compiler_params=pltpu.CompilerParams(vmem_limit_bytes=VMEM_BYTES),
        name="unpack",
    )(out_rows, in_rows, fsum, qsum, rows)


def whole_weights(qkv_weight, up_weight, proj_weight, down_weight):
    columns = lambda w: jnp.stack(jnp.split(w, 2, axis=-1))
    rows = lambda w: jnp.stack(jnp.split(w, 2, axis=0))
    gather = lambda w, dim: lax.all_gather(w, "tp", axis=dim, tiled=True)
    return (
        columns(gather(qkv_weight.transpose(1, 0, 2), 2)), columns(gather(up_weight, 1)),
        rows(gather(proj_weight, 0)), rows(gather(down_weight, 0)),
    )


def sum_grads(fgrads, qgrads, small):
    total_f, total_q, rows = lax.psum((fgrads, qgrads, small), ("mol", "tp"))
    share = D // lax.axis_size("tp")
    at = lax.axis_index("tp") * share

    def columns(halves):
        return lax.dynamic_slice_in_dim(jnp.concatenate(list(halves), axis=-1), at, share, halves.ndim - 2)

    def rows_of(block):
        part = total_f[:, D * block : D * (block + 1)]
        sides = jnp.concatenate([part[:, :HALF_D], part[:, HALF_D:]], axis=2).reshape(D, D)
        return lax.dynamic_slice_in_dim(sides, at, share, 0)

    qkv = columns(total_q.reshape(2, D, 3, HALF_D)).transpose(1, 0, 2)
    return [v.astype(f32) for v in (qkv, columns(total_f[:, :D]), rows_of(1), rows_of(2))], rows


def body(
    mesh_shape,
    hidden_in, positions, atom_types, hop_counts, edge_types, lengths, branches,
    attn_gain, attn_shift, qkv_weight, proj_weight, ffn_gain, ffn_shift, up_weight, up_bias, down_weight, down_bias,
    kernel_scale, kernel_shift, centers, spreads, first_weight, first_bias, second_weight, hop_table, edge_table,
    cotangent,
):
    remote = mesh_shape["tp"] == 2 and mesh_shape["mol"] == 16 and branches.shape[0] == 8
    if remote:
        weights = (qkv_weight.transpose(1, 0, 2), up_weight, proj_weight, down_weight)
    else:
        weights = whole_weights(qkv_weight, up_weight, proj_weight, down_weight)
    arrays = dict(
        lengths=lengths, flags=branches.T, positions=positions, atoms=atom_types, hops=hop_counts.T,
        edges=edge_types.T, kernel_scale=kernel_scale, kernel_shift=kernel_shift, centers=centers, spreads=spreads,
        first_weight=first_weight, first_bias=first_bias, second_weight=second_weight.T, hop_table=hop_table,
        edge_table=edge_table, attn_gain=attn_gain, attn_shift=attn_shift, ffn_gain=ffn_gain, ffn_shift=ffn_shift,
        up_bias=up_bias, down_bias=down_bias, hidden=hidden_in, cotangent=cotangent,
        qkv=weights[0], up=weights[1], proj=weights[2], down=weights[3],
    )
    output, grad_input, sums = layer(remote, arrays)
    if remote:
        fsum, qsum, rows = sums
    else:
        big, rows = sum_grads(*sums)
        fsum, qsum = jnp.zeros((3 * D, HALF_D), bf16), jnp.zeros((D, 3 * HALF_D), bf16)
    output, grad_input, *grads = unpack(output, grad_input, fsum, qsum, rows)
    if not remote:
        grads[2], grads[6], grads[3], grads[8] = big
    grads[2] = grads[2].transpose(1, 0, 2)
    grads[16] = grads[16].T
    return (output, grad_input, *grads)


def solution(mesh):
    rows = P(("mol", "tp"), None)
    all_of = P()
    in_specs = (
        rows, P(None, ("mol", "tp")), P(("mol", "tp")), rows, rows, P("mol"), rows, all_of, all_of,
        P(None, None, "tp"), P("tp", None), all_of, all_of, P(None, "tp"), all_of, P("tp", None),
    ) + (all_of,) * 10 + (rows,)
    out_specs = (
        rows, rows, all_of, all_of, P(None, None, "tp"), P("tp", None), all_of, all_of, P(None, "tp"), all_of,
        P("tp", None),
    ) + (all_of,) * 10
    step = functools.partial(body, dict(mesh.shape))
    return jax.shard_map(step, mesh=mesh, in_specs=in_specs, out_specs=out_specs, check_vma=False)
```

```python
import functools
from types import SimpleNamespace

import jax
import jax.numpy as jnp
from jax import lax
from jax.experimental import pallas as pl
from jax.experimental.pallas import tpu as pltpu
from jax.sharding import PartitionSpec as P

D = 768
H = 32
HD = 24
FF = 768
K = 128
SLOT = 64
HALF = SLOT // 2
HALF_D = D // 2
PAIRS = SLOT * SLOT
HOPS = 16
EDGES = 8
ATOMS = 16
GROUP = 4
GROUPS = H // GROUP
HOT = 32

highest = lax.Precision.HIGHEST
neg_large = -1e30
root_tau = 2.5066282746310002
root_half = 0.7071067811865476
inv_root_tau = 0.3989422804014327
head_scale = HD ** (-0.5)
VMEM_BYTES = 62 * 1024 * 1024
TILE = 1024

SECOND_ROWS = K
TABLE_ROWS = SECOND_ROWS + H
KERNEL_ROWS = TABLE_ROWS + H
VECTOR_ROWS = KERNEL_ROWS + 8
SMALL_ROWS = 256

MESH = pl.DeviceIdType.MESH
f32 = jnp.float32
bf16 = jnp.bfloat16


def dot_nn(left, right, precision=None):
    return lax.dot_general(left, right, (((1,), (0,)), ((), ())), precision=precision, preferred_element_type=f32)


def dot_nt(left, right, precision=None):
    return lax.dot_general(left, right, (((1,), (1,)), ((), ())), precision=precision, preferred_element_type=f32)


def dot_tn(left, right, precision=None):
    return lax.dot_general(left, right, (((0,), (0,)), ((), ())), precision=precision, preferred_element_type=f32)


def iota(shape, dim):
    return lax.broadcasted_iota(jnp.int32, shape, dim)


def gelu_parts(values):
    size = jnp.abs(values)
    bell = jnp.exp(values * values * -0.5)
    denominator = 1.0 + (0.3275911 * root_half) * size
    t = pl.reciprocal(denominator, approx=True)
    series = 0.5 * 1.061405429
    for factor in (-1.453152027, 1.421413741, -0.284496736, 0.254829592):
        series = series * t + 0.5 * factor
    tail = series * t * bell
    gelu = jnp.maximum(values, 0.0) - size * tail
    outer = tail - size * (bell * inv_root_tau)
    return gelu, jnp.where(values >= 0.0, 1.0 - outer, outer)


def to_column(row):
    size = row.shape[1]
    same = iota((size, size), 0) == iota((size, size), 1)
    return jnp.sum(jnp.where(same, row, 0.0), axis=1, keepdims=True)


def half_swap(values):
    return pltpu.roll(values, 64, 1)


def low_lanes(rows):
    return iota((rows, 128), 1) < 64


def vmem(count):
    return [pl.BlockSpec(memory_space=pltpu.VMEM)] * count


def row_of(ref):
    return ref[...].reshape(1, ref.shape[0])


def place():
    mol = lax.axis_index("mol")
    return mol % 2, (mol // 2) % 2, mol // 4, lax.axis_index("tp")


def greet(peers):
    barrier = pltpu.get_barrier_semaphore()
    for peer in peers:
        pl.semaphore_signal(barrier, inc=1, device_id=peer, device_id_type=MESH)
    pl.semaphore_wait(barrier, len(peers))


def window(group):
    first = GROUP * HD * group
    start = first // 128 * 128
    width = 128 if first - start + GROUP * HD <= 128 else 256
    return start, width, first - start


def head_masks(group, kind):
    _, width, offset = window(group)
    lane = iota((1, width), 1)
    return [
        ((lane >= offset + HD * h) & (lane < offset + HD * (h + 1))).astype(f32).astype(kind) for h in range(GROUP)
    ]


def spread_heads(values, group):
    return jnp.concatenate([values * mask for mask in head_masks(group, bf16)], axis=0)


def gather_heads(values, group):
    masks = head_masks(group, f32)
    total = values[:SLOT] * masks[0]
    for h in range(1, GROUP):
        total = total + values[SLOT * h : SLOT * (h + 1)] * masks[h]
    return total


def standardize(values):
    centred = values - jnp.mean(values, axis=-1, keepdims=True)
    inv_std = lax.rsqrt(jnp.mean(centred * centred, axis=-1, keepdims=True) + 1e-05)
    return centred * inv_std, inv_std


def norm_back(d_normed, scaled, inv_std, gain):
    weighted = d_normed * gain
    inner_a = jnp.mean(weighted, axis=-1, keepdims=True)
    inner_b = jnp.mean(weighted * scaled, axis=-1, keepdims=True)
    return inv_std * (weighted - inner_a - scaled * inner_b)


def column_sum(values):
    return jnp.sum(values, axis=0, keepdims=True)


class Peers:
    def __init__(self):
        self.core, self.x, self.z, self.tp = place()
        mol = lax.axis_index("mol")
        self.over_core = {"mol": mol + 1 - 2 * self.core}
        self.over_x = {"mol": mol + 2 - 4 * self.x}
        self.over_tp = {"tp": 1 - self.tp}
        self.turn = [lax.rem(self.z + d, 4) for d in range(4)]
        self.over_z = [{"mol": self.turn[d] * 4 + self.x * 2 + self.core} for d in range(4)]

    def neighbour(self, k):
        core = self.core + (1 - 2 * self.core) * (k & 1)
        x = self.x + (1 - 2 * self.x) * (k >> 1 & 1)
        tp = self.tp + (1 - 2 * self.tp) * (k >> 2)
        return core * 4 + tp * 2 + x, {"mol": self.z * 4 + x * 2 + core, "tp": tp}

    def everyone(self):
        return [self.neighbour(k)[1] for k in range(1, 8)] + self.over_z[1:]


def span(start, size):
    return pl.ds(pl.multiple_of(start, size), size)


def add_rows(target, source, rows):
    step = 96 if rows % 96 == 0 else min(rows, 32)

    def piece(i, _):
        at = pl.ds(pl.multiple_of(i * step, step), step)
        target[at, :] = target[at, :] + source[at, :]
        return 0

    lax.fori_loop(0, rows // step, piece, 0)


class Reduction:
    kinds = 11

    def __init__(self, peers, part, total, from_core, from_tp, from_x, from_z, sends, recvs):
        self.peers, self.part, self.total = peers, part, total
        self.from_core, self.from_tp, self.from_x, self.from_z = from_core, from_tp, from_x, from_z
        self.sends, self.recvs = sends, recvs
        self.half = from_core.shape[2]
        self.quarter, self.least = self.half // 2, self.half // 8

    def rows(self, b, level):
        p = self.peers
        at = b * 2 * self.half + p.core * self.half
        if level > 0:
            at = at + p.x * self.quarter
        return at + p.z * self.least if level > 1 else at

    def copy(self, b, kind):
        p = self.peers
        part, total = self.part, self.total
        half, quarter, least = self.half, self.quarter, self.least
        if kind == 0:
            src = part.at[:, span(b * 2 * half + (1 - p.core) * half, half)]
            dst, peer = self.from_core.at[b], p.over_core
        elif kind == 1:
            src, dst, peer = part.at[1 - p.tp, span(self.rows(b, 0), half)], self.from_tp.at[b], p.over_tp
        elif kind == 2:
            src = part.at[p.tp, span(self.rows(b, 0) + (1 - p.x) * quarter, quarter)]
            dst, peer = self.from_x.at[b], p.over_x
        elif kind < 6:
            d = kind - 2
            src = part.at[p.tp, span(self.rows(b, 1) + p.turn[d] * least, least)]
            dst, peer = self.from_z.at[b, d - 1], p.over_z[d]
        elif kind < 9:
            src = dst = total.at[span(self.rows(b, 2), least)]
            peer = p.over_z[kind - 5]
        elif kind == 9:
            src = dst = total.at[span(self.rows(b, 1), quarter)]
            peer = p.over_x
        else:
            src = dst = total.at[span(self.rows(b, 0), half)]
            peer = p.over_core
        return pltpu.make_async_remote_copy(
            src_ref=src, dst_ref=dst, send_sem=self.sends.at[b, kind], recv_sem=self.recvs.at[b, kind],
            device_id=peer, device_id_type=MESH,
        )

    def act(self, b, stage):
        p = self.peers
        half, quarter, least = self.half, self.quarter, self.least
        part = self.part
        if stage == 0:
            self.copy(b, 0).start()
        elif stage == 1:
            self.copy(b, 0).wait_recv()
            at = span(self.rows(b, 0), half)
            add_rows(part.at[1 - p.tp, at], self.from_core.at[b, 1 - p.tp], half)
            self.copy(b, 1).start()
            add_rows(part.at[p.tp, at], self.from_core.at[b, p.tp], half)
        elif stage == 2:
            self.copy(b, 1).wait_recv()
            away, mine = (1 - p.x) * quarter, p.x * quarter
            at = self.rows(b, 0)
            add_rows(part.at[p.tp, span(at + away, quarter)], self.from_tp.at[b, span(away, quarter)], quarter)
            self.copy(b, 2).start()
            add_rows(part.at[p.tp, span(at + mine, quarter)], self.from_tp.at[b, span(mine, quarter)], quarter)
        elif stage == 3:
            self.copy(b, 2).wait_recv()
            add_rows(part.at[p.tp, span(self.rows(b, 1), quarter)], self.from_x.at[b], quarter)
            for kind in (3, 4, 5):
                self.copy(b, kind).start()
        elif stage == 4:
            for kind in (3, 4, 5):
                self.copy(b, kind).wait_recv()
            mine = span(self.rows(b, 2), least)
            value = part[p.tp, mine, :].astype(f32)
            for d in range(3):
                value = value + self.from_z[b, d].astype(f32)
            self.total[mine, :] = value.astype(bf16)
            for kind in (6, 7, 8):
                self.copy(b, kind).start()
        elif stage == 5:
            for kind in (6, 7, 8):
                self.copy(b, kind).wait_recv()
            self.copy(b, 9).start()
        elif stage == 6:
            self.copy(b, 9).wait_recv()
            self.copy(b, 10).start()
        elif stage == 7:
            self.copy(b, 10).wait_recv()
        else:
            for kind in range(self.kinds):
                self.copy(b, kind).wait_send()


class SmallReduction:
    def __init__(self, peers, part, total, from_near, from_z, sends, recvs):
        self.peers, self.part, self.total, self.from_near, self.from_z = peers, part, total, from_near, from_z
        self.sends, self.recvs = sends, recvs
        p = peers
        self.near = [p.neighbour(k) for k in range(8)]
        self.mine = span(self.near[0][0] * 32, 32)

    def copy(self, kind):
        p = self.peers
        if kind < 7:
            index, peer = self.near[kind + 1]
            src, dst = self.part.at[span(index * 32, 32)], self.from_near.at[kind]
        elif kind < 10:
            src = dst = self.from_z.at[p.z]
            peer = p.over_z[kind - 6]
        else:
            src = dst = self.total.at[self.mine]
            peer = self.near[kind - 9][1]
        return pltpu.make_async_remote_copy(
            src_ref=src, dst_ref=dst, send_sem=self.sends.at[kind], recv_sem=self.recvs.at[kind],
            device_id=peer, device_id_type=MESH,
        )

    def act(self, stage):
        hops = (range(0, 7), range(7, 10), range(10, 17))
        if stage == 4:
            for kind in range(17):
                self.copy(kind).wait_send()
            return
        if stage > 0:
            for kind in hops[stage - 1]:
                self.copy(kind).wait_recv()
        if stage == 1:
            value = self.part[self.mine, :]
            for k in range(7):
                value = value + self.from_near[k]
            self.from_z[self.peers.z] = value
        elif stage == 2:
            self.total[self.mine, :] = (self.from_z[0] + self.from_z[1]) + (self.from_z[2] + self.from_z[3])
        if stage < 3:
            for kind in hops[stage]:
                self.copy(kind).start()


def big_scratch(rows, lanes):
    half = rows // 2
    sems = pltpu.SemaphoreType.DMA((3, Reduction.kinds))
    return [
        pltpu.VMEM((3, 2, half, lanes), bf16), pltpu.VMEM((3, half, lanes), bf16),
        pltpu.VMEM((3, half // 2, lanes), bf16), pltpu.VMEM((3, 3, half // 8, lanes), bf16), sems, sems,
    ]


def small_scratch():
    return [
        pltpu.VMEM((7, 32, 128), f32), pltpu.VMEM((4, 32, 128), f32),
        pltpu.SemaphoreType.DMA((17,)), pltpu.SemaphoreType.DMA((17,)),
    ]


class Gather:
    pieces = 6

    def __init__(self, peers, whole, sends, recvs):
        self.peers, self.whole, self.sends, self.recvs = peers, whole, sends, recvs
        self.quarter = peers.x * 2 + peers.core
        self.next_quarter = (1 - peers.x) * 2 + peers.core

    def rows(self, ref, quarter):
        count = ref.shape[0] // 4
        return ref.at[span(quarter * count, count), :]

    def copy(self, index, kind):
        p = self.peers
        if kind == 0:
            src = dst = self.rows(self.whole(index, p.tp), self.quarter)
            peer = p.over_tp
        elif kind == 1:
            src = dst = self.rows(self.whole(index, 1 - p.tp), self.quarter)
            peer = p.over_x
        else:
            src = dst = self.rows(self.whole(index, 1 - p.tp), self.quarter if kind == 2 else self.next_quarter)
            peer = p.over_core
        return pltpu.make_async_remote_copy(
            src_ref=src, dst_ref=dst, send_sem=self.sends.at[index, kind], recv_sem=self.recvs.at[index, kind],
            device_id=peer, device_id_type=MESH,
        )

    def start(self, indices):
        for index in indices:
            self.copy(index, 0).start()

    def onward_x(self, index):
        self.copy(index, 0).wait_recv()
        self.copy(index, 1).start()
        self.copy(index, 2).start()

    def onward_core(self, index):
        self.copy(index, 1).wait_recv()
        self.copy(index, 3).start()

    def arrive(self, index):
        self.copy(index, 2).wait_recv()
        self.copy(index, 3).wait_recv()

    def finish(self):
        for index in range(self.pieces):
            for kind in range(4):
                self.copy(index, kind).wait_send()


def square_turn(values):
    rows, lanes = values.shape
    if lanes < 128:
        values = jnp.concatenate([values, jnp.zeros((rows, 128 - lanes), f32)], axis=1)
    if rows < 128:
        values = jnp.concatenate([values, jnp.zeros((128 - rows, 128), f32)], axis=0)
    return values.T


def widen(values):
    return jnp.concatenate([values] * (TILE // 128), axis=1)


def strips():
    return [slice(16 * i, 16 * (i + 1)) for i in range(K // 16)]


def four_rows(ref, slot, first):
    return jnp.concatenate([ref[slot, pl.ds(first + i, 1), :] for i in range(TILE // 128)], axis=1)


def hot_rows(values, count):
    return (values == iota((count, TILE), 0).astype(f32)).astype(f32)


def fold_lanes(values):
    total = values[:, :128]
    for i in range(1, TILE // 128):
        total = total + values[:, 128 * i : 128 * (i + 1)]
    return total


def twice(ref, values):
    none = jnp.zeros_like(values)
    ref[...] = jnp.concatenate(
        [jnp.concatenate([values, none], axis=1), jnp.concatenate([none, values], axis=1)], axis=0
    ).astype(bf16)


def dot_halves(weights, pieces):
    values = jnp.concatenate(pieces, axis=0)
    half = TILE // 2
    both = dot_nn(weights, jnp.concatenate([values[:, :half], values[:, half:]], axis=0))
    rows = both.shape[0] // 2
    return jnp.concatenate([both[:rows], both[rows:]], axis=1)


def prepare_pairs(r):
    spr = to_column(row_of(r.spreads))
    r.cols[0] = jnp.broadcast_to(to_column(row_of(r.centers)), (K, 128))
    r.cols[1] = jnp.broadcast_to(root_half / spr, (K, 128))
    r.cols[2] = jnp.broadcast_to(-jnp.log(root_tau * spr), (K, 128))
    r.cols[3] = jnp.broadcast_to(to_column(row_of(r.first_bias)), (K, 128))
    r.cols[4] = jnp.broadcast_to(1.0 / spr, (K, 128))
    twice(r.w1, r.first_weight[...].astype(f32))
    twice(r.w1t, r.first_weight[...].astype(f32).T)
    r.w2[...] = square_turn(r.second_weight[...].astype(f32))
    table = jnp.concatenate([r.hop_table[...], r.edge_table[...], jnp.zeros((128 - HOPS - EDGES, H), f32)], axis=0)
    table = jnp.concatenate([table, jnp.zeros((128, 128 - H), f32)], axis=1).T[:H, :HOT]
    one = table.astype(bf16).astype(f32)
    r.base[...] = jnp.concatenate(
        [r.second_weight[...].astype(f32), one, table - one, jnp.zeros((H, 64), f32)], axis=1
    )


def bf16_parts(values, count):
    parts = []
    for _ in range(count):
        parts.append(values.astype(bf16))
        values = values - parts[-1].astype(f32)
    return parts


def pair_tables(r, slots):
    low = low_lanes(HALF)
    low_row = low_lanes(1)
    tables = [part.astype(f32) for ref in (r.kernel_scale, r.kernel_shift) for part in bf16_parts(ref[...], 3)]
    tables = jnp.concatenate([square_turn(part)[:ATOMS, :ATOMS] for part in tables], axis=1)
    tables = jnp.concatenate([tables, jnp.zeros((ATOMS, 128 - 6 * ATOMS), f32)], axis=1).astype(bf16)
    for group in range(slots // 2):
        lanes = slice(128 * group, 128 * (group + 1))
        atoms = r.atoms[lanes].astype(f32).reshape(1, 128)
        rows = jnp.concatenate([r.positions[:, lanes], atoms, jnp.zeros((4, 128), f32)], axis=0)
        columns = square_turn(rows)
        key_hot = (columns[:, 3:4] == iota((128, ATOMS), 1).astype(f32)).astype(f32).astype(bf16)
        picks = dot_nn(key_hot, tables).astype(bf16)
        turned = half_swap(rows)
        for s in range(2):
            slot = 2 * group + s
            tokens = slice(SLOT * s, SLOT * (s + 1))
            double = jnp.where(low_lanes(8), *((rows, turned) if s == 0 else (turned, rows)))
            total = None
            for c in range(3):
                column = columns[tokens, c : c + 1]
                offset = jnp.where(low, column[:HALF], column[HALF:]) - double[c : c + 1]
                total = offset * offset if total is None else total + offset * offset
            distance = jnp.sqrt(total)
            query_hot = (double[3:4] == iota((ATOMS, 128), 0).astype(f32)).astype(f32)
            three, none = [query_hot] * 3, [jnp.zeros((3 * ATOMS, 128), f32)]
            rest = [jnp.zeros((128 - 6 * ATOMS, 128), f32)]
            spread = jnp.concatenate(
                [jnp.concatenate(three + none + rest, axis=0), jnp.concatenate(none + three + rest, axis=0)], axis=1
            )
            both = dot_nn(picks[tokens], spread.astype(bf16))
            scale = jnp.where(low, both[:HALF, :128], both[HALF:, :128])
            shift = jnp.where(low, both[:HALF, 128:], both[HALF:, 128:])
            r.argument[slot] = scale * distance + shift
            r.distance[slot] = distance
            for source, target in ((r.hops, r.hop_rows), (r.edges, r.edge_rows)):
                values = source[:, lanes].astype(f32)
                top, bottom = values[:HALF], values[HALF:]
                if s == 0:
                    target[slot] = jnp.where(low, top, half_swap(bottom))
                else:
                    target[slot] = jnp.where(low, half_swap(top), bottom)
            r.atom_rows[slot] = jnp.broadcast_to(double[3:4], (8, 128))


def table_grads(r, slots):
    lefts, rights = [], []
    for slot in range(slots):
        query_hot = (r.atom_rows[slot, 0:1, :] == iota((ATOMS, 128), 0).astype(f32)).astype(f32)
        keys = jnp.concatenate([query_hot[:, :HALF], query_hot[:, HALF:SLOT]], axis=0)
        keys = jnp.concatenate([keys, keys], axis=1).astype(bf16)
        values = jnp.concatenate([r.dargs[slot] * r.distance[slot], r.dargs[slot]], axis=1)
        both = dot_nn(keys, jnp.concatenate(bf16_parts(values, 2), axis=0))
        low = low_lanes(ATOMS)
        for index in range(2):
            lanes = slice(128 * index, 128 * (index + 1))
            rights.append(bf16_parts(jnp.where(low, both[:ATOMS, lanes], both[ATOMS:, lanes]), 2))
        lefts.append(query_hot.astype(bf16))
    left = jnp.concatenate(lefts, axis=1)
    right = jnp.concatenate(
        [jnp.concatenate([rights[2 * s + index][part] for s in range(slots)], axis=1) for index in range(2) for part in range(2)],
        axis=0,
    )
    result = dot_nt(left, right)
    return [
        result[:, 2 * ATOMS * index : 2 * ATOMS * index + ATOMS] + result[:, 2 * ATOMS * index + ATOMS : 2 * ATOMS * (index + 1)]
        for index in range(2)
    ]


def in_stages(stages, count):
    held = {}
    for time in range(count + len(stages) - 1):
        for k, stage in reversed(list(enumerate(stages))):
            if 0 <= time - k < count:
                held[time - k] = stage(time - k, held.get(time - k))


TILES = PAIRS // TILE
ROWS = TILE // 128


def pair_forward(r, slot):
    bank = lax.rem(slot, 2)
    graph_on = r.flags[0, slot].astype(f32)
    space_on = r.flags[1, slot].astype(f32)
    factor = jnp.where(iota((H, 256), 1) < K, space_on, graph_on)
    r.lhs[...] = (r.base[...] * factor).astype(bf16)

    def kernels(tile, _):
        where = slice(tile * TILE, (tile + 1) * TILE)
        arg = four_rows(r.argument, slot, tile * ROWS)
        pieces = []
        for rows in strips():
            u = (arg - widen(r.cols[0, rows])) * widen(r.cols[1, rows])
            pieces.append(jnp.exp(widen(r.cols[2, rows]) - u * u).astype(bf16))
            r.left[bank, rows, where] = pieces[-1]
        return dot_halves(r.w1t[...], pieces)

    def hidden(tile, first):
        where = slice(tile * TILE, (tile + 1) * TILE)
        pieces = []
        for rows in strips():
            value, slope = gelu_parts(first[rows] + widen(r.cols[3, rows]))
            pieces.append(value.astype(bf16))
            r.left[bank, slice(K + rows.start, K + rows.stop), where] = pieces[-1]
            r.slope[bank, rows, where] = slope.astype(bf16)
        hot = jnp.concatenate(
            [
                hot_rows(four_rows(r.hop_rows, slot, tile * ROWS), HOPS),
                hot_rows(four_rows(r.edge_rows, slot, tile * ROWS), HOT - HOPS),
            ],
            axis=0,
        ).astype(bf16)
        return dot_nn(r.lhs[:, : K + 2 * HOT], jnp.concatenate(pieces + [hot] * 2, axis=0))

    def biases(tile, bias):
        bias = bias.astype(bf16).astype(f32)
        for i in range(ROWS):
            r.bias[slot, pl.ds(tile * ROWS + i, H, stride=HALF), :] = bias[:, 128 * i : 128 * (i + 1)]

    in_stages([kernels, hidden, biases], TILES)


def pair_backward(r, slot, between):
    bank = lax.rem(slot, 2)
    graph_on = r.flags[0, slot].astype(f32)
    space_on = r.flags[1, slot].astype(f32)
    twice(r.w2_twice, r.w2[:, :H] * space_on)

    def scores(tile, _):
        where = slice(tile * TILE, (tile + 1) * TILE)
        grad = jnp.concatenate(
            [r.bias[slot, pl.ds(tile * ROWS + i, H, stride=HALF), :] for i in range(ROWS)], axis=1
        )
        r.right[K:, where] = jnp.concatenate([grad * space_on, grad * graph_on], axis=0).astype(bf16)
        edge_hot = hot_rows(four_rows(r.edge_rows, slot, tile * ROWS), HOT - HOPS)
        edge_hot = jnp.where(iota((HOT - HOPS, TILE), 0) == EDGES, 1.0, edge_hot)
        r.left[bank, 2 * K :, where] = jnp.concatenate(
            [hot_rows(four_rows(r.hop_rows, slot, tile * ROWS), HOPS), edge_hot], axis=0
        ).astype(bf16)
        return dot_halves(r.w2_twice[...], [grad.astype(bf16)])

    def hidden(tile, d_second):
        where = slice(tile * TILE, (tile + 1) * TILE)
        pieces = []
        for rows in strips():
            pieces.append((d_second[rows] * r.slope[bank, rows, where].astype(f32)).astype(bf16))
            r.right[rows, where] = pieces[-1]
        return dot_halves(r.w1[...], pieces)

    def kernels(tile, d_gauss):
        where = slice(tile * TILE, (tile + 1) * TILE)
        arg = four_rows(r.argument, slot, tile * ROWS)
        d_arg = None
        for rows in strips():
            inv = widen(r.cols[4, rows])
            u = (arg - widen(r.cols[0, rows])) * inv
            q = d_gauss[rows] * r.left[bank, rows, where].astype(f32)
            w = q * u
            r.sums[0, rows] += fold_lanes(w)
            r.sums[1, rows] += fold_lanes(w * u - q)
            w = w * inv
            w = w[:8] + w[8:]
            d_arg = w if d_arg is None else d_arg + w
        d_arg = -jnp.sum(d_arg, axis=0, keepdims=True)
        for i in range(ROWS):
            at = tile * ROWS + i
            r.dargs[slot, at : at + 1, :] = d_arg[:, 128 * i : 128 * (i + 1)]

    in_stages([scores, hidden, kernels], TILES)
    between()
    r.acc_mixed[...] += dot_nt(r.left[bank], r.right[...])


def attend(r, s, first_slot):
    low = low_lanes(HALF)
    rows = span(s * SLOT, SLOT)
    valid = iota((SLOT, GROUP * SLOT), 0) < r.lengths[first_slot + s]
    r.work[0] = jnp.zeros((SLOT, D), f32)
    for g in range(GROUPS):
        start, width, _ = window(g)
        q = r.joined[rows, start : start + width]
        k = r.joined[rows, D + start : D + start + width]
        v = r.joined[rows, 2 * D + start : 2 * D + start + width]
        scores = dot_nt(k, spread_heads(q, g)) * head_scale
        parts = []
        for pair in range(GROUP // 2):
            head = GROUP * g + 2 * pair
            one = r.bias[s, head * HALF : (head + 1) * HALF, :]
            two = r.bias[s, (head + 1) * HALF : (head + 2) * HALF, :]
            top = jnp.where(low, one, half_swap(two))
            bottom = jnp.where(low, half_swap(one), two)
            parts.append(jnp.concatenate([top, bottom], axis=0))
        scores = jnp.where(valid, scores + jnp.concatenate(parts, axis=1), neg_large)
        weights = jnp.exp(scores - jnp.max(scores, axis=0, keepdims=True))
        prob = (weights * (1.0 / jnp.sum(weights, axis=0, keepdims=True))).astype(bf16)
        r.prob[s, :, g * GROUP * SLOT : (g + 1) * GROUP * SLOT] = prob
        r.work[0, :, start : start + width] += gather_heads(dot_tn(prob, v), g)
    r.attended[rows, :] = r.work[0].astype(bf16)


def attend_back(r, s):
    low = low_lanes(HALF)
    rows = span(s * SLOT, SLOT)
    r.work[...] = jnp.zeros((3, SLOT, D), f32)
    for g in range(GROUPS):
        start, width, _ = window(g)
        lanes = slice(start, start + width)
        k = r.joined[rows, D + start : D + start + width]
        v = r.joined[rows, 2 * D + start : 2 * D + start + width]
        q_heads = spread_heads(r.joined[rows, lanes], g)
        d_heads = spread_heads(r.d_attended[rows, lanes], g)
        prob = r.prob[s, :, g * GROUP * SLOT : (g + 1) * GROUP * SLOT]
        wide = prob.astype(f32)
        d_prob = dot_nt(v, d_heads)
        inner = jnp.sum(wide * d_prob, axis=0, keepdims=True)
        d_scores = (wide * (d_prob - inner)).astype(bf16)
        r.work[0, :, lanes] += gather_heads(dot_tn(d_scores, k), g)
        r.work[1, :, lanes] += dot_nn(d_scores, q_heads)
        r.work[2, :, lanes] += dot_nn(prob, d_heads)
        d_wide = d_scores.astype(f32)
        for pair in range(GROUP // 2):
            head = GROUP * g + 2 * pair
            top = d_wide[:HALF, 128 * pair : 128 * (pair + 1)]
            bottom = d_wide[HALF:, 128 * pair : 128 * (pair + 1)]
            r.bias[s, head * HALF : (head + 1) * HALF, :] = jnp.where(low, top, half_swap(bottom))
            r.bias[s, (head + 1) * HALF : (head + 2) * HALF, :] = jnp.where(low, half_swap(top), bottom)
    r.joined[rows, 0:D] = (r.work[0] * head_scale).astype(bf16)
    r.joined[rows, D : 2 * D] = (r.work[1] * head_scale).astype(bf16)
    r.joined[rows, 2 * D : 3 * D] = r.work[2].astype(bf16)


def project(r, rows):
    scaled, _ = standardize(r.hidden[rows, :].astype(f32))
    normed = (scaled * row_of(r.attn_gain) + row_of(r.attn_shift)).astype(bf16)
    r.normed_a[rows, :] = normed
    for m in range(3):
        for t in range(2):
            at = m * D + t * HALF_D
            r.joined[rows, at : at + HALF_D] = dot_nn(normed, r.wqkv[t, m]).astype(bf16)


def feed(r, rows):
    halves = [slice(0, HALF_D), slice(HALF_D, D)]
    resid = r.hidden[rows, :].astype(f32)
    for t in range(2):
        resid = resid + dot_nn(r.attended[rows, halves[t]], r.wproj[t])
    scaled, inv_std = standardize(resid)
    normed = (scaled * row_of(r.ffn_gain) + row_of(r.ffn_shift)).astype(bf16)
    r.normed_f[rows, :] = normed
    pre = jnp.concatenate([dot_nn(normed, r.wup[t]) for t in range(2)], axis=1)
    value, slope = gelu_parts(pre + row_of(r.up_bias))
    active = value.astype(bf16)
    r.activated[rows, :] = active
    result = resid + row_of(r.down_bias)
    for t in range(2):
        result = result + dot_nn(active[:, halves[t]], r.wdown[t])
    r.out_rows[rows, :] = result.astype(bf16)
    cot = r.cotangent[rows, :]
    cot_wide = cot.astype(f32)
    d_active = jnp.concatenate([dot_nt(cot, r.wdown[t]) for t in range(2)], axis=1)
    d_hidden = (d_active * slope).astype(bf16)
    r.d_pre[rows, :] = d_hidden
    d_normed = dot_nt(d_hidden[:, halves[0]], r.wup[0]) + dot_nt(d_hidden[:, halves[1]], r.wup[1])
    d_resid = cot_wide + norm_back(d_normed, scaled, inv_std, row_of(r.ffn_gain))
    r.d_resid[rows, :] = d_resid
    branch = d_resid.astype(bf16)
    r.d_branch[rows, :] = branch
    for t in range(2):
        r.d_attended[rows, halves[t]] = dot_nt(branch, r.wproj[t]).astype(bf16)
    r.vectors[2:3, :] += column_sum(d_normed * scaled)
    r.vectors[3:4, :] += column_sum(d_normed)
    r.vectors[4:5, :] += column_sum(d_hidden.astype(f32))
    r.vectors[5:6, :] += column_sum(cot_wide)


def feed_grads(r, block):
    halves = [slice(0, HALF_D), slice(HALF_D, D)]
    if block == 0:
        grad = dot_tn(r.normed_f[...], r.d_pre[...]).astype(bf16)
        for t in range(2):
            r.fpart[t, :D, :] = grad[:, halves[t]]
        return
    left, right = (r.attended, r.d_branch) if block == 1 else (r.activated, r.cotangent)
    for t in range(2):
        grad = dot_tn(left[:, halves[t]], right[...]).astype(bf16)
        for side in range(2):
            r.fpart[t, D * block + HALF_D * side : D * block + HALF_D * (side + 1), :] = grad[:, halves[side]]


def qkv_grads(r, block):
    rows = slice(256 * block, 256 * (block + 1))
    for m in range(3):
        grad = dot_tn(r.normed_a[:, rows], r.joined[:, m * D : (m + 1) * D]).astype(bf16)
        for t in range(2):
            r.qpart[t, rows, m * HALF_D : (m + 1) * HALF_D] = grad[:, t * HALF_D : (t + 1) * HALF_D]


def finish_input(r, rows):
    d_normed = None
    for m in range(3):
        for t in range(2):
            at = m * D + t * HALF_D
            term = dot_nt(r.joined[rows, at : at + HALF_D], r.wqkv[t, m])
            d_normed = term if d_normed is None else d_normed + term
    scaled, inv_std = standardize(r.hidden[rows, :].astype(f32))
    grad = r.d_resid[rows, :] + norm_back(d_normed, scaled, inv_std, row_of(r.attn_gain))
    r.in_rows[rows, :] = grad.astype(bf16)
    r.vectors[0:1, :] += column_sum(d_normed * scaled)
    r.vectors[1:2, :] += column_sum(d_normed)


def pack_small(r, slots):
    tables = table_grads(r, slots)
    for v in range(6):
        for i in range(D // 128):
            at = VECTOR_ROWS + v * (D // 128) + i
            r.spart[at : at + 1, :] = r.vectors[v : v + 1, 128 * i : 128 * (i + 1)]
    r.spart[0:K, :] = r.acc_mixed[0:K, :K]
    r.spart[SECOND_ROWS : SECOND_ROWS + H, :] = square_turn(r.acc_mixed[K : 2 * K, K:])[:H]
    r.spart[TABLE_ROWS : TABLE_ROWS + H, :HOT] = square_turn(r.acc_mixed[2 * K :, K:])[H : 2 * H, :HOT]
    for index in range(2):
        rows = slice(TABLE_ROWS + ATOMS * index, TABLE_ROWS + ATOMS * (index + 1))
        r.spart[rows, HOT : HOT + ATOMS] = tables[index]
    ones = 2 * K + HOPS + EDGES
    r.spart[KERNEL_ROWS : KERNEL_ROWS + 1, :] = r.acc_mixed[ones : ones + 1, :K]
    for index in range(2):
        column = jnp.sum(r.sums[index] * r.cols[4], axis=1, keepdims=True)
        same = iota((K, K), 0) == iota((K, K), 1)
        at = KERNEL_ROWS + 1 + index
        r.spart[at : at + 1, :] = jnp.sum(jnp.where(same, column, 0.0), axis=0, keepdims=True)


class Stage:
    def __init__(self, names, near_inputs, carried, refs):
        self.r = SimpleNamespace(**dict(zip(names, refs)))
        r = self.r
        self.loads = {
            name: pltpu.make_async_copy(getattr(r, "given_" + name), getattr(r, name), r.input_sems.at[i])
            for i, name in enumerate(near_inputs)
        }
        self.stores = {
            name: pltpu.make_async_copy(getattr(r, name), getattr(r, name + "_far"), r.carry_sems.at[i])
            for i, name in enumerate(carried)
        }

    def load(self, *names):
        for name in names:
            self.loads[name].start()

    def need(self, *names):
        for name in names:
            self.loads[name].wait()

    def store(self, *names):
        for name in names:
            self.stores[name].start()

    def stored(self):
        for copy in self.stores.values():
            copy.wait()


def each_chunk(r, tokens, work):
    chunk = min(256, tokens)

    def one(c, _):
        work(r, span(c * chunk, chunk))
        return 0

    lax.fori_loop(0, tokens // chunk, one, 0)


def pair_moves(r, slot, back):
    bank = lax.rem(slot, 2)
    both = (r.left_far.at[slot], r.left.at[bank, : 2 * K]), (r.slope_far.at[slot], r.slope.at[bank])
    for index, (far, near) in enumerate(both):
        yield pltpu.make_async_copy(*((far, near) if back else (near, far)), r.pair_sems.at[bank, index])


def start_moves(r, slot, back):
    for copy in pair_moves(r, slot, back):
        copy.start()


def wait_moves(r, slot, back):
    for copy in pair_moves(r, slot, back):
        copy.wait()


def run(steps):
    for act, *where in steps:
        act(*where)


def at_time(index, plan):
    for k, steps in plan.items():
        pl.when(index == k)(functools.partial(run, steps))


FFN_BACK = {0: [(1, 1), (2, 1)], 3: [(0, 2)], 7: [(0, 3), (1, 2)]}
AFTER_GRADS = ([(0, 4), (1, 3), (2, 2)], [(0, 1), (1, 1), (2, 1)])
AFTER_HALF = ([(0, 5)], [])
AFTER_INPUT = ([(2, 3), (1, 4)], [(0, 2)])
FFN_PAIRS = {
    0: [(0, 6)], 2: [(2, 4)], 3: [(1, 5), (0, 7)], 5: [(2, 5)], 7: [(1, 6)], 9: [(2, 6)], 10: [(1, 7)], 12: [(2, 7)],
}
QKV_PAIRS = {
    2: [(0, 3)], 3: [(1, 2)], 6: [(1, 3), (2, 2), (0, 4)], 9: [(1, 4)], 10: [(0, 5)], 11: [(2, 3)], 12: [(1, 5)],
    13: [(0, 6)], 14: [(2, 4)], 15: [(1, 6)],
}


def layer_kernel(remote, names, near_inputs, carried, *refs):
    stage = Stage(names, near_inputs, carried, refs)
    r = stage.r
    stage.load(*[name for name in near_inputs if name not in ("hidden", "cotangent")])
    tokens = r.hidden.shape[0]
    slots = tokens // SLOT
    peers = Peers()
    whole = [r.wqkv, r.wup, r.wproj, r.wdown]
    given = [r.given_qkv, r.given_up, r.given_proj, r.given_down]
    targets = [w.at[peers.tp] for w in whole] if remote else whole
    loads = [
        pltpu.make_async_copy(src, dst, r.load_sems.at[i]) for i, (src, dst) in enumerate(zip(given, targets))
    ]
    for load in loads:
        load.start()
    stage.load("hidden", "cotangent")
    gather_plan = {}
    if remote:

        def whole_piece(index, tp):
            return whole[0].at[tp, index] if index < 3 else whole[index - 2].at[tp]

        gather = Gather(peers, whole_piece, r.gather_sends, r.gather_recvs)
        ffn = Reduction(peers, r.fpart, r.ftotal, r.f_core, r.f_tp, r.f_x, r.f_z, r.f_sends, r.f_recvs)
        qkv = Reduction(peers, r.qpart, r.qtotal, r.q_core, r.q_tp, r.q_x, r.q_z, r.q_sends, r.q_recvs)
        small = SmallReduction(peers, r.spart, r.stotal, r.s_near, r.s_z, r.s_sends, r.s_recvs)
        greet(peers.everyone())
        for load, indices in zip(loads, ((0, 1, 2), (3,), (4,), (5,))):
            load.wait()
            gather.start(indices)
        x, core = gather.onward_x, gather.onward_core
        gather_plan = {
            0: [(x, 0)], 1: [(x, 1), (core, 0)], 2: [(x, 2), (core, 1)], 3: [(x, 3), (core, 2)],
            4: [(x, 4), (core, 3), (x, 5)], 5: [(core, 4)], 6: [(core, 5)],
        }

    def leave(which, block):
        near, far = ((r.ftotal, r.ftotal_far), (r.qtotal, r.qtotal_far))[which]
        rows = near.shape[0] // 3
        at = slice(block * rows, (block + 1) * rows)
        return pltpu.make_async_copy(near.at[at], far.at[at], r.leave_sems.at[3 * which + block])

    def advance(which, actions):
        if remote:
            for block, step in actions:
                (ffn, qkv)[which].act(block, step)
                if step == 7:
                    leave(which, block).start()

    def plan_of(*plans):
        times = sorted(set().union(*plans)) if remote else []
        return {
            k: [(advance, which, plan[k]) for which, plan in enumerate(plans) if k in plan] for k in times
        }

    stage.need(*[name for name in near_inputs if name not in ("hidden", "cotangent")])
    prepare_pairs(r)
    pair_tables(r, slots)

    def pairs(slot, _):
        pl.when(slot >= 2)(lambda: wait_moves(r, slot - 2, False))
        pair_forward(r, slot)
        start_moves(r, slot, False)
        at_time(slot, gather_plan)
        return 0

    lax.fori_loop(0, slots, pairs, 0)
    stage.need("hidden")
    if remote:
        for index in range(3):
            gather.arrive(index)
    else:
        for load in loads:
            load.wait()
    each_chunk(r, tokens, project)
    first_slot = peers.tp * slots

    def attend_one(s, _):
        attend(r, s, first_slot)
        return 0

    lax.fori_loop(0, slots, attend_one, 0)
    stage.need("cotangent")
    if remote:
        for index in range(3, 6):
            gather.arrive(index)
    r.vectors[...] = jnp.zeros_like(r.vectors)
    each_chunk(r, tokens, feed)
    stage.store("out_rows")
    for slot in (slots - 2, slots - 1):
        wait_moves(r, slot, False)
    start_moves(r, 0, True)
    start_moves(r, 1, True)
    for block in range(3):
        feed_grads(r, block)
        advance(0, [(block, 0)])
    advance(0, [(0, 1)])

    back_plan, pair_plan = plan_of(FFN_BACK), plan_of(FFN_PAIRS, QKV_PAIRS)

    def back_one(s, _):
        attend_back(r, s)
        at_time(s, back_plan)
        return 0

    lax.fori_loop(0, slots, back_one, 0)
    for block in range(3):
        qkv_grads(r, block)
        advance(1, [(block, 0)])
    for which in range(2):
        advance(which, AFTER_GRADS[which])
    each_chunk(r, tokens, finish_input)
    stage.store("in_rows")
    for which in range(2):
        advance(which, AFTER_HALF[which] + AFTER_INPUT[which])
    for ref in (r.sums, r.acc_mixed, r.spart):
        ref[...] = jnp.zeros_like(ref)

    def pairs_back(slot, _):
        wait_moves(r, slot, True)
        pair_backward(r, slot, lambda: at_time(2 * slot, pair_plan))
        pl.when(slot + 2 < slots)(lambda: start_moves(r, slot + 2, True))
        at_time(2 * slot + 1, pair_plan)
        return 0

    lax.fori_loop(0, slots, pairs_back, 0)
    pack_small(r, slots)
    if remote:
        small.act(0)
        advance(1, [(2, 5), (0, 7)])
        small.act(1)
        advance(1, [(1, 7)])
        advance(1, [(2, 6)])
        small.act(2)
        advance(1, [(2, 7)])
        small.act(3)
        rows = pltpu.make_async_copy(r.stotal, r.stotal_far, r.leave_sems.at[6])
        rows.start()
        for which in range(2):
            advance(which, [(b, 8) for b in range(3)])
        small.act(4)
        gather.finish()
        for which in range(2):
            for block in range(3):
                leave(which, block).wait()
        rows.wait()
    else:
        stage.store("fpart", "qpart", "spart")
    stage.stored()


def call_stage(kernel, name, remote, collective, arrays, scalars, far, outs, carried, scratch):
    vm, sem = pltpu.VMEM, pltpu.SemaphoreType.DMA
    near = {n: vm(a.shape, a.dtype) for n, a in arrays.items() if n not in scalars + far}
    in_names = [n if n in scalars or n.endswith("_far") else "given_" + n for n in arrays]
    results = outs | {n + "_far": item for n, item in carried.items()}
    scratch = near | {n: vm(*item) for n, item in carried.items()} | scratch
    scratch |= {"input_sems": sem((len(near),)), "carry_sems": sem((len(carried),))}
    names = in_names + list(results) + list(scratch)
    values = pl.pallas_call(
        functools.partial(kernel, remote, names, list(near), list(carried)),
        in_specs=[pl.BlockSpec(memory_space=pltpu.SMEM if n in scalars else pl.ANY) for n in arrays],
        out_specs=[pl.BlockSpec(memory_space=pl.ANY)] * len(results),
        out_shape=[jax.ShapeDtypeStruct(*item) for item in results.values()],
        scratch_shapes=list(scratch.values()),
        compiler_params=pltpu.CompilerParams(
            vmem_limit_bytes=VMEM_BYTES, **(dict(collective_id=collective, has_side_effects=True) if remote else {})
        ),
        name=name,
    )(*arrays.values())
    return dict(zip(results, values))


def layer(remote, arrays):
    tokens = arrays["hidden"].shape[0]
    slots = tokens // SLOT
    v, sem = pltpu.VMEM, pltpu.SemaphoreType.DMA
    of_tokens = (tokens, D)
    table = (slots, HALF, 128)
    fshape, qshape, sshape = (3 * D, HALF_D), (D, 3 * HALF_D), (SMALL_ROWS, 128)
    outs = {"left_far": ((slots, 2 * K, PAIRS), bf16), "slope_far": ((slots, K, PAIRS), bf16)}
    carried = {"out_rows": (of_tokens, bf16), "in_rows": (of_tokens, bf16)}
    scratch = {
        "wqkv": v((2, 3, D, HALF_D), bf16), "wup": v((2, D, HALF_D), bf16), "wproj": v((2, HALF_D, D), bf16),
        "wdown": v((2, HALF_D, D), bf16), "load_sems": sem((4,)), "pair_sems": sem((2, 2)),
        "left": v((2, 2 * K + HOT, PAIRS), bf16), "slope": v((2, K, PAIRS), bf16),
        "right": v((K + 2 * H, PAIRS), bf16), "cols": v((5, K, 128), f32), "w1": v((2 * K, 2 * K), bf16), "w1t": v((2 * K, 2 * K), bf16),
        "w2": v((K, 128), f32), "w2_twice": v((2 * K, 2 * H), bf16), "base": v((H, 256), f32), "lhs": v((H, 256), bf16),
        "argument": v(table, f32), "distance": v(table, f32), "hop_rows": v(table, f32), "edge_rows": v(table, f32),
        "atom_rows": v((slots, 8, 128), f32), "dargs": v(table, f32), "bias": v((slots, H * HALF, 128), f32),
        "work": v((3, SLOT, D), f32), "normed_a": v(of_tokens, bf16), "joined": v((tokens, 3 * D), bf16),
        "prob": v((slots, SLOT, H * SLOT), bf16), "attended": v(of_tokens, bf16), "normed_f": v(of_tokens, bf16),
        "activated": v(of_tokens, bf16), "d_pre": v(of_tokens, bf16), "d_branch": v(of_tokens, bf16),
        "d_attended": v(of_tokens, bf16), "d_resid": v(of_tokens, f32), "vectors": v((8, D), f32),
        "sums": v((2, K, 128), f32), "acc_mixed": v((2 * K + HOT, K + 2 * H), f32),
    }
    parts = {"fpart": ((2,) + fshape, bf16), "qpart": ((2,) + qshape, bf16), "spart": (sshape, f32)}
    totals = {"ftotal": (fshape, bf16), "qtotal": (qshape, bf16), "stotal": (sshape, f32)}
    if remote:
        outs |= {n + "_far": item for n, item in totals.items()}
        scratch |= {n: v(*item) for n, item in (parts | totals).items()}
        scratch |= {"leave_sems": sem((7,)), "gather_sends": sem((6, 4)), "gather_recvs": sem((6, 4))}
        for name, shape in (("f", (D, HALF_D)), ("q", (D // 3, 3 * HALF_D))):
            keys = ("_core", "_tp", "_x", "_z", "_sends", "_recvs")
            scratch |= {name + key: item for key, item in zip(keys, big_scratch(*shape))}
        scratch |= dict(zip(("s_near", "s_z", "s_sends", "s_recvs"), small_scratch()))
    else:
        carried |= parts
    results = call_stage(
        layer_kernel, "layer", remote, 0, arrays, ("lengths", "flags"), ("qkv", "up", "proj", "down"), outs, carried,
        scratch,
    )
    sums = [results[n + "_far"] for n in (totals if remote else parts)]
    return results["out_rows_far"], results["in_rows_far"], sums


RESULTS = (
    "output", "grad_input", "attn_gain", "attn_shift", "qkv", "proj", "ffn_gain", "ffn_shift", "up", "up_bias", "down",
    "down_bias", "scale", "shift", "centers", "spreads", "first", "first_bias", "second", "hop", "edge",
)


def unpack_kernel(*refs):
    given = SimpleNamespace(**dict(zip(("out_rows", "in_rows", "fsum", "qsum", "rows"), refs)))
    far = SimpleNamespace(**dict(zip(RESULTS, refs[5:])))
    count = len(RESULTS)
    near = SimpleNamespace(**dict(zip(RESULTS, refs[5 + count : 5 + 2 * count])))
    fsum, qsum, rows, load_sems, store_sems = refs[5 + 2 * count :]
    moves = [(given.rows, rows)]
    sources = ((given.qsum, qsum, 3), (given.fsum, fsum, 9), (given.out_rows, near.output, 1), (given.in_rows, near.grad_input, 1))
    for src, dst, pieces in sources:
        height = src.shape[0] // pieces
        for i in range(pieces):
            at = slice(i * height, (i + 1) * height)
            moves.append((src.at[at], dst.at[at]))
    loads = [pltpu.make_async_copy(src, dst, load_sems.at[i]) for i, (src, dst) in enumerate(moves)]
    for load in loads:
        load.start()
    stores = []

    def store(src, dst):
        stores.append(pltpu.make_async_copy(src, dst, store_sems.at[len(stores)]))
        stores[-1].start()

    for i in range(3):
        loads[1 + i].wait()
        at = slice(256 * i, 256 * (i + 1))
        for m in range(3):
            near.qkv[m, at] = qsum[at, m * HALF_D : (m + 1) * HALF_D].astype(f32)
        store(near.qkv.at[:, at], far.qkv.at[:, at])
    for i in range(3):
        loads[4 + i].wait()
        at = slice(256 * i, 256 * (i + 1))
        near.up[at, :] = fsum[at, :].astype(f32)
        store(near.up.at[at], far.up.at[at])
    for block, name in ((1, "proj"), (2, "down")):
        for i in range(3):
            loads[4 + 3 * block + i].wait()
        ref = getattr(near, name)
        at = D * block
        ref[:, :HALF_D] = fsum[at : at + HALF_D, :].astype(f32)
        ref[:, HALF_D:] = fsum[at + HALF_D : at + D, :].astype(f32)
        store(ref, getattr(far, name))
    loads[13].wait()
    store(near.output, far.output)
    loads[14].wait()
    store(near.grad_input, far.grad_input)
    loads[0].wait()
    names = ("attn_gain", "attn_shift", "ffn_gain", "ffn_shift", "up_bias", "down_bias")
    for v, name in enumerate(names):
        for i in range(D // 128):
            getattr(near, name)[pl.ds(128 * i, 128)] = rows[VECTOR_ROWS + v * (D // 128) + i, :]
    near.first[...] = rows[0:K, :]
    near.second[...] = rows[SECOND_ROWS : SECOND_ROWS + H, :]
    table = rows[TABLE_ROWS : TABLE_ROWS + H, :]
    near.scale[...] = table[:ATOMS, HOT : HOT + ATOMS]
    near.shift[...] = table[ATOMS:, HOT : HOT + ATOMS]
    turned = square_turn(table)
    near.hop[...] = turned[:HOPS, :H]
    near.edge[...] = turned[HOPS : HOPS + EDGES, :H]
    lines = ("first_bias", "centers", "spreads")
    for i, name in enumerate(lines):
        getattr(near, name)[...] = rows[KERNEL_ROWS + i, :]
    for name in names + ("first", "second", "scale", "shift", "hop", "edge") + lines:
        store(getattr(near, name), getattr(far, name))
    for copy in stores:
        copy.wait()


def unpack(out_rows, in_rows, fsum, qsum, rows):
    tokens = out_rows.shape[0]
    vec, line, types = ((D,), f32), ((K,), f32), ((ATOMS, ATOMS), f32)
    shapes = (
        ((tokens, D), bf16), ((tokens, D), bf16), vec, vec, ((3, D, HALF_D), f32), ((HALF_D, D), f32), vec, vec,
        ((D, HALF_D), f32), vec, ((HALF_D, D), f32), vec, types, types, line, line, ((K, K), f32), line, ((H, K), f32),
        ((HOPS, H), f32), ((EDGES, H), f32),
    )
    anywhere = pl.BlockSpec(memory_space=pl.ANY)
    return pl.pallas_call(
        unpack_kernel,
        in_specs=[anywhere] * 5,
        out_specs=[anywhere] * len(shapes),
        out_shape=[jax.ShapeDtypeStruct(*item) for item in shapes],
        scratch_shapes=[pltpu.VMEM(*item) for item in shapes] + [
            pltpu.VMEM(fsum.shape, bf16), pltpu.VMEM(qsum.shape, bf16), pltpu.VMEM(rows.shape, f32),
            pltpu.SemaphoreType.DMA((15,)), pltpu.SemaphoreType.DMA((25,)),
        ],
        compiler_params=pltpu.CompilerParams(vmem_limit_bytes=VMEM_BYTES),
        name="unpack",
    )(out_rows, in_rows, fsum, qsum, rows)


def whole_weights(qkv_weight, up_weight, proj_weight, down_weight):
    columns = lambda w: jnp.stack(jnp.split(w, 2, axis=-1))
    rows = lambda w: jnp.stack(jnp.split(w, 2, axis=0))
    gather = lambda w, dim: lax.all_gather(w, "tp", axis=dim, tiled=True)
    return (
        columns(gather(qkv_weight.transpose(1, 0, 2), 2)), columns(gather(up_weight, 1)),
        rows(gather(proj_weight, 0)), rows(gather(down_weight, 0)),
    )


def sum_grads(fgrads, qgrads, small):
    total_f, total_q, rows = lax.psum((fgrads, qgrads, small), ("mol", "tp"))
    share = D // lax.axis_size("tp")
    at = lax.axis_index("tp") * share

    def columns(halves):
        return lax.dynamic_slice_in_dim(jnp.concatenate(list(halves), axis=-1), at, share, halves.ndim - 2)

    def rows_of(block):
        part = total_f[:, D * block : D * (block + 1)]
        sides = jnp.concatenate([part[:, :HALF_D], part[:, HALF_D:]], axis=2).reshape(D, D)
        return lax.dynamic_slice_in_dim(sides, at, share, 0)

    qkv = columns(total_q.reshape(2, D, 3, HALF_D)).transpose(1, 0, 2)
    return [v.astype(f32) for v in (qkv, columns(total_f[:, :D]), rows_of(1), rows_of(2))], rows


def body(
    mesh_shape,
    hidden_in, positions, atom_types, hop_counts, edge_types, lengths, branches,
    attn_gain, attn_shift, qkv_weight, proj_weight, ffn_gain, ffn_shift, up_weight, up_bias, down_weight, down_bias,
    kernel_scale, kernel_shift, centers, spreads, first_weight, first_bias, second_weight, hop_table, edge_table,
    cotangent,
):
    remote = mesh_shape["tp"] == 2 and mesh_shape["mol"] == 16 and branches.shape[0] == 8
    if remote:
        weights = (qkv_weight.transpose(1, 0, 2), up_weight, proj_weight, down_weight)
    else:
        weights = whole_weights(qkv_weight, up_weight, proj_weight, down_weight)
    arrays = dict(
        lengths=lengths, flags=branches.T, positions=positions, atoms=atom_types, hops=hop_counts.T,
        edges=edge_types.T, kernel_scale=kernel_scale, kernel_shift=kernel_shift, centers=centers, spreads=spreads,
        first_weight=first_weight, first_bias=first_bias, second_weight=second_weight.T, hop_table=hop_table,
        edge_table=edge_table, attn_gain=attn_gain, attn_shift=attn_shift, ffn_gain=ffn_gain, ffn_shift=ffn_shift,
        up_bias=up_bias, down_bias=down_bias, hidden=hidden_in, cotangent=cotangent,
        qkv=weights[0], up=weights[1], proj=weights[2], down=weights[3],
    )
    output, grad_input, sums = layer(remote, arrays)
    if remote:
        fsum, qsum, rows = sums
    else:
        big, rows = sum_grads(*sums)
        fsum, qsum = jnp.zeros((3 * D, HALF_D), bf16), jnp.zeros((D, 3 * HALF_D), bf16)
    output, grad_input, *grads = unpack(output, grad_input, fsum, qsum, rows)
    if not remote:
        grads[2], grads[6], grads[3], grads[8] = big
    grads[2] = grads[2].transpose(1, 0, 2)
    grads[16] = grads[16].T
    return (output, grad_input, *grads)


def solution(mesh):
    rows = P(("mol", "tp"), None)
    all_of = P()
    in_specs = (
        rows, P(None, ("mol", "tp")), P(("mol", "tp")), rows, rows, P("mol"), rows, all_of, all_of,
        P(None, None, "tp"), P("tp", None), all_of, all_of, P(None, "tp"), all_of, P("tp", None),
    ) + (all_of,) * 10 + (rows,)
    out_specs = (
        rows, rows, all_of, all_of, P(None, None, "tp"), P("tp", None), all_of, all_of, P(None, "tp"), all_of,
        P("tp", None),
    ) + (all_of,) * 10
    step = functools.partial(body, dict(mesh.shape))
    return jax.shard_map(step, mesh=mesh, in_specs=in_specs, out_specs=out_specs, check_vma=False)
```

```python
import functools
from types import SimpleNamespace

import jax
import jax.numpy as jnp
from jax import lax
from jax.experimental import pallas as pl
from jax.experimental.pallas import tpu as pltpu
from jax.sharding import PartitionSpec as P

D = 768
H = 32
HD = 24
FF = 768
K = 128
SLOT = 64
HALF = SLOT // 2
HALF_D = D // 2
PAIRS = SLOT * SLOT
HOPS = 16
EDGES = 8
ATOMS = 16
GROUP = 4
GROUPS = H // GROUP
HOT = 32

highest = lax.Precision.HIGHEST
neg_large = -1e30
root_tau = 2.5066282746310002
root_half = 0.7071067811865476
inv_root_tau = 0.3989422804014327
head_scale = HD ** (-0.5)
VMEM_BYTES = 62 * 1024 * 1024
TILE = 1024

SECOND_ROWS = K
TABLE_ROWS = SECOND_ROWS + H
KERNEL_ROWS = TABLE_ROWS + H
VECTOR_ROWS = KERNEL_ROWS + 8
SMALL_ROWS = 256

MESH = pl.DeviceIdType.MESH
f32 = jnp.float32
bf16 = jnp.bfloat16


def dot_nn(left, right, precision=None):
    return lax.dot_general(left, right, (((1,), (0,)), ((), ())), precision=precision, preferred_element_type=f32)


def dot_nt(left, right, precision=None):
    return lax.dot_general(left, right, (((1,), (1,)), ((), ())), precision=precision, preferred_element_type=f32)


def dot_tn(left, right, precision=None):
    return lax.dot_general(left, right, (((0,), (0,)), ((), ())), precision=precision, preferred_element_type=f32)


def iota(shape, dim):
    return lax.broadcasted_iota(jnp.int32, shape, dim)


def gelu_parts(values):
    size = jnp.abs(values)
    bell = jnp.exp(values * values * -0.5)
    denominator = 1.0 + (0.3275911 * root_half) * size
    t = pl.reciprocal(denominator, approx=True)
    series = 0.5 * 1.061405429
    for factor in (-1.453152027, 1.421413741, -0.284496736, 0.254829592):
        series = series * t + 0.5 * factor
    tail = series * t * bell
    gelu = jnp.maximum(values, 0.0) - size * tail
    outer = tail - size * (bell * inv_root_tau)
    return gelu, jnp.where(values >= 0.0, 1.0 - outer, outer)


def to_column(row):
    size = row.shape[1]
    same = iota((size, size), 0) == iota((size, size), 1)
    return jnp.sum(jnp.where(same, row, 0.0), axis=1, keepdims=True)


def half_swap(values):
    return pltpu.roll(values, 64, 1)


def low_lanes(rows):
    return iota((rows, 128), 1) < 64


def vmem(count):
    return [pl.BlockSpec(memory_space=pltpu.VMEM)] * count


def row_of(ref):
    return ref[...].reshape(1, ref.shape[0])


def place():
    mol = lax.axis_index("mol")
    return mol % 2, (mol // 2) % 2, mol // 4, lax.axis_index("tp")


def greet(peers):
    barrier = pltpu.get_barrier_semaphore()
    for peer in peers:
        pl.semaphore_signal(barrier, inc=1, device_id=peer, device_id_type=MESH)
    pl.semaphore_wait(barrier, len(peers))


def window(group):
    first = GROUP * HD * group
    start = first // 128 * 128
    width = 128 if first - start + GROUP * HD <= 128 else 256
    return start, width, first - start


def head_masks(group, kind):
    _, width, offset = window(group)
    lane = iota((1, width), 1)
    return [
        ((lane >= offset + HD * h) & (lane < offset + HD * (h + 1))).astype(f32).astype(kind) for h in range(GROUP)
    ]


def spread_heads(values, group):
    return jnp.concatenate([values * mask for mask in head_masks(group, bf16)], axis=0)


TURNED = (0, 2, 1, 3)


def spread_turned(values, group):
    masks = head_masks(group, bf16)
    return jnp.concatenate([values * masks[h] for h in TURNED], axis=0)


def turn_heads(values):
    turned = jnp.concatenate([values[:, :128], values[:, 128:]], axis=0).T
    return jnp.concatenate([turned[:SLOT], turned[SLOT:]], axis=1)


def standardize(values):
    centred = values - jnp.mean(values, axis=-1, keepdims=True)
    inv_std = lax.rsqrt(jnp.mean(centred * centred, axis=-1, keepdims=True) + 1e-05)
    return centred * inv_std, inv_std


def norm_back(d_normed, scaled, inv_std, gain):
    weighted = d_normed * gain
    inner_a = jnp.mean(weighted, axis=-1, keepdims=True)
    inner_b = jnp.mean(weighted * scaled, axis=-1, keepdims=True)
    return inv_std * (weighted - inner_a - scaled * inner_b)


def column_sum(values):
    return jnp.sum(values, axis=0, keepdims=True)


class Peers:
    def __init__(self):
        self.core, self.x, self.z, self.tp = place()
        mol = lax.axis_index("mol")
        self.over_core = {"mol": mol + 1 - 2 * self.core}
        self.over_x = {"mol": mol + 2 - 4 * self.x}
        self.over_tp = {"tp": 1 - self.tp}
        self.turn = [lax.rem(self.z + d, 4) for d in range(4)]
        self.over_z = [{"mol": self.turn[d] * 4 + self.x * 2 + self.core} for d in range(4)]

    def neighbour(self, k):
        core = self.core + (1 - 2 * self.core) * (k & 1)
        x = self.x + (1 - 2 * self.x) * (k >> 1 & 1)
        tp = self.tp + (1 - 2 * self.tp) * (k >> 2)
        return core * 4 + tp * 2 + x, {"mol": self.z * 4 + x * 2 + core, "tp": tp}

    def everyone(self):
        return [self.neighbour(k)[1] for k in range(1, 8)] + self.over_z[1:]


def span(start, size):
    return pl.ds(pl.multiple_of(start, size), size)


def add_rows(target, source, rows):
    step = 96 if rows % 96 == 0 else min(rows, 32)

    def piece(i, _):
        at = pl.ds(pl.multiple_of(i * step, step), step)
        target[at, :] = target[at, :] + source[at, :]
        return 0

    lax.fori_loop(0, rows // step, piece, 0)


FFN_CHUNKS = tuple((D * b, D, 0, HALF_D) for b in range(3))
QKV_CHUNKS = ((0, 256, 0, 3 * HALF_D), (256, 256, 0, 3 * HALF_D), (512, 256, 0, 2 * HALF_D), (512, 256, 2 * HALF_D, HALF_D))


class Reduction:
    kinds = 11

    def __init__(self, peers, chunks, part, total, from_core, from_tp, from_x, from_z, sends, recvs):
        self.peers, self.chunks, self.part, self.total = peers, chunks, part, total
        self.from_core, self.from_tp, self.from_x, self.from_z = from_core, from_tp, from_x, from_z
        self.sends, self.recvs = sends, recvs

    def place(self, c):
        p = self.peers
        row, rows, lane, lanes = self.chunks[c]
        half, quarter, least = rows // 2, rows // 4, rows // 16
        at_core = row + p.core * half
        at_x = at_core + p.x * quarter
        return (at_core, at_x, at_x + p.z * least), (half, quarter, least), slice(lane, lane + lanes)

    def buffers(self, c):
        row, rows, lane, lanes = self.chunks[c]
        at = slice(lane, lane + lanes)
        cut = lambda share: slice(row // share, (row + rows) // share)
        return (
            self.from_core.at[:, cut(2), at], self.from_tp.at[cut(2), at], self.from_x.at[cut(4), at],
            [self.from_z.at[d, cut(16), at] for d in range(3)],
        )

    def copy(self, c, kind):
        p = self.peers
        part, total = self.part, self.total
        (at_core, at_x, at_z), (half, quarter, least), lanes = self.place(c)
        from_core, from_tp, from_x, from_z = self.buffers(c)
        if kind == 0:
            src = part.at[:, span(self.chunks[c][0] + (1 - p.core) * half, half), lanes]
            dst, peer = from_core, p.over_core
        elif kind == 1:
            src, dst, peer = part.at[1 - p.tp, span(at_core, half), lanes], from_tp, p.over_tp
        elif kind == 2:
            src, dst, peer = part.at[p.tp, span(at_core + (1 - p.x) * quarter, quarter), lanes], from_x, p.over_x
        elif kind < 6:
            d = kind - 2
            src = part.at[p.tp, span(at_x + p.turn[d] * least, least), lanes]
            dst, peer = from_z[d - 1], p.over_z[d]
        elif kind < 9:
            src = dst = total.at[span(at_z, least), lanes]
            peer = p.over_z[kind - 5]
        elif kind == 9:
            src = dst = total.at[span(at_x, quarter), lanes]
            peer = p.over_x
        else:
            src = dst = total.at[span(at_core, half), lanes]
            peer = p.over_core
        return pltpu.make_async_remote_copy(
            src_ref=src, dst_ref=dst, send_sem=self.sends.at[c, kind], recv_sem=self.recvs.at[c, kind],
            device_id=peer, device_id_type=MESH,
        )

    def act(self, c, stage):
        p = self.peers
        part = self.part
        (at_core, at_x, at_z), (half, quarter, least), lanes = self.place(c)
        from_core, from_tp, from_x, from_z = self.buffers(c)
        mine = lambda at, rows: part.at[p.tp, span(at, rows), lanes]
        if stage == 0:
            self.copy(c, 0).start()
        elif stage == 1:
            self.copy(c, 0).wait_recv()
            add_rows(part.at[1 - p.tp, span(at_core, half), lanes], from_core.at[1 - p.tp], half)
            self.copy(c, 1).start()
            add_rows(mine(at_core, half), from_core.at[p.tp], half)
        elif stage == 2:
            self.copy(c, 1).wait_recv()
            away, kept = (1 - p.x) * quarter, p.x * quarter
            add_rows(mine(at_core + away, quarter), from_tp.at[span(away, quarter)], quarter)
            self.copy(c, 2).start()
            add_rows(mine(at_core + kept, quarter), from_tp.at[span(kept, quarter)], quarter)
        elif stage == 3:
            self.copy(c, 2).wait_recv()
            add_rows(mine(at_x, quarter), from_x, quarter)
            for kind in (3, 4, 5):
                self.copy(c, kind).start()
        elif stage == 4:
            for kind in (3, 4, 5):
                self.copy(c, kind).wait_recv()
            value = mine(at_z, least)[...].astype(f32)
            for d in range(3):
                value = value + from_z[d][...].astype(f32)
            self.total[span(at_z, least), lanes] = value.astype(bf16)
            for kind in (6, 7, 8):
                self.copy(c, kind).start()
        elif stage == 5:
            for kind in (6, 7, 8):
                self.copy(c, kind).wait_recv()
            self.copy(c, 9).start()
        elif stage == 6:
            self.copy(c, 9).wait_recv()
            self.copy(c, 10).start()
        elif stage == 7:
            self.copy(c, 10).wait_recv()
        else:
            for kind in range(self.kinds):
                self.copy(c, kind).wait_send()


class SmallReduction:
    def __init__(self, peers, part, total, from_near, from_z, sends, recvs):
        self.peers, self.part, self.total, self.from_near, self.from_z = peers, part, total, from_near, from_z
        self.sends, self.recvs = sends, recvs
        p = peers
        self.near = [p.neighbour(k) for k in range(8)]
        self.mine = span(self.near[0][0] * 32, 32)

    def copy(self, kind):
        p = self.peers
        if kind < 7:
            index, peer = self.near[kind + 1]
            src, dst = self.part.at[span(index * 32, 32)], self.from_near.at[kind]
        elif kind < 10:
            src = dst = self.from_z.at[p.z]
            peer = p.over_z[kind - 6]
        else:
            src = dst = self.total.at[self.mine]
            peer = self.near[kind - 9][1]
        return pltpu.make_async_remote_copy(
            src_ref=src, dst_ref=dst, send_sem=self.sends.at[kind], recv_sem=self.recvs.at[kind],
            device_id=peer, device_id_type=MESH,
        )

    def act(self, stage):
        hops = (range(0, 7), range(7, 10), range(10, 17))
        if stage == 4:
            for kind in range(17):
                self.copy(kind).wait_send()
            return
        if stage > 0:
            for kind in hops[stage - 1]:
                self.copy(kind).wait_recv()
        if stage == 1:
            value = self.part[self.mine, :]
            for k in range(7):
                value = value + self.from_near[k]
            self.from_z[self.peers.z] = value
        elif stage == 2:
            self.total[self.mine, :] = (self.from_z[0] + self.from_z[1]) + (self.from_z[2] + self.from_z[3])
        if stage < 3:
            for kind in hops[stage]:
                self.copy(kind).start()


def big_scratch(rows, lanes, chunks):
    sems = pltpu.SemaphoreType.DMA((chunks, Reduction.kinds))
    return [
        pltpu.VMEM((2, rows // 2, lanes), bf16), pltpu.VMEM((rows // 2, lanes), bf16),
        pltpu.VMEM((rows // 4, lanes), bf16), pltpu.VMEM((3, rows // 16, lanes), bf16), sems, sems,
    ]


def small_scratch():
    return [
        pltpu.VMEM((7, 32, 128), f32), pltpu.VMEM((4, 32, 128), f32),
        pltpu.SemaphoreType.DMA((17,)), pltpu.SemaphoreType.DMA((17,)),
    ]


class Gather:
    pieces = 6

    def __init__(self, peers, whole, sends, recvs):
        self.peers, self.whole, self.sends, self.recvs = peers, whole, sends, recvs
        self.quarter = peers.x * 2 + peers.core
        self.next_quarter = (1 - peers.x) * 2 + peers.core

    def rows(self, ref, quarter):
        count = ref.shape[0] // 4
        return ref.at[span(quarter * count, count), :]

    def copy(self, index, kind):
        p = self.peers
        if kind == 0:
            src = dst = self.rows(self.whole(index, p.tp), self.quarter)
            peer = p.over_tp
        elif kind == 1:
            src = dst = self.rows(self.whole(index, 1 - p.tp), self.quarter)
            peer = p.over_x
        else:
            src = dst = self.rows(self.whole(index, 1 - p.tp), self.quarter if kind == 2 else self.next_quarter)
            peer = p.over_core
        return pltpu.make_async_remote_copy(
            src_ref=src, dst_ref=dst, send_sem=self.sends.at[index, kind], recv_sem=self.recvs.at[index, kind],
            device_id=peer, device_id_type=MESH,
        )

    def start(self, indices):
        for index in indices:
            self.copy(index, 0).start()

    def onward_x(self, index):
        self.copy(index, 0).wait_recv()
        self.copy(index, 1).start()
        self.copy(index, 2).start()

    def onward_core(self, index):
        self.copy(index, 1).wait_recv()
        self.copy(index, 3).start()

    def arrive(self, index):
        self.copy(index, 2).wait_recv()
        self.copy(index, 3).wait_recv()

    def finish(self):
        for index in range(self.pieces):
            for kind in range(4):
                self.copy(index, kind).wait_send()


def square_turn(values):
    rows, lanes = values.shape
    if lanes < 128:
        values = jnp.concatenate([values, jnp.zeros((rows, 128 - lanes), f32)], axis=1)
    if rows < 128:
        values = jnp.concatenate([values, jnp.zeros((128 - rows, 128), f32)], axis=0)
    return values.T


def widen(values):
    return jnp.concatenate([values] * (TILE // 128), axis=1)


def strips():
    return [slice(16 * i, 16 * (i + 1)) for i in range(K // 16)]


def four_rows(ref, slot, first):
    return jnp.concatenate([ref[slot, pl.ds(first + i, 1), :] for i in range(TILE // 128)], axis=1)


def hot_rows(values, count):
    return (values == iota((count, TILE), 0).astype(f32)).astype(f32)


def fold_lanes(values):
    total = values[:, :128]
    for i in range(1, TILE // 128):
        total = total + values[:, 128 * i : 128 * (i + 1)]
    return total


def twice(ref, values):
    none = jnp.zeros_like(values)
    ref[...] = jnp.concatenate(
        [jnp.concatenate([values, none], axis=1), jnp.concatenate([none, values], axis=1)], axis=0
    ).astype(bf16)


def dot_halves(weights, pieces):
    values = jnp.concatenate(pieces, axis=0)
    half = TILE // 2
    both = dot_nn(weights, jnp.concatenate([values[:, :half], values[:, half:]], axis=0))
    rows = both.shape[0] // 2
    return jnp.concatenate([both[:rows], both[rows:]], axis=1)


def prepare_pairs(r):
    spr = to_column(row_of(r.spreads))
    r.cols[0] = jnp.broadcast_to(to_column(row_of(r.centers)), (K, 128))
    r.cols[1] = jnp.broadcast_to(root_half / spr, (K, 128))
    r.cols[2] = jnp.broadcast_to(-jnp.log(root_tau * spr), (K, 128))
    r.cols[3] = jnp.broadcast_to(to_column(row_of(r.first_bias)), (K, 128))
    r.cols[4] = jnp.broadcast_to(1.0 / spr, (K, 128))
    twice(r.w1, r.first_weight[...].astype(f32))
    twice(r.w1t, r.first_weight[...].astype(f32).T)
    r.w2[...] = square_turn(r.second_weight[...].astype(f32))
    table = jnp.concatenate([r.hop_table[...], r.edge_table[...], jnp.zeros((128 - HOPS - EDGES, H), f32)], axis=0)
    table = jnp.concatenate([table, jnp.zeros((128, 128 - H), f32)], axis=1).T[:H, :HOT]
    one = table.astype(bf16).astype(f32)
    r.base[...] = jnp.concatenate(
        [r.second_weight[...].astype(f32), one, table - one, jnp.zeros((H, 64), f32)], axis=1
    )


def bf16_parts(values, count):
    parts = []
    for _ in range(count):
        parts.append(values.astype(bf16))
        values = values - parts[-1].astype(f32)
    return parts


def pair_tables(r, slots):
    low = low_lanes(HALF)
    low_row = low_lanes(1)
    tables = [part.astype(f32) for ref in (r.kernel_scale, r.kernel_shift) for part in bf16_parts(ref[...], 3)]
    tables = jnp.concatenate([square_turn(part)[:ATOMS, :ATOMS] for part in tables], axis=1)
    tables = jnp.concatenate([tables, jnp.zeros((ATOMS, 128 - 6 * ATOMS), f32)], axis=1).astype(bf16)
    for group in range(slots // 2):
        lanes = slice(128 * group, 128 * (group + 1))
        atoms = r.atoms[lanes].astype(f32).reshape(1, 128)
        rows = jnp.concatenate([r.positions[:, lanes], atoms, jnp.zeros((4, 128), f32)], axis=0)
        columns = square_turn(rows)
        key_hot = (columns[:, 3:4] == iota((128, ATOMS), 1).astype(f32)).astype(f32).astype(bf16)
        picks = dot_nn(key_hot, tables).astype(bf16)
        turned = half_swap(rows)
        for s in range(2):
            slot = 2 * group + s
            tokens = slice(SLOT * s, SLOT * (s + 1))
            double = jnp.where(low_lanes(8), *((rows, turned) if s == 0 else (turned, rows)))
            total = None
            for c in range(3):
                column = columns[tokens, c : c + 1]
                offset = jnp.where(low, column[:HALF], column[HALF:]) - double[c : c + 1]
                total = offset * offset if total is None else total + offset * offset
            distance = jnp.sqrt(total)
            query_hot = (double[3:4] == iota((ATOMS, 128), 0).astype(f32)).astype(f32)
            three, none = [query_hot] * 3, [jnp.zeros((3 * ATOMS, 128), f32)]
            rest = [jnp.zeros((128 - 6 * ATOMS, 128), f32)]
            spread = jnp.concatenate(
                [jnp.concatenate(three + none + rest, axis=0), jnp.concatenate(none + three + rest, axis=0)], axis=1
            )
            both = dot_nn(picks[tokens], spread.astype(bf16))
            scale = jnp.where(low, both[:HALF, :128], both[HALF:, :128])
            shift = jnp.where(low, both[:HALF, 128:], both[HALF:, 128:])
            r.argument[slot] = scale * distance + shift
            r.distance[slot] = distance
            for source, target in ((r.hops, r.hop_rows), (r.edges, r.edge_rows)):
                values = source[:, lanes].astype(f32)
                top, bottom = values[:HALF], values[HALF:]
                if s == 0:
                    target[slot] = jnp.where(low, top, half_swap(bottom))
                else:
                    target[slot] = jnp.where(low, half_swap(top), bottom)
            r.atom_rows[slot] = jnp.broadcast_to(double[3:4], (8, 128))


def table_grads(r, slots):
    lefts, rights = [], []
    for slot in range(slots):
        query_hot = (r.atom_rows[slot, 0:1, :] == iota((ATOMS, 128), 0).astype(f32)).astype(f32)
        keys = jnp.concatenate([query_hot[:, :HALF], query_hot[:, HALF:SLOT]], axis=0)
        keys = jnp.concatenate([keys, keys], axis=1).astype(bf16)
        values = jnp.concatenate([r.dargs[slot] * r.distance[slot], r.dargs[slot]], axis=1)
        both = dot_nn(keys, jnp.concatenate(bf16_parts(values, 2), axis=0))
        low = low_lanes(ATOMS)
        for index in range(2):
            lanes = slice(128 * index, 128 * (index + 1))
            rights.append(bf16_parts(jnp.where(low, both[:ATOMS, lanes], both[ATOMS:, lanes]), 2))
        lefts.append(query_hot.astype(bf16))
    left = jnp.concatenate(lefts, axis=1)
    right = jnp.concatenate(
        [jnp.concatenate([rights[2 * s + index][part] for s in range(slots)], axis=1) for index in range(2) for part in range(2)],
        axis=0,
    )
    result = dot_nt(left, right)
    return [
        result[:, 2 * ATOMS * index : 2 * ATOMS * index + ATOMS] + result[:, 2 * ATOMS * index + ATOMS : 2 * ATOMS * (index + 1)]
        for index in range(2)
    ]


def in_stages(stages, count):
    held = {}
    for time in range(count + len(stages) - 1):
        for k, stage in reversed(list(enumerate(stages))):
            if 0 <= time - k < count:
                held[time - k] = stage(time - k, held.get(time - k))


TILES = PAIRS // TILE
ROWS = TILE // 128


def pair_forward(r, slot):
    bank = lax.rem(slot, 2)
    graph_on = r.flags[0, slot].astype(f32)
    space_on = r.flags[1, slot].astype(f32)
    factor = jnp.where(iota((H, 256), 1) < K, space_on, graph_on)
    r.lhs[...] = (r.base[...] * factor).astype(bf16)

    def kernels(tile, _):
        where = slice(tile * TILE, (tile + 1) * TILE)
        arg = four_rows(r.argument, slot, tile * ROWS)
        pieces = []
        for rows in strips():
            u = (arg - widen(r.cols[0, rows])) * widen(r.cols[1, rows])
            pieces.append(jnp.exp(widen(r.cols[2, rows]) - u * u).astype(bf16))
            r.left[bank, rows, where] = pieces[-1]
        return dot_halves(r.w1t[...], pieces)

    def hidden(tile, first):
        where = slice(tile * TILE, (tile + 1) * TILE)
        pieces = []
        for rows in strips():
            value, slope = gelu_parts(first[rows] + widen(r.cols[3, rows]))
            pieces.append(value.astype(bf16))
            r.left[bank, slice(K + rows.start, K + rows.stop), where] = pieces[-1]
            r.slope[bank, rows, where] = slope.astype(bf16)
        hot = jnp.concatenate(
            [
                hot_rows(four_rows(r.hop_rows, slot, tile * ROWS), HOPS),
                hot_rows(four_rows(r.edge_rows, slot, tile * ROWS), HOT - HOPS),
            ],
            axis=0,
        ).astype(bf16)
        return dot_nn(r.lhs[:, : K + 2 * HOT], jnp.concatenate(pieces + [hot] * 2, axis=0))

    def biases(tile, bias):
        bias = bias.astype(bf16).astype(f32)
        for i in range(ROWS):
            r.bias[slot, pl.ds(tile * ROWS + i, H, stride=HALF), :] = bias[:, 128 * i : 128 * (i + 1)]

    in_stages([kernels, hidden, biases], TILES)


def pair_backward(r, slot, between):
    bank = lax.rem(slot, 2)
    graph_on = r.flags[0, slot].astype(f32)
    space_on = r.flags[1, slot].astype(f32)
    twice(r.w2_twice, r.w2[:, :H] * space_on)

    def scores(tile, _):
        where = slice(tile * TILE, (tile + 1) * TILE)
        grad = jnp.concatenate(
            [r.bias[slot, pl.ds(tile * ROWS + i, H, stride=HALF), :] for i in range(ROWS)], axis=1
        )
        r.right[K:, where] = jnp.concatenate([grad * space_on, grad * graph_on], axis=0).astype(bf16)
        edge_hot = hot_rows(four_rows(r.edge_rows, slot, tile * ROWS), HOT - HOPS)
        edge_hot = jnp.where(iota((HOT - HOPS, TILE), 0) == EDGES, 1.0, edge_hot)
        r.left[bank, 2 * K :, where] = jnp.concatenate(
            [hot_rows(four_rows(r.hop_rows, slot, tile * ROWS), HOPS), edge_hot], axis=0
        ).astype(bf16)
        return dot_halves(r.w2_twice[...], [grad.astype(bf16)])

    def hidden(tile, d_second):
        where = slice(tile * TILE, (tile + 1) * TILE)
        pieces = []
        for rows in strips():
            pieces.append((d_second[rows] * r.slope[bank, rows, where].astype(f32)).astype(bf16))
            r.right[rows, where] = pieces[-1]
        return dot_halves(r.w1[...], pieces)

    def kernels(tile, d_gauss):
        where = slice(tile * TILE, (tile + 1) * TILE)
        arg = four_rows(r.argument, slot, tile * ROWS)
        d_arg = None
        for rows in strips():
            inv = widen(r.cols[4, rows])
            u = (arg - widen(r.cols[0, rows])) * inv
            q = d_gauss[rows] * r.left[bank, rows, where].astype(f32)
            w = q * u
            r.sums[0, rows] += fold_lanes(w)
            r.sums[1, rows] += fold_lanes(w * u - q)
            w = w * inv
            w = w[:8] + w[8:]
            d_arg = w if d_arg is None else d_arg + w
        d_arg = -jnp.sum(d_arg, axis=0, keepdims=True)
        for i in range(ROWS):
            at = tile * ROWS + i
            r.dargs[slot, at : at + 1, :] = d_arg[:, 128 * i : 128 * (i + 1)]

    in_stages([scores, hidden, kernels], TILES)
    between()
    r.acc_mixed[...] += dot_nt(r.left[bank], r.right[...])


def attend(r, s, first_slot):
    low = low_lanes(HALF)
    rows = span(s * SLOT, SLOT)
    valid = iota((SLOT, GROUP * SLOT), 0) < r.lengths[first_slot + s]
    r.work[0] = jnp.zeros((SLOT, D), f32)
    for g in range(GROUPS):
        start, width, _ = window(g)
        q = r.joined[rows, start : start + width]
        k = r.joined[rows, D + start : D + start + width]
        v = r.joined[rows, 2 * D + start : 2 * D + start + width]
        scores = dot_nt(k, spread_heads(q, g)) * head_scale
        parts = []
        for pair in range(GROUP // 2):
            head = GROUP * g + 2 * pair
            one = r.bias[s, head * HALF : (head + 1) * HALF, :]
            two = r.bias[s, (head + 1) * HALF : (head + 2) * HALF, :]
            top = jnp.where(low, one, half_swap(two))
            bottom = jnp.where(low, half_swap(one), two)
            parts.append(jnp.concatenate([top, bottom], axis=0))
        scores = jnp.where(valid, scores + jnp.concatenate(parts, axis=1), neg_large)
        weights = jnp.exp(scores - jnp.max(scores, axis=0, keepdims=True))
        prob = weights * (1.0 / jnp.sum(weights, axis=0, keepdims=True))
        r.prob[s, :, g * GROUP * SLOT : (g + 1) * GROUP * SLOT] = prob.astype(bf16)
        r.work[0, :, start : start + width] += dot_nn(turn_heads(prob).astype(bf16), spread_turned(v, g))
    r.attended[rows, :] = r.work[0].astype(bf16)


def attend_back(r, s):
    low = low_lanes(HALF)
    rows = span(s * SLOT, SLOT)
    r.work[...] = jnp.zeros((3, SLOT, D), f32)
    for g in range(GROUPS):
        start, width, _ = window(g)
        lanes = slice(start, start + width)
        k = r.joined[rows, D + start : D + start + width]
        v = r.joined[rows, 2 * D + start : 2 * D + start + width]
        q_heads = spread_heads(r.joined[rows, lanes], g)
        d_heads = spread_heads(r.d_attended[rows, lanes], g)
        prob = r.prob[s, :, g * GROUP * SLOT : (g + 1) * GROUP * SLOT]
        wide = prob.astype(f32)
        d_prob = dot_nt(v, d_heads)
        inner = jnp.sum(wide * d_prob, axis=0, keepdims=True)
        d_scores = (wide * (d_prob - inner)).astype(bf16)
        d_wide = d_scores.astype(f32)
        r.work[0, :, lanes] += dot_nn(turn_heads(d_wide).astype(bf16), spread_turned(k, g))
        r.work[1, :, lanes] += dot_nn(d_scores, q_heads)
        r.work[2, :, lanes] += dot_nn(prob, d_heads)
        for pair in range(GROUP // 2):
            head = GROUP * g + 2 * pair
            top = d_wide[:HALF, 128 * pair : 128 * (pair + 1)]
            bottom = d_wide[HALF:, 128 * pair : 128 * (pair + 1)]
            r.bias[s, head * HALF : (head + 1) * HALF, :] = jnp.where(low, top, half_swap(bottom))
            r.bias[s, (head + 1) * HALF : (head + 2) * HALF, :] = jnp.where(low, half_swap(top), bottom)
    r.joined[rows, 0:D] = (r.work[0] * head_scale).astype(bf16)
    r.joined[rows, D : 2 * D] = (r.work[1] * head_scale).astype(bf16)
    r.joined[rows, 2 * D : 3 * D] = r.work[2].astype(bf16)


def project(r, rows):
    scaled, _ = standardize(r.hidden[rows, :].astype(f32))
    normed = (scaled * row_of(r.attn_gain) + row_of(r.attn_shift)).astype(bf16)
    r.normed_a[rows, :] = normed
    for m in range(3):
        for t in range(2):
            at = m * D + t * HALF_D
            r.joined[rows, at : at + HALF_D] = dot_nn(normed, r.wqkv[t, m]).astype(bf16)


def feed(r, rows):
    halves = [slice(0, HALF_D), slice(HALF_D, D)]
    resid = r.hidden[rows, :].astype(f32)
    for t in range(2):
        resid = resid + dot_nn(r.attended[rows, halves[t]], r.wproj[t])
    scaled, inv_std = standardize(resid)
    normed = (scaled * row_of(r.ffn_gain) + row_of(r.ffn_shift)).astype(bf16)
    r.normed_f[rows, :] = normed
    pre = jnp.concatenate([dot_nn(normed, r.wup[t]) for t in range(2)], axis=1)
    value, slope = gelu_parts(pre + row_of(r.up_bias))
    active = value.astype(bf16)
    r.activated[rows, :] = active
    result = resid + row_of(r.down_bias)
    for t in range(2):
        result = result + dot_nn(active[:, halves[t]], r.wdown[t])
    r.out_rows[rows, :] = result.astype(bf16)
    cot = r.cotangent[rows, :]
    cot_wide = cot.astype(f32)
    d_active = jnp.concatenate([dot_nt(cot, r.wdown[t]) for t in range(2)], axis=1)
    d_hidden = (d_active * slope).astype(bf16)
    r.d_pre[rows, :] = d_hidden
    d_normed = dot_nt(d_hidden[:, halves[0]], r.wup[0]) + dot_nt(d_hidden[:, halves[1]], r.wup[1])
    d_resid = cot_wide + norm_back(d_normed, scaled, inv_std, row_of(r.ffn_gain))
    r.d_resid[rows, :] = d_resid
    branch = d_resid.astype(bf16)
    r.d_branch[rows, :] = branch
    for t in range(2):
        r.d_attended[rows, halves[t]] = dot_nt(branch, r.wproj[t]).astype(bf16)
    r.vectors[2:3, :] += column_sum(d_normed * scaled)
    r.vectors[3:4, :] += column_sum(d_normed)
    r.vectors[4:5, :] += column_sum(d_hidden.astype(f32))
    r.vectors[5:6, :] += column_sum(cot_wide)


def feed_grads(r, block):
    halves = [slice(0, HALF_D), slice(HALF_D, D)]
    if block == 0:
        grad = dot_tn(r.normed_f[...], r.d_pre[...]).astype(bf16)
        for t in range(2):
            r.fpart[t, :D, :] = grad[:, halves[t]]
        return
    left, right = (r.attended, r.d_branch) if block == 1 else (r.activated, r.cotangent)
    for t in range(2):
        grad = dot_tn(left[:, halves[t]], right[...]).astype(bf16)
        for side in range(2):
            r.fpart[t, D * block + HALF_D * side : D * block + HALF_D * (side + 1), :] = grad[:, halves[side]]


def qkv_grads(r, rows, thirds):
    for m in thirds:
        grad = dot_tn(r.normed_a[:, rows], r.joined[:, m * D : (m + 1) * D]).astype(bf16)
        for t in range(2):
            r.qpart[t, rows, m * HALF_D : (m + 1) * HALF_D] = grad[:, t * HALF_D : (t + 1) * HALF_D]


def finish_input(r, rows):
    d_normed = None
    for m in range(3):
        for t in range(2):
            at = m * D + t * HALF_D
            term = dot_nt(r.joined[rows, at : at + HALF_D], r.wqkv[t, m])
            d_normed = term if d_normed is None else d_normed + term
    scaled, inv_std = standardize(r.hidden[rows, :].astype(f32))
    grad = r.d_resid[rows, :] + norm_back(d_normed, scaled, inv_std, row_of(r.attn_gain))
    r.in_rows[rows, :] = grad.astype(bf16)
    r.vectors[0:1, :] += column_sum(d_normed * scaled)
    r.vectors[1:2, :] += column_sum(d_normed)


def pack_small(r, slots):
    tables = table_grads(r, slots)
    for v in range(6):
        for i in range(D // 128):
            at = VECTOR_ROWS + v * (D // 128) + i
            r.spart[at : at + 1, :] = r.vectors[v : v + 1, 128 * i : 128 * (i + 1)]
    r.spart[0:K, :] = r.acc_mixed[0:K, :K]
    r.spart[SECOND_ROWS : SECOND_ROWS + H, :] = square_turn(r.acc_mixed[K : 2 * K, K:])[:H]
    r.spart[TABLE_ROWS : TABLE_ROWS + H, :HOT] = square_turn(r.acc_mixed[2 * K :, K:])[H : 2 * H, :HOT]
    for index in range(2):
        rows = slice(TABLE_ROWS + ATOMS * index, TABLE_ROWS + ATOMS * (index + 1))
        r.spart[rows, HOT : HOT + ATOMS] = tables[index]
    ones = 2 * K + HOPS + EDGES
    r.spart[KERNEL_ROWS : KERNEL_ROWS + 1, :] = r.acc_mixed[ones : ones + 1, :K]
    for index in range(2):
        column = jnp.sum(r.sums[index] * r.cols[4], axis=1, keepdims=True)
        same = iota((K, K), 0) == iota((K, K), 1)
        at = KERNEL_ROWS + 1 + index
        r.spart[at : at + 1, :] = jnp.sum(jnp.where(same, column, 0.0), axis=0, keepdims=True)


class Stage:
    def __init__(self, names, near_inputs, carried, refs):
        self.r = SimpleNamespace(**dict(zip(names, refs)))
        r = self.r
        self.loads = {
            name: pltpu.make_async_copy(getattr(r, "given_" + name), getattr(r, name), r.input_sems.at[i])
            for i, name in enumerate(near_inputs)
        }
        self.stores = {
            name: pltpu.make_async_copy(getattr(r, name), getattr(r, name + "_far"), r.carry_sems.at[i])
            for i, name in enumerate(carried)
        }

    def load(self, *names):
        for name in names:
            self.loads[name].start()

    def need(self, *names):
        for name in names:
            self.loads[name].wait()

    def store(self, *names):
        for name in names:
            self.stores[name].start()

    def stored(self):
        for copy in self.stores.values():
            copy.wait()


def each_chunk(r, tokens, work, after=lambda c: None):
    chunk = min(256, tokens)

    def one(c, _):
        work(r, span(c * chunk, chunk))
        after(c)
        return 0

    lax.fori_loop(0, tokens // chunk, one, 0)


def pair_moves(r, slot, back):
    bank = lax.rem(slot, 2)
    both = (r.left_far.at[slot], r.left.at[bank, : 2 * K]), (r.slope_far.at[slot], r.slope.at[bank])
    for index, (far, near) in enumerate(both):
        yield pltpu.make_async_copy(*((far, near) if back else (near, far)), r.pair_sems.at[bank, index])


def start_moves(r, slot, back):
    for copy in pair_moves(r, slot, back):
        copy.start()


def wait_moves(r, slot, back):
    for copy in pair_moves(r, slot, back):
        copy.wait()


def run(steps):
    for act, *where in steps:
        act(*where)


def at_time(index, plan):
    for k, steps in plan.items():
        pl.when(index == k)(functools.partial(run, steps))


AFTER_FEED = [("f", 0, 1)]
IN_BACK = {0: [("f", 1, 1)], 1: [("f", 2, 1)], 5: [("f", 0, 2)]}
IN_GRADS = {1: [("f", 0, 3), ("f", 1, 2)], 2: [("q", 0, 1)], 3: [("q", 1, 1)]}
IN_INPUT = {0: [("q", 2, 1), ("q", 3, 1), ("f", 0, 4), ("f", 1, 3), ("f", 2, 2)]}
IN_PAIRS = {
    0: [("f", 0, 5)], 1: [("f", 2, 3), ("q", 0, 2)], 2: [("f", 1, 4)], 4: [("f", 0, 6), ("f", 2, 4), ("q", 1, 2)],
    5: [("q", 0, 3), ("f", 0, 7), ("f", 1, 5)], 6: [("q", 2, 2)], 7: [("f", 2, 5), ("q", 1, 3), ("q", 3, 2)],
    8: [("q", 0, 4), ("f", 1, 6)], 9: [("q", 2, 3)], 10: [("f", 1, 7), ("q", 1, 4)],
    11: [("f", 2, 6), ("q", 3, 3), ("q", 0, 5)], 12: [("q", 2, 4), ("f", 2, 7)], 14: [("q", 1, 5), ("q", 0, 6)],
    15: [("q", 3, 4), ("q", 2, 5)],
}
AT_END = (
    [("q", 0, 7), ("q", 1, 6), ("q", 3, 5)], [("q", 2, 6), ("q", 1, 7)], [("q", 3, 6), ("q", 2, 7)], [("q", 3, 7)],
)


def layer_kernel(remote, names, near_inputs, carried, *refs):
    stage = Stage(names, near_inputs, carried, refs)
    r = stage.r
    stage.load(*[name for name in near_inputs if name not in ("hidden", "cotangent")])
    tokens = r.hidden.shape[0]
    slots = tokens // SLOT
    peers = Peers()
    whole = [r.wqkv, r.wup, r.wproj, r.wdown]
    given = [r.given_qkv, r.given_up, r.given_proj, r.given_down]
    targets = [w.at[peers.tp] for w in whole] if remote else whole
    loads = [
        pltpu.make_async_copy(src, dst, r.load_sems.at[i]) for i, (src, dst) in enumerate(zip(given, targets))
    ]
    for load in loads:
        load.start()
    stage.load("hidden", "cotangent")
    gather_plan = {}
    if remote:

        def whole_piece(index, tp):
            return whole[0].at[tp, index] if index < 3 else whole[index - 2].at[tp]

        gather = Gather(peers, whole_piece, r.gather_sends, r.gather_recvs)
        ffn = Reduction(peers, FFN_CHUNKS, r.fpart, r.ftotal, r.f_core, r.f_tp, r.f_x, r.f_z, r.f_sends, r.f_recvs)
        qkv = Reduction(peers, QKV_CHUNKS, r.qpart, r.qtotal, r.q_core, r.q_tp, r.q_x, r.q_z, r.q_sends, r.q_recvs)
        small = SmallReduction(peers, r.spart, r.stotal, r.s_near, r.s_z, r.s_sends, r.s_recvs)
        greet(peers.everyone())
        for load, indices in zip(loads, ((0, 1, 2), (3,), (4,), (5,))):
            load.wait()
            gather.start(indices)
        x, core = gather.onward_x, gather.onward_core
        gather_plan = {
            0: [(x, 0)], 1: [(x, 1), (core, 0)], 2: [(x, 2), (core, 1)], 3: [(x, 3), (core, 2)],
            4: [(x, 4), (core, 3), (x, 5)], 5: [(core, 4)], 6: [(core, 5)],
        }

    def leave(which, c):
        near, far, chunks = ((r.ftotal, r.ftotal_far, FFN_CHUNKS), (r.qtotal, r.qtotal_far, QKV_CHUNKS))[which == "q"]
        row, rows, lane, lanes = chunks[c]
        at = (slice(row, row + rows), slice(lane, lane + lanes))
        index = c + len(FFN_CHUNKS) * (which == "q")
        return pltpu.make_async_copy(near.at[at], far.at[at], r.leave_sems.at[index])

    def advance(actions):
        if remote:
            for which, c, step in actions:
                (qkv if which == "q" else ffn).act(c, step)
                if step == 7:
                    leave(which, c).start()

    def advance_at(index, plan):
        at_time(index, {k: [(advance, actions)] for k, actions in plan.items()} if remote else {})

    stage.need(*[name for name in near_inputs if name not in ("hidden", "cotangent")])
    prepare_pairs(r)
    pair_tables(r, slots)

    def pairs(slot, _):
        pl.when(slot >= 2)(lambda: wait_moves(r, slot - 2, False))
        pair_forward(r, slot)
        start_moves(r, slot, False)
        at_time(slot, gather_plan)
        return 0

    lax.fori_loop(0, slots, pairs, 0)
    stage.need("hidden")
    if remote:
        for index in range(3):
            gather.arrive(index)
    else:
        for load in loads:
            load.wait()
    each_chunk(r, tokens, project)
    first_slot = peers.tp * slots

    def attend_one(s, _):
        attend(r, s, first_slot)
        return 0

    lax.fori_loop(0, slots, attend_one, 0)
    stage.need("cotangent")
    if remote:
        for index in range(3, 6):
            gather.arrive(index)
    r.vectors[...] = jnp.zeros_like(r.vectors)
    each_chunk(r, tokens, feed)
    stage.store("out_rows")
    for slot in (slots - 2, slots - 1):
        wait_moves(r, slot, False)
    start_moves(r, 0, True)
    start_moves(r, 1, True)
    for block in range(3):
        feed_grads(r, block)
        advance([("f", block, 0)])
    advance(AFTER_FEED)

    def back_one(s, _):
        attend_back(r, s)
        advance_at(s, IN_BACK)
        return 0

    lax.fori_loop(0, slots, back_one, 0)
    for c, (row, rows, lane, lanes) in enumerate(QKV_CHUNKS):
        qkv_grads(r, slice(row, row + rows), range(lane // HALF_D, (lane + lanes) // HALF_D))
        advance([("q", c, 0)] + IN_GRADS.get(c, []))

    each_chunk(r, tokens, finish_input, lambda c: advance_at(c, IN_INPUT))
    stage.store("in_rows")
    for ref in (r.sums, r.acc_mixed, r.spart):
        ref[...] = jnp.zeros_like(ref)

    def pairs_back(slot, _):
        wait_moves(r, slot, True)
        pair_backward(r, slot, lambda: advance_at(2 * slot, IN_PAIRS))
        pl.when(slot + 2 < slots)(lambda: start_moves(r, slot + 2, True))
        advance_at(2 * slot + 1, IN_PAIRS)
        return 0

    lax.fori_loop(0, slots, pairs_back, 0)
    pack_small(r, slots)
    if remote:
        for step in range(4):
            small.act(step)
            advance(AT_END[step])
        rows = pltpu.make_async_copy(r.stotal, r.stotal_far, r.leave_sems.at[7])
        rows.start()
        ends = [("f", c) for c in range(len(FFN_CHUNKS))] + [("q", c) for c in range(len(QKV_CHUNKS))]
        advance([(which, c, 8) for which, c in ends])
        small.act(4)
        gather.finish()
        for which, c in ends:
            leave(which, c).wait()
        rows.wait()
    else:
        stage.store("fpart", "qpart", "spart")
    stage.stored()


def call_stage(kernel, name, remote, collective, arrays, scalars, far, outs, carried, scratch):
    vm, sem = pltpu.VMEM, pltpu.SemaphoreType.DMA
    near = {n: vm(a.shape, a.dtype) for n, a in arrays.items() if n not in scalars + far}
    in_names = [n if n in scalars or n.endswith("_far") else "given_" + n for n in arrays]
    results = outs | {n + "_far": item for n, item in carried.items()}
    scratch = near | {n: vm(*item) for n, item in carried.items()} | scratch
    scratch |= {"input_sems": sem((len(near),)), "carry_sems": sem((len(carried),))}
    names = in_names + list(results) + list(scratch)
    values = pl.pallas_call(
        functools.partial(kernel, remote, names, list(near), list(carried)),
        in_specs=[pl.BlockSpec(memory_space=pltpu.SMEM if n in scalars else pl.ANY) for n in arrays],
        out_specs=[pl.BlockSpec(memory_space=pl.ANY)] * len(results),
        out_shape=[jax.ShapeDtypeStruct(*item) for item in results.values()],
        scratch_shapes=list(scratch.values()),
        compiler_params=pltpu.CompilerParams(
            vmem_limit_bytes=VMEM_BYTES, **(dict(collective_id=collective, has_side_effects=True) if remote else {})
        ),
        name=name,
    )(*arrays.values())
    return dict(zip(results, values))


def layer(remote, arrays):
    tokens = arrays["hidden"].shape[0]
    slots = tokens // SLOT
    v, sem = pltpu.VMEM, pltpu.SemaphoreType.DMA
    of_tokens = (tokens, D)
    table = (slots, HALF, 128)
    fshape, qshape, sshape = (3 * D, HALF_D), (D, 3 * HALF_D), (SMALL_ROWS, 128)
    outs = {"left_far": ((slots, 2 * K, PAIRS), bf16), "slope_far": ((slots, K, PAIRS), bf16)}
    carried = {"out_rows": (of_tokens, bf16), "in_rows": (of_tokens, bf16)}
    scratch = {
        "wqkv": v((2, 3, D, HALF_D), bf16), "wup": v((2, D, HALF_D), bf16), "wproj": v((2, HALF_D, D), bf16),
        "wdown": v((2, HALF_D, D), bf16), "load_sems": sem((4,)), "pair_sems": sem((2, 2)),
        "left": v((2, 2 * K + HOT, PAIRS), bf16), "slope": v((2, K, PAIRS), bf16),
        "right": v((K + 2 * H, PAIRS), bf16), "cols": v((5, K, 128), f32), "w1": v((2 * K, 2 * K), bf16), "w1t": v((2 * K, 2 * K), bf16),
        "w2": v((K, 128), f32), "w2_twice": v((2 * K, 2 * H), bf16), "base": v((H, 256), f32), "lhs": v((H, 256), bf16),
        "argument": v(table, f32), "distance": v(table, f32), "hop_rows": v(table, f32), "edge_rows": v(table, f32),
        "atom_rows": v((slots, 8, 128), f32), "dargs": v(table, f32), "bias": v((slots, H * HALF, 128), f32),
        "work": v((3, SLOT, D), f32), "normed_a": v(of_tokens, bf16), "joined": v((tokens, 3 * D), bf16),
        "prob": v((slots, SLOT, H * SLOT), bf16), "attended": v(of_tokens, bf16), "normed_f": v(of_tokens, bf16),
        "activated": v(of_tokens, bf16), "d_pre": v(of_tokens, bf16), "d_branch": v(of_tokens, bf16),
        "d_attended": v(of_tokens, bf16), "d_resid": v(of_tokens, f32), "vectors": v((8, D), f32),
        "sums": v((2, K, 128), f32), "acc_mixed": v((2 * K + HOT, K + 2 * H), f32),
    }
    parts = {"fpart": ((2,) + fshape, bf16), "qpart": ((2,) + qshape, bf16), "spart": (sshape, f32)}
    totals = {"ftotal": (fshape, bf16), "qtotal": (qshape, bf16), "stotal": (sshape, f32)}
    if remote:
        outs |= {n + "_far": item for n, item in totals.items()}
        scratch |= {n: v(*item) for n, item in (parts | totals).items()}
        scratch |= {"leave_sems": sem((8,)), "gather_sends": sem((6, 4)), "gather_recvs": sem((6, 4))}
        for name, shape in (("f", fshape + (len(FFN_CHUNKS),)), ("q", qshape + (len(QKV_CHUNKS),))):
            keys = ("_core", "_tp", "_x", "_z", "_sends", "_recvs")
            scratch |= {name + key: item for key, item in zip(keys, big_scratch(*shape))}
        scratch |= dict(zip(("s_near", "s_z", "s_sends", "s_recvs"), small_scratch()))
    else:
        carried |= parts
    results = call_stage(
        layer_kernel, "layer", remote, 0, arrays, ("lengths", "flags"), ("qkv", "up", "proj", "down"), outs, carried,
        scratch,
    )
    sums = [results[n + "_far"] for n in (totals if remote else parts)]
    return results["out_rows_far"], results["in_rows_far"], sums


RESULTS = (
    "output", "grad_input", "attn_gain", "attn_shift", "qkv", "proj", "ffn_gain", "ffn_shift", "up", "up_bias", "down",
    "down_bias", "scale", "shift", "centers", "spreads", "first", "first_bias", "second", "hop", "edge",
)


def unpack_kernel(*refs):
    given = SimpleNamespace(**dict(zip(("out_rows", "in_rows", "fsum", "qsum", "rows"), refs)))
    far = SimpleNamespace(**dict(zip(RESULTS, refs[5:])))
    count = len(RESULTS)
    near = SimpleNamespace(**dict(zip(RESULTS, refs[5 + count : 5 + 2 * count])))
    fsum, qsum, rows, load_sems, store_sems = refs[5 + 2 * count :]
    moves = [(given.rows, rows)]
    sources = ((given.qsum, qsum, 3), (given.fsum, fsum, 9), (given.out_rows, near.output, 1), (given.in_rows, near.grad_input, 1))
    for src, dst, pieces in sources:
        height = src.shape[0] // pieces
        for i in range(pieces):
            at = slice(i * height, (i + 1) * height)
            moves.append((src.at[at], dst.at[at]))
    loads = [pltpu.make_async_copy(src, dst, load_sems.at[i]) for i, (src, dst) in enumerate(moves)]
    for load in loads:
        load.start()
    stores = []

    def store(src, dst):
        stores.append(pltpu.make_async_copy(src, dst, store_sems.at[len(stores)]))
        stores[-1].start()

    for i in range(3):
        loads[1 + i].wait()
        at = slice(256 * i, 256 * (i + 1))
        for m in range(3):
            near.qkv[m, at] = qsum[at, m * HALF_D : (m + 1) * HALF_D].astype(f32)
        store(near.qkv.at[:, at], far.qkv.at[:, at])
    for i in range(3):
        loads[4 + i].wait()
        at = slice(256 * i, 256 * (i + 1))
        near.up[at, :] = fsum[at, :].astype(f32)
        store(near.up.at[at], far.up.at[at])
    for block, name in ((1, "proj"), (2, "down")):
        for i in range(3):
            loads[4 + 3 * block + i].wait()
        ref = getattr(near, name)
        at = D * block
        ref[:, :HALF_D] = fsum[at : at + HALF_D, :].astype(f32)
        ref[:, HALF_D:] = fsum[at + HALF_D : at + D, :].astype(f32)
        store(ref, getattr(far, name))
    loads[13].wait()
    store(near.output, far.output)
    loads[14].wait()
    store(near.grad_input, far.grad_input)
    loads[0].wait()
    names = ("attn_gain", "attn_shift", "ffn_gain", "ffn_shift", "up_bias", "down_bias")
    for v, name in enumerate(names):
        for i in range(D // 128):
            getattr(near, name)[pl.ds(128 * i, 128)] = rows[VECTOR_ROWS + v * (D // 128) + i, :]
    near.first[...] = rows[0:K, :]
    near.second[...] = rows[SECOND_ROWS : SECOND_ROWS + H, :]
    table = rows[TABLE_ROWS : TABLE_ROWS + H, :]
    near.scale[...] = table[:ATOMS, HOT : HOT + ATOMS]
    near.shift[...] = table[ATOMS:, HOT : HOT + ATOMS]
    turned = square_turn(table)
    near.hop[...] = turned[:HOPS, :H]
    near.edge[...] = turned[HOPS : HOPS + EDGES, :H]
    lines = ("first_bias", "centers", "spreads")
    for i, name in enumerate(lines):
        getattr(near, name)[...] = rows[KERNEL_ROWS + i, :]
    for name in names + ("first", "second", "scale", "shift", "hop", "edge") + lines:
        store(getattr(near, name), getattr(far, name))
    for copy in stores:
        copy.wait()


def unpack(out_rows, in_rows, fsum, qsum, rows):
    tokens = out_rows.shape[0]
    vec, line, types = ((D,), f32), ((K,), f32), ((ATOMS, ATOMS), f32)
    shapes = (
        ((tokens, D), bf16), ((tokens, D), bf16), vec, vec, ((3, D, HALF_D), f32), ((HALF_D, D), f32), vec, vec,
        ((D, HALF_D), f32), vec, ((HALF_D, D), f32), vec, types, types, line, line, ((K, K), f32), line, ((H, K), f32),
        ((HOPS, H), f32), ((EDGES, H), f32),
    )
    anywhere = pl.BlockSpec(memory_space=pl.ANY)
    return pl.pallas_call(
        unpack_kernel,
        in_specs=[anywhere] * 5,
        out_specs=[anywhere] * len(shapes),
        out_shape=[jax.ShapeDtypeStruct(*item) for item in shapes],
        scratch_shapes=[pltpu.VMEM(*item) for item in shapes] + [
            pltpu.VMEM(fsum.shape, bf16), pltpu.VMEM(qsum.shape, bf16), pltpu.VMEM(rows.shape, f32),
            pltpu.SemaphoreType.DMA((15,)), pltpu.SemaphoreType.DMA((25,)),
        ],
        compiler_params=pltpu.CompilerParams(vmem_limit_bytes=VMEM_BYTES),
        name="unpack",
    )(out_rows, in_rows, fsum, qsum, rows)


def whole_weights(qkv_weight, up_weight, proj_weight, down_weight):
    columns = lambda w: jnp.stack(jnp.split(w, 2, axis=-1))
    rows = lambda w: jnp.stack(jnp.split(w, 2, axis=0))
    gather = lambda w, dim: lax.all_gather(w, "tp", axis=dim, tiled=True)
    return (
        columns(gather(qkv_weight.transpose(1, 0, 2), 2)), columns(gather(up_weight, 1)),
        rows(gather(proj_weight, 0)), rows(gather(down_weight, 0)),
    )


def sum_grads(fgrads, qgrads, small):
    total_f, total_q, rows = lax.psum((fgrads, qgrads, small), ("mol", "tp"))
    share = D // lax.axis_size("tp")
    at = lax.axis_index("tp") * share

    def columns(halves):
        return lax.dynamic_slice_in_dim(jnp.concatenate(list(halves), axis=-1), at, share, halves.ndim - 2)

    def rows_of(block):
        part = total_f[:, D * block : D * (block + 1)]
        sides = jnp.concatenate([part[:, :HALF_D], part[:, HALF_D:]], axis=2).reshape(D, D)
        return lax.dynamic_slice_in_dim(sides, at, share, 0)

    qkv = columns(total_q.reshape(2, D, 3, HALF_D)).transpose(1, 0, 2)
    return [v.astype(f32) for v in (qkv, columns(total_f[:, :D]), rows_of(1), rows_of(2))], rows


def body(
    mesh_shape,
    hidden_in, positions, atom_types, hop_counts, edge_types, lengths, branches,
    attn_gain, attn_shift, qkv_weight, proj_weight, ffn_gain, ffn_shift, up_weight, up_bias, down_weight, down_bias,
    kernel_scale, kernel_shift, centers, spreads, first_weight, first_bias, second_weight, hop_table, edge_table,
    cotangent,
):
    remote = mesh_shape["tp"] == 2 and mesh_shape["mol"] == 16 and branches.shape[0] == 8
    if remote:
        weights = (qkv_weight.transpose(1, 0, 2), up_weight, proj_weight, down_weight)
    else:
        weights = whole_weights(qkv_weight, up_weight, proj_weight, down_weight)
    arrays = dict(
        lengths=lengths, flags=branches.T, positions=positions, atoms=atom_types, hops=hop_counts.T,
        edges=edge_types.T, kernel_scale=kernel_scale, kernel_shift=kernel_shift, centers=centers, spreads=spreads,
        first_weight=first_weight, first_bias=first_bias, second_weight=second_weight.T, hop_table=hop_table,
        edge_table=edge_table, attn_gain=attn_gain, attn_shift=attn_shift, ffn_gain=ffn_gain, ffn_shift=ffn_shift,
        up_bias=up_bias, down_bias=down_bias, hidden=hidden_in, cotangent=cotangent,
        qkv=weights[0], up=weights[1], proj=weights[2], down=weights[3],
    )
    output, grad_input, sums = layer(remote, arrays)
    if remote:
        fsum, qsum, rows = sums
    else:
        big, rows = sum_grads(*sums)
        fsum, qsum = jnp.zeros((3 * D, HALF_D), bf16), jnp.zeros((D, 3 * HALF_D), bf16)
    output, grad_input, *grads = unpack(output, grad_input, fsum, qsum, rows)
    if not remote:
        grads[2], grads[6], grads[3], grads[8] = big
    grads[2] = grads[2].transpose(1, 0, 2)
    grads[16] = grads[16].T
    return (output, grad_input, *grads)


def solution(mesh):
    rows = P(("mol", "tp"), None)
    all_of = P()
    in_specs = (
        rows, P(None, ("mol", "tp")), P(("mol", "tp")), rows, rows, P("mol"), rows, all_of, all_of,
        P(None, None, "tp"), P("tp", None), all_of, all_of, P(None, "tp"), all_of, P("tp", None),
    ) + (all_of,) * 10 + (rows,)
    out_specs = (
        rows, rows, all_of, all_of, P(None, None, "tp"), P("tp", None), all_of, all_of, P(None, "tp"), all_of,
        P("tp", None),
    ) + (all_of,) * 10
    step = functools.partial(body, dict(mesh.shape))
    return jax.shard_map(step, mesh=mesh, in_specs=in_specs, out_specs=out_specs, check_vma=False)
```

```python
import functools
from types import SimpleNamespace

import jax
import jax.numpy as jnp
from jax import lax
from jax.experimental import pallas as pl
from jax.experimental.pallas import tpu as pltpu
from jax.sharding import PartitionSpec as P

D = 768
H = 32
HD = 24
FF = 768
K = 128
SLOT = 64
HALF = SLOT // 2
HALF_D = D // 2
PAIRS = SLOT * SLOT
HOPS = 16
EDGES = 8
ATOMS = 16
GROUP = 4
GROUPS = H // GROUP
HOT = 32

highest = lax.Precision.HIGHEST
neg_large = -1e30
root_tau = 2.5066282746310002
root_half = 0.7071067811865476
inv_root_tau = 0.3989422804014327
head_scale = HD ** (-0.5)
VMEM_BYTES = 62 * 1024 * 1024
TILE = 1024

SECOND_ROWS = K
TABLE_ROWS = SECOND_ROWS + H
KERNEL_ROWS = TABLE_ROWS + H
VECTOR_ROWS = KERNEL_ROWS + 8
SMALL_ROWS = 256

MESH = pl.DeviceIdType.MESH
f32 = jnp.float32
bf16 = jnp.bfloat16


def dot_nn(left, right, precision=None):
    return lax.dot_general(left, right, (((1,), (0,)), ((), ())), precision=precision, preferred_element_type=f32)


def dot_nt(left, right, precision=None):
    return lax.dot_general(left, right, (((1,), (1,)), ((), ())), precision=precision, preferred_element_type=f32)


def dot_tn(left, right, precision=None):
    return lax.dot_general(left, right, (((0,), (0,)), ((), ())), precision=precision, preferred_element_type=f32)


def iota(shape, dim):
    return lax.broadcasted_iota(jnp.int32, shape, dim)


def gelu_parts(values):
    size = jnp.abs(values)
    bell = jnp.exp(values * values * -0.5)
    denominator = 1.0 + (0.3275911 * root_half) * size
    t = pl.reciprocal(denominator, approx=True)
    series = 0.5 * 1.061405429
    for factor in (-1.453152027, 1.421413741, -0.284496736, 0.254829592):
        series = series * t + 0.5 * factor
    tail = series * t * bell
    gelu = jnp.maximum(values, 0.0) - size * tail
    outer = tail - size * (bell * inv_root_tau)
    return gelu, jnp.where(values >= 0.0, 1.0 - outer, outer)


def to_column(row):
    size = row.shape[1]
    same = iota((size, size), 0) == iota((size, size), 1)
    return jnp.sum(jnp.where(same, row, 0.0), axis=1, keepdims=True)


def half_swap(values):
    return pltpu.roll(values, 64, 1)


def low_lanes(rows):
    return iota((rows, 128), 1) < 64


def vmem(count):
    return [pl.BlockSpec(memory_space=pltpu.VMEM)] * count


def row_of(ref):
    return ref[...].reshape(1, ref.shape[0])


def place():
    mol = lax.axis_index("mol")
    return mol % 2, (mol // 2) % 2, mol // 4, lax.axis_index("tp")


def greet(peers):
    barrier = pltpu.get_barrier_semaphore()
    for peer in peers:
        pl.semaphore_signal(barrier, inc=1, device_id=peer, device_id_type=MESH)
    pl.semaphore_wait(barrier, len(peers))


def window(group):
    first = GROUP * HD * group
    start = first // 128 * 128
    width = 128 if first - start + GROUP * HD <= 128 else 256
    return start, width, first - start


def head_masks(group, kind):
    _, width, offset = window(group)
    lane = iota((1, width), 1)
    return [
        ((lane >= offset + HD * h) & (lane < offset + HD * (h + 1))).astype(f32).astype(kind) for h in range(GROUP)
    ]


def spread_heads(values, group):
    return jnp.concatenate([values * mask for mask in head_masks(group, bf16)], axis=0)


def gather_heads(values, group):
    masks = head_masks(group, f32)
    total = values[:SLOT] * masks[0]
    for h in range(1, GROUP):
        total = total + values[SLOT * h : SLOT * (h + 1)] * masks[h]
    return total


def standardize(values):
    centred = values - jnp.mean(values, axis=-1, keepdims=True)
    inv_std = lax.rsqrt(jnp.mean(centred * centred, axis=-1, keepdims=True) + 1e-05)
    return centred * inv_std, inv_std


def norm_back(d_normed, scaled, inv_std, gain):
    weighted = d_normed * gain
    inner_a = jnp.mean(weighted, axis=-1, keepdims=True)
    inner_b = jnp.mean(weighted * scaled, axis=-1, keepdims=True)
    return inv_std * (weighted - inner_a - scaled * inner_b)


def column_sum(values):
    return jnp.sum(values, axis=0, keepdims=True)


class Peers:
    def __init__(self):
        self.core, self.x, self.z, self.tp = place()
        mol = lax.axis_index("mol")
        self.over_core = {"mol": mol + 1 - 2 * self.core}
        self.over_x = {"mol": mol + 2 - 4 * self.x}
        self.over_tp = {"tp": 1 - self.tp}
        self.turn = [lax.rem(self.z + d, 4) for d in range(4)]
        self.over_z = [{"mol": self.turn[d] * 4 + self.x * 2 + self.core} for d in range(4)]

    def neighbour(self, k):
        core = self.core + (1 - 2 * self.core) * (k & 1)
        x = self.x + (1 - 2 * self.x) * (k >> 1 & 1)
        tp = self.tp + (1 - 2 * self.tp) * (k >> 2)
        return core * 4 + tp * 2 + x, {"mol": self.z * 4 + x * 2 + core, "tp": tp}

    def everyone(self):
        return [self.neighbour(k)[1] for k in range(1, 8)] + self.over_z[1:]


def span(start, size):
    return pl.ds(pl.multiple_of(start, size), size)


def add_rows(target, source, rows):
    step = 96 if rows % 96 == 0 else min(rows, 32)

    def piece(i, _):
        at = pl.ds(pl.multiple_of(i * step, step), step)
        target[at, :] = target[at, :] + source[at, :]
        return 0

    lax.fori_loop(0, rows // step, piece, 0)


FFN_CHUNKS = tuple((D * b, D, 0, HALF_D) for b in range(3))
QKV_CHUNKS = ((0, 256, 0, 3 * HALF_D), (256, 256, 0, 3 * HALF_D), (512, 256, 0, 2 * HALF_D), (512, 256, 2 * HALF_D, HALF_D))


class Reduction:
    kinds = 11

    def __init__(self, peers, chunks, part, total, from_core, from_tp, from_x, from_z, sends, recvs):
        self.peers, self.chunks, self.part, self.total = peers, chunks, part, total
        self.from_core, self.from_tp, self.from_x, self.from_z = from_core, from_tp, from_x, from_z
        self.sends, self.recvs = sends, recvs

    def place(self, c):
        p = self.peers
        row, rows, lane, lanes = self.chunks[c]
        half, quarter, least = rows // 2, rows // 4, rows // 16
        at_core = row + p.core * half
        at_x = at_core + p.x * quarter
        return (at_core, at_x, at_x + p.z * least), (half, quarter, least), slice(lane, lane + lanes)

    def buffers(self, c):
        row, rows, lane, lanes = self.chunks[c]
        at = slice(lane, lane + lanes)
        cut = lambda share: slice(row // share, (row + rows) // share)
        return (
            self.from_core.at[:, cut(2), at], self.from_tp.at[cut(2), at], self.from_x.at[cut(4), at],
            [self.from_z.at[d, cut(16), at] for d in range(3)],
        )

    def copy(self, c, kind):
        p = self.peers
        part, total = self.part, self.total
        (at_core, at_x, at_z), (half, quarter, least), lanes = self.place(c)
        from_core, from_tp, from_x, from_z = self.buffers(c)
        if kind == 0:
            src = part.at[:, span(self.chunks[c][0] + (1 - p.core) * half, half), lanes]
            dst, peer = from_core, p.over_core
        elif kind == 1:
            src, dst, peer = part.at[1 - p.tp, span(at_core, half), lanes], from_tp, p.over_tp
        elif kind == 2:
            src, dst, peer = part.at[p.tp, span(at_core + (1 - p.x) * quarter, quarter), lanes], from_x, p.over_x
        elif kind < 6:
            d = kind - 2
            src = part.at[p.tp, span(at_x + p.turn[d] * least, least), lanes]
            dst, peer = from_z[d - 1], p.over_z[d]
        elif kind < 9:
            src = dst = total.at[span(at_z, least), lanes]
            peer = p.over_z[kind - 5]
        elif kind == 9:
            src = dst = total.at[span(at_x, quarter), lanes]
            peer = p.over_x
        else:
            src = dst = total.at[span(at_core, half), lanes]
            peer = p.over_core
        return pltpu.make_async_remote_copy(
            src_ref=src, dst_ref=dst, send_sem=self.sends.at[c, kind], recv_sem=self.recvs.at[c, kind],
            device_id=peer, device_id_type=MESH,
        )

    def act(self, c, stage):
        p = self.peers
        part = self.part
        (at_core, at_x, at_z), (half, quarter, least), lanes = self.place(c)
        from_core, from_tp, from_x, from_z = self.buffers(c)
        mine = lambda at, rows: part.at[p.tp, span(at, rows), lanes]
        if stage == 0:
            self.copy(c, 0).start()
        elif stage == 1:
            self.copy(c, 0).wait_recv()
            add_rows(part.at[1 - p.tp, span(at_core, half), lanes], from_core.at[1 - p.tp], half)
            self.copy(c, 1).start()
            add_rows(mine(at_core, half), from_core.at[p.tp], half)
        elif stage == 2:
            self.copy(c, 1).wait_recv()
            away, kept = (1 - p.x) * quarter, p.x * quarter
            add_rows(mine(at_core + away, quarter), from_tp.at[span(away, quarter)], quarter)
            self.copy(c, 2).start()
            add_rows(mine(at_core + kept, quarter), from_tp.at[span(kept, quarter)], quarter)
        elif stage == 3:
            self.copy(c, 2).wait_recv()
            add_rows(mine(at_x, quarter), from_x, quarter)
            for kind in (3, 4, 5):
                self.copy(c, kind).start()
        elif stage == 4:
            for kind in (3, 4, 5):
                self.copy(c, kind).wait_recv()
            value = mine(at_z, least)[...].astype(f32)
            for d in range(3):
                value = value + from_z[d][...].astype(f32)
            self.total[span(at_z, least), lanes] = value.astype(bf16)
            for kind in (6, 7, 8):
                self.copy(c, kind).start()
        elif stage == 5:
            for kind in (6, 7, 8):
                self.copy(c, kind).wait_recv()
            self.copy(c, 9).start()
        elif stage == 6:
            self.copy(c, 9).wait_recv()
            self.copy(c, 10).start()
        elif stage == 7:
            self.copy(c, 10).wait_recv()
        else:
            for kind in range(self.kinds):
                self.copy(c, kind).wait_send()


class SmallReduction:
    def __init__(self, peers, part, total, from_near, from_z, sends, recvs):
        self.peers, self.part, self.total, self.from_near, self.from_z = peers, part, total, from_near, from_z
        self.sends, self.recvs = sends, recvs
        p = peers
        self.near = [p.neighbour(k) for k in range(8)]
        self.mine = span(self.near[0][0] * 32, 32)

    def copy(self, kind):
        p = self.peers
        if kind < 7:
            index, peer = self.near[kind + 1]
            src, dst = self.part.at[span(index * 32, 32)], self.from_near.at[kind]
        elif kind < 10:
            src = dst = self.from_z.at[p.z]
            peer = p.over_z[kind - 6]
        else:
            src = dst = self.total.at[self.mine]
            peer = self.near[kind - 9][1]
        return pltpu.make_async_remote_copy(
            src_ref=src, dst_ref=dst, send_sem=self.sends.at[kind], recv_sem=self.recvs.at[kind],
            device_id=peer, device_id_type=MESH,
        )

    def act(self, stage):
        hops = (range(0, 7), range(7, 10), range(10, 17))
        if stage == 4:
            for kind in range(17):
                self.copy(kind).wait_send()
            return
        if stage > 0:
            for kind in hops[stage - 1]:
                self.copy(kind).wait_recv()
        if stage == 1:
            value = self.part[self.mine, :]
            for k in range(7):
                value = value + self.from_near[k]
            self.from_z[self.peers.z] = value
        elif stage == 2:
            self.total[self.mine, :] = (self.from_z[0] + self.from_z[1]) + (self.from_z[2] + self.from_z[3])
        if stage < 3:
            for kind in hops[stage]:
                self.copy(kind).start()


def big_scratch(rows, lanes, chunks):
    sems = pltpu.SemaphoreType.DMA((chunks, Reduction.kinds))
    return [
        pltpu.VMEM((2, rows // 2, lanes), bf16), pltpu.VMEM((rows // 2, lanes), bf16),
        pltpu.VMEM((rows // 4, lanes), bf16), pltpu.VMEM((3, rows // 16, lanes), bf16), sems, sems,
    ]


def small_scratch():
    return [
        pltpu.VMEM((7, 32, 128), f32), pltpu.VMEM((4, 32, 128), f32),
        pltpu.SemaphoreType.DMA((17,)), pltpu.SemaphoreType.DMA((17,)),
    ]


class Gather:
    pieces = 6

    def __init__(self, peers, whole, sends, recvs):
        self.peers, self.whole, self.sends, self.recvs = peers, whole, sends, recvs
        self.quarter = peers.x * 2 + peers.core
        self.next_quarter = (1 - peers.x) * 2 + peers.core

    def rows(self, ref, quarter):
        count = ref.shape[0] // 4
        return ref.at[span(quarter * count, count), :]

    def copy(self, index, kind):
        p = self.peers
        if kind == 0:
            src = dst = self.rows(self.whole(index, p.tp), self.quarter)
            peer = p.over_tp
        elif kind == 1:
            src = dst = self.rows(self.whole(index, 1 - p.tp), self.quarter)
            peer = p.over_x
        else:
            src = dst = self.rows(self.whole(index, 1 - p.tp), self.quarter if kind == 2 else self.next_quarter)
            peer = p.over_core
        return pltpu.make_async_remote_copy(
            src_ref=src, dst_ref=dst, send_sem=self.sends.at[index, kind], recv_sem=self.recvs.at[index, kind],
            device_id=peer, device_id_type=MESH,
        )

    def start(self, indices):
        for index in indices:
            self.copy(index, 0).start()

    def onward_x(self, index):
        self.copy(index, 0).wait_recv()
        self.copy(index, 1).start()
        self.copy(index, 2).start()

    def onward_core(self, index):
        self.copy(index, 1).wait_recv()
        self.copy(index, 3).start()

    def arrive(self, index):
        self.copy(index, 2).wait_recv()
        self.copy(index, 3).wait_recv()

    def finish(self):
        for index in range(self.pieces):
            for kind in range(4):
                self.copy(index, kind).wait_send()


def square_turn(values):
    rows, lanes = values.shape
    if lanes < 128:
        values = jnp.concatenate([values, jnp.zeros((rows, 128 - lanes), f32)], axis=1)
    if rows < 128:
        values = jnp.concatenate([values, jnp.zeros((128 - rows, 128), f32)], axis=0)
    return values.T


def widen(values):
    return jnp.concatenate([values] * (TILE // 128), axis=1)


def strips():
    return [slice(16 * i, 16 * (i + 1)) for i in range(K // 16)]


def four_rows(ref, slot, first):
    return jnp.concatenate([ref[slot, pl.ds(first + i, 1), :] for i in range(TILE // 128)], axis=1)


def hot_rows(values, count):
    return (values == iota((count, TILE), 0).astype(f32)).astype(f32)


def fold_lanes(values):
    total = values[:, :128]
    for i in range(1, TILE // 128):
        total = total + values[:, 128 * i : 128 * (i + 1)]
    return total


def twice(ref, values):
    none = jnp.zeros_like(values)
    ref[...] = jnp.concatenate(
        [jnp.concatenate([values, none], axis=1), jnp.concatenate([none, values], axis=1)], axis=0
    ).astype(bf16)


def dot_halves(weights, pieces):
    values = jnp.concatenate(pieces, axis=0)
    half = TILE // 2
    both = dot_nn(weights, jnp.concatenate([values[:, :half], values[:, half:]], axis=0))
    rows = both.shape[0] // 2
    return jnp.concatenate([both[:rows], both[rows:]], axis=1)


def prepare_pairs(r):
    spr = to_column(row_of(r.spreads))
    r.cols[0] = jnp.broadcast_to(to_column(row_of(r.centers)), (K, 128))
    r.cols[1] = jnp.broadcast_to(root_half / spr, (K, 128))
    r.cols[2] = jnp.broadcast_to(-jnp.log(root_tau * spr), (K, 128))
    r.cols[3] = jnp.broadcast_to(to_column(row_of(r.first_bias)), (K, 128))
    r.cols[4] = jnp.broadcast_to(1.0 / spr, (K, 128))
    twice(r.w1, r.first_weight[...].astype(f32))
    twice(r.w1t, r.first_weight[...].astype(f32).T)
    r.w2[...] = square_turn(r.second_weight[...].astype(f32))
    table = jnp.concatenate([r.hop_table[...], r.edge_table[...], jnp.zeros((128 - HOPS - EDGES, H), f32)], axis=0)
    table = jnp.concatenate([table, jnp.zeros((128, 128 - H), f32)], axis=1).T[:H, :HOT]
    one = table.astype(bf16).astype(f32)
    r.base[...] = jnp.concatenate(
        [r.second_weight[...].astype(f32), one, table - one, jnp.zeros((H, 64), f32)], axis=1
    )


def bf16_parts(values, count):
    parts = []
    for _ in range(count):
        parts.append(values.astype(bf16))
        values = values - parts[-1].astype(f32)
    return parts


def pair_tables(r, slots):
    low = low_lanes(HALF)
    low_row = low_lanes(1)
    tables = [part.astype(f32) for ref in (r.kernel_scale, r.kernel_shift) for part in bf16_parts(ref[...], 3)]
    tables = jnp.concatenate([square_turn(part)[:ATOMS, :ATOMS] for part in tables], axis=1)
    tables = jnp.concatenate([tables, jnp.zeros((ATOMS, 128 - 6 * ATOMS), f32)], axis=1).astype(bf16)
    for group in range(slots // 2):
        lanes = slice(128 * group, 128 * (group + 1))
        atoms = r.atoms[lanes].astype(f32).reshape(1, 128)
        rows = jnp.concatenate([r.positions[:, lanes], atoms, jnp.zeros((4, 128), f32)], axis=0)
        columns = square_turn(rows)
        key_hot = (columns[:, 3:4] == iota((128, ATOMS), 1).astype(f32)).astype(f32).astype(bf16)
        picks = dot_nn(key_hot, tables).astype(bf16)
        turned = half_swap(rows)
        for s in range(2):
            slot = 2 * group + s
            tokens = slice(SLOT * s, SLOT * (s + 1))
            double = jnp.where(low_lanes(8), *((rows, turned) if s == 0 else (turned, rows)))
            total = None
            for c in range(3):
                column = columns[tokens, c : c + 1]
                offset = jnp.where(low, column[:HALF], column[HALF:]) - double[c : c + 1]
                total = offset * offset if total is None else total + offset * offset
            distance = jnp.sqrt(total)
            query_hot = (double[3:4] == iota((ATOMS, 128), 0).astype(f32)).astype(f32)
            three, none = [query_hot] * 3, [jnp.zeros((3 * ATOMS, 128), f32)]
            rest = [jnp.zeros((128 - 6 * ATOMS, 128), f32)]
            spread = jnp.concatenate(
                [jnp.concatenate(three + none + rest, axis=0), jnp.concatenate(none + three + rest, axis=0)], axis=1
            )
            both = dot_nn(picks[tokens], spread.astype(bf16))
            scale = jnp.where(low, both[:HALF, :128], both[HALF:, :128])
            shift = jnp.where(low, both[:HALF, 128:], both[HALF:, 128:])
            r.argument[slot] = scale * distance + shift
            r.distance[slot] = distance
            for source, target in ((r.hops, r.hop_rows), (r.edges, r.edge_rows)):
                values = source[:, lanes].astype(f32)
                top, bottom = values[:HALF], values[HALF:]
                if s == 0:
                    target[slot] = jnp.where(low, top, half_swap(bottom))
                else:
                    target[slot] = jnp.where(low, half_swap(top), bottom)
            r.atom_rows[slot] = jnp.broadcast_to(double[3:4], (8, 128))


def table_grads(r, slots):
    lefts, rights = [], []
    for slot in range(slots):
        query_hot = (r.atom_rows[slot, 0:1, :] == iota((ATOMS, 128), 0).astype(f32)).astype(f32)
        keys = jnp.concatenate([query_hot[:, :HALF], query_hot[:, HALF:SLOT]], axis=0)
        keys = jnp.concatenate([keys, keys], axis=1).astype(bf16)
        values = jnp.concatenate([r.dargs[slot] * r.distance[slot], r.dargs[slot]], axis=1)
        both = dot_nn(keys, jnp.concatenate(bf16_parts(values, 2), axis=0))
        low = low_lanes(ATOMS)
        for index in range(2):
            lanes = slice(128 * index, 128 * (index + 1))
            rights.append(bf16_parts(jnp.where(low, both[:ATOMS, lanes], both[ATOMS:, lanes]), 2))
        lefts.append(query_hot.astype(bf16))
    left = jnp.concatenate(lefts, axis=1)
    right = jnp.concatenate(
        [jnp.concatenate([rights[2 * s + index][part] for s in range(slots)], axis=1) for index in range(2) for part in range(2)],
        axis=0,
    )
    result = dot_nt(left, right)
    return [
        result[:, 2 * ATOMS * index : 2 * ATOMS * index + ATOMS] + result[:, 2 * ATOMS * index + ATOMS : 2 * ATOMS * (index + 1)]
        for index in range(2)
    ]


def in_stages(stages, count):
    held = {}
    for time in range(count + len(stages) - 1):
        for k, stage in reversed(list(enumerate(stages))):
            if 0 <= time - k < count:
                held[time - k] = stage(time - k, held.get(time - k))


TILES = PAIRS // TILE
ROWS = TILE // 128


def pair_forward(r, slot):
    bank = lax.rem(slot, 2)
    graph_on = r.flags[0, slot].astype(f32)
    space_on = r.flags[1, slot].astype(f32)
    factor = jnp.where(iota((H, 256), 1) < K, space_on, graph_on)
    r.lhs[...] = (r.base[...] * factor).astype(bf16)

    def kernels(tile, _):
        where = slice(tile * TILE, (tile + 1) * TILE)
        arg = four_rows(r.argument, slot, tile * ROWS)
        pieces = []
        for rows in strips():
            u = (arg - widen(r.cols[0, rows])) * widen(r.cols[1, rows])
            pieces.append(jnp.exp(widen(r.cols[2, rows]) - u * u).astype(bf16))
            r.left[bank, rows, where] = pieces[-1]
        return dot_halves(r.w1t[...], pieces)

    def hidden(tile, first):
        where = slice(tile * TILE, (tile + 1) * TILE)
        pieces = []
        for rows in strips():
            value, slope = gelu_parts(first[rows] + widen(r.cols[3, rows]))
            pieces.append(value.astype(bf16))
            r.left[bank, slice(K + rows.start, K + rows.stop), where] = pieces[-1]
            r.slope[bank, rows, where] = slope.astype(bf16)
        hot = jnp.concatenate(
            [
                hot_rows(four_rows(r.hop_rows, slot, tile * ROWS), HOPS),
                hot_rows(four_rows(r.edge_rows, slot, tile * ROWS), HOT - HOPS),
            ],
            axis=0,
        ).astype(bf16)
        return dot_nn(r.lhs[:, : K + 2 * HOT], jnp.concatenate(pieces + [hot] * 2, axis=0))

    def biases(tile, bias):
        bias = bias.astype(bf16).astype(f32)
        for i in range(ROWS):
            r.bias[slot, pl.ds(tile * ROWS + i, H, stride=HALF), :] = bias[:, 128 * i : 128 * (i + 1)]

    in_stages([kernels, hidden, biases], TILES)


def pair_backward(r, slot, between):
    bank = lax.rem(slot, 2)
    graph_on = r.flags[0, slot].astype(f32)
    space_on = r.flags[1, slot].astype(f32)
    twice(r.w2_twice, r.w2[:, :H] * space_on)

    def scores(tile, _):
        where = slice(tile * TILE, (tile + 1) * TILE)
        grad = jnp.concatenate(
            [r.bias[slot, pl.ds(tile * ROWS + i, H, stride=HALF), :] for i in range(ROWS)], axis=1
        )
        r.right[K:, where] = jnp.concatenate([grad * space_on, grad * graph_on], axis=0).astype(bf16)
        edge_hot = hot_rows(four_rows(r.edge_rows, slot, tile * ROWS), HOT - HOPS)
        edge_hot = jnp.where(iota((HOT - HOPS, TILE), 0) == EDGES, 1.0, edge_hot)
        r.left[bank, 2 * K :, where] = jnp.concatenate(
            [hot_rows(four_rows(r.hop_rows, slot, tile * ROWS), HOPS), edge_hot], axis=0
        ).astype(bf16)
        return dot_halves(r.w2_twice[...], [grad.astype(bf16)])

    def hidden(tile, d_second):
        where = slice(tile * TILE, (tile + 1) * TILE)
        pieces = []
        for rows in strips():
            pieces.append((d_second[rows] * r.slope[bank, rows, where].astype(f32)).astype(bf16))
            r.right[rows, where] = pieces[-1]
        return dot_halves(r.w1[...], pieces)

    def kernels(tile, d_gauss):
        where = slice(tile * TILE, (tile + 1) * TILE)
        arg = four_rows(r.argument, slot, tile * ROWS)
        d_arg = None
        for rows in strips():
            inv = widen(r.cols[4, rows])
            u = (arg - widen(r.cols[0, rows])) * inv
            q = d_gauss[rows] * r.left[bank, rows, where].astype(f32)
            w = q * u
            r.sums[0, rows] += fold_lanes(w)
            r.sums[1, rows] += fold_lanes(w * u - q)
            w = w * inv
            w = w[:8] + w[8:]
            d_arg = w if d_arg is None else d_arg + w
        d_arg = -jnp.sum(d_arg, axis=0, keepdims=True)
        for i in range(ROWS):
            at = tile * ROWS + i
            r.dargs[slot, at : at + 1, :] = d_arg[:, 128 * i : 128 * (i + 1)]

    in_stages([scores, hidden, kernels], TILES)
    between()
    r.acc_mixed[...] += dot_nt(r.left[bank], r.right[...])


def attend(r, s, first_slot):
    low = low_lanes(HALF)
    rows = span(s * SLOT, SLOT)
    valid = iota((SLOT, GROUP * SLOT), 0) < r.lengths[first_slot + s]
    r.work[0] = jnp.zeros((SLOT, D), f32)
    for g in range(GROUPS):
        start, width, _ = window(g)
        q = r.joined[rows, start : start + width]
        k = r.joined[rows, D + start : D + start + width]
        v = r.joined[rows, 2 * D + start : 2 * D + start + width]
        scores = dot_nt(k, spread_heads(q, g)) * head_scale
        parts = []
        for pair in range(GROUP // 2):
            head = GROUP * g + 2 * pair
            one = r.bias[s, head * HALF : (head + 1) * HALF, :]
            two = r.bias[s, (head + 1) * HALF : (head + 2) * HALF, :]
            top = jnp.where(low, one, half_swap(two))
            bottom = jnp.where(low, half_swap(one), two)
            parts.append(jnp.concatenate([top, bottom], axis=0))
        scores = jnp.where(valid, scores + jnp.concatenate(parts, axis=1), neg_large)
        weights = jnp.exp(scores - jnp.max(scores, axis=0, keepdims=True))
        prob = (weights * (1.0 / jnp.sum(weights, axis=0, keepdims=True))).astype(bf16)
        r.prob[s, :, g * GROUP * SLOT : (g + 1) * GROUP * SLOT] = prob
        r.work[0, :, start : start + width] += gather_heads(dot_tn(prob, v), g)
    r.attended[rows, :] = r.work[0].astype(bf16)


def attend_back(r, s):
    low = low_lanes(HALF)
    rows = span(s * SLOT, SLOT)
    r.work[...] = jnp.zeros((3, SLOT, D), f32)
    for g in range(GROUPS):
        start, width, _ = window(g)
        lanes = slice(start, start + width)
        k = r.joined[rows, D + start : D + start + width]
        v = r.joined[rows, 2 * D + start : 2 * D + start + width]
        q_heads = spread_heads(r.joined[rows, lanes], g)
        d_heads = spread_heads(r.d_attended[rows, lanes], g)
        prob = r.prob[s, :, g * GROUP * SLOT : (g + 1) * GROUP * SLOT]
        wide = prob.astype(f32)
        d_prob = dot_nt(v, d_heads)
        inner = jnp.sum(wide * d_prob, axis=0, keepdims=True)
        d_scores = (wide * (d_prob - inner)).astype(bf16)
        r.work[0, :, lanes] += gather_heads(dot_tn(d_scores, k), g)
        r.work[1, :, lanes] += dot_nn(d_scores, q_heads)
        r.work[2, :, lanes] += dot_nn(prob, d_heads)
        d_wide = d_scores.astype(f32)
        for pair in range(GROUP // 2):
            head = GROUP * g + 2 * pair
            top = d_wide[:HALF, 128 * pair : 128 * (pair + 1)]
            bottom = d_wide[HALF:, 128 * pair : 128 * (pair + 1)]
            r.bias[s, head * HALF : (head + 1) * HALF, :] = jnp.where(low, top, half_swap(bottom))
            r.bias[s, (head + 1) * HALF : (head + 2) * HALF, :] = jnp.where(low, half_swap(top), bottom)
    r.joined[rows, 0:D] = (r.work[0] * head_scale).astype(bf16)
    r.joined[rows, D : 2 * D] = (r.work[1] * head_scale).astype(bf16)
    r.joined[rows, 2 * D : 3 * D] = r.work[2].astype(bf16)


def project(r, rows):
    scaled, _ = standardize(r.hidden[rows, :].astype(f32))
    normed = (scaled * row_of(r.attn_gain) + row_of(r.attn_shift)).astype(bf16)
    r.normed_a[rows, :] = normed
    for m in range(3):
        for t in range(2):
            at = m * D + t * HALF_D
            r.joined[rows, at : at + HALF_D] = dot_nn(normed, r.wqkv[t, m]).astype(bf16)


def feed(r, rows):
    halves = [slice(0, HALF_D), slice(HALF_D, D)]
    resid = r.hidden[rows, :].astype(f32)
    for t in range(2):
        resid = resid + dot_nn(r.attended[rows, halves[t]], r.wproj[t])
    scaled, inv_std = standardize(resid)
    normed = (scaled * row_of(r.ffn_gain) + row_of(r.ffn_shift)).astype(bf16)
    r.normed_f[rows, :] = normed
    pre = jnp.concatenate([dot_nn(normed, r.wup[t]) for t in range(2)], axis=1)
    value, slope = gelu_parts(pre + row_of(r.up_bias))
    active = value.astype(bf16)
    r.activated[rows, :] = active
    result = resid + row_of(r.down_bias)
    for t in range(2):
        result = result + dot_nn(active[:, halves[t]], r.wdown[t])
    r.out_rows[rows, :] = result.astype(bf16)
    cot = r.cotangent[rows, :]
    cot_wide = cot.astype(f32)
    d_active = jnp.concatenate([dot_nt(cot, r.wdown[t]) for t in range(2)], axis=1)
    d_hidden = (d_active * slope).astype(bf16)
    r.d_pre[rows, :] = d_hidden
    d_normed = dot_nt(d_hidden[:, halves[0]], r.wup[0]) + dot_nt(d_hidden[:, halves[1]], r.wup[1])
    d_resid = cot_wide + norm_back(d_normed, scaled, inv_std, row_of(r.ffn_gain))
    r.d_resid[rows, :] = d_resid
    branch = d_resid.astype(bf16)
    r.d_branch[rows, :] = branch
    for t in range(2):
        r.d_attended[rows, halves[t]] = dot_nt(branch, r.wproj[t]).astype(bf16)
    r.vectors[2:3, :] += column_sum(d_normed * scaled)
    r.vectors[3:4, :] += column_sum(d_normed)
    r.vectors[4:5, :] += column_sum(d_hidden.astype(f32))
    r.vectors[5:6, :] += column_sum(cot_wide)


def feed_grads(r, block):
    halves = [slice(0, HALF_D), slice(HALF_D, D)]
    if block == 0:
        grad = dot_tn(r.normed_f[...], r.d_pre[...]).astype(bf16)
        for t in range(2):
            r.fpart[t, :D, :] = grad[:, halves[t]]
        return
    left, right = (r.attended, r.d_branch) if block == 1 else (r.activated, r.cotangent)
    for t in range(2):
        grad = dot_tn(left[:, halves[t]], right[...]).astype(bf16)
        for side in range(2):
            r.fpart[t, D * block + HALF_D * side : D * block + HALF_D * (side + 1), :] = grad[:, halves[side]]


def qkv_grads(r, rows, thirds):
    for m in thirds:
        grad = dot_tn(r.normed_a[:, rows], r.joined[:, m * D : (m + 1) * D]).astype(bf16)
        for t in range(2):
            r.qpart[t, rows, m * HALF_D : (m + 1) * HALF_D] = grad[:, t * HALF_D : (t + 1) * HALF_D]


def finish_input(r, rows):
    d_normed = None
    for m in range(3):
        for t in range(2):
            at = m * D + t * HALF_D
            term = dot_nt(r.joined[rows, at : at + HALF_D], r.wqkv[t, m])
            d_normed = term if d_normed is None else d_normed + term
    scaled, inv_std = standardize(r.hidden[rows, :].astype(f32))
    grad = r.d_resid[rows, :] + norm_back(d_normed, scaled, inv_std, row_of(r.attn_gain))
    r.in_rows[rows, :] = grad.astype(bf16)
    r.vectors[0:1, :] += column_sum(d_normed * scaled)
    r.vectors[1:2, :] += column_sum(d_normed)


def pack_small(r, slots):
    tables = table_grads(r, slots)
    for v in range(6):
        for i in range(D // 128):
            at = VECTOR_ROWS + v * (D // 128) + i
            r.spart[at : at + 1, :] = r.vectors[v : v + 1, 128 * i : 128 * (i + 1)]
    r.spart[0:K, :] = r.acc_mixed[0:K, :K]
    r.spart[SECOND_ROWS : SECOND_ROWS + H, :] = square_turn(r.acc_mixed[K : 2 * K, K:])[:H]
    r.spart[TABLE_ROWS : TABLE_ROWS + H, :HOT] = square_turn(r.acc_mixed[2 * K :, K:])[H : 2 * H, :HOT]
    for index in range(2):
        rows = slice(TABLE_ROWS + ATOMS * index, TABLE_ROWS + ATOMS * (index + 1))
        r.spart[rows, HOT : HOT + ATOMS] = tables[index]
    ones = 2 * K + HOPS + EDGES
    r.spart[KERNEL_ROWS : KERNEL_ROWS + 1, :] = r.acc_mixed[ones : ones + 1, :K]
    for index in range(2):
        column = jnp.sum(r.sums[index] * r.cols[4], axis=1, keepdims=True)
        same = iota((K, K), 0) == iota((K, K), 1)
        at = KERNEL_ROWS + 1 + index
        r.spart[at : at + 1, :] = jnp.sum(jnp.where(same, column, 0.0), axis=0, keepdims=True)


class Stage:
    def __init__(self, names, near_inputs, carried, refs):
        self.r = SimpleNamespace(**dict(zip(names, refs)))
        r = self.r
        self.loads = {
            name: pltpu.make_async_copy(getattr(r, "given_" + name), getattr(r, name), r.input_sems.at[i])
            for i, name in enumerate(near_inputs)
        }
        self.stores = {
            name: pltpu.make_async_copy(getattr(r, name), getattr(r, name + "_far"), r.carry_sems.at[i])
            for i, name in enumerate(carried)
        }

    def load(self, *names):
        for name in names:
            self.loads[name].start()

    def need(self, *names):
        for name in names:
            self.loads[name].wait()

    def store(self, *names):
        for name in names:
            self.stores[name].start()

    def stored(self):
        for copy in self.stores.values():
            copy.wait()


def each_chunk(r, tokens, work, after=lambda c: None):
    chunk = min(256, tokens)

    def one(c, _):
        work(r, span(c * chunk, chunk))
        after(c)
        return 0

    lax.fori_loop(0, tokens // chunk, one, 0)


def pair_moves(r, slot, back):
    bank = lax.rem(slot, 2)
    both = (r.left_far.at[slot], r.left.at[bank, : 2 * K]), (r.slope_far.at[slot], r.slope.at[bank])
    for index, (far, near) in enumerate(both):
        yield pltpu.make_async_copy(*((far, near) if back else (near, far)), r.pair_sems.at[bank, index])


def start_moves(r, slot, back):
    for copy in pair_moves(r, slot, back):
        copy.start()


def wait_moves(r, slot, back):
    for copy in pair_moves(r, slot, back):
        copy.wait()


def run(steps):
    for act, *where in steps:
        act(*where)


def at_time(index, plan):
    for k, steps in plan.items():
        pl.when(index == k)(functools.partial(run, steps))


AFTER_FEED = [("f", 0, 1)]
IN_BACK = {0: [("f", 1, 1)], 1: [("f", 2, 1)], 5: [("f", 0, 2)]}
IN_GRADS = {1: [("f", 0, 3), ("f", 1, 2)], 2: [("q", 0, 1)], 3: [("q", 1, 1)]}
IN_INPUT = {0: [("q", 2, 1), ("q", 3, 1), ("f", 0, 4), ("f", 1, 3), ("f", 2, 2)]}
IN_PAIRS = {
    0: [("f", 0, 5)], 1: [("f", 2, 3), ("q", 0, 2)], 2: [("f", 1, 4)], 4: [("f", 0, 6), ("f", 2, 4), ("q", 1, 2)],
    5: [("q", 0, 3), ("f", 0, 7), ("f", 1, 5)], 6: [("q", 2, 2)], 7: [("f", 2, 5), ("q", 1, 3), ("q", 3, 2)],
    8: [("q", 0, 4), ("f", 1, 6)], 9: [("q", 2, 3)], 10: [("f", 1, 7), ("q", 1, 4)],
    11: [("f", 2, 6), ("q", 3, 3), ("q", 0, 5)], 12: [("q", 2, 4), ("f", 2, 7)], 14: [("q", 1, 5), ("q", 0, 6)],
    15: [("q", 3, 4), ("q", 2, 5)],
}
AT_END = (
    [("q", 0, 7), ("q", 1, 6), ("q", 3, 5)], [("q", 2, 6), ("q", 1, 7)], [("q", 3, 6), ("q", 2, 7)], [("q", 3, 7)],
)


def layer_kernel(remote, names, near_inputs, carried, *refs):
    stage = Stage(names, near_inputs, carried, refs)
    r = stage.r
    stage.load(*[name for name in near_inputs if name not in ("hidden", "cotangent")])
    tokens = r.hidden.shape[0]
    slots = tokens // SLOT
    peers = Peers()
    whole = [r.wqkv, r.wup, r.wproj, r.wdown]
    given = [r.given_qkv, r.given_up, r.given_proj, r.given_down]
    targets = [w.at[peers.tp] for w in whole] if remote else whole
    loads = [
        pltpu.make_async_copy(src, dst, r.load_sems.at[i]) for i, (src, dst) in enumerate(zip(given, targets))
    ]
    for load in loads:
        load.start()
    stage.load("hidden", "cotangent")
    gather_plan = {}
    if remote:

        def whole_piece(index, tp):
            return whole[0].at[tp, index] if index < 3 else whole[index - 2].at[tp]

        gather = Gather(peers, whole_piece, r.gather_sends, r.gather_recvs)
        ffn = Reduction(peers, FFN_CHUNKS, r.fpart, r.ftotal, r.f_core, r.f_tp, r.f_x, r.f_z, r.f_sends, r.f_recvs)
        qkv = Reduction(peers, QKV_CHUNKS, r.qpart, r.qtotal, r.q_core, r.q_tp, r.q_x, r.q_z, r.q_sends, r.q_recvs)
        small = SmallReduction(peers, r.spart, r.stotal, r.s_near, r.s_z, r.s_sends, r.s_recvs)
        greet(peers.everyone())
        for load, indices in zip(loads, ((0, 1, 2), (3,), (4,), (5,))):
            load.wait()
            gather.start(indices)
        x, core = gather.onward_x, gather.onward_core
        gather_plan = {
            0: [(x, 0)], 1: [(x, 1), (core, 0)], 2: [(x, 2), (core, 1)], 3: [(x, 3), (core, 2)],
            4: [(x, 4), (core, 3), (x, 5)], 5: [(core, 4)], 6: [(core, 5)],
        }

    def leave(which, c):
        near, far, chunks = ((r.ftotal, r.ftotal_far, FFN_CHUNKS), (r.qtotal, r.qtotal_far, QKV_CHUNKS))[which == "q"]
        row, rows, lane, lanes = chunks[c]
        at = (slice(row, row + rows), slice(lane, lane + lanes))
        index = c + len(FFN_CHUNKS) * (which == "q")
        return pltpu.make_async_copy(near.at[at], far.at[at], r.leave_sems.at[index])

    def advance(actions):
        if remote:
            for which, c, step in actions:
                (qkv if which == "q" else ffn).act(c, step)
                if step == 7:
                    leave(which, c).start()

    def advance_at(index, plan):
        at_time(index, {k: [(advance, actions)] for k, actions in plan.items()} if remote else {})

    stage.need(*[name for name in near_inputs if name not in ("hidden", "cotangent")])
    prepare_pairs(r)
    pair_tables(r, slots)

    def pairs(slot, _):
        pl.when(slot >= 2)(lambda: wait_moves(r, slot - 2, False))
        pair_forward(r, slot)
        start_moves(r, slot, False)
        at_time(slot, gather_plan)
        return 0

    lax.fori_loop(0, slots, pairs, 0)
    stage.need("hidden")
    if remote:
        for index in range(3):
            gather.arrive(index)
    else:
        for load in loads:
            load.wait()
    each_chunk(r, tokens, project)
    first_slot = peers.tp * slots

    def attend_one(s, _):
        attend(r, s, first_slot)
        return 0

    lax.fori_loop(0, slots, attend_one, 0)
    stage.need("cotangent")
    if remote:
        for index in range(3, 6):
            gather.arrive(index)
    r.vectors[...] = jnp.zeros_like(r.vectors)
    each_chunk(r, tokens, feed)
    stage.store("out_rows")
    for slot in (slots - 2, slots - 1):
        wait_moves(r, slot, False)
    start_moves(r, 0, True)
    start_moves(r, 1, True)
    for block in range(3):
        feed_grads(r, block)
        advance([("f", block, 0)])
    advance(AFTER_FEED)

    def back_one(s, _):
        attend_back(r, s)
        advance_at(s, IN_BACK)
        return 0

    lax.fori_loop(0, slots, back_one, 0)
    for c, (row, rows, lane, lanes) in enumerate(QKV_CHUNKS):
        qkv_grads(r, slice(row, row + rows), range(lane // HALF_D, (lane + lanes) // HALF_D))
        advance([("q", c, 0)] + IN_GRADS.get(c, []))

    each_chunk(r, tokens, finish_input, lambda c: advance_at(c, IN_INPUT))
    stage.store("in_rows")
    for ref in (r.sums, r.acc_mixed, r.spart):
        ref[...] = jnp.zeros_like(ref)

    def pairs_back(slot, _):
        wait_moves(r, slot, True)
        pair_backward(r, slot, lambda: advance_at(2 * slot, IN_PAIRS))
        pl.when(slot + 2 < slots)(lambda: start_moves(r, slot + 2, True))
        advance_at(2 * slot + 1, IN_PAIRS)
        return 0

    lax.fori_loop(0, slots, pairs_back, 0)
    pack_small(r, slots)
    if remote:
        for step in range(4):
            small.act(step)
            advance(AT_END[step])
        rows = pltpu.make_async_copy(r.stotal, r.stotal_far, r.leave_sems.at[7])
        rows.start()
        ends = [("f", c) for c in range(len(FFN_CHUNKS))] + [("q", c) for c in range(len(QKV_CHUNKS))]
        advance([(which, c, 8) for which, c in ends])
        small.act(4)
        gather.finish()
        for which, c in ends:
            leave(which, c).wait()
        rows.wait()
    else:
        stage.store("fpart", "qpart", "spart")
    stage.stored()


def call_stage(kernel, name, remote, collective, arrays, scalars, far, outs, carried, scratch):
    vm, sem = pltpu.VMEM, pltpu.SemaphoreType.DMA
    near = {n: vm(a.shape, a.dtype) for n, a in arrays.items() if n not in scalars + far}
    in_names = [n if n in scalars or n.endswith("_far") else "given_" + n for n in arrays]
    results = outs | {n + "_far": item for n, item in carried.items()}
    scratch = near | {n: vm(*item) for n, item in carried.items()} | scratch
    scratch |= {"input_sems": sem((len(near),)), "carry_sems": sem((len(carried),))}
    names = in_names + list(results) + list(scratch)
    values = pl.pallas_call(
        functools.partial(kernel, remote, names, list(near), list(carried)),
        in_specs=[pl.BlockSpec(memory_space=pltpu.SMEM if n in scalars else pl.ANY) for n in arrays],
        out_specs=[pl.BlockSpec(memory_space=pl.ANY)] * len(results),
        out_shape=[jax.ShapeDtypeStruct(*item) for item in results.values()],
        scratch_shapes=list(scratch.values()),
        compiler_params=pltpu.CompilerParams(
            vmem_limit_bytes=VMEM_BYTES, **(dict(collective_id=collective, has_side_effects=True) if remote else {})
        ),
        name=name,
    )(*arrays.values())
    return dict(zip(results, values))


def layer(remote, arrays):
    tokens = arrays["hidden"].shape[0]
    slots = tokens // SLOT
    v, sem = pltpu.VMEM, pltpu.SemaphoreType.DMA
    of_tokens = (tokens, D)
    table = (slots, HALF, 128)
    fshape, qshape, sshape = (3 * D, HALF_D), (D, 3 * HALF_D), (SMALL_ROWS, 128)
    outs = {"left_far": ((slots, 2 * K, PAIRS), bf16), "slope_far": ((slots, K, PAIRS), bf16)}
    carried = {"out_rows": (of_tokens, bf16), "in_rows": (of_tokens, bf16)}
    scratch = {
        "wqkv": v((2, 3, D, HALF_D), bf16), "wup": v((2, D, HALF_D), bf16), "wproj": v((2, HALF_D, D), bf16),
        "wdown": v((2, HALF_D, D), bf16), "load_sems": sem((4,)), "pair_sems": sem((2, 2)),
        "left": v((2, 2 * K + HOT, PAIRS), bf16), "slope": v((2, K, PAIRS), bf16),
        "right": v((K + 2 * H, PAIRS), bf16), "cols": v((5, K, 128), f32), "w1": v((2 * K, 2 * K), bf16), "w1t": v((2 * K, 2 * K), bf16),
        "w2": v((K, 128), f32), "w2_twice": v((2 * K, 2 * H), bf16), "base": v((H, 256), f32), "lhs": v((H, 256), bf16),
        "argument": v(table, f32), "distance": v(table, f32), "hop_rows": v(table, f32), "edge_rows": v(table, f32),
        "atom_rows": v((slots, 8, 128), f32), "dargs": v(table, f32), "bias": v((slots, H * HALF, 128), f32),
        "work": v((3, SLOT, D), f32), "normed_a": v(of_tokens, bf16), "joined": v((tokens, 3 * D), bf16),
        "prob": v((slots, SLOT, H * SLOT), bf16), "attended": v(of_tokens, bf16), "normed_f": v(of_tokens, bf16),
        "activated": v(of_tokens, bf16), "d_pre": v(of_tokens, bf16), "d_branch": v(of_tokens, bf16),
        "d_attended": v(of_tokens, bf16), "d_resid": v(of_tokens, f32), "vectors": v((8, D), f32),
        "sums": v((2, K, 128), f32), "acc_mixed": v((2 * K + HOT, K + 2 * H), f32),
    }
    parts = {"fpart": ((2,) + fshape, bf16), "qpart": ((2,) + qshape, bf16), "spart": (sshape, f32)}
    totals = {"ftotal": (fshape, bf16), "qtotal": (qshape, bf16), "stotal": (sshape, f32)}
    if remote:
        outs |= {n + "_far": item for n, item in totals.items()}
        scratch |= {n: v(*item) for n, item in (parts | totals).items()}
        scratch |= {"leave_sems": sem((8,)), "gather_sends": sem((6, 4)), "gather_recvs": sem((6, 4))}
        for name, shape in (("f", fshape + (len(FFN_CHUNKS),)), ("q", qshape + (len(QKV_CHUNKS),))):
            keys = ("_core", "_tp", "_x", "_z", "_sends", "_recvs")
            scratch |= {name + key: item for key, item in zip(keys, big_scratch(*shape))}
        scratch |= dict(zip(("s_near", "s_z", "s_sends", "s_recvs"), small_scratch()))
    else:
        carried |= parts
    results = call_stage(
        layer_kernel, "layer", remote, 0, arrays, ("lengths", "flags"), ("qkv", "up", "proj", "down"), outs, carried,
        scratch,
    )
    sums = [results[n + "_far"] for n in (totals if remote else parts)]
    return results["out_rows_far"], results["in_rows_far"], sums


RESULTS = (
    "output", "grad_input", "attn_gain", "attn_shift", "qkv", "proj", "ffn_gain", "ffn_shift", "up", "up_bias", "down",
    "down_bias", "scale", "shift", "centers", "spreads", "first", "first_bias", "second", "hop", "edge",
)


def unpack_kernel(*refs):
    given = SimpleNamespace(**dict(zip(("out_rows", "in_rows", "fsum", "qsum", "rows"), refs)))
    far = SimpleNamespace(**dict(zip(RESULTS, refs[5:])))
    count = len(RESULTS)
    near = SimpleNamespace(**dict(zip(RESULTS, refs[5 + count : 5 + 2 * count])))
    fsum, qsum, rows, load_sems, store_sems = refs[5 + 2 * count :]
    moves = [(given.rows, rows)]
    sources = ((given.qsum, qsum, 3), (given.fsum, fsum, 9), (given.out_rows, near.output, 1), (given.in_rows, near.grad_input, 1))
    for src, dst, pieces in sources:
        height = src.shape[0] // pieces
        for i in range(pieces):
            at = slice(i * height, (i + 1) * height)
            moves.append((src.at[at], dst.at[at]))
    loads = [pltpu.make_async_copy(src, dst, load_sems.at[i]) for i, (src, dst) in enumerate(moves)]
    for load in loads:
        load.start()
    stores = []

    def store(src, dst):
        stores.append(pltpu.make_async_copy(src, dst, store_sems.at[len(stores)]))
        stores[-1].start()

    for i in range(3):
        loads[1 + i].wait()
        at = slice(256 * i, 256 * (i + 1))
        for m in range(3):
            near.qkv[m, at] = qsum[at, m * HALF_D : (m + 1) * HALF_D].astype(f32)
        store(near.qkv.at[:, at], far.qkv.at[:, at])
    for i in range(3):
        loads[4 + i].wait()
        at = slice(256 * i, 256 * (i + 1))
        near.up[at, :] = fsum[at, :].astype(f32)
        store(near.up.at[at], far.up.at[at])
    for block, name in ((1, "proj"), (2, "down")):
        for i in range(3):
            loads[4 + 3 * block + i].wait()
        ref = getattr(near, name)
        at = D * block
        ref[:, :HALF_D] = fsum[at : at + HALF_D, :].astype(f32)
        ref[:, HALF_D:] = fsum[at + HALF_D : at + D, :].astype(f32)
        store(ref, getattr(far, name))
    loads[13].wait()
    store(near.output, far.output)
    loads[14].wait()
    store(near.grad_input, far.grad_input)
    loads[0].wait()
    names = ("attn_gain", "attn_shift", "ffn_gain", "ffn_shift", "up_bias", "down_bias")
    for v, name in enumerate(names):
        for i in range(D // 128):
            getattr(near, name)[pl.ds(128 * i, 128)] = rows[VECTOR_ROWS + v * (D // 128) + i, :]
    near.first[...] = rows[0:K, :]
    near.second[...] = rows[SECOND_ROWS : SECOND_ROWS + H, :]
    table = rows[TABLE_ROWS : TABLE_ROWS + H, :]
    near.scale[...] = table[:ATOMS, HOT : HOT + ATOMS]
    near.shift[...] = table[ATOMS:, HOT : HOT + ATOMS]
    turned = square_turn(table)
    near.hop[...] = turned[:HOPS, :H]
    near.edge[...] = turned[HOPS : HOPS + EDGES, :H]
    lines = ("first_bias", "centers", "spreads")
    for i, name in enumerate(lines):
        getattr(near, name)[...] = rows[KERNEL_ROWS + i, :]
    for name in names + ("first", "second", "scale", "shift", "hop", "edge") + lines:
        store(getattr(near, name), getattr(far, name))
    for copy in stores:
        copy.wait()


def unpack(out_rows, in_rows, fsum, qsum, rows):
    tokens = out_rows.shape[0]
    vec, line, types = ((D,), f32), ((K,), f32), ((ATOMS, ATOMS), f32)
    shapes = (
        ((tokens, D), bf16), ((tokens, D), bf16), vec, vec, ((3, D, HALF_D), f32), ((HALF_D, D), f32), vec, vec,
        ((D, HALF_D), f32), vec, ((HALF_D, D), f32), vec, types, types, line, line, ((K, K), f32), line, ((H, K), f32),
        ((HOPS, H), f32), ((EDGES, H), f32),
    )
    anywhere = pl.BlockSpec(memory_space=pl.ANY)
    return pl.pallas_call(
        unpack_kernel,
        in_specs=[anywhere] * 5,
        out_specs=[anywhere] * len(shapes),
        out_shape=[jax.ShapeDtypeStruct(*item) for item in shapes],
        scratch_shapes=[pltpu.VMEM(*item) for item in shapes] + [
            pltpu.VMEM(fsum.shape, bf16), pltpu.VMEM(qsum.shape, bf16), pltpu.VMEM(rows.shape, f32),
            pltpu.SemaphoreType.DMA((15,)), pltpu.SemaphoreType.DMA((25,)),
        ],
        compiler_params=pltpu.CompilerParams(vmem_limit_bytes=VMEM_BYTES),
        name="unpack",
    )(out_rows, in_rows, fsum, qsum, rows)


def whole_weights(qkv_weight, up_weight, proj_weight, down_weight):
    columns = lambda w: jnp.stack(jnp.split(w, 2, axis=-1))
    rows = lambda w: jnp.stack(jnp.split(w, 2, axis=0))
    gather = lambda w, dim: lax.all_gather(w, "tp", axis=dim, tiled=True)
    return (
        columns(gather(qkv_weight.transpose(1, 0, 2), 2)), columns(gather(up_weight, 1)),
        rows(gather(proj_weight, 0)), rows(gather(down_weight, 0)),
    )


def sum_grads(fgrads, qgrads, small):
    total_f, total_q, rows = lax.psum((fgrads, qgrads, small), ("mol", "tp"))
    share = D // lax.axis_size("tp")
    at = lax.axis_index("tp") * share

    def columns(halves):
        return lax.dynamic_slice_in_dim(jnp.concatenate(list(halves), axis=-1), at, share, halves.ndim - 2)

    def rows_of(block):
        part = total_f[:, D * block : D * (block + 1)]
        sides = jnp.concatenate([part[:, :HALF_D], part[:, HALF_D:]], axis=2).reshape(D, D)
        return lax.dynamic_slice_in_dim(sides, at, share, 0)

    qkv = columns(total_q.reshape(2, D, 3, HALF_D)).transpose(1, 0, 2)
    return [v.astype(f32) for v in (qkv, columns(total_f[:, :D]), rows_of(1), rows_of(2))], rows


def body(
    mesh_shape,
    hidden_in, positions, atom_types, hop_counts, edge_types, lengths, branches,
    attn_gain, attn_shift, qkv_weight, proj_weight, ffn_gain, ffn_shift, up_weight, up_bias, down_weight, down_bias,
    kernel_scale, kernel_shift, centers, spreads, first_weight, first_bias, second_weight, hop_table, edge_table,
    cotangent,
):
    remote = mesh_shape["tp"] == 2 and mesh_shape["mol"] == 16 and branches.shape[0] == 8
    if remote:
        weights = (qkv_weight.transpose(1, 0, 2), up_weight, proj_weight, down_weight)
    else:
        weights = whole_weights(qkv_weight, up_weight, proj_weight, down_weight)
    arrays = dict(
        lengths=lengths, flags=branches.T, positions=positions, atoms=atom_types, hops=hop_counts.T,
        edges=edge_types.T, kernel_scale=kernel_scale, kernel_shift=kernel_shift, centers=centers, spreads=spreads,
        first_weight=first_weight, first_bias=first_bias, second_weight=second_weight.T, hop_table=hop_table,
        edge_table=edge_table, attn_gain=attn_gain, attn_shift=attn_shift, ffn_gain=ffn_gain, ffn_shift=ffn_shift,
        up_bias=up_bias, down_bias=down_bias, hidden=hidden_in, cotangent=cotangent,
        qkv=weights[0], up=weights[1], proj=weights[2], down=weights[3],
    )
    output, grad_input, sums = layer(remote, arrays)
    if remote:
        fsum, qsum, rows = sums
    else:
        big, rows = sum_grads(*sums)
        fsum, qsum = jnp.zeros((3 * D, HALF_D), bf16), jnp.zeros((D, 3 * HALF_D), bf16)
    output, grad_input, *grads = unpack(output, grad_input, fsum, qsum, rows)
    if not remote:
        grads[2], grads[6], grads[3], grads[8] = big
    grads[2] = grads[2].transpose(1, 0, 2)
    grads[16] = grads[16].T
    return (output, grad_input, *grads)


def solution(mesh):
    rows = P(("mol", "tp"), None)
    all_of = P()
    in_specs = (
        rows, P(None, ("mol", "tp")), P(("mol", "tp")), rows, rows, P("mol"), rows, all_of, all_of,
        P(None, None, "tp"), P("tp", None), all_of, all_of, P(None, "tp"), all_of, P("tp", None),
    ) + (all_of,) * 10 + (rows,)
    out_specs = (
        rows, rows, all_of, all_of, P(None, None, "tp"), P("tp", None), all_of, all_of, P(None, "tp"), all_of,
        P("tp", None),
    ) + (all_of,) * 10
    step = functools.partial(body, dict(mesh.shape))
    return jax.shard_map(step, mesh=mesh, in_specs=in_specs, out_specs=out_specs, check_vma=False)
```

```python
import functools
from types import SimpleNamespace

import jax
import jax.numpy as jnp
from jax import lax
from jax.experimental import pallas as pl
from jax.experimental.pallas import tpu as pltpu
from jax.sharding import PartitionSpec as P

D = 768
H = 32
HD = 24
FF = 768
K = 128
SLOT = 64
HALF = SLOT // 2
HALF_D = D // 2
PAIRS = SLOT * SLOT
HOPS = 16
EDGES = 8
ATOMS = 16
GROUP = 4
GROUPS = H // GROUP
HOT = 32

highest = lax.Precision.HIGHEST
neg_large = -1e30
root_tau = 2.5066282746310002
root_half = 0.7071067811865476
inv_root_tau = 0.3989422804014327
head_scale = HD ** (-0.5)
VMEM_BYTES = 62 * 1024 * 1024
TILE = 512

SECOND_ROWS = K
TABLE_ROWS = SECOND_ROWS + H
KERNEL_ROWS = TABLE_ROWS + H
VECTOR_ROWS = KERNEL_ROWS + 8
SMALL_ROWS = 256

MESH = pl.DeviceIdType.MESH
f32 = jnp.float32
bf16 = jnp.bfloat16


def dot_nn(left, right, precision=None):
    return lax.dot_general(left, right, (((1,), (0,)), ((), ())), precision=precision, preferred_element_type=f32)


def dot_nt(left, right, precision=None):
    return lax.dot_general(left, right, (((1,), (1,)), ((), ())), precision=precision, preferred_element_type=f32)


def dot_tn(left, right, precision=None):
    return lax.dot_general(left, right, (((0,), (0,)), ((), ())), precision=precision, preferred_element_type=f32)


def iota(shape, dim):
    return lax.broadcasted_iota(jnp.int32, shape, dim)


def gelu_parts(values):
    size = jnp.abs(values)
    bell = jnp.exp(values * values * -0.5)
    denominator = 1.0 + (0.3275911 * root_half) * size
    t = pl.reciprocal(denominator, approx=True)
    series = 0.5 * 1.061405429
    for factor in (-1.453152027, 1.421413741, -0.284496736, 0.254829592):
        series = series * t + 0.5 * factor
    tail = series * t * bell
    gelu = jnp.maximum(values, 0.0) - size * tail
    outer = tail - size * (bell * inv_root_tau)
    return gelu, jnp.where(values >= 0.0, 1.0 - outer, outer)


def gelu_pair(values):
    size = jnp.abs(values)
    bell = jnp.exp(values * values * -0.5)
    t = pl.reciprocal(1.0 + (0.3275911 * root_half) * size, approx=True)
    series = 0.5 * 1.061405429
    for factor in (-1.453152027, 1.421413741, -0.284496736, 0.254829592):
        series = series * t + 0.5 * factor
    tail = (series * t * bell).astype(bf16)
    density = (bell * inv_root_tau).astype(bf16)
    values = values.astype(bf16)
    size = jnp.abs(values)
    outer = tail - size * density
    one, zero = jnp.ones((), bf16), jnp.zeros((), bf16)
    return jnp.maximum(values, zero) - size * tail, jnp.where(values >= zero, one - outer, outer)


def to_column(row):
    size = row.shape[1]
    same = iota((size, size), 0) == iota((size, size), 1)
    return jnp.sum(jnp.where(same, row, 0.0), axis=1, keepdims=True)


def half_swap(values):
    return pltpu.roll(values, 64, 1)


def low_lanes(rows):
    return iota((rows, 128), 1) < 64


def vmem(count):
    return [pl.BlockSpec(memory_space=pltpu.VMEM)] * count


def row_of(ref):
    return ref[...].reshape(1, ref.shape[0])


def place():
    mol = lax.axis_index("mol")
    return mol % 2, (mol // 2) % 2, mol // 4, lax.axis_index("tp")


def greet(peers):
    for peer in peers:
        pl.semaphore_signal(pltpu.get_barrier_semaphore(), inc=1, device_id=peer, device_id_type=MESH)


def await_greetings(peers):
    pl.semaphore_wait(pltpu.get_barrier_semaphore(), len(peers))


def window(group):
    first = GROUP * HD * group
    start = first // 128 * 128
    width = 128 if first - start + GROUP * HD <= 128 else 256
    return start, width, first - start


def head_masks(group, kind):
    _, width, offset = window(group)
    lane = iota((1, width), 1)
    return [
        ((lane >= offset + HD * h) & (lane < offset + HD * (h + 1))).astype(f32).astype(kind) for h in range(GROUP)
    ]


def spread_heads(values, group):
    return jnp.concatenate([values * mask for mask in head_masks(group, bf16)], axis=0)


def gather_heads(values, group):
    masks = head_masks(group, f32)
    total = values[:SLOT] * masks[0]
    for h in range(1, GROUP):
        total = total + values[SLOT * h : SLOT * (h + 1)] * masks[h]
    return total


def standardize(values):
    centred = values - jnp.mean(values, axis=-1, keepdims=True)
    inv_std = lax.rsqrt(jnp.mean(centred * centred, axis=-1, keepdims=True) + 1e-05)
    return centred * inv_std, inv_std


def norm_back(d_normed, scaled, inv_std, gain):
    weighted = d_normed * gain
    inner_a = jnp.mean(weighted, axis=-1, keepdims=True)
    inner_b = jnp.mean(weighted * scaled, axis=-1, keepdims=True)
    return inv_std * (weighted - inner_a - scaled * inner_b)


def column_sum(values):
    return jnp.sum(values, axis=0, keepdims=True)


class Peers:
    def __init__(self):
        self.core, self.x, self.z, self.tp = place()
        mol = lax.axis_index("mol")
        self.over_core = {"mol": mol + 1 - 2 * self.core}
        self.over_x = {"mol": mol + 2 - 4 * self.x}
        self.over_tp = {"tp": 1 - self.tp}
        self.turn = [lax.rem(self.z + d, 4) for d in range(4)]
        self.over_z = [{"mol": self.turn[d] * 4 + self.x * 2 + self.core} for d in range(4)]

    def neighbour(self, k):
        core = self.core + (1 - 2 * self.core) * (k & 1)
        x = self.x + (1 - 2 * self.x) * (k >> 1 & 1)
        tp = self.tp + (1 - 2 * self.tp) * (k >> 2)
        return core * 4 + tp * 2 + x, {"mol": self.z * 4 + x * 2 + core, "tp": tp}

    def everyone(self):
        return [self.neighbour(k)[1] for k in range(1, 8)] + self.over_z[1:]


def span(start, size):
    return pl.ds(pl.multiple_of(start, size), size)


def add_rows(target, source, rows):
    step = 96 if rows % 96 == 0 else min(rows, 32)

    def piece(i, _):
        at = pl.ds(pl.multiple_of(i * step, step), step)
        target[at, :] = target[at, :] + source[at, :]
        return 0

    lax.fori_loop(0, rows // step, piece, 0)


class Reduction:
    kinds = 11

    def __init__(self, peers, part, total, from_core, from_tp, from_x, from_z, sends, recvs):
        self.peers, self.part, self.total = peers, part, total
        self.from_core, self.from_tp, self.from_x, self.from_z = from_core, from_tp, from_x, from_z
        self.sends, self.recvs = sends, recvs
        self.half = from_core.shape[2]
        self.quarter, self.least = self.half // 2, self.half // 8

    def rows(self, b, level):
        p = self.peers
        at = b * 2 * self.half + p.core * self.half
        if level > 0:
            at = at + p.x * self.quarter
        return at + p.z * self.least if level > 1 else at

    def copy(self, b, kind):
        p = self.peers
        part, total = self.part, self.total
        half, quarter, least = self.half, self.quarter, self.least
        if kind == 0:
            src = part.at[:, span(b * 2 * half + (1 - p.core) * half, half)]
            dst, peer = self.from_core.at[b], p.over_core
        elif kind == 1:
            src, dst, peer = part.at[1 - p.tp, span(self.rows(b, 0), half)], self.from_tp.at[b], p.over_tp
        elif kind == 2:
            src = part.at[p.tp, span(self.rows(b, 0) + (1 - p.x) * quarter, quarter)]
            dst, peer = self.from_x.at[b], p.over_x
        elif kind < 6:
            d = kind - 2
            src = part.at[p.tp, span(self.rows(b, 1) + p.turn[d] * least, least)]
            dst, peer = self.from_z.at[b, d - 1], p.over_z[d]
        elif kind < 9:
            src = dst = total.at[span(self.rows(b, 2), least)]
            peer = p.over_z[kind - 5]
        elif kind == 9:
            src = dst = total.at[span(self.rows(b, 1), quarter)]
            peer = p.over_x
        else:
            src = dst = total.at[span(self.rows(b, 0), half)]
            peer = p.over_core
        return pltpu.make_async_remote_copy(
            src_ref=src, dst_ref=dst, send_sem=self.sends.at[b, kind], recv_sem=self.recvs.at[b, kind],
            device_id=peer, device_id_type=MESH,
        )

    def act(self, b, stage):
        p = self.peers
        half, quarter, least = self.half, self.quarter, self.least
        part = self.part
        if stage == 0:
            self.copy(b, 0).start()
        elif stage == 1:
            self.copy(b, 0).wait_recv()
            at = span(self.rows(b, 0), half)
            add_rows(part.at[1 - p.tp, at], self.from_core.at[b, 1 - p.tp], half)
            self.copy(b, 1).start()
            add_rows(part.at[p.tp, at], self.from_core.at[b, p.tp], half)
        elif stage == 2:
            self.copy(b, 1).wait_recv()
            away, mine = (1 - p.x) * quarter, p.x * quarter
            at = self.rows(b, 0)
            add_rows(part.at[p.tp, span(at + away, quarter)], self.from_tp.at[b, span(away, quarter)], quarter)
            self.copy(b, 2).start()
            add_rows(part.at[p.tp, span(at + mine, quarter)], self.from_tp.at[b, span(mine, quarter)], quarter)
        elif stage == 3:
            self.copy(b, 2).wait_recv()
            add_rows(part.at[p.tp, span(self.rows(b, 1), quarter)], self.from_x.at[b], quarter)
            for kind in (3, 4, 5):
                self.copy(b, kind).start()
        elif stage == 4:
            for kind in (3, 4, 5):
                self.copy(b, kind).wait_recv()
            mine = span(self.rows(b, 2), least)
            value = part[p.tp, mine, :].astype(f32)
            for d in range(3):
                value = value + self.from_z[b, d].astype(f32)
            self.total[mine, :] = value.astype(bf16)
            for kind in (6, 7, 8):
                self.copy(b, kind).start()
        elif stage == 5:
            for kind in (6, 7, 8):
                self.copy(b, kind).wait_recv()
            self.copy(b, 9).start()
        elif stage == 6:
            self.copy(b, 9).wait_recv()
            self.copy(b, 10).start()
        elif stage == 7:
            self.copy(b, 10).wait_recv()
        else:
            for kind in range(self.kinds):
                self.copy(b, kind).wait_send()


class SmallReduction:
    def __init__(self, peers, part, total, from_near, from_z, sends, recvs):
        self.peers, self.part, self.total, self.from_near, self.from_z = peers, part, total, from_near, from_z
        self.sends, self.recvs = sends, recvs
        p = peers
        self.near = [p.neighbour(k) for k in range(8)]
        self.mine = span(self.near[0][0] * 32, 32)

    def copy(self, kind):
        p = self.peers
        if kind < 7:
            index, peer = self.near[kind + 1]
            src, dst = self.part.at[span(index * 32, 32)], self.from_near.at[kind]
        elif kind < 10:
            src = dst = self.from_z.at[p.z]
            peer = p.over_z[kind - 6]
        else:
            src = dst = self.total.at[self.mine]
            peer = self.near[kind - 9][1]
        return pltpu.make_async_remote_copy(
            src_ref=src, dst_ref=dst, send_sem=self.sends.at[kind], recv_sem=self.recvs.at[kind],
            device_id=peer, device_id_type=MESH,
        )

    def act(self, stage):
        hops = (range(0, 7), range(7, 10), range(10, 17))
        if stage == 4:
            for kind in range(17):
                self.copy(kind).wait_send()
            return
        if stage > 0:
            for kind in hops[stage - 1]:
                self.copy(kind).wait_recv()
        if stage == 1:
            value = self.part[self.mine, :]
            for k in range(7):
                value = value + self.from_near[k]
            self.from_z[self.peers.z] = value
        elif stage == 2:
            self.total[self.mine, :] = (self.from_z[0] + self.from_z[1]) + (self.from_z[2] + self.from_z[3])
        if stage < 3:
            for kind in hops[stage]:
                self.copy(kind).start()


def big_scratch(rows, lanes):
    half = rows // 2
    sems = pltpu.SemaphoreType.DMA((3, Reduction.kinds))
    return [
        pltpu.VMEM((3, 2, half, lanes), bf16), pltpu.VMEM((3, half, lanes), bf16),
        pltpu.VMEM((3, half // 2, lanes), bf16), pltpu.VMEM((3, 3, half // 8, lanes), bf16), sems, sems,
    ]


def small_scratch():
    return [
        pltpu.VMEM((7, 32, 128), f32), pltpu.VMEM((4, 32, 128), f32),
        pltpu.SemaphoreType.DMA((17,)), pltpu.SemaphoreType.DMA((17,)),
    ]


class Gather:
    pieces = 6

    def __init__(self, peers, whole, sends, recvs):
        self.peers, self.whole, self.sends, self.recvs = peers, whole, sends, recvs
        self.quarter = peers.x * 2 + peers.core
        self.next_quarter = (1 - peers.x) * 2 + peers.core

    def rows(self, ref, quarter):
        count = ref.shape[0] // 4
        return ref.at[span(quarter * count, count), :]

    def copy(self, index, kind):
        p = self.peers
        if kind == 0:
            src = dst = self.rows(self.whole(index, p.tp), self.quarter)
            peer = p.over_tp
        elif kind == 1:
            src = dst = self.rows(self.whole(index, 1 - p.tp), self.quarter)
            peer = p.over_x
        else:
            src = dst = self.rows(self.whole(index, 1 - p.tp), self.quarter if kind == 2 else self.next_quarter)
            peer = p.over_core
        return pltpu.make_async_remote_copy(
            src_ref=src, dst_ref=dst, send_sem=self.sends.at[index, kind], recv_sem=self.recvs.at[index, kind],
            device_id=peer, device_id_type=MESH,
        )

    def start(self, indices):
        for index in indices:
            self.copy(index, 0).start()

    def onward_x(self, index):
        self.copy(index, 0).wait_recv()
        self.copy(index, 1).start()
        self.copy(index, 2).start()

    def onward_core(self, index):
        self.copy(index, 1).wait_recv()
        self.copy(index, 3).start()

    def arrive(self, index):
        self.copy(index, 2).wait_recv()
        self.copy(index, 3).wait_recv()

    def finish(self):
        for index in range(self.pieces):
            for kind in range(4):
                self.copy(index, kind).wait_send()


def square_turn(values):
    rows, lanes = values.shape
    if lanes < 128:
        values = jnp.concatenate([values, jnp.zeros((rows, 128 - lanes), f32)], axis=1)
    if rows < 128:
        values = jnp.concatenate([values, jnp.zeros((128 - rows, 128), f32)], axis=0)
    return values.T


def widen(values):
    return jnp.concatenate([values] * (TILE // 128), axis=1)


def strips():
    return [slice(16 * i, 16 * (i + 1)) for i in range(K // 16)]


def four_rows(ref, slot, first):
    return jnp.concatenate([ref[slot, pl.ds(first + i, 1), :] for i in range(TILE // 128)], axis=1)


def hot_rows(values, count):
    return (values == iota((count, TILE), 0).astype(f32)).astype(f32)


def fold_lanes(values):
    total = values[:, :128]
    for i in range(1, TILE // 128):
        total = total + values[:, 128 * i : 128 * (i + 1)]
    return total


def twice(ref, values):
    none = jnp.zeros_like(values)
    ref[...] = jnp.concatenate(
        [jnp.concatenate([values, none], axis=1), jnp.concatenate([none, values], axis=1)], axis=0
    ).astype(bf16)


def dot_halves(weights, pieces):
    values = jnp.concatenate(pieces, axis=0)
    half = TILE // 2
    both = dot_nn(weights, jnp.concatenate([values[:, :half], values[:, half:]], axis=0))
    rows = both.shape[0] // 2
    return jnp.concatenate([both[:rows], both[rows:]], axis=1)


def prepare_pairs(r):
    spr = to_column(row_of(r.spreads))
    r.cols[0] = jnp.broadcast_to(to_column(row_of(r.centers)), (K, 128))
    r.cols[1] = jnp.broadcast_to(root_half / spr, (K, 128))
    r.cols[2] = jnp.broadcast_to(-jnp.log(root_tau * spr), (K, 128))
    r.cols[3] = jnp.broadcast_to(to_column(row_of(r.first_bias)), (K, 128))
    r.cols[4] = jnp.broadcast_to(1.0 / spr, (K, 128))
    twice(r.w1, r.first_weight[...].astype(f32))
    twice(r.w1t, r.first_weight[...].astype(f32).T)
    r.w2[...] = square_turn(r.second_weight[...].astype(f32))
    table = jnp.concatenate([r.hop_table[...], r.edge_table[...], jnp.zeros((128 - HOPS - EDGES, H), f32)], axis=0)
    table = jnp.concatenate([table, jnp.zeros((128, 128 - H), f32)], axis=1).T[:H, :HOT]
    one = table.astype(bf16).astype(f32)
    r.base[...] = jnp.concatenate(
        [r.second_weight[...].astype(f32), one, table - one, jnp.zeros((H, 64), f32)], axis=1
    )


def bf16_parts(values, count):
    parts = []
    for _ in range(count):
        parts.append(values.astype(bf16))
        values = values - parts[-1].astype(f32)
    return parts


def pair_tables(r, slots):
    low = low_lanes(HALF)
    low_row = low_lanes(1)
    tables = [part.astype(f32) for ref in (r.kernel_scale, r.kernel_shift) for part in bf16_parts(ref[...], 3)]
    tables = jnp.concatenate([square_turn(part)[:ATOMS, :ATOMS] for part in tables], axis=1)
    tables = jnp.concatenate([tables, jnp.zeros((ATOMS, 128 - 6 * ATOMS), f32)], axis=1).astype(bf16)
    for group in range(slots // 2):
        lanes = slice(128 * group, 128 * (group + 1))
        atoms = r.atoms[lanes].astype(f32).reshape(1, 128)
        rows = jnp.concatenate([r.positions[:, lanes], atoms, jnp.zeros((4, 128), f32)], axis=0)
        columns = square_turn(rows)
        key_hot = (columns[:, 3:4] == iota((128, ATOMS), 1).astype(f32)).astype(f32).astype(bf16)
        picks = dot_nn(key_hot, tables).astype(bf16)
        turned = half_swap(rows)
        for s in range(2):
            slot = 2 * group + s
            tokens = slice(SLOT * s, SLOT * (s + 1))
            double = jnp.where(low_lanes(8), *((rows, turned) if s == 0 else (turned, rows)))
            total = None
            for c in range(3):
                column = columns[tokens, c : c + 1]
                offset = jnp.where(low, column[:HALF], column[HALF:]) - double[c : c + 1]
                total = offset * offset if total is None else total + offset * offset
            distance = jnp.sqrt(total)
            query_hot = (double[3:4] == iota((ATOMS, 128), 0).astype(f32)).astype(f32)
            three, none = [query_hot] * 3, [jnp.zeros((3 * ATOMS, 128), f32)]
            rest = [jnp.zeros((128 - 6 * ATOMS, 128), f32)]
            spread = jnp.concatenate(
                [jnp.concatenate(three + none + rest, axis=0), jnp.concatenate(none + three + rest, axis=0)], axis=1
            )
            both = dot_nn(picks[tokens], spread.astype(bf16))
            scale = jnp.where(low, both[:HALF, :128], both[HALF:, :128])
            shift = jnp.where(low, both[:HALF, 128:], both[HALF:, 128:])
            r.argument[slot] = scale * distance + shift
            r.distance[slot] = distance
            for source, target in ((r.hops, r.hop_rows), (r.edges, r.edge_rows)):
                values = source[:, lanes].astype(f32)
                top, bottom = values[:HALF], values[HALF:]
                if s == 0:
                    target[slot] = jnp.where(low, top, half_swap(bottom))
                else:
                    target[slot] = jnp.where(low, half_swap(top), bottom)
            r.atom_rows[slot] = jnp.broadcast_to(double[3:4], (8, 128))


def table_grads(r, slots):
    lefts, rights = [], []
    for slot in range(slots):
        query_hot = (r.atom_rows[slot, 0:1, :] == iota((ATOMS, 128), 0).astype(f32)).astype(f32)
        keys = jnp.concatenate([query_hot[:, :HALF], query_hot[:, HALF:SLOT]], axis=0)
        keys = jnp.concatenate([keys, keys], axis=1).astype(bf16)
        values = jnp.concatenate([r.dargs[slot] * r.distance[slot], r.dargs[slot]], axis=1)
        both = dot_nn(keys, jnp.concatenate(bf16_parts(values, 2), axis=0))
        low = low_lanes(ATOMS)
        for index in range(2):
            lanes = slice(128 * index, 128 * (index + 1))
            rights.append(bf16_parts(jnp.where(low, both[:ATOMS, lanes], both[ATOMS:, lanes]), 2))
        lefts.append(query_hot.astype(bf16))
    left = jnp.concatenate(lefts, axis=1)
    right = jnp.concatenate(
        [jnp.concatenate([rights[2 * s + index][part] for s in range(slots)], axis=1) for index in range(2) for part in range(2)],
        axis=0,
    )
    result = dot_nt(left, right)
    return [
        result[:, 2 * ATOMS * index : 2 * ATOMS * index + ATOMS] + result[:, 2 * ATOMS * index + ATOMS : 2 * ATOMS * (index + 1)]
        for index in range(2)
    ]


def in_stages(stages, count, beside=lambda time: None):
    held = {}
    for time in range(count + len(stages) - 1):
        for k, stage in reversed(list(enumerate(stages))):
            if 0 <= time - k < count:
                held[time - k] = stage(time - k, held.get(time - k))
        beside(time)


TILES = PAIRS // TILE
ROWS = TILE // 128


def pair_forward(r, slot, beside=lambda time: None):
    bank = lax.rem(slot, 2)
    graph_on = r.flags[0, slot].astype(f32)
    space_on = r.flags[1, slot].astype(f32)
    factor = jnp.where(iota((H, 256), 1) < K, space_on, graph_on)
    r.lhs[...] = (r.base[...] * factor).astype(bf16)

    def kernels(tile, _):
        where = slice(tile * TILE, (tile + 1) * TILE)
        arg = four_rows(r.argument, slot, tile * ROWS)
        pieces = []
        for rows in strips():
            u = (arg - widen(r.cols[0, rows])) * widen(r.cols[1, rows])
            pieces.append(jnp.exp(widen(r.cols[2, rows]) - u * u).astype(bf16))
            r.left[bank, rows, where] = pieces[-1]
        return dot_halves(r.w1t[...], pieces)

    def hidden(tile, first):
        where = slice(tile * TILE, (tile + 1) * TILE)
        pieces = []
        for rows in strips():
            value, slope = gelu_pair(first[rows] + widen(r.cols[3, rows]))
            pieces.append(value)
            r.left[bank, slice(K + rows.start, K + rows.stop), where] = pieces[-1]
            r.slope[bank, rows, where] = slope
        hot = jnp.concatenate(
            [
                hot_rows(four_rows(r.hop_rows, slot, tile * ROWS), HOPS),
                hot_rows(four_rows(r.edge_rows, slot, tile * ROWS), HOT - HOPS),
            ],
            axis=0,
        ).astype(bf16)
        return dot_nn(r.lhs[:, : K + 2 * HOT], jnp.concatenate(pieces + [hot] * 2, axis=0))

    def biases(tile, bias):
        bias = bias.astype(bf16).astype(f32)
        for i in range(ROWS):
            r.bias[slot, pl.ds(tile * ROWS + i, H, stride=HALF), :] = bias[:, 128 * i : 128 * (i + 1)]

    in_stages([kernels, hidden, biases], TILES, beside)


def pair_backward(r, slot, between):
    bank = lax.rem(slot, 2)
    graph_on = r.flags[0, slot].astype(f32)
    space_on = r.flags[1, slot].astype(f32)
    twice(r.w2_twice, r.w2[:, :H] * space_on)

    def scores(tile, _):
        where = slice(tile * TILE, (tile + 1) * TILE)
        grad = jnp.concatenate(
            [r.bias[slot, pl.ds(tile * ROWS + i, H, stride=HALF), :] for i in range(ROWS)], axis=1
        )
        r.right[K:, where] = jnp.concatenate([grad * space_on, grad * graph_on], axis=0).astype(bf16)
        edge_hot = hot_rows(four_rows(r.edge_rows, slot, tile * ROWS), HOT - HOPS)
        edge_hot = jnp.where(iota((HOT - HOPS, TILE), 0) == EDGES, 1.0, edge_hot)
        r.left[bank, 2 * K :, where] = jnp.concatenate(
            [hot_rows(four_rows(r.hop_rows, slot, tile * ROWS), HOPS), edge_hot], axis=0
        ).astype(bf16)
        return dot_halves(r.w2_twice[...], [grad.astype(bf16)])

    def hidden(tile, d_second):
        where = slice(tile * TILE, (tile + 1) * TILE)
        pieces = []
        for rows in strips():
            pieces.append((d_second[rows] * r.slope[bank, rows, where].astype(f32)).astype(bf16))
            r.right[rows, where] = pieces[-1]
        return dot_halves(r.w1[...], pieces)

    def kernels(tile, d_gauss):
        where = slice(tile * TILE, (tile + 1) * TILE)
        arg = four_rows(r.argument, slot, tile * ROWS)
        d_arg = None
        for rows in strips():
            inv = widen(r.cols[4, rows])
            u = (arg - widen(r.cols[0, rows])) * inv
            q = d_gauss[rows] * r.left[bank, rows, where].astype(f32)
            w = q * u
            r.sums[0, rows] += fold_lanes(w)
            r.sums[1, rows] += fold_lanes(w * u - q)
            w = w * inv
            w = w[:8] + w[8:]
            d_arg = w if d_arg is None else d_arg + w
        d_arg = -jnp.sum(d_arg, axis=0, keepdims=True)
        for i in range(ROWS):
            at = tile * ROWS + i
            r.dargs[slot, at : at + 1, :] = d_arg[:, 128 * i : 128 * (i + 1)]

    in_stages([scores, hidden, kernels], TILES)
    between()
    r.acc_mixed[...] += dot_nt(r.left[bank], r.right[...])


def attend_group(r, s, first_slot, g):
    low = low_lanes(HALF)
    rows = span(s * SLOT, SLOT)
    if g == 0:
        r.work[0] = jnp.zeros((SLOT, D), f32)
    valid = iota((SLOT, GROUP * SLOT), 0) < r.lengths[first_slot + s]
    start, width, _ = window(g)
    q = r.joined[rows, start : start + width]
    k = r.joined[rows, D + start : D + start + width]
    v = r.joined[rows, 2 * D + start : 2 * D + start + width]
    scores = dot_nt(k, spread_heads(q, g)) * head_scale
    parts = []
    for pair in range(GROUP // 2):
        head = GROUP * g + 2 * pair
        one = r.bias[s, head * HALF : (head + 1) * HALF, :]
        two = r.bias[s, (head + 1) * HALF : (head + 2) * HALF, :]
        top = jnp.where(low, one, half_swap(two))
        bottom = jnp.where(low, half_swap(one), two)
        parts.append(jnp.concatenate([top, bottom], axis=0))
    scores = jnp.where(valid, scores + jnp.concatenate(parts, axis=1), neg_large)
    weights = jnp.exp(scores - jnp.max(scores, axis=0, keepdims=True))
    prob = (weights * (1.0 / jnp.sum(weights, axis=0, keepdims=True))).astype(bf16)
    r.prob[s, :, g * GROUP * SLOT : (g + 1) * GROUP * SLOT] = prob
    r.work[0, :, start : start + width] += gather_heads(dot_tn(prob, v), g)
    if g == GROUPS - 1:
        r.attended[rows, :] = r.work[0].astype(bf16)


def attend_back(r, s):
    low = low_lanes(HALF)
    rows = span(s * SLOT, SLOT)
    r.work[...] = jnp.zeros((3, SLOT, D), f32)
    for g in range(GROUPS):
        start, width, _ = window(g)
        lanes = slice(start, start + width)
        k = r.joined[rows, D + start : D + start + width]
        v = r.joined[rows, 2 * D + start : 2 * D + start + width]
        q_heads = spread_heads(r.joined[rows, lanes], g)
        d_heads = spread_heads(r.d_attended[rows, lanes], g)
        prob = r.prob[s, :, g * GROUP * SLOT : (g + 1) * GROUP * SLOT]
        wide = prob.astype(f32)
        d_prob = dot_nt(v, d_heads)
        inner = jnp.sum(wide * d_prob, axis=0, keepdims=True)
        d_scores = (wide * (d_prob - inner)).astype(bf16)
        r.work[0, :, lanes] += gather_heads(dot_tn(d_scores, k), g)
        r.work[1, :, lanes] += dot_nn(d_scores, q_heads)
        r.work[2, :, lanes] += dot_nn(prob, d_heads)
        d_wide = d_scores.astype(f32)
        for pair in range(GROUP // 2):
            head = GROUP * g + 2 * pair
            top = d_wide[:HALF, 128 * pair : 128 * (pair + 1)]
            bottom = d_wide[HALF:, 128 * pair : 128 * (pair + 1)]
            r.bias[s, head * HALF : (head + 1) * HALF, :] = jnp.where(low, top, half_swap(bottom))
            r.bias[s, (head + 1) * HALF : (head + 2) * HALF, :] = jnp.where(low, half_swap(top), bottom)
    r.joined[rows, 0:D] = (r.work[0] * head_scale).astype(bf16)
    r.joined[rows, D : 2 * D] = (r.work[1] * head_scale).astype(bf16)
    r.joined[rows, 2 * D : 3 * D] = r.work[2].astype(bf16)


def project(r, rows):
    scaled, _ = standardize(r.hidden[rows, :].astype(f32))
    normed = (scaled * row_of(r.attn_gain) + row_of(r.attn_shift)).astype(bf16)
    r.normed_a[rows, :] = normed
    for m in range(3):
        for t in range(2):
            at = m * D + t * HALF_D
            r.joined[rows, at : at + HALF_D] = dot_nn(normed, r.wqkv[t, m]).astype(bf16)


def feed(r, rows):
    halves = [slice(0, HALF_D), slice(HALF_D, D)]
    resid = r.hidden[rows, :].astype(f32)
    for t in range(2):
        resid = resid + dot_nn(r.attended[rows, halves[t]], r.wproj[t])
    scaled, inv_std = standardize(resid)
    normed = (scaled * row_of(r.ffn_gain) + row_of(r.ffn_shift)).astype(bf16)
    r.normed_f[rows, :] = normed
    pre = jnp.concatenate([dot_nn(normed, r.wup[t]) for t in range(2)], axis=1)
    value, slope = gelu_parts(pre + row_of(r.up_bias))
    active = value.astype(bf16)
    r.activated[rows, :] = active
    result = resid + row_of(r.down_bias)
    for t in range(2):
        result = result + dot_nn(active[:, halves[t]], r.wdown[t])
    r.out_rows[rows, :] = result.astype(bf16)
    cot = r.cotangent[rows, :]
    cot_wide = cot.astype(f32)
    d_active = jnp.concatenate([dot_nt(cot, r.wdown[t]) for t in range(2)], axis=1)
    d_hidden = (d_active * slope).astype(bf16)
    r.d_pre[rows, :] = d_hidden
    d_normed = dot_nt(d_hidden[:, halves[0]], r.wup[0]) + dot_nt(d_hidden[:, halves[1]], r.wup[1])
    d_resid = cot_wide + norm_back(d_normed, scaled, inv_std, row_of(r.ffn_gain))
    r.d_resid[rows, :] = d_resid
    branch = d_resid.astype(bf16)
    r.d_branch[rows, :] = branch
    for t in range(2):
        r.d_attended[rows, halves[t]] = dot_nt(branch, r.wproj[t]).astype(bf16)
    r.vectors[2:3, :] += column_sum(d_normed * scaled)
    r.vectors[3:4, :] += column_sum(d_normed)
    r.vectors[4:5, :] += column_sum(d_hidden.astype(f32))
    r.vectors[5:6, :] += column_sum(cot_wide)


def feed_grads(r, block):
    halves = [slice(0, HALF_D), slice(HALF_D, D)]
    if block == 0:
        grad = dot_tn(r.normed_f[...], r.d_pre[...]).astype(bf16)
        for t in range(2):
            r.fpart[t, :D, :] = grad[:, halves[t]]
        return
    left, right = (r.attended, r.d_branch) if block == 1 else (r.activated, r.cotangent)
    for t in range(2):
        grad = dot_tn(left[:, halves[t]], right[...]).astype(bf16)
        for side in range(2):
            r.fpart[t, D * block + HALF_D * side : D * block + HALF_D * (side + 1), :] = grad[:, halves[side]]


def qkv_grads(r, block):
    rows = slice(256 * block, 256 * (block + 1))
    for m in range(3):
        grad = dot_tn(r.normed_a[:, rows], r.joined[:, m * D : (m + 1) * D]).astype(bf16)
        for t in range(2):
            r.qpart[t, rows, m * HALF_D : (m + 1) * HALF_D] = grad[:, t * HALF_D : (t + 1) * HALF_D]


def finish_input(r, rows):
    d_normed = None
    for m in range(3):
        for t in range(2):
            at = m * D + t * HALF_D
            term = dot_nt(r.joined[rows, at : at + HALF_D], r.wqkv[t, m])
            d_normed = term if d_normed is None else d_normed + term
    scaled, inv_std = standardize(r.hidden[rows, :].astype(f32))
    grad = r.d_resid[rows, :] + norm_back(d_normed, scaled, inv_std, row_of(r.attn_gain))
    r.in_rows[rows, :] = grad.astype(bf16)
    r.vectors[0:1, :] += column_sum(d_normed * scaled)
    r.vectors[1:2, :] += column_sum(d_normed)


def pack_small(r, slots):
    tables = table_grads(r, slots)
    for v in range(6):
        for i in range(D // 128):
            at = VECTOR_ROWS + v * (D // 128) + i
            r.spart[at : at + 1, :] = r.vectors[v : v + 1, 128 * i : 128 * (i + 1)]
    r.spart[0:K, :] = r.acc_mixed[0:K, :K]
    r.spart[SECOND_ROWS : SECOND_ROWS + H, :] = square_turn(r.acc_mixed[K : 2 * K, K:])[:H]
    r.spart[TABLE_ROWS : TABLE_ROWS + H, :HOT] = square_turn(r.acc_mixed[2 * K :, K:])[H : 2 * H, :HOT]
    for index in range(2):
        rows = slice(TABLE_ROWS + ATOMS * index, TABLE_ROWS + ATOMS * (index + 1))
        r.spart[rows, HOT : HOT + ATOMS] = tables[index]
    ones = 2 * K + HOPS + EDGES
    r.spart[KERNEL_ROWS : KERNEL_ROWS + 1, :] = r.acc_mixed[ones : ones + 1, :K]
    for index in range(2):
        column = jnp.sum(r.sums[index] * r.cols[4], axis=1, keepdims=True)
        same = iota((K, K), 0) == iota((K, K), 1)
        at = KERNEL_ROWS + 1 + index
        r.spart[at : at + 1, :] = jnp.sum(jnp.where(same, column, 0.0), axis=0, keepdims=True)


class Stage:
    def __init__(self, names, near_inputs, carried, refs):
        self.r = SimpleNamespace(**dict(zip(names, refs)))
        r = self.r
        self.loads = {
            name: pltpu.make_async_copy(getattr(r, "given_" + name), getattr(r, name), r.input_sems.at[i])
            for i, name in enumerate(near_inputs)
        }
        self.stores = {
            name: pltpu.make_async_copy(getattr(r, name), getattr(r, name + "_far"), r.carry_sems.at[i])
            for i, name in enumerate(carried)
        }

    def load(self, *names):
        for name in names:
            self.loads[name].start()

    def need(self, *names):
        for name in names:
            self.loads[name].wait()

    def store(self, *names):
        for name in names:
            self.stores[name].start()

    def stored(self):
        for copy in self.stores.values():
            copy.wait()


def each_chunk(r, tokens, work):
    chunk = min(256, tokens)

    def one(c, _):
        work(r, span(c * chunk, chunk))
        return 0

    lax.fori_loop(0, tokens // chunk, one, 0)


def pair_moves(r, slot, back):
    bank = lax.rem(slot, 2)
    both = (r.left_far.at[slot], r.left.at[bank, : 2 * K]), (r.slope_far.at[slot], r.slope.at[bank])
    for index, (far, near) in enumerate(both):
        yield pltpu.make_async_copy(*((far, near) if back else (near, far)), r.pair_sems.at[bank, index])


def start_moves(r, slot, back):
    for copy in pair_moves(r, slot, back):
        copy.start()


def wait_moves(r, slot, back):
    for copy in pair_moves(r, slot, back):
        copy.wait()


def run(steps):
    for act, *where in steps:
        act(*where)


def at_time(index, plan):
    for k, steps in plan.items():
        pl.when(index == k)(functools.partial(run, steps))


FFN_BACK = {0: [(1, 1), (2, 1)], 3: [(0, 2)], 7: [(0, 3), (1, 2)]}
AFTER_GRADS = ([(0, 4), (1, 3), (2, 2)], [(0, 1), (1, 1), (2, 1)])
AFTER_HALF = ([(0, 5)], [])
AFTER_INPUT = ([(2, 3), (1, 4)], [(0, 2)])
FFN_PAIRS = {
    0: [(0, 6)], 2: [(2, 4)], 3: [(1, 5), (0, 7)], 5: [(2, 5)], 7: [(1, 6)], 9: [(2, 6)], 10: [(1, 7)], 12: [(2, 7)],
}
QKV_PAIRS = {
    2: [(0, 3)], 3: [(1, 2)], 6: [(1, 3), (2, 2), (0, 4)], 9: [(1, 4)], 10: [(0, 5)], 11: [(2, 3)], 12: [(1, 5)],
    13: [(0, 6)], 14: [(2, 4)], 15: [(1, 6)],
}


def layer_kernel(remote, names, near_inputs, carried, *refs):
    stage = Stage(names, near_inputs, carried, refs)
    r = stage.r
    stage.load(*[name for name in near_inputs if name not in ("hidden", "cotangent")])
    tokens = r.hidden.shape[0]
    slots = tokens // SLOT
    peers = Peers()
    if remote:
        greet(peers.everyone())
    whole = [r.wqkv, r.wup, r.wproj, r.wdown]
    given = [r.given_qkv, r.given_up, r.given_proj, r.given_down]
    targets = [w.at[peers.tp] for w in whole] if remote else whole
    loads = [
        pltpu.make_async_copy(src, dst, r.load_sems.at[i]) for i, (src, dst) in enumerate(zip(given, targets))
    ]
    for load in loads:
        load.start()
    stage.load("hidden", "cotangent")
    gather_plan = {}
    if remote:

        def whole_piece(index, tp):
            return whole[0].at[tp, index] if index < 3 else whole[index - 2].at[tp]

        gather = Gather(peers, whole_piece, r.gather_sends, r.gather_recvs)
        ffn = Reduction(peers, r.fpart, r.ftotal, r.f_core, r.f_tp, r.f_x, r.f_z, r.f_sends, r.f_recvs)
        qkv = Reduction(peers, r.qpart, r.qtotal, r.q_core, r.q_tp, r.q_x, r.q_z, r.q_sends, r.q_recvs)
        small = SmallReduction(peers, r.spart, r.stotal, r.s_near, r.s_z, r.s_sends, r.s_recvs)
        x, core = gather.onward_x, gather.onward_core
        gather_plan = {
            0: [(x, 0)], 1: [(x, 1)], 2: [(core, 0), (x, 2)], 3: [(core, 1), (x, 3), (core, 2)],
            4: [(x, 4)], 5: [(core, 3), (x, 5)], 6: [(core, 4)], 7: [(core, 5)],
        }

    def leave(which, block):
        near, far = ((r.ftotal, r.ftotal_far), (r.qtotal, r.qtotal_far))[which]
        rows = near.shape[0] // 3
        at = slice(block * rows, (block + 1) * rows)
        return pltpu.make_async_copy(near.at[at], far.at[at], r.leave_sems.at[3 * which + block])

    def advance(which, actions):
        if remote:
            for block, step in actions:
                (ffn, qkv)[which].act(block, step)
                if step == 7:
                    leave(which, block).start()

    def plan_of(*plans):
        times = sorted(set().union(*plans)) if remote else []
        return {
            k: [(advance, which, plan[k]) for which, plan in enumerate(plans) if k in plan] for k in times
        }

    stage.need(*[name for name in near_inputs if name not in ("hidden", "cotangent")])
    prepare_pairs(r)
    pair_tables(r, slots)
    if remote:
        await_greetings(peers.everyone())
        for load, indices in zip(loads, ((0, 1, 2), (3,), (4,), (5,))):
            load.wait()
            gather.start(indices)

    first_slot = peers.tp * slots
    alone = (5 * slots + 7) // 8

    def pairs(slot, _):
        pl.when(slot >= 2)(lambda: wait_moves(r, slot - 2, False))
        pair_forward(r, slot)
        start_moves(r, slot, False)
        at_time(slot, gather_plan)
        return 0

    def pairs_and_attention(slot, _):
        def beside(time):
            if 1 <= time <= GROUPS:
                attend_group(r, slot - alone, first_slot, time - 1)

        pl.when(slot >= 2)(lambda: wait_moves(r, slot - 2, False))
        pair_forward(r, slot, beside)
        start_moves(r, slot, False)
        at_time(slot, gather_plan)
        return 0

    def attend_one(s, _):
        for g in range(GROUPS):
            attend_group(r, s, first_slot, g)
        return 0

    lax.fori_loop(0, alone, pairs, 0)
    stage.need("hidden")
    if remote:
        for index in range(3):
            gather.arrive(index)
    else:
        for load in loads:
            load.wait()
    each_chunk(r, tokens, project)
    lax.fori_loop(alone, slots, pairs_and_attention, 0)
    lax.fori_loop(slots - alone, slots, attend_one, 0)
    stage.need("cotangent")
    if remote:
        for index in range(3, 6):
            gather.arrive(index)
    r.vectors[...] = jnp.zeros_like(r.vectors)
    each_chunk(r, tokens, feed)
    stage.store("out_rows")
    for slot in (slots - 2, slots - 1):
        wait_moves(r, slot, False)
    start_moves(r, 0, True)
    start_moves(r, 1, True)
    for block in range(3):
        feed_grads(r, block)
        advance(0, [(block, 0)])
    advance(0, [(0, 1)])

    back_plan, pair_plan = plan_of(FFN_BACK), plan_of(FFN_PAIRS, QKV_PAIRS)

    def back_one(s, _):
        attend_back(r, s)
        at_time(s, back_plan)
        return 0

    lax.fori_loop(0, slots, back_one, 0)
    for block in range(3):
        qkv_grads(r, block)
        advance(1, [(block, 0)])
    for which in range(2):
        advance(which, AFTER_GRADS[which])
    each_chunk(r, tokens, finish_input)
    stage.store("in_rows")
    for which in range(2):
        advance(which, AFTER_HALF[which] + AFTER_INPUT[which])
    for ref in (r.sums, r.acc_mixed, r.spart):
        ref[...] = jnp.zeros_like(ref)

    def pairs_back(slot, _):
        wait_moves(r, slot, True)
        pair_backward(r, slot, lambda: at_time(2 * slot, pair_plan))
        pl.when(slot + 2 < slots)(lambda: start_moves(r, slot + 2, True))
        at_time(2 * slot + 1, pair_plan)
        return 0

    lax.fori_loop(0, slots, pairs_back, 0)
    pack_small(r, slots)
    if remote:
        small.act(0)
        advance(1, [(2, 5), (0, 7)])
        small.act(1)
        advance(1, [(1, 7)])
        advance(1, [(2, 6)])
        small.act(2)
        advance(1, [(2, 7)])
        small.act(3)
        rows = pltpu.make_async_copy(r.stotal, r.stotal_far, r.leave_sems.at[6])
        rows.start()
        for which in range(2):
            advance(which, [(b, 8) for b in range(3)])
        small.act(4)
        gather.finish()
        for which in range(2):
            for block in range(3):
                leave(which, block).wait()
        rows.wait()
    else:
        stage.store("fpart", "qpart", "spart")
    stage.stored()


def call_stage(kernel, name, remote, collective, arrays, scalars, far, outs, carried, scratch):
    vm, sem = pltpu.VMEM, pltpu.SemaphoreType.DMA
    near = {n: vm(a.shape, a.dtype) for n, a in arrays.items() if n not in scalars + far}
    in_names = [n if n in scalars or n.endswith("_far") else "given_" + n for n in arrays]
    results = outs | {n + "_far": item for n, item in carried.items()}
    scratch = near | {n: vm(*item) for n, item in carried.items()} | scratch
    scratch |= {"input_sems": sem((len(near),)), "carry_sems": sem((len(carried),))}
    names = in_names + list(results) + list(scratch)
    values = pl.pallas_call(
        functools.partial(kernel, remote, names, list(near), list(carried)),
        in_specs=[pl.BlockSpec(memory_space=pltpu.SMEM if n in scalars else pl.ANY) for n in arrays],
        out_specs=[pl.BlockSpec(memory_space=pl.ANY)] * len(results),
        out_shape=[jax.ShapeDtypeStruct(*item) for item in results.values()],
        scratch_shapes=list(scratch.values()),
        compiler_params=pltpu.CompilerParams(
            vmem_limit_bytes=VMEM_BYTES, **(dict(collective_id=collective, has_side_effects=True) if remote else {})
        ),
        name=name,
    )(*arrays.values())
    return dict(zip(results, values))


def layer(remote, arrays):
    tokens = arrays["hidden"].shape[0]
    slots = tokens // SLOT
    v, sem = pltpu.VMEM, pltpu.SemaphoreType.DMA
    of_tokens = (tokens, D)
    table = (slots, HALF, 128)
    fshape, qshape, sshape = (3 * D, HALF_D), (D, 3 * HALF_D), (SMALL_ROWS, 128)
    outs = {"left_far": ((slots, 2 * K, PAIRS), bf16), "slope_far": ((slots, K, PAIRS), bf16)}
    carried = {"out_rows": (of_tokens, bf16), "in_rows": (of_tokens, bf16)}
    scratch = {
        "wqkv": v((2, 3, D, HALF_D), bf16), "wup": v((2, D, HALF_D), bf16), "wproj": v((2, HALF_D, D), bf16),
        "wdown": v((2, HALF_D, D), bf16), "load_sems": sem((4,)), "pair_sems": sem((2, 2)),
        "left": v((2, 2 * K + HOT, PAIRS), bf16), "slope": v((2, K, PAIRS), bf16),
        "right": v((K + 2 * H, PAIRS), bf16), "cols": v((5, K, 128), f32), "w1": v((2 * K, 2 * K), bf16), "w1t": v((2 * K, 2 * K), bf16),
        "w2": v((K, 128), f32), "w2_twice": v((2 * K, 2 * H), bf16), "base": v((H, 256), f32), "lhs": v((H, 256), bf16),
        "argument": v(table, f32), "distance": v(table, f32), "hop_rows": v(table, f32), "edge_rows": v(table, f32),
        "atom_rows": v((slots, 8, 128), f32), "dargs": v(table, f32), "bias": v((slots, H * HALF, 128), f32),
        "work": v((3, SLOT, D), f32), "normed_a": v(of_tokens, bf16), "joined": v((tokens, 3 * D), bf16),
        "prob": v((slots, SLOT, H * SLOT), bf16), "attended": v(of_tokens, bf16), "normed_f": v(of_tokens, bf16),
        "activated": v(of_tokens, bf16), "d_pre": v(of_tokens, bf16), "d_branch": v(of_tokens, bf16),
        "d_attended": v(of_tokens, bf16), "d_resid": v(of_tokens, f32), "vectors": v((8, D), f32),
        "sums": v((2, K, 128), f32), "acc_mixed": v((2 * K + HOT, K + 2 * H), f32),
    }
    parts = {"fpart": ((2,) + fshape, bf16), "qpart": ((2,) + qshape, bf16), "spart": (sshape, f32)}
    totals = {"ftotal": (fshape, bf16), "qtotal": (qshape, bf16), "stotal": (sshape, f32)}
    if remote:
        outs |= {n + "_far": item for n, item in totals.items()}
        scratch |= {n: v(*item) for n, item in (parts | totals).items()}
        scratch |= {"leave_sems": sem((7,)), "gather_sends": sem((6, 4)), "gather_recvs": sem((6, 4))}
        for name, shape in (("f", (D, HALF_D)), ("q", (D // 3, 3 * HALF_D))):
            keys = ("_core", "_tp", "_x", "_z", "_sends", "_recvs")
            scratch |= {name + key: item for key, item in zip(keys, big_scratch(*shape))}
        scratch |= dict(zip(("s_near", "s_z", "s_sends", "s_recvs"), small_scratch()))
    else:
        carried |= parts
    results = call_stage(
        layer_kernel, "layer", remote, 0, arrays, ("lengths", "flags"), ("qkv", "up", "proj", "down"), outs, carried,
        scratch,
    )
    sums = [results[n + "_far"] for n in (totals if remote else parts)]
    return results["out_rows_far"], results["in_rows_far"], sums


RESULTS = (
    "output", "grad_input", "attn_gain", "attn_shift", "qkv", "proj", "ffn_gain", "ffn_shift", "up", "up_bias", "down",
    "down_bias", "scale", "shift", "centers", "spreads", "first", "first_bias", "second", "hop", "edge",
)


def unpack_kernel(*refs):
    given = SimpleNamespace(**dict(zip(("out_rows", "in_rows", "fsum", "qsum", "rows"), refs)))
    far = SimpleNamespace(**dict(zip(RESULTS, refs[5:])))
    count = len(RESULTS)
    near = SimpleNamespace(**dict(zip(RESULTS, refs[5 + count : 5 + 2 * count])))
    fsum, qsum, rows, load_sems, store_sems = refs[5 + 2 * count :]
    moves = [(given.rows, rows)]
    sources = ((given.qsum, qsum, 3), (given.fsum, fsum, 9), (given.out_rows, near.output, 1), (given.in_rows, near.grad_input, 1))
    for src, dst, pieces in sources:
        height = src.shape[0] // pieces
        for i in range(pieces):
            at = slice(i * height, (i + 1) * height)
            moves.append((src.at[at], dst.at[at]))
    loads = [pltpu.make_async_copy(src, dst, load_sems.at[i]) for i, (src, dst) in enumerate(moves)]
    for load in loads:
        load.start()
    stores = []

    def store(src, dst):
        stores.append(pltpu.make_async_copy(src, dst, store_sems.at[len(stores)]))
        stores[-1].start()

    for i in range(3):
        loads[1 + i].wait()
        at = slice(256 * i, 256 * (i + 1))
        for m in range(3):
            near.qkv[m, at] = qsum[at, m * HALF_D : (m + 1) * HALF_D].astype(f32)
        store(near.qkv.at[:, at], far.qkv.at[:, at])
    for i in range(3):
        loads[4 + i].wait()
        at = slice(256 * i, 256 * (i + 1))
        near.up[at, :] = fsum[at, :].astype(f32)
        store(near.up.at[at], far.up.at[at])
    for block, name in ((1, "proj"), (2, "down")):
        for i in range(3):
            loads[4 + 3 * block + i].wait()
        ref = getattr(near, name)
        at = D * block
        ref[:, :HALF_D] = fsum[at : at + HALF_D, :].astype(f32)
        ref[:, HALF_D:] = fsum[at + HALF_D : at + D, :].astype(f32)
        store(ref, getattr(far, name))
    loads[13].wait()
    store(near.output, far.output)
    loads[14].wait()
    store(near.grad_input, far.grad_input)
    loads[0].wait()
    names = ("attn_gain", "attn_shift", "ffn_gain", "ffn_shift", "up_bias", "down_bias")
    for v, name in enumerate(names):
        for i in range(D // 128):
            getattr(near, name)[pl.ds(128 * i, 128)] = rows[VECTOR_ROWS + v * (D // 128) + i, :]
    near.first[...] = rows[0:K, :]
    near.second[...] = rows[SECOND_ROWS : SECOND_ROWS + H, :]
    table = rows[TABLE_ROWS : TABLE_ROWS + H, :]
    near.scale[...] = table[:ATOMS, HOT : HOT + ATOMS]
    near.shift[...] = table[ATOMS:, HOT : HOT + ATOMS]
    turned = square_turn(table)
    near.hop[...] = turned[:HOPS, :H]
    near.edge[...] = turned[HOPS : HOPS + EDGES, :H]
    lines = ("first_bias", "centers", "spreads")
    for i, name in enumerate(lines):
        getattr(near, name)[...] = rows[KERNEL_ROWS + i, :]
    for name in names + ("first", "second", "scale", "shift", "hop", "edge") + lines:
        store(getattr(near, name), getattr(far, name))
    for copy in stores:
        copy.wait()


def unpack(out_rows, in_rows, fsum, qsum, rows):
    tokens = out_rows.shape[0]
    vec, line, types = ((D,), f32), ((K,), f32), ((ATOMS, ATOMS), f32)
    shapes = (
        ((tokens, D), bf16), ((tokens, D), bf16), vec, vec, ((3, D, HALF_D), f32), ((HALF_D, D), f32), vec, vec,
        ((D, HALF_D), f32), vec, ((HALF_D, D), f32), vec, types, types, line, line, ((K, K), f32), line, ((H, K), f32),
        ((HOPS, H), f32), ((EDGES, H), f32),
    )
    anywhere = pl.BlockSpec(memory_space=pl.ANY)
    return pl.pallas_call(
        unpack_kernel,
        in_specs=[anywhere] * 5,
        out_specs=[anywhere] * len(shapes),
        out_shape=[jax.ShapeDtypeStruct(*item) for item in shapes],
        scratch_shapes=[pltpu.VMEM(*item) for item in shapes] + [
            pltpu.VMEM(fsum.shape, bf16), pltpu.VMEM(qsum.shape, bf16), pltpu.VMEM(rows.shape, f32),
            pltpu.SemaphoreType.DMA((15,)), pltpu.SemaphoreType.DMA((25,)),
        ],
        compiler_params=pltpu.CompilerParams(vmem_limit_bytes=VMEM_BYTES),
        name="unpack",
    )(out_rows, in_rows, fsum, qsum, rows)


def whole_weights(qkv_weight, up_weight, proj_weight, down_weight):
    columns = lambda w: jnp.stack(jnp.split(w, 2, axis=-1))
    rows = lambda w: jnp.stack(jnp.split(w, 2, axis=0))
    gather = lambda w, dim: lax.all_gather(w, "tp", axis=dim, tiled=True)
    return (
        columns(gather(qkv_weight.transpose(1, 0, 2), 2)), columns(gather(up_weight, 1)),
        rows(gather(proj_weight, 0)), rows(gather(down_weight, 0)),
    )


def sum_grads(fgrads, qgrads, small):
    total_f, total_q, rows = lax.psum((fgrads, qgrads, small), ("mol", "tp"))
    share = D // lax.axis_size("tp")
    at = lax.axis_index("tp") * share

    def columns(halves):
        return lax.dynamic_slice_in_dim(jnp.concatenate(list(halves), axis=-1), at, share, halves.ndim - 2)

    def rows_of(block):
        part = total_f[:, D * block : D * (block + 1)]
        sides = jnp.concatenate([part[:, :HALF_D], part[:, HALF_D:]], axis=2).reshape(D, D)
        return lax.dynamic_slice_in_dim(sides, at, share, 0)

    qkv = columns(total_q.reshape(2, D, 3, HALF_D)).transpose(1, 0, 2)
    return [v.astype(f32) for v in (qkv, columns(total_f[:, :D]), rows_of(1), rows_of(2))], rows


def body(
    mesh_shape,
    hidden_in, positions, atom_types, hop_counts, edge_types, lengths, branches,
    attn_gain, attn_shift, qkv_weight, proj_weight, ffn_gain, ffn_shift, up_weight, up_bias, down_weight, down_bias,
    kernel_scale, kernel_shift, centers, spreads, first_weight, first_bias, second_weight, hop_table, edge_table,
    cotangent,
):
    remote = mesh_shape["tp"] == 2 and mesh_shape["mol"] == 16 and branches.shape[0] == 8
    if remote:
        weights = (qkv_weight.transpose(1, 0, 2), up_weight, proj_weight, down_weight)
    else:
        weights = whole_weights(qkv_weight, up_weight, proj_weight, down_weight)
    arrays = dict(
        lengths=lengths, flags=branches.T, positions=positions, atoms=atom_types, hops=hop_counts.T,
        edges=edge_types.T, kernel_scale=kernel_scale, kernel_shift=kernel_shift, centers=centers, spreads=spreads,
        first_weight=first_weight, first_bias=first_bias, second_weight=second_weight.T, hop_table=hop_table,
        edge_table=edge_table, attn_gain=attn_gain, attn_shift=attn_shift, ffn_gain=ffn_gain, ffn_shift=ffn_shift,
        up_bias=up_bias, down_bias=down_bias, hidden=hidden_in, cotangent=cotangent,
        qkv=weights[0], up=weights[1], proj=weights[2], down=weights[3],
    )
    output, grad_input, sums = layer(remote, arrays)
    if remote:
        fsum, qsum, rows = sums
    else:
        big, rows = sum_grads(*sums)
        fsum, qsum = jnp.zeros((3 * D, HALF_D), bf16), jnp.zeros((D, 3 * HALF_D), bf16)
    output, grad_input, *grads = unpack(output, grad_input, fsum, qsum, rows)
    if not remote:
        grads[2], grads[6], grads[3], grads[8] = big
    grads[2] = grads[2].transpose(1, 0, 2)
    grads[16] = grads[16].T
    return (output, grad_input, *grads)


def solution(mesh):
    rows = P(("mol", "tp"), None)
    all_of = P()
    in_specs = (
        rows, P(None, ("mol", "tp")), P(("mol", "tp")), rows, rows, P("mol"), rows, all_of, all_of,
        P(None, None, "tp"), P("tp", None), all_of, all_of, P(None, "tp"), all_of, P("tp", None),
    ) + (all_of,) * 10 + (rows,)
    out_specs = (
        rows, rows, all_of, all_of, P(None, None, "tp"), P("tp", None), all_of, all_of, P(None, "tp"), all_of,
        P("tp", None),
    ) + (all_of,) * 10
    step = functools.partial(body, dict(mesh.shape))
    return jax.shard_map(step, mesh=mesh, in_specs=in_specs, out_specs=out_specs, check_vma=False)
```

```python
import functools
from types import SimpleNamespace

import jax
import jax.numpy as jnp
from jax import lax
from jax.experimental import pallas as pl
from jax.experimental.pallas import tpu as pltpu
from jax.sharding import PartitionSpec as P

D = 768
H = 32
HD = 24
FF = 768
K = 128
SLOT = 64
HALF = SLOT // 2
HALF_D = D // 2
PAIRS = SLOT * SLOT
HOPS = 16
EDGES = 8
ATOMS = 16
GROUP = 4
GROUPS = H // GROUP
HOT = 32

highest = lax.Precision.HIGHEST
neg_large = -1e30
root_tau = 2.5066282746310002
root_half = 0.7071067811865476
inv_root_tau = 0.3989422804014327
head_scale = HD ** (-0.5)
VMEM_BYTES = 62 * 1024 * 1024
TILE = 512

SECOND_ROWS = K
TABLE_ROWS = SECOND_ROWS + H
KERNEL_ROWS = TABLE_ROWS + H
VECTOR_ROWS = KERNEL_ROWS + 8
SMALL_ROWS = 256

MESH = pl.DeviceIdType.MESH
f32 = jnp.float32
bf16 = jnp.bfloat16


def dot_nn(left, right, precision=None):
    return lax.dot_general(left, right, (((1,), (0,)), ((), ())), precision=precision, preferred_element_type=f32)


def dot_nt(left, right, precision=None):
    return lax.dot_general(left, right, (((1,), (1,)), ((), ())), precision=precision, preferred_element_type=f32)


def dot_tn(left, right, precision=None):
    return lax.dot_general(left, right, (((0,), (0,)), ((), ())), precision=precision, preferred_element_type=f32)


def iota(shape, dim):
    return lax.broadcasted_iota(jnp.int32, shape, dim)


def gelu_parts(values):
    size = jnp.abs(values)
    bell = jnp.exp(values * values * -0.5)
    denominator = 1.0 + (0.3275911 * root_half) * size
    t = pl.reciprocal(denominator, approx=True)
    series = 0.5 * 1.061405429
    for factor in (-1.453152027, 1.421413741, -0.284496736, 0.254829592):
        series = series * t + 0.5 * factor
    tail = series * t * bell
    gelu = jnp.maximum(values, 0.0) - size * tail
    outer = tail - size * (bell * inv_root_tau)
    return gelu, jnp.where(values >= 0.0, 1.0 - outer, outer)


def gelu_pair(values):
    size = jnp.abs(values)
    bell = jnp.exp(values * values * -0.5)
    t = pl.reciprocal(1.0 + (0.3275911 * root_half) * size, approx=True)
    series = 0.5 * 1.061405429
    for factor in (-1.453152027, 1.421413741, -0.284496736, 0.254829592):
        series = series * t + 0.5 * factor
    tail = (series * t * bell).astype(bf16)
    density = (bell * inv_root_tau).astype(bf16)
    values = values.astype(bf16)
    size = jnp.abs(values)
    outer = tail - size * density
    one, zero = jnp.ones((), bf16), jnp.zeros((), bf16)
    return jnp.maximum(values, zero) - size * tail, jnp.where(values >= zero, one - outer, outer)


def to_column(row):
    size = row.shape[1]
    same = iota((size, size), 0) == iota((size, size), 1)
    return jnp.sum(jnp.where(same, row, 0.0), axis=1, keepdims=True)


def half_swap(values):
    return pltpu.roll(values, 64, 1)


def low_lanes(rows):
    return iota((rows, 128), 1) < 64


def vmem(count):
    return [pl.BlockSpec(memory_space=pltpu.VMEM)] * count


def row_of(ref):
    return ref[...].reshape(1, ref.shape[0])


def place():
    mol = lax.axis_index("mol")
    return mol % 2, (mol // 2) % 2, mol // 4, lax.axis_index("tp")


def greet(peers):
    for peer in peers:
        pl.semaphore_signal(pltpu.get_barrier_semaphore(), inc=1, device_id=peer, device_id_type=MESH)


def await_greetings(peers):
    pl.semaphore_wait(pltpu.get_barrier_semaphore(), len(peers))


def window(group):
    first = GROUP * HD * group
    start = first // 128 * 128
    width = 128 if first - start + GROUP * HD <= 128 else 256
    return start, width, first - start


def head_masks(group, kind):
    _, width, offset = window(group)
    lane = iota((1, width), 1)
    return [
        ((lane >= offset + HD * h) & (lane < offset + HD * (h + 1))).astype(f32).astype(kind) for h in range(GROUP)
    ]


def spread_heads(values, group):
    return jnp.concatenate([values * mask for mask in head_masks(group, bf16)], axis=0)


def gather_heads(values, group):
    masks = head_masks(group, f32)
    total = values[:SLOT] * masks[0]
    for h in range(1, GROUP):
        total = total + values[SLOT * h : SLOT * (h + 1)] * masks[h]
    return total


def standardize(values):
    centred = values - jnp.mean(values, axis=-1, keepdims=True)
    inv_std = lax.rsqrt(jnp.mean(centred * centred, axis=-1, keepdims=True) + 1e-05)
    return centred * inv_std, inv_std


def norm_back(d_normed, scaled, inv_std, gain):
    weighted = d_normed * gain
    inner_a = jnp.mean(weighted, axis=-1, keepdims=True)
    inner_b = jnp.mean(weighted * scaled, axis=-1, keepdims=True)
    return inv_std * (weighted - inner_a - scaled * inner_b)


def column_sum(values):
    return jnp.sum(values, axis=0, keepdims=True)


class Peers:
    def __init__(self):
        self.core, self.x, self.z, self.tp = place()
        mol = lax.axis_index("mol")
        self.over_core = {"mol": mol + 1 - 2 * self.core}
        self.over_x = {"mol": mol + 2 - 4 * self.x}
        self.over_tp = {"tp": 1 - self.tp}
        self.turn = [lax.rem(self.z + d, 4) for d in range(4)]
        self.over_z = [{"mol": self.turn[d] * 4 + self.x * 2 + self.core} for d in range(4)]

    def neighbour(self, k):
        core = self.core + (1 - 2 * self.core) * (k & 1)
        x = self.x + (1 - 2 * self.x) * (k >> 1 & 1)
        tp = self.tp + (1 - 2 * self.tp) * (k >> 2)
        return core * 4 + tp * 2 + x, {"mol": self.z * 4 + x * 2 + core, "tp": tp}

    def everyone(self):
        return [self.neighbour(k)[1] for k in range(1, 8)] + self.over_z[1:]


def span(start, size):
    return pl.ds(pl.multiple_of(start, size), size)


def add_rows(target, source, rows):
    step = 96 if rows % 96 == 0 else min(rows, 32)

    def piece(i, _):
        at = pl.ds(pl.multiple_of(i * step, step), step)
        target[at, :] = target[at, :] + source[at, :]
        return 0

    lax.fori_loop(0, rows // step, piece, 0)


class Reduction:
    kinds = 11

    def __init__(self, peers, part, total, from_core, from_tp, from_x, from_z, sends, recvs):
        self.peers, self.part, self.total = peers, part, total
        self.from_core, self.from_tp, self.from_x, self.from_z = from_core, from_tp, from_x, from_z
        self.sends, self.recvs = sends, recvs
        self.half = from_core.shape[2]
        self.quarter, self.least = self.half // 2, self.half // 8

    def rows(self, b, level):
        p = self.peers
        at = b * 2 * self.half + p.core * self.half
        if level > 0:
            at = at + p.x * self.quarter
        return at + p.z * self.least if level > 1 else at

    def copy(self, b, kind):
        p = self.peers
        part, total = self.part, self.total
        half, quarter, least = self.half, self.quarter, self.least
        if kind == 0:
            src = part.at[:, span(b * 2 * half + (1 - p.core) * half, half)]
            dst, peer = self.from_core.at[b], p.over_core
        elif kind == 1:
            src, dst, peer = part.at[1 - p.tp, span(self.rows(b, 0), half)], self.from_tp.at[b], p.over_tp
        elif kind == 2:
            src = part.at[p.tp, span(self.rows(b, 0) + (1 - p.x) * quarter, quarter)]
            dst, peer = self.from_x.at[b], p.over_x
        elif kind < 6:
            d = kind - 2
            src = part.at[p.tp, span(self.rows(b, 1) + p.turn[d] * least, least)]
            dst, peer = self.from_z.at[b, d - 1], p.over_z[d]
        elif kind < 9:
            src = dst = total.at[span(self.rows(b, 2), least)]
            peer = p.over_z[kind - 5]
        elif kind == 9:
            src = dst = total.at[span(self.rows(b, 1), quarter)]
            peer = p.over_x
        else:
            src = dst = total.at[span(self.rows(b, 0), half)]
            peer = p.over_core
        return pltpu.make_async_remote_copy(
            src_ref=src, dst_ref=dst, send_sem=self.sends.at[b, kind], recv_sem=self.recvs.at[b, kind],
            device_id=peer, device_id_type=MESH,
        )

    def act(self, b, stage):
        p = self.peers
        half, quarter, least = self.half, self.quarter, self.least
        part = self.part
        if stage == 0:
            self.copy(b, 0).start()
        elif stage == 1:
            self.copy(b, 0).wait_recv()
            at = span(self.rows(b, 0), half)
            add_rows(part.at[1 - p.tp, at], self.from_core.at[b, 1 - p.tp], half)
            self.copy(b, 1).start()
            add_rows(part.at[p.tp, at], self.from_core.at[b, p.tp], half)
        elif stage == 2:
            self.copy(b, 1).wait_recv()
            away, mine = (1 - p.x) * quarter, p.x * quarter
            at = self.rows(b, 0)
            add_rows(part.at[p.tp, span(at + away, quarter)], self.from_tp.at[b, span(away, quarter)], quarter)
            self.copy(b, 2).start()
            add_rows(part.at[p.tp, span(at + mine, quarter)], self.from_tp.at[b, span(mine, quarter)], quarter)
        elif stage == 3:
            self.copy(b, 2).wait_recv()
            add_rows(part.at[p.tp, span(self.rows(b, 1), quarter)], self.from_x.at[b], quarter)
            for kind in (3, 4, 5):
                self.copy(b, kind).start()
        elif stage == 4:
            for kind in (3, 4, 5):
                self.copy(b, kind).wait_recv()
            mine = span(self.rows(b, 2), least)
            value = part[p.tp, mine, :].astype(f32)
            for d in range(3):
                value = value + self.from_z[b, d].astype(f32)
            self.total[mine, :] = value.astype(bf16)
            for kind in (6, 7, 8):
                self.copy(b, kind).start()
        elif stage == 5:
            for kind in (6, 7, 8):
                self.copy(b, kind).wait_recv()
            self.copy(b, 9).start()
        elif stage == 6:
            self.copy(b, 9).wait_recv()
            self.copy(b, 10).start()
        elif stage == 7:
            self.copy(b, 10).wait_recv()
        else:
            for kind in range(self.kinds):
                self.copy(b, kind).wait_send()


class SmallReduction:
    def __init__(self, peers, part, total, from_near, from_z, sends, recvs):
        self.peers, self.part, self.total, self.from_near, self.from_z = peers, part, total, from_near, from_z
        self.sends, self.recvs = sends, recvs
        p = peers
        self.near = [p.neighbour(k) for k in range(8)]
        self.mine = span(self.near[0][0] * 32, 32)

    def copy(self, kind):
        p = self.peers
        if kind < 7:
            index, peer = self.near[kind + 1]
            src, dst = self.part.at[span(index * 32, 32)], self.from_near.at[kind]
        elif kind < 10:
            src = dst = self.from_z.at[p.z]
            peer = p.over_z[kind - 6]
        else:
            src = dst = self.total.at[self.mine]
            peer = self.near[kind - 9][1]
        return pltpu.make_async_remote_copy(
            src_ref=src, dst_ref=dst, send_sem=self.sends.at[kind], recv_sem=self.recvs.at[kind],
            device_id=peer, device_id_type=MESH,
        )

    def act(self, stage):
        hops = (range(0, 7), range(7, 10), range(10, 17))
        if stage == 4:
            for kind in range(17):
                self.copy(kind).wait_send()
            return
        if stage > 0:
            for kind in hops[stage - 1]:
                self.copy(kind).wait_recv()
        if stage == 1:
            value = self.part[self.mine, :]
            for k in range(7):
                value = value + self.from_near[k]
            self.from_z[self.peers.z] = value
        elif stage == 2:
            self.total[self.mine, :] = (self.from_z[0] + self.from_z[1]) + (self.from_z[2] + self.from_z[3])
        if stage < 3:
            for kind in hops[stage]:
                self.copy(kind).start()


def big_scratch(rows, lanes):
    half = rows // 2
    sems = pltpu.SemaphoreType.DMA((3, Reduction.kinds))
    return [
        pltpu.VMEM((3, 2, half, lanes), bf16), pltpu.VMEM((3, half, lanes), bf16),
        pltpu.VMEM((3, half // 2, lanes), bf16), pltpu.VMEM((3, 3, half // 8, lanes), bf16), sems, sems,
    ]


def small_scratch():
    return [
        pltpu.VMEM((7, 32, 128), f32), pltpu.VMEM((4, 32, 128), f32),
        pltpu.SemaphoreType.DMA((17,)), pltpu.SemaphoreType.DMA((17,)),
    ]


class Gather:
    pieces = 6

    def __init__(self, peers, whole, sends, recvs):
        self.peers, self.whole, self.sends, self.recvs = peers, whole, sends, recvs
        self.quarter = peers.x * 2 + peers.core
        self.next_quarter = (1 - peers.x) * 2 + peers.core

    def rows(self, ref, quarter):
        count = ref.shape[0] // 4
        return ref.at[span(quarter * count, count), :]

    def copy(self, index, kind):
        p = self.peers
        if kind == 0:
            src = dst = self.rows(self.whole(index, p.tp), self.quarter)
            peer = p.over_tp
        elif kind == 1:
            src = dst = self.rows(self.whole(index, 1 - p.tp), self.quarter)
            peer = p.over_x
        else:
            src = dst = self.rows(self.whole(index, 1 - p.tp), self.quarter if kind == 2 else self.next_quarter)
            peer = p.over_core
        return pltpu.make_async_remote_copy(
            src_ref=src, dst_ref=dst, send_sem=self.sends.at[index, kind], recv_sem=self.recvs.at[index, kind],
            device_id=peer, device_id_type=MESH,
        )

    def start(self, indices):
        for index in indices:
            self.copy(index, 0).start()

    def onward_x(self, index):
        self.copy(index, 0).wait_recv()
        self.copy(index, 1).start()
        self.copy(index, 2).start()

    def onward_core(self, index):
        self.copy(index, 1).wait_recv()
        self.copy(index, 3).start()

    def arrive(self, index):
        self.copy(index, 2).wait_recv()
        self.copy(index, 3).wait_recv()

    def finish(self):
        for index in range(self.pieces):
            for kind in range(4):
                self.copy(index, kind).wait_send()


def square_turn(values):
    rows, lanes = values.shape
    if lanes < 128:
        values = jnp.concatenate([values, jnp.zeros((rows, 128 - lanes), f32)], axis=1)
    if rows < 128:
        values = jnp.concatenate([values, jnp.zeros((128 - rows, 128), f32)], axis=0)
    return values.T


def widen(values):
    return jnp.concatenate([values] * (TILE // 128), axis=1)


def strips():
    return [slice(16 * i, 16 * (i + 1)) for i in range(K // 16)]


def four_rows(ref, slot, first):
    return jnp.concatenate([ref[slot, pl.ds(first + i, 1), :] for i in range(TILE // 128)], axis=1)


def hot_rows(values, count):
    return (values == iota((count, TILE), 0).astype(f32)).astype(f32)


def fold_lanes(values):
    total = values[:, :128]
    for i in range(1, TILE // 128):
        total = total + values[:, 128 * i : 128 * (i + 1)]
    return total


def twice(ref, values):
    none = jnp.zeros_like(values)
    ref[...] = jnp.concatenate(
        [jnp.concatenate([values, none], axis=1), jnp.concatenate([none, values], axis=1)], axis=0
    ).astype(bf16)


def dot_halves(weights, pieces):
    values = jnp.concatenate(pieces, axis=0)
    half = TILE // 2
    both = dot_nn(weights, jnp.concatenate([values[:, :half], values[:, half:]], axis=0))
    rows = both.shape[0] // 2
    return jnp.concatenate([both[:rows], both[rows:]], axis=1)


def prepare_pairs(r):
    spr = to_column(row_of(r.spreads))
    r.cols[0] = jnp.broadcast_to(to_column(row_of(r.centers)), (K, 128))
    r.cols[1] = jnp.broadcast_to(root_half / spr, (K, 128))
    r.cols[2] = jnp.broadcast_to(-jnp.log(root_tau * spr), (K, 128))
    r.cols[3] = jnp.broadcast_to(to_column(row_of(r.first_bias)), (K, 128))
    r.cols[4] = jnp.broadcast_to(1.0 / spr, (K, 128))
    twice(r.w1, r.first_weight[...].astype(f32))
    twice(r.w1t, r.first_weight[...].astype(f32).T)
    r.w2[...] = square_turn(r.second_weight[...].astype(f32))
    table = jnp.concatenate([r.hop_table[...], r.edge_table[...], jnp.zeros((128 - HOPS - EDGES, H), f32)], axis=0)
    table = jnp.concatenate([table, jnp.zeros((128, 128 - H), f32)], axis=1).T[:H, :HOT]
    one = table.astype(bf16).astype(f32)
    r.base[...] = jnp.concatenate(
        [r.second_weight[...].astype(f32), one, table - one, jnp.zeros((H, 64), f32)], axis=1
    )


def bf16_parts(values, count):
    parts = []
    for _ in range(count):
        parts.append(values.astype(bf16))
        values = values - parts[-1].astype(f32)
    return parts


def pair_tables(r, slots):
    low = low_lanes(HALF)
    low_row = low_lanes(1)
    tables = [part.astype(f32) for ref in (r.kernel_scale, r.kernel_shift) for part in bf16_parts(ref[...], 3)]
    tables = jnp.concatenate([square_turn(part)[:ATOMS, :ATOMS] for part in tables], axis=1)
    tables = jnp.concatenate([tables, jnp.zeros((ATOMS, 128 - 6 * ATOMS), f32)], axis=1).astype(bf16)
    for group in range(slots // 2):
        lanes = slice(128 * group, 128 * (group + 1))
        atoms = r.atoms[lanes].astype(f32).reshape(1, 128)
        rows = jnp.concatenate([r.positions[:, lanes], atoms, jnp.zeros((4, 128), f32)], axis=0)
        columns = square_turn(rows)
        key_hot = (columns[:, 3:4] == iota((128, ATOMS), 1).astype(f32)).astype(f32).astype(bf16)
        picks = dot_nn(key_hot, tables).astype(bf16)
        turned = half_swap(rows)
        for s in range(2):
            slot = 2 * group + s
            tokens = slice(SLOT * s, SLOT * (s + 1))
            double = jnp.where(low_lanes(8), *((rows, turned) if s == 0 else (turned, rows)))
            total = None
            for c in range(3):
                column = columns[tokens, c : c + 1]
                offset = jnp.where(low, column[:HALF], column[HALF:]) - double[c : c + 1]
                total = offset * offset if total is None else total + offset * offset
            distance = jnp.sqrt(total)
            query_hot = (double[3:4] == iota((ATOMS, 128), 0).astype(f32)).astype(f32)
            three, none = [query_hot] * 3, [jnp.zeros((3 * ATOMS, 128), f32)]
            rest = [jnp.zeros((128 - 6 * ATOMS, 128), f32)]
            spread = jnp.concatenate(
                [jnp.concatenate(three + none + rest, axis=0), jnp.concatenate(none + three + rest, axis=0)], axis=1
            )
            both = dot_nn(picks[tokens], spread.astype(bf16))
            scale = jnp.where(low, both[:HALF, :128], both[HALF:, :128])
            shift = jnp.where(low, both[:HALF, 128:], both[HALF:, 128:])
            r.argument[slot] = scale * distance + shift
            r.distance[slot] = distance
            for source, target in ((r.hops, r.hop_rows), (r.edges, r.edge_rows)):
                values = source[:, lanes].astype(f32)
                top, bottom = values[:HALF], values[HALF:]
                if s == 0:
                    target[slot] = jnp.where(low, top, half_swap(bottom))
                else:
                    target[slot] = jnp.where(low, half_swap(top), bottom)
            r.atom_rows[slot] = jnp.broadcast_to(double[3:4], (8, 128))


def table_grads(r, slots):
    lefts, rights = [], []
    for slot in range(slots):
        query_hot = (r.atom_rows[slot, 0:1, :] == iota((ATOMS, 128), 0).astype(f32)).astype(f32)
        keys = jnp.concatenate([query_hot[:, :HALF], query_hot[:, HALF:SLOT]], axis=0)
        keys = jnp.concatenate([keys, keys], axis=1).astype(bf16)
        values = jnp.concatenate([r.dargs[slot] * r.distance[slot], r.dargs[slot]], axis=1)
        both = dot_nn(keys, jnp.concatenate(bf16_parts(values, 2), axis=0))
        low = low_lanes(ATOMS)
        for index in range(2):
            lanes = slice(128 * index, 128 * (index + 1))
            rights.append(bf16_parts(jnp.where(low, both[:ATOMS, lanes], both[ATOMS:, lanes]), 2))
        lefts.append(query_hot.astype(bf16))
    left = jnp.concatenate(lefts, axis=1)
    right = jnp.concatenate(
        [jnp.concatenate([rights[2 * s + index][part] for s in range(slots)], axis=1) for index in range(2) for part in range(2)],
        axis=0,
    )
    result = dot_nt(left, right)
    return [
        result[:, 2 * ATOMS * index : 2 * ATOMS * index + ATOMS] + result[:, 2 * ATOMS * index + ATOMS : 2 * ATOMS * (index + 1)]
        for index in range(2)
    ]


def in_stages(stages, count, beside=lambda time: None):
    held = {}
    for time in range(count + len(stages) - 1):
        for k, stage in reversed(list(enumerate(stages))):
            if 0 <= time - k < count:
                held[time - k] = stage(time - k, held.get(time - k))
        beside(time)


TILES = PAIRS // TILE
ROWS = TILE // 128


def pair_forward(r, slot, beside=lambda time: None):
    bank = lax.rem(slot, 2)
    graph_on = r.flags[0, slot].astype(f32)
    space_on = r.flags[1, slot].astype(f32)
    factor = jnp.where(iota((H, 256), 1) < K, space_on, graph_on)
    r.lhs[...] = (r.base[...] * factor).astype(bf16)

    def kernels(tile, _):
        where = slice(tile * TILE, (tile + 1) * TILE)
        arg = four_rows(r.argument, slot, tile * ROWS)
        pieces = []
        for rows in strips():
            u = (arg - widen(r.cols[0, rows])) * widen(r.cols[1, rows])
            pieces.append(jnp.exp(widen(r.cols[2, rows]) - u * u).astype(bf16))
            r.left[bank, rows, where] = pieces[-1]
        return dot_halves(r.w1t[...], pieces)

    def hidden(tile, first):
        where = slice(tile * TILE, (tile + 1) * TILE)
        pieces = []
        for rows in strips():
            value, slope = gelu_pair(first[rows] + widen(r.cols[3, rows]))
            pieces.append(value)
            r.left[bank, slice(K + rows.start, K + rows.stop), where] = pieces[-1]
            r.slope[bank, rows, where] = slope
        hot = jnp.concatenate(
            [
                hot_rows(four_rows(r.hop_rows, slot, tile * ROWS), HOPS),
                hot_rows(four_rows(r.edge_rows, slot, tile * ROWS), HOT - HOPS),
            ],
            axis=0,
        ).astype(bf16)
        return dot_nn(r.lhs[:, : K + 2 * HOT], jnp.concatenate(pieces + [hot] * 2, axis=0))

    def biases(tile, bias):
        bias = bias.astype(bf16).astype(f32)
        for i in range(ROWS):
            r.bias[slot, pl.ds(tile * ROWS + i, H, stride=HALF), :] = bias[:, 128 * i : 128 * (i + 1)]

    in_stages([kernels, hidden, biases], TILES, beside)


def pair_backward(r, slot, between):
    bank = lax.rem(slot, 2)
    graph_on = r.flags[0, slot].astype(f32)
    space_on = r.flags[1, slot].astype(f32)
    twice(r.w2_twice, r.w2[:, :H] * space_on)

    def scores(tile, _):
        where = slice(tile * TILE, (tile + 1) * TILE)
        grad = jnp.concatenate(
            [r.bias[slot, pl.ds(tile * ROWS + i, H, stride=HALF), :] for i in range(ROWS)], axis=1
        )
        r.right[K:, where] = jnp.concatenate([grad * space_on, grad * graph_on], axis=0).astype(bf16)
        edge_hot = hot_rows(four_rows(r.edge_rows, slot, tile * ROWS), HOT - HOPS)
        edge_hot = jnp.where(iota((HOT - HOPS, TILE), 0) == EDGES, 1.0, edge_hot)
        r.left[bank, 2 * K :, where] = jnp.concatenate(
            [hot_rows(four_rows(r.hop_rows, slot, tile * ROWS), HOPS), edge_hot], axis=0
        ).astype(bf16)
        return dot_halves(r.w2_twice[...], [grad.astype(bf16)])

    def hidden(tile, d_second):
        where = slice(tile * TILE, (tile + 1) * TILE)
        pieces = []
        for rows in strips():
            pieces.append((d_second[rows] * r.slope[bank, rows, where].astype(f32)).astype(bf16))
            r.right[rows, where] = pieces[-1]
        return dot_halves(r.w1[...], pieces)

    def kernels(tile, d_gauss):
        where = slice(tile * TILE, (tile + 1) * TILE)
        arg = four_rows(r.argument, slot, tile * ROWS)
        d_arg = None
        for rows in strips():
            inv = widen(r.cols[4, rows])
            u = (arg - widen(r.cols[0, rows])) * inv
            q = d_gauss[rows] * r.left[bank, rows, where].astype(f32)
            w = q * u
            r.sums[0, rows] += fold_lanes(w)
            r.sums[1, rows] += fold_lanes(w * u - q)
            w = w * inv
            w = w[:8] + w[8:]
            d_arg = w if d_arg is None else d_arg + w
        d_arg = -jnp.sum(d_arg, axis=0, keepdims=True)
        for i in range(ROWS):
            at = tile * ROWS + i
            r.dargs[slot, at : at + 1, :] = d_arg[:, 128 * i : 128 * (i + 1)]

    in_stages([scores, hidden, kernels], TILES)
    between()
    r.acc_mixed[...] += dot_nt(r.left[bank], r.right[...])


def attend_group(r, s, first_slot, g):
    low = low_lanes(HALF)
    rows = span(s * SLOT, SLOT)
    if g == 0:
        r.work[0] = jnp.zeros((SLOT, D), f32)
    valid = iota((SLOT, GROUP * SLOT), 0) < r.lengths[first_slot + s]
    start, width, _ = window(g)
    q = r.joined[rows, start : start + width]
    k = r.joined[rows, D + start : D + start + width]
    v = r.joined[rows, 2 * D + start : 2 * D + start + width]
    scores = dot_nt(k, spread_heads(q, g)) * head_scale
    parts = []
    for pair in range(GROUP // 2):
        head = GROUP * g + 2 * pair
        one = r.bias[s, head * HALF : (head + 1) * HALF, :]
        two = r.bias[s, (head + 1) * HALF : (head + 2) * HALF, :]
        top = jnp.where(low, one, half_swap(two))
        bottom = jnp.where(low, half_swap(one), two)
        parts.append(jnp.concatenate([top, bottom], axis=0))
    scores = jnp.where(valid, scores + jnp.concatenate(parts, axis=1), neg_large)
    weights = jnp.exp(scores - jnp.max(scores, axis=0, keepdims=True))
    prob = (weights * (1.0 / jnp.sum(weights, axis=0, keepdims=True))).astype(bf16)
    r.prob[s, :, g * GROUP * SLOT : (g + 1) * GROUP * SLOT] = prob
    r.work[0, :, start : start + width] += gather_heads(dot_tn(prob, v), g)
    if g == GROUPS - 1:
        r.attended[rows, :] = r.work[0].astype(bf16)


def attend_back(r, s):
    low = low_lanes(HALF)
    rows = span(s * SLOT, SLOT)
    r.work[...] = jnp.zeros((3, SLOT, D), f32)
    for g in range(GROUPS):
        start, width, _ = window(g)
        lanes = slice(start, start + width)
        k = r.joined[rows, D + start : D + start + width]
        v = r.joined[rows, 2 * D + start : 2 * D + start + width]
        q_heads = spread_heads(r.joined[rows, lanes], g)
        d_heads = spread_heads(r.d_attended[rows, lanes], g)
        prob = r.prob[s, :, g * GROUP * SLOT : (g + 1) * GROUP * SLOT]
        wide = prob.astype(f32)
        d_prob = dot_nt(v, d_heads)
        inner = jnp.sum(wide * d_prob, axis=0, keepdims=True)
        d_scores = (wide * (d_prob - inner)).astype(bf16)
        r.work[0, :, lanes] += gather_heads(dot_tn(d_scores, k), g)
        r.work[1, :, lanes] += dot_nn(d_scores, q_heads)
        r.work[2, :, lanes] += dot_nn(prob, d_heads)
        d_wide = d_scores.astype(f32)
        for pair in range(GROUP // 2):
            head = GROUP * g + 2 * pair
            top = d_wide[:HALF, 128 * pair : 128 * (pair + 1)]
            bottom = d_wide[HALF:, 128 * pair : 128 * (pair + 1)]
            r.bias[s, head * HALF : (head + 1) * HALF, :] = jnp.where(low, top, half_swap(bottom))
            r.bias[s, (head + 1) * HALF : (head + 2) * HALF, :] = jnp.where(low, half_swap(top), bottom)
    r.joined[rows, 0:D] = (r.work[0] * head_scale).astype(bf16)
    r.joined[rows, D : 2 * D] = (r.work[1] * head_scale).astype(bf16)
    r.joined[rows, 2 * D : 3 * D] = r.work[2].astype(bf16)


def project(r, rows):
    scaled, _ = standardize(r.hidden[rows, :].astype(f32))
    normed = (scaled * row_of(r.attn_gain) + row_of(r.attn_shift)).astype(bf16)
    r.normed_a[rows, :] = normed
    for m in range(3):
        for t in range(2):
            at = m * D + t * HALF_D
            r.joined[rows, at : at + HALF_D] = dot_nn(normed, r.wqkv[t, m]).astype(bf16)


def feed(r, rows):
    halves = [slice(0, HALF_D), slice(HALF_D, D)]
    resid = r.hidden[rows, :].astype(f32)
    for t in range(2):
        resid = resid + dot_nn(r.attended[rows, halves[t]], r.wproj[t])
    scaled, inv_std = standardize(resid)
    normed = (scaled * row_of(r.ffn_gain) + row_of(r.ffn_shift)).astype(bf16)
    r.normed_f[rows, :] = normed
    pre = jnp.concatenate([dot_nn(normed, r.wup[t]) for t in range(2)], axis=1)
    value, slope = gelu_parts(pre + row_of(r.up_bias))
    active = value.astype(bf16)
    r.activated[rows, :] = active
    result = resid + row_of(r.down_bias)
    for t in range(2):
        result = result + dot_nn(active[:, halves[t]], r.wdown[t])
    r.out_rows[rows, :] = result.astype(bf16)
    cot = r.cotangent[rows, :]
    cot_wide = cot.astype(f32)
    d_active = jnp.concatenate([dot_nt(cot, r.wdown[t]) for t in range(2)], axis=1)
    d_hidden = (d_active * slope).astype(bf16)
    r.d_pre[rows, :] = d_hidden
    d_normed = dot_nt(d_hidden[:, halves[0]], r.wup[0]) + dot_nt(d_hidden[:, halves[1]], r.wup[1])
    d_resid = cot_wide + norm_back(d_normed, scaled, inv_std, row_of(r.ffn_gain))
    r.d_resid[rows, :] = d_resid
    branch = d_resid.astype(bf16)
    r.d_branch[rows, :] = branch
    for t in range(2):
        r.d_attended[rows, halves[t]] = dot_nt(branch, r.wproj[t]).astype(bf16)
    r.vectors[2:3, :] += column_sum(d_normed * scaled)
    r.vectors[3:4, :] += column_sum(d_normed)
    r.vectors[4:5, :] += column_sum(d_hidden.astype(f32))
    r.vectors[5:6, :] += column_sum(cot_wide)


def feed_grads(r, block):
    halves = [slice(0, HALF_D), slice(HALF_D, D)]
    if block == 0:
        grad = dot_tn(r.normed_f[...], r.d_pre[...]).astype(bf16)
        for t in range(2):
            r.fpart[t, :D, :] = grad[:, halves[t]]
        return
    left, right = (r.attended, r.d_branch) if block == 1 else (r.activated, r.cotangent)
    for t in range(2):
        grad = dot_tn(left[:, halves[t]], right[...]).astype(bf16)
        for side in range(2):
            r.fpart[t, D * block + HALF_D * side : D * block + HALF_D * (side + 1), :] = grad[:, halves[side]]


def qkv_grads(r, block):
    rows = slice(256 * block, 256 * (block + 1))
    for m in range(3):
        grad = dot_tn(r.normed_a[:, rows], r.joined[:, m * D : (m + 1) * D]).astype(bf16)
        for t in range(2):
            r.qpart[t, rows, m * HALF_D : (m + 1) * HALF_D] = grad[:, t * HALF_D : (t + 1) * HALF_D]


def finish_input(r, rows):
    d_normed = None
    for m in range(3):
        for t in range(2):
            at = m * D + t * HALF_D
            term = dot_nt(r.joined[rows, at : at + HALF_D], r.wqkv[t, m])
            d_normed = term if d_normed is None else d_normed + term
    scaled, inv_std = standardize(r.hidden[rows, :].astype(f32))
    grad = r.d_resid[rows, :] + norm_back(d_normed, scaled, inv_std, row_of(r.attn_gain))
    r.in_rows[rows, :] = grad.astype(bf16)
    r.vectors[0:1, :] += column_sum(d_normed * scaled)
    r.vectors[1:2, :] += column_sum(d_normed)


def pack_small(r, slots):
    tables = table_grads(r, slots)
    for v in range(6):
        for i in range(D // 128):
            at = VECTOR_ROWS + v * (D // 128) + i
            r.spart[at : at + 1, :] = r.vectors[v : v + 1, 128 * i : 128 * (i + 1)]
    r.spart[0:K, :] = r.acc_mixed[0:K, :K]
    r.spart[SECOND_ROWS : SECOND_ROWS + H, :] = square_turn(r.acc_mixed[K : 2 * K, K:])[:H]
    r.spart[TABLE_ROWS : TABLE_ROWS + H, :HOT] = square_turn(r.acc_mixed[2 * K :, K:])[H : 2 * H, :HOT]
    for index in range(2):
        rows = slice(TABLE_ROWS + ATOMS * index, TABLE_ROWS + ATOMS * (index + 1))
        r.spart[rows, HOT : HOT + ATOMS] = tables[index]
    ones = 2 * K + HOPS + EDGES
    r.spart[KERNEL_ROWS : KERNEL_ROWS + 1, :] = r.acc_mixed[ones : ones + 1, :K]
    for index in range(2):
        column = jnp.sum(r.sums[index] * r.cols[4], axis=1, keepdims=True)
        same = iota((K, K), 0) == iota((K, K), 1)
        at = KERNEL_ROWS + 1 + index
        r.spart[at : at + 1, :] = jnp.sum(jnp.where(same, column, 0.0), axis=0, keepdims=True)


class Stage:
    def __init__(self, names, near_inputs, carried, refs):
        self.r = SimpleNamespace(**dict(zip(names, refs)))
        r = self.r
        self.loads = {
            name: pltpu.make_async_copy(getattr(r, "given_" + name), getattr(r, name), r.input_sems.at[i])
            for i, name in enumerate(near_inputs)
        }
        self.stores = {
            name: pltpu.make_async_copy(getattr(r, name), getattr(r, name + "_far"), r.carry_sems.at[i])
            for i, name in enumerate(carried)
        }

    def load(self, *names):
        for name in names:
            self.loads[name].start()

    def need(self, *names):
        for name in names:
            self.loads[name].wait()

    def store(self, *names):
        for name in names:
            self.stores[name].start()

    def stored(self):
        for copy in self.stores.values():
            copy.wait()


def each_chunk(r, tokens, work):
    chunk = min(512, tokens)

    def one(c, _):
        work(r, span(c * chunk, chunk))
        return 0

    lax.fori_loop(0, tokens // chunk, one, 0)


def pair_moves(r, slot, back):
    bank = lax.rem(slot, 2)
    both = (r.left_far.at[slot], r.left.at[bank, : 2 * K]), (r.slope_far.at[slot], r.slope.at[bank])
    for index, (far, near) in enumerate(both):
        yield pltpu.make_async_copy(*((far, near) if back else (near, far)), r.pair_sems.at[bank, index])


def start_moves(r, slot, back):
    for copy in pair_moves(r, slot, back):
        copy.start()


def wait_moves(r, slot, back):
    for copy in pair_moves(r, slot, back):
        copy.wait()


def run(steps):
    for act, *where in steps:
        act(*where)


def at_time(index, plan):
    for k, steps in plan.items():
        pl.when(index == k)(functools.partial(run, steps))


FFN_BACK = {0: [(1, 1), (2, 1)], 3: [(0, 2)], 7: [(0, 3), (1, 2)]}
AFTER_GRADS = ([(0, 4), (1, 3), (2, 2)], [(0, 1), (1, 1), (2, 1)])
AFTER_HALF = ([(0, 5)], [])
AFTER_INPUT = ([(2, 3), (1, 4)], [(0, 2)])
FFN_PAIRS = {
    0: [(0, 6)], 2: [(2, 4)], 3: [(1, 5), (0, 7)], 5: [(2, 5)], 7: [(1, 6)], 9: [(2, 6)], 10: [(1, 7)], 12: [(2, 7)],
}
QKV_PAIRS = {
    2: [(0, 3)], 3: [(1, 2)], 6: [(1, 3), (2, 2), (0, 4)], 9: [(1, 4)], 10: [(0, 5)], 11: [(2, 3)], 12: [(1, 5)],
    13: [(0, 6)], 14: [(2, 4)], 15: [(1, 6)],
}


def layer_kernel(remote, names, near_inputs, carried, *refs):
    stage = Stage(names, near_inputs, carried, refs)
    r = stage.r
    stage.load(*[name for name in near_inputs if name not in ("hidden", "cotangent")])
    tokens = r.hidden.shape[0]
    slots = tokens // SLOT
    peers = Peers()
    if remote:
        greet(peers.everyone())
    whole = [r.wqkv, r.wup, r.wproj, r.wdown]
    given = [r.given_qkv, r.given_up, r.given_proj, r.given_down]
    targets = [w.at[peers.tp] for w in whole] if remote else whole
    loads = [
        pltpu.make_async_copy(src, dst, r.load_sems.at[i]) for i, (src, dst) in enumerate(zip(given, targets))
    ]
    for load in loads:
        load.start()
    stage.load("hidden", "cotangent")
    gather_plan = {}
    if remote:

        def whole_piece(index, tp):
            return whole[0].at[tp, index] if index < 3 else whole[index - 2].at[tp]

        gather = Gather(peers, whole_piece, r.gather_sends, r.gather_recvs)
        ffn = Reduction(peers, r.fpart, r.ftotal, r.f_core, r.f_tp, r.f_x, r.f_z, r.f_sends, r.f_recvs)
        qkv = Reduction(peers, r.qpart, r.qtotal, r.q_core, r.q_tp, r.q_x, r.q_z, r.q_sends, r.q_recvs)
        small = SmallReduction(peers, r.spart, r.stotal, r.s_near, r.s_z, r.s_sends, r.s_recvs)
        x, core = gather.onward_x, gather.onward_core
        gather_plan = {
            0: [(x, 0)], 1: [(x, 1)], 2: [(core, 0), (x, 2)], 3: [(core, 1), (x, 3), (core, 2)],
            4: [(x, 4)], 5: [(core, 3), (x, 5)], 6: [(core, 4)], 7: [(core, 5)],
        }

    def leave(which, block):
        near, far = ((r.ftotal, r.ftotal_far), (r.qtotal, r.qtotal_far))[which]
        rows = near.shape[0] // 3
        at = slice(block * rows, (block + 1) * rows)
        return pltpu.make_async_copy(near.at[at], far.at[at], r.leave_sems.at[3 * which + block])

    def advance(which, actions):
        if remote:
            for block, step in actions:
                (ffn, qkv)[which].act(block, step)
                if step == 7:
                    leave(which, block).start()

    def plan_of(*plans):
        times = sorted(set().union(*plans)) if remote else []
        return {
            k: [(advance, which, plan[k]) for which, plan in enumerate(plans) if k in plan] for k in times
        }

    stage.need(*[name for name in near_inputs if name not in ("hidden", "cotangent")])
    prepare_pairs(r)
    pair_tables(r, slots)
    if remote:
        await_greetings(peers.everyone())
        for load, indices in zip(loads, ((0, 1, 2), (3,), (4,), (5,))):
            load.wait()
            gather.start(indices)

    first_slot = peers.tp * slots
    alone = (5 * slots + 7) // 8

    def pairs(slot, _):
        pl.when(slot >= 2)(lambda: wait_moves(r, slot - 2, False))
        pair_forward(r, slot)
        start_moves(r, slot, False)
        at_time(slot, gather_plan)
        return 0

    def pairs_and_attention(slot, _):
        def beside(time):
            if 1 <= time <= GROUPS:
                attend_group(r, slot - alone, first_slot, time - 1)

        pl.when(slot >= 2)(lambda: wait_moves(r, slot - 2, False))
        pair_forward(r, slot, beside)
        start_moves(r, slot, False)
        at_time(slot, gather_plan)
        return 0

    def attend_one(s, _):
        for g in range(GROUPS):
            attend_group(r, s, first_slot, g)
        return 0

    lax.fori_loop(0, alone, pairs, 0)
    stage.need("hidden")
    if remote:
        for index in range(3):
            gather.arrive(index)
    else:
        for load in loads:
            load.wait()
    each_chunk(r, tokens, project)
    lax.fori_loop(alone, slots, pairs_and_attention, 0)
    lax.fori_loop(slots - alone, slots, attend_one, 0)
    stage.need("cotangent")
    if remote:
        for index in range(3, 6):
            gather.arrive(index)
    r.vectors[...] = jnp.zeros_like(r.vectors)
    each_chunk(r, tokens, feed)
    stage.store("out_rows")
    for slot in (slots - 2, slots - 1):
        wait_moves(r, slot, False)
    start_moves(r, 0, True)
    start_moves(r, 1, True)
    for block in range(3):
        feed_grads(r, block)
        advance(0, [(block, 0)])
    advance(0, [(0, 1)])

    back_plan, pair_plan = plan_of(FFN_BACK), plan_of(FFN_PAIRS, QKV_PAIRS)

    def back_one(s, _):
        attend_back(r, s)
        at_time(s, back_plan)
        return 0

    lax.fori_loop(0, slots, back_one, 0)
    for block in range(3):
        qkv_grads(r, block)
        advance(1, [(block, 0)])
    for which in range(2):
        advance(which, AFTER_GRADS[which])
    each_chunk(r, tokens, finish_input)
    stage.store("in_rows")
    for which in range(2):
        advance(which, AFTER_HALF[which] + AFTER_INPUT[which])
    for ref in (r.sums, r.acc_mixed, r.spart):
        ref[...] = jnp.zeros_like(ref)

    def pairs_back(slot, _):
        wait_moves(r, slot, True)
        pair_backward(r, slot, lambda: at_time(2 * slot, pair_plan))
        pl.when(slot + 2 < slots)(lambda: start_moves(r, slot + 2, True))
        at_time(2 * slot + 1, pair_plan)
        return 0

    lax.fori_loop(0, slots, pairs_back, 0)
    pack_small(r, slots)
    if remote:
        small.act(0)
        advance(1, [(2, 5), (0, 7)])
        small.act(1)
        advance(1, [(1, 7)])
        advance(1, [(2, 6)])
        small.act(2)
        advance(1, [(2, 7)])
        small.act(3)
        rows = pltpu.make_async_copy(r.stotal, r.stotal_far, r.leave_sems.at[6])
        rows.start()
        for which in range(2):
            advance(which, [(b, 8) for b in range(3)])
        small.act(4)
        gather.finish()
        for which in range(2):
            for block in range(3):
                leave(which, block).wait()
        rows.wait()
    else:
        stage.store("fpart", "qpart", "spart")
    stage.stored()


def call_stage(kernel, name, remote, collective, arrays, scalars, far, outs, carried, scratch):
    vm, sem = pltpu.VMEM, pltpu.SemaphoreType.DMA
    near = {n: vm(a.shape, a.dtype) for n, a in arrays.items() if n not in scalars + far}
    in_names = [n if n in scalars or n.endswith("_far") else "given_" + n for n in arrays]
    results = outs | {n + "_far": item for n, item in carried.items()}
    scratch = near | {n: vm(*item) for n, item in carried.items()} | scratch
    scratch |= {"input_sems": sem((len(near),)), "carry_sems": sem((len(carried),))}
    names = in_names + list(results) + list(scratch)
    values = pl.pallas_call(
        functools.partial(kernel, remote, names, list(near), list(carried)),
        in_specs=[pl.BlockSpec(memory_space=pltpu.SMEM if n in scalars else pl.ANY) for n in arrays],
        out_specs=[pl.BlockSpec(memory_space=pl.ANY)] * len(results),
        out_shape=[jax.ShapeDtypeStruct(*item) for item in results.values()],
        scratch_shapes=list(scratch.values()),
        compiler_params=pltpu.CompilerParams(
            vmem_limit_bytes=VMEM_BYTES, **(dict(collective_id=collective, has_side_effects=True) if remote else {})
        ),
        name=name,
    )(*arrays.values())
    return dict(zip(results, values))


def layer(remote, arrays):
    tokens = arrays["hidden"].shape[0]
    slots = tokens // SLOT
    v, sem = pltpu.VMEM, pltpu.SemaphoreType.DMA
    of_tokens = (tokens, D)
    table = (slots, HALF, 128)
    fshape, qshape, sshape = (3 * D, HALF_D), (D, 3 * HALF_D), (SMALL_ROWS, 128)
    outs = {"left_far": ((slots, 2 * K, PAIRS), bf16), "slope_far": ((slots, K, PAIRS), bf16)}
    carried = {"out_rows": (of_tokens, bf16), "in_rows": (of_tokens, bf16)}
    scratch = {
        "wqkv": v((2, 3, D, HALF_D), bf16), "wup": v((2, D, HALF_D), bf16), "wproj": v((2, HALF_D, D), bf16),
        "wdown": v((2, HALF_D, D), bf16), "load_sems": sem((4,)), "pair_sems": sem((2, 2)),
        "left": v((2, 2 * K + HOT, PAIRS), bf16), "slope": v((2, K, PAIRS), bf16),
        "right": v((K + 2 * H, PAIRS), bf16), "cols": v((5, K, 128), f32), "w1": v((2 * K, 2 * K), bf16), "w1t": v((2 * K, 2 * K), bf16),
        "w2": v((K, 128), f32), "w2_twice": v((2 * K, 2 * H), bf16), "base": v((H, 256), f32), "lhs": v((H, 256), bf16),
        "argument": v(table, f32), "distance": v(table, f32), "hop_rows": v(table, f32), "edge_rows": v(table, f32),
        "atom_rows": v((slots, 8, 128), f32), "dargs": v(table, f32), "bias": v((slots, H * HALF, 128), f32),
        "work": v((3, SLOT, D), f32), "normed_a": v(of_tokens, bf16), "joined": v((tokens, 3 * D), bf16),
        "prob": v((slots, SLOT, H * SLOT), bf16), "attended": v(of_tokens, bf16), "normed_f": v(of_tokens, bf16),
        "activated": v(of_tokens, bf16), "d_pre": v(of_tokens, bf16), "d_branch": v(of_tokens, bf16),
        "d_attended": v(of_tokens, bf16), "d_resid": v(of_tokens, f32), "vectors": v((8, D), f32),
        "sums": v((2, K, 128), f32), "acc_mixed": v((2 * K + HOT, K + 2 * H), f32),
    }
    parts = {"fpart": ((2,) + fshape, bf16), "qpart": ((2,) + qshape, bf16), "spart": (sshape, f32)}
    totals = {"ftotal": (fshape, bf16), "qtotal": (qshape, bf16), "stotal": (sshape, f32)}
    if remote:
        outs |= {n + "_far": item for n, item in totals.items()}
        scratch |= {n: v(*item) for n, item in (parts | totals).items()}
        scratch |= {"leave_sems": sem((7,)), "gather_sends": sem((6, 4)), "gather_recvs": sem((6, 4))}
        for name, shape in (("f", (D, HALF_D)), ("q", (D // 3, 3 * HALF_D))):
            keys = ("_core", "_tp", "_x", "_z", "_sends", "_recvs")
            scratch |= {name + key: item for key, item in zip(keys, big_scratch(*shape))}
        scratch |= dict(zip(("s_near", "s_z", "s_sends", "s_recvs"), small_scratch()))
    else:
        carried |= parts
    results = call_stage(
        layer_kernel, "layer", remote, 0, arrays, ("lengths", "flags"), ("qkv", "up", "proj", "down"), outs, carried,
        scratch,
    )
    sums = [results[n + "_far"] for n in (totals if remote else parts)]
    return results["out_rows_far"], results["in_rows_far"], sums


RESULTS = (
    "output", "grad_input", "attn_gain", "attn_shift", "qkv", "proj", "ffn_gain", "ffn_shift", "up", "up_bias", "down",
    "down_bias", "scale", "shift", "centers", "spreads", "first", "first_bias", "second", "hop", "edge",
)


def unpack_kernel(*refs):
    given = SimpleNamespace(**dict(zip(("out_rows", "in_rows", "fsum", "qsum", "rows"), refs)))
    far = SimpleNamespace(**dict(zip(RESULTS, refs[5:])))
    count = len(RESULTS)
    near = SimpleNamespace(**dict(zip(RESULTS, refs[5 + count : 5 + 2 * count])))
    fsum, qsum, rows, load_sems, store_sems = refs[5 + 2 * count :]
    moves = [(given.rows, rows)]
    sources = ((given.qsum, qsum, 3), (given.fsum, fsum, 9), (given.out_rows, near.output, 1), (given.in_rows, near.grad_input, 1))
    for src, dst, pieces in sources:
        height = src.shape[0] // pieces
        for i in range(pieces):
            at = slice(i * height, (i + 1) * height)
            moves.append((src.at[at], dst.at[at]))
    loads = [pltpu.make_async_copy(src, dst, load_sems.at[i]) for i, (src, dst) in enumerate(moves)]
    for load in loads:
        load.start()
    stores = []

    def store(src, dst):
        stores.append(pltpu.make_async_copy(src, dst, store_sems.at[len(stores)]))
        stores[-1].start()

    for i in range(3):
        loads[1 + i].wait()
        at = slice(256 * i, 256 * (i + 1))
        for m in range(3):
            near.qkv[m, at] = qsum[at, m * HALF_D : (m + 1) * HALF_D].astype(f32)
        store(near.qkv.at[:, at], far.qkv.at[:, at])
    for i in range(3):
        loads[4 + i].wait()
        at = slice(256 * i, 256 * (i + 1))
        near.up[at, :] = fsum[at, :].astype(f32)
        store(near.up.at[at], far.up.at[at])
    for block, name in ((1, "proj"), (2, "down")):
        for i in range(3):
            loads[4 + 3 * block + i].wait()
        ref = getattr(near, name)
        at = D * block
        ref[:, :HALF_D] = fsum[at : at + HALF_D, :].astype(f32)
        ref[:, HALF_D:] = fsum[at + HALF_D : at + D, :].astype(f32)
        store(ref, getattr(far, name))
    loads[13].wait()
    store(near.output, far.output)
    loads[14].wait()
    store(near.grad_input, far.grad_input)
    loads[0].wait()
    names = ("attn_gain", "attn_shift", "ffn_gain", "ffn_shift", "up_bias", "down_bias")
    for v, name in enumerate(names):
        for i in range(D // 128):
            getattr(near, name)[pl.ds(128 * i, 128)] = rows[VECTOR_ROWS + v * (D // 128) + i, :]
    near.first[...] = rows[0:K, :]
    near.second[...] = rows[SECOND_ROWS : SECOND_ROWS + H, :]
    table = rows[TABLE_ROWS : TABLE_ROWS + H, :]
    near.scale[...] = table[:ATOMS, HOT : HOT + ATOMS]
    near.shift[...] = table[ATOMS:, HOT : HOT + ATOMS]
    turned = square_turn(table)
    near.hop[...] = turned[:HOPS, :H]
    near.edge[...] = turned[HOPS : HOPS + EDGES, :H]
    lines = ("first_bias", "centers", "spreads")
    for i, name in enumerate(lines):
        getattr(near, name)[...] = rows[KERNEL_ROWS + i, :]
    for name in names + ("first", "second", "scale", "shift", "hop", "edge") + lines:
        store(getattr(near, name), getattr(far, name))
    for copy in stores:
        copy.wait()


def unpack(out_rows, in_rows, fsum, qsum, rows):
    tokens = out_rows.shape[0]
    vec, line, types = ((D,), f32), ((K,), f32), ((ATOMS, ATOMS), f32)
    shapes = (
        ((tokens, D), bf16), ((tokens, D), bf16), vec, vec, ((3, D, HALF_D), f32), ((HALF_D, D), f32), vec, vec,
        ((D, HALF_D), f32), vec, ((HALF_D, D), f32), vec, types, types, line, line, ((K, K), f32), line, ((H, K), f32),
        ((HOPS, H), f32), ((EDGES, H), f32),
    )
    anywhere = pl.BlockSpec(memory_space=pl.ANY)
    return pl.pallas_call(
        unpack_kernel,
        in_specs=[anywhere] * 5,
        out_specs=[anywhere] * len(shapes),
        out_shape=[jax.ShapeDtypeStruct(*item) for item in shapes],
        scratch_shapes=[pltpu.VMEM(*item) for item in shapes] + [
            pltpu.VMEM(fsum.shape, bf16), pltpu.VMEM(qsum.shape, bf16), pltpu.VMEM(rows.shape, f32),
            pltpu.SemaphoreType.DMA((15,)), pltpu.SemaphoreType.DMA((25,)),
        ],
        compiler_params=pltpu.CompilerParams(vmem_limit_bytes=VMEM_BYTES),
        name="unpack",
    )(out_rows, in_rows, fsum, qsum, rows)


def whole_weights(qkv_weight, up_weight, proj_weight, down_weight):
    columns = lambda w: jnp.stack(jnp.split(w, 2, axis=-1))
    rows = lambda w: jnp.stack(jnp.split(w, 2, axis=0))
    gather = lambda w, dim: lax.all_gather(w, "tp", axis=dim, tiled=True)
    return (
        columns(gather(qkv_weight.transpose(1, 0, 2), 2)), columns(gather(up_weight, 1)),
        rows(gather(proj_weight, 0)), rows(gather(down_weight, 0)),
    )


def sum_grads(fgrads, qgrads, small):
    total_f, total_q, rows = lax.psum((fgrads, qgrads, small), ("mol", "tp"))
    share = D // lax.axis_size("tp")
    at = lax.axis_index("tp") * share

    def columns(halves):
        return lax.dynamic_slice_in_dim(jnp.concatenate(list(halves), axis=-1), at, share, halves.ndim - 2)

    def rows_of(block):
        part = total_f[:, D * block : D * (block + 1)]
        sides = jnp.concatenate([part[:, :HALF_D], part[:, HALF_D:]], axis=2).reshape(D, D)
        return lax.dynamic_slice_in_dim(sides, at, share, 0)

    qkv = columns(total_q.reshape(2, D, 3, HALF_D)).transpose(1, 0, 2)
    return [v.astype(f32) for v in (qkv, columns(total_f[:, :D]), rows_of(1), rows_of(2))], rows


def body(
    mesh_shape,
    hidden_in, positions, atom_types, hop_counts, edge_types, lengths, branches,
    attn_gain, attn_shift, qkv_weight, proj_weight, ffn_gain, ffn_shift, up_weight, up_bias, down_weight, down_bias,
    kernel_scale, kernel_shift, centers, spreads, first_weight, first_bias, second_weight, hop_table, edge_table,
    cotangent,
):
    remote = mesh_shape["tp"] == 2 and mesh_shape["mol"] == 16 and branches.shape[0] == 8
    if remote:
        weights = (qkv_weight.transpose(1, 0, 2), up_weight, proj_weight, down_weight)
    else:
        weights = whole_weights(qkv_weight, up_weight, proj_weight, down_weight)
    arrays = dict(
        lengths=lengths, flags=branches.T, positions=positions, atoms=atom_types, hops=hop_counts.T,
        edges=edge_types.T, kernel_scale=kernel_scale, kernel_shift=kernel_shift, centers=centers, spreads=spreads,
        first_weight=first_weight, first_bias=first_bias, second_weight=second_weight.T, hop_table=hop_table,
        edge_table=edge_table, attn_gain=attn_gain, attn_shift=attn_shift, ffn_gain=ffn_gain, ffn_shift=ffn_shift,
        up_bias=up_bias, down_bias=down_bias, hidden=hidden_in, cotangent=cotangent,
        qkv=weights[0], up=weights[1], proj=weights[2], down=weights[3],
    )
    output, grad_input, sums = layer(remote, arrays)
    if remote:
        fsum, qsum, rows = sums
    else:
        big, rows = sum_grads(*sums)
        fsum, qsum = jnp.zeros((3 * D, HALF_D), bf16), jnp.zeros((D, 3 * HALF_D), bf16)
    output, grad_input, *grads = unpack(output, grad_input, fsum, qsum, rows)
    if not remote:
        grads[2], grads[6], grads[3], grads[8] = big
    grads[2] = grads[2].transpose(1, 0, 2)
    grads[16] = grads[16].T
    return (output, grad_input, *grads)


def solution(mesh):
    rows = P(("mol", "tp"), None)
    all_of = P()
    in_specs = (
        rows, P(None, ("mol", "tp")), P(("mol", "tp")), rows, rows, P("mol"), rows, all_of, all_of,
        P(None, None, "tp"), P("tp", None), all_of, all_of, P(None, "tp"), all_of, P("tp", None),
    ) + (all_of,) * 10 + (rows,)
    out_specs = (
        rows, rows, all_of, all_of, P(None, None, "tp"), P("tp", None), all_of, all_of, P(None, "tp"), all_of,
        P("tp", None),
    ) + (all_of,) * 10
    step = functools.partial(body, dict(mesh.shape))
    return jax.shard_map(step, mesh=mesh, in_specs=in_specs, out_specs=out_specs, check_vma=False)
```

```python
import functools
from types import SimpleNamespace

import jax
import jax.numpy as jnp
from jax import lax
from jax.experimental import pallas as pl
from jax.experimental.pallas import tpu as pltpu
from jax.sharding import PartitionSpec as P

D = 768
H = 32
HD = 24
FF = 768
K = 128
SLOT = 64
HALF = SLOT // 2
HALF_D = D // 2
PAIRS = SLOT * SLOT
HOPS = 16
EDGES = 8
ATOMS = 16
GROUP = 4
GROUPS = H // GROUP
HOT = 32

highest = lax.Precision.HIGHEST
neg_large = -1e30
root_tau = 2.5066282746310002
root_half = 0.7071067811865476
inv_root_tau = 0.3989422804014327
head_scale = HD ** (-0.5)
VMEM_BYTES = 62 * 1024 * 1024
TILE = 512

SECOND_ROWS = K
TABLE_ROWS = SECOND_ROWS + H
KERNEL_ROWS = TABLE_ROWS + H
VECTOR_ROWS = KERNEL_ROWS + 8
SMALL_ROWS = 256

MESH = pl.DeviceIdType.MESH
f32 = jnp.float32
bf16 = jnp.bfloat16


def dot_nn(left, right, precision=None):
    return lax.dot_general(left, right, (((1,), (0,)), ((), ())), precision=precision, preferred_element_type=f32)


def dot_nt(left, right, precision=None):
    return lax.dot_general(left, right, (((1,), (1,)), ((), ())), precision=precision, preferred_element_type=f32)


def dot_tn(left, right, precision=None):
    return lax.dot_general(left, right, (((0,), (0,)), ((), ())), precision=precision, preferred_element_type=f32)


def iota(shape, dim):
    return lax.broadcasted_iota(jnp.int32, shape, dim)


def gelu_parts(values):
    size = jnp.abs(values)
    bell = jnp.exp(values * values * -0.5)
    denominator = 1.0 + (0.3275911 * root_half) * size
    t = pl.reciprocal(denominator, approx=True)
    series = 0.5 * 1.061405429
    for factor in (-1.453152027, 1.421413741, -0.284496736, 0.254829592):
        series = series * t + 0.5 * factor
    tail = series * t * bell
    gelu = jnp.maximum(values, 0.0) - size * tail
    outer = tail - size * (bell * inv_root_tau)
    return gelu, jnp.where(values >= 0.0, 1.0 - outer, outer)


def gelu_pair(values):
    size = jnp.abs(values)
    bell = jnp.exp(values * values * -0.5)
    t = pl.reciprocal(1.0 + (0.3275911 * root_half) * size, approx=True)
    series = 0.5 * 1.061405429
    for factor in (-1.453152027, 1.421413741, -0.284496736, 0.254829592):
        series = series * t + 0.5 * factor
    tail = (series * t * bell).astype(bf16)
    density = (bell * inv_root_tau).astype(bf16)
    values = values.astype(bf16)
    size = jnp.abs(values)
    outer = tail - size * density
    one, zero = jnp.ones((), bf16), jnp.zeros((), bf16)
    return jnp.maximum(values, zero) - size * tail, jnp.where(values >= zero, one - outer, outer)


def to_column(row):
    size = row.shape[1]
    same = iota((size, size), 0) == iota((size, size), 1)
    return jnp.sum(jnp.where(same, row, 0.0), axis=1, keepdims=True)


def half_swap(values):
    return pltpu.roll(values, 64, 1)


def low_lanes(rows):
    return iota((rows, 128), 1) < 64


def vmem(count):
    return [pl.BlockSpec(memory_space=pltpu.VMEM)] * count


def row_of(ref):
    return ref[...].reshape(1, ref.shape[0])


def place():
    mol = lax.axis_index("mol")
    return mol % 2, (mol // 2) % 2, mol // 4, lax.axis_index("tp")


def greet(peers):
    for peer in peers:
        pl.semaphore_signal(pltpu.get_barrier_semaphore(), inc=1, device_id=peer, device_id_type=MESH)


def await_greetings(peers):
    pl.semaphore_wait(pltpu.get_barrier_semaphore(), len(peers))


def window(group):
    first = GROUP * HD * group
    start = first // 128 * 128
    width = 128 if first - start + GROUP * HD <= 128 else 256
    return start, width, first - start


def head_masks(group, kind):
    _, width, offset = window(group)
    lane = iota((1, width), 1)
    return [
        ((lane >= offset + HD * h) & (lane < offset + HD * (h + 1))).astype(f32).astype(kind) for h in range(GROUP)
    ]


def spread_heads(values, group):
    return jnp.concatenate([values * mask for mask in head_masks(group, bf16)], axis=0)


def gather_heads(values, group):
    masks = head_masks(group, f32)
    total = values[:SLOT] * masks[0]
    for h in range(1, GROUP):
        total = total + values[SLOT * h : SLOT * (h + 1)] * masks[h]
    return total


def standardize(values):
    centred = values - jnp.mean(values, axis=-1, keepdims=True)
    inv_std = lax.rsqrt(jnp.mean(centred * centred, axis=-1, keepdims=True) + 1e-05)
    return centred * inv_std, inv_std


def norm_back(d_normed, scaled, inv_std, gain):
    weighted = d_normed * gain
    inner_a = jnp.mean(weighted, axis=-1, keepdims=True)
    inner_b = jnp.mean(weighted * scaled, axis=-1, keepdims=True)
    return inv_std * (weighted - inner_a - scaled * inner_b)


def column_sum(values):
    return jnp.sum(values, axis=0, keepdims=True)


class Peers:
    def __init__(self):
        self.core, self.x, self.z, self.tp = place()
        mol = lax.axis_index("mol")
        self.over_core = {"mol": mol + 1 - 2 * self.core}
        self.over_x = {"mol": mol + 2 - 4 * self.x}
        self.over_tp = {"tp": 1 - self.tp}
        self.turn = [lax.rem(self.z + d, 4) for d in range(4)]
        self.over_z = [{"mol": self.turn[d] * 4 + self.x * 2 + self.core} for d in range(4)]

    def neighbour(self, k):
        core = self.core + (1 - 2 * self.core) * (k & 1)
        x = self.x + (1 - 2 * self.x) * (k >> 1 & 1)
        tp = self.tp + (1 - 2 * self.tp) * (k >> 2)
        return core * 4 + tp * 2 + x, {"mol": self.z * 4 + x * 2 + core, "tp": tp}

    def everyone(self):
        return [self.neighbour(k)[1] for k in range(1, 8)] + self.over_z[1:]


def span(start, size):
    return pl.ds(pl.multiple_of(start, size), size)


def add_rows(target, source, rows):
    step = 96 if rows % 96 == 0 else min(rows, 32)

    def piece(i, _):
        at = pl.ds(pl.multiple_of(i * step, step), step)
        target[at, :] = target[at, :] + source[at, :]
        return 0

    lax.fori_loop(0, rows // step, piece, 0)


class Reduction:
    kinds = 11

    def __init__(self, peers, part, total, from_core, from_tp, from_x, from_z, sends, recvs):
        self.peers, self.part, self.total = peers, part, total
        self.from_core, self.from_tp, self.from_x, self.from_z = from_core, from_tp, from_x, from_z
        self.sends, self.recvs = sends, recvs
        self.half = from_core.shape[2]
        self.quarter, self.least = self.half // 2, self.half // 8

    def rows(self, b, level):
        p = self.peers
        at = b * 2 * self.half + p.core * self.half
        if level > 0:
            at = at + p.x * self.quarter
        return at + p.z * self.least if level > 1 else at

    def copy(self, b, kind):
        p = self.peers
        part, total = self.part, self.total
        half, quarter, least = self.half, self.quarter, self.least
        if kind == 0:
            src = part.at[:, span(b * 2 * half + (1 - p.core) * half, half)]
            dst, peer = self.from_core.at[b], p.over_core
        elif kind == 1:
            src, dst, peer = part.at[1 - p.tp, span(self.rows(b, 0), half)], self.from_tp.at[b], p.over_tp
        elif kind == 2:
            src = part.at[p.tp, span(self.rows(b, 0) + (1 - p.x) * quarter, quarter)]
            dst, peer = self.from_x.at[b], p.over_x
        elif kind < 6:
            d = kind - 2
            src = part.at[p.tp, span(self.rows(b, 1) + p.turn[d] * least, least)]
            dst, peer = self.from_z.at[b, d - 1], p.over_z[d]
        elif kind < 9:
            src = dst = total.at[span(self.rows(b, 2), least)]
            peer = p.over_z[kind - 5]
        elif kind == 9:
            src = dst = total.at[span(self.rows(b, 1), quarter)]
            peer = p.over_x
        else:
            src = dst = total.at[span(self.rows(b, 0), half)]
            peer = p.over_core
        return pltpu.make_async_remote_copy(
            src_ref=src, dst_ref=dst, send_sem=self.sends.at[b, kind], recv_sem=self.recvs.at[b, kind],
            device_id=peer, device_id_type=MESH,
        )

    def act(self, b, stage):
        p = self.peers
        half, quarter, least = self.half, self.quarter, self.least
        part = self.part
        if stage == 0:
            self.copy(b, 0).start()
        elif stage == 1:
            self.copy(b, 0).wait_recv()
            at = span(self.rows(b, 0), half)
            add_rows(part.at[1 - p.tp, at], self.from_core.at[b, 1 - p.tp], half)
            self.copy(b, 1).start()
            add_rows(part.at[p.tp, at], self.from_core.at[b, p.tp], half)
        elif stage == 2:
            self.copy(b, 1).wait_recv()
            away, mine = (1 - p.x) * quarter, p.x * quarter
            at = self.rows(b, 0)
            add_rows(part.at[p.tp, span(at + away, quarter)], self.from_tp.at[b, span(away, quarter)], quarter)
            self.copy(b, 2).start()
            add_rows(part.at[p.tp, span(at + mine, quarter)], self.from_tp.at[b, span(mine, quarter)], quarter)
        elif stage == 3:
            self.copy(b, 2).wait_recv()
            add_rows(part.at[p.tp, span(self.rows(b, 1), quarter)], self.from_x.at[b], quarter)
            for kind in (3, 4, 5):
                self.copy(b, kind).start()
        elif stage == 4:
            for kind in (3, 4, 5):
                self.copy(b, kind).wait_recv()
            mine = span(self.rows(b, 2), least)
            value = part[p.tp, mine, :].astype(f32)
            for d in range(3):
                value = value + self.from_z[b, d].astype(f32)
            self.total[mine, :] = value.astype(bf16)
            for kind in (6, 7, 8):
                self.copy(b, kind).start()
        elif stage == 5:
            for kind in (6, 7, 8):
                self.copy(b, kind).wait_recv()
            self.copy(b, 9).start()
        elif stage == 6:
            self.copy(b, 9).wait_recv()
            self.copy(b, 10).start()
        elif stage == 7:
            self.copy(b, 10).wait_recv()
        else:
            for kind in range(self.kinds):
                self.copy(b, kind).wait_send()


class SmallReduction:
    def __init__(self, peers, part, total, from_near, from_z, sends, recvs):
        self.peers, self.part, self.total, self.from_near, self.from_z = peers, part, total, from_near, from_z
        self.sends, self.recvs = sends, recvs
        p = peers
        self.near = [p.neighbour(k) for k in range(8)]
        self.mine = span(self.near[0][0] * 32, 32)

    def copy(self, kind):
        p = self.peers
        if kind < 7:
            index, peer = self.near[kind + 1]
            src, dst = self.part.at[span(index * 32, 32)], self.from_near.at[kind]
        elif kind < 10:
            src = dst = self.from_z.at[p.z]
            peer = p.over_z[kind - 6]
        else:
            src = dst = self.total.at[self.mine]
            peer = self.near[kind - 9][1]
        return pltpu.make_async_remote_copy(
            src_ref=src, dst_ref=dst, send_sem=self.sends.at[kind], recv_sem=self.recvs.at[kind],
            device_id=peer, device_id_type=MESH,
        )

    def act(self, stage):
        hops = (range(0, 7), range(7, 10), range(10, 17))
        if stage == 4:
            for kind in range(17):
                self.copy(kind).wait_send()
            return
        if stage > 0:
            for kind in hops[stage - 1]:
                self.copy(kind).wait_recv()
        if stage == 1:
            value = self.part[self.mine, :]
            for k in range(7):
                value = value + self.from_near[k]
            self.from_z[self.peers.z] = value
        elif stage == 2:
            self.total[self.mine, :] = (self.from_z[0] + self.from_z[1]) + (self.from_z[2] + self.from_z[3])
        if stage < 3:
            for kind in hops[stage]:
                self.copy(kind).start()


def big_scratch(rows, lanes):
    half = rows // 2
    sems = pltpu.SemaphoreType.DMA((3, Reduction.kinds))
    return [
        pltpu.VMEM((3, 2, half, lanes), bf16), pltpu.VMEM((3, half, lanes), bf16),
        pltpu.VMEM((3, half // 2, lanes), bf16), pltpu.VMEM((3, 3, half // 8, lanes), bf16), sems, sems,
    ]


def small_scratch():
    return [
        pltpu.VMEM((7, 32, 128), f32), pltpu.VMEM((4, 32, 128), f32),
        pltpu.SemaphoreType.DMA((17,)), pltpu.SemaphoreType.DMA((17,)),
    ]


class Gather:
    pieces = 6

    def __init__(self, peers, whole, sends, recvs):
        self.peers, self.whole, self.sends, self.recvs = peers, whole, sends, recvs
        self.quarter = peers.x * 2 + peers.core
        self.next_quarter = (1 - peers.x) * 2 + peers.core

    def rows(self, ref, quarter):
        count = ref.shape[0] // 4
        return ref.at[span(quarter * count, count), :]

    def copy(self, index, kind):
        p = self.peers
        if kind == 0:
            src = dst = self.rows(self.whole(index, p.tp), self.quarter)
            peer = p.over_tp
        elif kind == 1:
            src = dst = self.rows(self.whole(index, 1 - p.tp), self.quarter)
            peer = p.over_x
        else:
            src = dst = self.rows(self.whole(index, 1 - p.tp), self.quarter if kind == 2 else self.next_quarter)
            peer = p.over_core
        return pltpu.make_async_remote_copy(
            src_ref=src, dst_ref=dst, send_sem=self.sends.at[index, kind], recv_sem=self.recvs.at[index, kind],
            device_id=peer, device_id_type=MESH,
        )

    def start(self, indices):
        for index in indices:
            self.copy(index, 0).start()

    def onward_x(self, index):
        self.copy(index, 0).wait_recv()
        self.copy(index, 1).start()
        self.copy(index, 2).start()

    def onward_core(self, index):
        self.copy(index, 1).wait_recv()
        self.copy(index, 3).start()

    def arrive(self, index):
        self.copy(index, 2).wait_recv()
        self.copy(index, 3).wait_recv()

    def finish(self):
        for index in range(self.pieces):
            for kind in range(4):
                self.copy(index, kind).wait_send()


def square_turn(values):
    rows, lanes = values.shape
    if lanes < 128:
        values = jnp.concatenate([values, jnp.zeros((rows, 128 - lanes), f32)], axis=1)
    if rows < 128:
        values = jnp.concatenate([values, jnp.zeros((128 - rows, 128), f32)], axis=0)
    return values.T


def widen(values):
    return jnp.concatenate([values] * (TILE // 128), axis=1)


def strips():
    return [slice(16 * i, 16 * (i + 1)) for i in range(K // 16)]


def four_rows(ref, slot, first):
    return jnp.concatenate([ref[slot, pl.ds(first + i, 1), :] for i in range(TILE // 128)], axis=1)


def hot_rows(values, count):
    return (values == iota((count, TILE), 0).astype(f32)).astype(f32)


def fold_lanes(values):
    total = values[:, :128]
    for i in range(1, TILE // 128):
        total = total + values[:, 128 * i : 128 * (i + 1)]
    return total


def twice(ref, values):
    none = jnp.zeros_like(values)
    ref[...] = jnp.concatenate(
        [jnp.concatenate([values, none], axis=1), jnp.concatenate([none, values], axis=1)], axis=0
    ).astype(bf16)


def dot_halves(weights, pieces):
    values = jnp.concatenate(pieces, axis=0)
    half = TILE // 2
    both = dot_nn(weights, jnp.concatenate([values[:, :half], values[:, half:]], axis=0))
    rows = both.shape[0] // 2
    return jnp.concatenate([both[:rows], both[rows:]], axis=1)


def prepare_pairs(r):
    spr = to_column(row_of(r.spreads))
    r.cols[0] = jnp.broadcast_to(to_column(row_of(r.centers)), (K, 128))
    r.cols[1] = jnp.broadcast_to(root_half / spr, (K, 128))
    r.cols[2] = jnp.broadcast_to(-jnp.log(root_tau * spr), (K, 128))
    r.cols[3] = jnp.broadcast_to(to_column(row_of(r.first_bias)), (K, 128))
    r.cols[4] = jnp.broadcast_to(1.0 / spr, (K, 128))
    twice(r.w1, r.first_weight[...].astype(f32))
    twice(r.w1t, r.first_weight[...].astype(f32).T)
    r.w2[...] = square_turn(r.second_weight[...].astype(f32))
    table = jnp.concatenate([r.hop_table[...], r.edge_table[...], jnp.zeros((128 - HOPS - EDGES, H), f32)], axis=0)
    table = jnp.concatenate([table, jnp.zeros((128, 128 - H), f32)], axis=1).T[:H, :HOT]
    one = table.astype(bf16).astype(f32)
    r.base[...] = jnp.concatenate(
        [r.second_weight[...].astype(f32), one, table - one, jnp.zeros((H, 64), f32)], axis=1
    )


def bf16_parts(values, count):
    parts = []
    for _ in range(count):
        parts.append(values.astype(bf16))
        values = values - parts[-1].astype(f32)
    return parts


def pair_tables(r, slots):
    low = low_lanes(HALF)
    low_row = low_lanes(1)
    tables = [part.astype(f32) for ref in (r.kernel_scale, r.kernel_shift) for part in bf16_parts(ref[...], 3)]
    tables = jnp.concatenate([square_turn(part)[:ATOMS, :ATOMS] for part in tables], axis=1)
    tables = jnp.concatenate([tables, jnp.zeros((ATOMS, 128 - 6 * ATOMS), f32)], axis=1).astype(bf16)
    for group in range(slots // 2):
        lanes = slice(128 * group, 128 * (group + 1))
        atoms = r.atoms[lanes].astype(f32).reshape(1, 128)
        rows = jnp.concatenate([r.positions[:, lanes], atoms, jnp.zeros((4, 128), f32)], axis=0)
        columns = square_turn(rows)
        key_hot = (columns[:, 3:4] == iota((128, ATOMS), 1).astype(f32)).astype(f32).astype(bf16)
        picks = dot_nn(key_hot, tables).astype(bf16)
        turned = half_swap(rows)
        for s in range(2):
            slot = 2 * group + s
            tokens = slice(SLOT * s, SLOT * (s + 1))
            double = jnp.where(low_lanes(8), *((rows, turned) if s == 0 else (turned, rows)))
            total = None
            for c in range(3):
                column = columns[tokens, c : c + 1]
                offset = jnp.where(low, column[:HALF], column[HALF:]) - double[c : c + 1]
                total = offset * offset if total is None else total + offset * offset
            distance = jnp.sqrt(total)
            query_hot = (double[3:4] == iota((ATOMS, 128), 0).astype(f32)).astype(f32)
            three, none = [query_hot] * 3, [jnp.zeros((3 * ATOMS, 128), f32)]
            rest = [jnp.zeros((128 - 6 * ATOMS, 128), f32)]
            spread = jnp.concatenate(
                [jnp.concatenate(three + none + rest, axis=0), jnp.concatenate(none + three + rest, axis=0)], axis=1
            )
            both = dot_nn(picks[tokens], spread.astype(bf16))
            scale = jnp.where(low, both[:HALF, :128], both[HALF:, :128])
            shift = jnp.where(low, both[:HALF, 128:], both[HALF:, 128:])
            r.argument[slot] = scale * distance + shift
            r.distance[slot] = distance
            for source, target in ((r.hops, r.hop_rows), (r.edges, r.edge_rows)):
                values = source[:, lanes].astype(f32)
                top, bottom = values[:HALF], values[HALF:]
                if s == 0:
                    target[slot] = jnp.where(low, top, half_swap(bottom))
                else:
                    target[slot] = jnp.where(low, half_swap(top), bottom)
            r.atom_rows[slot] = jnp.broadcast_to(double[3:4], (8, 128))


def table_grads(r, slots):
    lefts, rights = [], []
    for slot in range(slots):
        query_hot = (r.atom_rows[slot, 0:1, :] == iota((ATOMS, 128), 0).astype(f32)).astype(f32)
        keys = jnp.concatenate([query_hot[:, :HALF], query_hot[:, HALF:SLOT]], axis=0)
        keys = jnp.concatenate([keys, keys], axis=1).astype(bf16)
        values = jnp.concatenate([r.dargs[slot] * r.distance[slot], r.dargs[slot]], axis=1)
        both = dot_nn(keys, jnp.concatenate(bf16_parts(values, 2), axis=0))
        low = low_lanes(ATOMS)
        for index in range(2):
            lanes = slice(128 * index, 128 * (index + 1))
            rights.append(bf16_parts(jnp.where(low, both[:ATOMS, lanes], both[ATOMS:, lanes]), 2))
        lefts.append(query_hot.astype(bf16))
    left = jnp.concatenate(lefts, axis=1)
    right = jnp.concatenate(
        [jnp.concatenate([rights[2 * s + index][part] for s in range(slots)], axis=1) for index in range(2) for part in range(2)],
        axis=0,
    )
    result = dot_nt(left, right)
    return [
        result[:, 2 * ATOMS * index : 2 * ATOMS * index + ATOMS] + result[:, 2 * ATOMS * index + ATOMS : 2 * ATOMS * (index + 1)]
        for index in range(2)
    ]


def hold(tile, value):
    return value


def in_stages(stages, count, beside=lambda time: None):
    held = {}
    for time in range(count + len(stages) - 1):
        for k, stage in reversed(list(enumerate(stages))):
            if 0 <= time - k < count:
                held[time - k] = stage(time - k, held.get(time - k))
        beside(time)


TILES = PAIRS // TILE
ROWS = TILE // 128


def pair_forward(r, slot, beside=lambda time: None):
    bank = lax.rem(slot, 2)
    graph_on = r.flags[0, slot].astype(f32)
    space_on = r.flags[1, slot].astype(f32)
    factor = jnp.where(iota((H, 256), 1) < K, space_on, graph_on)
    r.lhs[...] = (r.base[...] * factor).astype(bf16)

    def kernels(tile, _):
        where = slice(tile * TILE, (tile + 1) * TILE)
        arg = four_rows(r.argument, slot, tile * ROWS)
        pieces = []
        for rows in strips():
            u = (arg - widen(r.cols[0, rows])) * widen(r.cols[1, rows])
            pieces.append(jnp.exp(widen(r.cols[2, rows]) - u * u).astype(bf16))
            r.left[bank, rows, where] = pieces[-1]
        return dot_halves(r.w1t[...], pieces)

    def hidden(tile, first):
        where = slice(tile * TILE, (tile + 1) * TILE)
        pieces = []
        for rows in strips():
            value, slope = gelu_pair(first[rows] + widen(r.cols[3, rows]))
            pieces.append(value)
            r.left[bank, slice(K + rows.start, K + rows.stop), where] = pieces[-1]
            r.slope[bank, rows, where] = slope
        hot = jnp.concatenate(
            [
                hot_rows(four_rows(r.hop_rows, slot, tile * ROWS), HOPS),
                hot_rows(four_rows(r.edge_rows, slot, tile * ROWS), HOT - HOPS),
            ],
            axis=0,
        ).astype(bf16)
        return dot_nn(r.lhs[:, : K + 2 * HOT], jnp.concatenate(pieces + [hot] * 2, axis=0))

    def biases(tile, bias):
        bias = bias.astype(bf16).astype(f32)
        for i in range(ROWS):
            r.bias[slot, pl.ds(tile * ROWS + i, H, stride=HALF), :] = bias[:, 128 * i : 128 * (i + 1)]

    in_stages([kernels, hold, hidden, hold, biases], TILES, beside)


def pair_backward(r, slot, between):
    bank = lax.rem(slot, 2)
    graph_on = r.flags[0, slot].astype(f32)
    space_on = r.flags[1, slot].astype(f32)
    twice(r.w2_twice, r.w2[:, :H] * space_on)

    def scores(tile, _):
        where = slice(tile * TILE, (tile + 1) * TILE)
        grad = jnp.concatenate(
            [r.bias[slot, pl.ds(tile * ROWS + i, H, stride=HALF), :] for i in range(ROWS)], axis=1
        )
        r.right[K:, where] = jnp.concatenate([grad * space_on, grad * graph_on], axis=0).astype(bf16)
        edge_hot = hot_rows(four_rows(r.edge_rows, slot, tile * ROWS), HOT - HOPS)
        edge_hot = jnp.where(iota((HOT - HOPS, TILE), 0) == EDGES, 1.0, edge_hot)
        r.left[bank, 2 * K :, where] = jnp.concatenate(
            [hot_rows(four_rows(r.hop_rows, slot, tile * ROWS), HOPS), edge_hot], axis=0
        ).astype(bf16)
        return dot_halves(r.w2_twice[...], [grad.astype(bf16)])

    def hidden(tile, d_second):
        where = slice(tile * TILE, (tile + 1) * TILE)
        pieces = []
        for rows in strips():
            pieces.append((d_second[rows] * r.slope[bank, rows, where].astype(f32)).astype(bf16))
            r.right[rows, where] = pieces[-1]
        return dot_halves(r.w1[...], pieces)

    def kernels(tile, d_gauss):
        where = slice(tile * TILE, (tile + 1) * TILE)
        arg = four_rows(r.argument, slot, tile * ROWS)
        d_arg = None
        for rows in strips():
            inv = widen(r.cols[4, rows])
            u = (arg - widen(r.cols[0, rows])) * inv
            q = d_gauss[rows] * r.left[bank, rows, where].astype(f32)
            w = q * u
            r.sums[0, rows] += fold_lanes(w)
            r.sums[1, rows] += fold_lanes(w * u - q)
            w = w * inv
            w = w[:8] + w[8:]
            d_arg = w if d_arg is None else d_arg + w
        d_arg = -jnp.sum(d_arg, axis=0, keepdims=True)
        for i in range(ROWS):
            at = tile * ROWS + i
            r.dargs[slot, at : at + 1, :] = d_arg[:, 128 * i : 128 * (i + 1)]

    in_stages([scores, hold, hidden, hold, kernels], TILES)
    between()
    r.acc_mixed[...] += dot_nt(r.left[bank], r.right[...])


def attend_group(r, s, first_slot, g):
    low = low_lanes(HALF)
    rows = span(s * SLOT, SLOT)
    if g == 0:
        r.work[0] = jnp.zeros((SLOT, D), f32)
    valid = iota((SLOT, GROUP * SLOT), 0) < r.lengths[first_slot + s]
    start, width, _ = window(g)
    q = r.joined[rows, start : start + width]
    k = r.joined[rows, D + start : D + start + width]
    v = r.joined[rows, 2 * D + start : 2 * D + start + width]
    scores = dot_nt(k, spread_heads(q, g)) * head_scale
    parts = []
    for pair in range(GROUP // 2):
        head = GROUP * g + 2 * pair
        one = r.bias[s, head * HALF : (head + 1) * HALF, :]
        two = r.bias[s, (head + 1) * HALF : (head + 2) * HALF, :]
        top = jnp.where(low, one, half_swap(two))
        bottom = jnp.where(low, half_swap(one), two)
        parts.append(jnp.concatenate([top, bottom], axis=0))
    scores = jnp.where(valid, scores + jnp.concatenate(parts, axis=1), neg_large)
    weights = jnp.exp(scores - jnp.max(scores, axis=0, keepdims=True))
    prob = (weights * (1.0 / jnp.sum(weights, axis=0, keepdims=True))).astype(bf16)
    r.prob[s, :, g * GROUP * SLOT : (g + 1) * GROUP * SLOT] = prob
    r.work[0, :, start : start + width] += gather_heads(dot_tn(prob, v), g)
    if g == GROUPS - 1:
        r.attended[rows, :] = r.work[0].astype(bf16)


def attend_back(r, s):
    low = low_lanes(HALF)
    rows = span(s * SLOT, SLOT)
    r.work[...] = jnp.zeros((3, SLOT, D), f32)
    for g in range(GROUPS):
        start, width, _ = window(g)
        lanes = slice(start, start + width)
        k = r.joined[rows, D + start : D + start + width]
        v = r.joined[rows, 2 * D + start : 2 * D + start + width]
        q_heads = spread_heads(r.joined[rows, lanes], g)
        d_heads = spread_heads(r.d_attended[rows, lanes], g)
        prob = r.prob[s, :, g * GROUP * SLOT : (g + 1) * GROUP * SLOT]
        wide = prob.astype(f32)
        d_prob = dot_nt(v, d_heads)
        inner = jnp.sum(wide * d_prob, axis=0, keepdims=True)
        d_scores = (wide * (d_prob - inner)).astype(bf16)
        r.work[0, :, lanes] += gather_heads(dot_tn(d_scores, k), g)
        r.work[1, :, lanes] += dot_nn(d_scores, q_heads)
        r.work[2, :, lanes] += dot_nn(prob, d_heads)
        d_wide = d_scores.astype(f32)
        for pair in range(GROUP // 2):
            head = GROUP * g + 2 * pair
            top = d_wide[:HALF, 128 * pair : 128 * (pair + 1)]
            bottom = d_wide[HALF:, 128 * pair : 128 * (pair + 1)]
            r.bias[s, head * HALF : (head + 1) * HALF, :] = jnp.where(low, top, half_swap(bottom))
            r.bias[s, (head + 1) * HALF : (head + 2) * HALF, :] = jnp.where(low, half_swap(top), bottom)
    r.joined[rows, 0:D] = (r.work[0] * head_scale).astype(bf16)
    r.joined[rows, D : 2 * D] = (r.work[1] * head_scale).astype(bf16)
    r.joined[rows, 2 * D : 3 * D] = r.work[2].astype(bf16)


def project(r, rows):
    scaled, _ = standardize(r.hidden[rows, :].astype(f32))
    normed = (scaled * row_of(r.attn_gain) + row_of(r.attn_shift)).astype(bf16)
    r.normed_a[rows, :] = normed
    for m in range(3):
        for t in range(2):
            at = m * D + t * HALF_D
            r.joined[rows, at : at + HALF_D] = dot_nn(normed, r.wqkv[t, m]).astype(bf16)


def feed(r, rows):
    halves = [slice(0, HALF_D), slice(HALF_D, D)]
    resid = r.hidden[rows, :].astype(f32)
    for t in range(2):
        resid = resid + dot_nn(r.attended[rows, halves[t]], r.wproj[t])
    scaled, inv_std = standardize(resid)
    normed = (scaled * row_of(r.ffn_gain) + row_of(r.ffn_shift)).astype(bf16)
    r.normed_f[rows, :] = normed
    pre = jnp.concatenate([dot_nn(normed, r.wup[t]) for t in range(2)], axis=1)
    value, slope = gelu_parts(pre + row_of(r.up_bias))
    active = value.astype(bf16)
    r.activated[rows, :] = active
    result = resid + row_of(r.down_bias)
    for t in range(2):
        result = result + dot_nn(active[:, halves[t]], r.wdown[t])
    r.out_rows[rows, :] = result.astype(bf16)
    cot = r.cotangent[rows, :]
    cot_wide = cot.astype(f32)
    d_active = jnp.concatenate([dot_nt(cot, r.wdown[t]) for t in range(2)], axis=1)
    d_hidden = (d_active * slope).astype(bf16)
    r.d_pre[rows, :] = d_hidden
    d_normed = dot_nt(d_hidden[:, halves[0]], r.wup[0]) + dot_nt(d_hidden[:, halves[1]], r.wup[1])
    d_resid = cot_wide + norm_back(d_normed, scaled, inv_std, row_of(r.ffn_gain))
    r.d_resid[rows, :] = d_resid
    branch = d_resid.astype(bf16)
    r.d_branch[rows, :] = branch
    for t in range(2):
        r.d_attended[rows, halves[t]] = dot_nt(branch, r.wproj[t]).astype(bf16)
    r.vectors[2:3, :] += column_sum(d_normed * scaled)
    r.vectors[3:4, :] += column_sum(d_normed)
    r.vectors[4:5, :] += column_sum(d_hidden.astype(f32))
    r.vectors[5:6, :] += column_sum(cot_wide)


def feed_grads(r, block):
    halves = [slice(0, HALF_D), slice(HALF_D, D)]
    if block == 0:
        grad = dot_tn(r.normed_f[...], r.d_pre[...]).astype(bf16)
        for t in range(2):
            r.fpart[t, :D, :] = grad[:, halves[t]]
        return
    left, right = (r.attended, r.d_branch) if block == 1 else (r.activated, r.cotangent)
    for t in range(2):
        grad = dot_tn(left[:, halves[t]], right[...]).astype(bf16)
        for side in range(2):
            r.fpart[t, D * block + HALF_D * side : D * block + HALF_D * (side + 1), :] = grad[:, halves[side]]


def qkv_grads(r, block):
    rows = slice(256 * block, 256 * (block + 1))
    for m in range(3):
        grad = dot_tn(r.normed_a[:, rows], r.joined[:, m * D : (m + 1) * D]).astype(bf16)
        for t in range(2):
            r.qpart[t, rows, m * HALF_D : (m + 1) * HALF_D] = grad[:, t * HALF_D : (t + 1) * HALF_D]


def finish_input(r, rows):
    d_normed = None
    for m in range(3):
        for t in range(2):
            at = m * D + t * HALF_D
            term = dot_nt(r.joined[rows, at : at + HALF_D], r.wqkv[t, m])
            d_normed = term if d_normed is None else d_normed + term
    scaled, inv_std = standardize(r.hidden[rows, :].astype(f32))
    grad = r.d_resid[rows, :] + norm_back(d_normed, scaled, inv_std, row_of(r.attn_gain))
    r.in_rows[rows, :] = grad.astype(bf16)
    r.vectors[0:1, :] += column_sum(d_normed * scaled)
    r.vectors[1:2, :] += column_sum(d_normed)


def pack_small(r, slots):
    tables = table_grads(r, slots)
    for v in range(6):
        for i in range(D // 128):
            at = VECTOR_ROWS + v * (D // 128) + i
            r.spart[at : at + 1, :] = r.vectors[v : v + 1, 128 * i : 128 * (i + 1)]
    r.spart[0:K, :] = r.acc_mixed[0:K, :K]
    r.spart[SECOND_ROWS : SECOND_ROWS + H, :] = square_turn(r.acc_mixed[K : 2 * K, K:])[:H]
    r.spart[TABLE_ROWS : TABLE_ROWS + H, :HOT] = square_turn(r.acc_mixed[2 * K :, K:])[H : 2 * H, :HOT]
    for index in range(2):
        rows = slice(TABLE_ROWS + ATOMS * index, TABLE_ROWS + ATOMS * (index + 1))
        r.spart[rows, HOT : HOT + ATOMS] = tables[index]
    ones = 2 * K + HOPS + EDGES
    r.spart[KERNEL_ROWS : KERNEL_ROWS + 1, :] = r.acc_mixed[ones : ones + 1, :K]
    for index in range(2):
        column = jnp.sum(r.sums[index] * r.cols[4], axis=1, keepdims=True)
        same = iota((K, K), 0) == iota((K, K), 1)
        at = KERNEL_ROWS + 1 + index
        r.spart[at : at + 1, :] = jnp.sum(jnp.where(same, column, 0.0), axis=0, keepdims=True)


class Stage:
    def __init__(self, names, near_inputs, carried, refs):
        self.r = SimpleNamespace(**dict(zip(names, refs)))
        r = self.r
        self.loads = {
            name: pltpu.make_async_copy(getattr(r, "given_" + name), getattr(r, name), r.input_sems.at[i])
            for i, name in enumerate(near_inputs)
        }
        self.stores = {
            name: pltpu.make_async_copy(getattr(r, name), getattr(r, name + "_far"), r.carry_sems.at[i])
            for i, name in enumerate(carried)
        }

    def load(self, *names):
        for name in names:
            self.loads[name].start()

    def need(self, *names):
        for name in names:
            self.loads[name].wait()

    def store(self, *names):
        for name in names:
            self.stores[name].start()

    def stored(self):
        for copy in self.stores.values():
            copy.wait()


def each_chunk(r, tokens, work):
    chunk = min(512, tokens)

    def one(c, _):
        work(r, span(c * chunk, chunk))
        return 0

    lax.fori_loop(0, tokens // chunk, one, 0)


def pair_moves(r, slot, back):
    bank = lax.rem(slot, 2)
    both = (r.left_far.at[slot], r.left.at[bank, : 2 * K]), (r.slope_far.at[slot], r.slope.at[bank])
    for index, (far, near) in enumerate(both):
        yield pltpu.make_async_copy(*((far, near) if back else (near, far)), r.pair_sems.at[bank, index])


def start_moves(r, slot, back):
    for copy in pair_moves(r, slot, back):
        copy.start()


def wait_moves(r, slot, back):
    for copy in pair_moves(r, slot, back):
        copy.wait()


def run(steps):
    for act, *where in steps:
        act(*where)


def at_time(index, plan):
    for k, steps in plan.items():
        pl.when(index == k)(functools.partial(run, steps))


FFN_BACK = {0: [(1, 1), (2, 1)], 3: [(0, 2)], 7: [(0, 3), (1, 2)]}
AFTER_GRADS = ([(0, 4), (1, 3), (2, 2)], [(0, 1), (1, 1), (2, 1)])
AFTER_HALF = ([(0, 5)], [])
AFTER_INPUT = ([(2, 3), (1, 4)], [(0, 2)])
FFN_PAIRS = {
    0: [(0, 6)], 2: [(2, 4)], 3: [(1, 5), (0, 7)], 5: [(2, 5)], 7: [(1, 6)], 9: [(2, 6)], 10: [(1, 7)], 12: [(2, 7)],
}
QKV_PAIRS = {
    2: [(0, 3)], 3: [(1, 2)], 6: [(1, 3), (2, 2), (0, 4)], 9: [(1, 4)], 10: [(0, 5)], 11: [(2, 3)], 12: [(1, 5)],
    13: [(0, 6)], 14: [(2, 4)], 15: [(1, 6)],
}


def layer_kernel(remote, names, near_inputs, carried, *refs):
    stage = Stage(names, near_inputs, carried, refs)
    r = stage.r
    stage.load(*[name for name in near_inputs if name not in ("hidden", "cotangent")])
    tokens = r.hidden.shape[0]
    slots = tokens // SLOT
    peers = Peers()
    if remote:
        greet(peers.everyone())
    whole = [r.wqkv, r.wup, r.wproj, r.wdown]
    given = [r.given_qkv, r.given_up, r.given_proj, r.given_down]
    targets = [w.at[peers.tp] for w in whole] if remote else whole
    loads = [
        pltpu.make_async_copy(src, dst, r.load_sems.at[i]) for i, (src, dst) in enumerate(zip(given, targets))
    ]
    for load in loads:
        load.start()
    stage.load("hidden", "cotangent")
    gather_plan = {}
    if remote:

        def whole_piece(index, tp):
            return whole[0].at[tp, index] if index < 3 else whole[index - 2].at[tp]

        gather = Gather(peers, whole_piece, r.gather_sends, r.gather_recvs)
        ffn = Reduction(peers, r.fpart, r.ftotal, r.f_core, r.f_tp, r.f_x, r.f_z, r.f_sends, r.f_recvs)
        qkv = Reduction(peers, r.qpart, r.qtotal, r.q_core, r.q_tp, r.q_x, r.q_z, r.q_sends, r.q_recvs)
        small = SmallReduction(peers, r.spart, r.stotal, r.s_near, r.s_z, r.s_sends, r.s_recvs)
        x, core = gather.onward_x, gather.onward_core
        gather_plan = {
            0: [(x, 0)], 1: [(x, 1)], 2: [(core, 0), (x, 2)], 3: [(core, 1), (x, 3), (core, 2)],
            4: [(x, 4)], 5: [(core, 3), (x, 5)], 6: [(core, 4)], 7: [(core, 5)],
        }

    def leave(which, block):
        near, far = ((r.ftotal, r.ftotal_far), (r.qtotal, r.qtotal_far))[which]
        rows = near.shape[0] // 3
        at = slice(block * rows, (block + 1) * rows)
        return pltpu.make_async_copy(near.at[at], far.at[at], r.leave_sems.at[3 * which + block])

    def advance(which, actions):
        if remote:
            for block, step in actions:
                (ffn, qkv)[which].act(block, step)
                if step == 7:
                    leave(which, block).start()

    def plan_of(*plans):
        times = sorted(set().union(*plans)) if remote else []
        return {
            k: [(advance, which, plan[k]) for which, plan in enumerate(plans) if k in plan] for k in times
        }

    stage.need(*[name for name in near_inputs if name not in ("hidden", "cotangent")])
    prepare_pairs(r)
    pair_tables(r, slots)
    if remote:
        await_greetings(peers.everyone())
        for load, indices in zip(loads, ((0, 1, 2), (3,), (4,), (5,))):
            load.wait()
            gather.start(indices)

    first_slot = peers.tp * slots
    alone = (5 * slots + 7) // 8

    def pairs(slot, _):
        pl.when(slot >= 2)(lambda: wait_moves(r, slot - 2, False))
        pair_forward(r, slot)
        start_moves(r, slot, False)
        at_time(slot, gather_plan)
        return 0

    def pairs_and_attention(slot, _):
        def beside(time):
            if 1 <= time <= GROUPS:
                attend_group(r, slot - alone, first_slot, time - 1)

        pl.when(slot >= 2)(lambda: wait_moves(r, slot - 2, False))
        pair_forward(r, slot, beside)
        start_moves(r, slot, False)
        at_time(slot, gather_plan)
        return 0

    def attend_one(s, _):
        for g in range(GROUPS):
            attend_group(r, s, first_slot, g)
        return 0

    lax.fori_loop(0, alone, pairs, 0)
    stage.need("hidden")
    if remote:
        for index in range(3):
            gather.arrive(index)
    else:
        for load in loads:
            load.wait()
    each_chunk(r, tokens, project)
    lax.fori_loop(alone, slots, pairs_and_attention, 0)
    lax.fori_loop(slots - alone, slots, attend_one, 0)
    stage.need("cotangent")
    if remote:
        for index in range(3, 6):
            gather.arrive(index)
    r.vectors[...] = jnp.zeros_like(r.vectors)
    each_chunk(r, tokens, feed)
    stage.store("out_rows")
    for slot in (slots - 2, slots - 1):
        wait_moves(r, slot, False)
    start_moves(r, 0, True)
    start_moves(r, 1, True)
    for block in range(3):
        feed_grads(r, block)
        advance(0, [(block, 0)])
    advance(0, [(0, 1)])

    back_plan, pair_plan = plan_of(FFN_BACK), plan_of(FFN_PAIRS, QKV_PAIRS)

    def back_one(s, _):
        attend_back(r, s)
        at_time(s, back_plan)
        return 0

    lax.fori_loop(0, slots, back_one, 0)
    for block in range(3):
        qkv_grads(r, block)
        advance(1, [(block, 0)])
    for which in range(2):
        advance(which, AFTER_GRADS[which])
    each_chunk(r, tokens, finish_input)
    stage.store("in_rows")
    for which in range(2):
        advance(which, AFTER_HALF[which] + AFTER_INPUT[which])
    for ref in (r.sums, r.acc_mixed, r.spart):
        ref[...] = jnp.zeros_like(ref)

    def pairs_back(slot, _):
        wait_moves(r, slot, True)
        pair_backward(r, slot, lambda: at_time(2 * slot, pair_plan))
        pl.when(slot + 2 < slots)(lambda: start_moves(r, slot + 2, True))
        at_time(2 * slot + 1, pair_plan)
        return 0

    lax.fori_loop(0, slots, pairs_back, 0)
    pack_small(r, slots)
    if remote:
        small.act(0)
        advance(1, [(2, 5), (0, 7)])
        small.act(1)
        advance(1, [(1, 7)])
        advance(1, [(2, 6)])
        small.act(2)
        advance(1, [(2, 7)])
        small.act(3)
        rows = pltpu.make_async_copy(r.stotal, r.stotal_far, r.leave_sems.at[6])
        rows.start()
        for which in range(2):
            advance(which, [(b, 8) for b in range(3)])
        small.act(4)
        gather.finish()
        for which in range(2):
            for block in range(3):
                leave(which, block).wait()
        rows.wait()
    else:
        stage.store("fpart", "qpart", "spart")
    stage.stored()


def call_stage(kernel, name, remote, collective, arrays, scalars, far, outs, carried, scratch):
    vm, sem = pltpu.VMEM, pltpu.SemaphoreType.DMA
    near = {n: vm(a.shape, a.dtype) for n, a in arrays.items() if n not in scalars + far}
    in_names = [n if n in scalars or n.endswith("_far") else "given_" + n for n in arrays]
    results = outs | {n + "_far": item for n, item in carried.items()}
    scratch = near | {n: vm(*item) for n, item in carried.items()} | scratch
    scratch |= {"input_sems": sem((len(near),)), "carry_sems": sem((len(carried),))}
    names = in_names + list(results) + list(scratch)
    values = pl.pallas_call(
        functools.partial(kernel, remote, names, list(near), list(carried)),
        in_specs=[pl.BlockSpec(memory_space=pltpu.SMEM if n in scalars else pl.ANY) for n in arrays],
        out_specs=[pl.BlockSpec(memory_space=pl.ANY)] * len(results),
        out_shape=[jax.ShapeDtypeStruct(*item) for item in results.values()],
        scratch_shapes=list(scratch.values()),
        compiler_params=pltpu.CompilerParams(
            vmem_limit_bytes=VMEM_BYTES, **(dict(collective_id=collective, has_side_effects=True) if remote else {})
        ),
        name=name,
    )(*arrays.values())
    return dict(zip(results, values))


def layer(remote, arrays):
    tokens = arrays["hidden"].shape[0]
    slots = tokens // SLOT
    v, sem = pltpu.VMEM, pltpu.SemaphoreType.DMA
    of_tokens = (tokens, D)
    table = (slots, HALF, 128)
    fshape, qshape, sshape = (3 * D, HALF_D), (D, 3 * HALF_D), (SMALL_ROWS, 128)
    outs = {"left_far": ((slots, 2 * K, PAIRS), bf16), "slope_far": ((slots, K, PAIRS), bf16)}
    carried = {"out_rows": (of_tokens, bf16), "in_rows": (of_tokens, bf16)}
    scratch = {
        "wqkv": v((2, 3, D, HALF_D), bf16), "wup": v((2, D, HALF_D), bf16), "wproj": v((2, HALF_D, D), bf16),
        "wdown": v((2, HALF_D, D), bf16), "load_sems": sem((4,)), "pair_sems": sem((2, 2)),
        "left": v((2, 2 * K + HOT, PAIRS), bf16), "slope": v((2, K, PAIRS), bf16),
        "right": v((K + 2 * H, PAIRS), bf16), "cols": v((5, K, 128), f32), "w1": v((2 * K, 2 * K), bf16), "w1t": v((2 * K, 2 * K), bf16),
        "w2": v((K, 128), f32), "w2_twice": v((2 * K, 2 * H), bf16), "base": v((H, 256), f32), "lhs": v((H, 256), bf16),
        "argument": v(table, f32), "distance": v(table, f32), "hop_rows": v(table, f32), "edge_rows": v(table, f32),
        "atom_rows": v((slots, 8, 128), f32), "dargs": v(table, f32), "bias": v((slots, H * HALF, 128), f32),
        "work": v((3, SLOT, D), f32), "normed_a": v(of_tokens, bf16), "joined": v((tokens, 3 * D), bf16),
        "prob": v((slots, SLOT, H * SLOT), bf16), "attended": v(of_tokens, bf16), "normed_f": v(of_tokens, bf16),
        "activated": v(of_tokens, bf16), "d_pre": v(of_tokens, bf16), "d_branch": v(of_tokens, bf16),
        "d_attended": v(of_tokens, bf16), "d_resid": v(of_tokens, f32), "vectors": v((8, D), f32),
        "sums": v((2, K, 128), f32), "acc_mixed": v((2 * K + HOT, K + 2 * H), f32),
    }
    parts = {"fpart": ((2,) + fshape, bf16), "qpart": ((2,) + qshape, bf16), "spart": (sshape, f32)}
    totals = {"ftotal": (fshape, bf16), "qtotal": (qshape, bf16), "stotal": (sshape, f32)}
    if remote:
        outs |= {n + "_far": item for n, item in totals.items()}
        scratch |= {n: v(*item) for n, item in (parts | totals).items()}
        scratch |= {"leave_sems": sem((7,)), "gather_sends": sem((6, 4)), "gather_recvs": sem((6, 4))}
        for name, shape in (("f", (D, HALF_D)), ("q", (D // 3, 3 * HALF_D))):
            keys = ("_core", "_tp", "_x", "_z", "_sends", "_recvs")
            scratch |= {name + key: item for key, item in zip(keys, big_scratch(*shape))}
        scratch |= dict(zip(("s_near", "s_z", "s_sends", "s_recvs"), small_scratch()))
    else:
        carried |= parts
    results = call_stage(
        layer_kernel, "layer", remote, 0, arrays, ("lengths", "flags"), ("qkv", "up", "proj", "down"), outs, carried,
        scratch,
    )
    sums = [results[n + "_far"] for n in (totals if remote else parts)]
    return results["out_rows_far"], results["in_rows_far"], sums


RESULTS = (
    "output", "grad_input", "attn_gain", "attn_shift", "qkv", "proj", "ffn_gain", "ffn_shift", "up", "up_bias", "down",
    "down_bias", "scale", "shift", "centers", "spreads", "first", "first_bias", "second", "hop", "edge",
)


def unpack_kernel(*refs):
    given = SimpleNamespace(**dict(zip(("out_rows", "in_rows", "fsum", "qsum", "rows"), refs)))
    far = SimpleNamespace(**dict(zip(RESULTS, refs[5:])))
    count = len(RESULTS)
    near = SimpleNamespace(**dict(zip(RESULTS, refs[5 + count : 5 + 2 * count])))
    fsum, qsum, rows, load_sems, store_sems = refs[5 + 2 * count :]
    moves = [(given.rows, rows)]
    sources = ((given.qsum, qsum, 3), (given.fsum, fsum, 9), (given.out_rows, near.output, 1), (given.in_rows, near.grad_input, 1))
    for src, dst, pieces in sources:
        height = src.shape[0] // pieces
        for i in range(pieces):
            at = slice(i * height, (i + 1) * height)
            moves.append((src.at[at], dst.at[at]))
    loads = [pltpu.make_async_copy(src, dst, load_sems.at[i]) for i, (src, dst) in enumerate(moves)]
    for load in loads:
        load.start()
    stores = []

    def store(src, dst):
        stores.append(pltpu.make_async_copy(src, dst, store_sems.at[len(stores)]))
        stores[-1].start()

    for i in range(3):
        loads[1 + i].wait()
        at = slice(256 * i, 256 * (i + 1))
        for m in range(3):
            near.qkv[m, at] = qsum[at, m * HALF_D : (m + 1) * HALF_D].astype(f32)
        store(near.qkv.at[:, at], far.qkv.at[:, at])
    for i in range(3):
        loads[4 + i].wait()
        at = slice(256 * i, 256 * (i + 1))
        near.up[at, :] = fsum[at, :].astype(f32)
        store(near.up.at[at], far.up.at[at])
    for block, name in ((1, "proj"), (2, "down")):
        for i in range(3):
            loads[4 + 3 * block + i].wait()
        ref = getattr(near, name)
        at = D * block
        ref[:, :HALF_D] = fsum[at : at + HALF_D, :].astype(f32)
        ref[:, HALF_D:] = fsum[at + HALF_D : at + D, :].astype(f32)
        store(ref, getattr(far, name))
    loads[13].wait()
    store(near.output, far.output)
    loads[14].wait()
    store(near.grad_input, far.grad_input)
    loads[0].wait()
    names = ("attn_gain", "attn_shift", "ffn_gain", "ffn_shift", "up_bias", "down_bias")
    for v, name in enumerate(names):
        for i in range(D // 128):
            getattr(near, name)[pl.ds(128 * i, 128)] = rows[VECTOR_ROWS + v * (D // 128) + i, :]
    near.first[...] = rows[0:K, :]
    near.second[...] = rows[SECOND_ROWS : SECOND_ROWS + H, :]
    table = rows[TABLE_ROWS : TABLE_ROWS + H, :]
    near.scale[...] = table[:ATOMS, HOT : HOT + ATOMS]
    near.shift[...] = table[ATOMS:, HOT : HOT + ATOMS]
    turned = square_turn(table)
    near.hop[...] = turned[:HOPS, :H]
    near.edge[...] = turned[HOPS : HOPS + EDGES, :H]
    lines = ("first_bias", "centers", "spreads")
    for i, name in enumerate(lines):
        getattr(near, name)[...] = rows[KERNEL_ROWS + i, :]
    for name in names + ("first", "second", "scale", "shift", "hop", "edge") + lines:
        store(getattr(near, name), getattr(far, name))
    for copy in stores:
        copy.wait()


def unpack(out_rows, in_rows, fsum, qsum, rows):
    tokens = out_rows.shape[0]
    vec, line, types = ((D,), f32), ((K,), f32), ((ATOMS, ATOMS), f32)
    shapes = (
        ((tokens, D), bf16), ((tokens, D), bf16), vec, vec, ((3, D, HALF_D), f32), ((HALF_D, D), f32), vec, vec,
        ((D, HALF_D), f32), vec, ((HALF_D, D), f32), vec, types, types, line, line, ((K, K), f32), line, ((H, K), f32),
        ((HOPS, H), f32), ((EDGES, H), f32),
    )
    anywhere = pl.BlockSpec(memory_space=pl.ANY)
    return pl.pallas_call(
        unpack_kernel,
        in_specs=[anywhere] * 5,
        out_specs=[anywhere] * len(shapes),
        out_shape=[jax.ShapeDtypeStruct(*item) for item in shapes],
        scratch_shapes=[pltpu.VMEM(*item) for item in shapes] + [
            pltpu.VMEM(fsum.shape, bf16), pltpu.VMEM(qsum.shape, bf16), pltpu.VMEM(rows.shape, f32),
            pltpu.SemaphoreType.DMA((15,)), pltpu.SemaphoreType.DMA((25,)),
        ],
        compiler_params=pltpu.CompilerParams(vmem_limit_bytes=VMEM_BYTES),
        name="unpack",
    )(out_rows, in_rows, fsum, qsum, rows)


def whole_weights(qkv_weight, up_weight, proj_weight, down_weight):
    columns = lambda w: jnp.stack(jnp.split(w, 2, axis=-1))
    rows = lambda w: jnp.stack(jnp.split(w, 2, axis=0))
    gather = lambda w, dim: lax.all_gather(w, "tp", axis=dim, tiled=True)
    return (
        columns(gather(qkv_weight.transpose(1, 0, 2), 2)), columns(gather(up_weight, 1)),
        rows(gather(proj_weight, 0)), rows(gather(down_weight, 0)),
    )


def sum_grads(fgrads, qgrads, small):
    total_f, total_q, rows = lax.psum((fgrads, qgrads, small), ("mol", "tp"))
    share = D // lax.axis_size("tp")
    at = lax.axis_index("tp") * share

    def columns(halves):
        return lax.dynamic_slice_in_dim(jnp.concatenate(list(halves), axis=-1), at, share, halves.ndim - 2)

    def rows_of(block):
        part = total_f[:, D * block : D * (block + 1)]
        sides = jnp.concatenate([part[:, :HALF_D], part[:, HALF_D:]], axis=2).reshape(D, D)
        return lax.dynamic_slice_in_dim(sides, at, share, 0)

    qkv = columns(total_q.reshape(2, D, 3, HALF_D)).transpose(1, 0, 2)
    return [v.astype(f32) for v in (qkv, columns(total_f[:, :D]), rows_of(1), rows_of(2))], rows


def body(
    mesh_shape,
    hidden_in, positions, atom_types, hop_counts, edge_types, lengths, branches,
    attn_gain, attn_shift, qkv_weight, proj_weight, ffn_gain, ffn_shift, up_weight, up_bias, down_weight, down_bias,
    kernel_scale, kernel_shift, centers, spreads, first_weight, first_bias, second_weight, hop_table, edge_table,
    cotangent,
):
    remote = mesh_shape["tp"] == 2 and mesh_shape["mol"] == 16 and branches.shape[0] == 8
    if remote:
        weights = (qkv_weight.transpose(1, 0, 2), up_weight, proj_weight, down_weight)
    else:
        weights = whole_weights(qkv_weight, up_weight, proj_weight, down_weight)
    arrays = dict(
        lengths=lengths, flags=branches.T, positions=positions, atoms=atom_types, hops=hop_counts.T,
        edges=edge_types.T, kernel_scale=kernel_scale, kernel_shift=kernel_shift, centers=centers, spreads=spreads,
        first_weight=first_weight, first_bias=first_bias, second_weight=second_weight.T, hop_table=hop_table,
        edge_table=edge_table, attn_gain=attn_gain, attn_shift=attn_shift, ffn_gain=ffn_gain, ffn_shift=ffn_shift,
        up_bias=up_bias, down_bias=down_bias, hidden=hidden_in, cotangent=cotangent,
        qkv=weights[0], up=weights[1], proj=weights[2], down=weights[3],
    )
    output, grad_input, sums = layer(remote, arrays)
    if remote:
        fsum, qsum, rows = sums
    else:
        big, rows = sum_grads(*sums)
        fsum, qsum = jnp.zeros((3 * D, HALF_D), bf16), jnp.zeros((D, 3 * HALF_D), bf16)
    output, grad_input, *grads = unpack(output, grad_input, fsum, qsum, rows)
    if not remote:
        grads[2], grads[6], grads[3], grads[8] = big
    grads[2] = grads[2].transpose(1, 0, 2)
    grads[16] = grads[16].T
    return (output, grad_input, *grads)


def solution(mesh):
    rows = P(("mol", "tp"), None)
    all_of = P()
    in_specs = (
        rows, P(None, ("mol", "tp")), P(("mol", "tp")), rows, rows, P("mol"), rows, all_of, all_of,
        P(None, None, "tp"), P("tp", None), all_of, all_of, P(None, "tp"), all_of, P("tp", None),
    ) + (all_of,) * 10 + (rows,)
    out_specs = (
        rows, rows, all_of, all_of, P(None, None, "tp"), P("tp", None), all_of, all_of, P(None, "tp"), all_of,
        P("tp", None),
    ) + (all_of,) * 10
    step = functools.partial(body, dict(mesh.shape))
    return jax.shard_map(step, mesh=mesh, in_specs=in_specs, out_specs=out_specs, check_vma=False)
```

```python
import functools
from types import SimpleNamespace

import jax
import jax.numpy as jnp
from jax import lax
from jax.experimental import pallas as pl
from jax.experimental.pallas import tpu as pltpu
from jax.sharding import PartitionSpec as P

D = 768
H = 32
HD = 24
FF = 768
K = 128
SLOT = 64
HALF = SLOT // 2
HALF_D = D // 2
PAIRS = SLOT * SLOT
HOPS = 16
EDGES = 8
ATOMS = 16
GROUP = 4
GROUPS = H // GROUP
HOT = 32

highest = lax.Precision.HIGHEST
neg_large = -1e30
root_tau = 2.5066282746310002
root_half = 0.7071067811865476
inv_root_tau = 0.3989422804014327
head_scale = HD ** (-0.5)
VMEM_BYTES = 62 * 1024 * 1024
TILE = 512

SECOND_ROWS = K
TABLE_ROWS = SECOND_ROWS + H
KERNEL_ROWS = TABLE_ROWS + H
VECTOR_ROWS = KERNEL_ROWS + 8
SMALL_ROWS = 256

MESH = pl.DeviceIdType.MESH
f32 = jnp.float32
bf16 = jnp.bfloat16


def dot_nn(left, right, precision=None):
    return lax.dot_general(left, right, (((1,), (0,)), ((), ())), precision=precision, preferred_element_type=f32)


def dot_nt(left, right, precision=None):
    return lax.dot_general(left, right, (((1,), (1,)), ((), ())), precision=precision, preferred_element_type=f32)


def dot_tn(left, right, precision=None):
    return lax.dot_general(left, right, (((0,), (0,)), ((), ())), precision=precision, preferred_element_type=f32)


def iota(shape, dim):
    return lax.broadcasted_iota(jnp.int32, shape, dim)


def gelu_parts(values):
    size = jnp.abs(values)
    bell = jnp.exp(values * values * -0.5)
    denominator = 1.0 + (0.3275911 * root_half) * size
    t = pl.reciprocal(denominator, approx=True)
    series = 0.5 * 1.061405429
    for factor in (-1.453152027, 1.421413741, -0.284496736, 0.254829592):
        series = series * t + 0.5 * factor
    tail = series * t * bell
    gelu = jnp.maximum(values, 0.0) - size * tail
    outer = tail - size * (bell * inv_root_tau)
    return gelu, jnp.where(values >= 0.0, 1.0 - outer, outer)


def gelu_pair(values):
    size = jnp.abs(values)
    bell = jnp.exp(values * values * -0.5)
    t = pl.reciprocal(1.0 + (0.3275911 * root_half) * size, approx=True)
    series = 0.5 * 1.061405429
    for factor in (-1.453152027, 1.421413741, -0.284496736, 0.254829592):
        series = series * t + 0.5 * factor
    tail = (series * t * bell).astype(bf16)
    density = (bell * inv_root_tau).astype(bf16)
    values = values.astype(bf16)
    size = jnp.abs(values)
    outer = tail - size * density
    one, zero = jnp.ones((), bf16), jnp.zeros((), bf16)
    return jnp.maximum(values, zero) - size * tail, jnp.where(values >= zero, one - outer, outer)


def to_column(row):
    size = row.shape[1]
    same = iota((size, size), 0) == iota((size, size), 1)
    return jnp.sum(jnp.where(same, row, 0.0), axis=1, keepdims=True)


def half_swap(values):
    return pltpu.roll(values, 64, 1)


def low_lanes(rows):
    return iota((rows, 128), 1) < 64


def vmem(count):
    return [pl.BlockSpec(memory_space=pltpu.VMEM)] * count


def row_of(ref):
    return ref[...].reshape(1, ref.shape[0])


def place():
    mol = lax.axis_index("mol")
    return mol % 2, (mol // 2) % 2, mol // 4, lax.axis_index("tp")


def greet(peers):
    for peer in peers:
        pl.semaphore_signal(pltpu.get_barrier_semaphore(), inc=1, device_id=peer, device_id_type=MESH)


def await_greetings(peers):
    pl.semaphore_wait(pltpu.get_barrier_semaphore(), len(peers))


def window(group):
    first = GROUP * HD * group
    start = first // 128 * 128
    width = 128 if first - start + GROUP * HD <= 128 else 256
    return start, width, first - start


def head_masks(group, kind):
    _, width, offset = window(group)
    lane = iota((1, width), 1)
    return [
        ((lane >= offset + HD * h) & (lane < offset + HD * (h + 1))).astype(f32).astype(kind) for h in range(GROUP)
    ]


def spread_heads(values, group):
    return jnp.concatenate([values * mask for mask in head_masks(group, bf16)], axis=0)


def gather_heads(values, group):
    masks = head_masks(group, f32)
    total = values[:SLOT] * masks[0]
    for h in range(1, GROUP):
        total = total + values[SLOT * h : SLOT * (h + 1)] * masks[h]
    return total


def standardize(values):
    centred = values - jnp.mean(values, axis=-1, keepdims=True)
    inv_std = lax.rsqrt(jnp.mean(centred * centred, axis=-1, keepdims=True) + 1e-05)
    return centred * inv_std, inv_std


def norm_back(d_normed, scaled, inv_std, gain):
    weighted = d_normed * gain
    inner_a = jnp.mean(weighted, axis=-1, keepdims=True)
    inner_b = jnp.mean(weighted * scaled, axis=-1, keepdims=True)
    return inv_std * (weighted - inner_a - scaled * inner_b)


def column_sum(values):
    return jnp.sum(values, axis=0, keepdims=True)


class Peers:
    def __init__(self):
        self.core, self.x, self.z, self.tp = place()
        mol = lax.axis_index("mol")
        self.over_core = {"mol": mol + 1 - 2 * self.core}
        self.over_x = {"mol": mol + 2 - 4 * self.x}
        self.over_tp = {"tp": 1 - self.tp}
        self.turn = [lax.rem(self.z + d, 4) for d in range(4)]
        self.over_z = [{"mol": self.turn[d] * 4 + self.x * 2 + self.core} for d in range(4)]

    def neighbour(self, k):
        core = self.core + (1 - 2 * self.core) * (k & 1)
        x = self.x + (1 - 2 * self.x) * (k >> 1 & 1)
        tp = self.tp + (1 - 2 * self.tp) * (k >> 2)
        return core * 4 + tp * 2 + x, {"mol": self.z * 4 + x * 2 + core, "tp": tp}

    def everyone(self):
        return [self.neighbour(k)[1] for k in range(1, 8)] + self.over_z[1:]


def span(start, size):
    return pl.ds(pl.multiple_of(start, size), size)


def add_rows(target, source, rows):
    step = 96 if rows % 96 == 0 else min(rows, 32)

    def piece(i, _):
        at = pl.ds(pl.multiple_of(i * step, step), step)
        target[at, :] = target[at, :] + source[at, :]
        return 0

    lax.fori_loop(0, rows // step, piece, 0)


class Reduction:
    kinds = 11

    def __init__(self, peers, part, total, from_core, from_tp, from_x, from_z, sends, recvs):
        self.peers, self.part, self.total = peers, part, total
        self.from_core, self.from_tp, self.from_x, self.from_z = from_core, from_tp, from_x, from_z
        self.sends, self.recvs = sends, recvs
        self.half = from_core.shape[2]
        self.quarter, self.least = self.half // 2, self.half // 8

    def rows(self, b, level):
        p = self.peers
        at = b * 2 * self.half + p.core * self.half
        if level > 0:
            at = at + p.x * self.quarter
        return at + p.z * self.least if level > 1 else at

    def copy(self, b, kind):
        p = self.peers
        part, total = self.part, self.total
        half, quarter, least = self.half, self.quarter, self.least
        if kind == 0:
            src = part.at[:, span(b * 2 * half + (1 - p.core) * half, half)]
            dst, peer = self.from_core.at[b], p.over_core
        elif kind == 1:
            src, dst, peer = part.at[1 - p.tp, span(self.rows(b, 0), half)], self.from_tp.at[b], p.over_tp
        elif kind == 2:
            src = part.at[p.tp, span(self.rows(b, 0) + (1 - p.x) * quarter, quarter)]
            dst, peer = self.from_x.at[b], p.over_x
        elif kind < 6:
            d = kind - 2
            src = part.at[p.tp, span(self.rows(b, 1) + p.turn[d] * least, least)]
            dst, peer = self.from_z.at[b, d - 1], p.over_z[d]
        elif kind < 9:
            src = dst = total.at[span(self.rows(b, 2), least)]
            peer = p.over_z[kind - 5]
        elif kind == 9:
            src = dst = total.at[span(self.rows(b, 1), quarter)]
            peer = p.over_x
        else:
            src = dst = total.at[span(self.rows(b, 0), half)]
            peer = p.over_core
        return pltpu.make_async_remote_copy(
            src_ref=src, dst_ref=dst, send_sem=self.sends.at[b, kind], recv_sem=self.recvs.at[b, kind],
            device_id=peer, device_id_type=MESH,
        )

    def act(self, b, stage):
        p = self.peers
        half, quarter, least = self.half, self.quarter, self.least
        part = self.part
        if stage == 0:
            self.copy(b, 0).start()
        elif stage == 1:
            self.copy(b, 0).wait_recv()
            at = span(self.rows(b, 0), half)
            add_rows(part.at[1 - p.tp, at], self.from_core.at[b, 1 - p.tp], half)
            self.copy(b, 1).start()
            add_rows(part.at[p.tp, at], self.from_core.at[b, p.tp], half)
        elif stage == 2:
            self.copy(b, 1).wait_recv()
            away, mine = (1 - p.x) * quarter, p.x * quarter
            at = self.rows(b, 0)
            add_rows(part.at[p.tp, span(at + away, quarter)], self.from_tp.at[b, span(away, quarter)], quarter)
            self.copy(b, 2).start()
            add_rows(part.at[p.tp, span(at + mine, quarter)], self.from_tp.at[b, span(mine, quarter)], quarter)
        elif stage == 3:
            self.copy(b, 2).wait_recv()
            add_rows(part.at[p.tp, span(self.rows(b, 1), quarter)], self.from_x.at[b], quarter)
            for kind in (3, 4, 5):
                self.copy(b, kind).start()
        elif stage == 4:
            for kind in (3, 4, 5):
                self.copy(b, kind).wait_recv()
            mine = span(self.rows(b, 2), least)
            value = part[p.tp, mine, :].astype(f32)
            for d in range(3):
                value = value + self.from_z[b, d].astype(f32)
            self.total[mine, :] = value.astype(bf16)
            for kind in (6, 7, 8):
                self.copy(b, kind).start()
        elif stage == 5:
            for kind in (6, 7, 8):
                self.copy(b, kind).wait_recv()
            self.copy(b, 9).start()
        elif stage == 6:
            self.copy(b, 9).wait_recv()
            self.copy(b, 10).start()
        elif stage == 7:
            self.copy(b, 10).wait_recv()
        else:
            for kind in range(self.kinds):
                self.copy(b, kind).wait_send()


class SmallReduction:
    def __init__(self, peers, part, total, from_near, from_z, sends, recvs):
        self.peers, self.part, self.total, self.from_near, self.from_z = peers, part, total, from_near, from_z
        self.sends, self.recvs = sends, recvs
        p = peers
        self.near = [p.neighbour(k) for k in range(8)]
        self.mine = span(self.near[0][0] * 32, 32)

    def copy(self, kind):
        p = self.peers
        if kind < 7:
            index, peer = self.near[kind + 1]
            src, dst = self.part.at[span(index * 32, 32)], self.from_near.at[kind]
        elif kind < 10:
            src = dst = self.from_z.at[p.z]
            peer = p.over_z[kind - 6]
        else:
            src = dst = self.total.at[self.mine]
            peer = self.near[kind - 9][1]
        return pltpu.make_async_remote_copy(
            src_ref=src, dst_ref=dst, send_sem=self.sends.at[kind], recv_sem=self.recvs.at[kind],
            device_id=peer, device_id_type=MESH,
        )

    def act(self, stage):
        hops = (range(0, 7), range(7, 10), range(10, 17))
        if stage == 4:
            for kind in range(17):
                self.copy(kind).wait_send()
            return
        if stage > 0:
            for kind in hops[stage - 1]:
                self.copy(kind).wait_recv()
        if stage == 1:
            value = self.part[self.mine, :]
            for k in range(7):
                value = value + self.from_near[k]
            self.from_z[self.peers.z] = value
        elif stage == 2:
            self.total[self.mine, :] = (self.from_z[0] + self.from_z[1]) + (self.from_z[2] + self.from_z[3])
        if stage < 3:
            for kind in hops[stage]:
                self.copy(kind).start()


def big_scratch(rows, lanes):
    half = rows // 2
    sems = pltpu.SemaphoreType.DMA((3, Reduction.kinds))
    return [
        pltpu.VMEM((3, 2, half, lanes), bf16), pltpu.VMEM((3, half, lanes), bf16),
        pltpu.VMEM((3, half // 2, lanes), bf16), pltpu.VMEM((3, 3, half // 8, lanes), bf16), sems, sems,
    ]


def small_scratch():
    return [
        pltpu.VMEM((7, 32, 128), f32), pltpu.VMEM((4, 32, 128), f32),
        pltpu.SemaphoreType.DMA((17,)), pltpu.SemaphoreType.DMA((17,)),
    ]


class Gather:
    pieces = 6

    def __init__(self, peers, whole, sends, recvs):
        self.peers, self.whole, self.sends, self.recvs = peers, whole, sends, recvs
        self.quarter = peers.x * 2 + peers.core
        self.next_quarter = (1 - peers.x) * 2 + peers.core

    def rows(self, ref, quarter):
        count = ref.shape[0] // 4
        return ref.at[span(quarter * count, count), :]

    def copy(self, index, kind):
        p = self.peers
        if kind == 0:
            src = dst = self.rows(self.whole(index, p.tp), self.quarter)
            peer = p.over_tp
        elif kind == 1:
            src = dst = self.rows(self.whole(index, 1 - p.tp), self.quarter)
            peer = p.over_x
        else:
            src = dst = self.rows(self.whole(index, 1 - p.tp), self.quarter if kind == 2 else self.next_quarter)
            peer = p.over_core
        return pltpu.make_async_remote_copy(
            src_ref=src, dst_ref=dst, send_sem=self.sends.at[index, kind], recv_sem=self.recvs.at[index, kind],
            device_id=peer, device_id_type=MESH,
        )

    def start(self, indices):
        for index in indices:
            self.copy(index, 0).start()

    def onward_x(self, index):
        self.copy(index, 0).wait_recv()
        self.copy(index, 1).start()
        self.copy(index, 2).start()

    def onward_core(self, index):
        self.copy(index, 1).wait_recv()
        self.copy(index, 3).start()

    def arrive(self, index):
        self.copy(index, 2).wait_recv()
        self.copy(index, 3).wait_recv()

    def finish(self):
        for index in range(self.pieces):
            for kind in range(4):
                self.copy(index, kind).wait_send()


def square_turn(values):
    rows, lanes = values.shape
    if lanes < 128:
        values = jnp.concatenate([values, jnp.zeros((rows, 128 - lanes), f32)], axis=1)
    if rows < 128:
        values = jnp.concatenate([values, jnp.zeros((128 - rows, 128), f32)], axis=0)
    return values.T


def widen(values):
    return jnp.concatenate([values] * (TILE // 128), axis=1)


def strips():
    return [slice(16 * i, 16 * (i + 1)) for i in range(K // 16)]


def four_rows(ref, slot, first):
    return jnp.concatenate([ref[slot, pl.ds(first + i, 1), :] for i in range(TILE // 128)], axis=1)


def hot_rows(values, count):
    return (values == iota((count, TILE), 0).astype(f32)).astype(f32)


def fold_lanes(values):
    total = values[:, :128]
    for i in range(1, TILE // 128):
        total = total + values[:, 128 * i : 128 * (i + 1)]
    return total


def twice(ref, values):
    none = jnp.zeros_like(values)
    ref[...] = jnp.concatenate(
        [jnp.concatenate([values, none], axis=1), jnp.concatenate([none, values], axis=1)], axis=0
    ).astype(bf16)


def dot_halves(weights, pieces):
    values = jnp.concatenate(pieces, axis=0)
    half = TILE // 2
    both = dot_nn(weights, jnp.concatenate([values[:, :half], values[:, half:]], axis=0))
    rows = both.shape[0] // 2
    return jnp.concatenate([both[:rows], both[rows:]], axis=1)


def prepare_pairs(r):
    spr = to_column(row_of(r.spreads))
    r.cols[0] = jnp.broadcast_to(to_column(row_of(r.centers)), (K, 128))
    r.cols[1] = jnp.broadcast_to(root_half / spr, (K, 128))
    r.cols[2] = jnp.broadcast_to(-jnp.log(root_tau * spr), (K, 128))
    r.cols[3] = jnp.broadcast_to(to_column(row_of(r.first_bias)), (K, 128))
    r.cols[4] = jnp.broadcast_to(1.0 / spr, (K, 128))
    twice(r.w1, r.first_weight[...].astype(f32))
    twice(r.w1t, r.first_weight[...].astype(f32).T)
    r.w2[...] = square_turn(r.second_weight[...].astype(f32))
    table = jnp.concatenate([r.hop_table[...], r.edge_table[...], jnp.zeros((128 - HOPS - EDGES, H), f32)], axis=0)
    table = jnp.concatenate([table, jnp.zeros((128, 128 - H), f32)], axis=1).T[:H, :HOT]
    one = table.astype(bf16).astype(f32)
    r.base[...] = jnp.concatenate(
        [r.second_weight[...].astype(f32), one, table - one, jnp.zeros((H, 64), f32)], axis=1
    )


def bf16_parts(values, count):
    parts = []
    for _ in range(count):
        parts.append(values.astype(bf16))
        values = values - parts[-1].astype(f32)
    return parts


def pair_tables(r, slots):
    low = low_lanes(HALF)
    low_row = low_lanes(1)
    tables = [part.astype(f32) for ref in (r.kernel_scale, r.kernel_shift) for part in bf16_parts(ref[...], 3)]
    tables = jnp.concatenate([square_turn(part)[:ATOMS, :ATOMS] for part in tables], axis=1)
    tables = jnp.concatenate([tables, jnp.zeros((ATOMS, 128 - 6 * ATOMS), f32)], axis=1).astype(bf16)
    for group in range(slots // 2):
        lanes = slice(128 * group, 128 * (group + 1))
        atoms = r.atoms[lanes].astype(f32).reshape(1, 128)
        rows = jnp.concatenate([r.positions[:, lanes], atoms, jnp.zeros((4, 128), f32)], axis=0)
        columns = square_turn(rows)
        key_hot = (columns[:, 3:4] == iota((128, ATOMS), 1).astype(f32)).astype(f32).astype(bf16)
        picks = dot_nn(key_hot, tables).astype(bf16)
        turned = half_swap(rows)
        for s in range(2):
            slot = 2 * group + s
            tokens = slice(SLOT * s, SLOT * (s + 1))
            double = jnp.where(low_lanes(8), *((rows, turned) if s == 0 else (turned, rows)))
            total = None
            for c in range(3):
                column = columns[tokens, c : c + 1]
                offset = jnp.where(low, column[:HALF], column[HALF:]) - double[c : c + 1]
                total = offset * offset if total is None else total + offset * offset
            distance = jnp.sqrt(total)
            query_hot = (double[3:4] == iota((ATOMS, 128), 0).astype(f32)).astype(f32)
            three, none = [query_hot] * 3, [jnp.zeros((3 * ATOMS, 128), f32)]
            rest = [jnp.zeros((128 - 6 * ATOMS, 128), f32)]
            spread = jnp.concatenate(
                [jnp.concatenate(three + none + rest, axis=0), jnp.concatenate(none + three + rest, axis=0)], axis=1
            )
            both = dot_nn(picks[tokens], spread.astype(bf16))
            scale = jnp.where(low, both[:HALF, :128], both[HALF:, :128])
            shift = jnp.where(low, both[:HALF, 128:], both[HALF:, 128:])
            r.argument[slot] = scale * distance + shift
            r.distance[slot] = distance
            for source, target in ((r.hops, r.hop_rows), (r.edges, r.edge_rows)):
                values = source[:, lanes].astype(f32)
                top, bottom = values[:HALF], values[HALF:]
                if s == 0:
                    target[slot] = jnp.where(low, top, half_swap(bottom))
                else:
                    target[slot] = jnp.where(low, half_swap(top), bottom)
            r.atom_rows[slot] = jnp.broadcast_to(double[3:4], (8, 128))


def table_grads(r, slots):
    lefts, rights = [], []
    for slot in range(slots):
        query_hot = (r.atom_rows[slot, 0:1, :] == iota((ATOMS, 128), 0).astype(f32)).astype(f32)
        keys = jnp.concatenate([query_hot[:, :HALF], query_hot[:, HALF:SLOT]], axis=0)
        keys = jnp.concatenate([keys, keys], axis=1).astype(bf16)
        values = jnp.concatenate([r.dargs[slot] * r.distance[slot], r.dargs[slot]], axis=1)
        both = dot_nn(keys, jnp.concatenate(bf16_parts(values, 2), axis=0))
        low = low_lanes(ATOMS)
        for index in range(2):
            lanes = slice(128 * index, 128 * (index + 1))
            rights.append(bf16_parts(jnp.where(low, both[:ATOMS, lanes], both[ATOMS:, lanes]), 2))
        lefts.append(query_hot.astype(bf16))
    left = jnp.concatenate(lefts, axis=1)
    right = jnp.concatenate(
        [jnp.concatenate([rights[2 * s + index][part] for s in range(slots)], axis=1) for index in range(2) for part in range(2)],
        axis=0,
    )
    result = dot_nt(left, right)
    return [
        result[:, 2 * ATOMS * index : 2 * ATOMS * index + ATOMS] + result[:, 2 * ATOMS * index + ATOMS : 2 * ATOMS * (index + 1)]
        for index in range(2)
    ]


def hold(tile, value):
    return value


def staged(stages, count):
    held = {}

    def step(time):
        for k, stage in reversed(list(enumerate(stages))):
            if 0 <= time - k < count:
                held[time - k] = stage(time - k, held.get(time - k))

    return [functools.partial(step, time) for time in range(count + len(stages) - 1)]


def run_beside(*step_lists):
    for time in range(max(map(len, step_lists))):
        for steps in step_lists:
            if time < len(steps):
                steps[time]()


TILES = PAIRS // TILE
ROWS = TILE // 128


def pair_forward(r, slot, beside=()):
    bank = lax.rem(slot, 2)
    graph_on = r.flags[0, slot].astype(f32)
    space_on = r.flags[1, slot].astype(f32)
    factor = jnp.where(iota((H, 256), 1) < K, space_on, graph_on)
    r.lhs[...] = (r.base[...] * factor).astype(bf16)

    def kernels(tile, _):
        where = slice(tile * TILE, (tile + 1) * TILE)
        arg = four_rows(r.argument, slot, tile * ROWS)
        pieces = []
        for rows in strips():
            u = (arg - widen(r.cols[0, rows])) * widen(r.cols[1, rows])
            pieces.append(jnp.exp(widen(r.cols[2, rows]) - u * u).astype(bf16))
            r.left[bank, rows, where] = pieces[-1]
        return dot_halves(r.w1t[...], pieces)

    def hidden(tile, first):
        where = slice(tile * TILE, (tile + 1) * TILE)
        pieces = []
        for rows in strips():
            value, slope = gelu_pair(first[rows] + widen(r.cols[3, rows]))
            pieces.append(value)
            r.left[bank, slice(K + rows.start, K + rows.stop), where] = pieces[-1]
            r.slope[bank, rows, where] = slope
        hot = jnp.concatenate(
            [
                hot_rows(four_rows(r.hop_rows, slot, tile * ROWS), HOPS),
                hot_rows(four_rows(r.edge_rows, slot, tile * ROWS), HOT - HOPS),
            ],
            axis=0,
        ).astype(bf16)
        return dot_nn(r.lhs[:, : K + 2 * HOT], jnp.concatenate(pieces + [hot] * 2, axis=0))

    def biases(tile, bias):
        bias = bias.astype(bf16).astype(f32)
        for i in range(ROWS):
            r.bias[slot, pl.ds(tile * ROWS + i, H, stride=HALF), :] = bias[:, 128 * i : 128 * (i + 1)]

    run_beside(staged([kernels, hold, hidden, hold, biases], TILES), beside)


def pair_backward(r, slot, between):
    bank = lax.rem(slot, 2)
    graph_on = r.flags[0, slot].astype(f32)
    space_on = r.flags[1, slot].astype(f32)
    twice(r.w2_twice, r.w2[:, :H] * space_on)

    def scores(tile, _):
        where = slice(tile * TILE, (tile + 1) * TILE)
        grad = jnp.concatenate(
            [r.bias[slot, pl.ds(tile * ROWS + i, H, stride=HALF), :] for i in range(ROWS)], axis=1
        )
        r.right[K:, where] = jnp.concatenate([grad * space_on, grad * graph_on], axis=0).astype(bf16)
        edge_hot = hot_rows(four_rows(r.edge_rows, slot, tile * ROWS), HOT - HOPS)
        edge_hot = jnp.where(iota((HOT - HOPS, TILE), 0) == EDGES, 1.0, edge_hot)
        r.left[bank, 2 * K :, where] = jnp.concatenate(
            [hot_rows(four_rows(r.hop_rows, slot, tile * ROWS), HOPS), edge_hot], axis=0
        ).astype(bf16)
        return dot_halves(r.w2_twice[...], [grad.astype(bf16)])

    def hidden(tile, d_second):
        where = slice(tile * TILE, (tile + 1) * TILE)
        pieces = []
        for rows in strips():
            pieces.append((d_second[rows] * r.slope[bank, rows, where].astype(f32)).astype(bf16))
            r.right[rows, where] = pieces[-1]
        return dot_halves(r.w1[...], pieces)

    def kernels(tile, d_gauss):
        where = slice(tile * TILE, (tile + 1) * TILE)
        arg = four_rows(r.argument, slot, tile * ROWS)
        d_arg = None
        for rows in strips():
            inv = widen(r.cols[4, rows])
            u = (arg - widen(r.cols[0, rows])) * inv
            q = d_gauss[rows] * r.left[bank, rows, where].astype(f32)
            w = q * u
            r.sums[0, rows] += fold_lanes(w)
            r.sums[1, rows] += fold_lanes(w * u - q)
            w = w * inv
            w = w[:8] + w[8:]
            d_arg = w if d_arg is None else d_arg + w
        d_arg = -jnp.sum(d_arg, axis=0, keepdims=True)
        for i in range(ROWS):
            at = tile * ROWS + i
            r.dargs[slot, at : at + 1, :] = d_arg[:, 128 * i : 128 * (i + 1)]

    run_beside(staged([scores, hold, hidden, hold, kernels], TILES))
    between()
    r.acc_mixed[...] += dot_nt(r.left[bank], r.right[...])


def attend_steps(r, s, first_slot):
    low = low_lanes(HALF)
    rows = span(s * SLOT, SLOT)

    def scores(g, _):
        if g == 0:
            r.work[0] = jnp.zeros((SLOT, D), f32)
        start, width, _ = window(g)
        q = r.joined[rows, start : start + width]
        return dot_nt(r.joined[rows, D + start : D + start + width], spread_heads(q, g))

    def mix(g, products):
        start, width, _ = window(g)
        valid = iota((SLOT, GROUP * SLOT), 0) < r.lengths[first_slot + s]
        parts = []
        for pair in range(GROUP // 2):
            head = GROUP * g + 2 * pair
            one = r.bias[s, head * HALF : (head + 1) * HALF, :]
            two = r.bias[s, (head + 1) * HALF : (head + 2) * HALF, :]
            top = jnp.where(low, one, half_swap(two))
            bottom = jnp.where(low, half_swap(one), two)
            parts.append(jnp.concatenate([top, bottom], axis=0))
        values = jnp.where(valid, products * head_scale + jnp.concatenate(parts, axis=1), neg_large)
        weights = jnp.exp(values - jnp.max(values, axis=0, keepdims=True))
        prob = (weights * (1.0 / jnp.sum(weights, axis=0, keepdims=True))).astype(bf16)
        r.prob[s, :, g * GROUP * SLOT : (g + 1) * GROUP * SLOT] = prob
        return dot_tn(prob, r.joined[rows, 2 * D + start : 2 * D + start + width])

    def gather(g, mixed):
        start, width, _ = window(g)
        r.work[0, :, start : start + width] += gather_heads(mixed, g)
        if g == GROUPS - 1:
            r.attended[rows, :] = r.work[0].astype(bf16)

    return staged([scores, hold, mix, hold, gather], GROUPS)


def attend_back(r, s):
    low = low_lanes(HALF)
    rows = span(s * SLOT, SLOT)
    r.work[...] = jnp.zeros((3, SLOT, D), f32)

    def lanes_of(g):
        start, width, _ = window(g)
        return slice(start, start + width)

    def probabilities(g, _):
        lanes = lanes_of(g)
        v = r.joined[rows, 2 * D + lanes.start : 2 * D + lanes.stop]
        return dot_nt(v, spread_heads(r.d_attended[rows, lanes], g))

    def scores(g, d_prob):
        lanes = lanes_of(g)
        prob = r.prob[s, :, g * GROUP * SLOT : (g + 1) * GROUP * SLOT]
        wide = prob.astype(f32)
        inner = jnp.sum(wide * d_prob, axis=0, keepdims=True)
        d_scores = (wide * (d_prob - inner)).astype(bf16)
        d_wide = d_scores.astype(f32)
        for pair in range(GROUP // 2):
            head = GROUP * g + 2 * pair
            top = d_wide[:HALF, 128 * pair : 128 * (pair + 1)]
            bottom = d_wide[HALF:, 128 * pair : 128 * (pair + 1)]
            r.bias[s, head * HALF : (head + 1) * HALF, :] = jnp.where(low, top, half_swap(bottom))
            r.bias[s, (head + 1) * HALF : (head + 2) * HALF, :] = jnp.where(low, half_swap(top), bottom)
        return (
            dot_tn(d_scores, r.joined[rows, D + lanes.start : D + lanes.stop]),
            dot_nn(d_scores, spread_heads(r.joined[rows, lanes], g)),
            dot_nn(prob, spread_heads(r.d_attended[rows, lanes], g)),
        )

    def gather(g, products):
        lanes = lanes_of(g)
        r.work[0, :, lanes] += gather_heads(products[0], g)
        r.work[1, :, lanes] += products[1]
        r.work[2, :, lanes] += products[2]

    run_beside(staged([probabilities, hold, scores, hold, gather], GROUPS))
    r.joined[rows, 0:D] = (r.work[0] * head_scale).astype(bf16)
    r.joined[rows, D : 2 * D] = (r.work[1] * head_scale).astype(bf16)
    r.joined[rows, 2 * D : 3 * D] = r.work[2].astype(bf16)


def project(r, rows):
    scaled, _ = standardize(r.hidden[rows, :].astype(f32))
    normed = (scaled * row_of(r.attn_gain) + row_of(r.attn_shift)).astype(bf16)
    r.normed_a[rows, :] = normed
    for m in range(3):
        for t in range(2):
            at = m * D + t * HALF_D
            r.joined[rows, at : at + HALF_D] = dot_nn(normed, r.wqkv[t, m]).astype(bf16)


def feed(r, rows):
    halves = [slice(0, HALF_D), slice(HALF_D, D)]
    resid = r.hidden[rows, :].astype(f32)
    for t in range(2):
        resid = resid + dot_nn(r.attended[rows, halves[t]], r.wproj[t])
    scaled, inv_std = standardize(resid)
    normed = (scaled * row_of(r.ffn_gain) + row_of(r.ffn_shift)).astype(bf16)
    r.normed_f[rows, :] = normed
    pre = jnp.concatenate([dot_nn(normed, r.wup[t]) for t in range(2)], axis=1)
    value, slope = gelu_parts(pre + row_of(r.up_bias))
    active = value.astype(bf16)
    r.activated[rows, :] = active
    result = resid + row_of(r.down_bias)
    for t in range(2):
        result = result + dot_nn(active[:, halves[t]], r.wdown[t])
    r.out_rows[rows, :] = result.astype(bf16)
    cot = r.cotangent[rows, :]
    cot_wide = cot.astype(f32)
    d_active = jnp.concatenate([dot_nt(cot, r.wdown[t]) for t in range(2)], axis=1)
    d_hidden = (d_active * slope).astype(bf16)
    r.d_pre[rows, :] = d_hidden
    d_normed = dot_nt(d_hidden[:, halves[0]], r.wup[0]) + dot_nt(d_hidden[:, halves[1]], r.wup[1])
    d_resid = cot_wide + norm_back(d_normed, scaled, inv_std, row_of(r.ffn_gain))
    r.d_resid[rows, :] = d_resid
    branch = d_resid.astype(bf16)
    r.d_branch[rows, :] = branch
    for t in range(2):
        r.d_attended[rows, halves[t]] = dot_nt(branch, r.wproj[t]).astype(bf16)
    r.vectors[2:3, :] += column_sum(d_normed * scaled)
    r.vectors[3:4, :] += column_sum(d_normed)
    r.vectors[4:5, :] += column_sum(d_hidden.astype(f32))
    r.vectors[5:6, :] += column_sum(cot_wide)


def feed_grads(r, block):
    halves = [slice(0, HALF_D), slice(HALF_D, D)]
    if block == 0:
        grad = dot_tn(r.normed_f[...], r.d_pre[...]).astype(bf16)
        for t in range(2):
            r.fpart[t, :D, :] = grad[:, halves[t]]
        return
    left, right = (r.attended, r.d_branch) if block == 1 else (r.activated, r.cotangent)
    for t in range(2):
        grad = dot_tn(left[:, halves[t]], right[...]).astype(bf16)
        for side in range(2):
            r.fpart[t, D * block + HALF_D * side : D * block + HALF_D * (side + 1), :] = grad[:, halves[side]]


def qkv_grads(r, block):
    rows = slice(256 * block, 256 * (block + 1))
    for m in range(3):
        grad = dot_tn(r.normed_a[:, rows], r.joined[:, m * D : (m + 1) * D]).astype(bf16)
        for t in range(2):
            r.qpart[t, rows, m * HALF_D : (m + 1) * HALF_D] = grad[:, t * HALF_D : (t + 1) * HALF_D]


def finish_input(r, rows):
    d_normed = None
    for m in range(3):
        for t in range(2):
            at = m * D + t * HALF_D
            term = dot_nt(r.joined[rows, at : at + HALF_D], r.wqkv[t, m])
            d_normed = term if d_normed is None else d_normed + term
    scaled, inv_std = standardize(r.hidden[rows, :].astype(f32))
    grad = r.d_resid[rows, :] + norm_back(d_normed, scaled, inv_std, row_of(r.attn_gain))
    r.in_rows[rows, :] = grad.astype(bf16)
    r.vectors[0:1, :] += column_sum(d_normed * scaled)
    r.vectors[1:2, :] += column_sum(d_normed)


def pack_small(r, slots):
    tables = table_grads(r, slots)
    for v in range(6):
        for i in range(D // 128):
            at = VECTOR_ROWS + v * (D // 128) + i
            r.spart[at : at + 1, :] = r.vectors[v : v + 1, 128 * i : 128 * (i + 1)]
    r.spart[0:K, :] = r.acc_mixed[0:K, :K]
    r.spart[SECOND_ROWS : SECOND_ROWS + H, :] = square_turn(r.acc_mixed[K : 2 * K, K:])[:H]
    r.spart[TABLE_ROWS : TABLE_ROWS + H, :HOT] = square_turn(r.acc_mixed[2 * K :, K:])[H : 2 * H, :HOT]
    for index in range(2):
        rows = slice(TABLE_ROWS + ATOMS * index, TABLE_ROWS + ATOMS * (index + 1))
        r.spart[rows, HOT : HOT + ATOMS] = tables[index]
    ones = 2 * K + HOPS + EDGES
    r.spart[KERNEL_ROWS : KERNEL_ROWS + 1, :] = r.acc_mixed[ones : ones + 1, :K]
    for index in range(2):
        column = jnp.sum(r.sums[index] * r.cols[4], axis=1, keepdims=True)
        same = iota((K, K), 0) == iota((K, K), 1)
        at = KERNEL_ROWS + 1 + index
        r.spart[at : at + 1, :] = jnp.sum(jnp.where(same, column, 0.0), axis=0, keepdims=True)


class Stage:
    def __init__(self, names, near_inputs, carried, refs):
        self.r = SimpleNamespace(**dict(zip(names, refs)))
        r = self.r
        self.loads = {
            name: pltpu.make_async_copy(getattr(r, "given_" + name), getattr(r, name), r.input_sems.at[i])
            for i, name in enumerate(near_inputs)
        }
        self.stores = {
            name: pltpu.make_async_copy(getattr(r, name), getattr(r, name + "_far"), r.carry_sems.at[i])
            for i, name in enumerate(carried)
        }

    def load(self, *names):
        for name in names:
            self.loads[name].start()

    def need(self, *names):
        for name in names:
            self.loads[name].wait()

    def store(self, *names):
        for name in names:
            self.stores[name].start()

    def stored(self):
        for copy in self.stores.values():
            copy.wait()


def each_chunk(r, tokens, work):
    chunk = min(512, tokens)

    def one(c, _):
        work(r, span(c * chunk, chunk))
        return 0

    lax.fori_loop(0, tokens // chunk, one, 0)


def pair_moves(r, slot, back):
    bank = lax.rem(slot, 2)
    both = (r.left_far.at[slot], r.left.at[bank, : 2 * K]), (r.slope_far.at[slot], r.slope.at[bank])
    for index, (far, near) in enumerate(both):
        yield pltpu.make_async_copy(*((far, near) if back else (near, far)), r.pair_sems.at[bank, index])


def start_moves(r, slot, back):
    for copy in pair_moves(r, slot, back):
        copy.start()


def wait_moves(r, slot, back):
    for copy in pair_moves(r, slot, back):
        copy.wait()


def run(steps):
    for act, *where in steps:
        act(*where)


def at_time(index, plan):
    for k, steps in plan.items():
        pl.when(index == k)(functools.partial(run, steps))


FFN_BACK = {0: [(1, 1), (2, 1)], 3: [(0, 2)], 7: [(0, 3), (1, 2)]}
AFTER_GRADS = ([(0, 4), (1, 3), (2, 2)], [(0, 1), (1, 1), (2, 1)])
AFTER_HALF = ([(0, 5)], [])
AFTER_INPUT = ([(2, 3), (1, 4)], [(0, 2)])
FFN_PAIRS = {
    0: [(0, 6)], 2: [(2, 4)], 3: [(1, 5), (0, 7)], 5: [(2, 5)], 7: [(1, 6)], 9: [(2, 6)], 10: [(1, 7)], 12: [(2, 7)],
}
QKV_PAIRS = {
    2: [(0, 3)], 3: [(1, 2)], 6: [(1, 3), (2, 2), (0, 4)], 9: [(1, 4)], 10: [(0, 5)], 11: [(2, 3)], 12: [(1, 5)],
    13: [(0, 6)], 14: [(2, 4)], 15: [(1, 6)],
}


def layer_kernel(remote, names, near_inputs, carried, *refs):
    stage = Stage(names, near_inputs, carried, refs)
    r = stage.r
    stage.load(*[name for name in near_inputs if name not in ("hidden", "cotangent")])
    tokens = r.hidden.shape[0]
    slots = tokens // SLOT
    peers = Peers()
    if remote:
        greet(peers.everyone())
    whole = [r.wqkv, r.wup, r.wproj, r.wdown]
    given = [r.given_qkv, r.given_up, r.given_proj, r.given_down]
    targets = [w.at[peers.tp] for w in whole] if remote else whole
    loads = [
        pltpu.make_async_copy(src, dst, r.load_sems.at[i]) for i, (src, dst) in enumerate(zip(given, targets))
    ]
    for load in loads:
        load.start()
    stage.load("hidden", "cotangent")
    gather_plan = {}
    if remote:

        def whole_piece(index, tp):
            return whole[0].at[tp, index] if index < 3 else whole[index - 2].at[tp]

        gather = Gather(peers, whole_piece, r.gather_sends, r.gather_recvs)
        ffn = Reduction(peers, r.fpart, r.ftotal, r.f_core, r.f_tp, r.f_x, r.f_z, r.f_sends, r.f_recvs)
        qkv = Reduction(peers, r.qpart, r.qtotal, r.q_core, r.q_tp, r.q_x, r.q_z, r.q_sends, r.q_recvs)
        small = SmallReduction(peers, r.spart, r.stotal, r.s_near, r.s_z, r.s_sends, r.s_recvs)
        x, core = gather.onward_x, gather.onward_core
        gather_plan = {
            0: [(x, 0)], 1: [(x, 1)], 2: [(core, 0), (x, 2)], 3: [(core, 1), (x, 3), (core, 2)],
            4: [(x, 4)], 5: [(core, 3), (x, 5)], 6: [(core, 4)], 7: [(core, 5)],
        }

    def leave(which, block):
        near, far = ((r.ftotal, r.ftotal_far), (r.qtotal, r.qtotal_far))[which]
        rows = near.shape[0] // 3
        at = slice(block * rows, (block + 1) * rows)
        return pltpu.make_async_copy(near.at[at], far.at[at], r.leave_sems.at[3 * which + block])

    def advance(which, actions):
        if remote:
            for block, step in actions:
                (ffn, qkv)[which].act(block, step)
                if step == 7:
                    leave(which, block).start()

    def plan_of(*plans):
        times = sorted(set().union(*plans)) if remote else []
        return {
            k: [(advance, which, plan[k]) for which, plan in enumerate(plans) if k in plan] for k in times
        }

    stage.need(*[name for name in near_inputs if name not in ("hidden", "cotangent")])
    prepare_pairs(r)
    pair_tables(r, slots)
    if remote:
        await_greetings(peers.everyone())
        for load, indices in zip(loads, ((0, 1, 2), (3,), (4,), (5,))):
            load.wait()
            gather.start(indices)

    first_slot = peers.tp * slots
    alone = (5 * slots + 7) // 8

    def pairs(slot, _):
        pl.when(slot >= 2)(lambda: wait_moves(r, slot - 2, False))
        pair_forward(r, slot)
        start_moves(r, slot, False)
        at_time(slot, gather_plan)
        return 0

    def pairs_and_attention(slot, _):
        pl.when(slot >= 2)(lambda: wait_moves(r, slot - 2, False))
        pair_forward(r, slot, attend_steps(r, slot - alone, first_slot))
        start_moves(r, slot, False)
        at_time(slot, gather_plan)
        return 0

    def attend_one(s, _):
        run_beside(attend_steps(r, s, first_slot))
        return 0

    lax.fori_loop(0, alone, pairs, 0)
    stage.need("hidden")
    if remote:
        for index in range(3):
            gather.arrive(index)
    else:
        for load in loads:
            load.wait()
    each_chunk(r, tokens, project)
    lax.fori_loop(alone, slots, pairs_and_attention, 0)
    lax.fori_loop(slots - alone, slots, attend_one, 0)
    stage.need("cotangent")
    if remote:
        for index in range(3, 6):
            gather.arrive(index)
    r.vectors[...] = jnp.zeros_like(r.vectors)
    each_chunk(r, tokens, feed)
    stage.store("out_rows")
    for slot in (slots - 2, slots - 1):
        wait_moves(r, slot, False)
    start_moves(r, 0, True)
    start_moves(r, 1, True)
    for block in range(3):
        feed_grads(r, block)
        advance(0, [(block, 0)])
    advance(0, [(0, 1)])

    back_plan, pair_plan = plan_of(FFN_BACK), plan_of(FFN_PAIRS, QKV_PAIRS)

    def back_one(s, _):
        attend_back(r, s)
        at_time(s, back_plan)
        return 0

    lax.fori_loop(0, slots, back_one, 0)
    for block in range(3):
        qkv_grads(r, block)
        advance(1, [(block, 0)])
    for which in range(2):
        advance(which, AFTER_GRADS[which])
    each_chunk(r, tokens, finish_input)
    stage.store("in_rows")
    for which in range(2):
        advance(which, AFTER_HALF[which] + AFTER_INPUT[which])
    for ref in (r.sums, r.acc_mixed, r.spart):
        ref[...] = jnp.zeros_like(ref)

    def pairs_back(slot, _):
        wait_moves(r, slot, True)
        pair_backward(r, slot, lambda: at_time(2 * slot, pair_plan))
        pl.when(slot + 2 < slots)(lambda: start_moves(r, slot + 2, True))
        at_time(2 * slot + 1, pair_plan)
        return 0

    lax.fori_loop(0, slots, pairs_back, 0)
    pack_small(r, slots)
    if remote:
        small.act(0)
        advance(1, [(2, 5), (0, 7)])
        small.act(1)
        advance(1, [(1, 7)])
        advance(1, [(2, 6)])
        small.act(2)
        advance(1, [(2, 7)])
        small.act(3)
        rows = pltpu.make_async_copy(r.stotal, r.stotal_far, r.leave_sems.at[6])
        rows.start()
        for which in range(2):
            advance(which, [(b, 8) for b in range(3)])
        small.act(4)
        gather.finish()
        for which in range(2):
            for block in range(3):
                leave(which, block).wait()
        rows.wait()
    else:
        stage.store("fpart", "qpart", "spart")
    stage.stored()


def call_stage(kernel, name, remote, collective, arrays, scalars, far, outs, carried, scratch):
    vm, sem = pltpu.VMEM, pltpu.SemaphoreType.DMA
    near = {n: vm(a.shape, a.dtype) for n, a in arrays.items() if n not in scalars + far}
    in_names = [n if n in scalars or n.endswith("_far") else "given_" + n for n in arrays]
    results = outs | {n + "_far": item for n, item in carried.items()}
    scratch = near | {n: vm(*item) for n, item in carried.items()} | scratch
    scratch |= {"input_sems": sem((len(near),)), "carry_sems": sem((len(carried),))}
    names = in_names + list(results) + list(scratch)
    values = pl.pallas_call(
        functools.partial(kernel, remote, names, list(near), list(carried)),
        in_specs=[pl.BlockSpec(memory_space=pltpu.SMEM if n in scalars else pl.ANY) for n in arrays],
        out_specs=[pl.BlockSpec(memory_space=pl.ANY)] * len(results),
        out_shape=[jax.ShapeDtypeStruct(*item) for item in results.values()],
        scratch_shapes=list(scratch.values()),
        compiler_params=pltpu.CompilerParams(
            vmem_limit_bytes=VMEM_BYTES, **(dict(collective_id=collective, has_side_effects=True) if remote else {})
        ),
        name=name,
    )(*arrays.values())
    return dict(zip(results, values))


def layer(remote, arrays):
    tokens = arrays["hidden"].shape[0]
    slots = tokens // SLOT
    v, sem = pltpu.VMEM, pltpu.SemaphoreType.DMA
    of_tokens = (tokens, D)
    table = (slots, HALF, 128)
    fshape, qshape, sshape = (3 * D, HALF_D), (D, 3 * HALF_D), (SMALL_ROWS, 128)
    outs = {"left_far": ((slots, 2 * K, PAIRS), bf16), "slope_far": ((slots, K, PAIRS), bf16)}
    carried = {"out_rows": (of_tokens, bf16), "in_rows": (of_tokens, bf16)}
    scratch = {
        "wqkv": v((2, 3, D, HALF_D), bf16), "wup": v((2, D, HALF_D), bf16), "wproj": v((2, HALF_D, D), bf16),
        "wdown": v((2, HALF_D, D), bf16), "load_sems": sem((4,)), "pair_sems": sem((2, 2)),
        "left": v((2, 2 * K + HOT, PAIRS), bf16), "slope": v((2, K, PAIRS), bf16),
        "right": v((K + 2 * H, PAIRS), bf16), "cols": v((5, K, 128), f32), "w1": v((2 * K, 2 * K), bf16), "w1t": v((2 * K, 2 * K), bf16),
        "w2": v((K, 128), f32), "w2_twice": v((2 * K, 2 * H), bf16), "base": v((H, 256), f32), "lhs": v((H, 256), bf16),
        "argument": v(table, f32), "distance": v(table, f32), "hop_rows": v(table, f32), "edge_rows": v(table, f32),
        "atom_rows": v((slots, 8, 128), f32), "dargs": v(table, f32), "bias": v((slots, H * HALF, 128), f32),
        "work": v((3, SLOT, D), f32), "normed_a": v(of_tokens, bf16), "joined": v((tokens, 3 * D), bf16),
        "prob": v((slots, SLOT, H * SLOT), bf16), "attended": v(of_tokens, bf16), "normed_f": v(of_tokens, bf16),
        "activated": v(of_tokens, bf16), "d_pre": v(of_tokens, bf16), "d_branch": v(of_tokens, bf16),
        "d_attended": v(of_tokens, bf16), "d_resid": v(of_tokens, f32), "vectors": v((8, D), f32),
        "sums": v((2, K, 128), f32), "acc_mixed": v((2 * K + HOT, K + 2 * H), f32),
    }
    parts = {"fpart": ((2,) + fshape, bf16), "qpart": ((2,) + qshape, bf16), "spart": (sshape, f32)}
    totals = {"ftotal": (fshape, bf16), "qtotal": (qshape, bf16), "stotal": (sshape, f32)}
    if remote:
        outs |= {n + "_far": item for n, item in totals.items()}
        scratch |= {n: v(*item) for n, item in (parts | totals).items()}
        scratch |= {"leave_sems": sem((7,)), "gather_sends": sem((6, 4)), "gather_recvs": sem((6, 4))}
        for name, shape in (("f", (D, HALF_D)), ("q", (D // 3, 3 * HALF_D))):
            keys = ("_core", "_tp", "_x", "_z", "_sends", "_recvs")
            scratch |= {name + key: item for key, item in zip(keys, big_scratch(*shape))}
        scratch |= dict(zip(("s_near", "s_z", "s_sends", "s_recvs"), small_scratch()))
    else:
        carried |= parts
    results = call_stage(
        layer_kernel, "layer", remote, 0, arrays, ("lengths", "flags"), ("qkv", "up", "proj", "down"), outs, carried,
        scratch,
    )
    sums = [results[n + "_far"] for n in (totals if remote else parts)]
    return results["out_rows_far"], results["in_rows_far"], sums


RESULTS = (
    "output", "grad_input", "attn_gain", "attn_shift", "qkv", "proj", "ffn_gain", "ffn_shift", "up", "up_bias", "down",
    "down_bias", "scale", "shift", "centers", "spreads", "first", "first_bias", "second", "hop", "edge",
)


def unpack_kernel(*refs):
    given = SimpleNamespace(**dict(zip(("out_rows", "in_rows", "fsum", "qsum", "rows"), refs)))
    far = SimpleNamespace(**dict(zip(RESULTS, refs[5:])))
    count = len(RESULTS)
    near = SimpleNamespace(**dict(zip(RESULTS, refs[5 + count : 5 + 2 * count])))
    fsum, qsum, rows, load_sems, store_sems = refs[5 + 2 * count :]
    moves = [(given.rows, rows)]
    sources = ((given.qsum, qsum, 3), (given.fsum, fsum, 9), (given.out_rows, near.output, 1), (given.in_rows, near.grad_input, 1))
    for src, dst, pieces in sources:
        height = src.shape[0] // pieces
        for i in range(pieces):
            at = slice(i * height, (i + 1) * height)
            moves.append((src.at[at], dst.at[at]))
    loads = [pltpu.make_async_copy(src, dst, load_sems.at[i]) for i, (src, dst) in enumerate(moves)]
    for load in loads:
        load.start()
    stores = []

    def store(src, dst):
        stores.append(pltpu.make_async_copy(src, dst, store_sems.at[len(stores)]))
        stores[-1].start()

    for i in range(3):
        loads[1 + i].wait()
        at = slice(256 * i, 256 * (i + 1))
        for m in range(3):
            near.qkv[m, at] = qsum[at, m * HALF_D : (m + 1) * HALF_D].astype(f32)
        store(near.qkv.at[:, at], far.qkv.at[:, at])
    for i in range(3):
        loads[4 + i].wait()
        at = slice(256 * i, 256 * (i + 1))
        near.up[at, :] = fsum[at, :].astype(f32)
        store(near.up.at[at], far.up.at[at])
    for block, name in ((1, "proj"), (2, "down")):
        for i in range(3):
            loads[4 + 3 * block + i].wait()
        ref = getattr(near, name)
        at = D * block
        ref[:, :HALF_D] = fsum[at : at + HALF_D, :].astype(f32)
        ref[:, HALF_D:] = fsum[at + HALF_D : at + D, :].astype(f32)
        store(ref, getattr(far, name))
    loads[13].wait()
    store(near.output, far.output)
    loads[14].wait()
    store(near.grad_input, far.grad_input)
    loads[0].wait()
    names = ("attn_gain", "attn_shift", "ffn_gain", "ffn_shift", "up_bias", "down_bias")
    for v, name in enumerate(names):
        for i in range(D // 128):
            getattr(near, name)[pl.ds(128 * i, 128)] = rows[VECTOR_ROWS + v * (D // 128) + i, :]
    near.first[...] = rows[0:K, :]
    near.second[...] = rows[SECOND_ROWS : SECOND_ROWS + H, :]
    table = rows[TABLE_ROWS : TABLE_ROWS + H, :]
    near.scale[...] = table[:ATOMS, HOT : HOT + ATOMS]
    near.shift[...] = table[ATOMS:, HOT : HOT + ATOMS]
    turned = square_turn(table)
    near.hop[...] = turned[:HOPS, :H]
    near.edge[...] = turned[HOPS : HOPS + EDGES, :H]
    lines = ("first_bias", "centers", "spreads")
    for i, name in enumerate(lines):
        getattr(near, name)[...] = rows[KERNEL_ROWS + i, :]
    for name in names + ("first", "second", "scale", "shift", "hop", "edge") + lines:
        store(getattr(near, name), getattr(far, name))
    for copy in stores:
        copy.wait()


def unpack(out_rows, in_rows, fsum, qsum, rows):
    tokens = out_rows.shape[0]
    vec, line, types = ((D,), f32), ((K,), f32), ((ATOMS, ATOMS), f32)
    shapes = (
        ((tokens, D), bf16), ((tokens, D), bf16), vec, vec, ((3, D, HALF_D), f32), ((HALF_D, D), f32), vec, vec,
        ((D, HALF_D), f32), vec, ((HALF_D, D), f32), vec, types, types, line, line, ((K, K), f32), line, ((H, K), f32),
        ((HOPS, H), f32), ((EDGES, H), f32),
    )
    anywhere = pl.BlockSpec(memory_space=pl.ANY)
    return pl.pallas_call(
        unpack_kernel,
        in_specs=[anywhere] * 5,
        out_specs=[anywhere] * len(shapes),
        out_shape=[jax.ShapeDtypeStruct(*item) for item in shapes],
        scratch_shapes=[pltpu.VMEM(*item) for item in shapes] + [
            pltpu.VMEM(fsum.shape, bf16), pltpu.VMEM(qsum.shape, bf16), pltpu.VMEM(rows.shape, f32),
            pltpu.SemaphoreType.DMA((15,)), pltpu.SemaphoreType.DMA((25,)),
        ],
        compiler_params=pltpu.CompilerParams(vmem_limit_bytes=VMEM_BYTES),
        name="unpack",
    )(out_rows, in_rows, fsum, qsum, rows)


def whole_weights(qkv_weight, up_weight, proj_weight, down_weight):
    columns = lambda w: jnp.stack(jnp.split(w, 2, axis=-1))
    rows = lambda w: jnp.stack(jnp.split(w, 2, axis=0))
    gather = lambda w, dim: lax.all_gather(w, "tp", axis=dim, tiled=True)
    return (
        columns(gather(qkv_weight.transpose(1, 0, 2), 2)), columns(gather(up_weight, 1)),
        rows(gather(proj_weight, 0)), rows(gather(down_weight, 0)),
    )


def sum_grads(fgrads, qgrads, small):
    total_f, total_q, rows = lax.psum((fgrads, qgrads, small), ("mol", "tp"))
    share = D // lax.axis_size("tp")
    at = lax.axis_index("tp") * share

    def columns(halves):
        return lax.dynamic_slice_in_dim(jnp.concatenate(list(halves), axis=-1), at, share, halves.ndim - 2)

    def rows_of(block):
        part = total_f[:, D * block : D * (block + 1)]
        sides = jnp.concatenate([part[:, :HALF_D], part[:, HALF_D:]], axis=2).reshape(D, D)
        return lax.dynamic_slice_in_dim(sides, at, share, 0)

    qkv = columns(total_q.reshape(2, D, 3, HALF_D)).transpose(1, 0, 2)
    return [v.astype(f32) for v in (qkv, columns(total_f[:, :D]), rows_of(1), rows_of(2))], rows


def body(
    mesh_shape,
    hidden_in, positions, atom_types, hop_counts, edge_types, lengths, branches,
    attn_gain, attn_shift, qkv_weight, proj_weight, ffn_gain, ffn_shift, up_weight, up_bias, down_weight, down_bias,
    kernel_scale, kernel_shift, centers, spreads, first_weight, first_bias, second_weight, hop_table, edge_table,
    cotangent,
):
    remote = mesh_shape["tp"] == 2 and mesh_shape["mol"] == 16 and branches.shape[0] == 8
    if remote:
        weights = (qkv_weight.transpose(1, 0, 2), up_weight, proj_weight, down_weight)
    else:
        weights = whole_weights(qkv_weight, up_weight, proj_weight, down_weight)
    arrays = dict(
        lengths=lengths, flags=branches.T, positions=positions, atoms=atom_types, hops=hop_counts.T,
        edges=edge_types.T, kernel_scale=kernel_scale, kernel_shift=kernel_shift, centers=centers, spreads=spreads,
        first_weight=first_weight, first_bias=first_bias, second_weight=second_weight.T, hop_table=hop_table,
        edge_table=edge_table, attn_gain=attn_gain, attn_shift=attn_shift, ffn_gain=ffn_gain, ffn_shift=ffn_shift,
        up_bias=up_bias, down_bias=down_bias, hidden=hidden_in, cotangent=cotangent,
        qkv=weights[0], up=weights[1], proj=weights[2], down=weights[3],
    )
    output, grad_input, sums = layer(remote, arrays)
    if remote:
        fsum, qsum, rows = sums
    else:
        big, rows = sum_grads(*sums)
        fsum, qsum = jnp.zeros((3 * D, HALF_D), bf16), jnp.zeros((D, 3 * HALF_D), bf16)
    output, grad_input, *grads = unpack(output, grad_input, fsum, qsum, rows)
    if not remote:
        grads[2], grads[6], grads[3], grads[8] = big
    grads[2] = grads[2].transpose(1, 0, 2)
    grads[16] = grads[16].T
    return (output, grad_input, *grads)


def solution(mesh):
    rows = P(("mol", "tp"), None)
    all_of = P()
    in_specs = (
        rows, P(None, ("mol", "tp")), P(("mol", "tp")), rows, rows, P("mol"), rows, all_of, all_of,
        P(None, None, "tp"), P("tp", None), all_of, all_of, P(None, "tp"), all_of, P("tp", None),
    ) + (all_of,) * 10 + (rows,)
    out_specs = (
        rows, rows, all_of, all_of, P(None, None, "tp"), P("tp", None), all_of, all_of, P(None, "tp"), all_of,
        P("tp", None),
    ) + (all_of,) * 10
    step = functools.partial(body, dict(mesh.shape))
    return jax.shard_map(step, mesh=mesh, in_specs=in_specs, out_specs=out_specs, check_vma=False)
```

```python
import functools
from types import SimpleNamespace

import jax
import jax.numpy as jnp
from jax import lax
from jax.experimental import pallas as pl
from jax.experimental.pallas import tpu as pltpu
from jax.sharding import PartitionSpec as P

D = 768
H = 32
HD = 24
FF = 768
K = 128
SLOT = 64
HALF = SLOT // 2
HALF_D = D // 2
PAIRS = SLOT * SLOT
HOPS = 16
EDGES = 8
ATOMS = 16
GROUP = 4
GROUPS = H // GROUP
HOT = 32

highest = lax.Precision.HIGHEST
neg_large = -1e30
root_tau = 2.5066282746310002
root_half = 0.7071067811865476
inv_root_tau = 0.3989422804014327
head_scale = HD ** (-0.5)
VMEM_BYTES = 62 * 1024 * 1024
TILE = 512

SECOND_ROWS = K
TABLE_ROWS = SECOND_ROWS + H
KERNEL_ROWS = TABLE_ROWS + H
VECTOR_ROWS = KERNEL_ROWS + 8
SMALL_ROWS = 256

MESH = pl.DeviceIdType.MESH
f32 = jnp.float32
bf16 = jnp.bfloat16


def dot_nn(left, right, precision=None):
    return lax.dot_general(left, right, (((1,), (0,)), ((), ())), precision=precision, preferred_element_type=f32)


def dot_nt(left, right, precision=None):
    return lax.dot_general(left, right, (((1,), (1,)), ((), ())), precision=precision, preferred_element_type=f32)


def dot_tn(left, right, precision=None):
    return lax.dot_general(left, right, (((0,), (0,)), ((), ())), precision=precision, preferred_element_type=f32)


def iota(shape, dim):
    return lax.broadcasted_iota(jnp.int32, shape, dim)


def gelu_parts(values):
    size = jnp.abs(values)
    bell = jnp.exp(values * values * -0.5)
    denominator = 1.0 + (0.3275911 * root_half) * size
    t = pl.reciprocal(denominator, approx=True)
    series = 0.5 * 1.061405429
    for factor in (-1.453152027, 1.421413741, -0.284496736, 0.254829592):
        series = series * t + 0.5 * factor
    tail = series * t * bell
    gelu = jnp.maximum(values, 0.0) - size * tail
    outer = tail - size * (bell * inv_root_tau)
    return gelu, jnp.where(values >= 0.0, 1.0 - outer, outer)


def gelu_pair(values):
    size = jnp.abs(values)
    bell = jnp.exp(values * values * -0.5)
    t = pl.reciprocal(1.0 + (0.3275911 * root_half) * size, approx=True)
    series = 0.5 * 1.061405429
    for factor in (-1.453152027, 1.421413741, -0.284496736, 0.254829592):
        series = series * t + 0.5 * factor
    tail = (series * t * bell).astype(bf16)
    density = (bell * inv_root_tau).astype(bf16)
    values = values.astype(bf16)
    size = jnp.abs(values)
    outer = tail - size * density
    one, zero = jnp.ones((), bf16), jnp.zeros((), bf16)
    return jnp.maximum(values, zero) - size * tail, jnp.where(values >= zero, one - outer, outer)


def to_column(row):
    size = row.shape[1]
    same = iota((size, size), 0) == iota((size, size), 1)
    return jnp.sum(jnp.where(same, row, 0.0), axis=1, keepdims=True)


def half_swap(values):
    return pltpu.roll(values, 64, 1)


def low_lanes(rows):
    return iota((rows, 128), 1) < 64


def vmem(count):
    return [pl.BlockSpec(memory_space=pltpu.VMEM)] * count


def row_of(ref):
    return ref[...].reshape(1, ref.shape[0])


def place():
    mol = lax.axis_index("mol")
    return mol % 2, (mol // 2) % 2, mol // 4, lax.axis_index("tp")


def greet(peers):
    for peer in peers:
        pl.semaphore_signal(pltpu.get_barrier_semaphore(), inc=1, device_id=peer, device_id_type=MESH)


def await_greetings(peers):
    pl.semaphore_wait(pltpu.get_barrier_semaphore(), len(peers))


def window(group):
    first = GROUP * HD * group
    start = first // 128 * 128
    width = 128 if first - start + GROUP * HD <= 128 else 256
    return start, width, first - start


def head_masks(group, kind):
    _, width, offset = window(group)
    lane = iota((1, width), 1)
    return [
        ((lane >= offset + HD * h) & (lane < offset + HD * (h + 1))).astype(f32).astype(kind) for h in range(GROUP)
    ]


def spread_heads(values, group):
    return jnp.concatenate([values * mask for mask in head_masks(group, bf16)], axis=0)


def gather_heads(values, group):
    masks = head_masks(group, f32)
    total = values[:SLOT] * masks[0]
    for h in range(1, GROUP):
        total = total + values[SLOT * h : SLOT * (h + 1)] * masks[h]
    return total


def standardize(values):
    centred = values - jnp.mean(values, axis=-1, keepdims=True)
    inv_std = lax.rsqrt(jnp.mean(centred * centred, axis=-1, keepdims=True) + 1e-05)
    return centred * inv_std, inv_std


def norm_back(d_normed, scaled, inv_std, gain):
    weighted = d_normed * gain
    inner_a = jnp.mean(weighted, axis=-1, keepdims=True)
    inner_b = jnp.mean(weighted * scaled, axis=-1, keepdims=True)
    return inv_std * (weighted - inner_a - scaled * inner_b)


def column_sum(values):
    return jnp.sum(values, axis=0, keepdims=True)


class Peers:
    def __init__(self):
        self.core, self.x, self.z, self.tp = place()
        mol = lax.axis_index("mol")
        self.over_core = {"mol": mol + 1 - 2 * self.core}
        self.over_x = {"mol": mol + 2 - 4 * self.x}
        self.over_tp = {"tp": 1 - self.tp}
        self.turn = [lax.rem(self.z + d, 4) for d in range(4)]
        self.over_z = [{"mol": self.turn[d] * 4 + self.x * 2 + self.core} for d in range(4)]

    def neighbour(self, k):
        core = self.core + (1 - 2 * self.core) * (k & 1)
        x = self.x + (1 - 2 * self.x) * (k >> 1 & 1)
        tp = self.tp + (1 - 2 * self.tp) * (k >> 2)
        return core * 4 + tp * 2 + x, {"mol": self.z * 4 + x * 2 + core, "tp": tp}

    def everyone(self):
        return [self.neighbour(k)[1] for k in range(1, 8)] + self.over_z[1:]


def span(start, size):
    return pl.ds(pl.multiple_of(start, size), size)


def add_rows(target, source, rows):
    step = 96 if rows % 96 == 0 else min(rows, 32)

    def piece(i, _):
        at = pl.ds(pl.multiple_of(i * step, step), step)
        target[at, :] = target[at, :] + source[at, :]
        return 0

    lax.fori_loop(0, rows // step, piece, 0)


class Reduction:
    kinds = 11

    def __init__(self, peers, part, total, from_core, from_tp, from_x, from_z, sends, recvs):
        self.peers, self.part, self.total = peers, part, total
        self.from_core, self.from_tp, self.from_x, self.from_z = from_core, from_tp, from_x, from_z
        self.sends, self.recvs = sends, recvs
        self.half = from_core.shape[2]
        self.quarter, self.least = self.half // 2, self.half // 8

    def rows(self, b, level):
        p = self.peers
        at = b * 2 * self.half + p.core * self.half
        if level > 0:
            at = at + p.x * self.quarter
        return at + p.z * self.least if level > 1 else at

    def copy(self, b, kind):
        p = self.peers
        part, total = self.part, self.total
        half, quarter, least = self.half, self.quarter, self.least
        if kind == 0:
            src = part.at[:, span(b * 2 * half + (1 - p.core) * half, half)]
            dst, peer = self.from_core.at[b], p.over_core
        elif kind == 1:
            src, dst, peer = part.at[1 - p.tp, span(self.rows(b, 0), half)], self.from_tp.at[b], p.over_tp
        elif kind == 2:
            src = part.at[p.tp, span(self.rows(b, 0) + (1 - p.x) * quarter, quarter)]
            dst, peer = self.from_x.at[b], p.over_x
        elif kind < 6:
            d = kind - 2
            src = part.at[p.tp, span(self.rows(b, 1) + p.turn[d] * least, least)]
            dst, peer = self.from_z.at[b, d - 1], p.over_z[d]
        elif kind < 9:
            src = dst = total.at[span(self.rows(b, 2), least)]
            peer = p.over_z[kind - 5]
        elif kind == 9:
            src = dst = total.at[span(self.rows(b, 1), quarter)]
            peer = p.over_x
        else:
            src = dst = total.at[span(self.rows(b, 0), half)]
            peer = p.over_core
        return pltpu.make_async_remote_copy(
            src_ref=src, dst_ref=dst, send_sem=self.sends.at[b, kind], recv_sem=self.recvs.at[b, kind],
            device_id=peer, device_id_type=MESH,
        )

    def act(self, b, stage):
        p = self.peers
        half, quarter, least = self.half, self.quarter, self.least
        part = self.part
        if stage == 0:
            self.copy(b, 0).start()
        elif stage == 1:
            self.copy(b, 0).wait_recv()
            at = span(self.rows(b, 0), half)
            add_rows(part.at[1 - p.tp, at], self.from_core.at[b, 1 - p.tp], half)
            self.copy(b, 1).start()
            add_rows(part.at[p.tp, at], self.from_core.at[b, p.tp], half)
        elif stage == 2:
            self.copy(b, 1).wait_recv()
            away, mine = (1 - p.x) * quarter, p.x * quarter
            at = self.rows(b, 0)
            add_rows(part.at[p.tp, span(at + away, quarter)], self.from_tp.at[b, span(away, quarter)], quarter)
            self.copy(b, 2).start()
            add_rows(part.at[p.tp, span(at + mine, quarter)], self.from_tp.at[b, span(mine, quarter)], quarter)
        elif stage == 3:
            self.copy(b, 2).wait_recv()
            add_rows(part.at[p.tp, span(self.rows(b, 1), quarter)], self.from_x.at[b], quarter)
            for kind in (3, 4, 5):
                self.copy(b, kind).start()
        elif stage == 4:
            for kind in (3, 4, 5):
                self.copy(b, kind).wait_recv()
            mine = span(self.rows(b, 2), least)
            value = part[p.tp, mine, :].astype(f32)
            for d in range(3):
                value = value + self.from_z[b, d].astype(f32)
            self.total[mine, :] = value.astype(bf16)
            for kind in (6, 7, 8):
                self.copy(b, kind).start()
        elif stage == 5:
            for kind in (6, 7, 8):
                self.copy(b, kind).wait_recv()
            self.copy(b, 9).start()
        elif stage == 6:
            self.copy(b, 9).wait_recv()
            self.copy(b, 10).start()
        elif stage == 7:
            self.copy(b, 10).wait_recv()
        else:
            for kind in range(self.kinds):
                self.copy(b, kind).wait_send()


class SmallReduction:
    def __init__(self, peers, part, total, from_near, from_z, sends, recvs):
        self.peers, self.part, self.total, self.from_near, self.from_z = peers, part, total, from_near, from_z
        self.sends, self.recvs = sends, recvs
        p = peers
        self.near = [p.neighbour(k) for k in range(8)]
        self.mine = span(self.near[0][0] * 32, 32)

    def copy(self, kind):
        p = self.peers
        if kind < 7:
            index, peer = self.near[kind + 1]
            src, dst = self.part.at[span(index * 32, 32)], self.from_near.at[kind]
        elif kind < 10:
            src = dst = self.from_z.at[p.z]
            peer = p.over_z[kind - 6]
        else:
            src = dst = self.total.at[self.mine]
            peer = self.near[kind - 9][1]
        return pltpu.make_async_remote_copy(
            src_ref=src, dst_ref=dst, send_sem=self.sends.at[kind], recv_sem=self.recvs.at[kind],
            device_id=peer, device_id_type=MESH,
        )

    def act(self, stage):
        hops = (range(0, 7), range(7, 10), range(10, 17))
        if stage == 4:
            for kind in range(17):
                self.copy(kind).wait_send()
            return
        if stage > 0:
            for kind in hops[stage - 1]:
                self.copy(kind).wait_recv()
        if stage == 1:
            value = self.part[self.mine, :]
            for k in range(7):
                value = value + self.from_near[k]
            self.from_z[self.peers.z] = value
        elif stage == 2:
            self.total[self.mine, :] = (self.from_z[0] + self.from_z[1]) + (self.from_z[2] + self.from_z[3])
        if stage < 3:
            for kind in hops[stage]:
                self.copy(kind).start()


def big_scratch(rows, lanes):
    half = rows // 2
    sems = pltpu.SemaphoreType.DMA((3, Reduction.kinds))
    return [
        pltpu.VMEM((3, 2, half, lanes), bf16), pltpu.VMEM((3, half, lanes), bf16),
        pltpu.VMEM((3, half // 2, lanes), bf16), pltpu.VMEM((3, 3, half // 8, lanes), bf16), sems, sems,
    ]


def small_scratch():
    return [
        pltpu.VMEM((7, 32, 128), f32), pltpu.VMEM((4, 32, 128), f32),
        pltpu.SemaphoreType.DMA((17,)), pltpu.SemaphoreType.DMA((17,)),
    ]


class Gather:
    pieces = 6

    def __init__(self, peers, whole, sends, recvs):
        self.peers, self.whole, self.sends, self.recvs = peers, whole, sends, recvs
        self.quarter = peers.x * 2 + peers.core
        self.next_quarter = (1 - peers.x) * 2 + peers.core

    def rows(self, ref, quarter):
        count = ref.shape[0] // 4
        return ref.at[span(quarter * count, count), :]

    def copy(self, index, kind):
        p = self.peers
        if kind == 0:
            src = dst = self.rows(self.whole(index, p.tp), self.quarter)
            peer = p.over_tp
        elif kind == 1:
            src = dst = self.rows(self.whole(index, 1 - p.tp), self.quarter)
            peer = p.over_x
        else:
            src = dst = self.rows(self.whole(index, 1 - p.tp), self.quarter if kind == 2 else self.next_quarter)
            peer = p.over_core
        return pltpu.make_async_remote_copy(
            src_ref=src, dst_ref=dst, send_sem=self.sends.at[index, kind], recv_sem=self.recvs.at[index, kind],
            device_id=peer, device_id_type=MESH,
        )

    def start(self, indices):
        for index in indices:
            self.copy(index, 0).start()

    def onward_x(self, index):
        self.copy(index, 0).wait_recv()
        self.copy(index, 1).start()
        self.copy(index, 2).start()

    def onward_core(self, index):
        self.copy(index, 1).wait_recv()
        self.copy(index, 3).start()

    def arrive(self, index):
        self.copy(index, 2).wait_recv()
        self.copy(index, 3).wait_recv()

    def finish(self):
        for index in range(self.pieces):
            for kind in range(4):
                self.copy(index, kind).wait_send()


def square_turn(values):
    rows, lanes = values.shape
    if lanes < 128:
        values = jnp.concatenate([values, jnp.zeros((rows, 128 - lanes), f32)], axis=1)
    if rows < 128:
        values = jnp.concatenate([values, jnp.zeros((128 - rows, 128), f32)], axis=0)
    return values.T


def widen(values):
    return jnp.concatenate([values] * (TILE // 128), axis=1)


def strips():
    return [slice(16 * i, 16 * (i + 1)) for i in range(K // 16)]


def four_rows(ref, slot, first):
    return jnp.concatenate([ref[slot, pl.ds(first + i, 1), :] for i in range(TILE // 128)], axis=1)


def hot_rows(values, count):
    return (values == iota((count, TILE), 0).astype(f32)).astype(f32)


def fold_lanes(values):
    total = values[:, :128]
    for i in range(1, TILE // 128):
        total = total + values[:, 128 * i : 128 * (i + 1)]
    return total


def twice(ref, values):
    none = jnp.zeros_like(values)
    ref[...] = jnp.concatenate(
        [jnp.concatenate([values, none], axis=1), jnp.concatenate([none, values], axis=1)], axis=0
    ).astype(bf16)


def dot_halves(weights, pieces):
    values = jnp.concatenate(pieces, axis=0)
    half = TILE // 2
    both = dot_nn(weights, jnp.concatenate([values[:, :half], values[:, half:]], axis=0))
    rows = both.shape[0] // 2
    return jnp.concatenate([both[:rows], both[rows:]], axis=1)


def prepare_pairs(r):
    spr = to_column(row_of(r.spreads))
    r.cols[0] = jnp.broadcast_to(to_column(row_of(r.centers)), (K, 128))
    r.cols[1] = jnp.broadcast_to(root_half / spr, (K, 128))
    r.cols[2] = jnp.broadcast_to(-jnp.log(root_tau * spr), (K, 128))
    r.cols[3] = jnp.broadcast_to(to_column(row_of(r.first_bias)), (K, 128))
    r.cols[4] = jnp.broadcast_to(1.0 / spr, (K, 128))
    twice(r.w1, r.first_weight[...].astype(f32))
    twice(r.w1t, r.first_weight[...].astype(f32).T)
    r.w2[...] = square_turn(r.second_weight[...].astype(f32))
    table = jnp.concatenate([r.hop_table[...], r.edge_table[...], jnp.zeros((128 - HOPS - EDGES, H), f32)], axis=0)
    table = jnp.concatenate([table, jnp.zeros((128, 128 - H), f32)], axis=1).T[:H, :HOT]
    one = table.astype(bf16).astype(f32)
    r.base[...] = jnp.concatenate(
        [r.second_weight[...].astype(f32), one, table - one, jnp.zeros((H, 64), f32)], axis=1
    )


def bf16_parts(values, count):
    parts = []
    for _ in range(count):
        parts.append(values.astype(bf16))
        values = values - parts[-1].astype(f32)
    return parts


def pair_tables(r, slots):
    low = low_lanes(HALF)
    low_row = low_lanes(1)
    tables = [part.astype(f32) for ref in (r.kernel_scale, r.kernel_shift) for part in bf16_parts(ref[...], 3)]
    tables = jnp.concatenate([square_turn(part)[:ATOMS, :ATOMS] for part in tables], axis=1)
    tables = jnp.concatenate([tables, jnp.zeros((ATOMS, 128 - 6 * ATOMS), f32)], axis=1).astype(bf16)
    for group in range(slots // 2):
        lanes = slice(128 * group, 128 * (group + 1))
        atoms = r.atoms[lanes].astype(f32).reshape(1, 128)
        rows = jnp.concatenate([r.positions[:, lanes], atoms, jnp.zeros((4, 128), f32)], axis=0)
        columns = square_turn(rows)
        key_hot = (columns[:, 3:4] == iota((128, ATOMS), 1).astype(f32)).astype(f32).astype(bf16)
        picks = dot_nn(key_hot, tables).astype(bf16)
        turned = half_swap(rows)
        for s in range(2):
            slot = 2 * group + s
            tokens = slice(SLOT * s, SLOT * (s + 1))
            double = jnp.where(low_lanes(8), *((rows, turned) if s == 0 else (turned, rows)))
            total = None
            for c in range(3):
                column = columns[tokens, c : c + 1]
                offset = jnp.where(low, column[:HALF], column[HALF:]) - double[c : c + 1]
                total = offset * offset if total is None else total + offset * offset
            distance = jnp.sqrt(total)
            query_hot = (double[3:4] == iota((ATOMS, 128), 0).astype(f32)).astype(f32)
            three, none = [query_hot] * 3, [jnp.zeros((3 * ATOMS, 128), f32)]
            rest = [jnp.zeros((128 - 6 * ATOMS, 128), f32)]
            spread = jnp.concatenate(
                [jnp.concatenate(three + none + rest, axis=0), jnp.concatenate(none + three + rest, axis=0)], axis=1
            )
            both = dot_nn(picks[tokens], spread.astype(bf16))
            scale = jnp.where(low, both[:HALF, :128], both[HALF:, :128])
            shift = jnp.where(low, both[:HALF, 128:], both[HALF:, 128:])
            r.argument[slot] = scale * distance + shift
            r.distance[slot] = distance
            for source, target in ((r.hops, r.hop_rows), (r.edges, r.edge_rows)):
                values = source[:, lanes].astype(f32)
                top, bottom = values[:HALF], values[HALF:]
                if s == 0:
                    target[slot] = jnp.where(low, top, half_swap(bottom))
                else:
                    target[slot] = jnp.where(low, half_swap(top), bottom)
            r.atom_rows[slot] = jnp.broadcast_to(double[3:4], (8, 128))


def table_grads(r, slots):
    lefts, rights = [], []
    for slot in range(slots):
        query_hot = (r.atom_rows[slot, 0:1, :] == iota((ATOMS, 128), 0).astype(f32)).astype(f32)
        keys = jnp.concatenate([query_hot[:, :HALF], query_hot[:, HALF:SLOT]], axis=0)
        keys = jnp.concatenate([keys, keys], axis=1).astype(bf16)
        values = jnp.concatenate([r.dargs[slot] * r.distance[slot], r.dargs[slot]], axis=1)
        both = dot_nn(keys, jnp.concatenate(bf16_parts(values, 2), axis=0))
        low = low_lanes(ATOMS)
        for index in range(2):
            lanes = slice(128 * index, 128 * (index + 1))
            rights.append(bf16_parts(jnp.where(low, both[:ATOMS, lanes], both[ATOMS:, lanes]), 2))
        lefts.append(query_hot.astype(bf16))
    left = jnp.concatenate(lefts, axis=1)
    right = jnp.concatenate(
        [jnp.concatenate([rights[2 * s + index][part] for s in range(slots)], axis=1) for index in range(2) for part in range(2)],
        axis=0,
    )
    result = dot_nt(left, right)
    return [
        result[:, 2 * ATOMS * index : 2 * ATOMS * index + ATOMS] + result[:, 2 * ATOMS * index + ATOMS : 2 * ATOMS * (index + 1)]
        for index in range(2)
    ]


def hold(tile, value):
    return value


def staged(stages, count):
    held = {}

    def step(time):
        for k, stage in reversed(list(enumerate(stages))):
            if 0 <= time - k < count:
                held[time - k] = stage(time - k, held.get(time - k))

    return [functools.partial(step, time) for time in range(count + len(stages) - 1)]


def run_beside(*step_lists):
    for time in range(max(map(len, step_lists))):
        for steps in step_lists:
            if time < len(steps):
                steps[time]()


TILES = PAIRS // TILE
ROWS = TILE // 128


def pair_forward(r, slot, beside=()):
    bank = lax.rem(slot, 2)
    graph_on = r.flags[0, slot].astype(f32)
    space_on = r.flags[1, slot].astype(f32)
    factor = jnp.where(iota((H, 256), 1) < K, space_on, graph_on)
    r.lhs[...] = (r.base[...] * factor).astype(bf16)

    def kernels(tile, _):
        where = slice(tile * TILE, (tile + 1) * TILE)
        arg = four_rows(r.argument, slot, tile * ROWS)
        pieces = []
        for rows in strips():
            u = (arg - widen(r.cols[0, rows])) * widen(r.cols[1, rows])
            pieces.append(jnp.exp(widen(r.cols[2, rows]) - u * u).astype(bf16))
            r.left[bank, rows, where] = pieces[-1]
        return dot_halves(r.w1t[...], pieces)

    def hidden(tile, first):
        where = slice(tile * TILE, (tile + 1) * TILE)
        pieces = []
        for rows in strips():
            value, slope = gelu_pair(first[rows] + widen(r.cols[3, rows]))
            pieces.append(value)
            r.left[bank, slice(K + rows.start, K + rows.stop), where] = pieces[-1]
            r.slope[bank, rows, where] = slope
        hot = jnp.concatenate(
            [
                hot_rows(four_rows(r.hop_rows, slot, tile * ROWS), HOPS),
                hot_rows(four_rows(r.edge_rows, slot, tile * ROWS), HOT - HOPS),
            ],
            axis=0,
        ).astype(bf16)
        return dot_nn(r.lhs[:, : K + 2 * HOT], jnp.concatenate(pieces + [hot] * 2, axis=0))

    def biases(tile, bias):
        bias = bias.astype(bf16).astype(f32)
        for i in range(ROWS):
            r.bias[slot, pl.ds(tile * ROWS + i, H, stride=HALF), :] = bias[:, 128 * i : 128 * (i + 1)]

    run_beside(staged([kernels, hold, hidden, hold, biases], TILES), beside)


def pair_backward(r, slot):
    bank = lax.rem(slot, 2)
    graph_on = r.flags[0, slot].astype(f32)
    space_on = r.flags[1, slot].astype(f32)
    twice(r.w2_twice, r.w2[:, :H] * space_on)

    def scores(tile, _):
        where = slice(tile * TILE, (tile + 1) * TILE)
        grad = jnp.concatenate(
            [r.bias[slot, pl.ds(tile * ROWS + i, H, stride=HALF), :] for i in range(ROWS)], axis=1
        )
        r.right[K:, where] = jnp.concatenate([grad * space_on, grad * graph_on], axis=0).astype(bf16)
        edge_hot = hot_rows(four_rows(r.edge_rows, slot, tile * ROWS), HOT - HOPS)
        edge_hot = jnp.where(iota((HOT - HOPS, TILE), 0) == EDGES, 1.0, edge_hot)
        r.left[bank, 2 * K :, where] = jnp.concatenate(
            [hot_rows(four_rows(r.hop_rows, slot, tile * ROWS), HOPS), edge_hot], axis=0
        ).astype(bf16)
        return dot_halves(r.w2_twice[...], [grad.astype(bf16)])

    def hidden(tile, d_second):
        where = slice(tile * TILE, (tile + 1) * TILE)
        pieces = []
        for rows in strips():
            pieces.append((d_second[rows] * r.slope[bank, rows, where].astype(f32)).astype(bf16))
            r.right[rows, where] = pieces[-1]
        return dot_halves(r.w1[...], pieces)

    def kernels(tile, d_gauss):
        where = slice(tile * TILE, (tile + 1) * TILE)
        arg = four_rows(r.argument, slot, tile * ROWS)
        d_arg = None
        for rows in strips():
            inv = widen(r.cols[4, rows])
            u = (arg - widen(r.cols[0, rows])) * inv
            q = d_gauss[rows] * r.left[bank, rows, where].astype(f32)
            w = q * u
            r.sums[0, rows] += fold_lanes(w)
            r.sums[1, rows] += fold_lanes(w * u - q)
            w = w * inv
            w = w[:8] + w[8:]
            d_arg = w if d_arg is None else d_arg + w
        d_arg = -jnp.sum(d_arg, axis=0, keepdims=True)
        for i in range(ROWS):
            at = tile * ROWS + i
            r.dargs[slot, at : at + 1, :] = d_arg[:, 128 * i : 128 * (i + 1)]

    def products(tile, _):
        if tile % 2 == 1:
            where = slice((tile - 1) * TILE, (tile + 1) * TILE)
            return dot_nt(r.left[bank, :, where], r.right[:, where])

    def add_products(tile, values):
        if tile % 2 == 1:
            r.acc_mixed[...] += values

    run_beside(staged([scores, hold, hidden, hold, kernels, products, hold, add_products], TILES))


def attend_steps(r, s, first_slot):
    low = low_lanes(HALF)
    rows = span(s * SLOT, SLOT)

    def scores(g, _):
        if g == 0:
            r.work[0] = jnp.zeros((SLOT, D), f32)
        start, width, _ = window(g)
        q = r.joined[rows, start : start + width]
        return dot_nt(r.joined[rows, D + start : D + start + width], spread_heads(q, g))

    def mix(g, products):
        start, width, _ = window(g)
        valid = iota((SLOT, GROUP * SLOT), 0) < r.lengths[first_slot + s]
        parts = []
        for pair in range(GROUP // 2):
            head = GROUP * g + 2 * pair
            one = r.bias[s, head * HALF : (head + 1) * HALF, :]
            two = r.bias[s, (head + 1) * HALF : (head + 2) * HALF, :]
            top = jnp.where(low, one, half_swap(two))
            bottom = jnp.where(low, half_swap(one), two)
            parts.append(jnp.concatenate([top, bottom], axis=0))
        values = jnp.where(valid, products * head_scale + jnp.concatenate(parts, axis=1), neg_large)
        weights = jnp.exp(values - jnp.max(values, axis=0, keepdims=True))
        prob = (weights * (1.0 / jnp.sum(weights, axis=0, keepdims=True))).astype(bf16)
        r.prob[s, :, g * GROUP * SLOT : (g + 1) * GROUP * SLOT] = prob
        return dot_tn(prob, r.joined[rows, 2 * D + start : 2 * D + start + width])

    def gather(g, mixed):
        start, width, _ = window(g)
        r.work[0, :, start : start + width] += gather_heads(mixed, g)
        if g == GROUPS - 1:
            r.attended[rows, :] = r.work[0].astype(bf16)

    return staged([scores, hold, mix, hold, gather], GROUPS)


def attend_back(r, s):
    low = low_lanes(HALF)
    rows = span(s * SLOT, SLOT)
    r.work[...] = jnp.zeros((3, SLOT, D), f32)

    def lanes_of(g):
        start, width, _ = window(g)
        return slice(start, start + width)

    def probabilities(g, _):
        lanes = lanes_of(g)
        v = r.joined[rows, 2 * D + lanes.start : 2 * D + lanes.stop]
        return dot_nt(v, spread_heads(r.d_attended[rows, lanes], g))

    def scores(g, d_prob):
        lanes = lanes_of(g)
        prob = r.prob[s, :, g * GROUP * SLOT : (g + 1) * GROUP * SLOT]
        wide = prob.astype(f32)
        inner = jnp.sum(wide * d_prob, axis=0, keepdims=True)
        d_scores = (wide * (d_prob - inner)).astype(bf16)
        d_wide = d_scores.astype(f32)
        for pair in range(GROUP // 2):
            head = GROUP * g + 2 * pair
            top = d_wide[:HALF, 128 * pair : 128 * (pair + 1)]
            bottom = d_wide[HALF:, 128 * pair : 128 * (pair + 1)]
            r.bias[s, head * HALF : (head + 1) * HALF, :] = jnp.where(low, top, half_swap(bottom))
            r.bias[s, (head + 1) * HALF : (head + 2) * HALF, :] = jnp.where(low, half_swap(top), bottom)
        return (
            dot_tn(d_scores, r.joined[rows, D + lanes.start : D + lanes.stop]),
            dot_nn(d_scores, spread_heads(r.joined[rows, lanes], g)),
            dot_nn(prob, spread_heads(r.d_attended[rows, lanes], g)),
        )

    def gather(g, products):
        lanes = lanes_of(g)
        r.work[0, :, lanes] += gather_heads(products[0], g)
        r.work[1, :, lanes] += products[1]
        r.work[2, :, lanes] += products[2]

    run_beside(staged([probabilities, hold, scores, hold, gather], GROUPS))
    r.joined[rows, 0:D] = (r.work[0] * head_scale).astype(bf16)
    r.joined[rows, D : 2 * D] = (r.work[1] * head_scale).astype(bf16)
    r.joined[rows, 2 * D : 3 * D] = r.work[2].astype(bf16)


def project(r, rows):
    scaled, _ = standardize(r.hidden[rows, :].astype(f32))
    normed = (scaled * row_of(r.attn_gain) + row_of(r.attn_shift)).astype(bf16)
    r.normed_a[rows, :] = normed
    for m in range(3):
        for t in range(2):
            at = m * D + t * HALF_D
            r.joined[rows, at : at + HALF_D] = dot_nn(normed, r.wqkv[t, m]).astype(bf16)


def feed(r, rows):
    halves = [slice(0, HALF_D), slice(HALF_D, D)]
    resid = r.hidden[rows, :].astype(f32)
    for t in range(2):
        resid = resid + dot_nn(r.attended[rows, halves[t]], r.wproj[t])
    scaled, inv_std = standardize(resid)
    normed = (scaled * row_of(r.ffn_gain) + row_of(r.ffn_shift)).astype(bf16)
    r.normed_f[rows, :] = normed
    pre = jnp.concatenate([dot_nn(normed, r.wup[t]) for t in range(2)], axis=1)
    value, slope = gelu_parts(pre + row_of(r.up_bias))
    active = value.astype(bf16)
    r.activated[rows, :] = active
    result = resid + row_of(r.down_bias)
    for t in range(2):
        result = result + dot_nn(active[:, halves[t]], r.wdown[t])
    r.out_rows[rows, :] = result.astype(bf16)
    cot = r.cotangent[rows, :]
    cot_wide = cot.astype(f32)
    d_active = jnp.concatenate([dot_nt(cot, r.wdown[t]) for t in range(2)], axis=1)
    d_hidden = (d_active * slope).astype(bf16)
    r.d_pre[rows, :] = d_hidden
    d_normed = dot_nt(d_hidden[:, halves[0]], r.wup[0]) + dot_nt(d_hidden[:, halves[1]], r.wup[1])
    d_resid = cot_wide + norm_back(d_normed, scaled, inv_std, row_of(r.ffn_gain))
    r.d_resid[rows, :] = d_resid
    branch = d_resid.astype(bf16)
    r.d_branch[rows, :] = branch
    for t in range(2):
        r.d_attended[rows, halves[t]] = dot_nt(branch, r.wproj[t]).astype(bf16)
    r.vectors[2:3, :] += column_sum(d_normed * scaled)
    r.vectors[3:4, :] += column_sum(d_normed)
    r.vectors[4:5, :] += column_sum(d_hidden.astype(f32))
    r.vectors[5:6, :] += column_sum(cot_wide)


def feed_grads(r, block):
    halves = [slice(0, HALF_D), slice(HALF_D, D)]
    if block == 0:
        grad = dot_tn(r.normed_f[...], r.d_pre[...]).astype(bf16)
        for t in range(2):
            r.fpart[t, :D, :] = grad[:, halves[t]]
        return
    left, right = (r.attended, r.d_branch) if block == 1 else (r.activated, r.cotangent)
    for t in range(2):
        grad = dot_tn(left[:, halves[t]], right[...]).astype(bf16)
        for side in range(2):
            r.fpart[t, D * block + HALF_D * side : D * block + HALF_D * (side + 1), :] = grad[:, halves[side]]


def qkv_grads(r, block):
    rows = slice(256 * block, 256 * (block + 1))
    for m in range(3):
        grad = dot_tn(r.normed_a[:, rows], r.joined[:, m * D : (m + 1) * D]).astype(bf16)
        for t in range(2):
            r.qpart[t, rows, m * HALF_D : (m + 1) * HALF_D] = grad[:, t * HALF_D : (t + 1) * HALF_D]


def finish_input(r, rows):
    d_normed = None
    for m in range(3):
        for t in range(2):
            at = m * D + t * HALF_D
            term = dot_nt(r.joined[rows, at : at + HALF_D], r.wqkv[t, m])
            d_normed = term if d_normed is None else d_normed + term
    scaled, inv_std = standardize(r.hidden[rows, :].astype(f32))
    grad = r.d_resid[rows, :] + norm_back(d_normed, scaled, inv_std, row_of(r.attn_gain))
    r.in_rows[rows, :] = grad.astype(bf16)
    r.vectors[0:1, :] += column_sum(d_normed * scaled)
    r.vectors[1:2, :] += column_sum(d_normed)


def pack_small(r, slots):
    tables = table_grads(r, slots)
    for v in range(6):
        for i in range(D // 128):
            at = VECTOR_ROWS + v * (D // 128) + i
            r.spart[at : at + 1, :] = r.vectors[v : v + 1, 128 * i : 128 * (i + 1)]
    r.spart[0:K, :] = r.acc_mixed[0:K, :K]
    r.spart[SECOND_ROWS : SECOND_ROWS + H, :] = square_turn(r.acc_mixed[K : 2 * K, K:])[:H]
    r.spart[TABLE_ROWS : TABLE_ROWS + H, :HOT] = square_turn(r.acc_mixed[2 * K :, K:])[H : 2 * H, :HOT]
    for index in range(2):
        rows = slice(TABLE_ROWS + ATOMS * index, TABLE_ROWS + ATOMS * (index + 1))
        r.spart[rows, HOT : HOT + ATOMS] = tables[index]
    ones = 2 * K + HOPS + EDGES
    r.spart[KERNEL_ROWS : KERNEL_ROWS + 1, :] = r.acc_mixed[ones : ones + 1, :K]
    for index in range(2):
        column = jnp.sum(r.sums[index] * r.cols[4], axis=1, keepdims=True)
        same = iota((K, K), 0) == iota((K, K), 1)
        at = KERNEL_ROWS + 1 + index
        r.spart[at : at + 1, :] = jnp.sum(jnp.where(same, column, 0.0), axis=0, keepdims=True)


class Stage:
    def __init__(self, names, near_inputs, carried, refs):
        self.r = SimpleNamespace(**dict(zip(names, refs)))
        r = self.r
        self.loads = {
            name: pltpu.make_async_copy(getattr(r, "given_" + name), getattr(r, name), r.input_sems.at[i])
            for i, name in enumerate(near_inputs)
        }
        self.stores = {
            name: pltpu.make_async_copy(getattr(r, name), getattr(r, name + "_far"), r.carry_sems.at[i])
            for i, name in enumerate(carried)
        }

    def load(self, *names):
        for name in names:
            self.loads[name].start()

    def need(self, *names):
        for name in names:
            self.loads[name].wait()

    def store(self, *names):
        for name in names:
            self.stores[name].start()

    def stored(self):
        for copy in self.stores.values():
            copy.wait()


def each_chunk(r, tokens, work):
    chunk = min(512, tokens)

    def one(c, _):
        work(r, span(c * chunk, chunk))
        return 0

    lax.fori_loop(0, tokens // chunk, one, 0)


def pair_moves(r, slot, back):
    bank = lax.rem(slot, 2)
    both = (r.left_far.at[slot], r.left.at[bank, : 2 * K]), (r.slope_far.at[slot], r.slope.at[bank])
    for index, (far, near) in enumerate(both):
        yield pltpu.make_async_copy(*((far, near) if back else (near, far)), r.pair_sems.at[bank, index])


def start_moves(r, slot, back):
    for copy in pair_moves(r, slot, back):
        copy.start()


def wait_moves(r, slot, back):
    for copy in pair_moves(r, slot, back):
        copy.wait()


def run(steps):
    for act, *where in steps:
        act(*where)


def at_time(index, plan):
    for k, steps in plan.items():
        pl.when(index == k)(functools.partial(run, steps))


FFN_BACK = {0: [(1, 1), (2, 1)], 3: [(0, 2)], 7: [(0, 3), (1, 2)]}
AFTER_GRADS = ([(0, 4), (1, 3), (2, 2)], [(0, 1), (1, 1), (2, 1)])
AFTER_HALF = ([(0, 5)], [])
AFTER_INPUT = ([(2, 3), (1, 4)], [(0, 2)])
FFN_PAIRS = {
    0: [(0, 6)], 2: [(2, 4)], 3: [(1, 5), (0, 7)], 5: [(2, 5)], 7: [(1, 6)], 9: [(2, 6)], 10: [(1, 7)], 12: [(2, 7)],
}
QKV_PAIRS = {
    2: [(0, 3)], 3: [(1, 2)], 6: [(1, 3), (2, 2), (0, 4)], 9: [(1, 4)], 10: [(0, 5)], 11: [(2, 3)], 12: [(1, 5)],
    13: [(0, 6)], 14: [(2, 4)], 15: [(1, 6)],
}


def layer_kernel(remote, names, near_inputs, carried, *refs):
    stage = Stage(names, near_inputs, carried, refs)
    r = stage.r
    stage.load(*[name for name in near_inputs if name not in ("hidden", "cotangent")])
    tokens = r.hidden.shape[0]
    slots = tokens // SLOT
    peers = Peers()
    if remote:
        greet(peers.everyone())
    whole = [r.wqkv, r.wup, r.wproj, r.wdown]
    given = [r.given_qkv, r.given_up, r.given_proj, r.given_down]
    targets = [w.at[peers.tp] for w in whole] if remote else whole
    loads = [
        pltpu.make_async_copy(src, dst, r.load_sems.at[i]) for i, (src, dst) in enumerate(zip(given, targets))
    ]
    for load in loads:
        load.start()
    stage.load("hidden", "cotangent")
    gather_plan = {}
    if remote:

        def whole_piece(index, tp):
            return whole[0].at[tp, index] if index < 3 else whole[index - 2].at[tp]

        gather = Gather(peers, whole_piece, r.gather_sends, r.gather_recvs)
        ffn = Reduction(peers, r.fpart, r.ftotal, r.f_core, r.f_tp, r.f_x, r.f_z, r.f_sends, r.f_recvs)
        qkv = Reduction(peers, r.qpart, r.qtotal, r.q_core, r.q_tp, r.q_x, r.q_z, r.q_sends, r.q_recvs)
        small = SmallReduction(peers, r.spart, r.stotal, r.s_near, r.s_z, r.s_sends, r.s_recvs)
        x, core = gather.onward_x, gather.onward_core
        gather_plan = {
            0: [(x, 0)], 1: [(x, 1)], 2: [(core, 0), (x, 2)], 3: [(core, 1), (x, 3), (core, 2)],
            4: [(x, 4)], 5: [(core, 3), (x, 5)], 6: [(core, 4)], 7: [(core, 5)],
        }

    def leave(which, block):
        near, far = ((r.ftotal, r.ftotal_far), (r.qtotal, r.qtotal_far))[which]
        rows = near.shape[0] // 3
        at = slice(block * rows, (block + 1) * rows)
        return pltpu.make_async_copy(near.at[at], far.at[at], r.leave_sems.at[3 * which + block])

    def advance(which, actions):
        if remote:
            for block, step in actions:
                (ffn, qkv)[which].act(block, step)
                if step == 7:
                    leave(which, block).start()

    def plan_of(*plans):
        times = sorted(set().union(*plans)) if remote else []
        return {
            k: [(advance, which, plan[k]) for which, plan in enumerate(plans) if k in plan] for k in times
        }

    stage.need(*[name for name in near_inputs if name not in ("hidden", "cotangent")])
    prepare_pairs(r)
    pair_tables(r, slots)
    if remote:
        await_greetings(peers.everyone())
        for load, indices in zip(loads, ((0, 1, 2), (3,), (4,), (5,))):
            load.wait()
            gather.start(indices)

    first_slot = peers.tp * slots
    alone = (5 * slots + 7) // 8

    def pairs(slot, _):
        pl.when(slot >= 2)(lambda: wait_moves(r, slot - 2, False))
        pair_forward(r, slot)
        start_moves(r, slot, False)
        at_time(slot, gather_plan)
        return 0

    def pairs_and_attention(slot, _):
        pl.when(slot >= 2)(lambda: wait_moves(r, slot - 2, False))
        pair_forward(r, slot, attend_steps(r, slot - alone, first_slot))
        start_moves(r, slot, False)
        at_time(slot, gather_plan)
        return 0

    def attend_one(s, _):
        run_beside(attend_steps(r, s, first_slot))
        return 0

    lax.fori_loop(0, alone, pairs, 0)
    stage.need("hidden")
    if remote:
        for index in range(3):
            gather.arrive(index)
    else:
        for load in loads:
            load.wait()
    each_chunk(r, tokens, project)
    lax.fori_loop(alone, slots, pairs_and_attention, 0)
    lax.fori_loop(slots - alone, slots, attend_one, 0)
    stage.need("cotangent")
    if remote:
        for index in range(3, 6):
            gather.arrive(index)
    r.vectors[...] = jnp.zeros_like(r.vectors)
    each_chunk(r, tokens, feed)
    stage.store("out_rows")
    for slot in (slots - 2, slots - 1):
        wait_moves(r, slot, False)
    start_moves(r, 0, True)
    start_moves(r, 1, True)
    for block in range(3):
        feed_grads(r, block)
        advance(0, [(block, 0)])
    advance(0, [(0, 1)])

    back_plan, pair_plan = plan_of(FFN_BACK), plan_of(FFN_PAIRS, QKV_PAIRS)

    def back_one(s, _):
        attend_back(r, s)
        at_time(s, back_plan)
        return 0

    lax.fori_loop(0, slots, back_one, 0)
    for block in range(3):
        qkv_grads(r, block)
        advance(1, [(block, 0)])
    for which in range(2):
        advance(which, AFTER_GRADS[which])
    each_chunk(r, tokens, finish_input)
    stage.store("in_rows")
    for which in range(2):
        advance(which, AFTER_HALF[which] + AFTER_INPUT[which])
    for ref in (r.sums, r.acc_mixed, r.spart):
        ref[...] = jnp.zeros_like(ref)

    def pairs_back(slot, _):
        wait_moves(r, slot, True)
        pair_backward(r, slot)
        at_time(2 * slot, pair_plan)
        pl.when(slot + 2 < slots)(lambda: start_moves(r, slot + 2, True))
        at_time(2 * slot + 1, pair_plan)
        return 0

    lax.fori_loop(0, slots, pairs_back, 0)
    pack_small(r, slots)
    if remote:
        small.act(0)
        advance(1, [(2, 5), (0, 7)])
        small.act(1)
        advance(1, [(1, 7)])
        advance(1, [(2, 6)])
        small.act(2)
        advance(1, [(2, 7)])
        small.act(3)
        rows = pltpu.make_async_copy(r.stotal, r.stotal_far, r.leave_sems.at[6])
        rows.start()
        for which in range(2):
            advance(which, [(b, 8) for b in range(3)])
        small.act(4)
        gather.finish()
        for which in range(2):
            for block in range(3):
                leave(which, block).wait()
        rows.wait()
    else:
        stage.store("fpart", "qpart", "spart")
    stage.stored()


def call_stage(kernel, name, remote, collective, arrays, scalars, far, outs, carried, scratch):
    vm, sem = pltpu.VMEM, pltpu.SemaphoreType.DMA
    near = {n: vm(a.shape, a.dtype) for n, a in arrays.items() if n not in scalars + far}
    in_names = [n if n in scalars or n.endswith("_far") else "given_" + n for n in arrays]
    results = outs | {n + "_far": item for n, item in carried.items()}
    scratch = near | {n: vm(*item) for n, item in carried.items()} | scratch
    scratch |= {"input_sems": sem((len(near),)), "carry_sems": sem((len(carried),))}
    names = in_names + list(results) + list(scratch)
    values = pl.pallas_call(
        functools.partial(kernel, remote, names, list(near), list(carried)),
        in_specs=[pl.BlockSpec(memory_space=pltpu.SMEM if n in scalars else pl.ANY) for n in arrays],
        out_specs=[pl.BlockSpec(memory_space=pl.ANY)] * len(results),
        out_shape=[jax.ShapeDtypeStruct(*item) for item in results.values()],
        scratch_shapes=list(scratch.values()),
        compiler_params=pltpu.CompilerParams(
            vmem_limit_bytes=VMEM_BYTES, **(dict(collective_id=collective, has_side_effects=True) if remote else {})
        ),
        name=name,
    )(*arrays.values())
    return dict(zip(results, values))


def layer(remote, arrays):
    tokens = arrays["hidden"].shape[0]
    slots = tokens // SLOT
    v, sem = pltpu.VMEM, pltpu.SemaphoreType.DMA
    of_tokens = (tokens, D)
    table = (slots, HALF, 128)
    fshape, qshape, sshape = (3 * D, HALF_D), (D, 3 * HALF_D), (SMALL_ROWS, 128)
    outs = {"left_far": ((slots, 2 * K, PAIRS), bf16), "slope_far": ((slots, K, PAIRS), bf16)}
    carried = {"out_rows": (of_tokens, bf16), "in_rows": (of_tokens, bf16)}
    scratch = {
        "wqkv": v((2, 3, D, HALF_D), bf16), "wup": v((2, D, HALF_D), bf16), "wproj": v((2, HALF_D, D), bf16),
        "wdown": v((2, HALF_D, D), bf16), "load_sems": sem((4,)), "pair_sems": sem((2, 2)),
        "left": v((2, 2 * K + HOT, PAIRS), bf16), "slope": v((2, K, PAIRS), bf16),
        "right": v((K + 2 * H, PAIRS), bf16), "cols": v((5, K, 128), f32), "w1": v((2 * K, 2 * K), bf16), "w1t": v((2 * K, 2 * K), bf16),
        "w2": v((K, 128), f32), "w2_twice": v((2 * K, 2 * H), bf16), "base": v((H, 256), f32), "lhs": v((H, 256), bf16),
        "argument": v(table, f32), "distance": v(table, f32), "hop_rows": v(table, f32), "edge_rows": v(table, f32),
        "atom_rows": v((slots, 8, 128), f32), "dargs": v(table, f32), "bias": v((slots, H * HALF, 128), f32),
        "work": v((3, SLOT, D), f32), "normed_a": v(of_tokens, bf16), "joined": v((tokens, 3 * D), bf16),
        "prob": v((slots, SLOT, H * SLOT), bf16), "attended": v(of_tokens, bf16), "normed_f": v(of_tokens, bf16),
        "activated": v(of_tokens, bf16), "d_pre": v(of_tokens, bf16), "d_branch": v(of_tokens, bf16),
        "d_attended": v(of_tokens, bf16), "d_resid": v(of_tokens, f32), "vectors": v((8, D), f32),
        "sums": v((2, K, 128), f32), "acc_mixed": v((2 * K + HOT, K + 2 * H), f32),
    }
    parts = {"fpart": ((2,) + fshape, bf16), "qpart": ((2,) + qshape, bf16), "spart": (sshape, f32)}
    totals = {"ftotal": (fshape, bf16), "qtotal": (qshape, bf16), "stotal": (sshape, f32)}
    if remote:
        outs |= {n + "_far": item for n, item in totals.items()}
        scratch |= {n: v(*item) for n, item in (parts | totals).items()}
        scratch |= {"leave_sems": sem((7,)), "gather_sends": sem((6, 4)), "gather_recvs": sem((6, 4))}
        for name, shape in (("f", (D, HALF_D)), ("q", (D // 3, 3 * HALF_D))):
            keys = ("_core", "_tp", "_x", "_z", "_sends", "_recvs")
            scratch |= {name + key: item for key, item in zip(keys, big_scratch(*shape))}
        scratch |= dict(zip(("s_near", "s_z", "s_sends", "s_recvs"), small_scratch()))
    else:
        carried |= parts
    results = call_stage(
        layer_kernel, "layer", remote, 0, arrays, ("lengths", "flags"), ("qkv", "up", "proj", "down"), outs, carried,
        scratch,
    )
    sums = [results[n + "_far"] for n in (totals if remote else parts)]
    return results["out_rows_far"], results["in_rows_far"], sums


RESULTS = (
    "output", "grad_input", "attn_gain", "attn_shift", "qkv", "proj", "ffn_gain", "ffn_shift", "up", "up_bias", "down",
    "down_bias", "scale", "shift", "centers", "spreads", "first", "first_bias", "second", "hop", "edge",
)


def unpack_kernel(*refs):
    given = SimpleNamespace(**dict(zip(("out_rows", "in_rows", "fsum", "qsum", "rows"), refs)))
    far = SimpleNamespace(**dict(zip(RESULTS, refs[5:])))
    count = len(RESULTS)
    near = SimpleNamespace(**dict(zip(RESULTS, refs[5 + count : 5 + 2 * count])))
    fsum, qsum, rows, load_sems, store_sems = refs[5 + 2 * count :]
    moves = [(given.rows, rows)]
    sources = ((given.qsum, qsum, 3), (given.fsum, fsum, 9), (given.out_rows, near.output, 1), (given.in_rows, near.grad_input, 1))
    for src, dst, pieces in sources:
        height = src.shape[0] // pieces
        for i in range(pieces):
            at = slice(i * height, (i + 1) * height)
            moves.append((src.at[at], dst.at[at]))
    loads = [pltpu.make_async_copy(src, dst, load_sems.at[i]) for i, (src, dst) in enumerate(moves)]
    for load in loads:
        load.start()
    stores = []

    def store(src, dst):
        stores.append(pltpu.make_async_copy(src, dst, store_sems.at[len(stores)]))
        stores[-1].start()

    for i in range(3):
        loads[1 + i].wait()
        at = slice(256 * i, 256 * (i + 1))
        for m in range(3):
            near.qkv[m, at] = qsum[at, m * HALF_D : (m + 1) * HALF_D].astype(f32)
        store(near.qkv.at[:, at], far.qkv.at[:, at])
    for i in range(3):
        loads[4 + i].wait()
        at = slice(256 * i, 256 * (i + 1))
        near.up[at, :] = fsum[at, :].astype(f32)
        store(near.up.at[at], far.up.at[at])
    for block, name in ((1, "proj"), (2, "down")):
        for i in range(3):
            loads[4 + 3 * block + i].wait()
        ref = getattr(near, name)
        at = D * block
        ref[:, :HALF_D] = fsum[at : at + HALF_D, :].astype(f32)
        ref[:, HALF_D:] = fsum[at + HALF_D : at + D, :].astype(f32)
        store(ref, getattr(far, name))
    loads[13].wait()
    store(near.output, far.output)
    loads[14].wait()
    store(near.grad_input, far.grad_input)
    loads[0].wait()
    names = ("attn_gain", "attn_shift", "ffn_gain", "ffn_shift", "up_bias", "down_bias")
    for v, name in enumerate(names):
        for i in range(D // 128):
            getattr(near, name)[pl.ds(128 * i, 128)] = rows[VECTOR_ROWS + v * (D // 128) + i, :]
    near.first[...] = rows[0:K, :]
    near.second[...] = rows[SECOND_ROWS : SECOND_ROWS + H, :]
    table = rows[TABLE_ROWS : TABLE_ROWS + H, :]
    near.scale[...] = table[:ATOMS, HOT : HOT + ATOMS]
    near.shift[...] = table[ATOMS:, HOT : HOT + ATOMS]
    turned = square_turn(table)
    near.hop[...] = turned[:HOPS, :H]
    near.edge[...] = turned[HOPS : HOPS + EDGES, :H]
    lines = ("first_bias", "centers", "spreads")
    for i, name in enumerate(lines):
        getattr(near, name)[...] = rows[KERNEL_ROWS + i, :]
    for name in names + ("first", "second", "scale", "shift", "hop", "edge") + lines:
        store(getattr(near, name), getattr(far, name))
    for copy in stores:
        copy.wait()


def unpack(out_rows, in_rows, fsum, qsum, rows):
    tokens = out_rows.shape[0]
    vec, line, types = ((D,), f32), ((K,), f32), ((ATOMS, ATOMS), f32)
    shapes = (
        ((tokens, D), bf16), ((tokens, D), bf16), vec, vec, ((3, D, HALF_D), f32), ((HALF_D, D), f32), vec, vec,
        ((D, HALF_D), f32), vec, ((HALF_D, D), f32), vec, types, types, line, line, ((K, K), f32), line, ((H, K), f32),
        ((HOPS, H), f32), ((EDGES, H), f32),
    )
    anywhere = pl.BlockSpec(memory_space=pl.ANY)
    return pl.pallas_call(
        unpack_kernel,
        in_specs=[anywhere] * 5,
        out_specs=[anywhere] * len(shapes),
        out_shape=[jax.ShapeDtypeStruct(*item) for item in shapes],
        scratch_shapes=[pltpu.VMEM(*item) for item in shapes] + [
            pltpu.VMEM(fsum.shape, bf16), pltpu.VMEM(qsum.shape, bf16), pltpu.VMEM(rows.shape, f32),
            pltpu.SemaphoreType.DMA((15,)), pltpu.SemaphoreType.DMA((25,)),
        ],
        compiler_params=pltpu.CompilerParams(vmem_limit_bytes=VMEM_BYTES),
        name="unpack",
    )(out_rows, in_rows, fsum, qsum, rows)


def whole_weights(qkv_weight, up_weight, proj_weight, down_weight):
    columns = lambda w: jnp.stack(jnp.split(w, 2, axis=-1))
    rows = lambda w: jnp.stack(jnp.split(w, 2, axis=0))
    gather = lambda w, dim: lax.all_gather(w, "tp", axis=dim, tiled=True)
    return (
        columns(gather(qkv_weight.transpose(1, 0, 2), 2)), columns(gather(up_weight, 1)),
        rows(gather(proj_weight, 0)), rows(gather(down_weight, 0)),
    )


def sum_grads(fgrads, qgrads, small):
    total_f, total_q, rows = lax.psum((fgrads, qgrads, small), ("mol", "tp"))
    share = D // lax.axis_size("tp")
    at = lax.axis_index("tp") * share

    def columns(halves):
        return lax.dynamic_slice_in_dim(jnp.concatenate(list(halves), axis=-1), at, share, halves.ndim - 2)

    def rows_of(block):
        part = total_f[:, D * block : D * (block + 1)]
        sides = jnp.concatenate([part[:, :HALF_D], part[:, HALF_D:]], axis=2).reshape(D, D)
        return lax.dynamic_slice_in_dim(sides, at, share, 0)

    qkv = columns(total_q.reshape(2, D, 3, HALF_D)).transpose(1, 0, 2)
    return [v.astype(f32) for v in (qkv, columns(total_f[:, :D]), rows_of(1), rows_of(2))], rows


def body(
    mesh_shape,
    hidden_in, positions, atom_types, hop_counts, edge_types, lengths, branches,
    attn_gain, attn_shift, qkv_weight, proj_weight, ffn_gain, ffn_shift, up_weight, up_bias, down_weight, down_bias,
    kernel_scale, kernel_shift, centers, spreads, first_weight, first_bias, second_weight, hop_table, edge_table,
    cotangent,
):
    remote = mesh_shape["tp"] == 2 and mesh_shape["mol"] == 16 and branches.shape[0] == 8
    if remote:
        weights = (qkv_weight.transpose(1, 0, 2), up_weight, proj_weight, down_weight)
    else:
        weights = whole_weights(qkv_weight, up_weight, proj_weight, down_weight)
    arrays = dict(
        lengths=lengths, flags=branches.T, positions=positions, atoms=atom_types, hops=hop_counts.T,
        edges=edge_types.T, kernel_scale=kernel_scale, kernel_shift=kernel_shift, centers=centers, spreads=spreads,
        first_weight=first_weight, first_bias=first_bias, second_weight=second_weight.T, hop_table=hop_table,
        edge_table=edge_table, attn_gain=attn_gain, attn_shift=attn_shift, ffn_gain=ffn_gain, ffn_shift=ffn_shift,
        up_bias=up_bias, down_bias=down_bias, hidden=hidden_in, cotangent=cotangent,
        qkv=weights[0], up=weights[1], proj=weights[2], down=weights[3],
    )
    output, grad_input, sums = layer(remote, arrays)
    if remote:
        fsum, qsum, rows = sums
    else:
        big, rows = sum_grads(*sums)
        fsum, qsum = jnp.zeros((3 * D, HALF_D), bf16), jnp.zeros((D, 3 * HALF_D), bf16)
    output, grad_input, *grads = unpack(output, grad_input, fsum, qsum, rows)
    if not remote:
        grads[2], grads[6], grads[3], grads[8] = big
    grads[2] = grads[2].transpose(1, 0, 2)
    grads[16] = grads[16].T
    return (output, grad_input, *grads)


def solution(mesh):
    rows = P(("mol", "tp"), None)
    all_of = P()
    in_specs = (
        rows, P(None, ("mol", "tp")), P(("mol", "tp")), rows, rows, P("mol"), rows, all_of, all_of,
        P(None, None, "tp"), P("tp", None), all_of, all_of, P(None, "tp"), all_of, P("tp", None),
    ) + (all_of,) * 10 + (rows,)
    out_specs = (
        rows, rows, all_of, all_of, P(None, None, "tp"), P("tp", None), all_of, all_of, P(None, "tp"), all_of,
        P("tp", None),
    ) + (all_of,) * 10
    step = functools.partial(body, dict(mesh.shape))
    return jax.shard_map(step, mesh=mesh, in_specs=in_specs, out_specs=out_specs, check_vma=False)
```

```python
import functools
from types import SimpleNamespace

import jax
import jax.numpy as jnp
from jax import lax
from jax.experimental import pallas as pl
from jax.experimental.pallas import tpu as pltpu
from jax.sharding import PartitionSpec as P

D = 768
H = 32
HD = 24
FF = 768
K = 128
SLOT = 64
HALF = SLOT // 2
HALF_D = D // 2
PAIRS = SLOT * SLOT
HOPS = 16
EDGES = 8
ATOMS = 16
GROUP = 4
GROUPS = H // GROUP
HOT = 32

highest = lax.Precision.HIGHEST
neg_large = -1e30
root_tau = 2.5066282746310002
root_half = 0.7071067811865476
inv_root_tau = 0.3989422804014327
head_scale = HD ** (-0.5)
VMEM_BYTES = 62 * 1024 * 1024
TILE = 512

SECOND_ROWS = K
TABLE_ROWS = SECOND_ROWS + H
KERNEL_ROWS = TABLE_ROWS + H
VECTOR_ROWS = KERNEL_ROWS + 8
SMALL_ROWS = 256

MESH = pl.DeviceIdType.MESH
f32 = jnp.float32
bf16 = jnp.bfloat16


def dot_nn(left, right, precision=None):
    return lax.dot_general(left, right, (((1,), (0,)), ((), ())), precision=precision, preferred_element_type=f32)


def dot_nt(left, right, precision=None):
    return lax.dot_general(left, right, (((1,), (1,)), ((), ())), precision=precision, preferred_element_type=f32)


def dot_tn(left, right, precision=None):
    return lax.dot_general(left, right, (((0,), (0,)), ((), ())), precision=precision, preferred_element_type=f32)


def iota(shape, dim):
    return lax.broadcasted_iota(jnp.int32, shape, dim)


def gelu_parts(values):
    size = jnp.abs(values)
    bell = jnp.exp(values * values * -0.5)
    denominator = 1.0 + (0.3275911 * root_half) * size
    t = pl.reciprocal(denominator, approx=True)
    series = 0.5 * 1.061405429
    for factor in (-1.453152027, 1.421413741, -0.284496736, 0.254829592):
        series = series * t + 0.5 * factor
    tail = series * t * bell
    gelu = jnp.maximum(values, 0.0) - size * tail
    outer = tail - size * (bell * inv_root_tau)
    return gelu, jnp.where(values >= 0.0, 1.0 - outer, outer)


def gelu_pair(values):
    size = jnp.abs(values)
    bell = jnp.exp(values * values * -0.5)
    t = pl.reciprocal(1.0 + (0.3275911 * root_half) * size, approx=True)
    series = 0.5 * 1.061405429
    for factor in (-1.453152027, 1.421413741, -0.284496736, 0.254829592):
        series = series * t + 0.5 * factor
    tail = (series * t * bell).astype(bf16)
    density = (bell * inv_root_tau).astype(bf16)
    values = values.astype(bf16)
    size = jnp.abs(values)
    outer = tail - size * density
    one, zero = jnp.ones((), bf16), jnp.zeros((), bf16)
    return jnp.maximum(values, zero) - size * tail, jnp.where(values >= zero, one - outer, outer)


def to_column(row):
    size = row.shape[1]
    same = iota((size, size), 0) == iota((size, size), 1)
    return jnp.sum(jnp.where(same, row, 0.0), axis=1, keepdims=True)


def half_swap(values):
    return pltpu.roll(values, 64, 1)


def low_lanes(rows):
    return iota((rows, 128), 1) < 64


def vmem(count):
    return [pl.BlockSpec(memory_space=pltpu.VMEM)] * count


def row_of(ref):
    return ref[...].reshape(1, ref.shape[0])


def place():
    mol = lax.axis_index("mol")
    return mol % 2, (mol // 2) % 2, mol // 4, lax.axis_index("tp")


def greet(peers):
    for peer in peers:
        pl.semaphore_signal(pltpu.get_barrier_semaphore(), inc=1, device_id=peer, device_id_type=MESH)


def await_greetings(peers):
    pl.semaphore_wait(pltpu.get_barrier_semaphore(), len(peers))


def window(group):
    first = GROUP * HD * group
    start = first // 128 * 128
    width = 128 if first - start + GROUP * HD <= 128 else 256
    return start, width, first - start


def head_masks(group, kind):
    _, width, offset = window(group)
    lane = iota((1, width), 1)
    return [
        ((lane >= offset + HD * h) & (lane < offset + HD * (h + 1))).astype(f32).astype(kind) for h in range(GROUP)
    ]


def spread_heads(values, group):
    return jnp.concatenate([values * mask for mask in head_masks(group, bf16)], axis=0)


def gather_heads(values, group):
    masks = head_masks(group, f32)
    total = values[:SLOT] * masks[0]
    for h in range(1, GROUP):
        total = total + values[SLOT * h : SLOT * (h + 1)] * masks[h]
    return total


def standardize(values):
    centred = values - jnp.mean(values, axis=-1, keepdims=True)
    inv_std = lax.rsqrt(jnp.mean(centred * centred, axis=-1, keepdims=True) + 1e-05)
    return centred * inv_std, inv_std


def norm_back(d_normed, scaled, inv_std, gain):
    weighted = d_normed * gain
    inner_a = jnp.mean(weighted, axis=-1, keepdims=True)
    inner_b = jnp.mean(weighted * scaled, axis=-1, keepdims=True)
    return inv_std * (weighted - inner_a - scaled * inner_b)


def column_sum(values):
    return jnp.sum(values, axis=0, keepdims=True)


class Peers:
    def __init__(self):
        self.core, self.x, self.z, self.tp = place()
        mol = lax.axis_index("mol")
        self.over_core = {"mol": mol + 1 - 2 * self.core}
        self.over_x = {"mol": mol + 2 - 4 * self.x}
        self.over_tp = {"tp": 1 - self.tp}
        self.turn = [lax.rem(self.z + d, 4) for d in range(4)]
        self.over_z = [{"mol": self.turn[d] * 4 + self.x * 2 + self.core} for d in range(4)]

    def neighbour(self, k):
        core = self.core + (1 - 2 * self.core) * (k & 1)
        x = self.x + (1 - 2 * self.x) * (k >> 1 & 1)
        tp = self.tp + (1 - 2 * self.tp) * (k >> 2)
        return core * 4 + tp * 2 + x, {"mol": self.z * 4 + x * 2 + core, "tp": tp}

    def everyone(self):
        return [self.neighbour(k)[1] for k in range(1, 8)] + self.over_z[1:]


def span(start, size):
    return pl.ds(pl.multiple_of(start, size), size)


def add_rows(target, source, rows):
    step = 96 if rows % 96 == 0 else min(rows, 32)

    def piece(i, _):
        at = pl.ds(pl.multiple_of(i * step, step), step)
        target[at, :] = target[at, :] + source[at, :]
        return 0

    lax.fori_loop(0, rows // step, piece, 0)


class Reduction:
    kinds = 11

    def __init__(self, peers, part, total, from_core, from_tp, from_x, from_z, sends, recvs):
        self.peers, self.part, self.total = peers, part, total
        self.from_core, self.from_tp, self.from_x, self.from_z = from_core, from_tp, from_x, from_z
        self.sends, self.recvs = sends, recvs
        self.half = from_core.shape[2]
        self.quarter, self.least = self.half // 2, self.half // 8

    def rows(self, b, level):
        p = self.peers
        at = b * 2 * self.half + p.core * self.half
        if level > 0:
            at = at + p.x * self.quarter
        return at + p.z * self.least if level > 1 else at

    def copy(self, b, kind):
        p = self.peers
        part, total = self.part, self.total
        half, quarter, least = self.half, self.quarter, self.least
        if kind == 0:
            src = part.at[:, span(b * 2 * half + (1 - p.core) * half, half)]
            dst, peer = self.from_core.at[b], p.over_core
        elif kind == 1:
            src, dst, peer = part.at[1 - p.tp, span(self.rows(b, 0), half)], self.from_tp.at[b], p.over_tp
        elif kind == 2:
            src = part.at[p.tp, span(self.rows(b, 0) + (1 - p.x) * quarter, quarter)]
            dst, peer = self.from_x.at[b], p.over_x
        elif kind < 6:
            d = kind - 2
            src = part.at[p.tp, span(self.rows(b, 1) + p.turn[d] * least, least)]
            dst, peer = self.from_z.at[b, d - 1], p.over_z[d]
        elif kind < 9:
            src = dst = total.at[span(self.rows(b, 2), least)]
            peer = p.over_z[kind - 5]
        elif kind == 9:
            src = dst = total.at[span(self.rows(b, 1), quarter)]
            peer = p.over_x
        else:
            src = dst = total.at[span(self.rows(b, 0), half)]
            peer = p.over_core
        return pltpu.make_async_remote_copy(
            src_ref=src, dst_ref=dst, send_sem=self.sends.at[b, kind], recv_sem=self.recvs.at[b, kind],
            device_id=peer, device_id_type=MESH,
        )

    def act(self, b, stage):
        p = self.peers
        half, quarter, least = self.half, self.quarter, self.least
        part = self.part
        if stage == 0:
            self.copy(b, 0).start()
        elif stage == 1:
            self.copy(b, 0).wait_recv()
            at = span(self.rows(b, 0), half)
            add_rows(part.at[1 - p.tp, at], self.from_core.at[b, 1 - p.tp], half)
            self.copy(b, 1).start()
            add_rows(part.at[p.tp, at], self.from_core.at[b, p.tp], half)
        elif stage == 2:
            self.copy(b, 1).wait_recv()
            away, mine = (1 - p.x) * quarter, p.x * quarter
            at = self.rows(b, 0)
            add_rows(part.at[p.tp, span(at + away, quarter)], self.from_tp.at[b, span(away, quarter)], quarter)
            self.copy(b, 2).start()
            add_rows(part.at[p.tp, span(at + mine, quarter)], self.from_tp.at[b, span(mine, quarter)], quarter)
        elif stage == 3:
            self.copy(b, 2).wait_recv()
            add_rows(part.at[p.tp, span(self.rows(b, 1), quarter)], self.from_x.at[b], quarter)
            for kind in (3, 4, 5):
                self.copy(b, kind).start()
        elif stage == 4:
            for kind in (3, 4, 5):
                self.copy(b, kind).wait_recv()
            mine = span(self.rows(b, 2), least)
            value = part[p.tp, mine, :].astype(f32)
            for d in range(3):
                value = value + self.from_z[b, d].astype(f32)
            self.total[mine, :] = value.astype(bf16)
            for kind in (6, 7, 8):
                self.copy(b, kind).start()
        elif stage == 5:
            for kind in (6, 7, 8):
                self.copy(b, kind).wait_recv()
            self.copy(b, 9).start()
        elif stage == 6:
            self.copy(b, 9).wait_recv()
            self.copy(b, 10).start()
        elif stage == 7:
            self.copy(b, 10).wait_recv()
        else:
            for kind in range(self.kinds):
                self.copy(b, kind).wait_send()


class SmallReduction:
    def __init__(self, peers, part, total, from_near, from_z, sends, recvs):
        self.peers, self.part, self.total, self.from_near, self.from_z = peers, part, total, from_near, from_z
        self.sends, self.recvs = sends, recvs
        p = peers
        self.near = [p.neighbour(k) for k in range(8)]
        self.mine = span(self.near[0][0] * 32, 32)

    def copy(self, kind):
        p = self.peers
        if kind < 7:
            index, peer = self.near[kind + 1]
            src, dst = self.part.at[span(index * 32, 32)], self.from_near.at[kind]
        elif kind < 10:
            src = dst = self.from_z.at[p.z]
            peer = p.over_z[kind - 6]
        else:
            src = dst = self.total.at[self.mine]
            peer = self.near[kind - 9][1]
        return pltpu.make_async_remote_copy(
            src_ref=src, dst_ref=dst, send_sem=self.sends.at[kind], recv_sem=self.recvs.at[kind],
            device_id=peer, device_id_type=MESH,
        )

    def act(self, stage):
        hops = (range(0, 7), range(7, 10), range(10, 17))
        if stage == 4:
            for kind in range(17):
                self.copy(kind).wait_send()
            return
        if stage > 0:
            for kind in hops[stage - 1]:
                self.copy(kind).wait_recv()
        if stage == 1:
            value = self.part[self.mine, :]
            for k in range(7):
                value = value + self.from_near[k]
            self.from_z[self.peers.z] = value
        elif stage == 2:
            self.total[self.mine, :] = (self.from_z[0] + self.from_z[1]) + (self.from_z[2] + self.from_z[3])
        if stage < 3:
            for kind in hops[stage]:
                self.copy(kind).start()


def big_scratch(rows, lanes):
    half = rows // 2
    sems = pltpu.SemaphoreType.DMA((3, Reduction.kinds))
    return [
        pltpu.VMEM((3, 2, half, lanes), bf16), pltpu.VMEM((3, half, lanes), bf16),
        pltpu.VMEM((3, half // 2, lanes), bf16), pltpu.VMEM((3, 3, half // 8, lanes), bf16), sems, sems,
    ]


def small_scratch():
    return [
        pltpu.VMEM((7, 32, 128), f32), pltpu.VMEM((4, 32, 128), f32),
        pltpu.SemaphoreType.DMA((17,)), pltpu.SemaphoreType.DMA((17,)),
    ]


class Gather:
    pieces = 6

    def __init__(self, peers, whole, sends, recvs):
        self.peers, self.whole, self.sends, self.recvs = peers, whole, sends, recvs
        self.quarter = peers.x * 2 + peers.core
        self.next_quarter = (1 - peers.x) * 2 + peers.core

    def rows(self, ref, quarter):
        count = ref.shape[0] // 4
        return ref.at[span(quarter * count, count), :]

    def copy(self, index, kind):
        p = self.peers
        if kind == 0:
            src = dst = self.rows(self.whole(index, p.tp), self.quarter)
            peer = p.over_tp
        elif kind == 1:
            src = dst = self.rows(self.whole(index, 1 - p.tp), self.quarter)
            peer = p.over_x
        else:
            src = dst = self.rows(self.whole(index, 1 - p.tp), self.quarter if kind == 2 else self.next_quarter)
            peer = p.over_core
        return pltpu.make_async_remote_copy(
            src_ref=src, dst_ref=dst, send_sem=self.sends.at[index, kind], recv_sem=self.recvs.at[index, kind],
            device_id=peer, device_id_type=MESH,
        )

    def start(self, indices):
        for index in indices:
            self.copy(index, 0).start()

    def onward_x(self, index):
        self.copy(index, 0).wait_recv()
        self.copy(index, 1).start()
        self.copy(index, 2).start()

    def onward_core(self, index):
        self.copy(index, 1).wait_recv()
        self.copy(index, 3).start()

    def arrive(self, index):
        self.copy(index, 2).wait_recv()
        self.copy(index, 3).wait_recv()

    def finish(self):
        for index in range(self.pieces):
            for kind in range(4):
                self.copy(index, kind).wait_send()


def square_turn(values):
    rows, lanes = values.shape
    if lanes < 128:
        values = jnp.concatenate([values, jnp.zeros((rows, 128 - lanes), f32)], axis=1)
    if rows < 128:
        values = jnp.concatenate([values, jnp.zeros((128 - rows, 128), f32)], axis=0)
    return values.T


def widen(values):
    return jnp.concatenate([values] * (TILE // 128), axis=1)


def strips():
    return [slice(16 * i, 16 * (i + 1)) for i in range(K // 16)]


def four_rows(ref, slot, first):
    return jnp.concatenate([ref[slot, pl.ds(first + i, 1), :] for i in range(TILE // 128)], axis=1)


def hot_rows(values, count):
    return (values == iota((count, TILE), 0).astype(f32)).astype(f32)


def fold_lanes(values):
    total = values[:, :128]
    for i in range(1, TILE // 128):
        total = total + values[:, 128 * i : 128 * (i + 1)]
    return total


def twice(ref, values):
    none = jnp.zeros_like(values)
    ref[...] = jnp.concatenate(
        [jnp.concatenate([values, none], axis=1), jnp.concatenate([none, values], axis=1)], axis=0
    ).astype(bf16)


def dot_halves(weights, pieces):
    values = jnp.concatenate(pieces, axis=0)
    half = TILE // 2
    both = dot_nn(weights, jnp.concatenate([values[:, :half], values[:, half:]], axis=0))
    rows = both.shape[0] // 2
    return jnp.concatenate([both[:rows], both[rows:]], axis=1)


def prepare_pairs(r):
    spr = to_column(row_of(r.spreads))
    r.cols[0] = jnp.broadcast_to(to_column(row_of(r.centers)), (K, 128))
    r.cols[1] = jnp.broadcast_to(root_half / spr, (K, 128))
    r.cols[2] = jnp.broadcast_to(-jnp.log(root_tau * spr), (K, 128))
    r.cols[3] = jnp.broadcast_to(to_column(row_of(r.first_bias)), (K, 128))
    r.cols[4] = jnp.broadcast_to(1.0 / spr, (K, 128))
    twice(r.w1, r.first_weight[...].astype(f32))
    twice(r.w1t, r.first_weight[...].astype(f32).T)
    r.w2[...] = square_turn(r.second_weight[...].astype(f32))
    table = jnp.concatenate([r.hop_table[...], r.edge_table[...], jnp.zeros((128 - HOPS - EDGES, H), f32)], axis=0)
    table = jnp.concatenate([table, jnp.zeros((128, 128 - H), f32)], axis=1).T[:H, :HOT]
    one = table.astype(bf16).astype(f32)
    r.base[...] = jnp.concatenate(
        [r.second_weight[...].astype(f32), one, table - one, jnp.zeros((H, 64), f32)], axis=1
    )


def bf16_parts(values, count):
    parts = []
    for _ in range(count):
        parts.append(values.astype(bf16))
        values = values - parts[-1].astype(f32)
    return parts


def pair_tables(r, slots):
    low = low_lanes(HALF)
    low_row = low_lanes(1)
    tables = [part.astype(f32) for ref in (r.kernel_scale, r.kernel_shift) for part in bf16_parts(ref[...], 3)]
    tables = jnp.concatenate([square_turn(part)[:ATOMS, :ATOMS] for part in tables], axis=1)
    tables = jnp.concatenate([tables, jnp.zeros((ATOMS, 128 - 6 * ATOMS), f32)], axis=1).astype(bf16)
    for group in range(slots // 2):
        lanes = slice(128 * group, 128 * (group + 1))
        atoms = r.atoms[lanes].astype(f32).reshape(1, 128)
        rows = jnp.concatenate([r.positions[:, lanes], atoms, jnp.zeros((4, 128), f32)], axis=0)
        columns = square_turn(rows)
        key_hot = (columns[:, 3:4] == iota((128, ATOMS), 1).astype(f32)).astype(f32).astype(bf16)
        picks = dot_nn(key_hot, tables).astype(bf16)
        turned = half_swap(rows)
        for s in range(2):
            slot = 2 * group + s
            tokens = slice(SLOT * s, SLOT * (s + 1))
            double = jnp.where(low_lanes(8), *((rows, turned) if s == 0 else (turned, rows)))
            total = None
            for c in range(3):
                column = columns[tokens, c : c + 1]
                offset = jnp.where(low, column[:HALF], column[HALF:]) - double[c : c + 1]
                total = offset * offset if total is None else total + offset * offset
            distance = jnp.sqrt(total)
            query_hot = (double[3:4] == iota((ATOMS, 128), 0).astype(f32)).astype(f32)
            three, none = [query_hot] * 3, [jnp.zeros((3 * ATOMS, 128), f32)]
            rest = [jnp.zeros((128 - 6 * ATOMS, 128), f32)]
            spread = jnp.concatenate(
                [jnp.concatenate(three + none + rest, axis=0), jnp.concatenate(none + three + rest, axis=0)], axis=1
            )
            both = dot_nn(picks[tokens], spread.astype(bf16))
            scale = jnp.where(low, both[:HALF, :128], both[HALF:, :128])
            shift = jnp.where(low, both[:HALF, 128:], both[HALF:, 128:])
            r.argument[slot] = scale * distance + shift
            r.distance[slot] = distance
            for source, target in ((r.hops, r.hop_rows), (r.edges, r.edge_rows)):
                values = source[:, lanes].astype(f32)
                top, bottom = values[:HALF], values[HALF:]
                if s == 0:
                    target[slot] = jnp.where(low, top, half_swap(bottom))
                else:
                    target[slot] = jnp.where(low, half_swap(top), bottom)
            r.atom_rows[slot] = jnp.broadcast_to(double[3:4], (8, 128))


def table_grads(r, slots):
    lefts, rights = [], []
    for slot in range(slots):
        query_hot = (r.atom_rows[slot, 0:1, :] == iota((ATOMS, 128), 0).astype(f32)).astype(f32)
        keys = jnp.concatenate([query_hot[:, :HALF], query_hot[:, HALF:SLOT]], axis=0)
        keys = jnp.concatenate([keys, keys], axis=1).astype(bf16)
        values = jnp.concatenate([r.dargs[slot] * r.distance[slot], r.dargs[slot]], axis=1)
        both = dot_nn(keys, jnp.concatenate(bf16_parts(values, 2), axis=0))
        low = low_lanes(ATOMS)
        for index in range(2):
            lanes = slice(128 * index, 128 * (index + 1))
            rights.append(bf16_parts(jnp.where(low, both[:ATOMS, lanes], both[ATOMS:, lanes]), 2))
        lefts.append(query_hot.astype(bf16))
    left = jnp.concatenate(lefts, axis=1)
    right = jnp.concatenate(
        [jnp.concatenate([rights[2 * s + index][part] for s in range(slots)], axis=1) for index in range(2) for part in range(2)],
        axis=0,
    )
    result = dot_nt(left, right)
    return [
        result[:, 2 * ATOMS * index : 2 * ATOMS * index + ATOMS] + result[:, 2 * ATOMS * index + ATOMS : 2 * ATOMS * (index + 1)]
        for index in range(2)
    ]


def hold(tile, value):
    return value


def staged(stages, count):
    held = {}

    def step(time):
        for k, stage in reversed(list(enumerate(stages))):
            if 0 <= time - k < count:
                held[time - k] = stage(time - k, held.get(time - k))

    return [functools.partial(step, time) for time in range(count + len(stages) - 1)]


def run_beside(*step_lists):
    for time in range(max(map(len, step_lists))):
        for steps in step_lists:
            if time < len(steps):
                steps[time]()


TILES = PAIRS // TILE
ROWS = TILE // 128


def pair_forward(r, slot, beside=()):
    bank = lax.rem(slot, 2)
    graph_on = r.flags[0, slot].astype(f32)
    space_on = r.flags[1, slot].astype(f32)
    factor = jnp.where(iota((H, 256), 1) < K, space_on, graph_on)
    r.lhs[...] = (r.base[...] * factor).astype(bf16)

    def kernels(tile, _):
        where = slice(tile * TILE, (tile + 1) * TILE)
        arg = four_rows(r.argument, slot, tile * ROWS)
        pieces = []
        for rows in strips():
            u = (arg - widen(r.cols[0, rows])) * widen(r.cols[1, rows])
            pieces.append(jnp.exp(widen(r.cols[2, rows]) - u * u).astype(bf16))
            r.left[bank, rows, where] = pieces[-1]
        return dot_halves(r.w1t[...], pieces)

    def hidden(tile, first):
        where = slice(tile * TILE, (tile + 1) * TILE)
        pieces = []
        for rows in strips():
            value, slope = gelu_pair(first[rows] + widen(r.cols[3, rows]))
            pieces.append(value)
            r.left[bank, slice(K + rows.start, K + rows.stop), where] = pieces[-1]
            r.slope[bank, rows, where] = slope
        hot = jnp.concatenate(
            [
                hot_rows(four_rows(r.hop_rows, slot, tile * ROWS), HOPS),
                hot_rows(four_rows(r.edge_rows, slot, tile * ROWS), HOT - HOPS),
            ],
            axis=0,
        ).astype(bf16)
        return dot_nn(r.lhs[:, : K + 2 * HOT], jnp.concatenate(pieces + [hot] * 2, axis=0))

    def biases(tile, bias):
        bias = bias.astype(bf16).astype(f32)
        for i in range(ROWS):
            r.bias[slot, pl.ds(tile * ROWS + i, H, stride=HALF), :] = bias[:, 128 * i : 128 * (i + 1)]

    run_beside(staged([kernels, hold, hidden, hold, biases], TILES), beside)


def pair_backward(r, slot):
    bank = lax.rem(slot, 2)
    graph_on = r.flags[0, slot].astype(f32)
    space_on = r.flags[1, slot].astype(f32)
    twice(r.w2_twice, r.w2[:, :H] * space_on)

    def scores(tile, _):
        where = slice(tile * TILE, (tile + 1) * TILE)
        grad = jnp.concatenate(
            [r.bias[slot, pl.ds(tile * ROWS + i, H, stride=HALF), :] for i in range(ROWS)], axis=1
        )
        r.right[K:, where] = jnp.concatenate([grad * space_on, grad * graph_on], axis=0).astype(bf16)
        edge_hot = hot_rows(four_rows(r.edge_rows, slot, tile * ROWS), HOT - HOPS)
        edge_hot = jnp.where(iota((HOT - HOPS, TILE), 0) == EDGES, 1.0, edge_hot)
        r.left[bank, 2 * K :, where] = jnp.concatenate(
            [hot_rows(four_rows(r.hop_rows, slot, tile * ROWS), HOPS), edge_hot], axis=0
        ).astype(bf16)
        return dot_halves(r.w2_twice[...], [grad.astype(bf16)])

    def hidden(tile, d_second):
        where = slice(tile * TILE, (tile + 1) * TILE)
        pieces = []
        for rows in strips():
            pieces.append((d_second[rows] * r.slope[bank, rows, where].astype(f32)).astype(bf16))
            r.right[rows, where] = pieces[-1]
        return dot_halves(r.w1[...], pieces)

    def kernels(tile, d_gauss):
        where = slice(tile * TILE, (tile + 1) * TILE)
        arg = four_rows(r.argument, slot, tile * ROWS)
        d_arg = None
        for rows in strips():
            inv = widen(r.cols[4, rows])
            u = (arg - widen(r.cols[0, rows])) * inv
            q = d_gauss[rows] * r.left[bank, rows, where].astype(f32)
            w = q * u
            r.sums[0, rows] += fold_lanes(w)
            r.sums[1, rows] += fold_lanes(w * u - q)
            w = w * inv
            w = w[:8] + w[8:]
            d_arg = w if d_arg is None else d_arg + w
        d_arg = -jnp.sum(d_arg, axis=0, keepdims=True)
        for i in range(ROWS):
            at = tile * ROWS + i
            r.dargs[slot, at : at + 1, :] = d_arg[:, 128 * i : 128 * (i + 1)]

    def products(tile, _):
        if tile % 2 == 1:
            where = slice((tile - 1) * TILE, (tile + 1) * TILE)
            return dot_nt(r.left[bank, :, where], r.right[:, where])

    def add_products(tile, values):
        if tile % 2 == 1:
            r.acc_mixed[...] += values

    run_beside(staged([scores, hold, hidden, hold, kernels, products, hold, add_products], TILES))


def attend_steps(r, s, first_slot, side=0):
    low = low_lanes(HALF)
    rows = span(s * SLOT, SLOT)

    def scores(g, _):
        if g == 0:
            r.work[3 * side] = jnp.zeros((SLOT, D), f32)
        start, width, _ = window(g)
        q = r.joined[rows, start : start + width]
        return dot_nt(r.joined[rows, D + start : D + start + width], spread_heads(q, g))

    def mix(g, products):
        start, width, _ = window(g)
        valid = iota((SLOT, GROUP * SLOT), 0) < r.lengths[first_slot + s]
        parts = []
        for pair in range(GROUP // 2):
            head = GROUP * g + 2 * pair
            one = r.bias[s, head * HALF : (head + 1) * HALF, :]
            two = r.bias[s, (head + 1) * HALF : (head + 2) * HALF, :]
            top = jnp.where(low, one, half_swap(two))
            bottom = jnp.where(low, half_swap(one), two)
            parts.append(jnp.concatenate([top, bottom], axis=0))
        values = jnp.where(valid, products * head_scale + jnp.concatenate(parts, axis=1), neg_large)
        weights = jnp.exp(values - jnp.max(values, axis=0, keepdims=True))
        prob = (weights * (1.0 / jnp.sum(weights, axis=0, keepdims=True))).astype(bf16)
        r.prob[s, :, g * GROUP * SLOT : (g + 1) * GROUP * SLOT] = prob
        return dot_tn(prob, r.joined[rows, 2 * D + start : 2 * D + start + width])

    def gather(g, mixed):
        start, width, _ = window(g)
        r.work[3 * side, :, start : start + width] += gather_heads(mixed, g)
        if g == GROUPS - 1:
            r.attended[rows, :] = r.work[3 * side].astype(bf16)

    return staged([scores, hold, mix, hold, gather], GROUPS)


def attend_back_steps(r, s, side):
    low = low_lanes(HALF)
    rows = span(s * SLOT, SLOT)

    def lanes_of(g):
        start, width, _ = window(g)
        return slice(start, start + width)

    def probabilities(g, _):
        lanes = lanes_of(g)
        if g == 0:
            for i in range(3):
                r.work[3 * side + i] = jnp.zeros((SLOT, D), f32)
        v = r.joined[rows, 2 * D + lanes.start : 2 * D + lanes.stop]
        return dot_nt(v, spread_heads(r.d_attended[rows, lanes], g))

    def scores(g, d_prob):
        lanes = lanes_of(g)
        prob = r.prob[s, :, g * GROUP * SLOT : (g + 1) * GROUP * SLOT]
        wide = prob.astype(f32)
        inner = jnp.sum(wide * d_prob, axis=0, keepdims=True)
        d_scores = (wide * (d_prob - inner)).astype(bf16)
        d_wide = d_scores.astype(f32)
        for pair in range(GROUP // 2):
            head = GROUP * g + 2 * pair
            top = d_wide[:HALF, 128 * pair : 128 * (pair + 1)]
            bottom = d_wide[HALF:, 128 * pair : 128 * (pair + 1)]
            r.bias[s, head * HALF : (head + 1) * HALF, :] = jnp.where(low, top, half_swap(bottom))
            r.bias[s, (head + 1) * HALF : (head + 2) * HALF, :] = jnp.where(low, half_swap(top), bottom)
        return (
            dot_tn(d_scores, r.joined[rows, D + lanes.start : D + lanes.stop]),
            dot_nn(d_scores, spread_heads(r.joined[rows, lanes], g)),
            dot_nn(prob, spread_heads(r.d_attended[rows, lanes], g)),
        )

    def gather(g, products):
        lanes = lanes_of(g)
        r.work[3 * side, :, lanes] += gather_heads(products[0], g)
        r.work[3 * side + 1, :, lanes] += products[1]
        r.work[3 * side + 2, :, lanes] += products[2]
        if g == GROUPS - 1:
            r.joined[rows, 0:D] = (r.work[3 * side] * head_scale).astype(bf16)
            r.joined[rows, D : 2 * D] = (r.work[3 * side + 1] * head_scale).astype(bf16)
            r.joined[rows, 2 * D : 3 * D] = r.work[3 * side + 2].astype(bf16)

    return staged([probabilities, hold, scores, hold, gather], GROUPS)


def project(r, rows):
    scaled, _ = standardize(r.hidden[rows, :].astype(f32))
    normed = (scaled * row_of(r.attn_gain) + row_of(r.attn_shift)).astype(bf16)
    r.normed_a[rows, :] = normed
    for m in range(3):
        for t in range(2):
            at = m * D + t * HALF_D
            r.joined[rows, at : at + HALF_D] = dot_nn(normed, r.wqkv[t, m]).astype(bf16)


def feed(r, rows):
    halves = [slice(0, HALF_D), slice(HALF_D, D)]
    resid = r.hidden[rows, :].astype(f32)
    for t in range(2):
        resid = resid + dot_nn(r.attended[rows, halves[t]], r.wproj[t])
    scaled, inv_std = standardize(resid)
    normed = (scaled * row_of(r.ffn_gain) + row_of(r.ffn_shift)).astype(bf16)
    r.normed_f[rows, :] = normed
    pre = jnp.concatenate([dot_nn(normed, r.wup[t]) for t in range(2)], axis=1)
    value, slope = gelu_parts(pre + row_of(r.up_bias))
    active = value.astype(bf16)
    r.activated[rows, :] = active
    result = resid + row_of(r.down_bias)
    for t in range(2):
        result = result + dot_nn(active[:, halves[t]], r.wdown[t])
    r.out_rows[rows, :] = result.astype(bf16)
    cot = r.cotangent[rows, :]
    cot_wide = cot.astype(f32)
    d_active = jnp.concatenate([dot_nt(cot, r.wdown[t]) for t in range(2)], axis=1)
    d_hidden = (d_active * slope).astype(bf16)
    r.d_pre[rows, :] = d_hidden
    d_normed = dot_nt(d_hidden[:, halves[0]], r.wup[0]) + dot_nt(d_hidden[:, halves[1]], r.wup[1])
    d_resid = cot_wide + norm_back(d_normed, scaled, inv_std, row_of(r.ffn_gain))
    r.d_resid[rows, :] = d_resid
    branch = d_resid.astype(bf16)
    r.d_branch[rows, :] = branch
    for t in range(2):
        r.d_attended[rows, halves[t]] = dot_nt(branch, r.wproj[t]).astype(bf16)
    r.vectors[2:3, :] += column_sum(d_normed * scaled)
    r.vectors[3:4, :] += column_sum(d_normed)
    r.vectors[4:5, :] += column_sum(d_hidden.astype(f32))
    r.vectors[5:6, :] += column_sum(cot_wide)


def feed_grads(r, block):
    halves = [slice(0, HALF_D), slice(HALF_D, D)]
    if block == 0:
        grad = dot_tn(r.normed_f[...], r.d_pre[...]).astype(bf16)
        for t in range(2):
            r.fpart[t, :D, :] = grad[:, halves[t]]
        return
    left, right = (r.attended, r.d_branch) if block == 1 else (r.activated, r.cotangent)
    for t in range(2):
        grad = dot_tn(left[:, halves[t]], right[...]).astype(bf16)
        for side in range(2):
            r.fpart[t, D * block + HALF_D * side : D * block + HALF_D * (side + 1), :] = grad[:, halves[side]]


def qkv_grads(r, block):
    rows = slice(256 * block, 256 * (block + 1))
    for m in range(3):
        grad = dot_tn(r.normed_a[:, rows], r.joined[:, m * D : (m + 1) * D]).astype(bf16)
        for t in range(2):
            r.qpart[t, rows, m * HALF_D : (m + 1) * HALF_D] = grad[:, t * HALF_D : (t + 1) * HALF_D]


def finish_input(r, rows):
    d_normed = None
    for m in range(3):
        for t in range(2):
            at = m * D + t * HALF_D
            term = dot_nt(r.joined[rows, at : at + HALF_D], r.wqkv[t, m])
            d_normed = term if d_normed is None else d_normed + term
    scaled, inv_std = standardize(r.hidden[rows, :].astype(f32))
    grad = r.d_resid[rows, :] + norm_back(d_normed, scaled, inv_std, row_of(r.attn_gain))
    r.in_rows[rows, :] = grad.astype(bf16)
    r.vectors[0:1, :] += column_sum(d_normed * scaled)
    r.vectors[1:2, :] += column_sum(d_normed)


def pack_small(r, slots):
    tables = table_grads(r, slots)
    for v in range(6):
        for i in range(D // 128):
            at = VECTOR_ROWS + v * (D // 128) + i
            r.spart[at : at + 1, :] = r.vectors[v : v + 1, 128 * i : 128 * (i + 1)]
    r.spart[0:K, :] = r.acc_mixed[0:K, :K]
    r.spart[SECOND_ROWS : SECOND_ROWS + H, :] = square_turn(r.acc_mixed[K : 2 * K, K:])[:H]
    r.spart[TABLE_ROWS : TABLE_ROWS + H, :HOT] = square_turn(r.acc_mixed[2 * K :, K:])[H : 2 * H, :HOT]
    for index in range(2):
        rows = slice(TABLE_ROWS + ATOMS * index, TABLE_ROWS + ATOMS * (index + 1))
        r.spart[rows, HOT : HOT + ATOMS] = tables[index]
    ones = 2 * K + HOPS + EDGES
    r.spart[KERNEL_ROWS : KERNEL_ROWS + 1, :] = r.acc_mixed[ones : ones + 1, :K]
    for index in range(2):
        column = jnp.sum(r.sums[index] * r.cols[4], axis=1, keepdims=True)
        same = iota((K, K), 0) == iota((K, K), 1)
        at = KERNEL_ROWS + 1 + index
        r.spart[at : at + 1, :] = jnp.sum(jnp.where(same, column, 0.0), axis=0, keepdims=True)


class Stage:
    def __init__(self, names, near_inputs, carried, refs):
        self.r = SimpleNamespace(**dict(zip(names, refs)))
        r = self.r
        self.loads = {
            name: pltpu.make_async_copy(getattr(r, "given_" + name), getattr(r, name), r.input_sems.at[i])
            for i, name in enumerate(near_inputs)
        }
        self.stores = {
            name: pltpu.make_async_copy(getattr(r, name), getattr(r, name + "_far"), r.carry_sems.at[i])
            for i, name in enumerate(carried)
        }

    def load(self, *names):
        for name in names:
            self.loads[name].start()

    def need(self, *names):
        for name in names:
            self.loads[name].wait()

    def store(self, *names):
        for name in names:
            self.stores[name].start()

    def stored(self):
        for copy in self.stores.values():
            copy.wait()


def each_chunk(r, tokens, work):
    chunk = min(512, tokens)

    def one(c, _):
        work(r, span(c * chunk, chunk))
        return 0

    lax.fori_loop(0, tokens // chunk, one, 0)


def pair_moves(r, slot, back):
    bank = lax.rem(slot, 2)
    both = (r.left_far.at[slot], r.left.at[bank, : 2 * K]), (r.slope_far.at[slot], r.slope.at[bank])
    for index, (far, near) in enumerate(both):
        yield pltpu.make_async_copy(*((far, near) if back else (near, far)), r.pair_sems.at[bank, index])


def start_moves(r, slot, back):
    for copy in pair_moves(r, slot, back):
        copy.start()


def wait_moves(r, slot, back):
    for copy in pair_moves(r, slot, back):
        copy.wait()


def run(steps):
    for act, *where in steps:
        act(*where)


def at_time(index, plan):
    for k, steps in plan.items():
        pl.when(index == k)(functools.partial(run, steps))


FFN_BACK = {0: [(1, 1), (2, 1)], 3: [(0, 2)], 7: [(0, 3), (1, 2)]}
AFTER_GRADS = ([(0, 4), (1, 3), (2, 2)], [(0, 1), (1, 1), (2, 1)])
AFTER_HALF = ([(0, 5)], [])
AFTER_INPUT = ([(2, 3), (1, 4)], [(0, 2)])
FFN_PAIRS = {
    0: [(0, 6)], 2: [(2, 4)], 3: [(1, 5), (0, 7)], 5: [(2, 5)], 7: [(1, 6)], 9: [(2, 6)], 10: [(1, 7)], 12: [(2, 7)],
}
QKV_PAIRS = {
    2: [(0, 3)], 3: [(1, 2)], 6: [(1, 3), (2, 2), (0, 4)], 9: [(1, 4)], 10: [(0, 5)], 11: [(2, 3)], 12: [(1, 5)],
    13: [(0, 6)], 14: [(2, 4)], 15: [(1, 6)],
}


def layer_kernel(remote, names, near_inputs, carried, *refs):
    stage = Stage(names, near_inputs, carried, refs)
    r = stage.r
    stage.load(*[name for name in near_inputs if name not in ("hidden", "cotangent")])
    tokens = r.hidden.shape[0]
    slots = tokens // SLOT
    peers = Peers()
    if remote:
        greet(peers.everyone())
    whole = [r.wqkv, r.wup, r.wproj, r.wdown]
    given = [r.given_qkv, r.given_up, r.given_proj, r.given_down]
    targets = [w.at[peers.tp] for w in whole] if remote else whole
    loads = [
        pltpu.make_async_copy(src, dst, r.load_sems.at[i]) for i, (src, dst) in enumerate(zip(given, targets))
    ]
    for load in loads:
        load.start()
    stage.load("hidden", "cotangent")
    gather_plan = {}
    if remote:

        def whole_piece(index, tp):
            return whole[0].at[tp, index] if index < 3 else whole[index - 2].at[tp]

        gather = Gather(peers, whole_piece, r.gather_sends, r.gather_recvs)
        ffn = Reduction(peers, r.fpart, r.ftotal, r.f_core, r.f_tp, r.f_x, r.f_z, r.f_sends, r.f_recvs)
        qkv = Reduction(peers, r.qpart, r.qtotal, r.q_core, r.q_tp, r.q_x, r.q_z, r.q_sends, r.q_recvs)
        small = SmallReduction(peers, r.spart, r.stotal, r.s_near, r.s_z, r.s_sends, r.s_recvs)
        x, core = gather.onward_x, gather.onward_core
        gather_plan = {
            0: [(x, 0)], 1: [(x, 1)], 2: [(core, 0), (x, 2)], 3: [(core, 1), (x, 3), (core, 2)],
            4: [(x, 4)], 5: [(core, 3), (x, 5)], 6: [(core, 4)], 7: [(core, 5)],
        }

    def leave(which, block):
        near, far = ((r.ftotal, r.ftotal_far), (r.qtotal, r.qtotal_far))[which]
        rows = near.shape[0] // 3
        at = slice(block * rows, (block + 1) * rows)
        return pltpu.make_async_copy(near.at[at], far.at[at], r.leave_sems.at[3 * which + block])

    def advance(which, actions):
        if remote:
            for block, step in actions:
                (ffn, qkv)[which].act(block, step)
                if step == 7:
                    leave(which, block).start()

    def plan_of(*plans):
        times = sorted(set().union(*plans)) if remote else []
        return {
            k: [(advance, which, plan[k]) for which, plan in enumerate(plans) if k in plan] for k in times
        }

    stage.need(*[name for name in near_inputs if name not in ("hidden", "cotangent")])
    prepare_pairs(r)
    pair_tables(r, slots)
    if remote:
        await_greetings(peers.everyone())
        for load, indices in zip(loads, ((0, 1, 2), (3,), (4,), (5,))):
            load.wait()
            gather.start(indices)

    first_slot = peers.tp * slots
    alone = (5 * slots + 7) // 8

    def pairs(slot, _):
        pl.when(slot >= 2)(lambda: wait_moves(r, slot - 2, False))
        pair_forward(r, slot)
        start_moves(r, slot, False)
        at_time(slot, gather_plan)
        return 0

    def pairs_and_attention(slot, _):
        pl.when(slot >= 2)(lambda: wait_moves(r, slot - 2, False))
        pair_forward(r, slot, attend_steps(r, slot - alone, first_slot))
        start_moves(r, slot, False)
        at_time(slot, gather_plan)
        return 0

    def attend_two(i, _):
        s = slots - alone + 2 * i
        run_beside(attend_steps(r, s, first_slot, 0), attend_steps(r, s + 1, first_slot, 1))
        return 0

    lax.fori_loop(0, alone, pairs, 0)
    stage.need("hidden")
    if remote:
        for index in range(3):
            gather.arrive(index)
    else:
        for load in loads:
            load.wait()
    each_chunk(r, tokens, project)
    lax.fori_loop(alone, slots, pairs_and_attention, 0)
    lax.fori_loop(0, alone // 2, attend_two, 0)
    if alone % 2 == 1:
        run_beside(attend_steps(r, slots - 1, first_slot))
    stage.need("cotangent")
    if remote:
        for index in range(3, 6):
            gather.arrive(index)
    r.vectors[...] = jnp.zeros_like(r.vectors)
    each_chunk(r, tokens, feed)
    stage.store("out_rows")
    for slot in (slots - 2, slots - 1):
        wait_moves(r, slot, False)
    start_moves(r, 0, True)
    start_moves(r, 1, True)
    for block in range(3):
        feed_grads(r, block)
        advance(0, [(block, 0)])
    advance(0, [(0, 1)])

    back_plan, pair_plan = plan_of(FFN_BACK), plan_of(FFN_PAIRS, QKV_PAIRS)

    def back_two(i, _):
        run_beside(attend_back_steps(r, 2 * i, 0), attend_back_steps(r, 2 * i + 1, 1))
        at_time(2 * i, back_plan)
        at_time(2 * i + 1, back_plan)
        return 0

    lax.fori_loop(0, slots // 2, back_two, 0)
    for block in range(3):
        qkv_grads(r, block)
        advance(1, [(block, 0)])
    for which in range(2):
        advance(which, AFTER_GRADS[which])
    each_chunk(r, tokens, finish_input)
    stage.store("in_rows")
    for which in range(2):
        advance(which, AFTER_HALF[which] + AFTER_INPUT[which])
    for ref in (r.sums, r.acc_mixed, r.spart):
        ref[...] = jnp.zeros_like(ref)

    def pairs_back(slot, _):
        wait_moves(r, slot, True)
        pair_backward(r, slot)
        at_time(2 * slot, pair_plan)
        pl.when(slot + 2 < slots)(lambda: start_moves(r, slot + 2, True))
        at_time(2 * slot + 1, pair_plan)
        return 0

    lax.fori_loop(0, slots, pairs_back, 0)
    pack_small(r, slots)
    if remote:
        small.act(0)
        advance(1, [(2, 5), (0, 7)])
        small.act(1)
        advance(1, [(1, 7)])
        advance(1, [(2, 6)])
        small.act(2)
        advance(1, [(2, 7)])
        small.act(3)
        rows = pltpu.make_async_copy(r.stotal, r.stotal_far, r.leave_sems.at[6])
        rows.start()
        for which in range(2):
            advance(which, [(b, 8) for b in range(3)])
        small.act(4)
        gather.finish()
        for which in range(2):
            for block in range(3):
                leave(which, block).wait()
        rows.wait()
    else:
        stage.store("fpart", "qpart", "spart")
    stage.stored()


def call_stage(kernel, name, remote, collective, arrays, scalars, far, outs, carried, scratch):
    vm, sem = pltpu.VMEM, pltpu.SemaphoreType.DMA
    near = {n: vm(a.shape, a.dtype) for n, a in arrays.items() if n not in scalars + far}
    in_names = [n if n in scalars or n.endswith("_far") else "given_" + n for n in arrays]
    results = outs | {n + "_far": item for n, item in carried.items()}
    scratch = near | {n: vm(*item) for n, item in carried.items()} | scratch
    scratch |= {"input_sems": sem((len(near),)), "carry_sems": sem((len(carried),))}
    names = in_names + list(results) + list(scratch)
    values = pl.pallas_call(
        functools.partial(kernel, remote, names, list(near), list(carried)),
        in_specs=[pl.BlockSpec(memory_space=pltpu.SMEM if n in scalars else pl.ANY) for n in arrays],
        out_specs=[pl.BlockSpec(memory_space=pl.ANY)] * len(results),
        out_shape=[jax.ShapeDtypeStruct(*item) for item in results.values()],
        scratch_shapes=list(scratch.values()),
        compiler_params=pltpu.CompilerParams(
            vmem_limit_bytes=VMEM_BYTES, **(dict(collective_id=collective, has_side_effects=True) if remote else {})
        ),
        name=name,
    )(*arrays.values())
    return dict(zip(results, values))


def layer(remote, arrays):
    tokens = arrays["hidden"].shape[0]
    slots = tokens // SLOT
    v, sem = pltpu.VMEM, pltpu.SemaphoreType.DMA
    of_tokens = (tokens, D)
    table = (slots, HALF, 128)
    fshape, qshape, sshape = (3 * D, HALF_D), (D, 3 * HALF_D), (SMALL_ROWS, 128)
    outs = {"left_far": ((slots, 2 * K, PAIRS), bf16), "slope_far": ((slots, K, PAIRS), bf16)}
    carried = {"out_rows": (of_tokens, bf16), "in_rows": (of_tokens, bf16)}
    scratch = {
        "wqkv": v((2, 3, D, HALF_D), bf16), "wup": v((2, D, HALF_D), bf16), "wproj": v((2, HALF_D, D), bf16),
        "wdown": v((2, HALF_D, D), bf16), "load_sems": sem((4,)), "pair_sems": sem((2, 2)),
        "left": v((2, 2 * K + HOT, PAIRS), bf16), "slope": v((2, K, PAIRS), bf16),
        "right": v((K + 2 * H, PAIRS), bf16), "cols": v((5, K, 128), f32), "w1": v((2 * K, 2 * K), bf16), "w1t": v((2 * K, 2 * K), bf16),
        "w2": v((K, 128), f32), "w2_twice": v((2 * K, 2 * H), bf16), "base": v((H, 256), f32), "lhs": v((H, 256), bf16),
        "argument": v(table, f32), "distance": v(table, f32), "hop_rows": v(table, f32), "edge_rows": v(table, f32),
        "atom_rows": v((slots, 8, 128), f32), "dargs": v(table, f32), "bias": v((slots, H * HALF, 128), f32),
        "work": v((6, SLOT, D), f32), "normed_a": v(of_tokens, bf16), "joined": v((tokens, 3 * D), bf16),
        "prob": v((slots, SLOT, H * SLOT), bf16), "attended": v(of_tokens, bf16), "normed_f": v(of_tokens, bf16),
        "activated": v(of_tokens, bf16), "d_pre": v(of_tokens, bf16), "d_branch": v(of_tokens, bf16),
        "d_attended": v(of_tokens, bf16), "d_resid": v(of_tokens, f32), "vectors": v((8, D), f32),
        "sums": v((2, K, 128), f32), "acc_mixed": v((2 * K + HOT, K + 2 * H), f32),
    }
    parts = {"fpart": ((2,) + fshape, bf16), "qpart": ((2,) + qshape, bf16), "spart": (sshape, f32)}
    totals = {"ftotal": (fshape, bf16), "qtotal": (qshape, bf16), "stotal": (sshape, f32)}
    if remote:
        outs |= {n + "_far": item for n, item in totals.items()}
        scratch |= {n: v(*item) for n, item in (parts | totals).items()}
        scratch |= {"leave_sems": sem((7,)), "gather_sends": sem((6, 4)), "gather_recvs": sem((6, 4))}
        for name, shape in (("f", (D, HALF_D)), ("q", (D // 3, 3 * HALF_D))):
            keys = ("_core", "_tp", "_x", "_z", "_sends", "_recvs")
            scratch |= {name + key: item for key, item in zip(keys, big_scratch(*shape))}
        scratch |= dict(zip(("s_near", "s_z", "s_sends", "s_recvs"), small_scratch()))
    else:
        carried |= parts
    results = call_stage(
        layer_kernel, "layer", remote, 0, arrays, ("lengths", "flags"), ("qkv", "up", "proj", "down"), outs, carried,
        scratch,
    )
    sums = [results[n + "_far"] for n in (totals if remote else parts)]
    return results["out_rows_far"], results["in_rows_far"], sums


RESULTS = (
    "output", "grad_input", "attn_gain", "attn_shift", "qkv", "proj", "ffn_gain", "ffn_shift", "up", "up_bias", "down",
    "down_bias", "scale", "shift", "centers", "spreads", "first", "first_bias", "second", "hop", "edge",
)


def unpack_kernel(*refs):
    given = SimpleNamespace(**dict(zip(("out_rows", "in_rows", "fsum", "qsum", "rows"), refs)))
    far = SimpleNamespace(**dict(zip(RESULTS, refs[5:])))
    count = len(RESULTS)
    near = SimpleNamespace(**dict(zip(RESULTS, refs[5 + count : 5 + 2 * count])))
    fsum, qsum, rows, load_sems, store_sems = refs[5 + 2 * count :]
    moves = [(given.rows, rows)]
    sources = ((given.qsum, qsum, 3), (given.fsum, fsum, 9), (given.out_rows, near.output, 1), (given.in_rows, near.grad_input, 1))
    for src, dst, pieces in sources:
        height = src.shape[0] // pieces
        for i in range(pieces):
            at = slice(i * height, (i + 1) * height)
            moves.append((src.at[at], dst.at[at]))
    loads = [pltpu.make_async_copy(src, dst, load_sems.at[i]) for i, (src, dst) in enumerate(moves)]
    for load in loads:
        load.start()
    stores = []

    def store(src, dst):
        stores.append(pltpu.make_async_copy(src, dst, store_sems.at[len(stores)]))
        stores[-1].start()

    for i in range(3):
        loads[1 + i].wait()
        at = slice(256 * i, 256 * (i + 1))
        for m in range(3):
            near.qkv[m, at] = qsum[at, m * HALF_D : (m + 1) * HALF_D].astype(f32)
        store(near.qkv.at[:, at], far.qkv.at[:, at])
    for i in range(3):
        loads[4 + i].wait()
        at = slice(256 * i, 256 * (i + 1))
        near.up[at, :] = fsum[at, :].astype(f32)
        store(near.up.at[at], far.up.at[at])
    for block, name in ((1, "proj"), (2, "down")):
        for i in range(3):
            loads[4 + 3 * block + i].wait()
        ref = getattr(near, name)
        at = D * block
        ref[:, :HALF_D] = fsum[at : at + HALF_D, :].astype(f32)
        ref[:, HALF_D:] = fsum[at + HALF_D : at + D, :].astype(f32)
        store(ref, getattr(far, name))
    loads[13].wait()
    store(near.output, far.output)
    loads[14].wait()
    store(near.grad_input, far.grad_input)
    loads[0].wait()
    names = ("attn_gain", "attn_shift", "ffn_gain", "ffn_shift", "up_bias", "down_bias")
    for v, name in enumerate(names):
        for i in range(D // 128):
            getattr(near, name)[pl.ds(128 * i, 128)] = rows[VECTOR_ROWS + v * (D // 128) + i, :]
    near.first[...] = rows[0:K, :]
    near.second[...] = rows[SECOND_ROWS : SECOND_ROWS + H, :]
    table = rows[TABLE_ROWS : TABLE_ROWS + H, :]
    near.scale[...] = table[:ATOMS, HOT : HOT + ATOMS]
    near.shift[...] = table[ATOMS:, HOT : HOT + ATOMS]
    turned = square_turn(table)
    near.hop[...] = turned[:HOPS, :H]
    near.edge[...] = turned[HOPS : HOPS + EDGES, :H]
    lines = ("first_bias", "centers", "spreads")
    for i, name in enumerate(lines):
        getattr(near, name)[...] = rows[KERNEL_ROWS + i, :]
    for name in names + ("first", "second", "scale", "shift", "hop", "edge") + lines:
        store(getattr(near, name), getattr(far, name))
    for copy in stores:
        copy.wait()


def unpack(out_rows, in_rows, fsum, qsum, rows):
    tokens = out_rows.shape[0]
    vec, line, types = ((D,), f32), ((K,), f32), ((ATOMS, ATOMS), f32)
    shapes = (
        ((tokens, D), bf16), ((tokens, D), bf16), vec, vec, ((3, D, HALF_D), f32), ((HALF_D, D), f32), vec, vec,
        ((D, HALF_D), f32), vec, ((HALF_D, D), f32), vec, types, types, line, line, ((K, K), f32), line, ((H, K), f32),
        ((HOPS, H), f32), ((EDGES, H), f32),
    )
    anywhere = pl.BlockSpec(memory_space=pl.ANY)
    return pl.pallas_call(
        unpack_kernel,
        in_specs=[anywhere] * 5,
        out_specs=[anywhere] * len(shapes),
        out_shape=[jax.ShapeDtypeStruct(*item) for item in shapes],
        scratch_shapes=[pltpu.VMEM(*item) for item in shapes] + [
            pltpu.VMEM(fsum.shape, bf16), pltpu.VMEM(qsum.shape, bf16), pltpu.VMEM(rows.shape, f32),
            pltpu.SemaphoreType.DMA((15,)), pltpu.SemaphoreType.DMA((25,)),
        ],
        compiler_params=pltpu.CompilerParams(vmem_limit_bytes=VMEM_BYTES),
        name="unpack",
    )(out_rows, in_rows, fsum, qsum, rows)


def whole_weights(qkv_weight, up_weight, proj_weight, down_weight):
    columns = lambda w: jnp.stack(jnp.split(w, 2, axis=-1))
    rows = lambda w: jnp.stack(jnp.split(w, 2, axis=0))
    gather = lambda w, dim: lax.all_gather(w, "tp", axis=dim, tiled=True)
    return (
        columns(gather(qkv_weight.transpose(1, 0, 2), 2)), columns(gather(up_weight, 1)),
        rows(gather(proj_weight, 0)), rows(gather(down_weight, 0)),
    )


def sum_grads(fgrads, qgrads, small):
    total_f, total_q, rows = lax.psum((fgrads, qgrads, small), ("mol", "tp"))
    share = D // lax.axis_size("tp")
    at = lax.axis_index("tp") * share

    def columns(halves):
        return lax.dynamic_slice_in_dim(jnp.concatenate(list(halves), axis=-1), at, share, halves.ndim - 2)

    def rows_of(block):
        part = total_f[:, D * block : D * (block + 1)]
        sides = jnp.concatenate([part[:, :HALF_D], part[:, HALF_D:]], axis=2).reshape(D, D)
        return lax.dynamic_slice_in_dim(sides, at, share, 0)

    qkv = columns(total_q.reshape(2, D, 3, HALF_D)).transpose(1, 0, 2)
    return [v.astype(f32) for v in (qkv, columns(total_f[:, :D]), rows_of(1), rows_of(2))], rows


def body(
    mesh_shape,
    hidden_in, positions, atom_types, hop_counts, edge_types, lengths, branches,
    attn_gain, attn_shift, qkv_weight, proj_weight, ffn_gain, ffn_shift, up_weight, up_bias, down_weight, down_bias,
    kernel_scale, kernel_shift, centers, spreads, first_weight, first_bias, second_weight, hop_table, edge_table,
    cotangent,
):
    remote = mesh_shape["tp"] == 2 and mesh_shape["mol"] == 16 and branches.shape[0] == 8
    if remote:
        weights = (qkv_weight.transpose(1, 0, 2), up_weight, proj_weight, down_weight)
    else:
        weights = whole_weights(qkv_weight, up_weight, proj_weight, down_weight)
    arrays = dict(
        lengths=lengths, flags=branches.T, positions=positions, atoms=atom_types, hops=hop_counts.T,
        edges=edge_types.T, kernel_scale=kernel_scale, kernel_shift=kernel_shift, centers=centers, spreads=spreads,
        first_weight=first_weight, first_bias=first_bias, second_weight=second_weight.T, hop_table=hop_table,
        edge_table=edge_table, attn_gain=attn_gain, attn_shift=attn_shift, ffn_gain=ffn_gain, ffn_shift=ffn_shift,
        up_bias=up_bias, down_bias=down_bias, hidden=hidden_in, cotangent=cotangent,
        qkv=weights[0], up=weights[1], proj=weights[2], down=weights[3],
    )
    output, grad_input, sums = layer(remote, arrays)
    if remote:
        fsum, qsum, rows = sums
    else:
        big, rows = sum_grads(*sums)
        fsum, qsum = jnp.zeros((3 * D, HALF_D), bf16), jnp.zeros((D, 3 * HALF_D), bf16)
    output, grad_input, *grads = unpack(output, grad_input, fsum, qsum, rows)
    if not remote:
        grads[2], grads[6], grads[3], grads[8] = big
    grads[2] = grads[2].transpose(1, 0, 2)
    grads[16] = grads[16].T
    return (output, grad_input, *grads)


def solution(mesh):
    rows = P(("mol", "tp"), None)
    all_of = P()
    in_specs = (
        rows, P(None, ("mol", "tp")), P(("mol", "tp")), rows, rows, P("mol"), rows, all_of, all_of,
        P(None, None, "tp"), P("tp", None), all_of, all_of, P(None, "tp"), all_of, P("tp", None),
    ) + (all_of,) * 10 + (rows,)
    out_specs = (
        rows, rows, all_of, all_of, P(None, None, "tp"), P("tp", None), all_of, all_of, P(None, "tp"), all_of,
        P("tp", None),
    ) + (all_of,) * 10
    step = functools.partial(body, dict(mesh.shape))
    return jax.shard_map(step, mesh=mesh, in_specs=in_specs, out_specs=out_specs, check_vma=False)
```
